32 devices in a mesh: seq: 8 (over z, core), fsdp: 4 (over y, x).
Axes of the slice: x: 2, y: 2, z: 4, core: 2. Of those that a mesh axis runs over, the one named last changes fastest.
Arguments:
- tokens: bfloat16 [4, 2048, 1536], P('fsdp', 'seq'), may hold values from -6 to 6
- positions: int32 [4, 2048], P('fsdp', 'seq'), may hold values from 0 to 3839, as said below
- first_gain: bfloat16 [1536], P('fsdp'), may hold values from 0.5 to 1.5
- query_weight: bfloat16 [1536, 1536], P('fsdp'), may hold values from -0.15625 to 0.15625
- key_weight: bfloat16 [1536, 768], P('fsdp'), may hold values from -0.15625 to 0.15625
- value_weight: bfloat16 [1536, 768], P('fsdp'), may hold values from -0.15625 to 0.15625
- output_weight: bfloat16 [1536, 1536], P('fsdp'), may hold values from -6 to 6
- second_gain: bfloat16 [1536], P('fsdp'), may hold values from 0.5 to 1.5
- gate_weight: bfloat16 [1536, 4096], P('fsdp'), may hold values from -0.15625 to 0.15625
- up_weight: bfloat16 [1536, 4096], P('fsdp'), may hold values from -0.15625 to 0.15625
- down_weight: bfloat16 [4096, 1536], P('fsdp'), may hold values from -0.09375 to 0.09375
- cotangent: bfloat16 [4, 2048, 1536], P('fsdp', 'seq'), may hold values from -6 to 6
Outputs:
- block_output: bfloat16 [4, 2048, 1536], P('fsdp', 'seq')
- input_grad: bfloat16 [4, 2048, 1536], P('fsdp', 'seq')
- first_gain_grad: float32 [1536], P('fsdp')
- query_grad: float32 [1536, 1536], P('fsdp')
- key_grad: float32 [1536, 768], P('fsdp')
- value_grad: float32 [1536, 768], P('fsdp')
- output_grad: float32 [1536, 1536], P('fsdp')
- second_gain_grad: float32 [1536], P('fsdp')
- gate_grad: float32 [1536, 4096], P('fsdp')
- up_grad: float32 [1536, 4096], P('fsdp')
- down_grad: float32 [4096, 1536], P('fsdp')
The draws below stay inside these ranges and needn't reach their ends.
Inputs may be any that keep to these rules, and one draw needn't show every extreme that they name: Each sequence is a pack of three documents; positions count from 0 at each document's first token; the middle document begins within the sequence's first 256 tokens, after its first token, and holds exactly 3840 tokens.
All inputs are finite; a program needn't handle non-finite values.
Results may differ from the reference program's by a relative error of at most 0.02.
Values may be sent and summed in bfloat16 or wider, within the bound.
No kernel may reach another device: no remote copies, remote signals or barrier semaphores. Data moves between devices by JAX's collectives and lax.ppermute only.
A program may use at most 320 MiB of HBM per device.

```python
import jax
import jax.numpy as jnp
from jax import lax

D = 1536
QH = 16
KVH = 8
HD = 96
FF = 4096
TOK_DEV = 256
HALF_LEN = 2048
SEQ_LEN = 4096
HALVES = 4
SEQS = 2


def draw_positions(key, part):
    key = jax.random.fold_in(key, 7)
    seq_keys = jax.random.split(key, SEQS)

    def one_sequence(seq_key):
        first = jax.random.randint(seq_key, (), 1, TOK_DEV)
        second = first + (SEQ_LEN - TOK_DEV)
        index = jnp.arange(SEQ_LEN, dtype=jnp.int32)
        start = jnp.where(index >= second, second, jnp.where(index >= first, first, 0))
        return (index - start).astype(jnp.int32).reshape(2, HALF_LEN)
    return jax.vmap(one_sequence)(seq_keys).reshape(HALVES, HALF_LEN)


def levels(key, shape, cuts, low, high):
    def one(position, parts):
        heights = jax.random.uniform(jax.random.fold_in(jax.random.fold_in(key, 6), position), (parts,), jnp.float32, low / len(cuts), high / len(cuts))
        return jnp.repeat(jnp.exp(heights), shape[position] // parts).reshape((-1,) + (1,) * (len(shape) - position - 1))

    factor_of = one(*cuts[0])
    for cut in cuts[1:]:
        factor_of = factor_of * one(*cut)
    return factor_of


def noise(own_key, extent, spread, most, shards=(), kind=jnp.bfloat16):
    entries = jax.random.normal(own_key, extent, jnp.float32) * spread
    if len(shards) > 0:
        entries = levels(own_key, extent, shards, -0.22, 0.18) * entries
    return jnp.clip(entries, min=-most, max=most).astype(kind)


def setup_inputs(seed: int = 0) -> dict:
    key_of = jax.random.split(jax.random.key(seed), 13)
    tokens = noise(key_of[0], (HALVES, HALF_LEN, D), 1.0, 6.0, ((0, 4), (1, 8)))
    positions = draw_positions(jax.random.fold_in(key_of[12], 71), 0)
    first_gain = jnp.clip(1.0 + 0.1 * jax.random.normal(key_of[2], (D,), jnp.float32), 0.5, 1.5).astype(jnp.bfloat16)
    query_weight = noise(key_of[3], (D, QH * HD), D ** -0.5, 0.15625, ((0, 4),))
    key_weight = noise(key_of[4], (D, KVH * HD), D ** -0.5, 0.15625, ((0, 4),))
    value_weight = noise(key_of[5], (D, KVH * HD), D ** -0.5, 0.15625, ((0, 4),))
    output_weight = noise(key_of[6], (QH * HD, D), 1 ** -0.5, 6.0, ((0, 4),))
    second_gain = jnp.clip(1.0 + 0.1 * jax.random.normal(key_of[7], (D,), jnp.float32), 0.5, 1.5).astype(jnp.bfloat16)
    gate_weight = noise(key_of[8], (D, FF), D ** -0.5, 0.15625, ((0, 4),))
    up_weight = noise(key_of[9], (D, FF), D ** -0.5, 0.15625, ((0, 4),))
    down_weight = noise(key_of[10], (FF, D), FF ** -0.5, 0.09375, ((0, 4),))
    cotangent = noise(key_of[11], (HALVES, HALF_LEN, D), 1.0, 6.0, ((0, 4), (1, 8)))
    return dict(tokens=tokens, positions=positions, first_gain=first_gain, query_weight=query_weight, key_weight=key_weight, value_weight=value_weight, output_weight=output_weight, second_gain=second_gain, gate_weight=gate_weight, up_weight=up_weight, down_weight=down_weight, cotangent=cotangent)


THETA = 100000.0
EPS = 1e-05

@jax.custom_vjp
def low(v):
    return lax.optimization_barrier(v.astype(jnp.bfloat16)).astype(jnp.float32)

@jax.custom_vjp
def low_back(v):
    return v

def low_keep(v):
    return (low(v), None)

def low_pass(kept, grad):
    return (grad,)

def back_keep(v):
    return (v, None)

def back_low(kept, grad):
    return (low(grad),)
low.defvjp(low_keep, low_pass)
low_back.defvjp(back_keep, back_low)

def rope_tables(position_rows):
    freq = THETA ** (-(jnp.arange(HD // 2, dtype=jnp.float32) * 2.0 / HD))
    angle = position_rows.astype(jnp.float32)[:, None] * freq[None, :]
    cosine = jnp.cos(angle)
    sine = jnp.sin(angle)
    return (jnp.concatenate([cosine, cosine], -1), jnp.concatenate([sine, sine], -1))

def rotate(values, cosine, sine):
    half = HD // 2
    turned = jnp.concatenate([-values[..., half:], values[..., :half]], -1)
    return values * cosine[:, None, :] + turned * sine[:, None, :]

def rms_norm(rows, gain):
    scale = lax.rsqrt(lax.optimization_barrier(jnp.mean(rows * rows, -1, keepdims=True)) + EPS)
    return rows * scale * gain

def matmul(left, right):
    return jnp.dot(left, right, precision=lax.Precision.HIGHEST)

def attend_sequence(query_rows, key_rows, value_rows, start_rows):
    block = min(512, SEQ_LEN)
    count = SEQ_LEN // block
    group = QH // KVH
    key_index = jnp.arange(SEQ_LEN, dtype=jnp.int32)

    def one_block(items):
        query_block, start_block, first = items
        row_index = first + jnp.arange(block, dtype=jnp.int32)
        grouped = query_block.reshape(block, KVH, group, HD)
        scores = jnp.einsum('bkgd,tkd->kgbt', grouped, key_rows, precision=lax.Precision.HIGHEST) * HD ** (-0.5)
        scores = low_back(scores)
        visible = (key_index[None, :] >= start_block[:, None]) & (key_index[None, :] <= row_index[:, None])
        scores = jnp.where(visible, scores, -1e+30)
        top = lax.optimization_barrier(jnp.max(scores, -1, keepdims=True))
        expo = jnp.exp(scores - top)
        probs = low(expo / lax.optimization_barrier(jnp.sum(expo, -1, keepdims=True)))
        mixed = jnp.einsum('kgbt,tkd->bkgd', probs, value_rows, precision=lax.Precision.HIGHEST)
        return mixed.reshape(block, QH, HD)
    firsts = jnp.arange(count, dtype=jnp.int32) * block
    result = lax.map(jax.checkpoint(one_block), (query_rows.reshape(count, block, QH, HD), start_rows.reshape(count, block), firsts))
    return result.reshape(SEQ_LEN, QH, HD)

def reference(tokens, positions, first_gain, query_weight, key_weight, value_weight, output_weight, second_gain, gate_weight, up_weight, down_weight, cotangent):
    flat_positions = positions.reshape(-1)
    cosine, sine = rope_tables(flat_positions)
    starts = (jnp.arange(SEQ_LEN, dtype=jnp.int32)[None, :] - positions.reshape(SEQS, SEQ_LEN)).astype(jnp.int32)

    def forward(rows, gain_one, wq_full, wk_full, wv_full, wo_full, gain_two, wg_full, wu_full, wd_full):
        normed = low(rms_norm(rows, gain_one))
        query_lin = low_back(matmul(normed, wq_full)).reshape(-1, QH, HD)
        key_lin = low_back(matmul(normed, wk_full)).reshape(-1, KVH, HD)
        value_lin = low_back(matmul(normed, wv_full)).reshape(-1, KVH, HD)
        query_rows = low(rotate(query_lin, cosine, sine))
        key_rows = low(rotate(key_lin, cosine, sine))
        value_rows = low(value_lin)

        def per_sequence(items):
            return attend_sequence(items[0], items[1], items[2], items[3])
        attended = lax.map(per_sequence, (query_rows.reshape(SEQS, SEQ_LEN, QH, HD), key_rows.reshape(SEQS, SEQ_LEN, KVH, HD), value_rows.reshape(SEQS, SEQ_LEN, KVH, HD), starts))
        heads = low(low_back(attended.reshape(-1, QH * HD)))
        middle = rows + low_back(matmul(heads, wo_full))
        normed_two = low(rms_norm(middle, gain_two))
        gate = low_back(matmul(normed_two, wg_full))
        upper = low_back(matmul(normed_two, wu_full))
        hidden = low(jax.nn.silu(gate) * upper)
        return middle + matmul(hidden, wd_full)
    inputs = (tokens.reshape(-1, D).astype(jnp.float32), first_gain.astype(jnp.float32), query_weight.astype(jnp.float32), key_weight.astype(jnp.float32), value_weight.astype(jnp.float32), output_weight.astype(jnp.float32), second_gain.astype(jnp.float32), gate_weight.astype(jnp.float32), up_weight.astype(jnp.float32), down_weight.astype(jnp.float32))
    result, pullback = jax.vjp(forward, *inputs)
    grads = pullback(cotangent.reshape(-1, D).astype(jnp.float32))
    block_output = result.astype(jnp.bfloat16).reshape(HALVES, HALF_LEN, D)
    input_grad = grads[0].astype(jnp.bfloat16).reshape(HALVES, HALF_LEN, D)
    return (block_output, input_grad, grads[1], grads[2], grads[3], grads[4], grads[5], grads[6], grads[7], grads[8], grads[9])
```

```python
import functools
import math

import jax
import jax.numpy as jnp
from jax import lax
from jax.experimental import pallas as pl
from jax.experimental.pallas import tpu as pltpu
from jax.sharding import Mesh
from jax.sharding import PartitionSpec as P

QH = 16
KVH = 8
HD = 96


THETA = 100000.0
EPS = 1e-05
LOW = jnp.bfloat16
F32 = jnp.float32
NEG = -1e30
LN2 = math.log(2.0)


def contract(left, right, left_axis, right_axis):
    return lax.dot_general(
        left, right, (((left_axis,), (right_axis,)), ((), ())), preferred_element_type=F32
    )


def visible(first, second, query_block, key_block, size):
    key = key_block * size + lax.broadcasted_iota(jnp.int32, (size, size), 0)
    query = query_block * size + lax.broadcasted_iota(jnp.int32, (1, size), 1)
    start = jnp.where(query >= second, second, jnp.where(query >= first, first, 0))
    return (key >= start) & (key <= query)


def forward_kernel(
    scalars,
    own_ref,
    other_ref,
    low_ref,
    full_ref,
    log_ref,
    query_s,
    key_s,
    value_s,
    top_s,
    total_s,
    mixed_s,
    *,
    size,
    count,
):
    half = scalars[0]
    first = scalars[1]
    second = scalars[2]
    here = pl.program_id(0)
    per_half = count // 2

    @pl.when(here == 0)
    def _():
        for ref, side in ((own_ref, half), (other_ref, 1 - half)):
            for step in range(per_half):
                block = side * per_half + step
                columns = slice(step * size, (step + 1) * size)
                query_s[block] = ref[0:HD, columns]
                key_s[block] = ref[HD : 2 * HD, columns].T
                value_s[block] = ref[2 * HD : 3 * HD, columns]

    query = query_s[here]
    top_s[...] = jnp.full_like(top_s, NEG)
    total_s[...] = jnp.zeros_like(total_s)
    mixed_s[...] = jnp.zeros_like(mixed_s)

    def add_block(block, masked):
        scores = contract(key_s[block], query, 1, 0)
        if masked:
            scores = jnp.where(visible(first, second, here, block, size), scores, NEG)
        old_top = top_s[...]
        top = jnp.maximum(old_top, jnp.max(scores, 0, keepdims=True))
        expo = jnp.exp2(scores - top)
        scale = jnp.exp2(old_top - top)
        top_s[...] = top
        total_s[...] = total_s[...] * scale + jnp.sum(expo, 0, keepdims=True)
        mixed_s[...] = mixed_s[...] * scale + contract(value_s[block], expo.astype(LOW), 1, 0)

    last = count - 1

    @pl.loop(1, jnp.where(here == last, 1, here))
    def _(block):
        add_block(block, False)

    @pl.loop(0, jnp.where(here == last, count, jnp.minimum(here + 1, 2)))
    def _(step):
        add_block(jnp.where(here == last, step, step * here), True)

    total = total_s[...]
    result = mixed_s[...] / total
    full_ref[0] = result
    low_ref[0] = result.astype(LOW)
    log_ref[0] = top_s[...] + jnp.log2(total)


def backward_kernel(
    scalars,
    own_ref,
    other_ref,
    grad_ref,
    full_ref,
    log_ref,
    out_ref,
    query_s,
    key_s,
    value_s,
    delta_s,
    query_grad_s,
    key_grad_s,
    value_grad_s,
    *,
    size,
    count,
):
    half = scalars[0]
    first = scalars[1]
    second = scalars[2]
    here = pl.program_id(0)
    per_half = count // 2

    def slot_of(block):
        return (block % per_half) * 2 + block // per_half

    @pl.when(here == 0)
    def _():
        for ref, side in ((own_ref, half), (other_ref, 1 - half)):
            for step in range(per_half):
                block = side * per_half + step
                columns = slice(step * size, (step + 1) * size)
                query_s[block] = ref[0:HD, columns]
                key_s[block] = ref[HD : 2 * HD, columns]
                value_s[block] = ref[2 * HD : 3 * HD, columns].T
        for block in range(count):
            delta_s[block] = jnp.sum(
                grad_ref[slot_of(block)].astype(F32) * full_ref[block], 0, keepdims=True
            )
        query_grad_s[...] = jnp.zeros_like(query_grad_s)

    key_grad_s[...] = jnp.zeros_like(key_grad_s)
    value_grad_s[...] = jnp.zeros_like(value_grad_s)
    key = key_s[here]
    key_rows = key.T
    value_rows = value_s[here]

    def add_block(block, masked):
        query = query_s[block]
        grad = grad_ref[slot_of(block)]
        scores = contract(key_rows, query, 1, 0)
        if masked:
            scores = jnp.where(visible(first, second, block, here, size), scores, NEG)
        probs = jnp.exp2(scores - log_ref[block])
        grad_probs = contract(value_rows, grad, 1, 0)
        grad_scores = (probs * (grad_probs - delta_s[block])).astype(LOW)
        value_grad_s[...] += contract(grad, probs.astype(LOW), 1, 1)
        key_grad_s[...] += contract(query, grad_scores, 1, 1)
        query_grad_s[block] += contract(key, grad_scores, 1, 0)

    last = count - 1

    @pl.loop(here + 1, jnp.where(here == 0, 1, last))
    def _(block):
        add_block(block, False)

    @pl.loop(0, jnp.where(here == 0, count, jnp.where(here == last, 1, 2)))
    def _(step):
        add_block(jnp.where(here == 0, step, jnp.where(step == 0, here, last)), True)

    side = here // per_half
    slot = jnp.where(side == half, 0, 1)
    columns = pl.ds(pl.multiple_of((here % per_half) * size, size), size)
    out_ref[slot, 0:HD, columns] = (query_grad_s[here] * HD**-0.5).astype(LOW)
    out_ref[slot, HD : 2 * HD, columns] = (key_grad_s[...] * LN2).astype(LOW)
    out_ref[slot, 2 * HD : 3 * HD, columns] = value_grad_s[...].astype(LOW)


def attend_forward(scalars, own, other, size):
    count = 2 * own.shape[1] // size
    whole = lambda shape: pl.BlockSpec(shape, lambda i, s: (0,) * len(shape))
    per_half = count // 2
    pairs = count * (count + 1) // 2
    return pl.pallas_call(
        functools.partial(forward_kernel, size=size, count=count),
        grid_spec=pltpu.PrefetchScalarGridSpec(
            num_scalar_prefetch=1,
            grid=(count,),
            in_specs=[whole(own.shape), whole(other.shape)],
            out_specs=[
                pl.BlockSpec(
                    (1, HD, size), lambda i, s: ((i % per_half) * 2 + i // per_half, 0, 0)
                ),
                pl.BlockSpec((1, HD, size), lambda i, s: (i, 0, 0)),
                pl.BlockSpec((1, 1, size), lambda i, s: (i, 0, 0)),
            ],
            scratch_shapes=[
                pltpu.VMEM((count, HD, size), LOW),
                pltpu.VMEM((count, size, HD), LOW),
                pltpu.VMEM((count, HD, size), LOW),
                pltpu.VMEM((1, size), F32),
                pltpu.VMEM((1, size), F32),
                pltpu.VMEM((HD, size), F32),
            ],
        ),
        out_shape=[
            jax.ShapeDtypeStruct((count, HD, size), LOW),
            jax.ShapeDtypeStruct((count, HD, size), F32),
            jax.ShapeDtypeStruct((count, 1, size), F32),
        ],
        compiler_params=pltpu.CompilerParams(
            dimension_semantics=("arbitrary",), vmem_limit_bytes=32 * 2**20
        ),
        cost_estimate=pl.CostEstimate(
            flops=pairs * size * size * HD * 4,
            bytes_accessed=10 * 2**20,
            transcendentals=pairs * size * size,
        ),
        name="attend_forward",
    )(scalars, own, other)


def attend_backward(scalars, own, other, grad, full, log_total, size):
    count = 2 * own.shape[1] // size
    whole = lambda shape: pl.BlockSpec(shape, lambda i, s: (0,) * len(shape))
    pairs = count * (count + 1) // 2
    out_shape = (2, 3 * HD, own.shape[1])
    return pl.pallas_call(
        functools.partial(backward_kernel, size=size, count=count),
        grid_spec=pltpu.PrefetchScalarGridSpec(
            num_scalar_prefetch=1,
            grid=(count,),
            in_specs=[
                whole(own.shape),
                whole(other.shape),
                whole(grad.shape),
                whole(full.shape),
                whole(log_total.shape),
            ],
            out_specs=whole(out_shape),
            scratch_shapes=[
                pltpu.VMEM((count, HD, size), LOW),
                pltpu.VMEM((count, HD, size), LOW),
                pltpu.VMEM((count, size, HD), LOW),
                pltpu.VMEM((count, 1, size), F32),
                pltpu.VMEM((count, HD, size), F32),
                pltpu.VMEM((HD, size), F32),
                pltpu.VMEM((HD, size), F32),
            ],
        ),
        out_shape=jax.ShapeDtypeStruct(out_shape, LOW),
        compiler_params=pltpu.CompilerParams(
            dimension_semantics=("arbitrary",), vmem_limit_bytes=32 * 2**20
        ),
        cost_estimate=pl.CostEstimate(
            flops=pairs * size * size * HD * 10,
            bytes_accessed=16 * 2**20,
            transcendentals=pairs * size * size,
        ),
        name="attend_backward",
    )(scalars, own, other, grad, full, log_total)


def swap(value, axis):
    return lax.ppermute(value, axis, [(0, 1), (1, 0)])


def line_sum(part, axis):
    place = lax.axis_index(axis)
    inner = (place == 1) | (place == 2)
    part = part + lax.ppermute(part, axis, [(0, 1), (3, 2)])
    part = part + lax.ppermute(part, axis, [(1, 2), (2, 1)])
    outer = lax.ppermute(part, axis, [(1, 0), (2, 3)])
    return jnp.where(inner, part, outer)


def in_order(core, own, other):
    return (jnp.where(core == 0, own, other), jnp.where(core == 0, other, own))


def turn(values, cosine, sine):
    half = HD // 2
    low, high = values[:, :half], values[:, half:]
    return jnp.concatenate([low * cosine - high * sine, high * cosine + low * sine], 1)


def turn_back(grads, cosine, sine):
    half = HD // 2
    low, high = grads[:, :half], grads[:, half:]
    return jnp.concatenate([low * cosine + high * sine, high * cosine - low * sine], 1)


def fast_body(
    tokens,
    positions,
    first_gain,
    query_weight,
    key_weight,
    value_weight,
    output_weight,
    second_gain,
    gate_weight,
    up_weight,
    down_weight,
    cotangent,
):
    seq = ("z", "c")
    fsdp = ("y", "x")
    z, core, half = lax.axis_index("z"), lax.axis_index("c"), lax.axis_index("x")
    lines = lax.axis_size("z")
    seq_count = 2 * lines
    shards = lax.axis_size("y") * 2
    spot = z * 2 + core
    rows = tokens[0]
    count, width = rows.shape
    chip_count = 2 * count
    half_len = count * seq_count
    seq_len = 2 * half_len
    block = chip_count

    begins = jnp.where(
        (spot == 0) & (half == 0),
        count - 1 - positions[0, count - 1],
        half * half_len + spot * count - positions[0, 0],
    )
    ends = begins + (seq_len - count)
    scalars = jnp.stack([half, begins, ends]).astype(jnp.int32)

    gain_one = first_gain.astype(F32)[:, None]
    gain_two = second_gain.astype(F32)[:, None]

    group = QH // KVH
    wide = group * HD
    take = functools.partial(lax.dynamic_slice_in_dim, axis=1)
    qkv_shard = (
        jnp.concatenate(
            [
                take(query_weight, spot * wide, wide),
                take(key_weight, spot * HD, HD),
                take(value_weight, spot * HD, HD),
            ],
            1,
        ).astype(F32)
        * gain_one
    ).astype(LOW)
    out_rows = output_weight.shape[0] // 2
    out_shard = lax.dynamic_slice_in_dim(output_weight, core * out_rows, out_rows, axis=0)
    hidden_rows = down_weight.shape[0] // 2
    down_shard = lax.dynamic_slice_in_dim(down_weight, core * hidden_rows, hidden_rows, axis=0)

    def core_columns(weight):
        parts = weight.reshape(weight.shape[0], shards, 2, hidden_rows)
        return lax.dynamic_index_in_dim(parts, core, axis=2, keepdims=False).reshape(
            weight.shape[0], shards * hidden_rows
        )

    gate_up_shard = (
        jnp.concatenate([core_columns(gate_weight), core_columns(up_weight)], 1).astype(F32)
        * gain_two
    ).astype(LOW)

    gather = lambda value, axes: lax.all_gather(value, axes, axis=0, tiled=True)
    qkv_w = gather(qkv_shard, fsdp)
    all_rows = gather(rows, seq)
    out_w = gather(out_shard, fsdp)
    gate_up_w = gather(gate_up_shard, fsdp)
    down_w = gather(down_shard, fsdp)
    hidden_width = down_w.shape[0]

    cot_first, cot_second = in_order(core, cotangent[0], swap(cotangent[0], "c"))
    chip_cot = jnp.concatenate([cot_first, cot_second], 0)

    place = half * half_len + jnp.arange(half_len, dtype=jnp.int32)
    start = jnp.where(place >= ends, ends, jnp.where(place >= begins, begins, 0))
    freq = THETA ** (-(jnp.arange(HD // 2, dtype=F32) * 2.0 / HD))
    angle = freq[:, None] * (place - start).astype(F32)[None, :]
    cosine, sine = jnp.cos(angle), jnp.sin(angle)
    rows_float = all_rows.astype(F32)
    scale_one = lax.rsqrt(jnp.mean(rows_float * rows_float, -1) + EPS)[None, :]
    qkv = contract(qkv_w, all_rows, 0, 1) * scale_one
    turned = turn(qkv[: wide + HD].reshape(group + 1, HD, half_len), cosine, sine)
    query_pair = turned[:group] * (HD**-0.5 / LN2)
    keys_values = jnp.concatenate([turned[group], qkv[wide + HD :]], 0).astype(LOW)
    mine = jnp.where(half == 0, query_pair[0], query_pair[1]).astype(LOW)
    theirs = jnp.where(half == 0, query_pair[1], query_pair[0]).astype(LOW)
    own = jnp.concatenate([mine, keys_values], 0)
    other = swap(jnp.concatenate([theirs, keys_values], 0), "x")

    head_low, head_full, log_total = attend_forward(scalars, own, other, block)
    exchange = lambda value: lax.all_to_all(
        value, ("z", "x"), split_axis=0, concat_axis=0, tiled=True
    )
    heads = exchange(head_low).reshape(QH // 2 * HD, chip_count)

    branch = contract(heads, out_w, 0, 0).astype(LOW)
    chip_rows = lax.dynamic_slice_in_dim(all_rows, z * chip_count, chip_count, axis=0)
    middle = chip_rows.astype(F32) + (branch.astype(F32) + swap(branch, "c").astype(F32))
    scale_two = lax.rsqrt(jnp.mean(middle * middle, -1, keepdims=True) + EPS)
    middle_low = middle.astype(LOW)
    gate_up = contract(middle_low, gate_up_w, 1, 0) * scale_two
    gate, upper = gate_up[:, :hidden_width], gate_up[:, hidden_width:]
    sigma = jax.nn.sigmoid(gate)
    silu = gate * sigma
    hidden = (silu * upper).astype(LOW)
    down_part = contract(hidden, down_w, 1, 0)
    mine_of = lambda value: lax.dynamic_slice_in_dim(value, core * count, count, axis=0)
    theirs_of = lambda value: lax.dynamic_slice_in_dim(value, (1 - core) * count, count, axis=0)
    block_output = (
        mine_of(middle)
        + mine_of(down_part)
        + swap(theirs_of(down_part).astype(LOW), "c").astype(F32)
    ).astype(LOW)[None]

    scatter = lambda value, axes: lax.psum_scatter(
        value.astype(LOW), axes, scatter_dimension=0, tiled=True
    )
    down_grad = scatter(contract(hidden, chip_cot, 0, 0), fsdp)
    grad_hidden = contract(chip_cot, down_w, 1, 1) * scale_two
    gate_low = (grad_hidden * upper * sigma * (1.0 + gate * (1.0 - sigma))).astype(LOW)
    upper_low = (grad_hidden * silu).astype(LOW)
    gate_upper_low = jnp.concatenate([gate_low, upper_low], 1)
    gate_up_grad = scatter(contract(middle_low, gate_upper_low, 0, 0), fsdp)
    grad_part = contract(gate_upper_low, gate_up_w, 1, 1).astype(LOW)
    grad_two = grad_part.astype(F32) + swap(grad_part, "c").astype(F32)
    grad_middle = (
        chip_cot.astype(F32)
        + grad_two
        - middle * (scale_two * scale_two * jnp.mean(grad_two * middle, -1, keepdims=True))
    )
    grad_branch = grad_middle.astype(LOW)
    output_grad = scatter(contract(heads, grad_branch, 1, 0), fsdp)
    grad_heads = contract(out_w, grad_branch, 1, 1).astype(LOW)
    grad_head = exchange(grad_heads.reshape(2 * lines, HD, chip_count))

    sides = attend_backward(scalars, own, other, grad_head, head_full, log_total, block)
    kept = sides[0].astype(F32)
    came = swap(sides[1], "x").astype(F32)
    first_query = jnp.where(half == 0, kept[:HD], came[:HD])
    second_query = jnp.where(half == 0, came[:HD], kept[:HD])
    grad_keys_values = kept[HD:] + came[HD:]
    turned_grads = turn_back(
        jnp.stack([first_query, second_query, grad_keys_values[:HD]]), cosine, sine
    )
    qkv_low = (
        jnp.concatenate(
            [turned_grads.reshape((group + 1) * HD, half_len), grad_keys_values[HD:]], 0
        )
        * scale_one
    ).astype(LOW)
    qkv_grad = scatter(contract(all_rows, qkv_low, 0, 1), fsdp)
    grad_one = scatter(contract(qkv_low, qkv_w, 0, 1), seq).astype(F32)
    own_rows = rows.astype(F32)
    own_scale = lax.rsqrt(jnp.mean(own_rows * own_rows, -1, keepdims=True) + EPS)
    input_grad = (
        mine_of(grad_middle)
        + grad_one
        - own_rows * (own_scale * own_scale * jnp.mean(grad_one * own_rows, -1, keepdims=True))
    ).astype(LOW)[None]

    def both_cores(value):
        return in_order(core, value, swap(value, "c"))

    down_both = jnp.concatenate(both_cores(line_sum(down_grad, "z")), 0).astype(F32)
    output_both = jnp.concatenate(both_cores(line_sum(output_grad, "z")), 0).astype(F32)
    gate_up_both = jnp.stack(
        [
            part.reshape(part.shape[0], 2, shards, hidden_rows)
            for part in both_cores(line_sum(gate_up_grad, "z"))
        ],
        3,
    )
    gate_up_both = gate_up_both.reshape(gate_up_both.shape[0], 2, -1).astype(F32)
    gate_grad, up_grad = gate_up_both[:, 0], gate_up_both[:, 1]
    second_gain_grad = jnp.sum(
        gate_grad * gate_weight.astype(F32) + up_grad * up_weight.astype(F32), 1
    )
    qkv_all = (
        lax.all_gather(qkv_grad, seq, axis=1, tiled=False).astype(F32)
    )
    query_grad = qkv_all[:, :, :wide].reshape(query_weight.shape)
    key_grad = qkv_all[:, :, wide : wide + HD].reshape(key_weight.shape)
    value_grad = qkv_all[:, :, wide + HD :].reshape(value_weight.shape)
    first_gain_grad = (
        jnp.sum(query_grad * query_weight.astype(F32), 1)
        + jnp.sum(key_grad * key_weight.astype(F32), 1)
        + jnp.sum(value_grad * value_weight.astype(F32), 1)
    )
    return (
        block_output,
        input_grad,
        first_gain_grad,
        query_grad * gain_one,
        key_grad * gain_one,
        value_grad * gain_one,
        output_both,
        second_gain_grad,
        gate_grad * gain_two,
        up_grad * gain_two,
        down_both,
    )


def fast_solution(mesh):
    seq_count, shard_count = mesh.devices.shape
    fine = Mesh(
        mesh.devices.reshape(seq_count // 2, 2, shard_count // 2, 2), ("z", "c", "y", "x")
    )
    seq, fsdp = ("z", "c"), ("y", "x")
    matrix = P(fsdp, None)
    return jax.shard_map(
        fast_body,
        mesh=fine,
        in_specs=(
            P(fsdp, seq, None),
            P(fsdp, seq),
            P(fsdp),
            matrix,
            matrix,
            matrix,
            matrix,
            P(fsdp),
            matrix,
            matrix,
            matrix,
            P(fsdp, seq, None),
        ),
        out_specs=(
            P(fsdp, seq, None),
            P(fsdp, seq, None),
            P(fsdp),
            matrix,
            matrix,
            matrix,
            matrix,
            P(fsdp),
            matrix,
            matrix,
            matrix,
        ),
        check_vma=False,
    )


def solution(mesh):
    shape = dict(mesh.shape)
    if shape["seq"] == KVH and shape["fsdp"] % 2 == 0:
        return fast_solution(mesh)
    return plain_solution(mesh)


def shifted(value, axis, steps):
    count = lax.axis_size(axis)
    first, last = (max(0, -steps), min(count, count - steps))
    return lax.ppermute(value, axis, [(source, source + steps) for source in range(first, last)])


def rope_tables(position_rows):
    freq = THETA ** (-(jnp.arange(HD // 2, dtype=jnp.float32) * 2.0 / HD))
    angle = position_rows.astype(jnp.float32)[:, None] * freq[None, :]
    cosine = jnp.cos(angle)
    sine = jnp.sin(angle)
    return (jnp.concatenate([cosine, cosine], -1), jnp.concatenate([sine, sine], -1))


def rotate(values, cosine, sine):
    half = HD // 2
    turned = jnp.concatenate([-values[..., half:], values[..., :half]], -1)
    return values * cosine[:, None, :] + turned * sine[:, None, :]


def rotate_back(grads, cosine, sine):
    half = HD // 2
    scaled = grads * sine[:, None, :]
    turned = jnp.concatenate([scaled[..., half:], -scaled[..., :half]], -1)
    return grads * cosine[:, None, :] + turned


def norm_forward(rows, gain):
    scale = lax.rsqrt(jnp.mean(rows * rows, -1, keepdims=True) + EPS)
    unit = rows * scale
    return (unit * gain, unit, scale)


def norm_backward(grad_out, unit, scale, gain):
    grad_unit = grad_out * gain
    gain_grad = jnp.sum(grad_out * unit, 0)
    grad_rows = scale * (grad_unit - unit * jnp.mean(grad_unit * unit, -1, keepdims=True))
    return (grad_rows, gain_grad)


def plain_body(
    tokens,
    positions,
    first_gain,
    query_weight,
    key_weight,
    value_weight,
    output_weight,
    second_gain,
    gate_weight,
    up_weight,
    down_weight,
    cotangent,
):
    seq_count = lax.axis_size("seq")
    local_rows = tokens[0]
    token_count = local_rows.shape[0]
    half_len = token_count * seq_count
    rows_float = local_rows.astype(jnp.float32)
    gain_one, wq_full, wk_full, wv_full, wo_full = (
        lax.all_gather(first_gain, "fsdp", axis=0, tiled=True),
        lax.all_gather(query_weight, "fsdp", axis=0, tiled=True),
        lax.all_gather(key_weight, "fsdp", axis=0, tiled=True),
        lax.all_gather(value_weight, "fsdp", axis=0, tiled=True),
        lax.all_gather(output_weight, "fsdp", axis=0, tiled=True),
    )
    gain_one = gain_one.astype(jnp.float32)
    normed_one, unit_one, scale_one = norm_forward(rows_float, gain_one)
    normed_low = normed_one.astype(jnp.bfloat16)
    cosine, sine = rope_tables(positions[0])
    query_lin = jnp.dot(normed_low, wq_full, preferred_element_type=jnp.float32).reshape(
        token_count, QH, HD
    )
    key_lin = jnp.dot(normed_low, wk_full, preferred_element_type=jnp.float32).reshape(
        token_count, KVH, HD
    )
    value_lin = jnp.dot(normed_low, wv_full, preferred_element_type=jnp.float32).reshape(
        token_count, KVH, HD
    )
    query_rows = rotate(query_lin, cosine, sine).astype(jnp.bfloat16)
    key_rows = rotate(key_lin, cosine, sine).astype(jnp.bfloat16)
    value_rows = value_lin.astype(jnp.bfloat16)
    repeat = max(1, seq_count // KVH)
    if repeat > 1:
        key_rows = jnp.repeat(key_rows, repeat, axis=1)
        value_rows = jnp.repeat(value_rows, repeat, axis=1)
    query_heads, key_heads, value_heads = (
        lax.all_to_all(query_rows, "seq", split_axis=1, concat_axis=0, tiled=True),
        lax.all_to_all(key_rows, "seq", split_axis=1, concat_axis=0, tiled=True),
        lax.all_to_all(value_rows, "seq", split_axis=1, concat_axis=0, tiled=True),
    )
    head_count = query_heads.shape[1]
    pair_count = key_heads.shape[1]
    group = head_count // pair_count
    half_positions = lax.all_gather(positions[0], "seq", axis=0, tiled=True)
    key_prior, value_prior = shifted((key_heads, value_heads), "fsdp", 1)
    key_all = jnp.concatenate([key_prior, key_heads], 0)
    value_all = jnp.concatenate([value_prior, value_heads], 0)
    half_index = lax.axis_index("fsdp") % 2
    key_index = (half_index - 1) * half_len + jnp.arange(2 * half_len, dtype=jnp.int32)
    row_index = half_index * half_len + jnp.arange(half_len, dtype=jnp.int32)
    row_start = row_index - half_positions
    block = min(512, half_len)
    count = half_len // block
    factor = HD ** (-0.5)
    query_blocks = query_heads.reshape(count, block, pair_count, group, HD)
    index_blocks = row_index.reshape(count, block)
    start_blocks = row_start.reshape(count, block)

    def block_scores(query_block, index_block, start_block):
        scores = (
            jnp.einsum("bkgd,tkd->kgbt", query_block, key_all, preferred_element_type=jnp.float32)
            * factor
        )
        visible = (key_index[None, :] >= start_block[:, None]) & (
            key_index[None, :] <= index_block[:, None]
        )
        return jnp.where(visible, scores, -1e30)

    def forward_block(items):
        query_block, index_block, start_block = items
        scores = block_scores(query_block, index_block, start_block)
        top = jnp.max(scores, -1, keepdims=True)
        expo = jnp.exp(scores - top)
        total = jnp.sum(expo, -1, keepdims=True)
        probs_low = (expo / total).astype(jnp.bfloat16)
        mixed = jnp.einsum(
            "kgbt,tkd->bkgd", probs_low, value_all, preferred_element_type=jnp.float32
        )
        return (mixed.reshape(block, head_count, HD).astype(jnp.bfloat16), top + jnp.log(total))

    head_blocks, log_totals = lax.map(forward_block, (query_blocks, index_blocks, start_blocks))
    head_out = head_blocks.reshape(half_len, head_count, HD)
    token_heads = lax.all_to_all(head_out, "seq", split_axis=0, concat_axis=1, tiled=True)
    heads_flat = token_heads.reshape(token_count, QH * HD)
    middle = rows_float + jnp.dot(heads_flat, wo_full, preferred_element_type=jnp.float32)
    gain_two, wg_full, wu_full, wd_full = (
        lax.all_gather(second_gain, "fsdp", axis=0, tiled=True),
        lax.all_gather(gate_weight, "fsdp", axis=0, tiled=True),
        lax.all_gather(up_weight, "fsdp", axis=0, tiled=True),
        lax.all_gather(down_weight, "fsdp", axis=0, tiled=True),
    )
    gain_two = gain_two.astype(jnp.float32)
    normed_two, unit_two, scale_two = norm_forward(middle, gain_two)
    normed_two_low = normed_two.astype(jnp.bfloat16)
    gate = jnp.dot(normed_two_low, wg_full, preferred_element_type=jnp.float32)
    upper = jnp.dot(normed_two_low, wu_full, preferred_element_type=jnp.float32)
    hidden = (jax.nn.silu(gate) * upper).astype(jnp.bfloat16)
    result = middle + jnp.dot(hidden, wd_full, preferred_element_type=jnp.float32)
    block_output = result.astype(jnp.bfloat16)[None]
    grad_low = cotangent[0]
    grad_rows = grad_low.astype(jnp.float32)
    down_grad = jnp.einsum("tf,td->fd", hidden, grad_low, preferred_element_type=jnp.float32)
    grad_hidden = jnp.einsum("td,fd->tf", grad_low, wd_full, preferred_element_type=jnp.float32)
    sigma = jax.nn.sigmoid(gate)
    gate_low = (grad_hidden * upper * sigma * (1.0 + gate * (1.0 - sigma))).astype(jnp.bfloat16)
    upper_low = (grad_hidden * gate * sigma).astype(jnp.bfloat16)
    gate_grad = jnp.einsum(
        "td,tf->df", normed_two_low, gate_low, preferred_element_type=jnp.float32
    )
    up_grad = jnp.einsum("td,tf->df", normed_two_low, upper_low, preferred_element_type=jnp.float32)
    grad_normed_two = jnp.einsum(
        "tf,df->td", gate_low, wg_full, preferred_element_type=jnp.float32
    ) + jnp.einsum("tf,df->td", upper_low, wu_full, preferred_element_type=jnp.float32)
    grad_middle_norm, second_gain_grad = norm_backward(
        grad_normed_two, unit_two, scale_two, gain_two
    )
    grad_middle = grad_rows + grad_middle_norm
    grad_branch = grad_middle.astype(jnp.bfloat16)
    output_grad = jnp.einsum(
        "tc,td->cd", heads_flat, grad_branch, preferred_element_type=jnp.float32
    )
    grad_heads = (
        jnp.einsum("td,cd->tc", grad_branch, wo_full, preferred_element_type=jnp.float32)
        .astype(jnp.bfloat16)
        .reshape(token_count, QH, HD)
    )
    grad_head_rows = lax.all_to_all(grad_heads, "seq", split_axis=1, concat_axis=0, tiled=True)
    grad_blocks = grad_head_rows.reshape(count, block, pair_count, group, HD)

    def backward_block(carry, items):
        key_acc, value_acc = carry
        query_block, index_block, start_block, grad_block, log_block = items
        scores = block_scores(query_block, index_block, start_block)
        probs = jnp.exp(scores - log_block)
        probs_low = probs.astype(jnp.bfloat16)
        grad_probs = jnp.einsum(
            "bkgd,tkd->kgbt", grad_block, value_all, preferred_element_type=jnp.float32
        )
        grad_scores = (
            probs * (grad_probs - jnp.sum(probs * grad_probs, -1, keepdims=True))
        ).astype(jnp.bfloat16)
        query_grad_block = (
            jnp.einsum("kgbt,tkd->bkgd", grad_scores, key_all, preferred_element_type=jnp.float32)
            * factor
        )
        key_acc = (
            key_acc
            + jnp.einsum(
                "kgbt,bkgd->tkd", grad_scores, query_block, preferred_element_type=jnp.float32
            )
            * factor
        )
        value_acc = value_acc + jnp.einsum(
            "kgbt,bkgd->tkd", probs_low, grad_block, preferred_element_type=jnp.float32
        )
        return ((key_acc, value_acc), query_grad_block.reshape(block, head_count, HD))

    empty = jnp.zeros((2 * half_len, pair_count, HD), jnp.float32)
    (key_acc, value_acc), query_grad_blocks = lax.scan(
        backward_block,
        (empty, empty),
        (query_blocks, index_blocks, start_blocks, grad_blocks, log_totals),
    )
    key_back, value_back = (
        shifted(key_acc[:half_len].astype(jnp.bfloat16), "fsdp", -1).astype(jnp.float32),
        shifted(value_acc[:half_len].astype(jnp.bfloat16), "fsdp", -1).astype(jnp.float32),
    )
    key_local = key_acc[half_len:] + key_back
    value_local = value_acc[half_len:] + value_back
    query_grad_heads = query_grad_blocks.reshape(half_len, head_count, HD)
    grad_query_tok, grad_key_tok, grad_value_tok = (
        lax.all_to_all(
            query_grad_heads.astype(jnp.bfloat16), "seq", split_axis=0, concat_axis=1, tiled=True
        ).astype(query_grad_heads.dtype),
        lax.all_to_all(
            key_local.astype(jnp.bfloat16), "seq", split_axis=0, concat_axis=1, tiled=True
        ).astype(key_local.dtype),
        lax.all_to_all(
            value_local.astype(jnp.bfloat16), "seq", split_axis=0, concat_axis=1, tiled=True
        ).astype(value_local.dtype),
    )
    if repeat > 1:
        grad_key_tok = grad_key_tok.reshape(token_count, KVH, repeat, HD).sum(2)
        grad_value_tok = grad_value_tok.reshape(token_count, KVH, repeat, HD).sum(2)
    query_lin_grad = (
        rotate_back(grad_query_tok, cosine, sine).astype(jnp.bfloat16).reshape(token_count, QH * HD)
    )
    key_lin_grad = (
        rotate_back(grad_key_tok, cosine, sine).astype(jnp.bfloat16).reshape(token_count, KVH * HD)
    )
    value_lin_grad = grad_value_tok.astype(jnp.bfloat16).reshape(token_count, KVH * HD)
    query_grad = jnp.einsum(
        "td,tc->dc", normed_low, query_lin_grad, preferred_element_type=jnp.float32
    )
    key_grad = jnp.einsum("td,tc->dc", normed_low, key_lin_grad, preferred_element_type=jnp.float32)
    value_grad = jnp.einsum(
        "td,tc->dc", normed_low, value_lin_grad, preferred_element_type=jnp.float32
    )
    grad_normed_one = jnp.einsum(
        "tc,dc->td", query_lin_grad, wq_full, preferred_element_type=jnp.float32
    )
    grad_normed_one = grad_normed_one + jnp.einsum(
        "tc,dc->td", key_lin_grad, wk_full, preferred_element_type=jnp.float32
    )
    grad_normed_one = grad_normed_one + jnp.einsum(
        "tc,dc->td", value_lin_grad, wv_full, preferred_element_type=jnp.float32
    )
    grad_rows_one, first_gain_grad = norm_backward(grad_normed_one, unit_one, scale_one, gain_one)
    input_grad = (grad_middle + grad_rows_one).astype(jnp.bfloat16)[None]
    pieces = (
        lax.psum_scatter(
            first_gain_grad.astype(jnp.bfloat16), "fsdp", scatter_dimension=0, tiled=True
        ).astype(jnp.float32),
        lax.psum_scatter(
            query_grad.astype(jnp.bfloat16), "fsdp", scatter_dimension=0, tiled=True
        ).astype(jnp.float32),
        lax.psum_scatter(
            key_grad.astype(jnp.bfloat16), "fsdp", scatter_dimension=0, tiled=True
        ).astype(jnp.float32),
        lax.psum_scatter(
            value_grad.astype(jnp.bfloat16), "fsdp", scatter_dimension=0, tiled=True
        ).astype(jnp.float32),
        lax.psum_scatter(
            output_grad.astype(jnp.bfloat16), "fsdp", scatter_dimension=0, tiled=True
        ).astype(jnp.float32),
        lax.psum_scatter(
            second_gain_grad.astype(jnp.bfloat16), "fsdp", scatter_dimension=0, tiled=True
        ).astype(jnp.float32),
        lax.psum_scatter(
            gate_grad.astype(jnp.bfloat16), "fsdp", scatter_dimension=0, tiled=True
        ).astype(jnp.float32),
        lax.psum_scatter(
            up_grad.astype(jnp.bfloat16), "fsdp", scatter_dimension=0, tiled=True
        ).astype(jnp.float32),
        lax.psum_scatter(
            down_grad.astype(jnp.bfloat16), "fsdp", scatter_dimension=0, tiled=True
        ).astype(jnp.float32),
    )
    shares = (
        lax.psum(pieces[0].astype(jnp.bfloat16), "seq").astype(jnp.float32),
        lax.psum(pieces[1].astype(jnp.bfloat16), "seq").astype(jnp.float32),
        lax.psum(pieces[2].astype(jnp.bfloat16), "seq").astype(jnp.float32),
        lax.psum(pieces[3].astype(jnp.bfloat16), "seq").astype(jnp.float32),
        lax.psum(pieces[4].astype(jnp.bfloat16), "seq").astype(jnp.float32),
        lax.psum(pieces[5].astype(jnp.bfloat16), "seq").astype(jnp.float32),
        lax.psum(pieces[6].astype(jnp.bfloat16), "seq").astype(jnp.float32),
        lax.psum(pieces[7].astype(jnp.bfloat16), "seq").astype(jnp.float32),
        lax.psum(pieces[8].astype(jnp.bfloat16), "seq").astype(jnp.float32),
    )
    return (
        block_output,
        input_grad,
        shares[0],
        shares[1],
        shares[2],
        shares[3],
        shares[4],
        shares[5],
        shares[6],
        shares[7],
        shares[8],
    )


def plain_solution(mesh):
    placed = (
        P("fsdp", "seq", None),
        P("fsdp", "seq"),
        P("fsdp"),
        P("fsdp", None),
        P("fsdp", None),
        P("fsdp", None),
        P("fsdp", None),
        P("fsdp"),
        P("fsdp", None),
        P("fsdp", None),
        P("fsdp", None),
        P("fsdp", "seq", None),
    )
    return jax.shard_map(
        plain_body,
        mesh=mesh,
        in_specs=placed,
        out_specs=(
            P("fsdp", "seq", None),
            P("fsdp", "seq", None),
            P("fsdp"),
            P("fsdp", None),
            P("fsdp", None),
            P("fsdp", None),
            P("fsdp", None),
            P("fsdp"),
            P("fsdp", None),
            P("fsdp", None),
            P("fsdp", None),
        ),
        check_vma=False,
    )
```

```python
import functools
import math

import jax
import jax.numpy as jnp
from jax import lax
from jax.experimental import pallas as pl
from jax.experimental.pallas import tpu as pltpu
from jax.sharding import Mesh
from jax.sharding import PartitionSpec as P

QH = 16
KVH = 8
HD = 96


THETA = 100000.0
EPS = 1e-05
LOW = jnp.bfloat16
F32 = jnp.float32
NEG = -1e30
LN2 = math.log(2.0)


def contract(left, right, left_axis, right_axis):
    return lax.dot_general(
        left, right, (((left_axis,), (right_axis,)), ((), ())), preferred_element_type=F32
    )


def visible(first, second, query_block, key_block, size):
    key = key_block * size + lax.broadcasted_iota(jnp.int32, (size, size), 0)
    query = query_block * size + lax.broadcasted_iota(jnp.int32, (1, size), 1)
    start = jnp.where(query >= second, second, jnp.where(query >= first, first, 0))
    return (key >= start) & (key <= query)


def forward_kernel(
    scalars,
    own_ref,
    other_ref,
    low_ref,
    full_ref,
    log_ref,
    query_s,
    key_s,
    value_s,
    top_s,
    total_s,
    mixed_s,
    *,
    size,
    count,
):
    half = scalars[0]
    first = scalars[1]
    second = scalars[2]
    here = pl.program_id(0)
    per_half = count // 2

    @pl.when(here == 0)
    def _():
        for ref, side in ((own_ref, half), (other_ref, 1 - half)):
            for step in range(per_half):
                block = side * per_half + step
                columns = slice(step * size, (step + 1) * size)
                query_s[block] = ref[0:HD, columns]
                key_s[block] = ref[HD : 2 * HD, columns].T
                value_s[block] = ref[2 * HD : 3 * HD, columns]

    query = query_s[here]
    top_s[...] = jnp.full_like(top_s, NEG)
    total_s[...] = jnp.zeros_like(total_s)
    mixed_s[...] = jnp.zeros_like(mixed_s)

    def add_block(block, masked):
        scores = contract(key_s[block], query, 1, 0)
        if masked:
            scores = jnp.where(visible(first, second, here, block, size), scores, NEG)
        old_top = top_s[...]
        top = jnp.maximum(old_top, jnp.max(scores, 0, keepdims=True))
        expo = jnp.exp2(scores - top)
        scale = jnp.exp2(old_top - top)
        top_s[...] = top
        total_s[...] = total_s[...] * scale + jnp.sum(expo, 0, keepdims=True)
        mixed_s[...] = mixed_s[...] * scale + contract(value_s[block], expo.astype(LOW), 1, 0)

    last = count - 1

    @pl.loop(1, jnp.where(here == last, 1, here))
    def _(block):
        add_block(block, False)

    @pl.loop(0, jnp.where(here == last, count, jnp.minimum(here + 1, 2)))
    def _(step):
        add_block(jnp.where(here == last, step, step * here), True)

    total = total_s[...]
    result = mixed_s[...] / total
    full_ref[0] = result
    low_ref[0] = result.astype(LOW)
    log_ref[0] = top_s[...] + jnp.log2(total)


def backward_kernel(
    scalars,
    own_ref,
    other_ref,
    grad_ref,
    full_ref,
    log_ref,
    out_ref,
    query_s,
    key_s,
    value_s,
    delta_s,
    query_grad_s,
    key_grad_s,
    value_grad_s,
    *,
    size,
    count,
):
    half = scalars[0]
    first = scalars[1]
    second = scalars[2]
    here = pl.program_id(0)
    per_half = count // 2

    def slot_of(block):
        return (block % per_half) * 2 + block // per_half

    @pl.when(here == 0)
    def _():
        for ref, side in ((own_ref, half), (other_ref, 1 - half)):
            for step in range(per_half):
                block = side * per_half + step
                columns = slice(step * size, (step + 1) * size)
                query_s[block] = ref[0:HD, columns]
                key_s[block] = ref[HD : 2 * HD, columns]
                value_s[block] = ref[2 * HD : 3 * HD, columns].T
        for block in range(count):
            delta_s[block] = jnp.sum(
                grad_ref[slot_of(block)].astype(F32) * full_ref[block], 0, keepdims=True
            )
        query_grad_s[...] = jnp.zeros_like(query_grad_s)

    key_grad_s[...] = jnp.zeros_like(key_grad_s)
    value_grad_s[...] = jnp.zeros_like(value_grad_s)
    key = key_s[here]
    key_rows = key.T
    value_rows = value_s[here]

    def add_block(block, masked):
        query = query_s[block]
        grad = grad_ref[slot_of(block)]
        scores = contract(key_rows, query, 1, 0)
        if masked:
            scores = jnp.where(visible(first, second, block, here, size), scores, NEG)
        probs = jnp.exp2(scores - log_ref[block])
        grad_probs = contract(value_rows, grad, 1, 0)
        grad_scores = (probs * (grad_probs - delta_s[block])).astype(LOW)
        value_grad_s[...] += contract(grad, probs.astype(LOW), 1, 1)
        key_grad_s[...] += contract(query, grad_scores, 1, 1)
        query_grad_s[block] += contract(key, grad_scores, 1, 0)

    last = count - 1

    @pl.loop(here + 1, jnp.where(here == 0, 1, last))
    def _(block):
        add_block(block, False)

    @pl.loop(0, jnp.where(here == 0, count, jnp.where(here == last, 1, 2)))
    def _(step):
        add_block(jnp.where(here == 0, step, jnp.where(step == 0, here, last)), True)

    side = here // per_half
    slot = jnp.where(side == half, 0, 1)
    columns = pl.ds(pl.multiple_of((here % per_half) * size, size), size)
    out_ref[slot, 0:HD, columns] = (query_grad_s[here] * HD**-0.5).astype(LOW)
    out_ref[slot, HD : 2 * HD, columns] = (key_grad_s[...] * LN2).astype(LOW)
    out_ref[slot, 2 * HD : 3 * HD, columns] = value_grad_s[...].astype(LOW)


def attend_forward(scalars, own, other, size):
    count = 2 * own.shape[1] // size
    whole = lambda shape: pl.BlockSpec(shape, lambda i, s: (0,) * len(shape))
    per_half = count // 2
    pairs = count * (count + 1) // 2
    return pl.pallas_call(
        functools.partial(forward_kernel, size=size, count=count),
        grid_spec=pltpu.PrefetchScalarGridSpec(
            num_scalar_prefetch=1,
            grid=(count,),
            in_specs=[whole(own.shape), whole(other.shape)],
            out_specs=[
                pl.BlockSpec(
                    (1, HD, size), lambda i, s: ((i % per_half) * 2 + i // per_half, 0, 0)
                ),
                pl.BlockSpec((1, HD, size), lambda i, s: (i, 0, 0)),
                pl.BlockSpec((1, 1, size), lambda i, s: (i, 0, 0)),
            ],
            scratch_shapes=[
                pltpu.VMEM((count, HD, size), LOW),
                pltpu.VMEM((count, size, HD), LOW),
                pltpu.VMEM((count, HD, size), LOW),
                pltpu.VMEM((1, size), F32),
                pltpu.VMEM((1, size), F32),
                pltpu.VMEM((HD, size), F32),
            ],
        ),
        out_shape=[
            jax.ShapeDtypeStruct((count, HD, size), LOW),
            jax.ShapeDtypeStruct((count, HD, size), F32),
            jax.ShapeDtypeStruct((count, 1, size), F32),
        ],
        compiler_params=pltpu.CompilerParams(
            dimension_semantics=("arbitrary",), vmem_limit_bytes=32 * 2**20
        ),
        cost_estimate=pl.CostEstimate(
            flops=pairs * size * size * HD * 4,
            bytes_accessed=10 * 2**20,
            transcendentals=pairs * size * size,
        ),
        name="attend_forward",
    )(scalars, own, other)


def attend_backward(scalars, own, other, grad, full, log_total, size):
    count = 2 * own.shape[1] // size
    whole = lambda shape: pl.BlockSpec(shape, lambda i, s: (0,) * len(shape))
    pairs = count * (count + 1) // 2
    out_shape = (2, 3 * HD, own.shape[1])
    return pl.pallas_call(
        functools.partial(backward_kernel, size=size, count=count),
        grid_spec=pltpu.PrefetchScalarGridSpec(
            num_scalar_prefetch=1,
            grid=(count,),
            in_specs=[
                whole(own.shape),
                whole(other.shape),
                whole(grad.shape),
                whole(full.shape),
                whole(log_total.shape),
            ],
            out_specs=whole(out_shape),
            scratch_shapes=[
                pltpu.VMEM((count, HD, size), LOW),
                pltpu.VMEM((count, HD, size), LOW),
                pltpu.VMEM((count, size, HD), LOW),
                pltpu.VMEM((count, 1, size), F32),
                pltpu.VMEM((count, HD, size), F32),
                pltpu.VMEM((HD, size), F32),
                pltpu.VMEM((HD, size), F32),
            ],
        ),
        out_shape=jax.ShapeDtypeStruct(out_shape, LOW),
        compiler_params=pltpu.CompilerParams(
            dimension_semantics=("arbitrary",), vmem_limit_bytes=32 * 2**20
        ),
        cost_estimate=pl.CostEstimate(
            flops=pairs * size * size * HD * 10,
            bytes_accessed=16 * 2**20,
            transcendentals=pairs * size * size,
        ),
        name="attend_backward",
    )(scalars, own, other, grad, full, log_total)


def place_rows_kernel(order, *refs):
    pieces, out_ref = refs[:-1], refs[-1]
    size = pieces[0].shape[0]
    for index, piece in enumerate(pieces):
        start = pl.multiple_of(order[index] * size, size)
        out_ref[pl.ds(start, size), :] = piece[...].astype(F32)


def place_rows(order, pieces):
    size, width = pieces[0].shape
    total = size * len(pieces)
    step = 512
    return pl.pallas_call(
        place_rows_kernel,
        grid_spec=pltpu.PrefetchScalarGridSpec(
            num_scalar_prefetch=1,
            grid=(width // step,),
            in_specs=[pl.BlockSpec((size, step), lambda i, s: (0, i)) for _ in pieces],
            out_specs=pl.BlockSpec((total, step), lambda i, s: (0, i)),
        ),
        out_shape=jax.ShapeDtypeStruct((total, width), F32),
        compiler_params=pltpu.CompilerParams(vmem_limit_bytes=24 * 2**20),
        cost_estimate=pl.CostEstimate(
            flops=0, bytes_accessed=total * width * 6, transcendentals=0
        ),
        name="place_rows",
    )(order, *pieces)


def place_columns_kernel(order, gain_ref, gate_w_ref, up_w_ref, *refs):
    count = (len(refs) - 3) // 2
    gates, ups = refs[:count], refs[count : 2 * count]
    gate_ref, up_ref, sum_ref = refs[2 * count :]
    size = gates[0].shape[1]
    gain = gain_ref[...]
    total = jnp.zeros((gate_ref.shape[0], size), F32)
    for index in range(count):
        columns = pl.ds(pl.multiple_of(order[index] * size, size), size)
        gate, up = gates[index][...].astype(F32), ups[index][...].astype(F32)
        total += gate * gate_w_ref[:, columns].astype(F32)
        total += up * up_w_ref[:, columns].astype(F32)
        gate_ref[:, columns] = gate * gain
        up_ref[:, columns] = up * gain

    @pl.when(pl.program_id(0) == 0)
    def _():
        sum_ref[...] = jnp.zeros_like(sum_ref)

    sum_ref[...] += jnp.sum(total, 1, keepdims=True)


def place_columns(order, gain, gate_weight, up_weight, pieces, shards):
    rows, width = gate_weight.shape
    span = width // shards
    size = span // len(pieces)
    wide = pl.BlockSpec((rows, span), lambda i, s: (0, i))
    thin = pl.BlockSpec((rows, 1), lambda i, s: (0, 0))
    gates = [pl.BlockSpec((rows, size), lambda i, s: (0, i)) for _ in pieces]
    ups = [pl.BlockSpec((rows, size), lambda i, s: (0, i + shards)) for _ in pieces]
    return pl.pallas_call(
        place_columns_kernel,
        grid_spec=pltpu.PrefetchScalarGridSpec(
            num_scalar_prefetch=1,
            grid=(shards,),
            in_specs=[thin, wide, wide, *gates, *ups],
            out_specs=[wide, wide, thin],
        ),
        out_shape=[
            jax.ShapeDtypeStruct((rows, width), F32),
            jax.ShapeDtypeStruct((rows, width), F32),
            jax.ShapeDtypeStruct((rows, 1), F32),
        ],
        compiler_params=pltpu.CompilerParams(
            dimension_semantics=("arbitrary",), vmem_limit_bytes=24 * 2**20
        ),
        cost_estimate=pl.CostEstimate(
            flops=rows * width * 6, bytes_accessed=rows * width * 16, transcendentals=0
        ),
        name="place_columns",
    )(order, gain, gate_weight, up_weight, *pieces, *pieces)


def swap(value, axis):
    return lax.ppermute(value, axis, [(0, 1), (1, 0)])


def swap_near(value):
    return lax.ppermute(value, "z", [(0, 1), (1, 0), (2, 3), (3, 2)])


def swap_far(value):
    return lax.ppermute(value, "z", [(0, 2), (2, 0), (1, 3), (3, 1)])


def line_sum(part, axis):
    place = lax.axis_index(axis)
    inner = (place == 1) | (place == 2)
    part = part + lax.ppermute(part, axis, [(0, 1), (3, 2)])
    part = part + lax.ppermute(part, axis, [(1, 2), (2, 1)])
    outer = lax.ppermute(part, axis, [(1, 0), (2, 3)])
    return jnp.where(inner, part, outer)


def line_scatter(parts, axis):
    place = lax.axis_index(axis)
    block = lambda at: lax.dynamic_index_in_dim(parts, jnp.clip(at, 0, 3), 0, keepdims=False)
    up, down = block(place + 3), block(place - 3)
    for step in (2, 1):
        up = lax.ppermute(up, axis, [(i, i + 1) for i in range(3 - step)])
        down = lax.ppermute(down, axis, [(3 - i, 2 - i) for i in range(3 - step)])
        up = (up.astype(F32) + block(place + step)).astype(LOW)
        down = (down.astype(F32) + block(place - step)).astype(LOW)
    up = lax.ppermute(up, axis, [(0, 1), (1, 2), (2, 3)])
    down = lax.ppermute(down, axis, [(3, 2), (2, 1), (1, 0)])
    return block(place).astype(F32) + up.astype(F32) + down.astype(F32)


def in_order(place, own, other):
    return (jnp.where(place == 0, own, other), jnp.where(place == 0, other, own))


def both(place, own, other):
    return jnp.concatenate(in_order(place, own, other), 0)


def turn(values, cosine, sine):
    half = HD // 2
    low, high = values[:, :half], values[:, half:]
    return jnp.concatenate([low * cosine - high * sine, high * cosine + low * sine], 1)


def turn_back(grads, cosine, sine):
    half = HD // 2
    low, high = grads[:, :half], grads[:, half:]
    return jnp.concatenate([low * cosine + high * sine, high * cosine - low * sine], 1)


def fast_body(
    tokens,
    positions,
    first_gain,
    query_weight,
    key_weight,
    value_weight,
    output_weight,
    second_gain,
    gate_weight,
    up_weight,
    down_weight,
    cotangent,
):
    seq = ("z", "c")
    fsdp = ("y", "x")
    z, core, half = lax.axis_index("z"), lax.axis_index("c"), lax.axis_index("x")
    near = z % 2
    lines = lax.axis_size("z")
    seq_count = 2 * lines
    shards = lax.axis_size("y") * 2
    spot = z * 2 + core
    quarter = near * 2 + core
    rows = tokens[0]
    count, width = rows.shape
    chip_count = 2 * count
    half_len = count * seq_count
    seq_len = 2 * half_len
    block = chip_count

    begins = jnp.where(
        (spot == 0) & (half == 0),
        count - 1 - positions[0, count - 1],
        half * half_len + spot * count - positions[0, 0],
    )
    ends = begins + (seq_len - count)
    scalars = jnp.stack([half, begins, ends]).astype(jnp.int32)

    gain_one = first_gain.astype(F32)[:, None]
    gain_two = second_gain.astype(F32)[:, None]

    group = QH // KVH
    wide = group * HD
    take = functools.partial(lax.dynamic_slice_in_dim, axis=1)
    take_rows = functools.partial(lax.dynamic_slice_in_dim, axis=0)
    qkv_shard = (
        jnp.concatenate(
            [
                take(query_weight, spot * wide, wide),
                take(key_weight, spot * HD, HD),
                take(value_weight, spot * HD, HD),
            ],
            1,
        ).astype(F32)
        * gain_one
    ).astype(LOW)
    out_rows = output_weight.shape[0] // 2
    out_shard = take_rows(output_weight, core * out_rows, out_rows)
    piece = down_weight.shape[0] // 4
    down_shard = take_rows(down_weight, quarter * piece, piece)
    gate_up_shard = (
        jnp.concatenate(
            [
                take(weight, shard * 4 * piece + quarter * piece, piece)
                for weight in (gate_weight, up_weight)
                for shard in range(shards)
            ],
            1,
        ).astype(F32)
        * gain_two
    ).astype(LOW)

    gather = lambda value, axes: lax.all_gather(value, axes, axis=0, tiled=True)
    all_rows = gather(rows, seq)
    qkv_pair = both(half, qkv_shard, swap(qkv_shard, "x"))
    qkv_w = both(lax.axis_index("y"), qkv_pair, swap(qkv_pair, "y"))
    out_w = gather(out_shard, fsdp)
    gate_up_w = gather(gate_up_shard, fsdp)
    down_w = gather(down_shard, fsdp)
    hidden_width = down_w.shape[0]

    chip_cot = both(core, cotangent[0], swap(cotangent[0], "c"))
    near_cot = swap_near(cotangent[0])
    near_cot = jnp.concatenate([near_cot, swap(near_cot, "c")], 0)
    all_cot = jnp.concatenate([chip_cot, near_cot], 0)

    place = half * half_len + jnp.arange(half_len, dtype=jnp.int32)
    start = jnp.where(place >= ends, ends, jnp.where(place >= begins, begins, 0))
    freq = THETA ** (-(jnp.arange(HD // 2, dtype=F32) * 2.0 / HD))
    angle = freq[:, None] * (place - start).astype(F32)[None, :]
    cosine, sine = jnp.cos(angle), jnp.sin(angle)
    rows_float = all_rows.astype(F32)
    scale_one = lax.rsqrt(jnp.mean(rows_float * rows_float, -1) + EPS)[None, :]
    qkv = contract(qkv_w, all_rows, 0, 1) * scale_one
    turned = turn(qkv[: wide + HD].reshape(group + 1, HD, half_len), cosine, sine)
    query_pair = turned[:group] * (HD**-0.5 / LN2)
    keys_values = jnp.concatenate([turned[group], qkv[wide + HD :]], 0).astype(LOW)
    mine = jnp.where(half == 0, query_pair[0], query_pair[1]).astype(LOW)
    theirs = jnp.where(half == 0, query_pair[1], query_pair[0]).astype(LOW)
    own = jnp.concatenate([mine, keys_values], 0)
    other = swap(jnp.concatenate([theirs, keys_values], 0), "x")

    head_low, head_full, log_total = attend_forward(scalars, own, other, block)
    exchange = lambda value: lax.all_to_all(
        value, ("z", "x"), split_axis=0, concat_axis=0, tiled=True
    )
    heads = exchange(head_low).reshape(QH // 2 * HD, chip_count)

    mine_of = lambda value: take_rows(value, core * count, count)
    theirs_of = lambda value: take_rows(value, (1 - core) * count, count)
    branch = contract(heads, out_w, 0, 0).astype(LOW)
    chip_rows = take_rows(all_rows, z * chip_count, chip_count)
    middle = chip_rows.astype(F32) + (branch.astype(F32) + swap(branch, "c").astype(F32))
    own_middle = mine_of(middle)
    middle_low = middle.astype(LOW)
    near_middle = swap_near(mine_of(middle_low))
    near_middle = jnp.concatenate([near_middle, swap(near_middle, "c")], 0)

    def row_scale(value):
        return lax.rsqrt(jnp.mean(value * value, -1, keepdims=True) + EPS)

    def feed(low, scale, cot):
        gate_up = contract(low, gate_up_w, 1, 0) * scale
        gate, upper = gate_up[:, :hidden_width], gate_up[:, hidden_width:]
        sigma = jax.nn.sigmoid(gate)
        silu = gate * sigma
        hidden = (silu * upper).astype(LOW)
        grad_hidden = contract(cot, down_w, 1, 1) * scale
        gate_low = (grad_hidden * upper * sigma * (1.0 + gate * (1.0 - sigma))).astype(LOW)
        upper_low = (grad_hidden * silu).astype(LOW)
        return hidden, jnp.concatenate([gate_low, upper_low], 1)

    chip_scale = row_scale(middle)
    near_scale = row_scale(near_middle.astype(F32))
    chip_hidden, chip_grads = feed(middle_low, chip_scale, chip_cot)
    near_hidden, near_grads = feed(near_middle, near_scale, near_cot)

    def own_sum(chip_part, near_part):
        near_sum = near_part[:count].astype(F32) + swap(near_part[count:].astype(LOW), "c")
        came = swap_near(near_sum.astype(LOW))
        chip_sum = mine_of(chip_part).astype(F32) + swap(theirs_of(chip_part).astype(LOW), "c")
        return chip_sum + came.astype(F32)

    grad_two = own_sum(
        contract(chip_grads, gate_up_w, 1, 1), contract(near_grads, gate_up_w, 1, 1)
    )
    own_scale = mine_of(chip_scale)
    grad_middle = (
        cotangent[0].astype(F32)
        + grad_two
        - own_middle * (own_scale * own_scale * jnp.mean(grad_two * own_middle, -1, keepdims=True))
    )
    own_branch = grad_middle.astype(LOW)
    grad_branch = both(core, own_branch, swap(own_branch, "c"))
    grad_heads = contract(out_w, grad_branch, 1, 1).astype(LOW)

    all_middle = jnp.concatenate([middle_low, near_middle], 0)
    all_hidden = jnp.concatenate([chip_hidden, near_hidden], 0)
    all_grads = jnp.concatenate([chip_grads, near_grads], 0)
    down_part = contract(all_hidden, all_cot, 0, 0).astype(LOW)
    gate_up_part = contract(all_middle, all_grads, 0, 0).astype(LOW)
    output_part = contract(heads, grad_branch, 1, 0).astype(LOW)
    grad_heads, down_part, gate_up_part, output_part = lax.optimization_barrier(
        (grad_heads, down_part, gate_up_part, output_part)
    )

    scatter = lambda value, axes: lax.psum_scatter(
        value.astype(LOW), axes, scatter_dimension=0, tiled=True
    )
    down_grad = scatter(down_part, fsdp)
    gate_up_grad = scatter(gate_up_part, fsdp)
    output_grad = scatter(output_part, fsdp)
    grad_head = exchange(grad_heads.reshape(2 * lines, HD, chip_count))
    grad_head, down_grad = lax.optimization_barrier((grad_head, down_grad))

    sides = attend_backward(scalars, own, other, grad_head, head_full, log_total, block)
    sides, gate_up_grad = lax.optimization_barrier((sides, gate_up_grad))
    kept = sides[0].astype(F32)
    came = swap(sides[1], "x").astype(F32)
    first_query = jnp.where(half == 0, kept[:HD], came[:HD])
    second_query = jnp.where(half == 0, came[:HD], kept[:HD])
    grad_keys_values = kept[HD:] + came[HD:]
    turned_grads = turn_back(
        jnp.stack([first_query, second_query, grad_keys_values[:HD]]), cosine, sine
    )
    qkv_low = (
        jnp.concatenate(
            [turned_grads.reshape((group + 1) * HD, half_len), grad_keys_values[HD:]], 0
        )
        * scale_one
    ).astype(LOW)
    qkv_grad = scatter(contract(all_rows, qkv_low, 0, 1), fsdp)
    by_core = qkv_low.reshape(qkv_low.shape[0], lines, 2, count)
    core_part = lambda which: contract(
        lax.dynamic_index_in_dim(by_core, which, 2, keepdims=False).reshape(-1, lines * count),
        qkv_w,
        0,
        1,
    ).astype(LOW)
    grad_one = core_part(core).astype(F32) + swap(core_part(1 - core), "c").astype(F32)
    grad_one = line_scatter(grad_one.astype(LOW).reshape(lines, count, width), "z")
    own_rows = rows.astype(F32)
    own_scale = row_scale(own_rows)
    input_grad = (
        grad_middle
        + grad_one
        - own_rows * (own_scale * own_scale * jnp.mean(grad_one * own_rows, -1, keepdims=True))
    ).astype(LOW)[None]

    down_sum = own_sum(contract(chip_hidden, down_w, 1, 0), contract(near_hidden, down_w, 1, 0))
    block_output = (own_middle + down_sum).astype(LOW)[None]

    def four(value):
        value = value + swap_far(value)
        value_near = swap_near(value)
        return value, swap(value, "c"), value_near, swap(value_near, "c")

    order = jnp.stack([quarter, quarter ^ 1, quarter ^ 2, quarter ^ 3]).astype(jnp.int32)
    core_order = jnp.stack([core, 1 - core]).astype(jnp.int32)
    down_total = place_rows(order, four(down_grad))
    output_own = line_sum(output_grad, "z")
    output_total = place_rows(core_order, (output_own, swap(output_own, "c")))
    gate_grad, up_grad, second_gain_grad = place_columns(
        order, gain_two, gate_weight, up_weight, four(gate_up_grad), shards
    )
    qkv_all = lax.all_gather(qkv_grad, seq, axis=1, tiled=False).astype(F32)
    query_grad = qkv_all[:, :, :wide].reshape(query_weight.shape)
    key_grad = qkv_all[:, :, wide : wide + HD].reshape(key_weight.shape)
    value_grad = qkv_all[:, :, wide + HD :].reshape(value_weight.shape)
    first_gain_grad = (
        jnp.sum(query_grad * query_weight.astype(F32), 1)
        + jnp.sum(key_grad * key_weight.astype(F32), 1)
        + jnp.sum(value_grad * value_weight.astype(F32), 1)
    )
    return (
        block_output,
        input_grad,
        first_gain_grad,
        query_grad * gain_one,
        key_grad * gain_one,
        value_grad * gain_one,
        output_total,
        second_gain_grad[:, 0],
        gate_grad,
        up_grad,
        down_total,
    )


def fast_solution(mesh):
    seq_count, shard_count = mesh.devices.shape
    fine = Mesh(
        mesh.devices.reshape(seq_count // 2, 2, shard_count // 2, 2), ("z", "c", "y", "x")
    )
    seq, fsdp = ("z", "c"), ("y", "x")
    matrix = P(fsdp, None)
    return jax.shard_map(
        fast_body,
        mesh=fine,
        in_specs=(
            P(fsdp, seq, None),
            P(fsdp, seq),
            P(fsdp),
            matrix,
            matrix,
            matrix,
            matrix,
            P(fsdp),
            matrix,
            matrix,
            matrix,
            P(fsdp, seq, None),
        ),
        out_specs=(
            P(fsdp, seq, None),
            P(fsdp, seq, None),
            P(fsdp),
            matrix,
            matrix,
            matrix,
            matrix,
            P(fsdp),
            matrix,
            matrix,
            matrix,
        ),
        check_vma=False,
    )


def solution(mesh):
    shape = dict(mesh.shape)
    if shape["seq"] == KVH and shape["fsdp"] == 4:
        return fast_solution(mesh)
    return plain_solution(mesh)


def shifted(value, axis, steps):
    count = lax.axis_size(axis)
    first, last = (max(0, -steps), min(count, count - steps))
    return lax.ppermute(value, axis, [(source, source + steps) for source in range(first, last)])


def rope_tables(position_rows):
    freq = THETA ** (-(jnp.arange(HD // 2, dtype=jnp.float32) * 2.0 / HD))
    angle = position_rows.astype(jnp.float32)[:, None] * freq[None, :]
    cosine = jnp.cos(angle)
    sine = jnp.sin(angle)
    return (jnp.concatenate([cosine, cosine], -1), jnp.concatenate([sine, sine], -1))


def rotate(values, cosine, sine):
    half = HD // 2
    turned = jnp.concatenate([-values[..., half:], values[..., :half]], -1)
    return values * cosine[:, None, :] + turned * sine[:, None, :]


def rotate_back(grads, cosine, sine):
    half = HD // 2
    scaled = grads * sine[:, None, :]
    turned = jnp.concatenate([scaled[..., half:], -scaled[..., :half]], -1)
    return grads * cosine[:, None, :] + turned


def norm_forward(rows, gain):
    scale = lax.rsqrt(jnp.mean(rows * rows, -1, keepdims=True) + EPS)
    unit = rows * scale
    return (unit * gain, unit, scale)


def norm_backward(grad_out, unit, scale, gain):
    grad_unit = grad_out * gain
    gain_grad = jnp.sum(grad_out * unit, 0)
    grad_rows = scale * (grad_unit - unit * jnp.mean(grad_unit * unit, -1, keepdims=True))
    return (grad_rows, gain_grad)


def plain_body(
    tokens,
    positions,
    first_gain,
    query_weight,
    key_weight,
    value_weight,
    output_weight,
    second_gain,
    gate_weight,
    up_weight,
    down_weight,
    cotangent,
):
    seq_count = lax.axis_size("seq")
    local_rows = tokens[0]
    token_count = local_rows.shape[0]
    half_len = token_count * seq_count
    rows_float = local_rows.astype(jnp.float32)
    gain_one, wq_full, wk_full, wv_full, wo_full = (
        lax.all_gather(first_gain, "fsdp", axis=0, tiled=True),
        lax.all_gather(query_weight, "fsdp", axis=0, tiled=True),
        lax.all_gather(key_weight, "fsdp", axis=0, tiled=True),
        lax.all_gather(value_weight, "fsdp", axis=0, tiled=True),
        lax.all_gather(output_weight, "fsdp", axis=0, tiled=True),
    )
    gain_one = gain_one.astype(jnp.float32)
    normed_one, unit_one, scale_one = norm_forward(rows_float, gain_one)
    normed_low = normed_one.astype(jnp.bfloat16)
    cosine, sine = rope_tables(positions[0])
    query_lin = jnp.dot(normed_low, wq_full, preferred_element_type=jnp.float32).reshape(
        token_count, QH, HD
    )
    key_lin = jnp.dot(normed_low, wk_full, preferred_element_type=jnp.float32).reshape(
        token_count, KVH, HD
    )
    value_lin = jnp.dot(normed_low, wv_full, preferred_element_type=jnp.float32).reshape(
        token_count, KVH, HD
    )
    query_rows = rotate(query_lin, cosine, sine).astype(jnp.bfloat16)
    key_rows = rotate(key_lin, cosine, sine).astype(jnp.bfloat16)
    value_rows = value_lin.astype(jnp.bfloat16)
    repeat = max(1, seq_count // KVH)
    if repeat > 1:
        key_rows = jnp.repeat(key_rows, repeat, axis=1)
        value_rows = jnp.repeat(value_rows, repeat, axis=1)
    query_heads, key_heads, value_heads = (
        lax.all_to_all(query_rows, "seq", split_axis=1, concat_axis=0, tiled=True),
        lax.all_to_all(key_rows, "seq", split_axis=1, concat_axis=0, tiled=True),
        lax.all_to_all(value_rows, "seq", split_axis=1, concat_axis=0, tiled=True),
    )
    head_count = query_heads.shape[1]
    pair_count = key_heads.shape[1]
    group = head_count // pair_count
    half_positions = lax.all_gather(positions[0], "seq", axis=0, tiled=True)
    key_prior, value_prior = shifted((key_heads, value_heads), "fsdp", 1)
    key_all = jnp.concatenate([key_prior, key_heads], 0)
    value_all = jnp.concatenate([value_prior, value_heads], 0)
    half_index = lax.axis_index("fsdp") % 2
    key_index = (half_index - 1) * half_len + jnp.arange(2 * half_len, dtype=jnp.int32)
    row_index = half_index * half_len + jnp.arange(half_len, dtype=jnp.int32)
    row_start = row_index - half_positions
    block = min(512, half_len)
    count = half_len // block
    factor = HD ** (-0.5)
    query_blocks = query_heads.reshape(count, block, pair_count, group, HD)
    index_blocks = row_index.reshape(count, block)
    start_blocks = row_start.reshape(count, block)

    def block_scores(query_block, index_block, start_block):
        scores = (
            jnp.einsum("bkgd,tkd->kgbt", query_block, key_all, preferred_element_type=jnp.float32)
            * factor
        )
        visible = (key_index[None, :] >= start_block[:, None]) & (
            key_index[None, :] <= index_block[:, None]
        )
        return jnp.where(visible, scores, -1e30)

    def forward_block(items):
        query_block, index_block, start_block = items
        scores = block_scores(query_block, index_block, start_block)
        top = jnp.max(scores, -1, keepdims=True)
        expo = jnp.exp(scores - top)
        total = jnp.sum(expo, -1, keepdims=True)
        probs_low = (expo / total).astype(jnp.bfloat16)
        mixed = jnp.einsum(
            "kgbt,tkd->bkgd", probs_low, value_all, preferred_element_type=jnp.float32
        )
        return (mixed.reshape(block, head_count, HD).astype(jnp.bfloat16), top + jnp.log(total))

    head_blocks, log_totals = lax.map(forward_block, (query_blocks, index_blocks, start_blocks))
    head_out = head_blocks.reshape(half_len, head_count, HD)
    token_heads = lax.all_to_all(head_out, "seq", split_axis=0, concat_axis=1, tiled=True)
    heads_flat = token_heads.reshape(token_count, QH * HD)
    middle = rows_float + jnp.dot(heads_flat, wo_full, preferred_element_type=jnp.float32)
    gain_two, wg_full, wu_full, wd_full = (
        lax.all_gather(second_gain, "fsdp", axis=0, tiled=True),
        lax.all_gather(gate_weight, "fsdp", axis=0, tiled=True),
        lax.all_gather(up_weight, "fsdp", axis=0, tiled=True),
        lax.all_gather(down_weight, "fsdp", axis=0, tiled=True),
    )
    gain_two = gain_two.astype(jnp.float32)
    normed_two, unit_two, scale_two = norm_forward(middle, gain_two)
    normed_two_low = normed_two.astype(jnp.bfloat16)
    gate = jnp.dot(normed_two_low, wg_full, preferred_element_type=jnp.float32)
    upper = jnp.dot(normed_two_low, wu_full, preferred_element_type=jnp.float32)
    hidden = (jax.nn.silu(gate) * upper).astype(jnp.bfloat16)
    result = middle + jnp.dot(hidden, wd_full, preferred_element_type=jnp.float32)
    block_output = result.astype(jnp.bfloat16)[None]
    grad_low = cotangent[0]
    grad_rows = grad_low.astype(jnp.float32)
    down_grad = jnp.einsum("tf,td->fd", hidden, grad_low, preferred_element_type=jnp.float32)
    grad_hidden = jnp.einsum("td,fd->tf", grad_low, wd_full, preferred_element_type=jnp.float32)
    sigma = jax.nn.sigmoid(gate)
    gate_low = (grad_hidden * upper * sigma * (1.0 + gate * (1.0 - sigma))).astype(jnp.bfloat16)
    upper_low = (grad_hidden * gate * sigma).astype(jnp.bfloat16)
    gate_grad = jnp.einsum(
        "td,tf->df", normed_two_low, gate_low, preferred_element_type=jnp.float32
    )
    up_grad = jnp.einsum("td,tf->df", normed_two_low, upper_low, preferred_element_type=jnp.float32)
    grad_normed_two = jnp.einsum(
        "tf,df->td", gate_low, wg_full, preferred_element_type=jnp.float32
    ) + jnp.einsum("tf,df->td", upper_low, wu_full, preferred_element_type=jnp.float32)
    grad_middle_norm, second_gain_grad = norm_backward(
        grad_normed_two, unit_two, scale_two, gain_two
    )
    grad_middle = grad_rows + grad_middle_norm
    grad_branch = grad_middle.astype(jnp.bfloat16)
    output_grad = jnp.einsum(
        "tc,td->cd", heads_flat, grad_branch, preferred_element_type=jnp.float32
    )
    grad_heads = (
        jnp.einsum("td,cd->tc", grad_branch, wo_full, preferred_element_type=jnp.float32)
        .astype(jnp.bfloat16)
        .reshape(token_count, QH, HD)
    )
    grad_head_rows = lax.all_to_all(grad_heads, "seq", split_axis=1, concat_axis=0, tiled=True)
    grad_blocks = grad_head_rows.reshape(count, block, pair_count, group, HD)

    def backward_block(carry, items):
        key_acc, value_acc = carry
        query_block, index_block, start_block, grad_block, log_block = items
        scores = block_scores(query_block, index_block, start_block)
        probs = jnp.exp(scores - log_block)
        probs_low = probs.astype(jnp.bfloat16)
        grad_probs = jnp.einsum(
            "bkgd,tkd->kgbt", grad_block, value_all, preferred_element_type=jnp.float32
        )
        grad_scores = (
            probs * (grad_probs - jnp.sum(probs * grad_probs, -1, keepdims=True))
        ).astype(jnp.bfloat16)
        query_grad_block = (
            jnp.einsum("kgbt,tkd->bkgd", grad_scores, key_all, preferred_element_type=jnp.float32)
            * factor
        )
        key_acc = (
            key_acc
            + jnp.einsum(
                "kgbt,bkgd->tkd", grad_scores, query_block, preferred_element_type=jnp.float32
            )
            * factor
        )
        value_acc = value_acc + jnp.einsum(
            "kgbt,bkgd->tkd", probs_low, grad_block, preferred_element_type=jnp.float32
        )
        return ((key_acc, value_acc), query_grad_block.reshape(block, head_count, HD))

    empty = jnp.zeros((2 * half_len, pair_count, HD), jnp.float32)
    (key_acc, value_acc), query_grad_blocks = lax.scan(
        backward_block,
        (empty, empty),
        (query_blocks, index_blocks, start_blocks, grad_blocks, log_totals),
    )
    key_back, value_back = (
        shifted(key_acc[:half_len].astype(jnp.bfloat16), "fsdp", -1).astype(jnp.float32),
        shifted(value_acc[:half_len].astype(jnp.bfloat16), "fsdp", -1).astype(jnp.float32),
    )
    key_local = key_acc[half_len:] + key_back
    value_local = value_acc[half_len:] + value_back
    query_grad_heads = query_grad_blocks.reshape(half_len, head_count, HD)
    grad_query_tok, grad_key_tok, grad_value_tok = (
        lax.all_to_all(
            query_grad_heads.astype(jnp.bfloat16), "seq", split_axis=0, concat_axis=1, tiled=True
        ).astype(query_grad_heads.dtype),
        lax.all_to_all(
            key_local.astype(jnp.bfloat16), "seq", split_axis=0, concat_axis=1, tiled=True
        ).astype(key_local.dtype),
        lax.all_to_all(
            value_local.astype(jnp.bfloat16), "seq", split_axis=0, concat_axis=1, tiled=True
        ).astype(value_local.dtype),
    )
    if repeat > 1:
        grad_key_tok = grad_key_tok.reshape(token_count, KVH, repeat, HD).sum(2)
        grad_value_tok = grad_value_tok.reshape(token_count, KVH, repeat, HD).sum(2)
    query_lin_grad = (
        rotate_back(grad_query_tok, cosine, sine).astype(jnp.bfloat16).reshape(token_count, QH * HD)
    )
    key_lin_grad = (
        rotate_back(grad_key_tok, cosine, sine).astype(jnp.bfloat16).reshape(token_count, KVH * HD)
    )
    value_lin_grad = grad_value_tok.astype(jnp.bfloat16).reshape(token_count, KVH * HD)
    query_grad = jnp.einsum(
        "td,tc->dc", normed_low, query_lin_grad, preferred_element_type=jnp.float32
    )
    key_grad = jnp.einsum("td,tc->dc", normed_low, key_lin_grad, preferred_element_type=jnp.float32)
    value_grad = jnp.einsum(
        "td,tc->dc", normed_low, value_lin_grad, preferred_element_type=jnp.float32
    )
    grad_normed_one = jnp.einsum(
        "tc,dc->td", query_lin_grad, wq_full, preferred_element_type=jnp.float32
    )
    grad_normed_one = grad_normed_one + jnp.einsum(
        "tc,dc->td", key_lin_grad, wk_full, preferred_element_type=jnp.float32
    )
    grad_normed_one = grad_normed_one + jnp.einsum(
        "tc,dc->td", value_lin_grad, wv_full, preferred_element_type=jnp.float32
    )
    grad_rows_one, first_gain_grad = norm_backward(grad_normed_one, unit_one, scale_one, gain_one)
    input_grad = (grad_middle + grad_rows_one).astype(jnp.bfloat16)[None]
    pieces = (
        lax.psum_scatter(
            first_gain_grad.astype(jnp.bfloat16), "fsdp", scatter_dimension=0, tiled=True
        ).astype(jnp.float32),
        lax.psum_scatter(
            query_grad.astype(jnp.bfloat16), "fsdp", scatter_dimension=0, tiled=True
        ).astype(jnp.float32),
        lax.psum_scatter(
            key_grad.astype(jnp.bfloat16), "fsdp", scatter_dimension=0, tiled=True
        ).astype(jnp.float32),
        lax.psum_scatter(
            value_grad.astype(jnp.bfloat16), "fsdp", scatter_dimension=0, tiled=True
        ).astype(jnp.float32),
        lax.psum_scatter(
            output_grad.astype(jnp.bfloat16), "fsdp", scatter_dimension=0, tiled=True
        ).astype(jnp.float32),
        lax.psum_scatter(
            second_gain_grad.astype(jnp.bfloat16), "fsdp", scatter_dimension=0, tiled=True
        ).astype(jnp.float32),
        lax.psum_scatter(
            gate_grad.astype(jnp.bfloat16), "fsdp", scatter_dimension=0, tiled=True
        ).astype(jnp.float32),
        lax.psum_scatter(
            up_grad.astype(jnp.bfloat16), "fsdp", scatter_dimension=0, tiled=True
        ).astype(jnp.float32),
        lax.psum_scatter(
            down_grad.astype(jnp.bfloat16), "fsdp", scatter_dimension=0, tiled=True
        ).astype(jnp.float32),
    )
    shares = (
        lax.psum(pieces[0].astype(jnp.bfloat16), "seq").astype(jnp.float32),
        lax.psum(pieces[1].astype(jnp.bfloat16), "seq").astype(jnp.float32),
        lax.psum(pieces[2].astype(jnp.bfloat16), "seq").astype(jnp.float32),
        lax.psum(pieces[3].astype(jnp.bfloat16), "seq").astype(jnp.float32),
        lax.psum(pieces[4].astype(jnp.bfloat16), "seq").astype(jnp.float32),
        lax.psum(pieces[5].astype(jnp.bfloat16), "seq").astype(jnp.float32),
        lax.psum(pieces[6].astype(jnp.bfloat16), "seq").astype(jnp.float32),
        lax.psum(pieces[7].astype(jnp.bfloat16), "seq").astype(jnp.float32),
        lax.psum(pieces[8].astype(jnp.bfloat16), "seq").astype(jnp.float32),
    )
    return (
        block_output,
        input_grad,
        shares[0],
        shares[1],
        shares[2],
        shares[3],
        shares[4],
        shares[5],
        shares[6],
        shares[7],
        shares[8],
    )


def plain_solution(mesh):
    placed = (
        P("fsdp", "seq", None),
        P("fsdp", "seq"),
        P("fsdp"),
        P("fsdp", None),
        P("fsdp", None),
        P("fsdp", None),
        P("fsdp", None),
        P("fsdp"),
        P("fsdp", None),
        P("fsdp", None),
        P("fsdp", None),
        P("fsdp", "seq", None),
    )
    return jax.shard_map(
        plain_body,
        mesh=mesh,
        in_specs=placed,
        out_specs=(
            P("fsdp", "seq", None),
            P("fsdp", "seq", None),
            P("fsdp"),
            P("fsdp", None),
            P("fsdp", None),
            P("fsdp", None),
            P("fsdp", None),
            P("fsdp"),
            P("fsdp", None),
            P("fsdp", None),
            P("fsdp", None),
        ),
        check_vma=False,
    )
```

```python
import functools
import math

import jax
import jax.numpy as jnp
from jax import lax
from jax.experimental import pallas as pl
from jax.experimental.pallas import tpu as pltpu
from jax.sharding import Mesh
from jax.sharding import PartitionSpec as P

QH = 16
KVH = 8
HD = 96


THETA = 100000.0
EPS = 1e-05
LOW = jnp.bfloat16
F32 = jnp.float32
NEG = -1e30
LN2 = math.log(2.0)


def contract(left, right, left_axis, right_axis):
    return lax.dot_general(
        left, right, (((left_axis,), (right_axis,)), ((), ())), preferred_element_type=F32
    )


def visible(first, second, query_block, key_block, size):
    key = key_block * size + lax.broadcasted_iota(jnp.int32, (size, size), 0)
    query = query_block * size + lax.broadcasted_iota(jnp.int32, (1, size), 1)
    start = jnp.where(query >= second, second, jnp.where(query >= first, first, 0))
    return (key >= start) & (key <= query)


def forward_kernel(
    scalars,
    own_ref,
    other_ref,
    low_ref,
    full_ref,
    log_ref,
    query_s,
    key_s,
    value_s,
    top_s,
    total_s,
    mixed_s,
    *,
    size,
    count,
):
    half = scalars[0]
    first = scalars[1]
    second = scalars[2]
    here = pl.program_id(0)
    per_half = count // 2

    @pl.when(here == 0)
    def _():
        for ref, side in ((own_ref, half), (other_ref, 1 - half)):
            for step in range(per_half):
                block = side * per_half + step
                columns = slice(step * size, (step + 1) * size)
                query_s[block] = ref[0:HD, columns]
                key_s[block] = ref[HD : 2 * HD, columns].T
                value_s[block] = ref[2 * HD : 3 * HD, columns]

    query = query_s[here]
    top_s[...] = jnp.full_like(top_s, NEG)
    total_s[...] = jnp.zeros_like(total_s)
    mixed_s[...] = jnp.zeros_like(mixed_s)

    def add_block(block, masked):
        scores = contract(key_s[block], query, 1, 0)
        if masked:
            scores = jnp.where(visible(first, second, here, block, size), scores, NEG)
        old_top = top_s[...]
        top = jnp.maximum(old_top, jnp.max(scores, 0, keepdims=True))
        expo = jnp.exp2(scores - top)
        scale = jnp.exp2(old_top - top)
        top_s[...] = top
        total_s[...] = total_s[...] * scale + jnp.sum(expo, 0, keepdims=True)
        mixed_s[...] = mixed_s[...] * scale + contract(value_s[block], expo.astype(LOW), 1, 0)

    last = count - 1

    @pl.loop(1, jnp.where(here == last, 1, here))
    def _(block):
        add_block(block, False)

    @pl.loop(0, jnp.where(here == last, count, jnp.minimum(here + 1, 2)))
    def _(step):
        add_block(jnp.where(here == last, step, step * here), True)

    total = total_s[...]
    result = mixed_s[...] / total
    full_ref[0] = result
    low_ref[0] = result.astype(LOW)
    log_ref[0] = top_s[...] + jnp.log2(total)


def backward_kernel(
    scalars,
    own_ref,
    other_ref,
    grad_ref,
    full_ref,
    log_ref,
    out_ref,
    query_s,
    key_s,
    value_s,
    delta_s,
    query_grad_s,
    key_grad_s,
    value_grad_s,
    *,
    size,
    count,
):
    half = scalars[0]
    first = scalars[1]
    second = scalars[2]
    here = pl.program_id(0)
    per_half = count // 2

    def slot_of(block):
        return (block % per_half) * 2 + block // per_half

    @pl.when(here == 0)
    def _():
        for ref, side in ((own_ref, half), (other_ref, 1 - half)):
            for step in range(per_half):
                block = side * per_half + step
                columns = slice(step * size, (step + 1) * size)
                query_s[block] = ref[0:HD, columns]
                key_s[block] = ref[HD : 2 * HD, columns]
                value_s[block] = ref[2 * HD : 3 * HD, columns].T
        for block in range(count):
            delta_s[block] = jnp.sum(
                grad_ref[slot_of(block)].astype(F32) * full_ref[block], 0, keepdims=True
            )
        query_grad_s[...] = jnp.zeros_like(query_grad_s)

    key_grad_s[...] = jnp.zeros_like(key_grad_s)
    value_grad_s[...] = jnp.zeros_like(value_grad_s)
    key = key_s[here]
    key_rows = key.T
    value_rows = value_s[here]

    def add_block(block, masked):
        query = query_s[block]
        grad = grad_ref[slot_of(block)]
        scores = contract(key_rows, query, 1, 0)
        if masked:
            scores = jnp.where(visible(first, second, block, here, size), scores, NEG)
        probs = jnp.exp2(scores - log_ref[block])
        grad_probs = contract(value_rows, grad, 1, 0)
        grad_scores = (probs * (grad_probs - delta_s[block])).astype(LOW)
        value_grad_s[...] += contract(grad, probs.astype(LOW), 1, 1)
        key_grad_s[...] += contract(query, grad_scores, 1, 1)
        query_grad_s[block] += contract(key, grad_scores, 1, 0)

    last = count - 1

    @pl.loop(here + 1, jnp.where(here == 0, 1, last))
    def _(block):
        add_block(block, False)

    @pl.loop(0, jnp.where(here == 0, count, jnp.where(here == last, 1, 2)))
    def _(step):
        add_block(jnp.where(here == 0, step, jnp.where(step == 0, here, last)), True)

    side = here // per_half
    slot = jnp.where(side == half, 0, 1)
    columns = pl.ds(pl.multiple_of((here % per_half) * size, size), size)
    out_ref[slot, 0:HD, columns] = (query_grad_s[here] * HD**-0.5).astype(LOW)
    out_ref[slot, HD : 2 * HD, columns] = (key_grad_s[...] * LN2).astype(LOW)
    out_ref[slot, 2 * HD : 3 * HD, columns] = value_grad_s[...].astype(LOW)


def attend_forward(scalars, own, other, size):
    count = 2 * own.shape[1] // size
    whole = lambda shape: pl.BlockSpec(shape, lambda i, s: (0,) * len(shape))
    per_half = count // 2
    pairs = count * (count + 1) // 2
    return pl.pallas_call(
        functools.partial(forward_kernel, size=size, count=count),
        grid_spec=pltpu.PrefetchScalarGridSpec(
            num_scalar_prefetch=1,
            grid=(count,),
            in_specs=[whole(own.shape), whole(other.shape)],
            out_specs=[
                pl.BlockSpec(
                    (1, HD, size), lambda i, s: ((i % per_half) * 2 + i // per_half, 0, 0)
                ),
                pl.BlockSpec((1, HD, size), lambda i, s: (i, 0, 0)),
                pl.BlockSpec((1, 1, size), lambda i, s: (i, 0, 0)),
            ],
            scratch_shapes=[
                pltpu.VMEM((count, HD, size), LOW),
                pltpu.VMEM((count, size, HD), LOW),
                pltpu.VMEM((count, HD, size), LOW),
                pltpu.VMEM((1, size), F32),
                pltpu.VMEM((1, size), F32),
                pltpu.VMEM((HD, size), F32),
            ],
        ),
        out_shape=[
            jax.ShapeDtypeStruct((count, HD, size), LOW),
            jax.ShapeDtypeStruct((count, HD, size), F32),
            jax.ShapeDtypeStruct((count, 1, size), F32),
        ],
        compiler_params=pltpu.CompilerParams(
            dimension_semantics=("arbitrary",), vmem_limit_bytes=32 * 2**20
        ),
        cost_estimate=pl.CostEstimate(
            flops=pairs * size * size * HD * 4,
            bytes_accessed=10 * 2**20,
            transcendentals=pairs * size * size,
        ),
        name="attend_forward",
    )(scalars, own, other)


def attend_backward(scalars, own, other, grad, full, log_total, size):
    count = 2 * own.shape[1] // size
    whole = lambda shape: pl.BlockSpec(shape, lambda i, s: (0,) * len(shape))
    pairs = count * (count + 1) // 2
    out_shape = (2, 3 * HD, own.shape[1])
    return pl.pallas_call(
        functools.partial(backward_kernel, size=size, count=count),
        grid_spec=pltpu.PrefetchScalarGridSpec(
            num_scalar_prefetch=1,
            grid=(count,),
            in_specs=[
                whole(own.shape),
                whole(other.shape),
                whole(grad.shape),
                whole(full.shape),
                whole(log_total.shape),
            ],
            out_specs=whole(out_shape),
            scratch_shapes=[
                pltpu.VMEM((count, HD, size), LOW),
                pltpu.VMEM((count, HD, size), LOW),
                pltpu.VMEM((count, size, HD), LOW),
                pltpu.VMEM((count, 1, size), F32),
                pltpu.VMEM((count, HD, size), F32),
                pltpu.VMEM((HD, size), F32),
                pltpu.VMEM((HD, size), F32),
            ],
        ),
        out_shape=jax.ShapeDtypeStruct(out_shape, LOW),
        compiler_params=pltpu.CompilerParams(
            dimension_semantics=("arbitrary",), vmem_limit_bytes=32 * 2**20
        ),
        cost_estimate=pl.CostEstimate(
            flops=pairs * size * size * HD * 10,
            bytes_accessed=16 * 2**20,
            transcendentals=pairs * size * size,
        ),
        name="attend_backward",
    )(scalars, own, other, grad, full, log_total)


def place_rows_kernel(order, *refs):
    pieces, out_ref = refs[:-1], refs[-1]
    size = pieces[0].shape[0]
    for index, piece in enumerate(pieces):
        start = pl.multiple_of(order[index] * size, size)
        out_ref[pl.ds(start, size), :] = piece[...].astype(F32)


def place_rows(order, pieces):
    size, width = pieces[0].shape
    total = size * len(pieces)
    step = 512
    return pl.pallas_call(
        place_rows_kernel,
        grid_spec=pltpu.PrefetchScalarGridSpec(
            num_scalar_prefetch=1,
            grid=(width // step,),
            in_specs=[pl.BlockSpec((size, step), lambda i, s: (0, i)) for _ in pieces],
            out_specs=pl.BlockSpec((total, step), lambda i, s: (0, i)),
        ),
        out_shape=jax.ShapeDtypeStruct((total, width), F32),
        compiler_params=pltpu.CompilerParams(vmem_limit_bytes=24 * 2**20),
        cost_estimate=pl.CostEstimate(
            flops=0, bytes_accessed=total * width * 6, transcendentals=0
        ),
        name="place_rows",
    )(order, *pieces)


def place_columns_kernel(order, gain_ref, gate_w_ref, up_w_ref, *refs):
    count = (len(refs) - 3) // 2
    gates, ups = refs[:count], refs[count : 2 * count]
    gate_ref, up_ref, sum_ref = refs[2 * count :]
    size = gates[0].shape[1]
    gain = gain_ref[...]
    total = jnp.zeros((gate_ref.shape[0], size), F32)
    for index in range(count):
        columns = pl.ds(pl.multiple_of(order[index] * size, size), size)
        gate, up = gates[index][...].astype(F32), ups[index][...].astype(F32)
        total += gate * gate_w_ref[:, columns].astype(F32)
        total += up * up_w_ref[:, columns].astype(F32)
        gate_ref[:, columns] = gate * gain
        up_ref[:, columns] = up * gain

    @pl.when(pl.program_id(0) == 0)
    def _():
        sum_ref[...] = jnp.zeros_like(sum_ref)

    sum_ref[...] += jnp.sum(total, 1, keepdims=True)


def place_columns(order, gain, gate_weight, up_weight, gates, ups, shards):
    rows, width = gate_weight.shape
    span = width // shards
    size = span // len(gates)
    wide = pl.BlockSpec((rows, span), lambda i, s: (0, i))
    thin = pl.BlockSpec((rows, 1), lambda i, s: (0, 0))
    pieces = [pl.BlockSpec((rows, size), lambda i, s: (0, i)) for _ in (*gates, *ups)]
    return pl.pallas_call(
        place_columns_kernel,
        grid_spec=pltpu.PrefetchScalarGridSpec(
            num_scalar_prefetch=1,
            grid=(shards,),
            in_specs=[thin, wide, wide, *pieces],
            out_specs=[wide, wide, thin],
        ),
        out_shape=[
            jax.ShapeDtypeStruct((rows, width), F32),
            jax.ShapeDtypeStruct((rows, width), F32),
            jax.ShapeDtypeStruct((rows, 1), F32),
        ],
        compiler_params=pltpu.CompilerParams(
            dimension_semantics=("arbitrary",), vmem_limit_bytes=24 * 2**20
        ),
        cost_estimate=pl.CostEstimate(
            flops=rows * width * 6, bytes_accessed=rows * width * 16, transcendentals=0
        ),
        name="place_columns",
    )(order, gain, gate_weight, up_weight, *gates, *ups)


def place_heads_kernel(gain_ref, query_w, key_w, value_w, all_ref, query_ref, key_ref, value_ref, sum_ref):
    rows = gain_ref.shape[0]
    wide = query_ref.shape[1] // KVH
    gain = gain_ref[...]
    total = jnp.zeros((rows, 4 * HD), F32)
    pieces = [all_ref[i * rows : (i + 1) * rows, :].astype(F32) for i in range(KVH)]
    for start in range(0, KVH, 2):
        value = jnp.concatenate([piece[:, :wide] for piece in pieces[start : start + 2]], 1)
        columns = slice(start * wide, (start + 2) * wide)
        total += value * query_w[:, columns].astype(F32)
        query_ref[:, columns] = value * gain
    for first, weight, out_ref in ((wide, key_w, key_ref), (wide + HD, value_w, value_ref)):
        for start in range(0, KVH, 4):
            value = jnp.concatenate(
                [piece[:, first : first + HD] for piece in pieces[start : start + 4]], 1
            )
            columns = slice(start * HD, (start + 4) * HD)
            total += value * weight[:, columns].astype(F32)
            out_ref[:, columns] = value * gain
    sum_ref[...] = jnp.sum(total, 1, keepdims=True)


def place_heads(gain, query_weight, key_weight, value_weight, pieces):
    weights = (query_weight, key_weight, value_weight)
    rows = gain.shape[0]
    return pl.pallas_call(
        place_heads_kernel,
        out_shape=[jax.ShapeDtypeStruct(weight.shape, F32) for weight in weights]
        + [jax.ShapeDtypeStruct((rows, 1), F32)],
        compiler_params=pltpu.CompilerParams(vmem_limit_bytes=32 * 2**20),
        cost_estimate=pl.CostEstimate(
            flops=rows * 3072 * 4, bytes_accessed=rows * 3072 * 8, transcendentals=0
        ),
        name="place_heads",
    )(gain, *weights, pieces)


def merge_kernel(scalars, kept_ref, came_ref, cosine_ref, sine_ref, scale_ref, out_ref, own_ref, other_ref, *, count):
    half, core = scalars[0], scalars[3]
    lines = out_ref.shape[1] // (2 * count)
    for line in range(lines):
        for which in range(2):
            start = (line * 2 + which) * count
            columns = slice(start, start + count)
            kept = kept_ref[:, columns].astype(F32)
            came = came_ref[:, columns].astype(F32)
            cosine, sine, scale = cosine_ref[:, columns], sine_ref[:, columns], scale_ref[:, columns]
            lead = half == 0
            joint = kept[HD:] + came[HD:]
            first = jnp.where(lead, kept[:HD], came[:HD])
            second = jnp.where(lead, came[:HD], kept[:HD])
            turned = []
            for value in (first, second, joint[:HD]):
                low, high = value[: HD // 2], value[HD // 2 :]
                turned.append((low * cosine + high * sine) * scale)
                turned.append((high * cosine - low * sine) * scale)
            turned.append(joint[HD:] * scale)
            result = jnp.concatenate([part.astype(LOW) for part in turned], 0)
            out_ref[:, columns] = result
            place = slice(line * count, (line + 1) * count)

            @pl.when(core == which)
            def _():
                own_ref[:, place] = result

            @pl.when(core != which)
            def _():
                other_ref[:, place] = result


def merge(scalars, kept, came, cosine, sine, scale, count):
    tokens = kept.shape[1]
    whole = lambda value: pl.BlockSpec(value.shape, lambda i, s: (0, 0))
    outs = [
        jax.ShapeDtypeStruct((4 * HD, tokens), LOW),
        jax.ShapeDtypeStruct((4 * HD, tokens // 2), LOW),
        jax.ShapeDtypeStruct((4 * HD, tokens // 2), LOW),
    ]
    return pl.pallas_call(
        functools.partial(merge_kernel, count=count),
        grid_spec=pltpu.PrefetchScalarGridSpec(
            num_scalar_prefetch=1,
            grid=(1,),
            in_specs=[whole(value) for value in (kept, came, cosine, sine, scale)],
            out_specs=[whole(value) for value in outs],
        ),
        out_shape=outs,
        compiler_params=pltpu.CompilerParams(vmem_limit_bytes=24 * 2**20),
        cost_estimate=pl.CostEstimate(
            flops=tokens * HD * 24, bytes_accessed=tokens * HD * 30, transcendentals=0
        ),
        name="merge",
    )(scalars, kept, came, cosine, sine, scale)


def swap(value, axis):
    return lax.ppermute(value, axis, [(0, 1), (1, 0)])


def swap_near(value):
    return lax.ppermute(value, "z", [(0, 1), (1, 0), (2, 3), (3, 2)])


def swap_far(value):
    return lax.ppermute(value, "z", [(0, 2), (2, 0), (1, 3), (3, 1)])


def line_sum(part, axis):
    place = lax.axis_index(axis)
    inner = (place == 1) | (place == 2)
    part = part + lax.ppermute(part, axis, [(0, 1), (3, 2)])
    part = part + lax.ppermute(part, axis, [(1, 2), (2, 1)])
    outer = lax.ppermute(part, axis, [(1, 0), (2, 3)])
    return jnp.where(inner, part, outer)


def line_scatter(parts, axis):
    place = lax.axis_index(axis)
    block = lambda at: lax.dynamic_index_in_dim(parts, jnp.clip(at, 0, 3), 0, keepdims=False)
    up, down = block(place + 3), block(place - 3)
    for step in (2, 1):
        up = lax.ppermute(up, axis, [(i, i + 1) for i in range(3 - step)])
        down = lax.ppermute(down, axis, [(3 - i, 2 - i) for i in range(3 - step)])
        up = (up.astype(F32) + block(place + step)).astype(LOW)
        down = (down.astype(F32) + block(place - step)).astype(LOW)
    up = lax.ppermute(up, axis, [(0, 1), (1, 2), (2, 3)])
    down = lax.ppermute(down, axis, [(3, 2), (2, 1), (1, 0)])
    return block(place).astype(F32) + up.astype(F32) + down.astype(F32)


def in_order(place, own, other):
    return (jnp.where(place == 0, own, other), jnp.where(place == 0, other, own))


def both(place, own, other):
    return jnp.concatenate(in_order(place, own, other), 0)


def turn(values, cosine, sine):
    half = HD // 2
    low, high = values[:, :half], values[:, half:]
    return jnp.concatenate([low * cosine - high * sine, high * cosine + low * sine], 1)


def turn_back(grads, cosine, sine):
    half = HD // 2
    low, high = grads[:, :half], grads[:, half:]
    return jnp.concatenate([low * cosine + high * sine, high * cosine - low * sine], 1)


def fast_body(
    tokens,
    positions,
    first_gain,
    query_weight,
    key_weight,
    value_weight,
    output_weight,
    second_gain,
    gate_weight,
    up_weight,
    down_weight,
    cotangent,
):
    seq = ("z", "c")
    fsdp = ("y", "x")
    z, core, half = lax.axis_index("z"), lax.axis_index("c"), lax.axis_index("x")
    near = z % 2
    lines = lax.axis_size("z")
    seq_count = 2 * lines
    shards = lax.axis_size("y") * 2
    spot = z * 2 + core
    quarter = near * 2 + core
    rows = tokens[0]
    count, width = rows.shape
    chip_count = 2 * count
    half_len = count * seq_count
    seq_len = 2 * half_len
    block = chip_count

    begins = jnp.where(
        (spot == 0) & (half == 0),
        count - 1 - positions[0, count - 1],
        half * half_len + spot * count - positions[0, 0],
    )
    ends = begins + (seq_len - count)
    scalars = jnp.stack([half, begins, ends, core]).astype(jnp.int32)

    gain_one = first_gain.astype(F32)[:, None]
    gain_two = second_gain.astype(F32)[:, None]

    group = QH // KVH
    wide = group * HD
    take = functools.partial(lax.dynamic_slice_in_dim, axis=1)
    take_rows = functools.partial(lax.dynamic_slice_in_dim, axis=0)
    qkv_shard = (
        jnp.concatenate(
            [
                take(query_weight, spot * wide, wide),
                take(key_weight, spot * HD, HD),
                take(value_weight, spot * HD, HD),
            ],
            1,
        ).astype(F32)
        * gain_one
    ).astype(LOW)
    out_rows = output_weight.shape[0] // 2
    out_shard = take_rows(output_weight, core * out_rows, out_rows)
    piece = down_weight.shape[0] // 4
    down_shard = take_rows(down_weight, quarter * piece, piece)
    gate_shard, up_shard = (
        (
            jnp.concatenate(
                [
                    take(weight, shard * 4 * piece + quarter * piece, piece)
                    for shard in range(shards)
                ],
                1,
            ).astype(F32)
            * gain_two
        ).astype(LOW)
        for weight in (gate_weight, up_weight)
    )

    gather = lambda value, axes: lax.all_gather(value, axes, axis=0, tiled=True)
    all_rows = gather(rows, seq)
    qkv_pair = both(half, qkv_shard, swap(qkv_shard, "x"))
    qkv_w = both(lax.axis_index("y"), qkv_pair, swap(qkv_pair, "y"))
    side = lax.axis_index("y")
    gate_pair = both(half, gate_shard, swap(gate_shard, "x"))
    up_pair = jnp.stack(in_order(side, up_shard, swap(up_shard, "y")))
    qkv_w, gate_pair, up_pair = lax.optimization_barrier((qkv_w, gate_pair, up_pair))
    gate_w = both(side, gate_pair, swap(gate_pair, "y"))
    up_w = jnp.stack(in_order(half, up_pair, swap(up_pair, "x")), 1).reshape(gate_w.shape)

    chip_cot = both(core, cotangent[0], swap(cotangent[0], "c"))
    near_cot = swap_near(cotangent[0])
    near_cot = jnp.concatenate([near_cot, swap(near_cot, "c")], 0)
    all_cot = jnp.concatenate([chip_cot, near_cot], 0)

    place = half * half_len + jnp.arange(half_len, dtype=jnp.int32)
    start = jnp.where(place >= ends, ends, jnp.where(place >= begins, begins, 0))
    freq = THETA ** (-(jnp.arange(HD // 2, dtype=F32) * 2.0 / HD))
    angle = freq[:, None] * (place - start).astype(F32)[None, :]
    cosine, sine = jnp.cos(angle), jnp.sin(angle)
    rows_float = all_rows.astype(F32)
    scale_one = lax.rsqrt(jnp.mean(rows_float * rows_float, -1) + EPS)[None, :]
    qkv = contract(qkv_w, all_rows, 0, 1) * scale_one
    turned = turn(qkv[: wide + HD].reshape(group + 1, HD, half_len), cosine, sine)
    query_pair = turned[:group] * (HD**-0.5 / LN2)
    keys_values = jnp.concatenate([turned[group], qkv[wide + HD :]], 0).astype(LOW)
    mine = jnp.where(half == 0, query_pair[0], query_pair[1]).astype(LOW)
    theirs = jnp.where(half == 0, query_pair[1], query_pair[0]).astype(LOW)
    own = jnp.concatenate([mine, keys_values], 0)
    leaving = jnp.concatenate([theirs, keys_values], 0)
    leaving, gate_w, up_w = lax.optimization_barrier((leaving, gate_w, up_w))
    other = swap(leaving, "x")
    other, out_shard, down_shard = lax.optimization_barrier((other, out_shard, down_shard))
    out_w = gather(out_shard, fsdp)
    down_w = gather(down_shard, fsdp)

    head_low, head_full, log_total = attend_forward(scalars, own, other, block)
    exchange = lambda value: lax.all_to_all(
        value, ("z", "x"), split_axis=0, concat_axis=0, tiled=True
    )
    heads = exchange(head_low).reshape(QH // 2 * HD, chip_count)

    mine_of = lambda value: take_rows(value, core * count, count)
    theirs_of = lambda value: take_rows(value, (1 - core) * count, count)
    branch = contract(heads, out_w, 0, 0).astype(LOW)
    chip_rows = take_rows(all_rows, z * chip_count, chip_count)
    middle = chip_rows.astype(F32) + (branch.astype(F32) + swap(branch, "c").astype(F32))
    own_middle = mine_of(middle)
    middle_low = middle.astype(LOW)
    near_middle = swap_near(mine_of(middle_low))
    near_middle = jnp.concatenate([near_middle, swap(near_middle, "c")], 0)

    def row_scale(value):
        return lax.rsqrt(jnp.mean(value * value, -1, keepdims=True) + EPS)

    def feed(low, scale):
        gate, upper = contract(low, gate_w, 1, 0) * scale, contract(low, up_w, 1, 0) * scale
        sigma = jax.nn.sigmoid(gate)
        silu = gate * sigma
        return (silu * upper).astype(LOW), (gate, upper, sigma, silu)

    def feed_back(cot, scale, kept):
        gate, upper, sigma, silu = kept
        grad_hidden = contract(cot, down_w, 1, 1) * scale
        gate_low = (grad_hidden * upper * sigma * (1.0 + gate * (1.0 - sigma))).astype(LOW)
        upper_low = (grad_hidden * silu).astype(LOW)
        part = contract(gate_low, gate_w, 1, 1) + contract(upper_low, up_w, 1, 1)
        return gate_low, upper_low, part

    chip_scale = row_scale(middle)
    near_scale = row_scale(near_middle.astype(F32))
    chip_hidden, chip_kept = feed(middle_low, chip_scale)
    near_hidden, near_kept = feed(near_middle, near_scale)
    stack = lambda first, second: jnp.concatenate([first, second], 0)
    down_part = contract(stack(chip_hidden, near_hidden), all_cot, 0, 0).astype(LOW)
    near_cot, down_part = lax.optimization_barrier((near_cot, down_part))
    near_gate, near_upper, near_part = feed_back(near_cot, near_scale, near_kept)
    chip_gate, chip_upper, chip_part = feed_back(chip_cot, chip_scale, chip_kept)

    def own_sum(chip_part, near_part):
        near_sum = near_part[:count].astype(F32) + swap(near_part[count:].astype(LOW), "c")
        came = swap_near(near_sum.astype(LOW))
        chip_sum = mine_of(chip_part).astype(F32) + swap(theirs_of(chip_part).astype(LOW), "c")
        return chip_sum + came.astype(F32)

    grad_two = own_sum(chip_part, near_part)
    all_middle = stack(middle_low, near_middle)
    gate_part = contract(all_middle, stack(chip_gate, near_gate), 0, 0).astype(LOW)
    up_part = contract(all_middle, stack(chip_upper, near_upper), 0, 0).astype(LOW)
    grad_two, gate_part, up_part = lax.optimization_barrier((grad_two, gate_part, up_part))
    own_scale = mine_of(chip_scale)
    grad_middle = (
        cotangent[0].astype(F32)
        + grad_two
        - own_middle * (own_scale * own_scale * jnp.mean(grad_two * own_middle, -1, keepdims=True))
    )
    own_branch = grad_middle.astype(LOW)
    grad_branch = both(core, own_branch, swap(own_branch, "c"))
    grad_heads = contract(out_w, grad_branch, 1, 1).astype(LOW)

    output_part = contract(heads, grad_branch, 1, 0).astype(LOW)

    scatter = lambda value, axes: lax.psum_scatter(
        value.astype(LOW), axes, scatter_dimension=0, tiled=True
    )
    down_grad = scatter(down_part, fsdp)
    gate_grad = scatter(gate_part, fsdp)
    up_grad = scatter(up_part, fsdp)
    output_grad = scatter(output_part, fsdp)
    grad_head = exchange(grad_heads.reshape(2 * lines, HD, chip_count))
    grad_head, down_grad, output_part = lax.optimization_barrier(
        (grad_head, down_grad, output_part)
    )

    def far_sum(value):
        return value + swap_far(value)

    def with_near(value):
        return value, swap_near(value)

    def four(value, near_value):
        return value, swap(value, "c"), near_value, swap(near_value, "c")

    sides = attend_backward(scalars, own, other, grad_head, head_full, log_total, block)
    down_sum = far_sum(down_grad)
    sides, gate_grad, down_sum = lax.optimization_barrier((sides, gate_grad, down_sum))
    gate_sum = far_sum(gate_grad)
    came = swap(sides[1], "x")
    down_pair = with_near(down_sum)
    came, up_grad, gate_sum, down_pair = lax.optimization_barrier(
        (came, up_grad, gate_sum, down_pair)
    )
    up_sum = far_sum(up_grad)
    qkv_low, own_low, other_low = merge(scalars, sides[0], came, cosine, sine, scale_one, count)
    qkv_grad = scatter(contract(all_rows, qkv_low, 0, 1), fsdp)
    grad_one = contract(other_low, qkv_w, 0, 1).astype(LOW)
    grad_one = contract(own_low, qkv_w, 0, 1) + swap(grad_one, "c").astype(F32)
    gate_pair = with_near(gate_sum)
    grad_one, up_sum, gate_pair = lax.optimization_barrier((grad_one, up_sum, gate_pair))
    grad_one = line_scatter(grad_one.astype(LOW).reshape(lines, count, width), "z")
    own_rows = rows.astype(F32)
    own_scale = row_scale(own_rows)
    input_grad = (
        grad_middle
        + grad_one
        - own_rows * (own_scale * own_scale * jnp.mean(grad_one * own_rows, -1, keepdims=True))
    ).astype(LOW)[None]

    feed_sum = own_sum(contract(chip_hidden, down_w, 1, 0), contract(near_hidden, down_w, 1, 0))
    block_output = (own_middle + feed_sum).astype(LOW)[None]

    order = jnp.stack([quarter, quarter ^ 1, quarter ^ 2, quarter ^ 3]).astype(jnp.int32)
    core_order = jnp.stack([core, 1 - core]).astype(jnp.int32)
    down_total = place_rows(order, four(*down_pair))
    output_own = line_sum(output_grad, "z")
    output_total = place_rows(core_order, (output_own, swap(output_own, "c")))
    gate_total, up_total, second_gain_grad = place_columns(
        order, gain_two, gate_weight, up_weight, four(*gate_pair), four(*with_near(up_sum)), shards
    )
    query_grad, key_grad, value_grad, first_gain_grad = place_heads(
        gain_one, query_weight, key_weight, value_weight, gather(qkv_grad, seq)
    )
    return (
        block_output,
        input_grad,
        first_gain_grad[:, 0],
        query_grad,
        key_grad,
        value_grad,
        output_total,
        second_gain_grad[:, 0],
        gate_total,
        up_total,
        down_total,
    )


def fast_solution(mesh):
    seq_count, shard_count = mesh.devices.shape
    fine = Mesh(
        mesh.devices.reshape(seq_count // 2, 2, shard_count // 2, 2), ("z", "c", "y", "x")
    )
    seq, fsdp = ("z", "c"), ("y", "x")
    matrix = P(fsdp, None)
    return jax.shard_map(
        fast_body,
        mesh=fine,
        in_specs=(
            P(fsdp, seq, None),
            P(fsdp, seq),
            P(fsdp),
            matrix,
            matrix,
            matrix,
            matrix,
            P(fsdp),
            matrix,
            matrix,
            matrix,
            P(fsdp, seq, None),
        ),
        out_specs=(
            P(fsdp, seq, None),
            P(fsdp, seq, None),
            P(fsdp),
            matrix,
            matrix,
            matrix,
            matrix,
            P(fsdp),
            matrix,
            matrix,
            matrix,
        ),
        check_vma=False,
    )


def solution(mesh):
    shape = dict(mesh.shape)
    if shape["seq"] == KVH and shape["fsdp"] == 4:
        return fast_solution(mesh)
    return plain_solution(mesh)


def shifted(value, axis, steps):
    count = lax.axis_size(axis)
    first, last = (max(0, -steps), min(count, count - steps))
    return lax.ppermute(value, axis, [(source, source + steps) for source in range(first, last)])


def rope_tables(position_rows):
    freq = THETA ** (-(jnp.arange(HD // 2, dtype=jnp.float32) * 2.0 / HD))
    angle = position_rows.astype(jnp.float32)[:, None] * freq[None, :]
    cosine = jnp.cos(angle)
    sine = jnp.sin(angle)
    return (jnp.concatenate([cosine, cosine], -1), jnp.concatenate([sine, sine], -1))


def rotate(values, cosine, sine):
    half = HD // 2
    turned = jnp.concatenate([-values[..., half:], values[..., :half]], -1)
    return values * cosine[:, None, :] + turned * sine[:, None, :]


def rotate_back(grads, cosine, sine):
    half = HD // 2
    scaled = grads * sine[:, None, :]
    turned = jnp.concatenate([scaled[..., half:], -scaled[..., :half]], -1)
    return grads * cosine[:, None, :] + turned


def norm_forward(rows, gain):
    scale = lax.rsqrt(jnp.mean(rows * rows, -1, keepdims=True) + EPS)
    unit = rows * scale
    return (unit * gain, unit, scale)


def norm_backward(grad_out, unit, scale, gain):
    grad_unit = grad_out * gain
    gain_grad = jnp.sum(grad_out * unit, 0)
    grad_rows = scale * (grad_unit - unit * jnp.mean(grad_unit * unit, -1, keepdims=True))
    return (grad_rows, gain_grad)


def plain_body(
    tokens,
    positions,
    first_gain,
    query_weight,
    key_weight,
    value_weight,
    output_weight,
    second_gain,
    gate_weight,
    up_weight,
    down_weight,
    cotangent,
):
    seq_count = lax.axis_size("seq")
    local_rows = tokens[0]
    token_count = local_rows.shape[0]
    half_len = token_count * seq_count
    rows_float = local_rows.astype(jnp.float32)
    gain_one, wq_full, wk_full, wv_full, wo_full = (
        lax.all_gather(first_gain, "fsdp", axis=0, tiled=True),
        lax.all_gather(query_weight, "fsdp", axis=0, tiled=True),
        lax.all_gather(key_weight, "fsdp", axis=0, tiled=True),
        lax.all_gather(value_weight, "fsdp", axis=0, tiled=True),
        lax.all_gather(output_weight, "fsdp", axis=0, tiled=True),
    )
    gain_one = gain_one.astype(jnp.float32)
    normed_one, unit_one, scale_one = norm_forward(rows_float, gain_one)
    normed_low = normed_one.astype(jnp.bfloat16)
    cosine, sine = rope_tables(positions[0])
    query_lin = jnp.dot(normed_low, wq_full, preferred_element_type=jnp.float32).reshape(
        token_count, QH, HD
    )
    key_lin = jnp.dot(normed_low, wk_full, preferred_element_type=jnp.float32).reshape(
        token_count, KVH, HD
    )
    value_lin = jnp.dot(normed_low, wv_full, preferred_element_type=jnp.float32).reshape(
        token_count, KVH, HD
    )
    query_rows = rotate(query_lin, cosine, sine).astype(jnp.bfloat16)
    key_rows = rotate(key_lin, cosine, sine).astype(jnp.bfloat16)
    value_rows = value_lin.astype(jnp.bfloat16)
    repeat = max(1, seq_count // KVH)
    if repeat > 1:
        key_rows = jnp.repeat(key_rows, repeat, axis=1)
        value_rows = jnp.repeat(value_rows, repeat, axis=1)
    query_heads, key_heads, value_heads = (
        lax.all_to_all(query_rows, "seq", split_axis=1, concat_axis=0, tiled=True),
        lax.all_to_all(key_rows, "seq", split_axis=1, concat_axis=0, tiled=True),
        lax.all_to_all(value_rows, "seq", split_axis=1, concat_axis=0, tiled=True),
    )
    head_count = query_heads.shape[1]
    pair_count = key_heads.shape[1]
    group = head_count // pair_count
    half_positions = lax.all_gather(positions[0], "seq", axis=0, tiled=True)
    key_prior, value_prior = shifted((key_heads, value_heads), "fsdp", 1)
    key_all = jnp.concatenate([key_prior, key_heads], 0)
    value_all = jnp.concatenate([value_prior, value_heads], 0)
    half_index = lax.axis_index("fsdp") % 2
    key_index = (half_index - 1) * half_len + jnp.arange(2 * half_len, dtype=jnp.int32)
    row_index = half_index * half_len + jnp.arange(half_len, dtype=jnp.int32)
    row_start = row_index - half_positions
    block = min(512, half_len)
    count = half_len // block
    factor = HD ** (-0.5)
    query_blocks = query_heads.reshape(count, block, pair_count, group, HD)
    index_blocks = row_index.reshape(count, block)
    start_blocks = row_start.reshape(count, block)

    def block_scores(query_block, index_block, start_block):
        scores = (
            jnp.einsum("bkgd,tkd->kgbt", query_block, key_all, preferred_element_type=jnp.float32)
            * factor
        )
        visible = (key_index[None, :] >= start_block[:, None]) & (
            key_index[None, :] <= index_block[:, None]
        )
        return jnp.where(visible, scores, -1e30)

    def forward_block(items):
        query_block, index_block, start_block = items
        scores = block_scores(query_block, index_block, start_block)
        top = jnp.max(scores, -1, keepdims=True)
        expo = jnp.exp(scores - top)
        total = jnp.sum(expo, -1, keepdims=True)
        probs_low = (expo / total).astype(jnp.bfloat16)
        mixed = jnp.einsum(
            "kgbt,tkd->bkgd", probs_low, value_all, preferred_element_type=jnp.float32
        )
        return (mixed.reshape(block, head_count, HD).astype(jnp.bfloat16), top + jnp.log(total))

    head_blocks, log_totals = lax.map(forward_block, (query_blocks, index_blocks, start_blocks))
    head_out = head_blocks.reshape(half_len, head_count, HD)
    token_heads = lax.all_to_all(head_out, "seq", split_axis=0, concat_axis=1, tiled=True)
    heads_flat = token_heads.reshape(token_count, QH * HD)
    middle = rows_float + jnp.dot(heads_flat, wo_full, preferred_element_type=jnp.float32)
    gain_two, wg_full, wu_full, wd_full = (
        lax.all_gather(second_gain, "fsdp", axis=0, tiled=True),
        lax.all_gather(gate_weight, "fsdp", axis=0, tiled=True),
        lax.all_gather(up_weight, "fsdp", axis=0, tiled=True),
        lax.all_gather(down_weight, "fsdp", axis=0, tiled=True),
    )
    gain_two = gain_two.astype(jnp.float32)
    normed_two, unit_two, scale_two = norm_forward(middle, gain_two)
    normed_two_low = normed_two.astype(jnp.bfloat16)
    gate = jnp.dot(normed_two_low, wg_full, preferred_element_type=jnp.float32)
    upper = jnp.dot(normed_two_low, wu_full, preferred_element_type=jnp.float32)
    hidden = (jax.nn.silu(gate) * upper).astype(jnp.bfloat16)
    result = middle + jnp.dot(hidden, wd_full, preferred_element_type=jnp.float32)
    block_output = result.astype(jnp.bfloat16)[None]
    grad_low = cotangent[0]
    grad_rows = grad_low.astype(jnp.float32)
    down_grad = jnp.einsum("tf,td->fd", hidden, grad_low, preferred_element_type=jnp.float32)
    grad_hidden = jnp.einsum("td,fd->tf", grad_low, wd_full, preferred_element_type=jnp.float32)
    sigma = jax.nn.sigmoid(gate)
    gate_low = (grad_hidden * upper * sigma * (1.0 + gate * (1.0 - sigma))).astype(jnp.bfloat16)
    upper_low = (grad_hidden * gate * sigma).astype(jnp.bfloat16)
    gate_grad = jnp.einsum(
        "td,tf->df", normed_two_low, gate_low, preferred_element_type=jnp.float32
    )
    up_grad = jnp.einsum("td,tf->df", normed_two_low, upper_low, preferred_element_type=jnp.float32)
    grad_normed_two = jnp.einsum(
        "tf,df->td", gate_low, wg_full, preferred_element_type=jnp.float32
    ) + jnp.einsum("tf,df->td", upper_low, wu_full, preferred_element_type=jnp.float32)
    grad_middle_norm, second_gain_grad = norm_backward(
        grad_normed_two, unit_two, scale_two, gain_two
    )
    grad_middle = grad_rows + grad_middle_norm
    grad_branch = grad_middle.astype(jnp.bfloat16)
    output_grad = jnp.einsum(
        "tc,td->cd", heads_flat, grad_branch, preferred_element_type=jnp.float32
    )
    grad_heads = (
        jnp.einsum("td,cd->tc", grad_branch, wo_full, preferred_element_type=jnp.float32)
        .astype(jnp.bfloat16)
        .reshape(token_count, QH, HD)
    )
    grad_head_rows = lax.all_to_all(grad_heads, "seq", split_axis=1, concat_axis=0, tiled=True)
    grad_blocks = grad_head_rows.reshape(count, block, pair_count, group, HD)

    def backward_block(carry, items):
        key_acc, value_acc = carry
        query_block, index_block, start_block, grad_block, log_block = items
        scores = block_scores(query_block, index_block, start_block)
        probs = jnp.exp(scores - log_block)
        probs_low = probs.astype(jnp.bfloat16)
        grad_probs = jnp.einsum(
            "bkgd,tkd->kgbt", grad_block, value_all, preferred_element_type=jnp.float32
        )
        grad_scores = (
            probs * (grad_probs - jnp.sum(probs * grad_probs, -1, keepdims=True))
        ).astype(jnp.bfloat16)
        query_grad_block = (
            jnp.einsum("kgbt,tkd->bkgd", grad_scores, key_all, preferred_element_type=jnp.float32)
            * factor
        )
        key_acc = (
            key_acc
            + jnp.einsum(
                "kgbt,bkgd->tkd", grad_scores, query_block, preferred_element_type=jnp.float32
            )
            * factor
        )
        value_acc = value_acc + jnp.einsum(
            "kgbt,bkgd->tkd", probs_low, grad_block, preferred_element_type=jnp.float32
        )
        return ((key_acc, value_acc), query_grad_block.reshape(block, head_count, HD))

    empty = jnp.zeros((2 * half_len, pair_count, HD), jnp.float32)
    (key_acc, value_acc), query_grad_blocks = lax.scan(
        backward_block,
        (empty, empty),
        (query_blocks, index_blocks, start_blocks, grad_blocks, log_totals),
    )
    key_back, value_back = (
        shifted(key_acc[:half_len].astype(jnp.bfloat16), "fsdp", -1).astype(jnp.float32),
        shifted(value_acc[:half_len].astype(jnp.bfloat16), "fsdp", -1).astype(jnp.float32),
    )
    key_local = key_acc[half_len:] + key_back
    value_local = value_acc[half_len:] + value_back
    query_grad_heads = query_grad_blocks.reshape(half_len, head_count, HD)
    grad_query_tok, grad_key_tok, grad_value_tok = (
        lax.all_to_all(
            query_grad_heads.astype(jnp.bfloat16), "seq", split_axis=0, concat_axis=1, tiled=True
        ).astype(query_grad_heads.dtype),
        lax.all_to_all(
            key_local.astype(jnp.bfloat16), "seq", split_axis=0, concat_axis=1, tiled=True
        ).astype(key_local.dtype),
        lax.all_to_all(
            value_local.astype(jnp.bfloat16), "seq", split_axis=0, concat_axis=1, tiled=True
        ).astype(value_local.dtype),
    )
    if repeat > 1:
        grad_key_tok = grad_key_tok.reshape(token_count, KVH, repeat, HD).sum(2)
        grad_value_tok = grad_value_tok.reshape(token_count, KVH, repeat, HD).sum(2)
    query_lin_grad = (
        rotate_back(grad_query_tok, cosine, sine).astype(jnp.bfloat16).reshape(token_count, QH * HD)
    )
    key_lin_grad = (
        rotate_back(grad_key_tok, cosine, sine).astype(jnp.bfloat16).reshape(token_count, KVH * HD)
    )
    value_lin_grad = grad_value_tok.astype(jnp.bfloat16).reshape(token_count, KVH * HD)
    query_grad = jnp.einsum(
        "td,tc->dc", normed_low, query_lin_grad, preferred_element_type=jnp.float32
    )
    key_grad = jnp.einsum("td,tc->dc", normed_low, key_lin_grad, preferred_element_type=jnp.float32)
    value_grad = jnp.einsum(
        "td,tc->dc", normed_low, value_lin_grad, preferred_element_type=jnp.float32
    )
    grad_normed_one = jnp.einsum(
        "tc,dc->td", query_lin_grad, wq_full, preferred_element_type=jnp.float32
    )
    grad_normed_one = grad_normed_one + jnp.einsum(
        "tc,dc->td", key_lin_grad, wk_full, preferred_element_type=jnp.float32
    )
    grad_normed_one = grad_normed_one + jnp.einsum(
        "tc,dc->td", value_lin_grad, wv_full, preferred_element_type=jnp.float32
    )
    grad_rows_one, first_gain_grad = norm_backward(grad_normed_one, unit_one, scale_one, gain_one)
    input_grad = (grad_middle + grad_rows_one).astype(jnp.bfloat16)[None]
    pieces = (
        lax.psum_scatter(
            first_gain_grad.astype(jnp.bfloat16), "fsdp", scatter_dimension=0, tiled=True
        ).astype(jnp.float32),
        lax.psum_scatter(
            query_grad.astype(jnp.bfloat16), "fsdp", scatter_dimension=0, tiled=True
        ).astype(jnp.float32),
        lax.psum_scatter(
            key_grad.astype(jnp.bfloat16), "fsdp", scatter_dimension=0, tiled=True
        ).astype(jnp.float32),
        lax.psum_scatter(
            value_grad.astype(jnp.bfloat16), "fsdp", scatter_dimension=0, tiled=True
        ).astype(jnp.float32),
        lax.psum_scatter(
            output_grad.astype(jnp.bfloat16), "fsdp", scatter_dimension=0, tiled=True
        ).astype(jnp.float32),
        lax.psum_scatter(
            second_gain_grad.astype(jnp.bfloat16), "fsdp", scatter_dimension=0, tiled=True
        ).astype(jnp.float32),
        lax.psum_scatter(
            gate_grad.astype(jnp.bfloat16), "fsdp", scatter_dimension=0, tiled=True
        ).astype(jnp.float32),
        lax.psum_scatter(
            up_grad.astype(jnp.bfloat16), "fsdp", scatter_dimension=0, tiled=True
        ).astype(jnp.float32),
        lax.psum_scatter(
            down_grad.astype(jnp.bfloat16), "fsdp", scatter_dimension=0, tiled=True
        ).astype(jnp.float32),
    )
    shares = (
        lax.psum(pieces[0].astype(jnp.bfloat16), "seq").astype(jnp.float32),
        lax.psum(pieces[1].astype(jnp.bfloat16), "seq").astype(jnp.float32),
        lax.psum(pieces[2].astype(jnp.bfloat16), "seq").astype(jnp.float32),
        lax.psum(pieces[3].astype(jnp.bfloat16), "seq").astype(jnp.float32),
        lax.psum(pieces[4].astype(jnp.bfloat16), "seq").astype(jnp.float32),
        lax.psum(pieces[5].astype(jnp.bfloat16), "seq").astype(jnp.float32),
        lax.psum(pieces[6].astype(jnp.bfloat16), "seq").astype(jnp.float32),
        lax.psum(pieces[7].astype(jnp.bfloat16), "seq").astype(jnp.float32),
        lax.psum(pieces[8].astype(jnp.bfloat16), "seq").astype(jnp.float32),
    )
    return (
        block_output,
        input_grad,
        shares[0],
        shares[1],
        shares[2],
        shares[3],
        shares[4],
        shares[5],
        shares[6],
        shares[7],
        shares[8],
    )


def plain_solution(mesh):
    placed = (
        P("fsdp", "seq", None),
        P("fsdp", "seq"),
        P("fsdp"),
        P("fsdp", None),
        P("fsdp", None),
        P("fsdp", None),
        P("fsdp", None),
        P("fsdp"),
        P("fsdp", None),
        P("fsdp", None),
        P("fsdp", None),
        P("fsdp", "seq", None),
    )
    return jax.shard_map(
        plain_body,
        mesh=mesh,
        in_specs=placed,
        out_specs=(
            P("fsdp", "seq", None),
            P("fsdp", "seq", None),
            P("fsdp"),
            P("fsdp", None),
            P("fsdp", None),
            P("fsdp", None),
            P("fsdp", None),
            P("fsdp"),
            P("fsdp", None),
            P("fsdp", None),
            P("fsdp", None),
        ),
        check_vma=False,
    )
```

```python
import functools
import math

import jax
import jax.numpy as jnp
from jax import lax
from jax.experimental import pallas as pl
from jax.experimental.pallas import tpu as pltpu
from jax.sharding import Mesh
from jax.sharding import PartitionSpec as P

QH = 16
KVH = 8
HD = 96


THETA = 100000.0
EPS = 1e-05
LOW = jnp.bfloat16
F32 = jnp.float32
NEG = -1e30
LN2 = math.log(2.0)


def contract(left, right, left_axis, right_axis):
    return lax.dot_general(
        left, right, (((left_axis,), (right_axis,)), ((), ())), preferred_element_type=F32
    )


def visible(first, second, query_block, key_block, size):
    key = key_block * size + lax.broadcasted_iota(jnp.int32, (size, size), 0)
    query = query_block * size + lax.broadcasted_iota(jnp.int32, (1, size), 1)
    start = jnp.where(query >= second, second, jnp.where(query >= first, first, 0))
    return (key >= start) & (key <= query)


def slot_of(block, count):
    return (block % (count // 2)) * 2 + block // (count // 2)


def forward_kernel(
    scalars,
    rows_ref,
    low_ref,
    full_ref,
    log_ref,
    query_s,
    key_s,
    value_s,
    top_s,
    total_s,
    mixed_s,
    *,
    size,
    count,
):
    first = scalars[1]
    second = scalars[2]
    here = pl.program_id(0)

    @pl.when(here == 0)
    def _():
        for block in range(count):
            slot = slot_of(block, count)
            query_s[block] = rows_ref[slot, 0:HD]
            key_s[block] = rows_ref[slot, HD : 2 * HD].T
            value_s[block] = rows_ref[slot, 2 * HD : 3 * HD]

    query = query_s[here]
    top_s[...] = jnp.full_like(top_s, NEG)
    total_s[...] = jnp.zeros_like(total_s)
    mixed_s[...] = jnp.zeros_like(mixed_s)

    def add_block(block, masked):
        scores = contract(key_s[block], query, 1, 0)
        if masked:
            scores = jnp.where(visible(first, second, here, block, size), scores, NEG)
        old_top = top_s[...]
        top = jnp.maximum(old_top, jnp.max(scores, 0, keepdims=True))
        expo = jnp.exp2(scores - top)
        scale = jnp.exp2(old_top - top)
        top_s[...] = top
        total_s[...] = total_s[...] * scale + jnp.sum(expo, 0, keepdims=True)
        mixed_s[...] = mixed_s[...] * scale + contract(value_s[block], expo.astype(LOW), 1, 0)

    last = count - 1

    @pl.loop(1, jnp.where(here == last, 1, here))
    def _(block):
        add_block(block, False)

    @pl.loop(0, jnp.where(here == last, count, jnp.minimum(here + 1, 2)))
    def _(step):
        add_block(jnp.where(here == last, step, step * here), True)

    total = total_s[...]
    result = mixed_s[...] / total
    full_ref[0] = result
    low_ref[0] = result.astype(LOW)
    log_ref[0] = top_s[...] + jnp.log2(total)


def backward_kernel(
    scalars,
    rows_ref,
    grad_ref,
    full_ref,
    log_ref,
    kept_ref,
    leaving_ref,
    query_s,
    key_s,
    value_s,
    delta_s,
    query_grad_s,
    key_grad_s,
    value_grad_s,
    *,
    size,
    count,
):
    half = scalars[0]
    first = scalars[1]
    second = scalars[2]
    here = pl.program_id(0)
    per_half = count // 2

    @pl.when(here == 0)
    def _():
        for block in range(count):
            slot = slot_of(block, count)
            query_s[block] = rows_ref[slot, 0:HD]
            key_s[block] = rows_ref[slot, HD : 2 * HD]
            value_s[block] = rows_ref[slot, 2 * HD : 3 * HD].T
            delta_s[block] = jnp.sum(
                grad_ref[slot].astype(F32) * full_ref[block], 0, keepdims=True
            )
        query_grad_s[...] = jnp.zeros_like(query_grad_s)

    key_grad_s[...] = jnp.zeros_like(key_grad_s)
    value_grad_s[...] = jnp.zeros_like(value_grad_s)
    key = key_s[here]
    key_rows = key.T
    value_rows = value_s[here]

    def add_block(block, masked):
        query = query_s[block]
        grad = grad_ref[slot_of(block, count)]
        scores = contract(key_rows, query, 1, 0)
        if masked:
            scores = jnp.where(visible(first, second, block, here, size), scores, NEG)
        probs = jnp.exp2(scores - log_ref[block])
        grad_probs = contract(value_rows, grad, 1, 0)
        grad_scores = (probs * (grad_probs - delta_s[block])).astype(LOW)
        value_grad_s[...] += contract(grad, probs.astype(LOW), 1, 1)
        key_grad_s[...] += contract(query, grad_scores, 1, 1)
        query_grad_s[block] += contract(key, grad_scores, 1, 0)

    last = count - 1

    @pl.loop(here + 1, jnp.where(here == 0, 1, last))
    def _(block):
        add_block(block, False)

    @pl.loop(0, jnp.where(here == 0, count, jnp.where(here == last, 1, 2)))
    def _(step):
        add_block(jnp.where(here == 0, step, jnp.where(step == 0, here, last)), True)

    side = here // per_half
    columns = pl.ds(pl.multiple_of((here % per_half) * size, size), size)

    def write(out_ref):
        out_ref[0:HD, columns] = (query_grad_s[here] * HD**-0.5).astype(LOW)
        out_ref[HD : 2 * HD, columns] = (key_grad_s[...] * LN2).astype(LOW)
        out_ref[2 * HD : 3 * HD, columns] = value_grad_s[...].astype(LOW)

    @pl.when(side == half)
    def _():
        write(kept_ref)

    @pl.when(side != half)
    def _():
        write(leaving_ref)


def attend_forward(scalars, rows):
    count, _, size = rows.shape
    whole = lambda shape: pl.BlockSpec(shape, lambda i, s: (0,) * len(shape))
    pairs = count * (count + 1) // 2
    return pl.pallas_call(
        functools.partial(forward_kernel, size=size, count=count),
        grid_spec=pltpu.PrefetchScalarGridSpec(
            num_scalar_prefetch=1,
            grid=(count,),
            in_specs=[whole(rows.shape)],
            out_specs=[
                pl.BlockSpec(
                    (1, HD, size), lambda i, s: (slot_of(i, count), 0, 0)
                ),
                pl.BlockSpec((1, HD, size), lambda i, s: (i, 0, 0)),
                pl.BlockSpec((1, 1, size), lambda i, s: (i, 0, 0)),
            ],
            scratch_shapes=[
                pltpu.VMEM((count, HD, size), LOW),
                pltpu.VMEM((count, size, HD), LOW),
                pltpu.VMEM((count, HD, size), LOW),
                pltpu.VMEM((1, size), F32),
                pltpu.VMEM((1, size), F32),
                pltpu.VMEM((HD, size), F32),
            ],
        ),
        out_shape=[
            jax.ShapeDtypeStruct((count, HD, size), LOW),
            jax.ShapeDtypeStruct((count, HD, size), F32),
            jax.ShapeDtypeStruct((count, 1, size), F32),
        ],
        compiler_params=pltpu.CompilerParams(
            dimension_semantics=("arbitrary",), vmem_limit_bytes=32 * 2**20
        ),
        cost_estimate=pl.CostEstimate(
            flops=pairs * size * size * HD * 4,
            bytes_accessed=10 * 2**20,
            transcendentals=pairs * size * size,
        ),
        name="attend_forward",
    )(scalars, rows)


def attend_backward(scalars, rows, grad, full, log_total):
    count, _, size = rows.shape
    whole = lambda shape: pl.BlockSpec(shape, lambda i, s: (0,) * len(shape))
    pairs = count * (count + 1) // 2
    out_shape = (3 * HD, count // 2 * size)
    return pl.pallas_call(
        functools.partial(backward_kernel, size=size, count=count),
        grid_spec=pltpu.PrefetchScalarGridSpec(
            num_scalar_prefetch=1,
            grid=(count,),
            in_specs=[
                whole(rows.shape),
                whole(grad.shape),
                whole(full.shape),
                whole(log_total.shape),
            ],
            out_specs=[whole(out_shape)] * 2,
            scratch_shapes=[
                pltpu.VMEM((count, HD, size), LOW),
                pltpu.VMEM((count, HD, size), LOW),
                pltpu.VMEM((count, size, HD), LOW),
                pltpu.VMEM((count, 1, size), F32),
                pltpu.VMEM((count, HD, size), F32),
                pltpu.VMEM((HD, size), F32),
                pltpu.VMEM((HD, size), F32),
            ],
        ),
        out_shape=[jax.ShapeDtypeStruct(out_shape, LOW)] * 2,
        compiler_params=pltpu.CompilerParams(
            dimension_semantics=("arbitrary",), vmem_limit_bytes=32 * 2**20
        ),
        cost_estimate=pl.CostEstimate(
            flops=pairs * size * size * HD * 10,
            bytes_accessed=16 * 2**20,
            transcendentals=pairs * size * size,
        ),
        name="attend_backward",
    )(scalars, rows, grad, full, log_total)


def place_rows_kernel(order, *refs):
    pieces, out_ref = refs[:-1], refs[-1]
    size = pieces[0].shape[0]
    for index, piece in enumerate(pieces):
        start = pl.multiple_of(order[index] * size, size)
        out_ref[pl.ds(start, size), :] = piece[...].astype(F32)


def place_rows(order, pieces):
    size, width = pieces[0].shape
    total = size * len(pieces)
    step = 512
    return pl.pallas_call(
        place_rows_kernel,
        grid_spec=pltpu.PrefetchScalarGridSpec(
            num_scalar_prefetch=1,
            grid=(width // step,),
            in_specs=[pl.BlockSpec((size, step), lambda i, s: (0, i)) for _ in pieces],
            out_specs=pl.BlockSpec((total, step), lambda i, s: (0, i)),
        ),
        out_shape=jax.ShapeDtypeStruct((total, width), F32),
        compiler_params=pltpu.CompilerParams(vmem_limit_bytes=24 * 2**20),
        cost_estimate=pl.CostEstimate(
            flops=0, bytes_accessed=total * width * 6, transcendentals=0
        ),
        name="place_rows",
    )(order, *pieces)


def place_columns_kernel(order, gain_ref, gate_w_ref, up_w_ref, *refs):
    count = (len(refs) - 3) // 2
    gates, ups = refs[:count], refs[count : 2 * count]
    gate_ref, up_ref, sum_ref = refs[2 * count :]
    size = gates[0].shape[1]
    gain = gain_ref[...]
    total = jnp.zeros((gate_ref.shape[0], size), F32)
    for index in range(count):
        columns = pl.ds(pl.multiple_of(order[index] * size, size), size)
        gate, up = gates[index][...].astype(F32), ups[index][...].astype(F32)
        total += gate * gate_w_ref[:, columns].astype(F32)
        total += up * up_w_ref[:, columns].astype(F32)
        gate_ref[:, columns] = gate * gain
        up_ref[:, columns] = up * gain

    @pl.when(pl.program_id(0) == 0)
    def _():
        sum_ref[...] = jnp.zeros_like(sum_ref)

    sum_ref[...] += jnp.sum(total, 1, keepdims=True)


def place_columns(order, gain, gate_weight, up_weight, gates, ups, shards):
    rows, width = gate_weight.shape
    span = width // shards
    size = span // len(gates)
    wide = pl.BlockSpec((rows, span), lambda i, s: (0, i))
    thin = pl.BlockSpec((rows, 1), lambda i, s: (0, 0))
    pieces = [pl.BlockSpec((rows, size), lambda i, s: (0, i)) for _ in (*gates, *ups)]
    return pl.pallas_call(
        place_columns_kernel,
        grid_spec=pltpu.PrefetchScalarGridSpec(
            num_scalar_prefetch=1,
            grid=(shards,),
            in_specs=[thin, wide, wide, *pieces],
            out_specs=[wide, wide, thin],
        ),
        out_shape=[
            jax.ShapeDtypeStruct((rows, width), F32),
            jax.ShapeDtypeStruct((rows, width), F32),
            jax.ShapeDtypeStruct((rows, 1), F32),
        ],
        compiler_params=pltpu.CompilerParams(
            dimension_semantics=("arbitrary",), vmem_limit_bytes=24 * 2**20
        ),
        cost_estimate=pl.CostEstimate(
            flops=rows * width * 6, bytes_accessed=rows * width * 16, transcendentals=0
        ),
        name="place_columns",
    )(order, gain, gate_weight, up_weight, *gates, *ups)


def place_heads_kernel(gain_ref, query_w, key_w, value_w, all_ref, query_ref, key_ref, value_ref, sum_ref):
    rows = gain_ref.shape[0]
    wide = query_ref.shape[1] // KVH
    gain = gain_ref[...]
    total = jnp.zeros((rows, 4 * HD), F32)
    pieces = [all_ref[i * rows : (i + 1) * rows, :].astype(F32) for i in range(KVH)]
    for start in range(0, KVH, 2):
        value = jnp.concatenate([piece[:, :wide] for piece in pieces[start : start + 2]], 1)
        columns = slice(start * wide, (start + 2) * wide)
        total += value * query_w[:, columns].astype(F32)
        query_ref[:, columns] = value * gain
    for first, weight, out_ref in ((wide, key_w, key_ref), (wide + HD, value_w, value_ref)):
        for start in range(0, KVH, 4):
            value = jnp.concatenate(
                [piece[:, first : first + HD] for piece in pieces[start : start + 4]], 1
            )
            columns = slice(start * HD, (start + 4) * HD)
            total += value * weight[:, columns].astype(F32)
            out_ref[:, columns] = value * gain
    sum_ref[...] = jnp.sum(total, 1, keepdims=True)


def place_heads(gain, query_weight, key_weight, value_weight, pieces):
    weights = (query_weight, key_weight, value_weight)
    rows = gain.shape[0]
    return pl.pallas_call(
        place_heads_kernel,
        out_shape=[jax.ShapeDtypeStruct(weight.shape, F32) for weight in weights]
        + [jax.ShapeDtypeStruct((rows, 1), F32)],
        compiler_params=pltpu.CompilerParams(vmem_limit_bytes=32 * 2**20),
        cost_estimate=pl.CostEstimate(
            flops=rows * 3072 * 4, bytes_accessed=rows * 3072 * 8, transcendentals=0
        ),
        name="place_heads",
    )(gain, *weights, pieces)


def merge_kernel(scalars, kept_ref, came_ref, cosine_ref, sine_ref, scale_ref, out_ref, split_ref):
    lead = scalars[0] == 0
    lines, _, size = split_ref.shape
    for line in range(lines):
        columns = slice(line * size, (line + 1) * size)
        kept = kept_ref[:, columns].astype(F32)
        came = came_ref[:, columns].astype(F32)
        cosine, sine, scale = cosine_ref[:, columns], sine_ref[:, columns], scale_ref[:, columns]
        joint = kept[HD:] + came[HD:]
        first = jnp.where(lead, kept[:HD], came[:HD])
        second = jnp.where(lead, came[:HD], kept[:HD])
        turned = []
        for value in (first, second, joint[:HD]):
            low, high = value[: HD // 2], value[HD // 2 :]
            turned.append((low * cosine + high * sine) * scale)
            turned.append((high * cosine - low * sine) * scale)
        turned.append(joint[HD:] * scale)
        result = jnp.concatenate([part.astype(LOW) for part in turned], 0)
        out_ref[:, columns] = result
        split_ref[line] = result


def merge(scalars, kept, came, cosine, sine, scale, lines):
    tokens = kept.shape[1]
    whole = lambda value: pl.BlockSpec(value.shape, lambda i, s: (0,) * len(value.shape))
    outs = [
        jax.ShapeDtypeStruct((4 * HD, tokens), LOW),
        jax.ShapeDtypeStruct((lines, 4 * HD, tokens // lines), LOW),
    ]
    return pl.pallas_call(
        merge_kernel,
        grid_spec=pltpu.PrefetchScalarGridSpec(
            num_scalar_prefetch=1,
            grid=(1,),
            in_specs=[whole(value) for value in (kept, came, cosine, sine, scale)],
            out_specs=[whole(value) for value in outs],
        ),
        out_shape=outs,
        compiler_params=pltpu.CompilerParams(vmem_limit_bytes=24 * 2**20),
        cost_estimate=pl.CostEstimate(
            flops=tokens * HD * 24, bytes_accessed=tokens * HD * 30, transcendentals=0
        ),
        name="merge",
    )(scalars, kept, came, cosine, sine, scale)


def pack_kernel(scalars, gain_ref, query_ref, key_ref, value_ref, *outs):
    core = scalars[3]
    gain = gain_ref[...]
    wide = query_ref.shape[1] // KVH
    span = wide + 2 * HD
    for which in range(2):

        @pl.when(core == which)
        def _():
            for line in range(KVH // 2):
                head = 2 * line + which
                value = jnp.concatenate(
                    [
                        query_ref[:, head * wide : (head + 1) * wide].astype(F32),
                        key_ref[:, head * HD : (head + 1) * HD].astype(F32),
                        value_ref[:, head * HD : (head + 1) * HD].astype(F32),
                    ],
                    1,
                )
                place = (line % 2) * span
                outs[line // 2][:, place : place + span] = (value * gain).astype(LOW)


def pack(scalars, gain, query_weight, key_weight, value_weight):
    rows, width = query_weight.shape
    whole = lambda value: pl.BlockSpec(value.shape, lambda i, s: (0, 0))
    weights = (gain, query_weight, key_weight, value_weight)
    outs = [jax.ShapeDtypeStruct((rows, width // 2), LOW)] * 2
    return pl.pallas_call(
        pack_kernel,
        grid_spec=pltpu.PrefetchScalarGridSpec(
            num_scalar_prefetch=1,
            grid=(1,),
            in_specs=[whole(value) for value in weights],
            out_specs=[whole(value) for value in outs],
        ),
        out_shape=outs,
        compiler_params=pltpu.CompilerParams(vmem_limit_bytes=24 * 2**20),
        cost_estimate=pl.CostEstimate(
            flops=rows * width, bytes_accessed=rows * width * 6, transcendentals=0
        ),
        name="pack",
    )(scalars, *weights)


def spread_kernel(lead_ref, tail_ref, cosine_ref, sine_ref, scale_ref, out_ref):
    cosine, sine, scale = cosine_ref[...], sine_ref[...], scale_ref[...]
    span = 4 * HD

    def turn(value, factor):
        low, high = value[: HD // 2], value[HD // 2 :]
        return jnp.concatenate(
            [
                ((low * cosine - high * sine) * (scale * factor)).astype(LOW),
                ((high * cosine + low * sine) * (scale * factor)).astype(LOW),
            ],
            0,
        )

    for line in range(out_ref.shape[0] // 2):
        source = (lead_ref, tail_ref)[line // 2]
        base = (line % 2) * span
        key = turn(source[base + 2 * HD : base + 3 * HD], 1.0)
        value = (source[base + 3 * HD : base + 4 * HD] * scale).astype(LOW)
        for which in range(2):
            query = source[base + which * HD : base + (which + 1) * HD]
            out_ref[2 * line + which, 0:HD] = turn(query, HD**-0.5 / LN2)
            out_ref[2 * line + which, HD : 2 * HD] = key
            out_ref[2 * line + which, 2 * HD : 3 * HD] = value


def spread(lead, tail, cosine, sine, scale):
    tokens = lead.shape[1]
    return pl.pallas_call(
        spread_kernel,
        out_shape=jax.ShapeDtypeStruct((KVH, 3 * HD, tokens), LOW),
        compiler_params=pltpu.CompilerParams(vmem_limit_bytes=24 * 2**20),
        cost_estimate=pl.CostEstimate(
            flops=tokens * HD * 100, bytes_accessed=tokens * HD * 120, transcendentals=0
        ),
        name="spread",
    )(lead, tail, cosine, sine, scale)


def swap(value, axis):
    return lax.ppermute(value, axis, [(0, 1), (1, 0)])


def swap_near(value):
    return lax.ppermute(value, "z", [(0, 1), (1, 0), (2, 3), (3, 2)])


def swap_far(value):
    return lax.ppermute(value, "z", [(0, 2), (2, 0), (1, 3), (3, 1)])


def line_sum(part, axis):
    place = lax.axis_index(axis)
    inner = (place == 1) | (place == 2)
    part = part + lax.ppermute(part, axis, [(0, 1), (3, 2)])
    part = part + lax.ppermute(part, axis, [(1, 2), (2, 1)])
    outer = lax.ppermute(part, axis, [(1, 0), (2, 3)])
    return jnp.where(inner, part, outer)


def in_order(place, own, other):
    return (jnp.where(place == 0, own, other), jnp.where(place == 0, other, own))


def both(place, own, other):
    return jnp.concatenate(in_order(place, own, other), 0)


def spread_out(value, first, second):
    other = swap(value, first)
    pair = jnp.stack(in_order(lax.axis_index(first), value, other))
    return pair, swap(pair, second)


def placed(pair, other, second):
    pairs = in_order(lax.axis_index(second), pair, other)
    grid = jnp.stack(pairs, 0 if second == "y" else 1)
    return grid.reshape(-1, *grid.shape[3:])


def halving(value, first, second):
    grid = value.reshape(2, 2, -1, value.shape[-1])
    pick = lambda array, axis, at: lax.dynamic_index_in_dim(array, at, axis, keepdims=False)
    at = lax.axis_index(first)
    which = 0 if first == "y" else 1
    pair = pick(grid, which, at) + swap(pick(grid, which, 1 - at), first)
    at = lax.axis_index(second)
    return pick(pair, 0, at) + swap(pick(pair, 0, 1 - at), second)


def fast_body(
    tokens,
    positions,
    first_gain,
    query_weight,
    key_weight,
    value_weight,
    output_weight,
    second_gain,
    gate_weight,
    up_weight,
    down_weight,
    cotangent,
):
    seq = ("z", "c")
    fsdp = ("y", "x")
    z, core, half = lax.axis_index("z"), lax.axis_index("c"), lax.axis_index("x")
    near = z % 2
    lines = lax.axis_size("z")
    seq_count = 2 * lines
    shards = lax.axis_size("y") * 2
    spot = z * 2 + core
    quarter = near * 2 + core
    rows = tokens[0]
    count, width = rows.shape
    chip_count = 2 * count
    half_len = count * seq_count
    seq_len = 2 * half_len

    begins = jnp.where(
        (spot == 0) & (half == 0),
        count - 1 - positions[0, count - 1],
        half * half_len + spot * count - positions[0, 0],
    )
    ends = begins + (seq_len - count)
    scalars = jnp.stack([half, begins, ends, core]).astype(jnp.int32)

    gain_one = first_gain.astype(F32)[:, None]
    gain_two = second_gain.astype(F32)[:, None]

    take = functools.partial(lax.dynamic_slice_in_dim, axis=1)
    take_rows = functools.partial(lax.dynamic_slice_in_dim, axis=0)
    gather = lambda value, axes: lax.all_gather(value, axes, axis=0, tiled=True)
    lead_shard, tail_shard = pack(scalars, gain_one, query_weight, key_weight, value_weight)
    lead_parts = spread_out(lead_shard, "x", "y")
    tail_parts = spread_out(tail_shard, "y", "x")
    all_rows = gather(rows, seq)
    out_rows = output_weight.shape[0] // 2
    out_shard = take_rows(output_weight, core * out_rows, out_rows)
    piece = down_weight.shape[0] // 4
    down_shard = take_rows(down_weight, quarter * piece, piece)
    gate_shard, up_shard = (
        (
            jnp.concatenate(
                [
                    take(weight, shard * 4 * piece + quarter * piece, piece)
                    for shard in range(shards)
                ],
                1,
            ).astype(F32)
            * gain_two
        ).astype(LOW)
        for weight in (gate_weight, up_weight)
    )

    chip_rows = both(core, rows, swap(rows, "c"))
    chip_cot = both(core, cotangent[0], swap(cotangent[0], "c"))
    near_cot = swap_near(cotangent[0])
    near_cot = jnp.concatenate([near_cot, swap(near_cot, "c")], 0)
    lead_parts, tail_parts, gate_shard, up_shard, chip_rows, chip_cot, near_cot = (
        lax.optimization_barrier(
            (lead_parts, tail_parts, gate_shard, up_shard, chip_rows, chip_cot, near_cot)
        )
    )
    lead_w, tail_w = placed(*lead_parts, "y"), placed(*tail_parts, "x")
    gate_parts = spread_out(gate_shard, "x", "y")
    up_parts = spread_out(up_shard, "y", "x")

    def row_scale(value):
        return lax.rsqrt(jnp.mean(value * value, -1, keepdims=True) + EPS)

    place = half * half_len + jnp.arange(half_len, dtype=jnp.int32)
    start = jnp.where(place >= ends, ends, jnp.where(place >= begins, begins, 0))
    freq = THETA ** (-(jnp.arange(HD // 2, dtype=F32) * 2.0 / HD))
    angle = freq[:, None] * (place - start).astype(F32)[None, :]
    cosine, sine = jnp.cos(angle), jnp.sin(angle)
    ours = lambda value: take(value, z * chip_count, chip_count)
    scale_chip = row_scale(chip_rows.astype(F32)).reshape(1, chip_count)
    leaving = spread(
        contract(lead_w, chip_rows, 0, 1),
        contract(tail_w, chip_rows, 0, 1),
        ours(cosine),
        ours(sine),
        scale_chip,
    )
    exchange = lambda value: lax.all_to_all(
        value, ("z", "x"), split_axis=0, concat_axis=0, tiled=True
    )
    all_rows, out_shard = lax.optimization_barrier((all_rows, out_shard))
    out_w = gather(out_shard, fsdp)
    head_rows, down_shard, gate_pair, up_pair = lax.optimization_barrier(
        (exchange(leaving), down_shard, gate_parts[0], up_parts[0])
    )
    gate_parts, up_parts = (gate_pair, gate_parts[1]), (up_pair, up_parts[1])
    down_w = gather(down_shard, fsdp)

    head_low, head_full, log_total = attend_forward(scalars, head_rows)
    head_low, gate_parts, up_parts = lax.optimization_barrier((head_low, gate_parts, up_parts))
    heads = exchange(head_low).reshape(QH // 2 * HD, chip_count)

    mine_of = lambda value: take_rows(value, core * count, count)
    theirs_of = lambda value: take_rows(value, (1 - core) * count, count)
    branch = contract(heads, out_w, 0, 0).astype(LOW)
    gate_w, up_w = placed(*gate_parts, "y"), placed(*up_parts, "x")
    middle = chip_rows.astype(F32) + (branch.astype(F32) + swap(branch, "c").astype(F32))
    own_middle = mine_of(middle)
    middle_low = middle.astype(LOW)
    near_middle = swap_near(mine_of(middle_low))
    near_middle = jnp.concatenate([near_middle, swap(near_middle, "c")], 0)

    def feed(low, scale):
        gate, upper = contract(low, gate_w, 1, 0) * scale, contract(low, up_w, 1, 0) * scale
        sigma = jax.nn.sigmoid(gate)
        silu = gate * sigma
        return (silu * upper).astype(LOW), (gate, upper, sigma, silu)

    def feed_back(cot, scale, kept):
        gate, upper, sigma, silu = kept
        grad_hidden = contract(cot, down_w, 1, 1) * scale
        gate_low = (grad_hidden * upper * sigma * (1.0 + gate * (1.0 - sigma))).astype(LOW)
        upper_low = (grad_hidden * silu).astype(LOW)
        part = contract(gate_low, gate_w, 1, 1) + contract(upper_low, up_w, 1, 1)
        return gate_low, upper_low, part

    chip_scale = row_scale(middle)
    near_scale = row_scale(near_middle.astype(F32))
    chip_hidden, chip_kept = feed(middle_low, chip_scale)
    near_hidden, near_kept = feed(near_middle, near_scale)
    stack = lambda first, second: jnp.concatenate([first, second], 0)
    down_part = contract(
        stack(chip_hidden, near_hidden), stack(chip_cot, near_cot), 0, 0
    ).astype(LOW)
    near_cot, down_part = lax.optimization_barrier((near_cot, down_part))
    near_gate, near_upper, near_part = feed_back(near_cot, near_scale, near_kept)
    chip_gate, chip_upper, chip_part = feed_back(chip_cot, chip_scale, chip_kept)

    def own_sum(chip_part, near_part):
        near_sum = near_part[:count].astype(F32) + swap(near_part[count:].astype(LOW), "c")
        came = swap_near(near_sum.astype(LOW))
        chip_sum = mine_of(chip_part).astype(F32) + swap(theirs_of(chip_part).astype(LOW), "c")
        return chip_sum + came.astype(F32)

    grad_two = own_sum(chip_part, near_part)
    all_middle = stack(middle_low, near_middle)
    gate_part = contract(all_middle, stack(chip_gate, near_gate), 0, 0).astype(LOW)
    up_part = contract(all_middle, stack(chip_upper, near_upper), 0, 0).astype(LOW)
    grad_two, gate_part, up_part = lax.optimization_barrier((grad_two, gate_part, up_part))
    own_scale = mine_of(chip_scale)
    grad_middle = (
        cotangent[0].astype(F32)
        + grad_two
        - own_middle * (own_scale * own_scale * jnp.mean(grad_two * own_middle, -1, keepdims=True))
    )
    own_branch = grad_middle.astype(LOW)
    grad_branch = both(core, own_branch, swap(own_branch, "c"))
    grad_heads = contract(out_w, grad_branch, 1, 1).astype(LOW)

    output_part = contract(heads, grad_branch, 1, 0).astype(LOW)

    scatter = lambda value, axes: lax.psum_scatter(
        value.astype(LOW), axes, scatter_dimension=0, tiled=True
    )
    down_grad = scatter(down_part, fsdp)
    gate_grad = halving(gate_part, "x", "y")
    up_grad = halving(up_part, "y", "x")
    output_grad = scatter(output_part, fsdp)
    grad_head = exchange(grad_heads.reshape(2 * lines, HD, chip_count))
    grad_head, down_grad, output_part = lax.optimization_barrier(
        (grad_head, down_grad, output_part)
    )

    def far_sum(value):
        return value + swap_far(value)

    def with_near(value):
        return value, swap_near(value)

    def four(value, near_value):
        return value, swap(value, "c"), near_value, swap(near_value, "c")

    kept, leaving = attend_backward(scalars, head_rows, grad_head, head_full, log_total)
    down_sum = far_sum(down_grad)
    leaving, down_sum, gate_grad, up_grad = lax.optimization_barrier(
        (leaving, down_sum, gate_grad, up_grad)
    )
    gate_sum = far_sum(gate_grad)
    came = swap(leaving, "x")
    down_pair = with_near(down_sum)
    came, gate_sum, down_pair = lax.optimization_barrier((came, gate_sum, down_pair))
    up_sum = far_sum(up_grad)
    rows_float = all_rows.astype(F32)
    scale_one = row_scale(rows_float).reshape(1, half_len)
    qkv_low, by_line = merge(scalars, kept, came, cosine, sine, scale_one, lines)
    qkv_part = contract(all_rows, qkv_low, 0, 1).astype(LOW).reshape(2, 2, 2, -1, 4 * HD)
    qkv_grad = jnp.concatenate(
        [halving(qkv_part[:, :, 0], "x", "y"), halving(qkv_part[:, :, 1], "y", "x")], 0
    )
    token_grads = lax.all_to_all(by_line, "z", split_axis=0, concat_axis=0, tiled=True)
    token_grads = token_grads.reshape(-1, chip_count)
    gate_pair = with_near(gate_sum)
    token_grads, qkv_part, up_sum, gate_pair = lax.optimization_barrier(
        (token_grads, qkv_part, up_sum, gate_pair)
    )
    split = lead_w.shape[1]
    grad_one = contract(token_grads[:split], lead_w, 0, 1) + contract(
        token_grads[split:], tail_w, 0, 1
    )
    grad_one = mine_of(grad_one) + swap(theirs_of(grad_one).astype(LOW), "c").astype(F32)
    own_rows = rows.astype(F32)
    own_scale = row_scale(own_rows)
    input_grad = (
        grad_middle
        + grad_one
        - own_rows * (own_scale * own_scale * jnp.mean(grad_one * own_rows, -1, keepdims=True))
    ).astype(LOW)[None]

    feed_sum = own_sum(contract(chip_hidden, down_w, 1, 0), contract(near_hidden, down_w, 1, 0))
    block_output = (own_middle + feed_sum).astype(LOW)[None]

    order = jnp.stack([quarter, quarter ^ 1, quarter ^ 2, quarter ^ 3]).astype(jnp.int32)
    core_order = jnp.stack([core, 1 - core]).astype(jnp.int32)
    down_total = place_rows(order, four(*down_pair))
    output_own = line_sum(output_grad, "z")
    output_total = place_rows(core_order, (output_own, swap(output_own, "c")))
    gate_total, up_total, second_gain_grad = place_columns(
        order, gain_two, gate_weight, up_weight, four(*gate_pair), four(*with_near(up_sum)), shards
    )
    query_grad, key_grad, value_grad, first_gain_grad = place_heads(
        gain_one, query_weight, key_weight, value_weight, gather(qkv_grad, seq)
    )
    return (
        block_output,
        input_grad,
        first_gain_grad[:, 0],
        query_grad,
        key_grad,
        value_grad,
        output_total,
        second_gain_grad[:, 0],
        gate_total,
        up_total,
        down_total,
    )


def fast_solution(mesh):
    seq_count, shard_count = mesh.devices.shape
    fine = Mesh(
        mesh.devices.reshape(seq_count // 2, 2, shard_count // 2, 2), ("z", "c", "y", "x")
    )
    seq, fsdp = ("z", "c"), ("y", "x")
    matrix = P(fsdp, None)
    return jax.shard_map(
        fast_body,
        mesh=fine,
        in_specs=(
            P(fsdp, seq, None),
            P(fsdp, seq),
            P(fsdp),
            matrix,
            matrix,
            matrix,
            matrix,
            P(fsdp),
            matrix,
            matrix,
            matrix,
            P(fsdp, seq, None),
        ),
        out_specs=(
            P(fsdp, seq, None),
            P(fsdp, seq, None),
            P(fsdp),
            matrix,
            matrix,
            matrix,
            matrix,
            P(fsdp),
            matrix,
            matrix,
            matrix,
        ),
        check_vma=False,
    )


def solution(mesh):
    shape = dict(mesh.shape)
    if shape["seq"] == KVH and shape["fsdp"] == 4:
        return fast_solution(mesh)
    return plain_solution(mesh)


def shifted(value, axis, steps):
    count = lax.axis_size(axis)
    first, last = (max(0, -steps), min(count, count - steps))
    return lax.ppermute(value, axis, [(source, source + steps) for source in range(first, last)])


def rope_tables(position_rows):
    freq = THETA ** (-(jnp.arange(HD // 2, dtype=jnp.float32) * 2.0 / HD))
    angle = position_rows.astype(jnp.float32)[:, None] * freq[None, :]
    cosine = jnp.cos(angle)
    sine = jnp.sin(angle)
    return (jnp.concatenate([cosine, cosine], -1), jnp.concatenate([sine, sine], -1))


def rotate(values, cosine, sine):
    half = HD // 2
    turned = jnp.concatenate([-values[..., half:], values[..., :half]], -1)
    return values * cosine[:, None, :] + turned * sine[:, None, :]


def rotate_back(grads, cosine, sine):
    half = HD // 2
    scaled = grads * sine[:, None, :]
    turned = jnp.concatenate([scaled[..., half:], -scaled[..., :half]], -1)
    return grads * cosine[:, None, :] + turned


def norm_forward(rows, gain):
    scale = lax.rsqrt(jnp.mean(rows * rows, -1, keepdims=True) + EPS)
    unit = rows * scale
    return (unit * gain, unit, scale)


def norm_backward(grad_out, unit, scale, gain):
    grad_unit = grad_out * gain
    gain_grad = jnp.sum(grad_out * unit, 0)
    grad_rows = scale * (grad_unit - unit * jnp.mean(grad_unit * unit, -1, keepdims=True))
    return (grad_rows, gain_grad)


def plain_body(
    tokens,
    positions,
    first_gain,
    query_weight,
    key_weight,
    value_weight,
    output_weight,
    second_gain,
    gate_weight,
    up_weight,
    down_weight,
    cotangent,
):
    seq_count = lax.axis_size("seq")
    local_rows = tokens[0]
    token_count = local_rows.shape[0]
    half_len = token_count * seq_count
    rows_float = local_rows.astype(jnp.float32)
    gain_one, wq_full, wk_full, wv_full, wo_full = (
        lax.all_gather(first_gain, "fsdp", axis=0, tiled=True),
        lax.all_gather(query_weight, "fsdp", axis=0, tiled=True),
        lax.all_gather(key_weight, "fsdp", axis=0, tiled=True),
        lax.all_gather(value_weight, "fsdp", axis=0, tiled=True),
        lax.all_gather(output_weight, "fsdp", axis=0, tiled=True),
    )
    gain_one = gain_one.astype(jnp.float32)
    normed_one, unit_one, scale_one = norm_forward(rows_float, gain_one)
    normed_low = normed_one.astype(jnp.bfloat16)
    cosine, sine = rope_tables(positions[0])
    query_lin = jnp.dot(normed_low, wq_full, preferred_element_type=jnp.float32).reshape(
        token_count, QH, HD
    )
    key_lin = jnp.dot(normed_low, wk_full, preferred_element_type=jnp.float32).reshape(
        token_count, KVH, HD
    )
    value_lin = jnp.dot(normed_low, wv_full, preferred_element_type=jnp.float32).reshape(
        token_count, KVH, HD
    )
    query_rows = rotate(query_lin, cosine, sine).astype(jnp.bfloat16)
    key_rows = rotate(key_lin, cosine, sine).astype(jnp.bfloat16)
    value_rows = value_lin.astype(jnp.bfloat16)
    repeat = max(1, seq_count // KVH)
    if repeat > 1:
        key_rows = jnp.repeat(key_rows, repeat, axis=1)
        value_rows = jnp.repeat(value_rows, repeat, axis=1)
    query_heads, key_heads, value_heads = (
        lax.all_to_all(query_rows, "seq", split_axis=1, concat_axis=0, tiled=True),
        lax.all_to_all(key_rows, "seq", split_axis=1, concat_axis=0, tiled=True),
        lax.all_to_all(value_rows, "seq", split_axis=1, concat_axis=0, tiled=True),
    )
    head_count = query_heads.shape[1]
    pair_count = key_heads.shape[1]
    group = head_count // pair_count
    half_positions = lax.all_gather(positions[0], "seq", axis=0, tiled=True)
    key_prior, value_prior = shifted((key_heads, value_heads), "fsdp", 1)
    key_all = jnp.concatenate([key_prior, key_heads], 0)
    value_all = jnp.concatenate([value_prior, value_heads], 0)
    half_index = lax.axis_index("fsdp") % 2
    key_index = (half_index - 1) * half_len + jnp.arange(2 * half_len, dtype=jnp.int32)
    row_index = half_index * half_len + jnp.arange(half_len, dtype=jnp.int32)
    row_start = row_index - half_positions
    block = min(512, half_len)
    count = half_len // block
    factor = HD ** (-0.5)
    query_blocks = query_heads.reshape(count, block, pair_count, group, HD)
    index_blocks = row_index.reshape(count, block)
    start_blocks = row_start.reshape(count, block)

    def block_scores(query_block, index_block, start_block):
        scores = (
            jnp.einsum("bkgd,tkd->kgbt", query_block, key_all, preferred_element_type=jnp.float32)
            * factor
        )
        visible = (key_index[None, :] >= start_block[:, None]) & (
            key_index[None, :] <= index_block[:, None]
        )
        return jnp.where(visible, scores, -1e30)

    def forward_block(items):
        query_block, index_block, start_block = items
        scores = block_scores(query_block, index_block, start_block)
        top = jnp.max(scores, -1, keepdims=True)
        expo = jnp.exp(scores - top)
        total = jnp.sum(expo, -1, keepdims=True)
        probs_low = (expo / total).astype(jnp.bfloat16)
        mixed = jnp.einsum(
            "kgbt,tkd->bkgd", probs_low, value_all, preferred_element_type=jnp.float32
        )
        return (mixed.reshape(block, head_count, HD).astype(jnp.bfloat16), top + jnp.log(total))

    head_blocks, log_totals = lax.map(forward_block, (query_blocks, index_blocks, start_blocks))
    head_out = head_blocks.reshape(half_len, head_count, HD)
    token_heads = lax.all_to_all(head_out, "seq", split_axis=0, concat_axis=1, tiled=True)
    heads_flat = token_heads.reshape(token_count, QH * HD)
    middle = rows_float + jnp.dot(heads_flat, wo_full, preferred_element_type=jnp.float32)
    gain_two, wg_full, wu_full, wd_full = (
        lax.all_gather(second_gain, "fsdp", axis=0, tiled=True),
        lax.all_gather(gate_weight, "fsdp", axis=0, tiled=True),
        lax.all_gather(up_weight, "fsdp", axis=0, tiled=True),
        lax.all_gather(down_weight, "fsdp", axis=0, tiled=True),
    )
    gain_two = gain_two.astype(jnp.float32)
    normed_two, unit_two, scale_two = norm_forward(middle, gain_two)
    normed_two_low = normed_two.astype(jnp.bfloat16)
    gate = jnp.dot(normed_two_low, wg_full, preferred_element_type=jnp.float32)
    upper = jnp.dot(normed_two_low, wu_full, preferred_element_type=jnp.float32)
    hidden = (jax.nn.silu(gate) * upper).astype(jnp.bfloat16)
    result = middle + jnp.dot(hidden, wd_full, preferred_element_type=jnp.float32)
    block_output = result.astype(jnp.bfloat16)[None]
    grad_low = cotangent[0]
    grad_rows = grad_low.astype(jnp.float32)
    down_grad = jnp.einsum("tf,td->fd", hidden, grad_low, preferred_element_type=jnp.float32)
    grad_hidden = jnp.einsum("td,fd->tf", grad_low, wd_full, preferred_element_type=jnp.float32)
    sigma = jax.nn.sigmoid(gate)
    gate_low = (grad_hidden * upper * sigma * (1.0 + gate * (1.0 - sigma))).astype(jnp.bfloat16)
    upper_low = (grad_hidden * gate * sigma).astype(jnp.bfloat16)
    gate_grad = jnp.einsum(
        "td,tf->df", normed_two_low, gate_low, preferred_element_type=jnp.float32
    )
    up_grad = jnp.einsum("td,tf->df", normed_two_low, upper_low, preferred_element_type=jnp.float32)
    grad_normed_two = jnp.einsum(
        "tf,df->td", gate_low, wg_full, preferred_element_type=jnp.float32
    ) + jnp.einsum("tf,df->td", upper_low, wu_full, preferred_element_type=jnp.float32)
    grad_middle_norm, second_gain_grad = norm_backward(
        grad_normed_two, unit_two, scale_two, gain_two
    )
    grad_middle = grad_rows + grad_middle_norm
    grad_branch = grad_middle.astype(jnp.bfloat16)
    output_grad = jnp.einsum(
        "tc,td->cd", heads_flat, grad_branch, preferred_element_type=jnp.float32
    )
    grad_heads = (
        jnp.einsum("td,cd->tc", grad_branch, wo_full, preferred_element_type=jnp.float32)
        .astype(jnp.bfloat16)
        .reshape(token_count, QH, HD)
    )
    grad_head_rows = lax.all_to_all(grad_heads, "seq", split_axis=1, concat_axis=0, tiled=True)
    grad_blocks = grad_head_rows.reshape(count, block, pair_count, group, HD)

    def backward_block(carry, items):
        key_acc, value_acc = carry
        query_block, index_block, start_block, grad_block, log_block = items
        scores = block_scores(query_block, index_block, start_block)
        probs = jnp.exp(scores - log_block)
        probs_low = probs.astype(jnp.bfloat16)
        grad_probs = jnp.einsum(
            "bkgd,tkd->kgbt", grad_block, value_all, preferred_element_type=jnp.float32
        )
        grad_scores = (
            probs * (grad_probs - jnp.sum(probs * grad_probs, -1, keepdims=True))
        ).astype(jnp.bfloat16)
        query_grad_block = (
            jnp.einsum("kgbt,tkd->bkgd", grad_scores, key_all, preferred_element_type=jnp.float32)
            * factor
        )
        key_acc = (
            key_acc
            + jnp.einsum(
                "kgbt,bkgd->tkd", grad_scores, query_block, preferred_element_type=jnp.float32
            )
            * factor
        )
        value_acc = value_acc + jnp.einsum(
            "kgbt,bkgd->tkd", probs_low, grad_block, preferred_element_type=jnp.float32
        )
        return ((key_acc, value_acc), query_grad_block.reshape(block, head_count, HD))

    empty = jnp.zeros((2 * half_len, pair_count, HD), jnp.float32)
    (key_acc, value_acc), query_grad_blocks = lax.scan(
        backward_block,
        (empty, empty),
        (query_blocks, index_blocks, start_blocks, grad_blocks, log_totals),
    )
    key_back, value_back = (
        shifted(key_acc[:half_len].astype(jnp.bfloat16), "fsdp", -1).astype(jnp.float32),
        shifted(value_acc[:half_len].astype(jnp.bfloat16), "fsdp", -1).astype(jnp.float32),
    )
    key_local = key_acc[half_len:] + key_back
    value_local = value_acc[half_len:] + value_back
    query_grad_heads = query_grad_blocks.reshape(half_len, head_count, HD)
    grad_query_tok, grad_key_tok, grad_value_tok = (
        lax.all_to_all(
            query_grad_heads.astype(jnp.bfloat16), "seq", split_axis=0, concat_axis=1, tiled=True
        ).astype(query_grad_heads.dtype),
        lax.all_to_all(
            key_local.astype(jnp.bfloat16), "seq", split_axis=0, concat_axis=1, tiled=True
        ).astype(key_local.dtype),
        lax.all_to_all(
            value_local.astype(jnp.bfloat16), "seq", split_axis=0, concat_axis=1, tiled=True
        ).astype(value_local.dtype),
    )
    if repeat > 1:
        grad_key_tok = grad_key_tok.reshape(token_count, KVH, repeat, HD).sum(2)
        grad_value_tok = grad_value_tok.reshape(token_count, KVH, repeat, HD).sum(2)
    query_lin_grad = (
        rotate_back(grad_query_tok, cosine, sine).astype(jnp.bfloat16).reshape(token_count, QH * HD)
    )
    key_lin_grad = (
        rotate_back(grad_key_tok, cosine, sine).astype(jnp.bfloat16).reshape(token_count, KVH * HD)
    )
    value_lin_grad = grad_value_tok.astype(jnp.bfloat16).reshape(token_count, KVH * HD)
    query_grad = jnp.einsum(
        "td,tc->dc", normed_low, query_lin_grad, preferred_element_type=jnp.float32
    )
    key_grad = jnp.einsum("td,tc->dc", normed_low, key_lin_grad, preferred_element_type=jnp.float32)
    value_grad = jnp.einsum(
        "td,tc->dc", normed_low, value_lin_grad, preferred_element_type=jnp.float32
    )
    grad_normed_one = jnp.einsum(
        "tc,dc->td", query_lin_grad, wq_full, preferred_element_type=jnp.float32
    )
    grad_normed_one = grad_normed_one + jnp.einsum(
        "tc,dc->td", key_lin_grad, wk_full, preferred_element_type=jnp.float32
    )
    grad_normed_one = grad_normed_one + jnp.einsum(
        "tc,dc->td", value_lin_grad, wv_full, preferred_element_type=jnp.float32
    )
    grad_rows_one, first_gain_grad = norm_backward(grad_normed_one, unit_one, scale_one, gain_one)
    input_grad = (grad_middle + grad_rows_one).astype(jnp.bfloat16)[None]
    pieces = (
        lax.psum_scatter(
            first_gain_grad.astype(jnp.bfloat16), "fsdp", scatter_dimension=0, tiled=True
        ).astype(jnp.float32),
        lax.psum_scatter(
            query_grad.astype(jnp.bfloat16), "fsdp", scatter_dimension=0, tiled=True
        ).astype(jnp.float32),
        lax.psum_scatter(
            key_grad.astype(jnp.bfloat16), "fsdp", scatter_dimension=0, tiled=True
        ).astype(jnp.float32),
        lax.psum_scatter(
            value_grad.astype(jnp.bfloat16), "fsdp", scatter_dimension=0, tiled=True
        ).astype(jnp.float32),
        lax.psum_scatter(
            output_grad.astype(jnp.bfloat16), "fsdp", scatter_dimension=0, tiled=True
        ).astype(jnp.float32),
        lax.psum_scatter(
            second_gain_grad.astype(jnp.bfloat16), "fsdp", scatter_dimension=0, tiled=True
        ).astype(jnp.float32),
        lax.psum_scatter(
            gate_grad.astype(jnp.bfloat16), "fsdp", scatter_dimension=0, tiled=True
        ).astype(jnp.float32),
        lax.psum_scatter(
            up_grad.astype(jnp.bfloat16), "fsdp", scatter_dimension=0, tiled=True
        ).astype(jnp.float32),
        lax.psum_scatter(
            down_grad.astype(jnp.bfloat16), "fsdp", scatter_dimension=0, tiled=True
        ).astype(jnp.float32),
    )
    shares = (
        lax.psum(pieces[0].astype(jnp.bfloat16), "seq").astype(jnp.float32),
        lax.psum(pieces[1].astype(jnp.bfloat16), "seq").astype(jnp.float32),
        lax.psum(pieces[2].astype(jnp.bfloat16), "seq").astype(jnp.float32),
        lax.psum(pieces[3].astype(jnp.bfloat16), "seq").astype(jnp.float32),
        lax.psum(pieces[4].astype(jnp.bfloat16), "seq").astype(jnp.float32),
        lax.psum(pieces[5].astype(jnp.bfloat16), "seq").astype(jnp.float32),
        lax.psum(pieces[6].astype(jnp.bfloat16), "seq").astype(jnp.float32),
        lax.psum(pieces[7].astype(jnp.bfloat16), "seq").astype(jnp.float32),
        lax.psum(pieces[8].astype(jnp.bfloat16), "seq").astype(jnp.float32),
    )
    return (
        block_output,
        input_grad,
        shares[0],
        shares[1],
        shares[2],
        shares[3],
        shares[4],
        shares[5],
        shares[6],
        shares[7],
        shares[8],
    )


def plain_solution(mesh):
    placed = (
        P("fsdp", "seq", None),
        P("fsdp", "seq"),
        P("fsdp"),
        P("fsdp", None),
        P("fsdp", None),
        P("fsdp", None),
        P("fsdp", None),
        P("fsdp"),
        P("fsdp", None),
        P("fsdp", None),
        P("fsdp", None),
        P("fsdp", "seq", None),
    )
    return jax.shard_map(
        plain_body,
        mesh=mesh,
        in_specs=placed,
        out_specs=(
            P("fsdp", "seq", None),
            P("fsdp", "seq", None),
            P("fsdp"),
            P("fsdp", None),
            P("fsdp", None),
            P("fsdp", None),
            P("fsdp", None),
            P("fsdp"),
            P("fsdp", None),
            P("fsdp", None),
            P("fsdp", None),
        ),
        check_vma=False,
    )
```

```python
import functools
import math

import jax
import jax.numpy as jnp
from jax import lax
from jax.experimental import pallas as pl
from jax.experimental.pallas import tpu as pltpu
from jax.sharding import Mesh
from jax.sharding import PartitionSpec as P

QH = 16
KVH = 8
HD = 96


THETA = 100000.0
EPS = 1e-05
LOW = jnp.bfloat16
F32 = jnp.float32
NEG = -1e30
LN2 = math.log(2.0)


def contract(left, right, left_axis, right_axis):
    return lax.dot_general(
        left, right, (((left_axis,), (right_axis,)), ((), ())), preferred_element_type=F32
    )


def visible(first, second, query_block, key_block, size):
    key = key_block * size + lax.broadcasted_iota(jnp.int32, (size, size), 0)
    query = query_block * size + lax.broadcasted_iota(jnp.int32, (1, size), 1)
    start = jnp.where(query >= second, second, jnp.where(query >= first, first, 0))
    return (key >= start) & (key <= query)


def slot_of(block, count):
    return (block % (count // 2)) * 2 + block // (count // 2)


def forward_kernel(
    scalars,
    rows_ref,
    low_ref,
    full_ref,
    log_ref,
    query_s,
    key_s,
    value_s,
    top_s,
    total_s,
    mixed_s,
    *,
    size,
    count,
):
    first = scalars[1]
    second = scalars[2]
    here = pl.program_id(0)

    @pl.when(here == 0)
    def _():
        for block in range(count):
            slot = slot_of(block, count)
            query_s[block] = rows_ref[slot, 0:HD]
            key_s[block] = rows_ref[slot, HD : 2 * HD].T
            value_s[block] = rows_ref[slot, 2 * HD : 3 * HD]

    query = query_s[here]
    top_s[...] = jnp.full_like(top_s, NEG)
    total_s[...] = jnp.zeros_like(total_s)
    mixed_s[...] = jnp.zeros_like(mixed_s)

    def add_block(block, masked):
        scores = contract(key_s[block], query, 1, 0)
        if masked:
            scores = jnp.where(visible(first, second, here, block, size), scores, NEG)
        old_top = top_s[...]
        top = jnp.maximum(old_top, jnp.max(scores, 0, keepdims=True))
        expo = jnp.exp2(scores - top)
        scale = jnp.exp2(old_top - top)
        top_s[...] = top
        total_s[...] = total_s[...] * scale + jnp.sum(expo, 0, keepdims=True)
        mixed_s[...] = mixed_s[...] * scale + contract(value_s[block], expo.astype(LOW), 1, 0)

    last = count - 1

    @pl.loop(1, jnp.where(here == last, 1, here))
    def _(block):
        add_block(block, False)

    @pl.loop(0, jnp.where(here == last, count, jnp.minimum(here + 1, 2)))
    def _(step):
        add_block(jnp.where(here == last, step, step * here), True)

    total = total_s[...]
    result = mixed_s[...] / total
    full_ref[0] = result
    low_ref[0] = result.astype(LOW)
    log_ref[0] = top_s[...] + jnp.log2(total)


def backward_kernel(
    scalars,
    rows_ref,
    grad_ref,
    full_ref,
    log_ref,
    kept_ref,
    leaving_ref,
    query_s,
    key_s,
    value_s,
    delta_s,
    query_grad_s,
    key_grad_s,
    value_grad_s,
    *,
    size,
    count,
):
    half = scalars[0]
    first = scalars[1]
    second = scalars[2]
    here = pl.program_id(0)
    per_half = count // 2

    @pl.when(here == 0)
    def _():
        for block in range(count):
            slot = slot_of(block, count)
            query_s[block] = rows_ref[slot, 0:HD]
            key_s[block] = rows_ref[slot, HD : 2 * HD]
            value_s[block] = rows_ref[slot, 2 * HD : 3 * HD].T
            delta_s[block] = jnp.sum(
                grad_ref[slot].astype(F32) * full_ref[block], 0, keepdims=True
            )
        query_grad_s[...] = jnp.zeros_like(query_grad_s)

    key_grad_s[...] = jnp.zeros_like(key_grad_s)
    value_grad_s[...] = jnp.zeros_like(value_grad_s)
    key = key_s[here]
    key_rows = key.T
    value_rows = value_s[here]

    def add_block(block, masked):
        query = query_s[block]
        grad = grad_ref[slot_of(block, count)]
        scores = contract(key_rows, query, 1, 0)
        if masked:
            scores = jnp.where(visible(first, second, block, here, size), scores, NEG)
        probs = jnp.exp2(scores - log_ref[block])
        grad_probs = contract(value_rows, grad, 1, 0)
        grad_scores = (probs * (grad_probs - delta_s[block])).astype(LOW)
        value_grad_s[...] += contract(grad, probs.astype(LOW), 1, 1)
        key_grad_s[...] += contract(query, grad_scores, 1, 1)
        query_grad_s[block] += contract(key, grad_scores, 1, 0)

    last = count - 1

    @pl.loop(here + 1, jnp.where(here == 0, 1, last))
    def _(block):
        add_block(block, False)

    @pl.loop(0, jnp.where(here == 0, count, jnp.where(here == last, 1, 2)))
    def _(step):
        add_block(jnp.where(here == 0, step, jnp.where(step == 0, here, last)), True)

    side = here // per_half
    columns = pl.ds(pl.multiple_of((here % per_half) * size, size), size)

    def write(out_ref):
        out_ref[0:HD, columns] = (query_grad_s[here] * HD**-0.5).astype(LOW)
        out_ref[HD : 2 * HD, columns] = (key_grad_s[...] * LN2).astype(LOW)
        out_ref[2 * HD : 3 * HD, columns] = value_grad_s[...].astype(LOW)

    @pl.when(side == half)
    def _():
        write(kept_ref)

    @pl.when(side != half)
    def _():
        write(leaving_ref)


def attend_forward(scalars, rows):
    count, _, size = rows.shape
    whole = lambda shape: pl.BlockSpec(shape, lambda i, s: (0,) * len(shape))
    pairs = count * (count + 1) // 2
    return pl.pallas_call(
        functools.partial(forward_kernel, size=size, count=count),
        grid_spec=pltpu.PrefetchScalarGridSpec(
            num_scalar_prefetch=1,
            grid=(count,),
            in_specs=[whole(rows.shape)],
            out_specs=[
                pl.BlockSpec(
                    (1, HD, size), lambda i, s: (slot_of(i, count), 0, 0)
                ),
                pl.BlockSpec((1, HD, size), lambda i, s: (i, 0, 0)),
                pl.BlockSpec((1, 1, size), lambda i, s: (i, 0, 0)),
            ],
            scratch_shapes=[
                pltpu.VMEM((count, HD, size), LOW),
                pltpu.VMEM((count, size, HD), LOW),
                pltpu.VMEM((count, HD, size), LOW),
                pltpu.VMEM((1, size), F32),
                pltpu.VMEM((1, size), F32),
                pltpu.VMEM((HD, size), F32),
            ],
        ),
        out_shape=[
            jax.ShapeDtypeStruct((count, HD, size), LOW),
            jax.ShapeDtypeStruct((count, HD, size), F32),
            jax.ShapeDtypeStruct((count, 1, size), F32),
        ],
        compiler_params=pltpu.CompilerParams(
            dimension_semantics=("arbitrary",), vmem_limit_bytes=32 * 2**20
        ),
        cost_estimate=pl.CostEstimate(
            flops=pairs * size * size * HD * 32,
            bytes_accessed=10 * 2**20,
            transcendentals=pairs * size * size,
        ),
        name="attend_forward",
    )(scalars, rows)


def attend_backward(scalars, rows, grad, full, log_total):
    count, _, size = rows.shape
    whole = lambda shape: pl.BlockSpec(shape, lambda i, s: (0,) * len(shape))
    pairs = count * (count + 1) // 2
    out_shape = (3 * HD, count // 2 * size)
    return pl.pallas_call(
        functools.partial(backward_kernel, size=size, count=count),
        grid_spec=pltpu.PrefetchScalarGridSpec(
            num_scalar_prefetch=1,
            grid=(count,),
            in_specs=[
                whole(rows.shape),
                whole(grad.shape),
                whole(full.shape),
                whole(log_total.shape),
            ],
            out_specs=[whole(out_shape)] * 2,
            scratch_shapes=[
                pltpu.VMEM((count, HD, size), LOW),
                pltpu.VMEM((count, HD, size), LOW),
                pltpu.VMEM((count, size, HD), LOW),
                pltpu.VMEM((count, 1, size), F32),
                pltpu.VMEM((count, HD, size), F32),
                pltpu.VMEM((HD, size), F32),
                pltpu.VMEM((HD, size), F32),
            ],
        ),
        out_shape=[jax.ShapeDtypeStruct(out_shape, LOW)] * 2,
        compiler_params=pltpu.CompilerParams(
            dimension_semantics=("arbitrary",), vmem_limit_bytes=32 * 2**20
        ),
        cost_estimate=pl.CostEstimate(
            flops=pairs * size * size * HD * 42,
            bytes_accessed=16 * 2**20,
            transcendentals=pairs * size * size,
        ),
        name="attend_backward",
    )(scalars, rows, grad, full, log_total)


def place_rows_kernel(order, *refs):
    pieces, out_ref = refs[:-1], refs[-1]
    size = pieces[0].shape[0]
    for index, piece in enumerate(pieces):
        start = pl.multiple_of(order[index] * size, size)
        out_ref[pl.ds(start, size), :] = piece[...].astype(F32)


def place_rows(order, pieces):
    size, width = pieces[0].shape
    total = size * len(pieces)
    step = 512
    return pl.pallas_call(
        place_rows_kernel,
        grid_spec=pltpu.PrefetchScalarGridSpec(
            num_scalar_prefetch=1,
            grid=(width // step,),
            in_specs=[pl.BlockSpec((size, step), lambda i, s: (0, i)) for _ in pieces],
            out_specs=pl.BlockSpec((total, step), lambda i, s: (0, i)),
        ),
        out_shape=jax.ShapeDtypeStruct((total, width), F32),
        compiler_params=pltpu.CompilerParams(vmem_limit_bytes=24 * 2**20),
        cost_estimate=pl.CostEstimate(
            flops=0, bytes_accessed=total * width * 6, transcendentals=0
        ),
        name="place_rows",
    )(order, *pieces)


def place_columns_kernel(order, gain_ref, gate_w_ref, up_w_ref, *refs):
    count = (len(refs) - 3) // 2
    gates, ups = refs[:count], refs[count : 2 * count]
    gate_ref, up_ref, sum_ref = refs[2 * count :]
    size = gates[0].shape[1]
    gain = gain_ref[...]
    total = jnp.zeros((gate_ref.shape[0], size), F32)
    for index in range(count):
        columns = pl.ds(pl.multiple_of(order[index] * size, size), size)
        gate, up = gates[index][...].astype(F32), ups[index][...].astype(F32)
        total += gate * gate_w_ref[:, columns].astype(F32)
        total += up * up_w_ref[:, columns].astype(F32)
        gate_ref[:, columns] = gate * gain
        up_ref[:, columns] = up * gain

    @pl.when(pl.program_id(0) == 0)
    def _():
        sum_ref[...] = jnp.zeros_like(sum_ref)

    sum_ref[...] += jnp.sum(total, 1, keepdims=True)


def place_columns(order, gain, gate_weight, up_weight, gates, ups, shards):
    rows, width = gate_weight.shape
    span = width // shards
    size = span // len(gates)
    wide = pl.BlockSpec((rows, span), lambda i, s: (0, i))
    thin = pl.BlockSpec((rows, 1), lambda i, s: (0, 0))
    pieces = [pl.BlockSpec((rows, size), lambda i, s: (0, i)) for _ in (*gates, *ups)]
    return pl.pallas_call(
        place_columns_kernel,
        grid_spec=pltpu.PrefetchScalarGridSpec(
            num_scalar_prefetch=1,
            grid=(shards,),
            in_specs=[thin, wide, wide, *pieces],
            out_specs=[wide, wide, thin],
        ),
        out_shape=[
            jax.ShapeDtypeStruct((rows, width), F32),
            jax.ShapeDtypeStruct((rows, width), F32),
            jax.ShapeDtypeStruct((rows, 1), F32),
        ],
        compiler_params=pltpu.CompilerParams(
            dimension_semantics=("arbitrary",), vmem_limit_bytes=24 * 2**20
        ),
        cost_estimate=pl.CostEstimate(
            flops=rows * width * 6, bytes_accessed=rows * width * 16, transcendentals=0
        ),
        name="place_columns",
    )(order, gain, gate_weight, up_weight, *gates, *ups)


def place_heads_kernel(gain_ref, query_w, key_w, value_w, all_ref, query_ref, key_ref, value_ref, sum_ref):
    rows = gain_ref.shape[0]
    wide = query_ref.shape[1] // KVH
    gain = gain_ref[...]
    total = jnp.zeros((rows, 4 * HD), F32)
    pieces = [all_ref[i * rows : (i + 1) * rows, :].astype(F32) for i in range(KVH)]
    for start in range(0, KVH, 2):
        value = jnp.concatenate([piece[:, :wide] for piece in pieces[start : start + 2]], 1)
        columns = slice(start * wide, (start + 2) * wide)
        total += value * query_w[:, columns].astype(F32)
        query_ref[:, columns] = value * gain
    for first, weight, out_ref in ((wide, key_w, key_ref), (wide + HD, value_w, value_ref)):
        for start in range(0, KVH, 4):
            value = jnp.concatenate(
                [piece[:, first : first + HD] for piece in pieces[start : start + 4]], 1
            )
            columns = slice(start * HD, (start + 4) * HD)
            total += value * weight[:, columns].astype(F32)
            out_ref[:, columns] = value * gain
    sum_ref[...] = jnp.sum(total, 1, keepdims=True)


def place_heads(gain, query_weight, key_weight, value_weight, pieces):
    weights = (query_weight, key_weight, value_weight)
    rows = gain.shape[0]
    return pl.pallas_call(
        place_heads_kernel,
        out_shape=[jax.ShapeDtypeStruct(weight.shape, F32) for weight in weights]
        + [jax.ShapeDtypeStruct((rows, 1), F32)],
        compiler_params=pltpu.CompilerParams(vmem_limit_bytes=32 * 2**20),
        cost_estimate=pl.CostEstimate(
            flops=rows * 3072 * 4, bytes_accessed=rows * 3072 * 8, transcendentals=0
        ),
        name="place_heads",
    )(gain, *weights, pieces)


def merge_kernel(scalars, kept_ref, came_ref, cosine_ref, sine_ref, scale_ref, out_ref, split_ref):
    lead = scalars[0] == 0
    lines, _, size = split_ref.shape
    for line in range(lines):
        columns = slice(line * size, (line + 1) * size)
        kept = kept_ref[:, columns].astype(F32)
        came = came_ref[:, columns].astype(F32)
        cosine, sine, scale = cosine_ref[:, columns], sine_ref[:, columns], scale_ref[:, columns]
        joint = kept[HD:] + came[HD:]
        first = jnp.where(lead, kept[:HD], came[:HD])
        second = jnp.where(lead, came[:HD], kept[:HD])
        turned = []
        for value in (first, second, joint[:HD]):
            low, high = value[: HD // 2], value[HD // 2 :]
            turned.append((low * cosine + high * sine) * scale)
            turned.append((high * cosine - low * sine) * scale)
        turned.append(joint[HD:] * scale)
        result = jnp.concatenate([part.astype(LOW) for part in turned], 0)
        out_ref[:, columns] = result
        split_ref[line] = result


def merge(scalars, kept, came, cosine, sine, scale, lines):
    tokens = kept.shape[1]
    whole = lambda value: pl.BlockSpec(value.shape, lambda i, s: (0,) * len(value.shape))
    outs = [
        jax.ShapeDtypeStruct((4 * HD, tokens), LOW),
        jax.ShapeDtypeStruct((lines, 4 * HD, tokens // lines), LOW),
    ]
    return pl.pallas_call(
        merge_kernel,
        grid_spec=pltpu.PrefetchScalarGridSpec(
            num_scalar_prefetch=1,
            grid=(1,),
            in_specs=[whole(value) for value in (kept, came, cosine, sine, scale)],
            out_specs=[whole(value) for value in outs],
        ),
        out_shape=outs,
        compiler_params=pltpu.CompilerParams(vmem_limit_bytes=24 * 2**20),
        cost_estimate=pl.CostEstimate(
            flops=tokens * HD * 24, bytes_accessed=tokens * HD * 30, transcendentals=0
        ),
        name="merge",
    )(scalars, kept, came, cosine, sine, scale)


def pack_kernel(scalars, gain_ref, query_ref, key_ref, value_ref, *outs):
    core = scalars[3]
    gain = gain_ref[...]
    wide = query_ref.shape[1] // KVH
    span = wide + 2 * HD
    for which in range(2):

        @pl.when(core == which)
        def _():
            for line in range(KVH // 2):
                head = 2 * line + which
                value = jnp.concatenate(
                    [
                        query_ref[:, head * wide : (head + 1) * wide].astype(F32),
                        key_ref[:, head * HD : (head + 1) * HD].astype(F32),
                        value_ref[:, head * HD : (head + 1) * HD].astype(F32),
                    ],
                    1,
                )
                place = (line % 2) * span
                outs[line // 2][:, place : place + span] = (value * gain).astype(LOW)


def pack(scalars, gain, query_weight, key_weight, value_weight):
    rows, width = query_weight.shape
    whole = lambda value: pl.BlockSpec(value.shape, lambda i, s: (0, 0))
    weights = (gain, query_weight, key_weight, value_weight)
    outs = [jax.ShapeDtypeStruct((rows, width // 2), LOW)] * 2
    return pl.pallas_call(
        pack_kernel,
        grid_spec=pltpu.PrefetchScalarGridSpec(
            num_scalar_prefetch=1,
            grid=(1,),
            in_specs=[whole(value) for value in weights],
            out_specs=[whole(value) for value in outs],
        ),
        out_shape=outs,
        compiler_params=pltpu.CompilerParams(vmem_limit_bytes=24 * 2**20),
        cost_estimate=pl.CostEstimate(
            flops=rows * width, bytes_accessed=rows * width * 6, transcendentals=0
        ),
        name="pack",
    )(scalars, *weights)


def spread_kernel(lead_ref, tail_ref, cosine_ref, sine_ref, scale_ref, out_ref):
    cosine, sine, scale = cosine_ref[...], sine_ref[...], scale_ref[...]
    span = 4 * HD

    def turn(value, factor):
        low, high = value[: HD // 2], value[HD // 2 :]
        return jnp.concatenate(
            [
                ((low * cosine - high * sine) * (scale * factor)).astype(LOW),
                ((high * cosine + low * sine) * (scale * factor)).astype(LOW),
            ],
            0,
        )

    for line in range(out_ref.shape[0] // 2):
        source = (lead_ref, tail_ref)[line // 2]
        base = (line % 2) * span
        key = turn(source[base + 2 * HD : base + 3 * HD], 1.0)
        value = (source[base + 3 * HD : base + 4 * HD] * scale).astype(LOW)
        for which in range(2):
            query = source[base + which * HD : base + (which + 1) * HD]
            out_ref[2 * line + which, 0:HD] = turn(query, HD**-0.5 / LN2)
            out_ref[2 * line + which, HD : 2 * HD] = key
            out_ref[2 * line + which, 2 * HD : 3 * HD] = value


def spread(lead, tail, cosine, sine, scale):
    tokens = lead.shape[1]
    return pl.pallas_call(
        spread_kernel,
        out_shape=jax.ShapeDtypeStruct((KVH, 3 * HD, tokens), LOW),
        compiler_params=pltpu.CompilerParams(vmem_limit_bytes=24 * 2**20),
        cost_estimate=pl.CostEstimate(
            flops=tokens * HD * 100, bytes_accessed=tokens * HD * 120, transcendentals=0
        ),
        name="spread",
    )(lead, tail, cosine, sine, scale)


def swap(value, axis):
    return lax.ppermute(value, axis, [(0, 1), (1, 0)])


def swap_near(value):
    return lax.ppermute(value, "z", [(0, 1), (1, 0), (2, 3), (3, 2)])


def swap_far(value):
    return lax.ppermute(value, "z", [(0, 2), (2, 0), (1, 3), (3, 1)])


def tie(*values):
    return lax.optimization_barrier(values)


def in_order(place, own, other):
    return (jnp.where(place == 0, own, other), jnp.where(place == 0, other, own))


def both(place, own, other):
    return jnp.concatenate(in_order(place, own, other), 0)


def spread_out(value, first, second):
    other = swap(value, first)
    pair = jnp.stack(in_order(lax.axis_index(first), value, other))
    return pair, swap(pair, second)


def placed(pair, other, second):
    pairs = in_order(lax.axis_index(second), pair, other)
    grid = jnp.stack(pairs, 0 if second == "y" else 1)
    return grid.reshape(-1, *grid.shape[3:])


def pick(array, axis, at):
    return lax.dynamic_index_in_dim(array, at, axis, keepdims=False)


def halve(value, axis, along=0):
    at = lax.axis_index(axis)
    return pick(value, along, at), swap(pick(value, along, 1 - at), axis)


def halve_x(value):
    return halve(value.reshape(2, 2, -1, value.shape[-1]), "x", 1)


def halve_y(value):
    return halve(value.reshape(2, 2, -1, value.shape[-1]), "y", 0)


def fast_body(
    tokens,
    positions,
    first_gain,
    query_weight,
    key_weight,
    value_weight,
    output_weight,
    second_gain,
    gate_weight,
    up_weight,
    down_weight,
    cotangent,
):
    seq = ("z", "c")
    fsdp = ("y", "x")
    z, core, half = lax.axis_index("z"), lax.axis_index("c"), lax.axis_index("x")
    near = z % 2
    lines = lax.axis_size("z")
    seq_count = 2 * lines
    shards = lax.axis_size("y") * 2
    spot = z * 2 + core
    quarter = near * 2 + core
    rows = tokens[0]
    count, width = rows.shape
    chip_count = 2 * count
    half_len = count * seq_count
    seq_len = 2 * half_len

    begins = jnp.where(
        (spot == 0) & (half == 0),
        count - 1 - positions[0, count - 1],
        half * half_len + spot * count - positions[0, 0],
    )
    ends = begins + (seq_len - count)
    scalars = jnp.stack([half, begins, ends, core]).astype(jnp.int32)

    gain_one = first_gain.astype(F32)[:, None]
    gain_two = second_gain.astype(F32)[:, None]

    take = functools.partial(lax.dynamic_slice_in_dim, axis=1)
    take_rows = functools.partial(lax.dynamic_slice_in_dim, axis=0)
    gather = lambda value, axes: lax.all_gather(value, axes, axis=0, tiled=True)
    lead_shard, tail_shard = pack(scalars, gain_one, query_weight, key_weight, value_weight)
    lead_parts = spread_out(lead_shard, "x", "y")
    tail_parts = spread_out(tail_shard, "y", "x")
    all_rows = gather(rows, seq)
    out_rows = output_weight.shape[0] // 2
    out_shard = take_rows(output_weight, core * out_rows, out_rows)
    piece = down_weight.shape[0] // 4
    down_shard = take_rows(down_weight, quarter * piece, piece)
    gate_shard, up_shard = (
        (
            jnp.concatenate(
                [
                    take(weight, shard * 4 * piece + quarter * piece, piece)
                    for shard in range(shards)
                ],
                1,
            ).astype(F32)
            * gain_two
        ).astype(LOW)
        for weight in (gate_weight, up_weight)
    )

    chip_rows = both(core, rows, swap(rows, "c"))
    chip_cot = both(core, cotangent[0], swap(cotangent[0], "c"))
    near_cot = swap_near(cotangent[0])
    near_cot = jnp.concatenate([near_cot, swap(near_cot, "c")], 0)
    lead_parts, tail_parts, gate_shard, up_shard, chip_rows, chip_cot, near_cot = (
        lax.optimization_barrier(
            (lead_parts, tail_parts, gate_shard, up_shard, chip_rows, chip_cot, near_cot)
        )
    )
    lead_w, tail_w = placed(*lead_parts, "y"), placed(*tail_parts, "x")
    gate_parts = spread_out(gate_shard, "x", "y")
    up_parts = spread_out(up_shard, "y", "x")

    def row_scale(value):
        return lax.rsqrt(jnp.mean(value * value, -1, keepdims=True) + EPS)

    place = half * half_len + jnp.arange(half_len, dtype=jnp.int32)
    start = jnp.where(place >= ends, ends, jnp.where(place >= begins, begins, 0))
    freq = THETA ** (-(jnp.arange(HD // 2, dtype=F32) * 2.0 / HD))
    angle = freq[:, None] * (place - start).astype(F32)[None, :]
    cosine, sine = jnp.cos(angle), jnp.sin(angle)
    ours = lambda value: take(value, z * chip_count, chip_count)
    scale_chip = row_scale(chip_rows.astype(F32)).reshape(1, chip_count)
    leaving = spread(
        contract(lead_w, chip_rows, 0, 1),
        contract(tail_w, chip_rows, 0, 1),
        ours(cosine),
        ours(sine),
        scale_chip,
    )
    exchange = lambda value: lax.all_to_all(
        value, ("z", "x"), split_axis=0, concat_axis=0, tiled=True
    )
    head_rows, all_rows, out_shard, down_shard, gate_pair, up_pair = tie(
        exchange(leaving), all_rows, out_shard, down_shard, gate_parts[0], up_parts[0]
    )
    gate_parts, up_parts = (gate_pair, gate_parts[1]), (up_pair, up_parts[1])
    out_w = gather(out_shard, fsdp)
    down_w = gather(down_shard, fsdp)

    head_low, head_full, log_total = attend_forward(scalars, head_rows)
    head_low, gate_parts, up_parts = tie(head_low, gate_parts, up_parts)
    gate_w, up_w = placed(*gate_parts, "y"), placed(*up_parts, "x")
    heads, gate_w, up_w = tie(exchange(head_low), gate_w, up_w)
    heads = heads.reshape(QH // 2 * HD, chip_count)

    mine_of = lambda value: take_rows(value, core * count, count)
    theirs_of = lambda value: take_rows(value, (1 - core) * count, count)
    branch = contract(heads, out_w, 0, 0).astype(LOW)
    middle = chip_rows.astype(F32) + (branch.astype(F32) + swap(branch, "c").astype(F32))
    own_middle = mine_of(middle)
    middle_low = middle.astype(LOW)
    near_middle = swap_near(mine_of(middle_low))
    near_middle = jnp.concatenate([near_middle, swap(near_middle, "c")], 0)

    def feed(low, scale):
        gate, upper = contract(low, gate_w, 1, 0) * scale, contract(low, up_w, 1, 0) * scale
        sigma = jax.nn.sigmoid(gate)
        silu = gate * sigma
        return (silu * upper).astype(LOW), (gate, upper, sigma, silu)

    def feed_back(cot, scale, kept):
        gate, upper, sigma, silu = kept
        grad_hidden = contract(cot, down_w, 1, 1) * scale
        gate_low = (grad_hidden * upper * sigma * (1.0 + gate * (1.0 - sigma))).astype(LOW)
        upper_low = (grad_hidden * silu).astype(LOW)
        part = contract(gate_low, gate_w, 1, 1) + contract(upper_low, up_w, 1, 1)
        return gate_low, upper_low, part

    chip_scale = row_scale(middle)
    near_scale = row_scale(near_middle.astype(F32))
    chip_hidden, chip_kept = feed(middle_low, chip_scale)
    near_hidden, near_kept = feed(near_middle, near_scale)
    stack = lambda first, second: jnp.concatenate([first, second], 0)
    down_part = contract(
        stack(chip_hidden, near_hidden), stack(chip_cot, near_cot), 0, 0
    ).astype(LOW)
    near_cot, down_part = tie(near_cot, down_part)
    cut = width // 2
    down_x, down_y = halve_x(down_part[:, :cut]), halve_y(down_part[:, cut:])
    near_gate, near_upper, near_part = feed_back(near_cot, near_scale, near_kept)
    chip_gate, chip_upper, chip_part = feed_back(chip_cot, chip_scale, chip_kept)

    near_part, down_x, down_y = tie(near_part, down_x, down_y)
    down_x, down_y = halve(sum(down_x), "y"), halve(sum(down_y), "x")
    all_middle = stack(middle_low, near_middle)
    gate_part = contract(all_middle, stack(chip_gate, near_gate), 0, 0).astype(LOW)
    up_part = contract(all_middle, stack(chip_upper, near_upper), 0, 0).astype(LOW)

    def own_sum(chip_part, near_part):
        near_sum = near_part[:count].astype(F32) + swap(near_part[count:].astype(LOW), "c")
        came = swap_near(near_sum.astype(LOW))
        chip_sum = mine_of(chip_part).astype(F32) + swap(theirs_of(chip_part).astype(LOW), "c")
        return chip_sum + came.astype(F32)

    grad_two, gate_part, up_part, down_x, down_y = tie(
        own_sum(chip_part, near_part), gate_part, up_part, down_x, down_y
    )
    down_grad = jnp.concatenate([sum(down_x), sum(down_y)], 1)
    down_far = swap_far(down_grad)
    gate_half, up_half = halve_x(gate_part), halve_y(up_part)
    own_scale = mine_of(chip_scale)
    grad_middle = (
        cotangent[0].astype(F32)
        + grad_two
        - own_middle * (own_scale * own_scale * jnp.mean(grad_two * own_middle, -1, keepdims=True))
    )
    own_branch = grad_middle.astype(LOW)
    grad_branch = both(core, own_branch, swap(own_branch, "c"))
    grad_heads = contract(out_w, grad_branch, 1, 1).astype(LOW)
    grad_heads, grad_branch = tie(grad_heads, grad_branch)
    output_part = contract(heads, grad_branch, 1, 0).astype(LOW)
    scatter = lambda value, axes: lax.psum_scatter(value, axes, scatter_dimension=0, tiled=True)
    output_grad = scatter(output_part, fsdp)
    grad_head, output_part, down_grad, down_far, gate_half, up_half = tie(
        exchange(grad_heads.reshape(2 * lines, HD, chip_count)),
        output_part,
        down_grad,
        down_far,
        gate_half,
        up_half,
    )

    gate_half, up_half = halve(sum(gate_half), "y"), halve(sum(up_half), "x")
    kept, leaving = attend_backward(scalars, head_rows, grad_head, head_full, log_total)
    kept, leaving, gate_half, up_half = tie(kept, leaving, gate_half, up_half)
    gate_grad, up_grad = sum(gate_half), sum(up_half)
    gate_far = swap_far(gate_grad)
    down_sum = down_grad + down_far
    down_near = swap_near(down_sum)
    feed_sum = own_sum(contract(chip_hidden, down_w, 1, 0), contract(near_hidden, down_w, 1, 0))
    block_output = (own_middle + feed_sum).astype(LOW)[None]
    rows_float = all_rows.astype(F32)
    scale_one = row_scale(rows_float).reshape(1, half_len)
    came, gate_grad, gate_far, down_sum, down_near, block_output, scale_one = tie(
        swap(leaving, "x"), gate_grad, gate_far, down_sum, down_near, block_output, scale_one
    )
    up_far = swap_far(up_grad)
    gate_sum = gate_grad + gate_far
    gate_near = swap_near(gate_sum)
    qkv_low, by_line = merge(scalars, kept, came, cosine, sine, scale_one, lines)
    token_grads = lax.all_to_all(by_line, "z", split_axis=0, concat_axis=0, tiled=True)
    qkv_part = contract(all_rows, qkv_low, 0, 1).astype(LOW).reshape(shards, 2, -1, 4 * HD)
    qkv_x, qkv_y = halve_x(qkv_part[:, 0]), halve_y(qkv_part[:, 1])
    token_grads, qkv_x, qkv_y, up_grad, up_far, gate_sum, gate_near, output_grad = tie(
        token_grads, qkv_x, qkv_y, up_grad, up_far, gate_sum, gate_near, output_grad
    )
    qkv_x, qkv_y = halve(sum(qkv_x), "y"), halve(sum(qkv_y), "x")
    qkv_grad = jnp.concatenate([sum(qkv_x), sum(qkv_y)], 0)
    token_grads = token_grads.reshape(-1, chip_count)
    split = lead_w.shape[1]
    grad_one = contract(token_grads[:split], lead_w, 0, 1) + contract(
        token_grads[split:], tail_w, 0, 1
    )
    grad_one = mine_of(grad_one) + swap(theirs_of(grad_one).astype(LOW), "c").astype(F32)
    up_sum = up_grad + up_far
    up_near = swap_near(up_sum)
    output_own = output_grad + swap_near(output_grad)
    output_own = output_own + swap_far(output_own)
    own_rows = rows.astype(F32)
    own_scale = row_scale(own_rows)
    input_grad = (
        grad_middle
        + grad_one
        - own_rows * (own_scale * own_scale * jnp.mean(grad_one * own_rows, -1, keepdims=True))
    ).astype(LOW)[None]

    def four(value, near_value):
        return value, swap(value, "c"), near_value, swap(near_value, "c")

    order = jnp.stack([quarter, quarter ^ 1, quarter ^ 2, quarter ^ 3]).astype(jnp.int32)
    core_order = jnp.stack([core, 1 - core]).astype(jnp.int32)
    down_total = place_rows(order, four(down_sum, down_near))
    output_total = place_rows(core_order, (output_own, swap(output_own, "c")))
    gate_total, up_total, second_gain_grad = place_columns(
        order, gain_two, gate_weight, up_weight, four(gate_sum, gate_near), four(up_sum, up_near), shards
    )
    query_grad, key_grad, value_grad, first_gain_grad = place_heads(
        gain_one, query_weight, key_weight, value_weight, gather(qkv_grad, seq)
    )
    return (
        block_output,
        input_grad,
        first_gain_grad[:, 0],
        query_grad,
        key_grad,
        value_grad,
        output_total,
        second_gain_grad[:, 0],
        gate_total,
        up_total,
        down_total,
    )


def fast_solution(mesh):
    seq_count, shard_count = mesh.devices.shape
    fine = Mesh(
        mesh.devices.reshape(seq_count // 2, 2, shard_count // 2, 2), ("z", "c", "y", "x")
    )
    seq, fsdp = ("z", "c"), ("y", "x")
    matrix = P(fsdp, None)
    return jax.shard_map(
        fast_body,
        mesh=fine,
        in_specs=(
            P(fsdp, seq, None),
            P(fsdp, seq),
            P(fsdp),
            matrix,
            matrix,
            matrix,
            matrix,
            P(fsdp),
            matrix,
            matrix,
            matrix,
            P(fsdp, seq, None),
        ),
        out_specs=(
            P(fsdp, seq, None),
            P(fsdp, seq, None),
            P(fsdp),
            matrix,
            matrix,
            matrix,
            matrix,
            P(fsdp),
            matrix,
            matrix,
            matrix,
        ),
        check_vma=False,
    )


def solution(mesh):
    shape = dict(mesh.shape)
    if shape["seq"] == KVH and shape["fsdp"] == 4:
        return fast_solution(mesh)
    return plain_solution(mesh)


def shifted(value, axis, steps):
    count = lax.axis_size(axis)
    first, last = (max(0, -steps), min(count, count - steps))
    return lax.ppermute(value, axis, [(source, source + steps) for source in range(first, last)])


def rope_tables(position_rows):
    freq = THETA ** (-(jnp.arange(HD // 2, dtype=jnp.float32) * 2.0 / HD))
    angle = position_rows.astype(jnp.float32)[:, None] * freq[None, :]
    cosine = jnp.cos(angle)
    sine = jnp.sin(angle)
    return (jnp.concatenate([cosine, cosine], -1), jnp.concatenate([sine, sine], -1))


def rotate(values, cosine, sine):
    half = HD // 2
    turned = jnp.concatenate([-values[..., half:], values[..., :half]], -1)
    return values * cosine[:, None, :] + turned * sine[:, None, :]


def rotate_back(grads, cosine, sine):
    half = HD // 2
    scaled = grads * sine[:, None, :]
    turned = jnp.concatenate([scaled[..., half:], -scaled[..., :half]], -1)
    return grads * cosine[:, None, :] + turned


def norm_forward(rows, gain):
    scale = lax.rsqrt(jnp.mean(rows * rows, -1, keepdims=True) + EPS)
    unit = rows * scale
    return (unit * gain, unit, scale)


def norm_backward(grad_out, unit, scale, gain):
    grad_unit = grad_out * gain
    gain_grad = jnp.sum(grad_out * unit, 0)
    grad_rows = scale * (grad_unit - unit * jnp.mean(grad_unit * unit, -1, keepdims=True))
    return (grad_rows, gain_grad)


def plain_body(
    tokens,
    positions,
    first_gain,
    query_weight,
    key_weight,
    value_weight,
    output_weight,
    second_gain,
    gate_weight,
    up_weight,
    down_weight,
    cotangent,
):
    seq_count = lax.axis_size("seq")
    local_rows = tokens[0]
    token_count = local_rows.shape[0]
    half_len = token_count * seq_count
    rows_float = local_rows.astype(jnp.float32)
    gain_one, wq_full, wk_full, wv_full, wo_full = (
        lax.all_gather(first_gain, "fsdp", axis=0, tiled=True),
        lax.all_gather(query_weight, "fsdp", axis=0, tiled=True),
        lax.all_gather(key_weight, "fsdp", axis=0, tiled=True),
        lax.all_gather(value_weight, "fsdp", axis=0, tiled=True),
        lax.all_gather(output_weight, "fsdp", axis=0, tiled=True),
    )
    gain_one = gain_one.astype(jnp.float32)
    normed_one, unit_one, scale_one = norm_forward(rows_float, gain_one)
    normed_low = normed_one.astype(jnp.bfloat16)
    cosine, sine = rope_tables(positions[0])
    query_lin = jnp.dot(normed_low, wq_full, preferred_element_type=jnp.float32).reshape(
        token_count, QH, HD
    )
    key_lin = jnp.dot(normed_low, wk_full, preferred_element_type=jnp.float32).reshape(
        token_count, KVH, HD
    )
    value_lin = jnp.dot(normed_low, wv_full, preferred_element_type=jnp.float32).reshape(
        token_count, KVH, HD
    )
    query_rows = rotate(query_lin, cosine, sine).astype(jnp.bfloat16)
    key_rows = rotate(key_lin, cosine, sine).astype(jnp.bfloat16)
    value_rows = value_lin.astype(jnp.bfloat16)
    repeat = max(1, seq_count // KVH)
    if repeat > 1:
        key_rows = jnp.repeat(key_rows, repeat, axis=1)
        value_rows = jnp.repeat(value_rows, repeat, axis=1)
    query_heads, key_heads, value_heads = (
        lax.all_to_all(query_rows, "seq", split_axis=1, concat_axis=0, tiled=True),
        lax.all_to_all(key_rows, "seq", split_axis=1, concat_axis=0, tiled=True),
        lax.all_to_all(value_rows, "seq", split_axis=1, concat_axis=0, tiled=True),
    )
    head_count = query_heads.shape[1]
    pair_count = key_heads.shape[1]
    group = head_count // pair_count
    half_positions = lax.all_gather(positions[0], "seq", axis=0, tiled=True)
    key_prior, value_prior = shifted((key_heads, value_heads), "fsdp", 1)
    key_all = jnp.concatenate([key_prior, key_heads], 0)
    value_all = jnp.concatenate([value_prior, value_heads], 0)
    half_index = lax.axis_index("fsdp") % 2
    key_index = (half_index - 1) * half_len + jnp.arange(2 * half_len, dtype=jnp.int32)
    row_index = half_index * half_len + jnp.arange(half_len, dtype=jnp.int32)
    row_start = row_index - half_positions
    block = min(512, half_len)
    count = half_len // block
    factor = HD ** (-0.5)
    query_blocks = query_heads.reshape(count, block, pair_count, group, HD)
    index_blocks = row_index.reshape(count, block)
    start_blocks = row_start.reshape(count, block)

    def block_scores(query_block, index_block, start_block):
        scores = (
            jnp.einsum("bkgd,tkd->kgbt", query_block, key_all, preferred_element_type=jnp.float32)
            * factor
        )
        visible = (key_index[None, :] >= start_block[:, None]) & (
            key_index[None, :] <= index_block[:, None]
        )
        return jnp.where(visible, scores, -1e30)

    def forward_block(items):
        query_block, index_block, start_block = items
        scores = block_scores(query_block, index_block, start_block)
        top = jnp.max(scores, -1, keepdims=True)
        expo = jnp.exp(scores - top)
        total = jnp.sum(expo, -1, keepdims=True)
        probs_low = (expo / total).astype(jnp.bfloat16)
        mixed = jnp.einsum(
            "kgbt,tkd->bkgd", probs_low, value_all, preferred_element_type=jnp.float32
        )
        return (mixed.reshape(block, head_count, HD).astype(jnp.bfloat16), top + jnp.log(total))

    head_blocks, log_totals = lax.map(forward_block, (query_blocks, index_blocks, start_blocks))
    head_out = head_blocks.reshape(half_len, head_count, HD)
    token_heads = lax.all_to_all(head_out, "seq", split_axis=0, concat_axis=1, tiled=True)
    heads_flat = token_heads.reshape(token_count, QH * HD)
    middle = rows_float + jnp.dot(heads_flat, wo_full, preferred_element_type=jnp.float32)
    gain_two, wg_full, wu_full, wd_full = (
        lax.all_gather(second_gain, "fsdp", axis=0, tiled=True),
        lax.all_gather(gate_weight, "fsdp", axis=0, tiled=True),
        lax.all_gather(up_weight, "fsdp", axis=0, tiled=True),
        lax.all_gather(down_weight, "fsdp", axis=0, tiled=True),
    )
    gain_two = gain_two.astype(jnp.float32)
    normed_two, unit_two, scale_two = norm_forward(middle, gain_two)
    normed_two_low = normed_two.astype(jnp.bfloat16)
    gate = jnp.dot(normed_two_low, wg_full, preferred_element_type=jnp.float32)
    upper = jnp.dot(normed_two_low, wu_full, preferred_element_type=jnp.float32)
    hidden = (jax.nn.silu(gate) * upper).astype(jnp.bfloat16)
    result = middle + jnp.dot(hidden, wd_full, preferred_element_type=jnp.float32)
    block_output = result.astype(jnp.bfloat16)[None]
    grad_low = cotangent[0]
    grad_rows = grad_low.astype(jnp.float32)
    down_grad = jnp.einsum("tf,td->fd", hidden, grad_low, preferred_element_type=jnp.float32)
    grad_hidden = jnp.einsum("td,fd->tf", grad_low, wd_full, preferred_element_type=jnp.float32)
    sigma = jax.nn.sigmoid(gate)
    gate_low = (grad_hidden * upper * sigma * (1.0 + gate * (1.0 - sigma))).astype(jnp.bfloat16)
    upper_low = (grad_hidden * gate * sigma).astype(jnp.bfloat16)
    gate_grad = jnp.einsum(
        "td,tf->df", normed_two_low, gate_low, preferred_element_type=jnp.float32
    )
    up_grad = jnp.einsum("td,tf->df", normed_two_low, upper_low, preferred_element_type=jnp.float32)
    grad_normed_two = jnp.einsum(
        "tf,df->td", gate_low, wg_full, preferred_element_type=jnp.float32
    ) + jnp.einsum("tf,df->td", upper_low, wu_full, preferred_element_type=jnp.float32)
    grad_middle_norm, second_gain_grad = norm_backward(
        grad_normed_two, unit_two, scale_two, gain_two
    )
    grad_middle = grad_rows + grad_middle_norm
    grad_branch = grad_middle.astype(jnp.bfloat16)
    output_grad = jnp.einsum(
        "tc,td->cd", heads_flat, grad_branch, preferred_element_type=jnp.float32
    )
    grad_heads = (
        jnp.einsum("td,cd->tc", grad_branch, wo_full, preferred_element_type=jnp.float32)
        .astype(jnp.bfloat16)
        .reshape(token_count, QH, HD)
    )
    grad_head_rows = lax.all_to_all(grad_heads, "seq", split_axis=1, concat_axis=0, tiled=True)
    grad_blocks = grad_head_rows.reshape(count, block, pair_count, group, HD)

    def backward_block(carry, items):
        key_acc, value_acc = carry
        query_block, index_block, start_block, grad_block, log_block = items
        scores = block_scores(query_block, index_block, start_block)
        probs = jnp.exp(scores - log_block)
        probs_low = probs.astype(jnp.bfloat16)
        grad_probs = jnp.einsum(
            "bkgd,tkd->kgbt", grad_block, value_all, preferred_element_type=jnp.float32
        )
        grad_scores = (
            probs * (grad_probs - jnp.sum(probs * grad_probs, -1, keepdims=True))
        ).astype(jnp.bfloat16)
        query_grad_block = (
            jnp.einsum("kgbt,tkd->bkgd", grad_scores, key_all, preferred_element_type=jnp.float32)
            * factor
        )
        key_acc = (
            key_acc
            + jnp.einsum(
                "kgbt,bkgd->tkd", grad_scores, query_block, preferred_element_type=jnp.float32
            )
            * factor
        )
        value_acc = value_acc + jnp.einsum(
            "kgbt,bkgd->tkd", probs_low, grad_block, preferred_element_type=jnp.float32
        )
        return ((key_acc, value_acc), query_grad_block.reshape(block, head_count, HD))

    empty = jnp.zeros((2 * half_len, pair_count, HD), jnp.float32)
    (key_acc, value_acc), query_grad_blocks = lax.scan(
        backward_block,
        (empty, empty),
        (query_blocks, index_blocks, start_blocks, grad_blocks, log_totals),
    )
    key_back, value_back = (
        shifted(key_acc[:half_len].astype(jnp.bfloat16), "fsdp", -1).astype(jnp.float32),
        shifted(value_acc[:half_len].astype(jnp.bfloat16), "fsdp", -1).astype(jnp.float32),
    )
    key_local = key_acc[half_len:] + key_back
    value_local = value_acc[half_len:] + value_back
    query_grad_heads = query_grad_blocks.reshape(half_len, head_count, HD)
    grad_query_tok, grad_key_tok, grad_value_tok = (
        lax.all_to_all(
            query_grad_heads.astype(jnp.bfloat16), "seq", split_axis=0, concat_axis=1, tiled=True
        ).astype(query_grad_heads.dtype),
        lax.all_to_all(
            key_local.astype(jnp.bfloat16), "seq", split_axis=0, concat_axis=1, tiled=True
        ).astype(key_local.dtype),
        lax.all_to_all(
            value_local.astype(jnp.bfloat16), "seq", split_axis=0, concat_axis=1, tiled=True
        ).astype(value_local.dtype),
    )
    if repeat > 1:
        grad_key_tok = grad_key_tok.reshape(token_count, KVH, repeat, HD).sum(2)
        grad_value_tok = grad_value_tok.reshape(token_count, KVH, repeat, HD).sum(2)
    query_lin_grad = (
        rotate_back(grad_query_tok, cosine, sine).astype(jnp.bfloat16).reshape(token_count, QH * HD)
    )
    key_lin_grad = (
        rotate_back(grad_key_tok, cosine, sine).astype(jnp.bfloat16).reshape(token_count, KVH * HD)
    )
    value_lin_grad = grad_value_tok.astype(jnp.bfloat16).reshape(token_count, KVH * HD)
    query_grad = jnp.einsum(
        "td,tc->dc", normed_low, query_lin_grad, preferred_element_type=jnp.float32
    )
    key_grad = jnp.einsum("td,tc->dc", normed_low, key_lin_grad, preferred_element_type=jnp.float32)
    value_grad = jnp.einsum(
        "td,tc->dc", normed_low, value_lin_grad, preferred_element_type=jnp.float32
    )
    grad_normed_one = jnp.einsum(
        "tc,dc->td", query_lin_grad, wq_full, preferred_element_type=jnp.float32
    )
    grad_normed_one = grad_normed_one + jnp.einsum(
        "tc,dc->td", key_lin_grad, wk_full, preferred_element_type=jnp.float32
    )
    grad_normed_one = grad_normed_one + jnp.einsum(
        "tc,dc->td", value_lin_grad, wv_full, preferred_element_type=jnp.float32
    )
    grad_rows_one, first_gain_grad = norm_backward(grad_normed_one, unit_one, scale_one, gain_one)
    input_grad = (grad_middle + grad_rows_one).astype(jnp.bfloat16)[None]
    pieces = (
        lax.psum_scatter(
            first_gain_grad.astype(jnp.bfloat16), "fsdp", scatter_dimension=0, tiled=True
        ).astype(jnp.float32),
        lax.psum_scatter(
            query_grad.astype(jnp.bfloat16), "fsdp", scatter_dimension=0, tiled=True
        ).astype(jnp.float32),
        lax.psum_scatter(
            key_grad.astype(jnp.bfloat16), "fsdp", scatter_dimension=0, tiled=True
        ).astype(jnp.float32),
        lax.psum_scatter(
            value_grad.astype(jnp.bfloat16), "fsdp", scatter_dimension=0, tiled=True
        ).astype(jnp.float32),
        lax.psum_scatter(
            output_grad.astype(jnp.bfloat16), "fsdp", scatter_dimension=0, tiled=True
        ).astype(jnp.float32),
        lax.psum_scatter(
            second_gain_grad.astype(jnp.bfloat16), "fsdp", scatter_dimension=0, tiled=True
        ).astype(jnp.float32),
        lax.psum_scatter(
            gate_grad.astype(jnp.bfloat16), "fsdp", scatter_dimension=0, tiled=True
        ).astype(jnp.float32),
        lax.psum_scatter(
            up_grad.astype(jnp.bfloat16), "fsdp", scatter_dimension=0, tiled=True
        ).astype(jnp.float32),
        lax.psum_scatter(
            down_grad.astype(jnp.bfloat16), "fsdp", scatter_dimension=0, tiled=True
        ).astype(jnp.float32),
    )
    shares = (
        lax.psum(pieces[0].astype(jnp.bfloat16), "seq").astype(jnp.float32),
        lax.psum(pieces[1].astype(jnp.bfloat16), "seq").astype(jnp.float32),
        lax.psum(pieces[2].astype(jnp.bfloat16), "seq").astype(jnp.float32),
        lax.psum(pieces[3].astype(jnp.bfloat16), "seq").astype(jnp.float32),
        lax.psum(pieces[4].astype(jnp.bfloat16), "seq").astype(jnp.float32),
        lax.psum(pieces[5].astype(jnp.bfloat16), "seq").astype(jnp.float32),
        lax.psum(pieces[6].astype(jnp.bfloat16), "seq").astype(jnp.float32),
        lax.psum(pieces[7].astype(jnp.bfloat16), "seq").astype(jnp.float32),
        lax.psum(pieces[8].astype(jnp.bfloat16), "seq").astype(jnp.float32),
    )
    return (
        block_output,
        input_grad,
        shares[0],
        shares[1],
        shares[2],
        shares[3],
        shares[4],
        shares[5],
        shares[6],
        shares[7],
        shares[8],
    )


def plain_solution(mesh):
    placed = (
        P("fsdp", "seq", None),
        P("fsdp", "seq"),
        P("fsdp"),
        P("fsdp", None),
        P("fsdp", None),
        P("fsdp", None),
        P("fsdp", None),
        P("fsdp"),
        P("fsdp", None),
        P("fsdp", None),
        P("fsdp", None),
        P("fsdp", "seq", None),
    )
    return jax.shard_map(
        plain_body,
        mesh=mesh,
        in_specs=placed,
        out_specs=(
            P("fsdp", "seq", None),
            P("fsdp", "seq", None),
            P("fsdp"),
            P("fsdp", None),
            P("fsdp", None),
            P("fsdp", None),
            P("fsdp", None),
            P("fsdp"),
            P("fsdp", None),
            P("fsdp", None),
            P("fsdp", None),
        ),
        check_vma=False,
    )
```

```python
import functools
import math

import jax
import jax.numpy as jnp
from jax import lax
from jax.experimental import pallas as pl
from jax.experimental.pallas import tpu as pltpu
from jax.sharding import Mesh
from jax.sharding import PartitionSpec as P

QH = 16
KVH = 8
HD = 96


THETA = 100000.0
EPS = 1e-05
LOW = jnp.bfloat16
F32 = jnp.float32
NEG = -1e30
LN2 = math.log(2.0)


def contract(left, right, left_axis, right_axis):
    return lax.dot_general(
        left, right, (((left_axis,), (right_axis,)), ((), ())), preferred_element_type=F32
    )


def visible(first, second, query_block, key_block, size):
    key = key_block * size + lax.broadcasted_iota(jnp.int32, (size, size), 0)
    query = query_block * size + lax.broadcasted_iota(jnp.int32, (1, size), 1)
    start = jnp.where(query >= second, second, jnp.where(query >= first, first, 0))
    return (key >= start) & (key <= query)


def slot_of(block, count):
    return (block % (count // 2)) * 2 + block // (count // 2)


def forward_kernel(
    scalars,
    own_ref,
    other_ref,
    low_ref,
    full_ref,
    log_ref,
    query_s,
    key_s,
    value_s,
    top_s,
    total_s,
    mixed_s,
    *,
    size,
    count,
):
    half = scalars[0]
    first = scalars[1]
    second = scalars[2]
    here = pl.program_id(0)
    per_half = count // 2

    @pl.when(here == 0)
    def _():
        for ref, side in ((own_ref, half), (other_ref, 1 - half)):
            for step in range(per_half):
                block = side * per_half + step
                columns = slice(step * size, (step + 1) * size)
                query_s[block] = ref[0:HD, columns]
                key_s[block] = ref[HD : 2 * HD, columns].T
                value_s[block] = ref[2 * HD : 3 * HD, columns]

    query = query_s[here]
    top_s[...] = jnp.full_like(top_s, NEG)
    total_s[...] = jnp.zeros_like(total_s)
    mixed_s[...] = jnp.zeros_like(mixed_s)

    def add_block(block, masked):
        scores = contract(key_s[block], query, 1, 0)
        if masked:
            scores = jnp.where(visible(first, second, here, block, size), scores, NEG)
        old_top = top_s[...]
        top = jnp.maximum(old_top, jnp.max(scores, 0, keepdims=True))
        expo = jnp.exp2(scores - top)
        scale = jnp.exp2(old_top - top)
        top_s[...] = top
        total_s[...] = total_s[...] * scale + jnp.sum(expo, 0, keepdims=True)
        mixed_s[...] = mixed_s[...] * scale + contract(value_s[block], expo.astype(LOW), 1, 0)

    last = count - 1

    @pl.loop(1, jnp.where(here == last, 1, here))
    def _(block):
        add_block(block, False)

    @pl.loop(0, jnp.where(here == last, count, jnp.minimum(here + 1, 2)))
    def _(step):
        add_block(jnp.where(here == last, step, step * here), True)

    total = total_s[...]
    result = mixed_s[...] / total
    full_ref[0] = result
    low_ref[0] = result.astype(LOW)
    log_ref[0] = top_s[...] + jnp.log2(total)


def backward_kernel(
    scalars,
    own_ref,
    other_ref,
    grad_ref,
    full_ref,
    log_ref,
    kept_ref,
    leaving_ref,
    query_s,
    key_s,
    value_s,
    delta_s,
    query_grad_s,
    key_grad_s,
    value_grad_s,
    *,
    size,
    count,
):
    half = scalars[0]
    first = scalars[1]
    second = scalars[2]
    here = pl.program_id(0)
    per_half = count // 2

    @pl.when(here == 0)
    def _():
        for ref, side in ((own_ref, half), (other_ref, 1 - half)):
            for step in range(per_half):
                block = side * per_half + step
                columns = slice(step * size, (step + 1) * size)
                query_s[block] = ref[0:HD, columns]
                key_s[block] = ref[HD : 2 * HD, columns]
                value_s[block] = ref[2 * HD : 3 * HD, columns].T
        for block in range(count):
            delta_s[block] = jnp.sum(
                grad_ref[slot_of(block, count)].astype(F32) * full_ref[block], 0, keepdims=True
            )
        query_grad_s[...] = jnp.zeros_like(query_grad_s)

    key_grad_s[...] = jnp.zeros_like(key_grad_s)
    value_grad_s[...] = jnp.zeros_like(value_grad_s)
    key = key_s[here]
    key_rows = key.T
    value_rows = value_s[here]

    def add_block(block, masked):
        query = query_s[block]
        grad = grad_ref[slot_of(block, count)]
        scores = contract(key_rows, query, 1, 0)
        if masked:
            scores = jnp.where(visible(first, second, block, here, size), scores, NEG)
        probs = jnp.exp2(scores - log_ref[block])
        grad_probs = contract(value_rows, grad, 1, 0)
        grad_scores = (probs * (grad_probs - delta_s[block])).astype(LOW)
        value_grad_s[...] += contract(grad, probs.astype(LOW), 1, 1)
        key_grad_s[...] += contract(query, grad_scores, 1, 1)
        query_grad_s[block] += contract(key, grad_scores, 1, 0)

    last = count - 1

    @pl.loop(here + 1, jnp.where(here == 0, 1, last))
    def _(block):
        add_block(block, False)

    @pl.loop(0, jnp.where(here == 0, count, jnp.where(here == last, 1, 2)))
    def _(step):
        add_block(jnp.where(here == 0, step, jnp.where(step == 0, here, last)), True)

    side = here // per_half
    columns = pl.ds(pl.multiple_of((here % per_half) * size, size), size)

    def write(out_ref):
        out_ref[0:HD, columns] = (query_grad_s[here] * HD**-0.5).astype(LOW)
        out_ref[HD : 2 * HD, columns] = (key_grad_s[...] * LN2).astype(LOW)
        out_ref[2 * HD : 3 * HD, columns] = value_grad_s[...].astype(LOW)

    @pl.when(side == half)
    def _():
        write(kept_ref)

    @pl.when(side != half)
    def _():
        write(leaving_ref)


def attend_forward(scalars, own, other, size):
    count = 2 * own.shape[1] // size
    whole = lambda shape: pl.BlockSpec(shape, lambda i, s: (0,) * len(shape))
    pairs = count * (count + 1) // 2
    return pl.pallas_call(
        functools.partial(forward_kernel, size=size, count=count),
        grid_spec=pltpu.PrefetchScalarGridSpec(
            num_scalar_prefetch=1,
            grid=(count,),
            in_specs=[whole(own.shape), whole(other.shape)],
            out_specs=[
                pl.BlockSpec(
                    (1, HD, size), lambda i, s: (slot_of(i, count), 0, 0)
                ),
                pl.BlockSpec((1, HD, size), lambda i, s: (i, 0, 0)),
                pl.BlockSpec((1, 1, size), lambda i, s: (i, 0, 0)),
            ],
            scratch_shapes=[
                pltpu.VMEM((count, HD, size), LOW),
                pltpu.VMEM((count, size, HD), LOW),
                pltpu.VMEM((count, HD, size), LOW),
                pltpu.VMEM((1, size), F32),
                pltpu.VMEM((1, size), F32),
                pltpu.VMEM((HD, size), F32),
            ],
        ),
        out_shape=[
            jax.ShapeDtypeStruct((count, HD, size), LOW),
            jax.ShapeDtypeStruct((count, HD, size), F32),
            jax.ShapeDtypeStruct((count, 1, size), F32),
        ],
        compiler_params=pltpu.CompilerParams(
            dimension_semantics=("arbitrary",), vmem_limit_bytes=32 * 2**20
        ),
        cost_estimate=pl.CostEstimate(
            flops=pairs * size * size * HD * 32,
            bytes_accessed=10 * 2**20,
            transcendentals=pairs * size * size,
        ),
        name="attend_forward",
    )(scalars, own, other)


def attend_backward(scalars, own, other, grad, full, log_total):
    count, _, size = grad.shape
    whole = lambda shape: pl.BlockSpec(shape, lambda i, s: (0,) * len(shape))
    pairs = count * (count + 1) // 2
    out_shape = own.shape
    return pl.pallas_call(
        functools.partial(backward_kernel, size=size, count=count),
        grid_spec=pltpu.PrefetchScalarGridSpec(
            num_scalar_prefetch=1,
            grid=(count,),
            in_specs=[
                whole(own.shape),
                whole(other.shape),
                whole(grad.shape),
                whole(full.shape),
                whole(log_total.shape),
            ],
            out_specs=[whole(out_shape)] * 2,
            scratch_shapes=[
                pltpu.VMEM((count, HD, size), LOW),
                pltpu.VMEM((count, HD, size), LOW),
                pltpu.VMEM((count, size, HD), LOW),
                pltpu.VMEM((count, 1, size), F32),
                pltpu.VMEM((count, HD, size), F32),
                pltpu.VMEM((HD, size), F32),
                pltpu.VMEM((HD, size), F32),
            ],
        ),
        out_shape=[jax.ShapeDtypeStruct(out_shape, LOW)] * 2,
        compiler_params=pltpu.CompilerParams(
            dimension_semantics=("arbitrary",), vmem_limit_bytes=32 * 2**20
        ),
        cost_estimate=pl.CostEstimate(
            flops=pairs * size * size * HD * 42,
            bytes_accessed=16 * 2**20,
            transcendentals=pairs * size * size,
        ),
        name="attend_backward",
    )(scalars, own, other, grad, full, log_total)


def place_rows_kernel(order, *refs):
    pieces, out_ref = refs[:-1], refs[-1]
    size = pieces[0].shape[0]
    for index, piece in enumerate(pieces):
        start = pl.multiple_of(order[index] * size, size)
        out_ref[pl.ds(start, size), :] = piece[...].astype(F32)


def place_rows(order, pieces):
    size, width = pieces[0].shape
    total = size * len(pieces)
    step = 512
    return pl.pallas_call(
        place_rows_kernel,
        grid_spec=pltpu.PrefetchScalarGridSpec(
            num_scalar_prefetch=1,
            grid=(width // step,),
            in_specs=[pl.BlockSpec((size, step), lambda i, s: (0, i)) for _ in pieces],
            out_specs=pl.BlockSpec((total, step), lambda i, s: (0, i)),
        ),
        out_shape=jax.ShapeDtypeStruct((total, width), F32),
        compiler_params=pltpu.CompilerParams(vmem_limit_bytes=24 * 2**20),
        cost_estimate=pl.CostEstimate(
            flops=0, bytes_accessed=total * width * 6, transcendentals=0
        ),
        name="place_rows",
    )(order, *pieces)


def place_columns_kernel(order, gain_ref, gate_w_ref, up_w_ref, *refs):
    count = (len(refs) - 3) // 2
    gates, ups = refs[:count], refs[count : 2 * count]
    gate_ref, up_ref, sum_ref = refs[2 * count :]
    size = gates[0].shape[1]
    gain = gain_ref[...]
    total = jnp.zeros((gate_ref.shape[0], size), F32)
    for index in range(count):
        columns = pl.ds(pl.multiple_of(order[index] * size, size), size)
        gate, up = gates[index][...].astype(F32), ups[index][...].astype(F32)
        total += gate * gate_w_ref[:, columns].astype(F32)
        total += up * up_w_ref[:, columns].astype(F32)
        gate_ref[:, columns] = gate * gain
        up_ref[:, columns] = up * gain

    @pl.when(pl.program_id(0) == 0)
    def _():
        sum_ref[...] = jnp.zeros_like(sum_ref)

    sum_ref[...] += jnp.sum(total, 1, keepdims=True)


def place_columns(order, gain, gate_weight, up_weight, gates, ups, shards):
    rows, width = gate_weight.shape
    span = width // shards
    size = span // len(gates)
    wide = pl.BlockSpec((rows, span), lambda i, s: (0, i))
    thin = pl.BlockSpec((rows, 1), lambda i, s: (0, 0))
    pieces = [pl.BlockSpec((rows, size), lambda i, s: (0, i)) for _ in (*gates, *ups)]
    return pl.pallas_call(
        place_columns_kernel,
        grid_spec=pltpu.PrefetchScalarGridSpec(
            num_scalar_prefetch=1,
            grid=(shards,),
            in_specs=[thin, wide, wide, *pieces],
            out_specs=[wide, wide, thin],
        ),
        out_shape=[
            jax.ShapeDtypeStruct((rows, width), F32),
            jax.ShapeDtypeStruct((rows, width), F32),
            jax.ShapeDtypeStruct((rows, 1), F32),
        ],
        compiler_params=pltpu.CompilerParams(
            dimension_semantics=("arbitrary",), vmem_limit_bytes=24 * 2**20
        ),
        cost_estimate=pl.CostEstimate(
            flops=rows * width * 6, bytes_accessed=rows * width * 16, transcendentals=0
        ),
        name="place_columns",
    )(order, gain, gate_weight, up_weight, *gates, *ups)


def place_heads_kernel(gain_ref, query_w, key_w, value_w, all_ref, query_ref, key_ref, value_ref, sum_ref):
    rows = gain_ref.shape[0]
    wide = query_ref.shape[1] // KVH
    gain = gain_ref[...]
    total = jnp.zeros((rows, 4 * HD), F32)
    pieces = [all_ref[i * rows : (i + 1) * rows, :].astype(F32) for i in range(KVH)]
    for start in range(0, KVH, 2):
        value = jnp.concatenate([piece[:, :wide] for piece in pieces[start : start + 2]], 1)
        columns = slice(start * wide, (start + 2) * wide)
        total += value * query_w[:, columns].astype(F32)
        query_ref[:, columns] = value * gain
    for first, weight, out_ref in ((wide, key_w, key_ref), (wide + HD, value_w, value_ref)):
        for start in range(0, KVH, 4):
            value = jnp.concatenate(
                [piece[:, first : first + HD] for piece in pieces[start : start + 4]], 1
            )
            columns = slice(start * HD, (start + 4) * HD)
            total += value * weight[:, columns].astype(F32)
            out_ref[:, columns] = value * gain
    sum_ref[...] = jnp.sum(total, 1, keepdims=True)


def place_heads(gain, query_weight, key_weight, value_weight, pieces):
    weights = (query_weight, key_weight, value_weight)
    rows = gain.shape[0]
    return pl.pallas_call(
        place_heads_kernel,
        out_shape=[jax.ShapeDtypeStruct(weight.shape, F32) for weight in weights]
        + [jax.ShapeDtypeStruct((rows, 1), F32)],
        compiler_params=pltpu.CompilerParams(vmem_limit_bytes=32 * 2**20),
        cost_estimate=pl.CostEstimate(
            flops=rows * 3072 * 4, bytes_accessed=rows * 3072 * 8, transcendentals=0
        ),
        name="place_heads",
    )(gain, *weights, pieces)


def merge_kernel(scalars, kept_ref, came_ref, cosine_ref, sine_ref, out_ref, split_ref):
    lead = scalars[0] == 0
    lines, _, size = split_ref.shape
    for line in range(lines):
        columns = slice(line * size, (line + 1) * size)
        kept = kept_ref[:, columns].astype(F32)
        came = came_ref[:, columns].astype(F32)
        cosine, sine = cosine_ref[:, columns], sine_ref[:, columns]
        joint = kept[HD:] + came[HD:]
        first = jnp.where(lead, kept[:HD], came[:HD])
        second = jnp.where(lead, came[:HD], kept[:HD])
        turned = []
        for value in (first, second, joint[:HD]):
            low, high = value[: HD // 2], value[HD // 2 :]
            turned.append(low * cosine + high * sine)
            turned.append(high * cosine - low * sine)
        turned.append(joint[HD:])
        result = jnp.concatenate([part.astype(LOW) for part in turned], 0)
        out_ref[:, columns] = result
        split_ref[line] = result


def merge(scalars, kept, came, cosine, sine, lines):
    tokens = kept.shape[1]
    whole = lambda value: pl.BlockSpec(value.shape, lambda i, s: (0,) * len(value.shape))
    outs = [
        jax.ShapeDtypeStruct((4 * HD, tokens), LOW),
        jax.ShapeDtypeStruct((lines, 4 * HD, tokens // lines), LOW),
    ]
    return pl.pallas_call(
        merge_kernel,
        grid_spec=pltpu.PrefetchScalarGridSpec(
            num_scalar_prefetch=1,
            grid=(1,),
            in_specs=[whole(value) for value in (kept, came, cosine, sine)],
            out_specs=[whole(value) for value in outs],
        ),
        out_shape=outs,
        compiler_params=pltpu.CompilerParams(vmem_limit_bytes=24 * 2**20),
        cost_estimate=pl.CostEstimate(
            flops=tokens * HD * 24, bytes_accessed=tokens * HD * 30, transcendentals=0
        ),
        name="merge",
    )(scalars, kept, came, cosine, sine)


def pack_kernel(scalars, gain_ref, query_ref, key_ref, value_ref, *outs):
    core = scalars[3]
    gain = gain_ref[...]
    wide = query_ref.shape[1] // KVH
    span = wide + 2 * HD
    for which in range(2):

        @pl.when(core == which)
        def _():
            for line in range(KVH // 2):
                head = 2 * line + which
                value = jnp.concatenate(
                    [
                        query_ref[:, head * wide : (head + 1) * wide].astype(F32),
                        key_ref[:, head * HD : (head + 1) * HD].astype(F32),
                        value_ref[:, head * HD : (head + 1) * HD].astype(F32),
                    ],
                    1,
                )
                place = (line % 2) * span
                outs[line // 2][:, place : place + span] = (value * gain).astype(LOW)


def pack(scalars, gain, query_weight, key_weight, value_weight):
    rows, width = query_weight.shape
    whole = lambda value: pl.BlockSpec(value.shape, lambda i, s: (0, 0))
    weights = (gain, query_weight, key_weight, value_weight)
    outs = [jax.ShapeDtypeStruct((rows, width // 2), LOW)] * 2
    return pl.pallas_call(
        pack_kernel,
        grid_spec=pltpu.PrefetchScalarGridSpec(
            num_scalar_prefetch=1,
            grid=(1,),
            in_specs=[whole(value) for value in weights],
            out_specs=[whole(value) for value in outs],
        ),
        out_shape=outs,
        compiler_params=pltpu.CompilerParams(vmem_limit_bytes=24 * 2**20),
        cost_estimate=pl.CostEstimate(
            flops=rows * width, bytes_accessed=rows * width * 6, transcendentals=0
        ),
        name="pack",
    )(scalars, *weights)


def spread_kernel(scalars, lin_ref, cosine_ref, sine_ref, own_ref, leaving_ref):
    cosine, sine = cosine_ref[...], sine_ref[...]

    def turn(start, factor):
        low = lin_ref[start : start + HD // 2, :]
        high = lin_ref[start + HD // 2 : start + HD, :]
        turned = ((low * cosine - high * sine) * factor, (high * cosine + low * sine) * factor)
        return jnp.concatenate([part.astype(LOW) for part in turned], 0)

    lead = scalars[0] == 0
    first, second = turn(0, HD**-0.5 / LN2), turn(HD, HD**-0.5 / LN2)

    @pl.when(lead)
    def _():
        own_ref[0:HD] = first
        leaving_ref[0:HD] = second

    @pl.when(jnp.logical_not(lead))
    def _():
        own_ref[0:HD] = second
        leaving_ref[0:HD] = first

    key = turn(2 * HD, 1.0)
    value = lin_ref[3 * HD : 4 * HD].astype(LOW)
    for ref in (own_ref, leaving_ref):
        ref[HD : 2 * HD] = key
        ref[2 * HD : 3 * HD] = value


def spread(scalars, lin, cosine, sine):
    tokens = lin.shape[1]
    step = 512
    column = lambda rows: pl.BlockSpec((rows, step), lambda i, s: (0, i))
    return pl.pallas_call(
        spread_kernel,
        grid_spec=pltpu.PrefetchScalarGridSpec(
            num_scalar_prefetch=1,
            grid=(tokens // step,),
            in_specs=[column(4 * HD), column(HD // 2), column(HD // 2)],
            out_specs=[column(3 * HD)] * 2,
        ),
        out_shape=[jax.ShapeDtypeStruct((3 * HD, tokens), LOW)] * 2,
        compiler_params=pltpu.CompilerParams(vmem_limit_bytes=24 * 2**20),
        cost_estimate=pl.CostEstimate(
            flops=tokens * HD * 24, bytes_accessed=tokens * HD * 36, transcendentals=0
        ),
        name="spread",
    )(scalars, lin, cosine, sine)


def swap(value, axis):
    return lax.ppermute(value, axis, [(0, 1), (1, 0)])


def swap_near(value):
    return lax.ppermute(value, "z", [(0, 1), (1, 0), (2, 3), (3, 2)])


def swap_far(value):
    return lax.ppermute(value, "z", [(0, 2), (2, 0), (1, 3), (3, 1)])


def tie(*values):
    return lax.optimization_barrier(values)


def in_order(place, own, other):
    return (jnp.where(place == 0, own, other), jnp.where(place == 0, other, own))


def both(place, own, other):
    return jnp.concatenate(in_order(place, own, other), 0)


def spread_out(value, first, second):
    other = swap(value, first)
    pair = jnp.stack(in_order(lax.axis_index(first), value, other))
    return pair, swap(pair, second)


def placed(pair, other, second):
    pairs = in_order(lax.axis_index(second), pair, other)
    grid = jnp.stack(pairs, 0 if second == "y" else 1)
    return grid.reshape(-1, *grid.shape[3:])


def pick(array, axis, at):
    return lax.dynamic_index_in_dim(array, at, axis, keepdims=False)


def halve(value, axis, along=0):
    at = lax.axis_index(axis)
    return pick(value, along, at), swap(pick(value, along, 1 - at), axis)


def halve_x(value):
    return halve(value.reshape(2, 2, -1, value.shape[-1]), "x", 1)


def halve_y(value):
    return halve(value.reshape(2, 2, -1, value.shape[-1]), "y", 0)


def fast_body(
    tokens,
    positions,
    first_gain,
    query_weight,
    key_weight,
    value_weight,
    output_weight,
    second_gain,
    gate_weight,
    up_weight,
    down_weight,
    cotangent,
):
    seq = ("z", "c")
    fsdp = ("y", "x")
    z, core, half = lax.axis_index("z"), lax.axis_index("c"), lax.axis_index("x")
    near = z % 2
    lines = lax.axis_size("z")
    seq_count = 2 * lines
    shards = lax.axis_size("y") * 2
    spot = z * 2 + core
    quarter = near * 2 + core
    rows = tokens[0]
    count, width = rows.shape
    chip_count = 2 * count
    half_len = count * seq_count
    seq_len = 2 * half_len

    begins = jnp.where(
        (spot == 0) & (half == 0),
        count - 1 - positions[0, count - 1],
        half * half_len + spot * count - positions[0, 0],
    )
    ends = begins + (seq_len - count)
    scalars = jnp.stack([half, begins, ends, core]).astype(jnp.int32)

    gain_one = first_gain.astype(F32)[:, None]
    gain_two = second_gain.astype(F32)[:, None]

    def row_scale(value):
        return lax.rsqrt(jnp.mean(value * value, -1, keepdims=True) + EPS)

    take = functools.partial(lax.dynamic_slice_in_dim, axis=1)
    take_rows = functools.partial(lax.dynamic_slice_in_dim, axis=0)
    gather = lambda value, axes: lax.all_gather(value, axes, axis=0, tiled=True)
    own_rows = rows.astype(F32)
    own_unit_scale = row_scale(own_rows)
    own_unit = own_rows * own_unit_scale
    units = gather(own_unit.astype(LOW), seq)
    wide = QH // KVH * HD
    qkv_shard = (
        jnp.concatenate(
            [
                take(query_weight, spot * wide, wide),
                take(key_weight, spot * HD, HD),
                take(value_weight, spot * HD, HD),
            ],
            1,
        ).astype(F32)
        * gain_one
    ).astype(LOW)
    out_rows = output_weight.shape[0] // 2
    out_shard = take_rows(output_weight, core * out_rows, out_rows)
    piece = down_weight.shape[0] // 4
    down_shard = take_rows(down_weight, quarter * piece, piece)
    gate_shard, up_shard = (
        (
            jnp.concatenate(
                [
                    take(weight, shard * 4 * piece + quarter * piece, piece)
                    for shard in range(shards)
                ],
                1,
            ).astype(F32)
            * gain_two
        ).astype(LOW)
        for weight in (gate_weight, up_weight)
    )
    side = lax.axis_index("y")
    qkv_pair = jnp.stack(in_order(half, qkv_shard, swap(qkv_shard, "x")))
    gate_pair = jnp.stack(in_order(half, gate_shard, swap(gate_shard, "x")))
    up_pair = jnp.stack(in_order(side, up_shard, swap(up_shard, "y")))
    qkv_pair, gate_pair, up_pair = tie(qkv_pair, gate_pair, up_pair)
    qkv_w = placed(qkv_pair, swap(qkv_pair, "y"), "y")
    gate_pair, up_pair = (gate_pair, swap(gate_pair, "y")), (up_pair, swap(up_pair, "x"))

    place = half * half_len + jnp.arange(half_len, dtype=jnp.int32)
    start = jnp.where(place >= ends, ends, jnp.where(place >= begins, begins, 0))
    freq = THETA ** (-(jnp.arange(HD // 2, dtype=F32) * 2.0 / HD))
    angle = freq[:, None] * (place - start).astype(F32)[None, :]
    cosine, sine = jnp.cos(angle), jnp.sin(angle)
    chip_rows = both(core, rows, swap(rows, "c"))
    units, own_cot, chip_rows = tie(units, cotangent[0], chip_rows)
    own, leaving = spread(scalars, contract(qkv_w, units, 0, 1), cosine, sine)
    leaving, gate_pair, up_pair = tie(leaving, gate_pair, up_pair)

    near_cot = swap_near(own_cot)
    other, out_shard, down_shard, near_cot, chip_cot, gate_pair, up_pair = tie(
        swap(leaving, "x"),
        out_shard,
        down_shard,
        near_cot,
        both(core, own_cot, swap(own_cot, "c")),
        gate_pair,
        up_pair,
    )
    out_w = gather(out_shard, fsdp)
    down_w = gather(down_shard, fsdp)
    near_cot = jnp.concatenate([near_cot, swap(near_cot, "c")], 0)
    head_low, head_full, log_total = attend_forward(scalars, own, other, chip_count)
    exchange = lambda value: lax.all_to_all(
        value, ("z", "x"), split_axis=0, concat_axis=0, tiled=True
    )
    head_low, gate_pair, up_pair, near_cot = tie(head_low, gate_pair, up_pair, near_cot)
    heads, gate_w, up_w = tie(
        exchange(head_low), placed(*gate_pair, "y"), placed(*up_pair, "x")
    )
    heads = heads.reshape(QH // 2 * HD, chip_count)

    mine_of = lambda value: take_rows(value, core * count, count)
    theirs_of = lambda value: take_rows(value, (1 - core) * count, count)
    branch = contract(heads, out_w, 0, 0).astype(LOW)
    middle = chip_rows.astype(F32) + (branch.astype(F32) + swap(branch, "c").astype(F32))
    middle_scale = row_scale(middle)
    chip_unit = middle * middle_scale
    own_middle, own_scale, own_middle_unit = (
        mine_of(middle),
        mine_of(middle_scale),
        mine_of(chip_unit),
    )
    chip_unit = chip_unit.astype(LOW)
    near_unit = swap_near(mine_of(chip_unit))
    near_unit = jnp.concatenate([near_unit, swap(near_unit, "c")], 0)

    def feed(unit):
        gate, upper = contract(unit, gate_w, 1, 0), contract(unit, up_w, 1, 0)
        sigma = jax.nn.sigmoid(gate)
        silu = gate * sigma
        return (silu * upper).astype(LOW), (gate, upper, sigma, silu)

    def feed_back(cot, kept):
        gate, upper, sigma, silu = kept
        grad_hidden = contract(cot, down_w, 1, 1)
        gate_low = (grad_hidden * upper * sigma * (1.0 + gate * (1.0 - sigma))).astype(LOW)
        upper_low = (grad_hidden * silu).astype(LOW)
        part = contract(gate_low, gate_w, 1, 1) + contract(upper_low, up_w, 1, 1)
        return gate_low, upper_low, part

    def chip_sum(chip_part, near_part):
        near_sum = near_part[:count].astype(F32) + swap(near_part[count:].astype(LOW), "c")
        own_sum = mine_of(chip_part).astype(F32) + swap(theirs_of(chip_part).astype(LOW), "c")
        return own_sum, near_sum.astype(LOW)

    stack = lambda first, second: jnp.concatenate([first, second], 0)
    scatter = lambda value: lax.psum_scatter(value, fsdp, scatter_dimension=0, tiled=True)
    chip_hidden, chip_kept = feed(chip_unit)
    near_hidden, near_kept = feed(near_unit)
    down_part = contract(
        stack(chip_hidden, near_hidden), stack(chip_cot, near_cot), 0, 0
    ).astype(LOW)
    near_cot, down_part = tie(near_cot, down_part)
    down_grad = scatter(down_part)
    near_gate, near_upper, near_part = feed_back(near_cot, near_kept)
    chip_gate, chip_upper, chip_part = feed_back(chip_cot, chip_kept)
    grad_two, near_sum = chip_sum(chip_part, near_part)
    grad_two = grad_two + swap_near(near_sum).astype(F32)

    def halves_first(value):
        cut = value.shape[-1] // 2
        return halve_x(value[:, :cut]), halve_y(value[:, cut:])

    def halves_second(firsts):
        return halve(sum(firsts[0]), "y"), halve(sum(firsts[1]), "x")

    def halves_end(seconds):
        return jnp.concatenate([sum(seconds[0]), sum(seconds[1])], 1)

    all_units = stack(chip_unit, near_unit)
    gate_part = contract(all_units, stack(chip_gate, near_gate), 0, 0).astype(LOW)
    gate_first = halves_first(gate_part)
    up_part = contract(all_units, stack(chip_upper, near_upper), 0, 0).astype(LOW)
    grad_two, gate_part, up_part = tie(grad_two, gate_part, up_part)
    grad_middle = own_cot.astype(F32) + own_scale * (
        grad_two - own_middle_unit * jnp.mean(grad_two * own_middle_unit, -1, keepdims=True)
    )
    own_branch = grad_middle.astype(LOW)
    grad_branch = both(core, own_branch, swap(own_branch, "c"))
    grad_heads = contract(out_w, grad_branch, 1, 1).astype(LOW)
    grad_heads, grad_branch, gate_first, down_grad, up_part = tie(
        grad_heads, grad_branch, gate_first, down_grad, up_part
    )

    down_far = swap_far(down_grad)
    gate_second = halves_second(gate_first)
    up_first = halves_first(up_part)
    output_part = contract(heads, grad_branch, 1, 0).astype(LOW)
    feed_own, feed_near = chip_sum(
        contract(chip_hidden, down_w, 1, 0), contract(near_hidden, down_w, 1, 0)
    )
    grad_head, output_part, down_far, gate_second, up_first, feed_own, feed_near = tie(
        exchange(grad_heads.reshape(2 * lines, HD, chip_count)),
        output_part,
        down_far,
        gate_second,
        up_first,
        feed_own,
        feed_near,
    )

    output_grad = scatter(output_part)
    gate_grad = halves_end(gate_second)
    gate_far = swap_far(gate_grad)
    up_second = halves_second(up_first)
    feed_near = swap_near(feed_near)
    kept, leaving = attend_backward(scalars, own, other, grad_head, head_full, log_total)
    kept, leaving, gate_far, up_second, feed_near = tie(
        kept, leaving, gate_far, up_second, feed_near
    )

    lead_shard, tail_shard = pack(scalars, gain_one, query_weight, key_weight, value_weight)
    up_grad = halves_end(up_second)
    up_far = swap_far(up_grad)
    down_sum = down_grad + down_far
    down_near = swap_near(down_sum)
    block_output = (own_middle + feed_own + feed_near.astype(F32)).astype(LOW)[None]
    came, up_far, down_near, block_output, output_grad = tie(
        swap(leaving, "x"), up_far, down_near, block_output, output_grad
    )

    place = lax.axis_index("z")
    inner = (place == 1) | (place == 2)
    qkv_low, by_line = merge(scalars, kept, came, cosine, sine, lines)
    token_grads = lax.all_to_all(by_line, "z", split_axis=0, concat_axis=0, tiled=True)
    qkv_part = contract(units, qkv_low, 0, 1).astype(LOW).reshape(shards, 2, -1, 4 * HD)
    qkv_first = halve_x(qkv_part[:, 0]), halve_y(qkv_part[:, 1])
    output_came = lax.ppermute(output_grad, "z", [(0, 1), (3, 2)])
    gate_sum = gate_grad + gate_far
    gate_near = swap_near(gate_sum)
    up_sum = up_grad + up_far
    lead_w, tail_w = gather(lead_shard, fsdp), gather(tail_shard, fsdp)
    token_grads, qkv_first, output_came, gate_near, up_sum = tie(
        token_grads, qkv_first, output_came, gate_near, up_sum
    )

    up_near = swap_near(up_sum)
    output_sum = output_grad + output_came
    output_sum = output_sum + lax.ppermute(output_sum, "z", [(1, 2), (2, 1)])
    qkv_second = halves_second(qkv_first)
    qkv_grad = jnp.concatenate([sum(qkv_second[0]), sum(qkv_second[1])], 0)
    token_grads = token_grads.reshape(-1, chip_count)
    split = lead_w.shape[1]
    grad_one = contract(token_grads[:split], lead_w, 0, 1) + contract(
        token_grads[split:], tail_w, 0, 1
    )
    grad_one = mine_of(grad_one) + swap(theirs_of(grad_one).astype(LOW), "c").astype(F32)
    grad_rows = own_unit_scale * (
        grad_one - own_unit * jnp.mean(grad_one * own_unit, -1, keepdims=True)
    )
    input_grad = (grad_middle + grad_rows).astype(LOW)[None]
    output_far = lax.ppermute(output_sum, "z", [(1, 0), (2, 3)])
    output_own = jnp.where(inner, output_sum, output_far)

    def four(value, near_value):
        return value, swap(value, "c"), near_value, swap(near_value, "c")

    order = jnp.stack([quarter, quarter ^ 1, quarter ^ 2, quarter ^ 3]).astype(jnp.int32)
    core_order = jnp.stack([core, 1 - core]).astype(jnp.int32)
    down_total = place_rows(order, four(down_sum, down_near))
    output_total = place_rows(core_order, (output_own, swap(output_own, "c")))
    gate_total, up_total, second_gain_grad = place_columns(
        order, gain_two, gate_weight, up_weight, four(gate_sum, gate_near), four(up_sum, up_near), shards
    )
    query_grad, key_grad, value_grad, first_gain_grad = place_heads(
        gain_one, query_weight, key_weight, value_weight, gather(qkv_grad, seq)
    )
    return (
        block_output,
        input_grad,
        first_gain_grad[:, 0],
        query_grad,
        key_grad,
        value_grad,
        output_total,
        second_gain_grad[:, 0],
        gate_total,
        up_total,
        down_total,
    )


def fast_solution(mesh):
    seq_count, shard_count = mesh.devices.shape
    fine = Mesh(
        mesh.devices.reshape(seq_count // 2, 2, shard_count // 2, 2), ("z", "c", "y", "x")
    )
    seq, fsdp = ("z", "c"), ("y", "x")
    matrix = P(fsdp, None)
    return jax.shard_map(
        fast_body,
        mesh=fine,
        in_specs=(
            P(fsdp, seq, None),
            P(fsdp, seq),
            P(fsdp),
            matrix,
            matrix,
            matrix,
            matrix,
            P(fsdp),
            matrix,
            matrix,
            matrix,
            P(fsdp, seq, None),
        ),
        out_specs=(
            P(fsdp, seq, None),
            P(fsdp, seq, None),
            P(fsdp),
            matrix,
            matrix,
            matrix,
            matrix,
            P(fsdp),
            matrix,
            matrix,
            matrix,
        ),
        check_vma=False,
    )


def solution(mesh):
    shape = dict(mesh.shape)
    if shape["seq"] == KVH and shape["fsdp"] == 4:
        return fast_solution(mesh)
    return plain_solution(mesh)


def shifted(value, axis, steps):
    count = lax.axis_size(axis)
    first, last = (max(0, -steps), min(count, count - steps))
    return lax.ppermute(value, axis, [(source, source + steps) for source in range(first, last)])


def rope_tables(position_rows):
    freq = THETA ** (-(jnp.arange(HD // 2, dtype=jnp.float32) * 2.0 / HD))
    angle = position_rows.astype(jnp.float32)[:, None] * freq[None, :]
    cosine = jnp.cos(angle)
    sine = jnp.sin(angle)
    return (jnp.concatenate([cosine, cosine], -1), jnp.concatenate([sine, sine], -1))


def rotate(values, cosine, sine):
    half = HD // 2
    turned = jnp.concatenate([-values[..., half:], values[..., :half]], -1)
    return values * cosine[:, None, :] + turned * sine[:, None, :]


def rotate_back(grads, cosine, sine):
    half = HD // 2
    scaled = grads * sine[:, None, :]
    turned = jnp.concatenate([scaled[..., half:], -scaled[..., :half]], -1)
    return grads * cosine[:, None, :] + turned


def norm_forward(rows, gain):
    scale = lax.rsqrt(jnp.mean(rows * rows, -1, keepdims=True) + EPS)
    unit = rows * scale
    return (unit * gain, unit, scale)


def norm_backward(grad_out, unit, scale, gain):
    grad_unit = grad_out * gain
    gain_grad = jnp.sum(grad_out * unit, 0)
    grad_rows = scale * (grad_unit - unit * jnp.mean(grad_unit * unit, -1, keepdims=True))
    return (grad_rows, gain_grad)


def plain_body(
    tokens,
    positions,
    first_gain,
    query_weight,
    key_weight,
    value_weight,
    output_weight,
    second_gain,
    gate_weight,
    up_weight,
    down_weight,
    cotangent,
):
    seq_count = lax.axis_size("seq")
    local_rows = tokens[0]
    token_count = local_rows.shape[0]
    half_len = token_count * seq_count
    rows_float = local_rows.astype(jnp.float32)
    gain_one, wq_full, wk_full, wv_full, wo_full = (
        lax.all_gather(first_gain, "fsdp", axis=0, tiled=True),
        lax.all_gather(query_weight, "fsdp", axis=0, tiled=True),
        lax.all_gather(key_weight, "fsdp", axis=0, tiled=True),
        lax.all_gather(value_weight, "fsdp", axis=0, tiled=True),
        lax.all_gather(output_weight, "fsdp", axis=0, tiled=True),
    )
    gain_one = gain_one.astype(jnp.float32)
    normed_one, unit_one, scale_one = norm_forward(rows_float, gain_one)
    normed_low = normed_one.astype(jnp.bfloat16)
    cosine, sine = rope_tables(positions[0])
    query_lin = jnp.dot(normed_low, wq_full, preferred_element_type=jnp.float32).reshape(
        token_count, QH, HD
    )
    key_lin = jnp.dot(normed_low, wk_full, preferred_element_type=jnp.float32).reshape(
        token_count, KVH, HD
    )
    value_lin = jnp.dot(normed_low, wv_full, preferred_element_type=jnp.float32).reshape(
        token_count, KVH, HD
    )
    query_rows = rotate(query_lin, cosine, sine).astype(jnp.bfloat16)
    key_rows = rotate(key_lin, cosine, sine).astype(jnp.bfloat16)
    value_rows = value_lin.astype(jnp.bfloat16)
    repeat = max(1, seq_count // KVH)
    if repeat > 1:
        key_rows = jnp.repeat(key_rows, repeat, axis=1)
        value_rows = jnp.repeat(value_rows, repeat, axis=1)
    query_heads, key_heads, value_heads = (
        lax.all_to_all(query_rows, "seq", split_axis=1, concat_axis=0, tiled=True),
        lax.all_to_all(key_rows, "seq", split_axis=1, concat_axis=0, tiled=True),
        lax.all_to_all(value_rows, "seq", split_axis=1, concat_axis=0, tiled=True),
    )
    head_count = query_heads.shape[1]
    pair_count = key_heads.shape[1]
    group = head_count // pair_count
    half_positions = lax.all_gather(positions[0], "seq", axis=0, tiled=True)
    key_prior, value_prior = shifted((key_heads, value_heads), "fsdp", 1)
    key_all = jnp.concatenate([key_prior, key_heads], 0)
    value_all = jnp.concatenate([value_prior, value_heads], 0)
    half_index = lax.axis_index("fsdp") % 2
    key_index = (half_index - 1) * half_len + jnp.arange(2 * half_len, dtype=jnp.int32)
    row_index = half_index * half_len + jnp.arange(half_len, dtype=jnp.int32)
    row_start = row_index - half_positions
    block = min(512, half_len)
    count = half_len // block
    factor = HD ** (-0.5)
    query_blocks = query_heads.reshape(count, block, pair_count, group, HD)
    index_blocks = row_index.reshape(count, block)
    start_blocks = row_start.reshape(count, block)

    def block_scores(query_block, index_block, start_block):
        scores = (
            jnp.einsum("bkgd,tkd->kgbt", query_block, key_all, preferred_element_type=jnp.float32)
            * factor
        )
        visible = (key_index[None, :] >= start_block[:, None]) & (
            key_index[None, :] <= index_block[:, None]
        )
        return jnp.where(visible, scores, -1e30)

    def forward_block(items):
        query_block, index_block, start_block = items
        scores = block_scores(query_block, index_block, start_block)
        top = jnp.max(scores, -1, keepdims=True)
        expo = jnp.exp(scores - top)
        total = jnp.sum(expo, -1, keepdims=True)
        probs_low = (expo / total).astype(jnp.bfloat16)
        mixed = jnp.einsum(
            "kgbt,tkd->bkgd", probs_low, value_all, preferred_element_type=jnp.float32
        )
        return (mixed.reshape(block, head_count, HD).astype(jnp.bfloat16), top + jnp.log(total))

    head_blocks, log_totals = lax.map(forward_block, (query_blocks, index_blocks, start_blocks))
    head_out = head_blocks.reshape(half_len, head_count, HD)
    token_heads = lax.all_to_all(head_out, "seq", split_axis=0, concat_axis=1, tiled=True)
    heads_flat = token_heads.reshape(token_count, QH * HD)
    middle = rows_float + jnp.dot(heads_flat, wo_full, preferred_element_type=jnp.float32)
    gain_two, wg_full, wu_full, wd_full = (
        lax.all_gather(second_gain, "fsdp", axis=0, tiled=True),
        lax.all_gather(gate_weight, "fsdp", axis=0, tiled=True),
        lax.all_gather(up_weight, "fsdp", axis=0, tiled=True),
        lax.all_gather(down_weight, "fsdp", axis=0, tiled=True),
    )
    gain_two = gain_two.astype(jnp.float32)
    normed_two, unit_two, scale_two = norm_forward(middle, gain_two)
    normed_two_low = normed_two.astype(jnp.bfloat16)
    gate = jnp.dot(normed_two_low, wg_full, preferred_element_type=jnp.float32)
    upper = jnp.dot(normed_two_low, wu_full, preferred_element_type=jnp.float32)
    hidden = (jax.nn.silu(gate) * upper).astype(jnp.bfloat16)
    result = middle + jnp.dot(hidden, wd_full, preferred_element_type=jnp.float32)
    block_output = result.astype(jnp.bfloat16)[None]
    grad_low = cotangent[0]
    grad_rows = grad_low.astype(jnp.float32)
    down_grad = jnp.einsum("tf,td->fd", hidden, grad_low, preferred_element_type=jnp.float32)
    grad_hidden = jnp.einsum("td,fd->tf", grad_low, wd_full, preferred_element_type=jnp.float32)
    sigma = jax.nn.sigmoid(gate)
    gate_low = (grad_hidden * upper * sigma * (1.0 + gate * (1.0 - sigma))).astype(jnp.bfloat16)
    upper_low = (grad_hidden * gate * sigma).astype(jnp.bfloat16)
    gate_grad = jnp.einsum(
        "td,tf->df", normed_two_low, gate_low, preferred_element_type=jnp.float32
    )
    up_grad = jnp.einsum("td,tf->df", normed_two_low, upper_low, preferred_element_type=jnp.float32)
    grad_normed_two = jnp.einsum(
        "tf,df->td", gate_low, wg_full, preferred_element_type=jnp.float32
    ) + jnp.einsum("tf,df->td", upper_low, wu_full, preferred_element_type=jnp.float32)
    grad_middle_norm, second_gain_grad = norm_backward(
        grad_normed_two, unit_two, scale_two, gain_two
    )
    grad_middle = grad_rows + grad_middle_norm
    grad_branch = grad_middle.astype(jnp.bfloat16)
    output_grad = jnp.einsum(
        "tc,td->cd", heads_flat, grad_branch, preferred_element_type=jnp.float32
    )
    grad_heads = (
        jnp.einsum("td,cd->tc", grad_branch, wo_full, preferred_element_type=jnp.float32)
        .astype(jnp.bfloat16)
        .reshape(token_count, QH, HD)
    )
    grad_head_rows = lax.all_to_all(grad_heads, "seq", split_axis=1, concat_axis=0, tiled=True)
    grad_blocks = grad_head_rows.reshape(count, block, pair_count, group, HD)

    def backward_block(carry, items):
        key_acc, value_acc = carry
        query_block, index_block, start_block, grad_block, log_block = items
        scores = block_scores(query_block, index_block, start_block)
        probs = jnp.exp(scores - log_block)
        probs_low = probs.astype(jnp.bfloat16)
        grad_probs = jnp.einsum(
            "bkgd,tkd->kgbt", grad_block, value_all, preferred_element_type=jnp.float32
        )
        grad_scores = (
            probs * (grad_probs - jnp.sum(probs * grad_probs, -1, keepdims=True))
        ).astype(jnp.bfloat16)
        query_grad_block = (
            jnp.einsum("kgbt,tkd->bkgd", grad_scores, key_all, preferred_element_type=jnp.float32)
            * factor
        )
        key_acc = (
            key_acc
            + jnp.einsum(
                "kgbt,bkgd->tkd", grad_scores, query_block, preferred_element_type=jnp.float32
            )
            * factor
        )
        value_acc = value_acc + jnp.einsum(
            "kgbt,bkgd->tkd", probs_low, grad_block, preferred_element_type=jnp.float32
        )
        return ((key_acc, value_acc), query_grad_block.reshape(block, head_count, HD))

    empty = jnp.zeros((2 * half_len, pair_count, HD), jnp.float32)
    (key_acc, value_acc), query_grad_blocks = lax.scan(
        backward_block,
        (empty, empty),
        (query_blocks, index_blocks, start_blocks, grad_blocks, log_totals),
    )
    key_back, value_back = (
        shifted(key_acc[:half_len].astype(jnp.bfloat16), "fsdp", -1).astype(jnp.float32),
        shifted(value_acc[:half_len].astype(jnp.bfloat16), "fsdp", -1).astype(jnp.float32),
    )
    key_local = key_acc[half_len:] + key_back
    value_local = value_acc[half_len:] + value_back
    query_grad_heads = query_grad_blocks.reshape(half_len, head_count, HD)
    grad_query_tok, grad_key_tok, grad_value_tok = (
        lax.all_to_all(
            query_grad_heads.astype(jnp.bfloat16), "seq", split_axis=0, concat_axis=1, tiled=True
        ).astype(query_grad_heads.dtype),
        lax.all_to_all(
            key_local.astype(jnp.bfloat16), "seq", split_axis=0, concat_axis=1, tiled=True
        ).astype(key_local.dtype),
        lax.all_to_all(
            value_local.astype(jnp.bfloat16), "seq", split_axis=0, concat_axis=1, tiled=True
        ).astype(value_local.dtype),
    )
    if repeat > 1:
        grad_key_tok = grad_key_tok.reshape(token_count, KVH, repeat, HD).sum(2)
        grad_value_tok = grad_value_tok.reshape(token_count, KVH, repeat, HD).sum(2)
    query_lin_grad = (
        rotate_back(grad_query_tok, cosine, sine).astype(jnp.bfloat16).reshape(token_count, QH * HD)
    )
    key_lin_grad = (
        rotate_back(grad_key_tok, cosine, sine).astype(jnp.bfloat16).reshape(token_count, KVH * HD)
    )
    value_lin_grad = grad_value_tok.astype(jnp.bfloat16).reshape(token_count, KVH * HD)
    query_grad = jnp.einsum(
        "td,tc->dc", normed_low, query_lin_grad, preferred_element_type=jnp.float32
    )
    key_grad = jnp.einsum("td,tc->dc", normed_low, key_lin_grad, preferred_element_type=jnp.float32)
    value_grad = jnp.einsum(
        "td,tc->dc", normed_low, value_lin_grad, preferred_element_type=jnp.float32
    )
    grad_normed_one = jnp.einsum(
        "tc,dc->td", query_lin_grad, wq_full, preferred_element_type=jnp.float32
    )
    grad_normed_one = grad_normed_one + jnp.einsum(
        "tc,dc->td", key_lin_grad, wk_full, preferred_element_type=jnp.float32
    )
    grad_normed_one = grad_normed_one + jnp.einsum(
        "tc,dc->td", value_lin_grad, wv_full, preferred_element_type=jnp.float32
    )
    grad_rows_one, first_gain_grad = norm_backward(grad_normed_one, unit_one, scale_one, gain_one)
    input_grad = (grad_middle + grad_rows_one).astype(jnp.bfloat16)[None]
    pieces = (
        lax.psum_scatter(
            first_gain_grad.astype(jnp.bfloat16), "fsdp", scatter_dimension=0, tiled=True
        ).astype(jnp.float32),
        lax.psum_scatter(
            query_grad.astype(jnp.bfloat16), "fsdp", scatter_dimension=0, tiled=True
        ).astype(jnp.float32),
        lax.psum_scatter(
            key_grad.astype(jnp.bfloat16), "fsdp", scatter_dimension=0, tiled=True
        ).astype(jnp.float32),
        lax.psum_scatter(
            value_grad.astype(jnp.bfloat16), "fsdp", scatter_dimension=0, tiled=True
        ).astype(jnp.float32),
        lax.psum_scatter(
            output_grad.astype(jnp.bfloat16), "fsdp", scatter_dimension=0, tiled=True
        ).astype(jnp.float32),
        lax.psum_scatter(
            second_gain_grad.astype(jnp.bfloat16), "fsdp", scatter_dimension=0, tiled=True
        ).astype(jnp.float32),
        lax.psum_scatter(
            gate_grad.astype(jnp.bfloat16), "fsdp", scatter_dimension=0, tiled=True
        ).astype(jnp.float32),
        lax.psum_scatter(
            up_grad.astype(jnp.bfloat16), "fsdp", scatter_dimension=0, tiled=True
        ).astype(jnp.float32),
        lax.psum_scatter(
            down_grad.astype(jnp.bfloat16), "fsdp", scatter_dimension=0, tiled=True
        ).astype(jnp.float32),
    )
    shares = (
        lax.psum(pieces[0].astype(jnp.bfloat16), "seq").astype(jnp.float32),
        lax.psum(pieces[1].astype(jnp.bfloat16), "seq").astype(jnp.float32),
        lax.psum(pieces[2].astype(jnp.bfloat16), "seq").astype(jnp.float32),
        lax.psum(pieces[3].astype(jnp.bfloat16), "seq").astype(jnp.float32),
        lax.psum(pieces[4].astype(jnp.bfloat16), "seq").astype(jnp.float32),
        lax.psum(pieces[5].astype(jnp.bfloat16), "seq").astype(jnp.float32),
        lax.psum(pieces[6].astype(jnp.bfloat16), "seq").astype(jnp.float32),
        lax.psum(pieces[7].astype(jnp.bfloat16), "seq").astype(jnp.float32),
        lax.psum(pieces[8].astype(jnp.bfloat16), "seq").astype(jnp.float32),
    )
    return (
        block_output,
        input_grad,
        shares[0],
        shares[1],
        shares[2],
        shares[3],
        shares[4],
        shares[5],
        shares[6],
        shares[7],
        shares[8],
    )


def plain_solution(mesh):
    placed = (
        P("fsdp", "seq", None),
        P("fsdp", "seq"),
        P("fsdp"),
        P("fsdp", None),
        P("fsdp", None),
        P("fsdp", None),
        P("fsdp", None),
        P("fsdp"),
        P("fsdp", None),
        P("fsdp", None),
        P("fsdp", None),
        P("fsdp", "seq", None),
    )
    return jax.shard_map(
        plain_body,
        mesh=mesh,
        in_specs=placed,
        out_specs=(
            P("fsdp", "seq", None),
            P("fsdp", "seq", None),
            P("fsdp"),
            P("fsdp", None),
            P("fsdp", None),
            P("fsdp", None),
            P("fsdp", None),
            P("fsdp"),
            P("fsdp", None),
            P("fsdp", None),
            P("fsdp", None),
        ),
        check_vma=False,
    )
```

```python
import functools
import math

import jax
import jax.numpy as jnp
from jax import lax
from jax.experimental import pallas as pl
from jax.experimental.pallas import tpu as pltpu
from jax.sharding import Mesh
from jax.sharding import PartitionSpec as P

QH = 16
KVH = 8
HD = 96


THETA = 100000.0
EPS = 1e-05
LOW = jnp.bfloat16
F32 = jnp.float32
NEG = -1e30
LN2 = math.log(2.0)


def contract(left, right, left_axis, right_axis):
    return lax.dot_general(
        left, right, (((left_axis,), (right_axis,)), ((), ())), preferred_element_type=F32
    )


def visible(first, second, query_block, key_block, size):
    key = key_block * size + lax.broadcasted_iota(jnp.int32, (size, size), 0)
    query = query_block * size + lax.broadcasted_iota(jnp.int32, (1, size), 1)
    start = jnp.where(query >= second, second, jnp.where(query >= first, first, 0))
    return (key >= start) & (key <= query)


def slot_of(block, count):
    return (block % (count // 2)) * 2 + block // (count // 2)


def forward_kernel(
    scalars,
    own_ref,
    other_ref,
    low_ref,
    full_ref,
    log_ref,
    query_s,
    key_s,
    value_s,
    top_s,
    total_s,
    mixed_s,
    *,
    size,
    count,
):
    half = scalars[0]
    first = scalars[1]
    second = scalars[2]
    here = pl.program_id(0)
    per_half = count // 2

    @pl.when(here == 0)
    def _():
        for ref, side in ((own_ref, half), (other_ref, 1 - half)):
            for step in range(per_half):
                block = side * per_half + step
                columns = slice(step * size, (step + 1) * size)
                query_s[block] = ref[0:HD, columns]
                key_s[block] = ref[HD : 2 * HD, columns].T
                value_s[block] = ref[2 * HD : 3 * HD, columns]

    query = query_s[here]
    top_s[...] = jnp.full_like(top_s, NEG)
    total_s[...] = jnp.zeros_like(total_s)
    mixed_s[...] = jnp.zeros_like(mixed_s)

    def add_block(block, masked):
        scores = contract(key_s[block], query, 1, 0)
        if masked:
            scores = jnp.where(visible(first, second, here, block, size), scores, NEG)
        old_top = top_s[...]
        top = jnp.maximum(old_top, jnp.max(scores, 0, keepdims=True))
        expo = jnp.exp2(scores - top)
        scale = jnp.exp2(old_top - top)
        top_s[...] = top
        total_s[...] = total_s[...] * scale + jnp.sum(expo, 0, keepdims=True)
        mixed_s[...] = mixed_s[...] * scale + contract(value_s[block], expo.astype(LOW), 1, 0)

    last = count - 1

    @pl.loop(1, jnp.where(here == last, 1, here))
    def _(block):
        add_block(block, False)

    @pl.loop(0, jnp.where(here == last, count, jnp.minimum(here + 1, 2)))
    def _(step):
        add_block(jnp.where(here == last, step, step * here), True)

    total = total_s[...]
    result = mixed_s[...] / total
    full_ref[0] = result
    low_ref[0] = result.astype(LOW)
    log_ref[0] = top_s[...] + jnp.log2(total)


def backward_kernel(
    scalars,
    own_ref,
    other_ref,
    grad_ref,
    full_ref,
    log_ref,
    kept_ref,
    leaving_ref,
    query_s,
    key_s,
    value_s,
    delta_s,
    query_grad_s,
    key_grad_s,
    value_grad_s,
    *,
    size,
    count,
):
    half = scalars[0]
    first = scalars[1]
    second = scalars[2]
    here = pl.program_id(0)
    per_half = count // 2

    @pl.when(here == 0)
    def _():
        for ref, side in ((own_ref, half), (other_ref, 1 - half)):
            for step in range(per_half):
                block = side * per_half + step
                columns = slice(step * size, (step + 1) * size)
                query_s[block] = ref[0:HD, columns]
                key_s[block] = ref[HD : 2 * HD, columns]
                value_s[block] = ref[2 * HD : 3 * HD, columns].T
        for block in range(count):
            delta_s[block] = jnp.sum(
                grad_ref[slot_of(block, count)].astype(F32) * full_ref[block], 0, keepdims=True
            )
        query_grad_s[...] = jnp.zeros_like(query_grad_s)

    key_grad_s[...] = jnp.zeros_like(key_grad_s)
    value_grad_s[...] = jnp.zeros_like(value_grad_s)
    key = key_s[here]
    key_rows = key.T
    value_rows = value_s[here]

    def add_block(block, masked):
        query = query_s[block]
        grad = grad_ref[slot_of(block, count)]
        scores = contract(key_rows, query, 1, 0)
        if masked:
            scores = jnp.where(visible(first, second, block, here, size), scores, NEG)
        probs = jnp.exp2(scores - log_ref[block])
        grad_probs = contract(value_rows, grad, 1, 0)
        grad_scores = (probs * (grad_probs - delta_s[block])).astype(LOW)
        value_grad_s[...] += contract(grad, probs.astype(LOW), 1, 1)
        key_grad_s[...] += contract(query, grad_scores, 1, 1)
        query_grad_s[block] += contract(key, grad_scores, 1, 0)

    last = count - 1

    @pl.loop(here + 1, jnp.where(here == 0, 1, last))
    def _(block):
        add_block(block, False)

    @pl.loop(0, jnp.where(here == 0, count, jnp.where(here == last, 1, 2)))
    def _(step):
        add_block(jnp.where(here == 0, step, jnp.where(step == 0, here, last)), True)

    side = here // per_half
    columns = pl.ds(pl.multiple_of((here % per_half) * size, size), size)

    def write(out_ref):
        out_ref[0:HD, columns] = (query_grad_s[here] * HD**-0.5).astype(LOW)
        out_ref[HD : 2 * HD, columns] = (key_grad_s[...] * LN2).astype(LOW)
        out_ref[2 * HD : 3 * HD, columns] = value_grad_s[...].astype(LOW)

    @pl.when(side == half)
    def _():
        write(kept_ref)

    @pl.when(side != half)
    def _():
        write(leaving_ref)


def attend_forward(scalars, own, other, size):
    count = 2 * own.shape[1] // size
    whole = lambda shape: pl.BlockSpec(shape, lambda i, s: (0,) * len(shape))
    pairs = count * (count + 1) // 2
    return pl.pallas_call(
        functools.partial(forward_kernel, size=size, count=count),
        grid_spec=pltpu.PrefetchScalarGridSpec(
            num_scalar_prefetch=1,
            grid=(count,),
            in_specs=[whole(own.shape), whole(other.shape)],
            out_specs=[
                pl.BlockSpec(
                    (1, HD, size), lambda i, s: (slot_of(i, count), 0, 0)
                ),
                pl.BlockSpec((1, HD, size), lambda i, s: (i, 0, 0)),
                pl.BlockSpec((1, 1, size), lambda i, s: (i, 0, 0)),
            ],
            scratch_shapes=[
                pltpu.VMEM((count, HD, size), LOW),
                pltpu.VMEM((count, size, HD), LOW),
                pltpu.VMEM((count, HD, size), LOW),
                pltpu.VMEM((1, size), F32),
                pltpu.VMEM((1, size), F32),
                pltpu.VMEM((HD, size), F32),
            ],
        ),
        out_shape=[
            jax.ShapeDtypeStruct((count, HD, size), LOW),
            jax.ShapeDtypeStruct((count, HD, size), F32),
            jax.ShapeDtypeStruct((count, 1, size), F32),
        ],
        compiler_params=pltpu.CompilerParams(
            dimension_semantics=("arbitrary",), vmem_limit_bytes=32 * 2**20
        ),
        cost_estimate=pl.CostEstimate(
            flops=pairs * size * size * HD * 32,
            bytes_accessed=10 * 2**20,
            transcendentals=pairs * size * size,
        ),
        name="attend_forward",
    )(scalars, own, other)


def attend_backward(scalars, own, other, grad, full, log_total):
    count, _, size = grad.shape
    whole = lambda shape: pl.BlockSpec(shape, lambda i, s: (0,) * len(shape))
    pairs = count * (count + 1) // 2
    out_shape = own.shape
    return pl.pallas_call(
        functools.partial(backward_kernel, size=size, count=count),
        grid_spec=pltpu.PrefetchScalarGridSpec(
            num_scalar_prefetch=1,
            grid=(count,),
            in_specs=[
                whole(own.shape),
                whole(other.shape),
                whole(grad.shape),
                whole(full.shape),
                whole(log_total.shape),
            ],
            out_specs=[whole(out_shape)] * 2,
            scratch_shapes=[
                pltpu.VMEM((count, HD, size), LOW),
                pltpu.VMEM((count, HD, size), LOW),
                pltpu.VMEM((count, size, HD), LOW),
                pltpu.VMEM((count, 1, size), F32),
                pltpu.VMEM((count, HD, size), F32),
                pltpu.VMEM((HD, size), F32),
                pltpu.VMEM((HD, size), F32),
            ],
        ),
        out_shape=[jax.ShapeDtypeStruct(out_shape, LOW)] * 2,
        compiler_params=pltpu.CompilerParams(
            dimension_semantics=("arbitrary",), vmem_limit_bytes=32 * 2**20
        ),
        cost_estimate=pl.CostEstimate(
            flops=pairs * size * size * HD * 42,
            bytes_accessed=16 * 2**20,
            transcendentals=pairs * size * size,
        ),
        name="attend_backward",
    )(scalars, own, other, grad, full, log_total)


def place_rows_kernel(order, *refs):
    pieces, out_ref = refs[:-1], refs[-1]
    size = pieces[0].shape[0]
    for index, piece in enumerate(pieces):
        start = pl.multiple_of(order[index] * size, size)
        out_ref[pl.ds(start, size), :] = piece[...].astype(F32)


def place_rows(order, pieces):
    size, width = pieces[0].shape
    total = size * len(pieces)
    step = 512
    return pl.pallas_call(
        place_rows_kernel,
        grid_spec=pltpu.PrefetchScalarGridSpec(
            num_scalar_prefetch=1,
            grid=(width // step,),
            in_specs=[pl.BlockSpec((size, step), lambda i, s: (0, i)) for _ in pieces],
            out_specs=pl.BlockSpec((total, step), lambda i, s: (0, i)),
        ),
        out_shape=jax.ShapeDtypeStruct((total, width), F32),
        compiler_params=pltpu.CompilerParams(vmem_limit_bytes=24 * 2**20),
        cost_estimate=pl.CostEstimate(
            flops=0, bytes_accessed=total * width * 6, transcendentals=0
        ),
        name="place_rows",
    )(order, *pieces)


def place_columns_kernel(order, gain_ref, gate_w_ref, up_w_ref, *refs):
    count = (len(refs) - 3) // 2
    gates, ups = refs[:count], refs[count : 2 * count]
    gate_ref, up_ref, sum_ref = refs[2 * count :]
    size = gates[0].shape[1]
    gain = gain_ref[...]
    total = jnp.zeros((gate_ref.shape[0], size), F32)
    for index in range(count):
        columns = pl.ds(pl.multiple_of(order[index] * size, size), size)
        gate, up = gates[index][...].astype(F32), ups[index][...].astype(F32)
        total += gate * gate_w_ref[:, columns].astype(F32)
        total += up * up_w_ref[:, columns].astype(F32)
        gate_ref[:, columns] = gate * gain
        up_ref[:, columns] = up * gain

    @pl.when(pl.program_id(0) == 0)
    def _():
        sum_ref[...] = jnp.zeros_like(sum_ref)

    sum_ref[...] += jnp.sum(total, 1, keepdims=True)


def place_columns(order, gain, gate_weight, up_weight, gates, ups, shards):
    rows, width = gate_weight.shape
    span = width // shards
    size = span // len(gates)
    wide = pl.BlockSpec((rows, span), lambda i, s: (0, i))
    thin = pl.BlockSpec((rows, 1), lambda i, s: (0, 0))
    pieces = [pl.BlockSpec((rows, size), lambda i, s: (0, i)) for _ in (*gates, *ups)]
    return pl.pallas_call(
        place_columns_kernel,
        grid_spec=pltpu.PrefetchScalarGridSpec(
            num_scalar_prefetch=1,
            grid=(shards,),
            in_specs=[thin, wide, wide, *pieces],
            out_specs=[wide, wide, thin],
        ),
        out_shape=[
            jax.ShapeDtypeStruct((rows, width), F32),
            jax.ShapeDtypeStruct((rows, width), F32),
            jax.ShapeDtypeStruct((rows, 1), F32),
        ],
        compiler_params=pltpu.CompilerParams(
            dimension_semantics=("arbitrary",), vmem_limit_bytes=24 * 2**20
        ),
        cost_estimate=pl.CostEstimate(
            flops=rows * width * 6, bytes_accessed=rows * width * 16, transcendentals=0
        ),
        name="place_columns",
    )(order, gain, gate_weight, up_weight, *gates, *ups)


def place_heads_kernel(gain_ref, query_w, key_w, value_w, all_ref, query_ref, key_ref, value_ref, sum_ref):
    rows = gain_ref.shape[0]
    wide = query_ref.shape[1] // KVH
    gain = gain_ref[...]
    total = jnp.zeros((rows, 4 * HD), F32)
    pieces = [all_ref[i * rows : (i + 1) * rows, :].astype(F32) for i in range(KVH)]
    for start in range(0, KVH, 2):
        value = jnp.concatenate([piece[:, :wide] for piece in pieces[start : start + 2]], 1)
        columns = slice(start * wide, (start + 2) * wide)
        total += value * query_w[:, columns].astype(F32)
        query_ref[:, columns] = value * gain
    for first, weight, out_ref in ((wide, key_w, key_ref), (wide + HD, value_w, value_ref)):
        for start in range(0, KVH, 4):
            value = jnp.concatenate(
                [piece[:, first : first + HD] for piece in pieces[start : start + 4]], 1
            )
            columns = slice(start * HD, (start + 4) * HD)
            total += value * weight[:, columns].astype(F32)
            out_ref[:, columns] = value * gain
    sum_ref[...] = jnp.sum(total, 1, keepdims=True)


def place_heads(gain, query_weight, key_weight, value_weight, pieces):
    weights = (query_weight, key_weight, value_weight)
    rows = gain.shape[0]
    return pl.pallas_call(
        place_heads_kernel,
        out_shape=[jax.ShapeDtypeStruct(weight.shape, F32) for weight in weights]
        + [jax.ShapeDtypeStruct((rows, 1), F32)],
        compiler_params=pltpu.CompilerParams(vmem_limit_bytes=32 * 2**20),
        cost_estimate=pl.CostEstimate(
            flops=rows * 3072 * 4, bytes_accessed=rows * 3072 * 8, transcendentals=0
        ),
        name="place_heads",
    )(gain, *weights, pieces)


def merge_kernel(scalars, kept_ref, came_ref, cosine_ref, sine_ref, out_ref, split_ref):
    lead = scalars[0] == 0
    lines, _, size = split_ref.shape
    for line in range(lines):
        columns = slice(line * size, (line + 1) * size)
        kept = kept_ref[:, columns].astype(F32)
        came = came_ref[:, columns].astype(F32)
        cosine, sine = cosine_ref[:, columns], sine_ref[:, columns]
        joint = kept[HD:] + came[HD:]
        first = jnp.where(lead, kept[:HD], came[:HD])
        second = jnp.where(lead, came[:HD], kept[:HD])
        turned = []
        for value in (first, second, joint[:HD]):
            low, high = value[: HD // 2], value[HD // 2 :]
            turned.append(low * cosine + high * sine)
            turned.append(high * cosine - low * sine)
        turned.append(joint[HD:])
        result = jnp.concatenate([part.astype(LOW) for part in turned], 0)
        out_ref[:, columns] = result
        split_ref[line] = result


def merge(scalars, kept, came, cosine, sine, lines):
    tokens = kept.shape[1]
    whole = lambda value: pl.BlockSpec(value.shape, lambda i, s: (0,) * len(value.shape))
    outs = [
        jax.ShapeDtypeStruct((4 * HD, tokens), LOW),
        jax.ShapeDtypeStruct((lines, 4 * HD, tokens // lines), LOW),
    ]
    return pl.pallas_call(
        merge_kernel,
        grid_spec=pltpu.PrefetchScalarGridSpec(
            num_scalar_prefetch=1,
            grid=(1,),
            in_specs=[whole(value) for value in (kept, came, cosine, sine)],
            out_specs=[whole(value) for value in outs],
        ),
        out_shape=outs,
        compiler_params=pltpu.CompilerParams(vmem_limit_bytes=24 * 2**20),
        cost_estimate=pl.CostEstimate(
            flops=tokens * HD * 24, bytes_accessed=tokens * HD * 30, transcendentals=0
        ),
        name="merge",
    )(scalars, kept, came, cosine, sine)


def pack_kernel(scalars, gain_ref, query_ref, key_ref, value_ref, *outs):
    core = scalars[3]
    gain = gain_ref[...]
    wide = query_ref.shape[1] // KVH
    span = wide + 2 * HD
    for which in range(2):

        @pl.when(core == which)
        def _():
            for line in range(KVH // 2):
                head = 2 * line + which
                value = jnp.concatenate(
                    [
                        query_ref[:, head * wide : (head + 1) * wide].astype(F32),
                        key_ref[:, head * HD : (head + 1) * HD].astype(F32),
                        value_ref[:, head * HD : (head + 1) * HD].astype(F32),
                    ],
                    1,
                )
                place = (line % 2) * span
                outs[line // 2][:, place : place + span] = (value * gain).astype(LOW)


def pack(scalars, gain, query_weight, key_weight, value_weight):
    rows, width = query_weight.shape
    whole = lambda value: pl.BlockSpec(value.shape, lambda i, s: (0, 0))
    weights = (gain, query_weight, key_weight, value_weight)
    outs = [jax.ShapeDtypeStruct((rows, width // 2), LOW)] * 2
    return pl.pallas_call(
        pack_kernel,
        grid_spec=pltpu.PrefetchScalarGridSpec(
            num_scalar_prefetch=1,
            grid=(1,),
            in_specs=[whole(value) for value in weights],
            out_specs=[whole(value) for value in outs],
        ),
        out_shape=outs,
        compiler_params=pltpu.CompilerParams(vmem_limit_bytes=24 * 2**20),
        cost_estimate=pl.CostEstimate(
            flops=rows * width, bytes_accessed=rows * width * 6, transcendentals=0
        ),
        name="pack",
    )(scalars, *weights)


def spread_kernel(scalars, lin_ref, cosine_ref, sine_ref, own_ref, leaving_ref):
    cosine, sine = cosine_ref[...], sine_ref[...]

    def turn(start, factor):
        low = lin_ref[start : start + HD // 2, :]
        high = lin_ref[start + HD // 2 : start + HD, :]
        turned = ((low * cosine - high * sine) * factor, (high * cosine + low * sine) * factor)
        return jnp.concatenate([part.astype(LOW) for part in turned], 0)

    lead = scalars[0] == 0
    first, second = turn(0, HD**-0.5 / LN2), turn(HD, HD**-0.5 / LN2)

    @pl.when(lead)
    def _():
        own_ref[0:HD] = first
        leaving_ref[0:HD] = second

    @pl.when(jnp.logical_not(lead))
    def _():
        own_ref[0:HD] = second
        leaving_ref[0:HD] = first

    key = turn(2 * HD, 1.0)
    value = lin_ref[3 * HD : 4 * HD].astype(LOW)
    for ref in (own_ref, leaving_ref):
        ref[HD : 2 * HD] = key
        ref[2 * HD : 3 * HD] = value


def spread(scalars, lin, cosine, sine):
    tokens = lin.shape[1]
    step = 512
    column = lambda rows: pl.BlockSpec((rows, step), lambda i, s: (0, i))
    return pl.pallas_call(
        spread_kernel,
        grid_spec=pltpu.PrefetchScalarGridSpec(
            num_scalar_prefetch=1,
            grid=(tokens // step,),
            in_specs=[column(4 * HD), column(HD // 2), column(HD // 2)],
            out_specs=[column(3 * HD)] * 2,
        ),
        out_shape=[jax.ShapeDtypeStruct((3 * HD, tokens), LOW)] * 2,
        compiler_params=pltpu.CompilerParams(vmem_limit_bytes=24 * 2**20),
        cost_estimate=pl.CostEstimate(
            flops=tokens * HD * 24, bytes_accessed=tokens * HD * 36, transcendentals=0
        ),
        name="spread",
    )(scalars, lin, cosine, sine)


def swap(value, axis):
    return lax.ppermute(value, axis, [(0, 1), (1, 0)])


def swap_near(value):
    return lax.ppermute(value, "z", [(0, 1), (1, 0), (2, 3), (3, 2)])


def swap_far(value):
    return lax.ppermute(value, "z", [(0, 2), (2, 0), (1, 3), (3, 1)])


def tie(*values):
    return lax.optimization_barrier(values)


def in_order(place, own, other):
    return (jnp.where(place == 0, own, other), jnp.where(place == 0, other, own))


def both(place, own, other):
    return jnp.concatenate(in_order(place, own, other), 0)


def spread_out(value, first, second):
    other = swap(value, first)
    pair = jnp.stack(in_order(lax.axis_index(first), value, other))
    return pair, swap(pair, second)


def placed(pair, other, second):
    pairs = in_order(lax.axis_index(second), pair, other)
    grid = jnp.stack(pairs, 0 if second == "y" else 1)
    return grid.reshape(-1, *grid.shape[3:])


def pick(array, axis, at):
    return lax.dynamic_index_in_dim(array, at, axis, keepdims=False)


def halve(value, axis, along=0):
    at = lax.axis_index(axis)
    return pick(value, along, at), swap(pick(value, along, 1 - at), axis)


def halve_x(value):
    return halve(value.reshape(2, 2, -1, value.shape[-1]), "x", 1)


def halve_y(value):
    return halve(value.reshape(2, 2, -1, value.shape[-1]), "y", 0)


def fast_body(
    tokens,
    positions,
    first_gain,
    query_weight,
    key_weight,
    value_weight,
    output_weight,
    second_gain,
    gate_weight,
    up_weight,
    down_weight,
    cotangent,
):
    seq = ("z", "c")
    fsdp = ("y", "x")
    z, core, half = lax.axis_index("z"), lax.axis_index("c"), lax.axis_index("x")
    near = z % 2
    lines = lax.axis_size("z")
    seq_count = 2 * lines
    shards = lax.axis_size("y") * 2
    spot = z * 2 + core
    quarter = near * 2 + core
    rows = tokens[0]
    count, width = rows.shape
    chip_count = 2 * count
    half_len = count * seq_count
    seq_len = 2 * half_len

    begins = jnp.where(
        (spot == 0) & (half == 0),
        count - 1 - positions[0, count - 1],
        half * half_len + spot * count - positions[0, 0],
    )
    ends = begins + (seq_len - count)
    scalars = jnp.stack([half, begins, ends, core]).astype(jnp.int32)

    gain_one = first_gain.astype(F32)[:, None]
    gain_two = second_gain.astype(F32)[:, None]

    def row_scale(value):
        return lax.rsqrt(jnp.mean(value * value, -1, keepdims=True) + EPS)

    take = functools.partial(lax.dynamic_slice_in_dim, axis=1)
    take_rows = functools.partial(lax.dynamic_slice_in_dim, axis=0)
    gather = lambda value, axes: lax.all_gather(value, axes, axis=0, tiled=True)
    own_rows = rows.astype(F32)
    own_unit_scale = row_scale(own_rows)
    own_unit = own_rows * own_unit_scale
    units = gather(own_unit.astype(LOW), seq)
    lead_shard, tail_shard = pack(scalars, gain_one, query_weight, key_weight, value_weight)
    out_rows = output_weight.shape[0] // 2
    out_shard = take_rows(output_weight, core * out_rows, out_rows)
    piece = down_weight.shape[0] // 4
    down_shard = take_rows(down_weight, quarter * piece, piece)
    gate_shard, up_shard = (
        (
            jnp.concatenate(
                [
                    take(weight, shard * 4 * piece + quarter * piece, piece)
                    for shard in range(shards)
                ],
                1,
            ).astype(F32)
            * gain_two
        ).astype(LOW)
        for weight in (gate_weight, up_weight)
    )
    side = lax.axis_index("y")
    lead_pair = jnp.stack(in_order(half, lead_shard, swap(lead_shard, "x")))
    tail_pair = jnp.stack(in_order(side, tail_shard, swap(tail_shard, "y")))
    gate_pair = jnp.stack(in_order(half, gate_shard, swap(gate_shard, "x")))
    lead_far, tail_far, gate_pair, up_shard = tie(
        swap(lead_pair, "y"), swap(tail_pair, "x"), gate_pair, up_shard
    )
    lead_w, tail_w = placed(lead_pair, lead_far, "y"), placed(tail_pair, tail_far, "x")
    span = lead_w.shape[1] // 2
    qkv_w = take(jnp.where(z < 2, lead_w, tail_w), near * span, span)
    gate_far = swap(gate_pair, "y")
    up_pair = jnp.stack(in_order(half, up_shard, swap(up_shard, "x")))

    place = half * half_len + jnp.arange(half_len, dtype=jnp.int32)
    start = jnp.where(place >= ends, ends, jnp.where(place >= begins, begins, 0))
    freq = THETA ** (-(jnp.arange(HD // 2, dtype=F32) * 2.0 / HD))
    angle = freq[:, None] * (place - start).astype(F32)[None, :]
    cosine, sine = jnp.cos(angle), jnp.sin(angle)
    chip_rows = both(core, rows, swap(rows, "c"))
    units, own_cot, chip_rows = tie(units, cotangent[0], chip_rows)
    own, leaving = spread(scalars, contract(qkv_w, units, 0, 1), cosine, sine)
    leaving, up_pair = tie(leaving, up_pair)

    up_far = swap(up_pair, "y")
    near_cot = swap_near(own_cot)
    other, out_shard, down_shard, near_cot, chip_cot, gate_far = tie(
        swap(leaving, "x"),
        out_shard,
        down_shard,
        near_cot,
        both(core, own_cot, swap(own_cot, "c")),
        gate_far,
    )
    out_w = gather(out_shard, fsdp)
    down_pair = jnp.stack(in_order(half, down_shard, swap(down_shard, "x")))
    near_cot = jnp.concatenate([near_cot, swap(near_cot, "c")], 0)
    gate_w = placed(gate_pair, gate_far, "y")
    head_low, head_full, log_total = attend_forward(scalars, own, other, chip_count)
    exchange = lambda value: lax.all_to_all(
        value, ("z", "x"), split_axis=0, concat_axis=0, tiled=True
    )
    head_low, up_far, near_cot, down_pair, gate_w = tie(
        head_low, up_far, near_cot, down_pair, gate_w
    )
    down_far = swap(down_pair, "y")
    heads, up_w = tie(exchange(head_low), placed(up_pair, up_far, "y"))
    down_w = placed(down_pair, down_far, "y")
    heads = heads.reshape(QH // 2 * HD, chip_count)

    mine_of = lambda value: take_rows(value, core * count, count)
    theirs_of = lambda value: take_rows(value, (1 - core) * count, count)
    branch = contract(heads, out_w, 0, 0).astype(LOW)
    middle = chip_rows.astype(F32) + (branch.astype(F32) + swap(branch, "c").astype(F32))
    middle_scale = row_scale(middle)
    chip_unit = middle * middle_scale
    own_middle, own_scale, own_middle_unit = (
        mine_of(middle),
        mine_of(middle_scale),
        mine_of(chip_unit),
    )
    chip_unit = chip_unit.astype(LOW)
    near_unit = swap_near(mine_of(chip_unit))
    near_unit = jnp.concatenate([near_unit, swap(near_unit, "c")], 0)

    def feed(unit):
        gate, upper = contract(unit, gate_w, 1, 0), contract(unit, up_w, 1, 0)
        sigma = jax.nn.sigmoid(gate)
        silu = gate * sigma
        return (silu * upper).astype(LOW), (gate, upper, sigma, silu)

    def feed_back(cot, kept):
        gate, upper, sigma, silu = kept
        grad_hidden = contract(cot, down_w, 1, 1)
        gate_low = (grad_hidden * upper * sigma * (1.0 + gate * (1.0 - sigma))).astype(LOW)
        upper_low = (grad_hidden * silu).astype(LOW)
        part = contract(gate_low, gate_w, 1, 1) + contract(upper_low, up_w, 1, 1)
        return gate_low, upper_low, part

    def chip_sum(chip_part, near_part):
        near_sum = near_part[:count].astype(F32) + swap(near_part[count:].astype(LOW), "c")
        own_sum = mine_of(chip_part).astype(F32) + swap(theirs_of(chip_part).astype(LOW), "c")
        return own_sum, near_sum.astype(LOW)

    stack = lambda first, second: jnp.concatenate([first, second], 0)
    scatter = lambda value: lax.psum_scatter(value, fsdp, scatter_dimension=0, tiled=True)
    chip_hidden, chip_kept = feed(chip_unit)
    near_hidden, near_kept = feed(near_unit)
    down_part = contract(
        stack(chip_hidden, near_hidden), stack(chip_cot, near_cot), 0, 0
    ).astype(LOW)
    near_cot, down_part = tie(near_cot, down_part)
    near_gate, near_upper, near_part = feed_back(near_cot, near_kept)
    chip_gate, chip_upper, chip_part = feed_back(chip_cot, chip_kept)
    grad_two, near_sum = chip_sum(chip_part, near_part)
    grad_two = grad_two + swap_near(near_sum).astype(F32)

    def halves_first(value):
        cut = value.shape[-1] // 2
        return halve_x(value[:, :cut]), halve_y(value[:, cut:])

    def halves_second(firsts):
        return halve(sum(firsts[0]), "y"), halve(sum(firsts[1]), "x")

    def halves_end(seconds):
        return jnp.concatenate([sum(seconds[0]), sum(seconds[1])], 1)

    down_first = halves_first(down_part)
    all_units = stack(chip_unit, near_unit)
    gate_part = contract(all_units, stack(chip_gate, near_gate), 0, 0).astype(LOW)
    gate_part, down_first = tie(gate_part, down_first)
    down_second, gate_first = halves_second(down_first), halves_first(gate_part)
    up_part = contract(all_units, stack(chip_upper, near_upper), 0, 0).astype(LOW)
    grad_two, up_part, down_second, gate_first = tie(
        grad_two, up_part, down_second, gate_first
    )
    down_grad = halves_end(down_second)
    down_far = swap_far(down_grad)
    gate_second, up_first = halves_second(gate_first), halves_first(up_part)
    grad_middle = own_cot.astype(F32) + own_scale * (
        grad_two - own_middle_unit * jnp.mean(grad_two * own_middle_unit, -1, keepdims=True)
    )
    own_branch = grad_middle.astype(LOW)
    grad_branch = both(core, own_branch, swap(own_branch, "c"))
    grad_heads = contract(out_w, grad_branch, 1, 1).astype(LOW)
    grad_heads, grad_branch = tie(grad_heads, grad_branch)
    output_part = contract(heads, grad_branch, 1, 0).astype(LOW)
    feed_own, feed_near = chip_sum(
        contract(chip_hidden, down_w, 1, 0), contract(near_hidden, down_w, 1, 0)
    )
    grad_head, output_part, gate_second, up_first, feed_own, feed_near = tie(
        exchange(grad_heads.reshape(2 * lines, HD, chip_count)),
        output_part,
        gate_second,
        up_first,
        feed_own,
        feed_near,
    )

    output_grad = scatter(output_part)
    gate_grad = halves_end(gate_second)
    gate_far = swap_far(gate_grad)
    up_second = halves_second(up_first)
    feed_near = swap_near(feed_near)
    kept, leaving = attend_backward(scalars, own, other, grad_head, head_full, log_total)
    kept, leaving, down_far, gate_far, up_second, feed_near = tie(
        kept, leaving, down_far, gate_far, up_second, feed_near
    )

    up_grad = halves_end(up_second)
    up_far = swap_far(up_grad)
    down_sum = down_grad + down_far
    down_near = swap_near(down_sum)
    gate_sum = gate_grad + gate_far
    gate_near = swap_near(gate_sum)
    block_output = (own_middle + feed_own + feed_near.astype(F32)).astype(LOW)[None]
    came, block_output = tie(swap(leaving, "x"), block_output)

    place = lax.axis_index("z")
    inner = (place == 1) | (place == 2)
    qkv_low, by_line = merge(scalars, kept, came, cosine, sine, lines)
    token_grads = lax.all_to_all(by_line, "z", split_axis=0, concat_axis=0, tiled=True)
    qkv_part = contract(units, qkv_low, 0, 1).astype(LOW).reshape(shards, 2, -1, 4 * HD)
    qkv_first = halve_x(qkv_part[:, 0]), halve_y(qkv_part[:, 1])
    token_grads, qkv_first, output_grad, up_far, down_near, gate_near = tie(
        token_grads, qkv_first, output_grad, up_far, down_near, gate_near
    )
    output_came = lax.ppermute(output_grad, "z", [(0, 1), (3, 2)])

    up_sum = up_grad + up_far
    up_near = swap_near(up_sum)
    output_sum = output_grad + output_came
    output_sum = output_sum + lax.ppermute(output_sum, "z", [(1, 2), (2, 1)])
    qkv_second = halves_second(qkv_first)
    qkv_grad = jnp.concatenate([sum(qkv_second[0]), sum(qkv_second[1])], 0)
    token_grads = token_grads.reshape(-1, chip_count)
    split = lead_w.shape[1]
    grad_one = contract(token_grads[:split], lead_w, 0, 1) + contract(
        token_grads[split:], tail_w, 0, 1
    )
    grad_one = mine_of(grad_one) + swap(theirs_of(grad_one).astype(LOW), "c").astype(F32)
    grad_rows = own_unit_scale * (
        grad_one - own_unit * jnp.mean(grad_one * own_unit, -1, keepdims=True)
    )
    input_grad = (grad_middle + grad_rows).astype(LOW)[None]
    output_far = lax.ppermute(output_sum, "z", [(1, 0), (2, 3)])
    output_own = jnp.where(inner, output_sum, output_far)

    def four(value, near_value):
        return value, swap(value, "c"), near_value, swap(near_value, "c")

    order = jnp.stack([quarter, quarter ^ 1, quarter ^ 2, quarter ^ 3]).astype(jnp.int32)
    core_order = jnp.stack([core, 1 - core]).astype(jnp.int32)
    down_total = place_rows(order, four(down_sum, down_near))
    output_total = place_rows(core_order, (output_own, swap(output_own, "c")))
    gate_total, up_total, second_gain_grad = place_columns(
        order, gain_two, gate_weight, up_weight, four(gate_sum, gate_near), four(up_sum, up_near), shards
    )
    query_grad, key_grad, value_grad, first_gain_grad = place_heads(
        gain_one, query_weight, key_weight, value_weight, gather(qkv_grad, seq)
    )
    return (
        block_output,
        input_grad,
        first_gain_grad[:, 0],
        query_grad,
        key_grad,
        value_grad,
        output_total,
        second_gain_grad[:, 0],
        gate_total,
        up_total,
        down_total,
    )


def fast_solution(mesh):
    seq_count, shard_count = mesh.devices.shape
    fine = Mesh(
        mesh.devices.reshape(seq_count // 2, 2, shard_count // 2, 2), ("z", "c", "y", "x")
    )
    seq, fsdp = ("z", "c"), ("y", "x")
    matrix = P(fsdp, None)
    return jax.shard_map(
        fast_body,
        mesh=fine,
        in_specs=(
            P(fsdp, seq, None),
            P(fsdp, seq),
            P(fsdp),
            matrix,
            matrix,
            matrix,
            matrix,
            P(fsdp),
            matrix,
            matrix,
            matrix,
            P(fsdp, seq, None),
        ),
        out_specs=(
            P(fsdp, seq, None),
            P(fsdp, seq, None),
            P(fsdp),
            matrix,
            matrix,
            matrix,
            matrix,
            P(fsdp),
            matrix,
            matrix,
            matrix,
        ),
        check_vma=False,
    )


def solution(mesh):
    shape = dict(mesh.shape)
    if shape["seq"] == KVH and shape["fsdp"] == 4:
        return fast_solution(mesh)
    return plain_solution(mesh)


def shifted(value, axis, steps):
    count = lax.axis_size(axis)
    first, last = (max(0, -steps), min(count, count - steps))
    return lax.ppermute(value, axis, [(source, source + steps) for source in range(first, last)])


def rope_tables(position_rows):
    freq = THETA ** (-(jnp.arange(HD // 2, dtype=jnp.float32) * 2.0 / HD))
    angle = position_rows.astype(jnp.float32)[:, None] * freq[None, :]
    cosine = jnp.cos(angle)
    sine = jnp.sin(angle)
    return (jnp.concatenate([cosine, cosine], -1), jnp.concatenate([sine, sine], -1))


def rotate(values, cosine, sine):
    half = HD // 2
    turned = jnp.concatenate([-values[..., half:], values[..., :half]], -1)
    return values * cosine[:, None, :] + turned * sine[:, None, :]


def rotate_back(grads, cosine, sine):
    half = HD // 2
    scaled = grads * sine[:, None, :]
    turned = jnp.concatenate([scaled[..., half:], -scaled[..., :half]], -1)
    return grads * cosine[:, None, :] + turned


def norm_forward(rows, gain):
    scale = lax.rsqrt(jnp.mean(rows * rows, -1, keepdims=True) + EPS)
    unit = rows * scale
    return (unit * gain, unit, scale)


def norm_backward(grad_out, unit, scale, gain):
    grad_unit = grad_out * gain
    gain_grad = jnp.sum(grad_out * unit, 0)
    grad_rows = scale * (grad_unit - unit * jnp.mean(grad_unit * unit, -1, keepdims=True))
    return (grad_rows, gain_grad)


def plain_body(
    tokens,
    positions,
    first_gain,
    query_weight,
    key_weight,
    value_weight,
    output_weight,
    second_gain,
    gate_weight,
    up_weight,
    down_weight,
    cotangent,
):
    seq_count = lax.axis_size("seq")
    local_rows = tokens[0]
    token_count = local_rows.shape[0]
    half_len = token_count * seq_count
    rows_float = local_rows.astype(jnp.float32)
    gain_one, wq_full, wk_full, wv_full, wo_full = (
        lax.all_gather(first_gain, "fsdp", axis=0, tiled=True),
        lax.all_gather(query_weight, "fsdp", axis=0, tiled=True),
        lax.all_gather(key_weight, "fsdp", axis=0, tiled=True),
        lax.all_gather(value_weight, "fsdp", axis=0, tiled=True),
        lax.all_gather(output_weight, "fsdp", axis=0, tiled=True),
    )
    gain_one = gain_one.astype(jnp.float32)
    normed_one, unit_one, scale_one = norm_forward(rows_float, gain_one)
    normed_low = normed_one.astype(jnp.bfloat16)
    cosine, sine = rope_tables(positions[0])
    query_lin = jnp.dot(normed_low, wq_full, preferred_element_type=jnp.float32).reshape(
        token_count, QH, HD
    )
    key_lin = jnp.dot(normed_low, wk_full, preferred_element_type=jnp.float32).reshape(
        token_count, KVH, HD
    )
    value_lin = jnp.dot(normed_low, wv_full, preferred_element_type=jnp.float32).reshape(
        token_count, KVH, HD
    )
    query_rows = rotate(query_lin, cosine, sine).astype(jnp.bfloat16)
    key_rows = rotate(key_lin, cosine, sine).astype(jnp.bfloat16)
    value_rows = value_lin.astype(jnp.bfloat16)
    repeat = max(1, seq_count // KVH)
    if repeat > 1:
        key_rows = jnp.repeat(key_rows, repeat, axis=1)
        value_rows = jnp.repeat(value_rows, repeat, axis=1)
    query_heads, key_heads, value_heads = (
        lax.all_to_all(query_rows, "seq", split_axis=1, concat_axis=0, tiled=True),
        lax.all_to_all(key_rows, "seq", split_axis=1, concat_axis=0, tiled=True),
        lax.all_to_all(value_rows, "seq", split_axis=1, concat_axis=0, tiled=True),
    )
    head_count = query_heads.shape[1]
    pair_count = key_heads.shape[1]
    group = head_count // pair_count
    half_positions = lax.all_gather(positions[0], "seq", axis=0, tiled=True)
    key_prior, value_prior = shifted((key_heads, value_heads), "fsdp", 1)
    key_all = jnp.concatenate([key_prior, key_heads], 0)
    value_all = jnp.concatenate([value_prior, value_heads], 0)
    half_index = lax.axis_index("fsdp") % 2
    key_index = (half_index - 1) * half_len + jnp.arange(2 * half_len, dtype=jnp.int32)
    row_index = half_index * half_len + jnp.arange(half_len, dtype=jnp.int32)
    row_start = row_index - half_positions
    block = min(512, half_len)
    count = half_len // block
    factor = HD ** (-0.5)
    query_blocks = query_heads.reshape(count, block, pair_count, group, HD)
    index_blocks = row_index.reshape(count, block)
    start_blocks = row_start.reshape(count, block)

    def block_scores(query_block, index_block, start_block):
        scores = (
            jnp.einsum("bkgd,tkd->kgbt", query_block, key_all, preferred_element_type=jnp.float32)
            * factor
        )
        visible = (key_index[None, :] >= start_block[:, None]) & (
            key_index[None, :] <= index_block[:, None]
        )
        return jnp.where(visible, scores, -1e30)

    def forward_block(items):
        query_block, index_block, start_block = items
        scores = block_scores(query_block, index_block, start_block)
        top = jnp.max(scores, -1, keepdims=True)
        expo = jnp.exp(scores - top)
        total = jnp.sum(expo, -1, keepdims=True)
        probs_low = (expo / total).astype(jnp.bfloat16)
        mixed = jnp.einsum(
            "kgbt,tkd->bkgd", probs_low, value_all, preferred_element_type=jnp.float32
        )
        return (mixed.reshape(block, head_count, HD).astype(jnp.bfloat16), top + jnp.log(total))

    head_blocks, log_totals = lax.map(forward_block, (query_blocks, index_blocks, start_blocks))
    head_out = head_blocks.reshape(half_len, head_count, HD)
    token_heads = lax.all_to_all(head_out, "seq", split_axis=0, concat_axis=1, tiled=True)
    heads_flat = token_heads.reshape(token_count, QH * HD)
    middle = rows_float + jnp.dot(heads_flat, wo_full, preferred_element_type=jnp.float32)
    gain_two, wg_full, wu_full, wd_full = (
        lax.all_gather(second_gain, "fsdp", axis=0, tiled=True),
        lax.all_gather(gate_weight, "fsdp", axis=0, tiled=True),
        lax.all_gather(up_weight, "fsdp", axis=0, tiled=True),
        lax.all_gather(down_weight, "fsdp", axis=0, tiled=True),
    )
    gain_two = gain_two.astype(jnp.float32)
    normed_two, unit_two, scale_two = norm_forward(middle, gain_two)
    normed_two_low = normed_two.astype(jnp.bfloat16)
    gate = jnp.dot(normed_two_low, wg_full, preferred_element_type=jnp.float32)
    upper = jnp.dot(normed_two_low, wu_full, preferred_element_type=jnp.float32)
    hidden = (jax.nn.silu(gate) * upper).astype(jnp.bfloat16)
    result = middle + jnp.dot(hidden, wd_full, preferred_element_type=jnp.float32)
    block_output = result.astype(jnp.bfloat16)[None]
    grad_low = cotangent[0]
    grad_rows = grad_low.astype(jnp.float32)
    down_grad = jnp.einsum("tf,td->fd", hidden, grad_low, preferred_element_type=jnp.float32)
    grad_hidden = jnp.einsum("td,fd->tf", grad_low, wd_full, preferred_element_type=jnp.float32)
    sigma = jax.nn.sigmoid(gate)
    gate_low = (grad_hidden * upper * sigma * (1.0 + gate * (1.0 - sigma))).astype(jnp.bfloat16)
    upper_low = (grad_hidden * gate * sigma).astype(jnp.bfloat16)
    gate_grad = jnp.einsum(
        "td,tf->df", normed_two_low, gate_low, preferred_element_type=jnp.float32
    )
    up_grad = jnp.einsum("td,tf->df", normed_two_low, upper_low, preferred_element_type=jnp.float32)
    grad_normed_two = jnp.einsum(
        "tf,df->td", gate_low, wg_full, preferred_element_type=jnp.float32
    ) + jnp.einsum("tf,df->td", upper_low, wu_full, preferred_element_type=jnp.float32)
    grad_middle_norm, second_gain_grad = norm_backward(
        grad_normed_two, unit_two, scale_two, gain_two
    )
    grad_middle = grad_rows + grad_middle_norm
    grad_branch = grad_middle.astype(jnp.bfloat16)
    output_grad = jnp.einsum(
        "tc,td->cd", heads_flat, grad_branch, preferred_element_type=jnp.float32
    )
    grad_heads = (
        jnp.einsum("td,cd->tc", grad_branch, wo_full, preferred_element_type=jnp.float32)
        .astype(jnp.bfloat16)
        .reshape(token_count, QH, HD)
    )
    grad_head_rows = lax.all_to_all(grad_heads, "seq", split_axis=1, concat_axis=0, tiled=True)
    grad_blocks = grad_head_rows.reshape(count, block, pair_count, group, HD)

    def backward_block(carry, items):
        key_acc, value_acc = carry
        query_block, index_block, start_block, grad_block, log_block = items
        scores = block_scores(query_block, index_block, start_block)
        probs = jnp.exp(scores - log_block)
        probs_low = probs.astype(jnp.bfloat16)
        grad_probs = jnp.einsum(
            "bkgd,tkd->kgbt", grad_block, value_all, preferred_element_type=jnp.float32
        )
        grad_scores = (
            probs * (grad_probs - jnp.sum(probs * grad_probs, -1, keepdims=True))
        ).astype(jnp.bfloat16)
        query_grad_block = (
            jnp.einsum("kgbt,tkd->bkgd", grad_scores, key_all, preferred_element_type=jnp.float32)
            * factor
        )
        key_acc = (
            key_acc
            + jnp.einsum(
                "kgbt,bkgd->tkd", grad_scores, query_block, preferred_element_type=jnp.float32
            )
            * factor
        )
        value_acc = value_acc + jnp.einsum(
            "kgbt,bkgd->tkd", probs_low, grad_block, preferred_element_type=jnp.float32
        )
        return ((key_acc, value_acc), query_grad_block.reshape(block, head_count, HD))

    empty = jnp.zeros((2 * half_len, pair_count, HD), jnp.float32)
    (key_acc, value_acc), query_grad_blocks = lax.scan(
        backward_block,
        (empty, empty),
        (query_blocks, index_blocks, start_blocks, grad_blocks, log_totals),
    )
    key_back, value_back = (
        shifted(key_acc[:half_len].astype(jnp.bfloat16), "fsdp", -1).astype(jnp.float32),
        shifted(value_acc[:half_len].astype(jnp.bfloat16), "fsdp", -1).astype(jnp.float32),
    )
    key_local = key_acc[half_len:] + key_back
    value_local = value_acc[half_len:] + value_back
    query_grad_heads = query_grad_blocks.reshape(half_len, head_count, HD)
    grad_query_tok, grad_key_tok, grad_value_tok = (
        lax.all_to_all(
            query_grad_heads.astype(jnp.bfloat16), "seq", split_axis=0, concat_axis=1, tiled=True
        ).astype(query_grad_heads.dtype),
        lax.all_to_all(
            key_local.astype(jnp.bfloat16), "seq", split_axis=0, concat_axis=1, tiled=True
        ).astype(key_local.dtype),
        lax.all_to_all(
            value_local.astype(jnp.bfloat16), "seq", split_axis=0, concat_axis=1, tiled=True
        ).astype(value_local.dtype),
    )
    if repeat > 1:
        grad_key_tok = grad_key_tok.reshape(token_count, KVH, repeat, HD).sum(2)
        grad_value_tok = grad_value_tok.reshape(token_count, KVH, repeat, HD).sum(2)
    query_lin_grad = (
        rotate_back(grad_query_tok, cosine, sine).astype(jnp.bfloat16).reshape(token_count, QH * HD)
    )
    key_lin_grad = (
        rotate_back(grad_key_tok, cosine, sine).astype(jnp.bfloat16).reshape(token_count, KVH * HD)
    )
    value_lin_grad = grad_value_tok.astype(jnp.bfloat16).reshape(token_count, KVH * HD)
    query_grad = jnp.einsum(
        "td,tc->dc", normed_low, query_lin_grad, preferred_element_type=jnp.float32
    )
    key_grad = jnp.einsum("td,tc->dc", normed_low, key_lin_grad, preferred_element_type=jnp.float32)
    value_grad = jnp.einsum(
        "td,tc->dc", normed_low, value_lin_grad, preferred_element_type=jnp.float32
    )
    grad_normed_one = jnp.einsum(
        "tc,dc->td", query_lin_grad, wq_full, preferred_element_type=jnp.float32
    )
    grad_normed_one = grad_normed_one + jnp.einsum(
        "tc,dc->td", key_lin_grad, wk_full, preferred_element_type=jnp.float32
    )
    grad_normed_one = grad_normed_one + jnp.einsum(
        "tc,dc->td", value_lin_grad, wv_full, preferred_element_type=jnp.float32
    )
    grad_rows_one, first_gain_grad = norm_backward(grad_normed_one, unit_one, scale_one, gain_one)
    input_grad = (grad_middle + grad_rows_one).astype(jnp.bfloat16)[None]
    pieces = (
        lax.psum_scatter(
            first_gain_grad.astype(jnp.bfloat16), "fsdp", scatter_dimension=0, tiled=True
        ).astype(jnp.float32),
        lax.psum_scatter(
            query_grad.astype(jnp.bfloat16), "fsdp", scatter_dimension=0, tiled=True
        ).astype(jnp.float32),
        lax.psum_scatter(
            key_grad.astype(jnp.bfloat16), "fsdp", scatter_dimension=0, tiled=True
        ).astype(jnp.float32),
        lax.psum_scatter(
            value_grad.astype(jnp.bfloat16), "fsdp", scatter_dimension=0, tiled=True
        ).astype(jnp.float32),
        lax.psum_scatter(
            output_grad.astype(jnp.bfloat16), "fsdp", scatter_dimension=0, tiled=True
        ).astype(jnp.float32),
        lax.psum_scatter(
            second_gain_grad.astype(jnp.bfloat16), "fsdp", scatter_dimension=0, tiled=True
        ).astype(jnp.float32),
        lax.psum_scatter(
            gate_grad.astype(jnp.bfloat16), "fsdp", scatter_dimension=0, tiled=True
        ).astype(jnp.float32),
        lax.psum_scatter(
            up_grad.astype(jnp.bfloat16), "fsdp", scatter_dimension=0, tiled=True
        ).astype(jnp.float32),
        lax.psum_scatter(
            down_grad.astype(jnp.bfloat16), "fsdp", scatter_dimension=0, tiled=True
        ).astype(jnp.float32),
    )
    shares = (
        lax.psum(pieces[0].astype(jnp.bfloat16), "seq").astype(jnp.float32),
        lax.psum(pieces[1].astype(jnp.bfloat16), "seq").astype(jnp.float32),
        lax.psum(pieces[2].astype(jnp.bfloat16), "seq").astype(jnp.float32),
        lax.psum(pieces[3].astype(jnp.bfloat16), "seq").astype(jnp.float32),
        lax.psum(pieces[4].astype(jnp.bfloat16), "seq").astype(jnp.float32),
        lax.psum(pieces[5].astype(jnp.bfloat16), "seq").astype(jnp.float32),
        lax.psum(pieces[6].astype(jnp.bfloat16), "seq").astype(jnp.float32),
        lax.psum(pieces[7].astype(jnp.bfloat16), "seq").astype(jnp.float32),
        lax.psum(pieces[8].astype(jnp.bfloat16), "seq").astype(jnp.float32),
    )
    return (
        block_output,
        input_grad,
        shares[0],
        shares[1],
        shares[2],
        shares[3],
        shares[4],
        shares[5],
        shares[6],
        shares[7],
        shares[8],
    )


def plain_solution(mesh):
    placed = (
        P("fsdp", "seq", None),
        P("fsdp", "seq"),
        P("fsdp"),
        P("fsdp", None),
        P("fsdp", None),
        P("fsdp", None),
        P("fsdp", None),
        P("fsdp"),
        P("fsdp", None),
        P("fsdp", None),
        P("fsdp", None),
        P("fsdp", "seq", None),
    )
    return jax.shard_map(
        plain_body,
        mesh=mesh,
        in_specs=placed,
        out_specs=(
            P("fsdp", "seq", None),
            P("fsdp", "seq", None),
            P("fsdp"),
            P("fsdp", None),
            P("fsdp", None),
            P("fsdp", None),
            P("fsdp", None),
            P("fsdp"),
            P("fsdp", None),
            P("fsdp", None),
            P("fsdp", None),
        ),
        check_vma=False,
    )
```

```python
import functools
import math

import jax
import jax.numpy as jnp
from jax import lax
from jax.experimental import pallas as pl
from jax.experimental.pallas import tpu as pltpu
from jax.sharding import Mesh
from jax.sharding import PartitionSpec as P

QH = 16
KVH = 8
HD = 96


THETA = 100000.0
EPS = 1e-05
LOW = jnp.bfloat16
F32 = jnp.float32
NEG = -1e30
LN2 = math.log(2.0)


def contract(left, right, left_axis, right_axis):
    return lax.dot_general(
        left, right, (((left_axis,), (right_axis,)), ((), ())), preferred_element_type=F32
    )


def visible(first, second, query_block, key_block, size):
    key = key_block * size + lax.broadcasted_iota(jnp.int32, (size, size), 0)
    query = query_block * size + lax.broadcasted_iota(jnp.int32, (1, size), 1)
    start = jnp.where(query >= second, second, jnp.where(query >= first, first, 0))
    return (key >= start) & (key <= query)


def slot_of(block, count):
    return (block % (count // 2)) * 2 + block // (count // 2)


def forward_kernel(
    scalars,
    own_ref,
    other_ref,
    low_ref,
    full_ref,
    log_ref,
    query_s,
    key_s,
    value_s,
    top_s,
    total_s,
    mixed_s,
    *,
    size,
    count,
):
    half = scalars[0]
    first = scalars[1]
    second = scalars[2]
    here = pl.program_id(0)
    per_half = count // 2

    @pl.when(here == 0)
    def _():
        for ref, side in ((own_ref, half), (other_ref, 1 - half)):
            for step in range(per_half):
                block = side * per_half + step
                columns = slice(step * size, (step + 1) * size)
                query_s[block] = ref[0:HD, columns]
                key_s[block] = ref[HD : 2 * HD, columns].T
                value_s[block] = ref[2 * HD : 3 * HD, columns]

    query = query_s[here]
    top_s[...] = jnp.full_like(top_s, NEG)
    total_s[...] = jnp.zeros_like(total_s)
    mixed_s[...] = jnp.zeros_like(mixed_s)

    def add_block(block, masked):
        scores = contract(key_s[block], query, 1, 0)
        if masked:
            scores = jnp.where(visible(first, second, here, block, size), scores, NEG)
        old_top = top_s[...]
        top = jnp.maximum(old_top, jnp.max(scores, 0, keepdims=True))
        expo = jnp.exp2(scores - top)
        scale = jnp.exp2(old_top - top)
        top_s[...] = top
        total_s[...] = total_s[...] * scale + jnp.sum(expo, 0, keepdims=True)
        mixed_s[...] = mixed_s[...] * scale + contract(value_s[block], expo.astype(LOW), 1, 0)

    last = count - 1

    @pl.loop(1, jnp.where(here == last, 1, here))
    def _(block):
        add_block(block, False)

    @pl.loop(0, jnp.where(here == last, count, jnp.minimum(here + 1, 2)))
    def _(step):
        add_block(jnp.where(here == last, step, step * here), True)

    total = total_s[...]
    result = mixed_s[...] / total
    full_ref[0] = result
    low_ref[0] = result.astype(LOW)
    log_ref[0] = top_s[...] + jnp.log2(total)


def backward_kernel(
    scalars,
    own_ref,
    other_ref,
    grad_ref,
    full_ref,
    log_ref,
    kept_ref,
    leaving_ref,
    query_s,
    key_s,
    value_s,
    delta_s,
    query_grad_s,
    key_grad_s,
    value_grad_s,
    *,
    size,
    count,
):
    half = scalars[0]
    first = scalars[1]
    second = scalars[2]
    here = pl.program_id(0)
    per_half = count // 2

    @pl.when(here == 0)
    def _():
        for ref, side in ((own_ref, half), (other_ref, 1 - half)):
            for step in range(per_half):
                block = side * per_half + step
                columns = slice(step * size, (step + 1) * size)
                query_s[block] = ref[0:HD, columns]
                key_s[block] = ref[HD : 2 * HD, columns]
                value_s[block] = ref[2 * HD : 3 * HD, columns].T
        for block in range(count):
            delta_s[block] = jnp.sum(
                grad_ref[slot_of(block, count)].astype(F32) * full_ref[block], 0, keepdims=True
            )
        query_grad_s[...] = jnp.zeros_like(query_grad_s)

    key_grad_s[...] = jnp.zeros_like(key_grad_s)
    value_grad_s[...] = jnp.zeros_like(value_grad_s)
    key = key_s[here]
    key_rows = key.T
    value_rows = value_s[here]

    def add_block(block, masked):
        query = query_s[block]
        grad = grad_ref[slot_of(block, count)]
        scores = contract(key_rows, query, 1, 0)
        if masked:
            scores = jnp.where(visible(first, second, block, here, size), scores, NEG)
        probs = jnp.exp2(scores - log_ref[block])
        grad_probs = contract(value_rows, grad, 1, 0)
        grad_scores = (probs * (grad_probs - delta_s[block])).astype(LOW)
        value_grad_s[...] += contract(grad, probs.astype(LOW), 1, 1)
        key_grad_s[...] += contract(query, grad_scores, 1, 1)
        query_grad_s[block] += contract(key, grad_scores, 1, 0)

    last = count - 1

    @pl.loop(here + 1, jnp.where(here == 0, 1, last))
    def _(block):
        add_block(block, False)

    @pl.loop(0, jnp.where(here == 0, count, jnp.where(here == last, 1, 2)))
    def _(step):
        add_block(jnp.where(here == 0, step, jnp.where(step == 0, here, last)), True)

    side = here // per_half
    columns = pl.ds(pl.multiple_of((here % per_half) * size, size), size)

    def write(out_ref):
        out_ref[0:HD, columns] = (query_grad_s[here] * HD**-0.5).astype(LOW)
        out_ref[HD : 2 * HD, columns] = (key_grad_s[...] * LN2).astype(LOW)
        out_ref[2 * HD : 3 * HD, columns] = value_grad_s[...].astype(LOW)

    @pl.when(side == half)
    def _():
        write(kept_ref)

    @pl.when(side != half)
    def _():
        write(leaving_ref)


def attend_forward(scalars, own, other, size):
    count = 2 * own.shape[1] // size
    whole = lambda shape: pl.BlockSpec(shape, lambda i, s: (0,) * len(shape))
    pairs = count * (count + 1) // 2
    return pl.pallas_call(
        functools.partial(forward_kernel, size=size, count=count),
        grid_spec=pltpu.PrefetchScalarGridSpec(
            num_scalar_prefetch=1,
            grid=(count,),
            in_specs=[whole(own.shape), whole(other.shape)],
            out_specs=[
                pl.BlockSpec(
                    (1, HD, size), lambda i, s: (slot_of(i, count), 0, 0)
                ),
                pl.BlockSpec((1, HD, size), lambda i, s: (i, 0, 0)),
                pl.BlockSpec((1, 1, size), lambda i, s: (i, 0, 0)),
            ],
            scratch_shapes=[
                pltpu.VMEM((count, HD, size), LOW),
                pltpu.VMEM((count, size, HD), LOW),
                pltpu.VMEM((count, HD, size), LOW),
                pltpu.VMEM((1, size), F32),
                pltpu.VMEM((1, size), F32),
                pltpu.VMEM((HD, size), F32),
            ],
        ),
        out_shape=[
            jax.ShapeDtypeStruct((count, HD, size), LOW),
            jax.ShapeDtypeStruct((count, HD, size), F32),
            jax.ShapeDtypeStruct((count, 1, size), F32),
        ],
        compiler_params=pltpu.CompilerParams(
            dimension_semantics=("arbitrary",), vmem_limit_bytes=32 * 2**20
        ),
        cost_estimate=pl.CostEstimate(
            flops=pairs * size * size * HD * 32,
            bytes_accessed=10 * 2**20,
            transcendentals=pairs * size * size,
        ),
        name="attend_forward",
    )(scalars, own, other)


def attend_backward(scalars, own, other, grad, full, log_total):
    count, _, size = grad.shape
    whole = lambda shape: pl.BlockSpec(shape, lambda i, s: (0,) * len(shape))
    pairs = count * (count + 1) // 2
    out_shape = own.shape
    return pl.pallas_call(
        functools.partial(backward_kernel, size=size, count=count),
        grid_spec=pltpu.PrefetchScalarGridSpec(
            num_scalar_prefetch=1,
            grid=(count,),
            in_specs=[
                whole(own.shape),
                whole(other.shape),
                whole(grad.shape),
                whole(full.shape),
                whole(log_total.shape),
            ],
            out_specs=[whole(out_shape)] * 2,
            scratch_shapes=[
                pltpu.VMEM((count, HD, size), LOW),
                pltpu.VMEM((count, HD, size), LOW),
                pltpu.VMEM((count, size, HD), LOW),
                pltpu.VMEM((count, 1, size), F32),
                pltpu.VMEM((count, HD, size), F32),
                pltpu.VMEM((HD, size), F32),
                pltpu.VMEM((HD, size), F32),
            ],
        ),
        out_shape=[jax.ShapeDtypeStruct(out_shape, LOW)] * 2,
        compiler_params=pltpu.CompilerParams(
            dimension_semantics=("arbitrary",), vmem_limit_bytes=32 * 2**20
        ),
        cost_estimate=pl.CostEstimate(
            flops=pairs * size * size * HD * 42,
            bytes_accessed=16 * 2**20,
            transcendentals=pairs * size * size,
        ),
        name="attend_backward",
    )(scalars, own, other, grad, full, log_total)


def place_rows_kernel(order, *refs):
    pieces, out_ref = refs[:-1], refs[-1]
    size = pieces[0].shape[0]
    for index, piece in enumerate(pieces):
        start = pl.multiple_of(order[index] * size, size)
        out_ref[pl.ds(start, size), :] = piece[...].astype(F32)


def place_rows(order, pieces):
    size, width = pieces[0].shape
    total = size * len(pieces)
    step = 512
    return pl.pallas_call(
        place_rows_kernel,
        grid_spec=pltpu.PrefetchScalarGridSpec(
            num_scalar_prefetch=1,
            grid=(width // step,),
            in_specs=[pl.BlockSpec((size, step), lambda i, s: (0, i)) for _ in pieces],
            out_specs=pl.BlockSpec((total, step), lambda i, s: (0, i)),
        ),
        out_shape=jax.ShapeDtypeStruct((total, width), F32),
        compiler_params=pltpu.CompilerParams(vmem_limit_bytes=24 * 2**20),
        cost_estimate=pl.CostEstimate(
            flops=0, bytes_accessed=total * width * 6, transcendentals=0
        ),
        name="place_rows",
    )(order, *pieces)


def place_columns_kernel(order, gain_ref, gate_w_ref, up_w_ref, *refs):
    count = (len(refs) - 3) // 2
    gates, ups = refs[:count], refs[count : 2 * count]
    gate_ref, up_ref, sum_ref = refs[2 * count :]
    size = gates[0].shape[1]
    gain = gain_ref[...]
    total = jnp.zeros((gate_ref.shape[0], size), F32)
    for index in range(count):
        columns = pl.ds(pl.multiple_of(order[index] * size, size), size)
        gate, up = gates[index][...].astype(F32), ups[index][...].astype(F32)
        total += gate * gate_w_ref[:, columns].astype(F32)
        total += up * up_w_ref[:, columns].astype(F32)
        gate_ref[:, columns] = gate * gain
        up_ref[:, columns] = up * gain

    @pl.when(pl.program_id(0) == 0)
    def _():
        sum_ref[...] = jnp.zeros_like(sum_ref)

    sum_ref[...] += jnp.sum(total, 1, keepdims=True)


def place_columns(order, gain, gate_weight, up_weight, gates, ups, shards):
    rows, width = gate_weight.shape
    span = width // shards
    size = span // len(gates)
    wide = pl.BlockSpec((rows, span), lambda i, s: (0, i))
    thin = pl.BlockSpec((rows, 1), lambda i, s: (0, 0))
    pieces = [pl.BlockSpec((rows, size), lambda i, s: (0, i)) for _ in (*gates, *ups)]
    return pl.pallas_call(
        place_columns_kernel,
        grid_spec=pltpu.PrefetchScalarGridSpec(
            num_scalar_prefetch=1,
            grid=(shards,),
            in_specs=[thin, wide, wide, *pieces],
            out_specs=[wide, wide, thin],
        ),
        out_shape=[
            jax.ShapeDtypeStruct((rows, width), F32),
            jax.ShapeDtypeStruct((rows, width), F32),
            jax.ShapeDtypeStruct((rows, 1), F32),
        ],
        compiler_params=pltpu.CompilerParams(
            dimension_semantics=("arbitrary",), vmem_limit_bytes=24 * 2**20
        ),
        cost_estimate=pl.CostEstimate(
            flops=rows * width * 6, bytes_accessed=rows * width * 16, transcendentals=0
        ),
        name="place_columns",
    )(order, gain, gate_weight, up_weight, *gates, *ups)


def place_heads_kernel(gain_ref, query_w, key_w, value_w, all_ref, query_ref, key_ref, value_ref, sum_ref):
    rows = gain_ref.shape[0]
    wide = query_ref.shape[1] // KVH
    gain = gain_ref[...]
    total = jnp.zeros((rows, 4 * HD), F32)
    pieces = [all_ref[i * rows : (i + 1) * rows, :].astype(F32) for i in range(KVH)]
    for start in range(0, KVH, 2):
        value = jnp.concatenate([piece[:, :wide] for piece in pieces[start : start + 2]], 1)
        columns = slice(start * wide, (start + 2) * wide)
        total += value * query_w[:, columns].astype(F32)
        query_ref[:, columns] = value * gain
    for first, weight, out_ref in ((wide, key_w, key_ref), (wide + HD, value_w, value_ref)):
        for start in range(0, KVH, 4):
            value = jnp.concatenate(
                [piece[:, first : first + HD] for piece in pieces[start : start + 4]], 1
            )
            columns = slice(start * HD, (start + 4) * HD)
            total += value * weight[:, columns].astype(F32)
            out_ref[:, columns] = value * gain
    sum_ref[...] = jnp.sum(total, 1, keepdims=True)


def place_heads(gain, query_weight, key_weight, value_weight, pieces):
    weights = (query_weight, key_weight, value_weight)
    rows = gain.shape[0]
    return pl.pallas_call(
        place_heads_kernel,
        out_shape=[jax.ShapeDtypeStruct(weight.shape, F32) for weight in weights]
        + [jax.ShapeDtypeStruct((rows, 1), F32)],
        compiler_params=pltpu.CompilerParams(vmem_limit_bytes=32 * 2**20),
        cost_estimate=pl.CostEstimate(
            flops=rows * 3072 * 4, bytes_accessed=rows * 3072 * 8, transcendentals=0
        ),
        name="place_heads",
    )(gain, *weights, pieces)


def merge_kernel(scalars, kept_ref, came_ref, cosine_ref, sine_ref, out_ref, split_ref):
    lead = scalars[0] == 0
    lines, _, size = split_ref.shape
    for line in range(lines):
        columns = slice(line * size, (line + 1) * size)
        kept = kept_ref[:, columns].astype(F32)
        came = came_ref[:, columns].astype(F32)
        cosine, sine = cosine_ref[:, columns], sine_ref[:, columns]
        joint = kept[HD:] + came[HD:]
        first = jnp.where(lead, kept[:HD], came[:HD])
        second = jnp.where(lead, came[:HD], kept[:HD])
        turned = []
        for value in (first, second, joint[:HD]):
            low, high = value[: HD // 2], value[HD // 2 :]
            turned.append(low * cosine + high * sine)
            turned.append(high * cosine - low * sine)
        turned.append(joint[HD:])
        result = jnp.concatenate([part.astype(LOW) for part in turned], 0)
        out_ref[:, columns] = result
        split_ref[line] = result


def merge(scalars, kept, came, cosine, sine, lines):
    tokens = kept.shape[1]
    whole = lambda value: pl.BlockSpec(value.shape, lambda i, s: (0,) * len(value.shape))
    outs = [
        jax.ShapeDtypeStruct((4 * HD, tokens), LOW),
        jax.ShapeDtypeStruct((lines, 4 * HD, tokens // lines), LOW),
    ]
    return pl.pallas_call(
        merge_kernel,
        grid_spec=pltpu.PrefetchScalarGridSpec(
            num_scalar_prefetch=1,
            grid=(1,),
            in_specs=[whole(value) for value in (kept, came, cosine, sine)],
            out_specs=[whole(value) for value in outs],
        ),
        out_shape=outs,
        compiler_params=pltpu.CompilerParams(vmem_limit_bytes=24 * 2**20),
        cost_estimate=pl.CostEstimate(
            flops=tokens * HD * 24, bytes_accessed=tokens * HD * 30, transcendentals=0
        ),
        name="merge",
    )(scalars, kept, came, cosine, sine)


def pack_kernel(scalars, gain_ref, query_ref, key_ref, value_ref, *outs):
    core = scalars[3]
    gain = gain_ref[...]
    wide = query_ref.shape[1] // KVH
    span = wide + 2 * HD
    for which in range(2):

        @pl.when(core == which)
        def _():
            for line in range(KVH // 2):
                head = 2 * line + which
                value = jnp.concatenate(
                    [
                        query_ref[:, head * wide : (head + 1) * wide].astype(F32),
                        key_ref[:, head * HD : (head + 1) * HD].astype(F32),
                        value_ref[:, head * HD : (head + 1) * HD].astype(F32),
                    ],
                    1,
                )
                place = (line % 2) * span
                outs[line // 2][:, place : place + span] = (value * gain).astype(LOW)


def pack(scalars, gain, query_weight, key_weight, value_weight):
    rows, width = query_weight.shape
    whole = lambda value: pl.BlockSpec(value.shape, lambda i, s: (0, 0))
    weights = (gain, query_weight, key_weight, value_weight)
    outs = [jax.ShapeDtypeStruct((rows, width // 2), LOW)] * 2
    return pl.pallas_call(
        pack_kernel,
        grid_spec=pltpu.PrefetchScalarGridSpec(
            num_scalar_prefetch=1,
            grid=(1,),
            in_specs=[whole(value) for value in weights],
            out_specs=[whole(value) for value in outs],
        ),
        out_shape=outs,
        compiler_params=pltpu.CompilerParams(vmem_limit_bytes=24 * 2**20),
        cost_estimate=pl.CostEstimate(
            flops=rows * width, bytes_accessed=rows * width * 6, transcendentals=0
        ),
        name="pack",
    )(scalars, *weights)


def spread_kernel(scalars, lin_ref, cosine_ref, sine_ref, own_ref, leaving_ref):
    cosine, sine = cosine_ref[...], sine_ref[...]

    def turn(start, factor):
        low = lin_ref[start : start + HD // 2, :]
        high = lin_ref[start + HD // 2 : start + HD, :]
        turned = ((low * cosine - high * sine) * factor, (high * cosine + low * sine) * factor)
        return jnp.concatenate([part.astype(LOW) for part in turned], 0)

    lead = scalars[0] == 0
    first, second = turn(0, HD**-0.5 / LN2), turn(HD, HD**-0.5 / LN2)

    @pl.when(lead)
    def _():
        own_ref[0:HD] = first
        leaving_ref[0:HD] = second

    @pl.when(jnp.logical_not(lead))
    def _():
        own_ref[0:HD] = second
        leaving_ref[0:HD] = first

    key = turn(2 * HD, 1.0)
    value = lin_ref[3 * HD : 4 * HD].astype(LOW)
    for ref in (own_ref, leaving_ref):
        ref[HD : 2 * HD] = key
        ref[2 * HD : 3 * HD] = value


def spread(scalars, lin, cosine, sine):
    tokens = lin.shape[1]
    step = 512
    column = lambda rows: pl.BlockSpec((rows, step), lambda i, s: (0, i))
    return pl.pallas_call(
        spread_kernel,
        grid_spec=pltpu.PrefetchScalarGridSpec(
            num_scalar_prefetch=1,
            grid=(tokens // step,),
            in_specs=[column(4 * HD), column(HD // 2), column(HD // 2)],
            out_specs=[column(3 * HD)] * 2,
        ),
        out_shape=[jax.ShapeDtypeStruct((3 * HD, tokens), LOW)] * 2,
        compiler_params=pltpu.CompilerParams(vmem_limit_bytes=24 * 2**20),
        cost_estimate=pl.CostEstimate(
            flops=tokens * HD * 24, bytes_accessed=tokens * HD * 36, transcendentals=0
        ),
        name="spread",
    )(scalars, lin, cosine, sine)


def swap(value, axis):
    return lax.ppermute(value, axis, [(0, 1), (1, 0)])


def swap_near(value):
    return lax.ppermute(value, "z", [(0, 1), (1, 0), (2, 3), (3, 2)])


def swap_far(value):
    return lax.ppermute(value, "z", [(0, 2), (2, 0), (1, 3), (3, 1)])


def tie(*values):
    return lax.optimization_barrier(values)


def in_order(place, own, other):
    return (jnp.where(place == 0, own, other), jnp.where(place == 0, other, own))


def both(place, own, other):
    return jnp.concatenate(in_order(place, own, other), 0)


def spread_out(value, first, second):
    other = swap(value, first)
    pair = jnp.stack(in_order(lax.axis_index(first), value, other))
    return pair, swap(pair, second)


def placed(pair, other, second):
    pairs = in_order(lax.axis_index(second), pair, other)
    grid = jnp.stack(pairs, 0 if second == "y" else 1)
    return grid.reshape(-1, *grid.shape[3:])


def pick(array, axis, at):
    return lax.dynamic_index_in_dim(array, at, axis, keepdims=False)


def halve(value, axis, along=0):
    at = lax.axis_index(axis)
    return pick(value, along, at), swap(pick(value, along, 1 - at), axis)


def halve_x(value):
    return halve(value.reshape(2, 2, -1, value.shape[-1]), "x", 1)


def halve_y(value):
    return halve(value.reshape(2, 2, -1, value.shape[-1]), "y", 0)


def fast_body(
    tokens,
    positions,
    first_gain,
    query_weight,
    key_weight,
    value_weight,
    output_weight,
    second_gain,
    gate_weight,
    up_weight,
    down_weight,
    cotangent,
):
    seq = ("z", "c")
    fsdp = ("y", "x")
    z, core, half = lax.axis_index("z"), lax.axis_index("c"), lax.axis_index("x")
    near = z % 2
    lines = lax.axis_size("z")
    seq_count = 2 * lines
    shards = lax.axis_size("y") * 2
    spot = z * 2 + core
    quarter = near * 2 + core
    rows = tokens[0]
    count, width = rows.shape
    chip_count = 2 * count
    half_len = count * seq_count
    seq_len = 2 * half_len

    begins = jnp.where(
        (spot == 0) & (half == 0),
        count - 1 - positions[0, count - 1],
        half * half_len + spot * count - positions[0, 0],
    )
    ends = begins + (seq_len - count)
    scalars = jnp.stack([half, begins, ends, core]).astype(jnp.int32)

    gain_one = first_gain.astype(F32)[:, None]
    gain_two = second_gain.astype(F32)[:, None]

    def row_scale(value):
        return lax.rsqrt(jnp.mean(value * value, -1, keepdims=True) + EPS)

    take = functools.partial(lax.dynamic_slice_in_dim, axis=1)
    take_rows = functools.partial(lax.dynamic_slice_in_dim, axis=0)
    gather = lambda value, axes: lax.all_gather(value, axes, axis=0, tiled=True)
    own_rows = rows.astype(F32)
    own_unit_scale = row_scale(own_rows)
    own_unit = own_rows * own_unit_scale
    units = gather(own_unit.astype(LOW), seq)
    wide = QH // KVH * HD
    qkv_shard = (
        jnp.concatenate(
            [
                take(query_weight, spot * wide, wide),
                take(key_weight, spot * HD, HD),
                take(value_weight, spot * HD, HD),
            ],
            1,
        ).astype(F32)
        * gain_one
    ).astype(LOW)
    out_rows = output_weight.shape[0] // 2
    out_shard = take_rows(output_weight, core * out_rows, out_rows)
    piece = down_weight.shape[0] // 4
    down_shard = take_rows(down_weight, quarter * piece, piece)
    gate_shard, up_shard = (
        (
            jnp.concatenate(
                [
                    take(weight, shard * 4 * piece + quarter * piece, piece)
                    for shard in range(shards)
                ],
                1,
            ).astype(F32)
            * gain_two
        ).astype(LOW)
        for weight in (gate_weight, up_weight)
    )
    side = lax.axis_index("y")
    qkv_pair = jnp.stack(in_order(half, qkv_shard, swap(qkv_shard, "x")))
    gate_pair = jnp.stack(in_order(half, gate_shard, swap(gate_shard, "x")))
    up_pair = jnp.stack(in_order(side, up_shard, swap(up_shard, "y")))
    qkv_pair, gate_pair, up_pair = tie(qkv_pair, gate_pair, up_pair)
    qkv_w = placed(qkv_pair, swap(qkv_pair, "y"), "y")
    gate_pair, up_pair = (gate_pair, swap(gate_pair, "y")), (up_pair, swap(up_pair, "x"))

    place = half * half_len + jnp.arange(half_len, dtype=jnp.int32)
    start = jnp.where(place >= ends, ends, jnp.where(place >= begins, begins, 0))
    freq = THETA ** (-(jnp.arange(HD // 2, dtype=F32) * 2.0 / HD))
    angle = freq[:, None] * (place - start).astype(F32)[None, :]
    cosine, sine = jnp.cos(angle), jnp.sin(angle)
    chip_rows = both(core, rows, swap(rows, "c"))
    units, own_cot, chip_rows = tie(units, cotangent[0], chip_rows)
    own, leaving = spread(scalars, contract(qkv_w, units, 0, 1), cosine, sine)

    near_cot = swap_near(own_cot)
    other, out_shard, down_shard, near_cot, chip_cot, gate_pair, up_pair = tie(
        swap(leaving, "x"),
        out_shard,
        down_shard,
        near_cot,
        both(core, own_cot, swap(own_cot, "c")),
        gate_pair,
        up_pair,
    )
    out_w = gather(out_shard, fsdp)
    cut = piece // 2
    down_x = jnp.stack(in_order(half, down_shard[:cut], swap(down_shard[:cut], "x")))
    down_y = jnp.stack(in_order(side, down_shard[cut:], swap(down_shard[cut:], "y")))
    near_other = swap(near_cot, "c")
    head_low, head_full, log_total = attend_forward(scalars, own, other, chip_count)
    exchange = lambda value: lax.all_to_all(
        value, ("z", "x"), split_axis=0, concat_axis=0, tiled=True
    )
    head_low, down_x, down_y, near_other = tie(head_low, down_x, down_y, near_other)
    down_x, down_y = (down_x, swap(down_x, "y")), (down_y, swap(down_y, "x"))
    lead_shard, tail_shard = pack(scalars, gain_one, query_weight, key_weight, value_weight)
    lead_w, tail_w = gather(lead_shard, fsdp), gather(tail_shard, fsdp)
    heads, gate_w, up_w, near_cot, lead_shard = tie(
        exchange(head_low),
        placed(*gate_pair, "y"),
        placed(*up_pair, "x"),
        jnp.concatenate([near_cot, near_other], 0),
        lead_shard,
    )
    down_halves = placed(*down_x, "y"), placed(*down_y, "x")
    down_w = jnp.stack([value.reshape(shards, cut, width) for value in down_halves], 1)
    down_w = down_w.reshape(-1, width)
    heads = heads.reshape(QH // 2 * HD, chip_count)

    mine_of = lambda value: take_rows(value, core * count, count)
    theirs_of = lambda value: take_rows(value, (1 - core) * count, count)
    branch = contract(heads, out_w, 0, 0).astype(LOW)
    middle = chip_rows.astype(F32) + (branch.astype(F32) + swap(branch, "c").astype(F32))
    middle_scale = row_scale(middle)
    chip_unit = middle * middle_scale
    own_middle, own_scale, own_middle_unit = (
        mine_of(middle),
        mine_of(middle_scale),
        mine_of(chip_unit),
    )
    chip_unit = chip_unit.astype(LOW)
    near_unit = swap_near(mine_of(chip_unit))
    near_unit = jnp.concatenate([near_unit, swap(near_unit, "c")], 0)

    def feed(unit):
        gate, upper = contract(unit, gate_w, 1, 0), contract(unit, up_w, 1, 0)
        sigma = jax.nn.sigmoid(gate)
        silu = gate * sigma
        return (silu * upper).astype(LOW), (gate, upper, sigma, silu)

    def feed_back(cot, kept):
        gate, upper, sigma, silu = kept
        grad_hidden = contract(cot, down_w, 1, 1)
        gate_low = (grad_hidden * upper * sigma * (1.0 + gate * (1.0 - sigma))).astype(LOW)
        upper_low = (grad_hidden * silu).astype(LOW)
        part = contract(gate_low, gate_w, 1, 1) + contract(upper_low, up_w, 1, 1)
        return gate_low, upper_low, part

    def chip_sum(chip_part, near_part):
        near_sum = near_part[:count].astype(F32) + swap(near_part[count:].astype(LOW), "c")
        own_sum = mine_of(chip_part).astype(F32) + swap(theirs_of(chip_part).astype(LOW), "c")
        return own_sum, near_sum.astype(LOW)

    stack = lambda first, second: jnp.concatenate([first, second], 0)
    scatter = lambda value: lax.psum_scatter(value, fsdp, scatter_dimension=0, tiled=True)
    chip_hidden, chip_kept = feed(chip_unit)
    near_hidden, near_kept = feed(near_unit)
    down_part = contract(
        stack(chip_hidden, near_hidden), stack(chip_cot, near_cot), 0, 0
    ).astype(LOW)
    near_cot, down_part = tie(near_cot, down_part)
    feed_own, feed_near = chip_sum(
        contract(chip_hidden, down_w, 1, 0), contract(near_hidden, down_w, 1, 0)
    )
    feed_near = swap_near(feed_near)
    near_gate, near_upper, near_part = feed_back(near_cot, near_kept)
    chip_gate, chip_upper, chip_part = feed_back(chip_cot, chip_kept)
    grad_two, near_sum = chip_sum(chip_part, near_part)

    def halves_first(value):
        cut = value.shape[-1] // 2
        return halve_x(value[:, :cut]), halve_y(value[:, cut:])

    def halves_second(firsts):
        return halve(sum(firsts[0]), "y"), halve(sum(firsts[1]), "x")

    def halves_end(seconds):
        return jnp.concatenate([sum(seconds[0]), sum(seconds[1])], 1)

    down_first = halves_first(down_part)
    near_sum, near_gate, near_upper = tie(near_sum, near_gate, near_upper)
    grad_two = grad_two + swap_near(near_sum).astype(F32)
    all_units = stack(chip_unit, near_unit)
    gate_part = contract(all_units, stack(chip_gate, near_gate), 0, 0).astype(LOW)
    gate_half = halve_x(gate_part)
    up_part = contract(all_units, stack(chip_upper, near_upper), 0, 0).astype(LOW)
    up_half = halve_y(up_part)
    up_part, down_first = tie(up_part, down_first)
    down_second = halves_second(down_first)
    grad_two, down_second = tie(grad_two, down_second)
    down_grad = halves_end(down_second)
    down_far = swap_far(down_grad)
    grad_middle = own_cot.astype(F32) + own_scale * (
        grad_two - own_middle_unit * jnp.mean(grad_two * own_middle_unit, -1, keepdims=True)
    )
    own_branch = grad_middle.astype(LOW)
    grad_branch = both(core, own_branch, swap(own_branch, "c"))
    grad_heads = contract(out_w, grad_branch, 1, 1).astype(LOW)
    grad_heads, grad_branch, gate_half, up_half, feed_near, lead_w, tail_w = tie(
        grad_heads, grad_branch, gate_half, up_half, feed_near, lead_w, tail_w
    )

    gate_half, up_half = halve(sum(gate_half), "y"), halve(sum(up_half), "x")
    output_part = contract(heads, grad_branch, 1, 0).astype(LOW)
    output_grad = scatter(output_part)
    grad_head, output_part, gate_half, up_half, down_far = tie(
        exchange(grad_heads.reshape(2 * lines, HD, chip_count)),
        output_part,
        gate_half,
        up_half,
        down_far,
    )

    gate_grad, up_grad = sum(gate_half), sum(up_half)
    gate_far = swap_far(gate_grad)
    down_sum = down_grad + down_far
    down_near = swap_near(down_sum)
    kept, leaving = attend_backward(scalars, own, other, grad_head, head_full, log_total)
    kept, leaving, gate_far, down_near, up_grad = tie(
        kept, leaving, gate_far, down_near, up_grad
    )

    up_far = swap_far(up_grad)
    gate_sum = gate_grad + gate_far
    gate_near = swap_near(gate_sum)
    block_output = (own_middle + feed_own + feed_near.astype(F32)).astype(LOW)[None]
    came, up_far, block_output = tie(swap(leaving, "x"), up_far, block_output)

    place = lax.axis_index("z")
    inner = (place == 1) | (place == 2)
    qkv_low, by_line = merge(scalars, kept, came, cosine, sine, lines)
    token_grads = lax.all_to_all(by_line, "z", split_axis=0, concat_axis=0, tiled=True)
    qkv_part = contract(units, qkv_low, 0, 1).astype(LOW).reshape(shards, 2, -1, 4 * HD)
    qkv_first = halve_x(qkv_part[:, 0]), halve_y(qkv_part[:, 1])
    qkv_second = halves_second(qkv_first)
    output_came = lax.ppermute(output_grad, "z", [(0, 1), (3, 2)])
    up_sum = up_grad + up_far
    up_near = swap_near(up_sum)
    token_grads, qkv_second, output_came, gate_near, up_near = tie(
        token_grads, qkv_second, output_came, gate_near, up_near
    )

    output_sum = output_grad + output_came
    output_sum = output_sum + lax.ppermute(output_sum, "z", [(1, 2), (2, 1)])
    qkv_grad = jnp.concatenate([sum(qkv_second[0]), sum(qkv_second[1])], 0)
    token_grads = token_grads.reshape(-1, chip_count)
    split = lead_w.shape[1]
    grad_one = contract(token_grads[:split], lead_w, 0, 1) + contract(
        token_grads[split:], tail_w, 0, 1
    )
    grad_one = mine_of(grad_one) + swap(theirs_of(grad_one).astype(LOW), "c").astype(F32)
    grad_rows = own_unit_scale * (
        grad_one - own_unit * jnp.mean(grad_one * own_unit, -1, keepdims=True)
    )
    input_grad = (grad_middle + grad_rows).astype(LOW)[None]
    output_far = lax.ppermute(output_sum, "z", [(1, 0), (2, 3)])
    output_own = jnp.where(inner, output_sum, output_far)

    def four(value, near_value):
        return value, swap(value, "c"), near_value, swap(near_value, "c")

    order = jnp.stack([quarter, quarter ^ 1, quarter ^ 2, quarter ^ 3]).astype(jnp.int32)
    core_order = jnp.stack([core, 1 - core]).astype(jnp.int32)
    down_total = place_rows(order, four(down_sum, down_near))
    output_total = place_rows(core_order, (output_own, swap(output_own, "c")))
    gate_total, up_total, second_gain_grad = place_columns(
        order, gain_two, gate_weight, up_weight, four(gate_sum, gate_near), four(up_sum, up_near), shards
    )
    query_grad, key_grad, value_grad, first_gain_grad = place_heads(
        gain_one, query_weight, key_weight, value_weight, gather(qkv_grad, seq)
    )
    return (
        block_output,
        input_grad,
        first_gain_grad[:, 0],
        query_grad,
        key_grad,
        value_grad,
        output_total,
        second_gain_grad[:, 0],
        gate_total,
        up_total,
        down_total,
    )


def fast_solution(mesh):
    seq_count, shard_count = mesh.devices.shape
    fine = Mesh(
        mesh.devices.reshape(seq_count // 2, 2, shard_count // 2, 2), ("z", "c", "y", "x")
    )
    seq, fsdp = ("z", "c"), ("y", "x")
    matrix = P(fsdp, None)
    return jax.shard_map(
        fast_body,
        mesh=fine,
        in_specs=(
            P(fsdp, seq, None),
            P(fsdp, seq),
            P(fsdp),
            matrix,
            matrix,
            matrix,
            matrix,
            P(fsdp),
            matrix,
            matrix,
            matrix,
            P(fsdp, seq, None),
        ),
        out_specs=(
            P(fsdp, seq, None),
            P(fsdp, seq, None),
            P(fsdp),
            matrix,
            matrix,
            matrix,
            matrix,
            P(fsdp),
            matrix,
            matrix,
            matrix,
        ),
        check_vma=False,
    )


def solution(mesh):
    shape = dict(mesh.shape)
    if shape["seq"] == KVH and shape["fsdp"] == 4:
        return fast_solution(mesh)
    return plain_solution(mesh)


def shifted(value, axis, steps):
    count = lax.axis_size(axis)
    first, last = (max(0, -steps), min(count, count - steps))
    return lax.ppermute(value, axis, [(source, source + steps) for source in range(first, last)])


def rope_tables(position_rows):
    freq = THETA ** (-(jnp.arange(HD // 2, dtype=jnp.float32) * 2.0 / HD))
    angle = position_rows.astype(jnp.float32)[:, None] * freq[None, :]
    cosine = jnp.cos(angle)
    sine = jnp.sin(angle)
    return (jnp.concatenate([cosine, cosine], -1), jnp.concatenate([sine, sine], -1))


def rotate(values, cosine, sine):
    half = HD // 2
    turned = jnp.concatenate([-values[..., half:], values[..., :half]], -1)
    return values * cosine[:, None, :] + turned * sine[:, None, :]


def rotate_back(grads, cosine, sine):
    half = HD // 2
    scaled = grads * sine[:, None, :]
    turned = jnp.concatenate([scaled[..., half:], -scaled[..., :half]], -1)
    return grads * cosine[:, None, :] + turned


def norm_forward(rows, gain):
    scale = lax.rsqrt(jnp.mean(rows * rows, -1, keepdims=True) + EPS)
    unit = rows * scale
    return (unit * gain, unit, scale)


def norm_backward(grad_out, unit, scale, gain):
    grad_unit = grad_out * gain
    gain_grad = jnp.sum(grad_out * unit, 0)
    grad_rows = scale * (grad_unit - unit * jnp.mean(grad_unit * unit, -1, keepdims=True))
    return (grad_rows, gain_grad)


def plain_body(
    tokens,
    positions,
    first_gain,
    query_weight,
    key_weight,
    value_weight,
    output_weight,
    second_gain,
    gate_weight,
    up_weight,
    down_weight,
    cotangent,
):
    seq_count = lax.axis_size("seq")
    local_rows = tokens[0]
    token_count = local_rows.shape[0]
    half_len = token_count * seq_count
    rows_float = local_rows.astype(jnp.float32)
    gain_one, wq_full, wk_full, wv_full, wo_full = (
        lax.all_gather(first_gain, "fsdp", axis=0, tiled=True),
        lax.all_gather(query_weight, "fsdp", axis=0, tiled=True),
        lax.all_gather(key_weight, "fsdp", axis=0, tiled=True),
        lax.all_gather(value_weight, "fsdp", axis=0, tiled=True),
        lax.all_gather(output_weight, "fsdp", axis=0, tiled=True),
    )
    gain_one = gain_one.astype(jnp.float32)
    normed_one, unit_one, scale_one = norm_forward(rows_float, gain_one)
    normed_low = normed_one.astype(jnp.bfloat16)
    cosine, sine = rope_tables(positions[0])
    query_lin = jnp.dot(normed_low, wq_full, preferred_element_type=jnp.float32).reshape(
        token_count, QH, HD
    )
    key_lin = jnp.dot(normed_low, wk_full, preferred_element_type=jnp.float32).reshape(
        token_count, KVH, HD
    )
    value_lin = jnp.dot(normed_low, wv_full, preferred_element_type=jnp.float32).reshape(
        token_count, KVH, HD
    )
    query_rows = rotate(query_lin, cosine, sine).astype(jnp.bfloat16)
    key_rows = rotate(key_lin, cosine, sine).astype(jnp.bfloat16)
    value_rows = value_lin.astype(jnp.bfloat16)
    repeat = max(1, seq_count // KVH)
    if repeat > 1:
        key_rows = jnp.repeat(key_rows, repeat, axis=1)
        value_rows = jnp.repeat(value_rows, repeat, axis=1)
    query_heads, key_heads, value_heads = (
        lax.all_to_all(query_rows, "seq", split_axis=1, concat_axis=0, tiled=True),
        lax.all_to_all(key_rows, "seq", split_axis=1, concat_axis=0, tiled=True),
        lax.all_to_all(value_rows, "seq", split_axis=1, concat_axis=0, tiled=True),
    )
    head_count = query_heads.shape[1]
    pair_count = key_heads.shape[1]
    group = head_count // pair_count
    half_positions = lax.all_gather(positions[0], "seq", axis=0, tiled=True)
    key_prior, value_prior = shifted((key_heads, value_heads), "fsdp", 1)
    key_all = jnp.concatenate([key_prior, key_heads], 0)
    value_all = jnp.concatenate([value_prior, value_heads], 0)
    half_index = lax.axis_index("fsdp") % 2
    key_index = (half_index - 1) * half_len + jnp.arange(2 * half_len, dtype=jnp.int32)
    row_index = half_index * half_len + jnp.arange(half_len, dtype=jnp.int32)
    row_start = row_index - half_positions
    block = min(512, half_len)
    count = half_len // block
    factor = HD ** (-0.5)
    query_blocks = query_heads.reshape(count, block, pair_count, group, HD)
    index_blocks = row_index.reshape(count, block)
    start_blocks = row_start.reshape(count, block)

    def block_scores(query_block, index_block, start_block):
        scores = (
            jnp.einsum("bkgd,tkd->kgbt", query_block, key_all, preferred_element_type=jnp.float32)
            * factor
        )
        visible = (key_index[None, :] >= start_block[:, None]) & (
            key_index[None, :] <= index_block[:, None]
        )
        return jnp.where(visible, scores, -1e30)

    def forward_block(items):
        query_block, index_block, start_block = items
        scores = block_scores(query_block, index_block, start_block)
        top = jnp.max(scores, -1, keepdims=True)
        expo = jnp.exp(scores - top)
        total = jnp.sum(expo, -1, keepdims=True)
        probs_low = (expo / total).astype(jnp.bfloat16)
        mixed = jnp.einsum(
            "kgbt,tkd->bkgd", probs_low, value_all, preferred_element_type=jnp.float32
        )
        return (mixed.reshape(block, head_count, HD).astype(jnp.bfloat16), top + jnp.log(total))

    head_blocks, log_totals = lax.map(forward_block, (query_blocks, index_blocks, start_blocks))
    head_out = head_blocks.reshape(half_len, head_count, HD)
    token_heads = lax.all_to_all(head_out, "seq", split_axis=0, concat_axis=1, tiled=True)
    heads_flat = token_heads.reshape(token_count, QH * HD)
    middle = rows_float + jnp.dot(heads_flat, wo_full, preferred_element_type=jnp.float32)
    gain_two, wg_full, wu_full, wd_full = (
        lax.all_gather(second_gain, "fsdp", axis=0, tiled=True),
        lax.all_gather(gate_weight, "fsdp", axis=0, tiled=True),
        lax.all_gather(up_weight, "fsdp", axis=0, tiled=True),
        lax.all_gather(down_weight, "fsdp", axis=0, tiled=True),
    )
    gain_two = gain_two.astype(jnp.float32)
    normed_two, unit_two, scale_two = norm_forward(middle, gain_two)
    normed_two_low = normed_two.astype(jnp.bfloat16)
    gate = jnp.dot(normed_two_low, wg_full, preferred_element_type=jnp.float32)
    upper = jnp.dot(normed_two_low, wu_full, preferred_element_type=jnp.float32)
    hidden = (jax.nn.silu(gate) * upper).astype(jnp.bfloat16)
    result = middle + jnp.dot(hidden, wd_full, preferred_element_type=jnp.float32)
    block_output = result.astype(jnp.bfloat16)[None]
    grad_low = cotangent[0]
    grad_rows = grad_low.astype(jnp.float32)
    down_grad = jnp.einsum("tf,td->fd", hidden, grad_low, preferred_element_type=jnp.float32)
    grad_hidden = jnp.einsum("td,fd->tf", grad_low, wd_full, preferred_element_type=jnp.float32)
    sigma = jax.nn.sigmoid(gate)
    gate_low = (grad_hidden * upper * sigma * (1.0 + gate * (1.0 - sigma))).astype(jnp.bfloat16)
    upper_low = (grad_hidden * gate * sigma).astype(jnp.bfloat16)
    gate_grad = jnp.einsum(
        "td,tf->df", normed_two_low, gate_low, preferred_element_type=jnp.float32
    )
    up_grad = jnp.einsum("td,tf->df", normed_two_low, upper_low, preferred_element_type=jnp.float32)
    grad_normed_two = jnp.einsum(
        "tf,df->td", gate_low, wg_full, preferred_element_type=jnp.float32
    ) + jnp.einsum("tf,df->td", upper_low, wu_full, preferred_element_type=jnp.float32)
    grad_middle_norm, second_gain_grad = norm_backward(
        grad_normed_two, unit_two, scale_two, gain_two
    )
    grad_middle = grad_rows + grad_middle_norm
    grad_branch = grad_middle.astype(jnp.bfloat16)
    output_grad = jnp.einsum(
        "tc,td->cd", heads_flat, grad_branch, preferred_element_type=jnp.float32
    )
    grad_heads = (
        jnp.einsum("td,cd->tc", grad_branch, wo_full, preferred_element_type=jnp.float32)
        .astype(jnp.bfloat16)
        .reshape(token_count, QH, HD)
    )
    grad_head_rows = lax.all_to_all(grad_heads, "seq", split_axis=1, concat_axis=0, tiled=True)
    grad_blocks = grad_head_rows.reshape(count, block, pair_count, group, HD)

    def backward_block(carry, items):
        key_acc, value_acc = carry
        query_block, index_block, start_block, grad_block, log_block = items
        scores = block_scores(query_block, index_block, start_block)
        probs = jnp.exp(scores - log_block)
        probs_low = probs.astype(jnp.bfloat16)
        grad_probs = jnp.einsum(
            "bkgd,tkd->kgbt", grad_block, value_all, preferred_element_type=jnp.float32
        )
        grad_scores = (
            probs * (grad_probs - jnp.sum(probs * grad_probs, -1, keepdims=True))
        ).astype(jnp.bfloat16)
        query_grad_block = (
            jnp.einsum("kgbt,tkd->bkgd", grad_scores, key_all, preferred_element_type=jnp.float32)
            * factor
        )
        key_acc = (
            key_acc
            + jnp.einsum(
                "kgbt,bkgd->tkd", grad_scores, query_block, preferred_element_type=jnp.float32
            )
            * factor
        )
        value_acc = value_acc + jnp.einsum(
            "kgbt,bkgd->tkd", probs_low, grad_block, preferred_element_type=jnp.float32
        )
        return ((key_acc, value_acc), query_grad_block.reshape(block, head_count, HD))

    empty = jnp.zeros((2 * half_len, pair_count, HD), jnp.float32)
    (key_acc, value_acc), query_grad_blocks = lax.scan(
        backward_block,
        (empty, empty),
        (query_blocks, index_blocks, start_blocks, grad_blocks, log_totals),
    )
    key_back, value_back = (
        shifted(key_acc[:half_len].astype(jnp.bfloat16), "fsdp", -1).astype(jnp.float32),
        shifted(value_acc[:half_len].astype(jnp.bfloat16), "fsdp", -1).astype(jnp.float32),
    )
    key_local = key_acc[half_len:] + key_back
    value_local = value_acc[half_len:] + value_back
    query_grad_heads = query_grad_blocks.reshape(half_len, head_count, HD)
    grad_query_tok, grad_key_tok, grad_value_tok = (
        lax.all_to_all(
            query_grad_heads.astype(jnp.bfloat16), "seq", split_axis=0, concat_axis=1, tiled=True
        ).astype(query_grad_heads.dtype),
        lax.all_to_all(
            key_local.astype(jnp.bfloat16), "seq", split_axis=0, concat_axis=1, tiled=True
        ).astype(key_local.dtype),
        lax.all_to_all(
            value_local.astype(jnp.bfloat16), "seq", split_axis=0, concat_axis=1, tiled=True
        ).astype(value_local.dtype),
    )
    if repeat > 1:
        grad_key_tok = grad_key_tok.reshape(token_count, KVH, repeat, HD).sum(2)
        grad_value_tok = grad_value_tok.reshape(token_count, KVH, repeat, HD).sum(2)
    query_lin_grad = (
        rotate_back(grad_query_tok, cosine, sine).astype(jnp.bfloat16).reshape(token_count, QH * HD)
    )
    key_lin_grad = (
        rotate_back(grad_key_tok, cosine, sine).astype(jnp.bfloat16).reshape(token_count, KVH * HD)
    )
    value_lin_grad = grad_value_tok.astype(jnp.bfloat16).reshape(token_count, KVH * HD)
    query_grad = jnp.einsum(
        "td,tc->dc", normed_low, query_lin_grad, preferred_element_type=jnp.float32
    )
    key_grad = jnp.einsum("td,tc->dc", normed_low, key_lin_grad, preferred_element_type=jnp.float32)
    value_grad = jnp.einsum(
        "td,tc->dc", normed_low, value_lin_grad, preferred_element_type=jnp.float32
    )
    grad_normed_one = jnp.einsum(
        "tc,dc->td", query_lin_grad, wq_full, preferred_element_type=jnp.float32
    )
    grad_normed_one = grad_normed_one + jnp.einsum(
        "tc,dc->td", key_lin_grad, wk_full, preferred_element_type=jnp.float32
    )
    grad_normed_one = grad_normed_one + jnp.einsum(
        "tc,dc->td", value_lin_grad, wv_full, preferred_element_type=jnp.float32
    )
    grad_rows_one, first_gain_grad = norm_backward(grad_normed_one, unit_one, scale_one, gain_one)
    input_grad = (grad_middle + grad_rows_one).astype(jnp.bfloat16)[None]
    pieces = (
        lax.psum_scatter(
            first_gain_grad.astype(jnp.bfloat16), "fsdp", scatter_dimension=0, tiled=True
        ).astype(jnp.float32),
        lax.psum_scatter(
            query_grad.astype(jnp.bfloat16), "fsdp", scatter_dimension=0, tiled=True
        ).astype(jnp.float32),
        lax.psum_scatter(
            key_grad.astype(jnp.bfloat16), "fsdp", scatter_dimension=0, tiled=True
        ).astype(jnp.float32),
        lax.psum_scatter(
            value_grad.astype(jnp.bfloat16), "fsdp", scatter_dimension=0, tiled=True
        ).astype(jnp.float32),
        lax.psum_scatter(
            output_grad.astype(jnp.bfloat16), "fsdp", scatter_dimension=0, tiled=True
        ).astype(jnp.float32),
        lax.psum_scatter(
            second_gain_grad.astype(jnp.bfloat16), "fsdp", scatter_dimension=0, tiled=True
        ).astype(jnp.float32),
        lax.psum_scatter(
            gate_grad.astype(jnp.bfloat16), "fsdp", scatter_dimension=0, tiled=True
        ).astype(jnp.float32),
        lax.psum_scatter(
            up_grad.astype(jnp.bfloat16), "fsdp", scatter_dimension=0, tiled=True
        ).astype(jnp.float32),
        lax.psum_scatter(
            down_grad.astype(jnp.bfloat16), "fsdp", scatter_dimension=0, tiled=True
        ).astype(jnp.float32),
    )
    shares = (
        lax.psum(pieces[0].astype(jnp.bfloat16), "seq").astype(jnp.float32),
        lax.psum(pieces[1].astype(jnp.bfloat16), "seq").astype(jnp.float32),
        lax.psum(pieces[2].astype(jnp.bfloat16), "seq").astype(jnp.float32),
        lax.psum(pieces[3].astype(jnp.bfloat16), "seq").astype(jnp.float32),
        lax.psum(pieces[4].astype(jnp.bfloat16), "seq").astype(jnp.float32),
        lax.psum(pieces[5].astype(jnp.bfloat16), "seq").astype(jnp.float32),
        lax.psum(pieces[6].astype(jnp.bfloat16), "seq").astype(jnp.float32),
        lax.psum(pieces[7].astype(jnp.bfloat16), "seq").astype(jnp.float32),
        lax.psum(pieces[8].astype(jnp.bfloat16), "seq").astype(jnp.float32),
    )
    return (
        block_output,
        input_grad,
        shares[0],
        shares[1],
        shares[2],
        shares[3],
        shares[4],
        shares[5],
        shares[6],
        shares[7],
        shares[8],
    )


def plain_solution(mesh):
    placed = (
        P("fsdp", "seq", None),
        P("fsdp", "seq"),
        P("fsdp"),
        P("fsdp", None),
        P("fsdp", None),
        P("fsdp", None),
        P("fsdp", None),
        P("fsdp"),
        P("fsdp", None),
        P("fsdp", None),
        P("fsdp", None),
        P("fsdp", "seq", None),
    )
    return jax.shard_map(
        plain_body,
        mesh=mesh,
        in_specs=placed,
        out_specs=(
            P("fsdp", "seq", None),
            P("fsdp", "seq", None),
            P("fsdp"),
            P("fsdp", None),
            P("fsdp", None),
            P("fsdp", None),
            P("fsdp", None),
            P("fsdp"),
            P("fsdp", None),
            P("fsdp", None),
            P("fsdp", None),
        ),
        check_vma=False,
    )
```

```python
import functools
import math

import jax
import jax.numpy as jnp
from jax import lax
from jax.experimental import pallas as pl
from jax.experimental.pallas import tpu as pltpu
from jax.sharding import Mesh
from jax.sharding import PartitionSpec as P

QH = 16
KVH = 8
HD = 96


THETA = 100000.0
EPS = 1e-05
LOW = jnp.bfloat16
F32 = jnp.float32
NEG = -1e30
LN2 = math.log(2.0)


def contract(left, right, left_axis, right_axis):
    return lax.dot_general(
        left, right, (((left_axis,), (right_axis,)), ((), ())), preferred_element_type=F32
    )


def visible(first, second, query_block, key_block, size):
    key = key_block * size + lax.broadcasted_iota(jnp.int32, (size, size), 0)
    query = query_block * size + lax.broadcasted_iota(jnp.int32, (1, size), 1)
    start = jnp.where(query >= second, second, jnp.where(query >= first, first, 0))
    return (key >= start) & (key <= query)


def slot_of(block, count):
    return (block % (count // 2)) * 2 + block // (count // 2)


def forward_kernel(
    scalars,
    own_ref,
    other_ref,
    low_ref,
    full_ref,
    log_ref,
    query_s,
    key_s,
    value_s,
    top_s,
    total_s,
    mixed_s,
    *,
    size,
    count,
):
    half = scalars[0]
    first = scalars[1]
    second = scalars[2]
    here = pl.program_id(0)
    per_half = count // 2

    @pl.when(here == 0)
    def _():
        for ref, side in ((own_ref, half), (other_ref, 1 - half)):
            for step in range(per_half):
                block = side * per_half + step
                columns = slice(step * size, (step + 1) * size)
                query_s[block] = ref[0:HD, columns]
                key_s[block] = ref[HD : 2 * HD, columns].T
                value_s[block] = ref[2 * HD : 3 * HD, columns]

    query = query_s[here]
    top_s[...] = jnp.full_like(top_s, NEG)
    total_s[...] = jnp.zeros_like(total_s)
    mixed_s[...] = jnp.zeros_like(mixed_s)

    def add_block(block, masked):
        scores = contract(key_s[block], query, 1, 0)
        if masked:
            scores = jnp.where(visible(first, second, here, block, size), scores, NEG)
        old_top = top_s[...]
        top = jnp.maximum(old_top, jnp.max(scores, 0, keepdims=True))
        expo = jnp.exp2(scores - top)
        scale = jnp.exp2(old_top - top)
        top_s[...] = top
        total_s[...] = total_s[...] * scale + jnp.sum(expo, 0, keepdims=True)
        mixed_s[...] = mixed_s[...] * scale + contract(value_s[block], expo.astype(LOW), 1, 0)

    last = count - 1

    @pl.loop(1, jnp.where(here == last, 1, here))
    def _(block):
        add_block(block, False)

    @pl.loop(0, jnp.where(here == last, count, jnp.minimum(here + 1, 2)))
    def _(step):
        add_block(jnp.where(here == last, step, step * here), True)

    total = total_s[...]
    result = mixed_s[...] / total
    full_ref[0] = result
    low_ref[0] = result.astype(LOW)
    log_ref[0] = top_s[...] + jnp.log2(total)


def backward_kernel(
    scalars,
    own_ref,
    other_ref,
    grad_ref,
    full_ref,
    log_ref,
    kept_ref,
    leaving_ref,
    query_s,
    key_s,
    value_s,
    delta_s,
    query_grad_s,
    key_grad_s,
    value_grad_s,
    *,
    size,
    count,
):
    half = scalars[0]
    first = scalars[1]
    second = scalars[2]
    here = pl.program_id(0)
    per_half = count // 2

    @pl.when(here == 0)
    def _():
        for ref, side in ((own_ref, half), (other_ref, 1 - half)):
            for step in range(per_half):
                block = side * per_half + step
                columns = slice(step * size, (step + 1) * size)
                query_s[block] = ref[0:HD, columns]
                key_s[block] = ref[HD : 2 * HD, columns]
                value_s[block] = ref[2 * HD : 3 * HD, columns].T
        for block in range(count):
            delta_s[block] = jnp.sum(
                grad_ref[slot_of(block, count)].astype(F32) * full_ref[block], 0, keepdims=True
            )
        query_grad_s[...] = jnp.zeros_like(query_grad_s)

    key_grad_s[...] = jnp.zeros_like(key_grad_s)
    value_grad_s[...] = jnp.zeros_like(value_grad_s)
    key = key_s[here]
    key_rows = key.T
    value_rows = value_s[here]

    def add_block(block, masked):
        query = query_s[block]
        grad = grad_ref[slot_of(block, count)]
        scores = contract(key_rows, query, 1, 0)
        if masked:
            scores = jnp.where(visible(first, second, block, here, size), scores, NEG)
        probs = jnp.exp2(scores - log_ref[block])
        grad_probs = contract(value_rows, grad, 1, 0)
        grad_scores = (probs * (grad_probs - delta_s[block])).astype(LOW)
        value_grad_s[...] += contract(grad, probs.astype(LOW), 1, 1)
        key_grad_s[...] += contract(query, grad_scores, 1, 1)
        query_grad_s[block] += contract(key, grad_scores, 1, 0)

    last = count - 1

    @pl.loop(here + 1, jnp.where(here == 0, 1, last))
    def _(block):
        add_block(block, False)

    @pl.loop(0, jnp.where(here == 0, count, jnp.where(here == last, 1, 2)))
    def _(step):
        add_block(jnp.where(here == 0, step, jnp.where(step == 0, here, last)), True)

    side = here // per_half
    columns = pl.ds(pl.multiple_of((here % per_half) * size, size), size)

    def write(out_ref):
        out_ref[0:HD, columns] = (query_grad_s[here] * HD**-0.5).astype(LOW)
        out_ref[HD : 2 * HD, columns] = (key_grad_s[...] * LN2).astype(LOW)
        out_ref[2 * HD : 3 * HD, columns] = value_grad_s[...].astype(LOW)

    @pl.when(side == half)
    def _():
        write(kept_ref)

    @pl.when(side != half)
    def _():
        write(leaving_ref)


def attend_forward(scalars, own, other, size):
    count = 2 * own.shape[1] // size
    whole = lambda shape: pl.BlockSpec(shape, lambda i, s: (0,) * len(shape))
    pairs = count * (count + 1) // 2
    return pl.pallas_call(
        functools.partial(forward_kernel, size=size, count=count),
        grid_spec=pltpu.PrefetchScalarGridSpec(
            num_scalar_prefetch=1,
            grid=(count,),
            in_specs=[whole(own.shape), whole(other.shape)],
            out_specs=[
                pl.BlockSpec(
                    (1, HD, size), lambda i, s: (slot_of(i, count), 0, 0)
                ),
                pl.BlockSpec((1, HD, size), lambda i, s: (i, 0, 0)),
                pl.BlockSpec((1, 1, size), lambda i, s: (i, 0, 0)),
            ],
            scratch_shapes=[
                pltpu.VMEM((count, HD, size), LOW),
                pltpu.VMEM((count, size, HD), LOW),
                pltpu.VMEM((count, HD, size), LOW),
                pltpu.VMEM((1, size), F32),
                pltpu.VMEM((1, size), F32),
                pltpu.VMEM((HD, size), F32),
            ],
        ),
        out_shape=[
            jax.ShapeDtypeStruct((count, HD, size), LOW),
            jax.ShapeDtypeStruct((count, HD, size), F32),
            jax.ShapeDtypeStruct((count, 1, size), F32),
        ],
        compiler_params=pltpu.CompilerParams(
            dimension_semantics=("arbitrary",), vmem_limit_bytes=32 * 2**20
        ),
        cost_estimate=pl.CostEstimate(
            flops=pairs * size * size * HD * 32,
            bytes_accessed=10 * 2**20,
            transcendentals=pairs * size * size,
        ),
        name="attend_forward",
    )(scalars, own, other)


def attend_backward(scalars, own, other, grad, full, log_total):
    count, _, size = grad.shape
    whole = lambda shape: pl.BlockSpec(shape, lambda i, s: (0,) * len(shape))
    pairs = count * (count + 1) // 2
    out_shape = own.shape
    return pl.pallas_call(
        functools.partial(backward_kernel, size=size, count=count),
        grid_spec=pltpu.PrefetchScalarGridSpec(
            num_scalar_prefetch=1,
            grid=(count,),
            in_specs=[
                whole(own.shape),
                whole(other.shape),
                whole(grad.shape),
                whole(full.shape),
                whole(log_total.shape),
            ],
            out_specs=[whole(out_shape)] * 2,
            scratch_shapes=[
                pltpu.VMEM((count, HD, size), LOW),
                pltpu.VMEM((count, HD, size), LOW),
                pltpu.VMEM((count, size, HD), LOW),
                pltpu.VMEM((count, 1, size), F32),
                pltpu.VMEM((count, HD, size), F32),
                pltpu.VMEM((HD, size), F32),
                pltpu.VMEM((HD, size), F32),
            ],
        ),
        out_shape=[jax.ShapeDtypeStruct(out_shape, LOW)] * 2,
        compiler_params=pltpu.CompilerParams(
            dimension_semantics=("arbitrary",), vmem_limit_bytes=32 * 2**20
        ),
        cost_estimate=pl.CostEstimate(
            flops=pairs * size * size * HD * 42,
            bytes_accessed=16 * 2**20,
            transcendentals=pairs * size * size,
        ),
        name="attend_backward",
    )(scalars, own, other, grad, full, log_total)


def place_rows_kernel(order, *refs):
    pieces, out_ref = refs[:-1], refs[-1]
    size = pieces[0].shape[0]
    for index, piece in enumerate(pieces):
        start = pl.multiple_of(order[index] * size, size)
        out_ref[pl.ds(start, size), :] = piece[...].astype(F32)


def place_rows(order, pieces):
    size, width = pieces[0].shape
    total = size * len(pieces)
    step = 512
    return pl.pallas_call(
        place_rows_kernel,
        grid_spec=pltpu.PrefetchScalarGridSpec(
            num_scalar_prefetch=1,
            grid=(width // step,),
            in_specs=[pl.BlockSpec((size, step), lambda i, s: (0, i)) for _ in pieces],
            out_specs=pl.BlockSpec((total, step), lambda i, s: (0, i)),
        ),
        out_shape=jax.ShapeDtypeStruct((total, width), F32),
        compiler_params=pltpu.CompilerParams(vmem_limit_bytes=24 * 2**20),
        cost_estimate=pl.CostEstimate(
            flops=0, bytes_accessed=total * width * 6, transcendentals=0
        ),
        name="place_rows",
    )(order, *pieces)


def place_columns_kernel(order, gain_ref, gate_w_ref, up_w_ref, *refs):
    count = (len(refs) - 3) // 2
    gates, ups = refs[:count], refs[count : 2 * count]
    gate_ref, up_ref, sum_ref = refs[2 * count :]
    size = gates[0].shape[1]
    gain = gain_ref[...]
    total = jnp.zeros((gate_ref.shape[0], size), F32)
    for index in range(count):
        columns = pl.ds(pl.multiple_of(order[index] * size, size), size)
        gate, up = gates[index][...].astype(F32), ups[index][...].astype(F32)
        total += gate * gate_w_ref[:, columns].astype(F32)
        total += up * up_w_ref[:, columns].astype(F32)
        gate_ref[:, columns] = gate * gain
        up_ref[:, columns] = up * gain

    @pl.when(pl.program_id(0) == 0)
    def _():
        sum_ref[...] = jnp.zeros_like(sum_ref)

    sum_ref[...] += jnp.sum(total, 1, keepdims=True)


def place_columns(order, gain, gate_weight, up_weight, gates, ups, shards):
    rows, width = gate_weight.shape
    span = width // shards
    size = span // len(gates)
    wide = pl.BlockSpec((rows, span), lambda i, s: (0, i))
    thin = pl.BlockSpec((rows, 1), lambda i, s: (0, 0))
    pieces = [pl.BlockSpec((rows, size), lambda i, s: (0, i)) for _ in (*gates, *ups)]
    return pl.pallas_call(
        place_columns_kernel,
        grid_spec=pltpu.PrefetchScalarGridSpec(
            num_scalar_prefetch=1,
            grid=(shards,),
            in_specs=[thin, wide, wide, *pieces],
            out_specs=[wide, wide, thin],
        ),
        out_shape=[
            jax.ShapeDtypeStruct((rows, width), F32),
            jax.ShapeDtypeStruct((rows, width), F32),
            jax.ShapeDtypeStruct((rows, 1), F32),
        ],
        compiler_params=pltpu.CompilerParams(
            dimension_semantics=("arbitrary",), vmem_limit_bytes=24 * 2**20
        ),
        cost_estimate=pl.CostEstimate(
            flops=rows * width * 6, bytes_accessed=rows * width * 16, transcendentals=0
        ),
        name="place_columns",
    )(order, gain, gate_weight, up_weight, *gates, *ups)


def place_heads_kernel(gain_ref, query_w, key_w, value_w, all_ref, query_ref, key_ref, value_ref, sum_ref):
    rows = gain_ref.shape[0]
    wide = query_ref.shape[1] // KVH
    gain = gain_ref[...]
    total = jnp.zeros((rows, 4 * HD), F32)
    pieces = [all_ref[i * rows : (i + 1) * rows, :].astype(F32) for i in range(KVH)]
    for start in range(0, KVH, 2):
        value = jnp.concatenate([piece[:, :wide] for piece in pieces[start : start + 2]], 1)
        columns = slice(start * wide, (start + 2) * wide)
        total += value * query_w[:, columns].astype(F32)
        query_ref[:, columns] = value * gain
    for first, weight, out_ref in ((wide, key_w, key_ref), (wide + HD, value_w, value_ref)):
        for start in range(0, KVH, 4):
            value = jnp.concatenate(
                [piece[:, first : first + HD] for piece in pieces[start : start + 4]], 1
            )
            columns = slice(start * HD, (start + 4) * HD)
            total += value * weight[:, columns].astype(F32)
            out_ref[:, columns] = value * gain
    sum_ref[...] = jnp.sum(total, 1, keepdims=True)


def place_heads(gain, query_weight, key_weight, value_weight, pieces):
    weights = (query_weight, key_weight, value_weight)
    rows = gain.shape[0]
    return pl.pallas_call(
        place_heads_kernel,
        out_shape=[jax.ShapeDtypeStruct(weight.shape, F32) for weight in weights]
        + [jax.ShapeDtypeStruct((rows, 1), F32)],
        compiler_params=pltpu.CompilerParams(vmem_limit_bytes=32 * 2**20),
        cost_estimate=pl.CostEstimate(
            flops=rows * 3072 * 4, bytes_accessed=rows * 3072 * 8, transcendentals=0
        ),
        name="place_heads",
    )(gain, *weights, pieces)


def merge_kernel(scalars, kept_ref, came_ref, cosine_ref, sine_ref, out_ref, split_ref):
    lead = scalars[0] == 0
    lines, _, size = split_ref.shape
    for line in range(lines):
        columns = slice(line * size, (line + 1) * size)
        kept = kept_ref[:, columns].astype(F32)
        came = came_ref[:, columns].astype(F32)
        cosine, sine = cosine_ref[:, columns], sine_ref[:, columns]
        joint = kept[HD:] + came[HD:]
        first = jnp.where(lead, kept[:HD], came[:HD])
        second = jnp.where(lead, came[:HD], kept[:HD])
        turned = []
        for value in (first, second, joint[:HD]):
            low, high = value[: HD // 2], value[HD // 2 :]
            turned.append(low * cosine + high * sine)
            turned.append(high * cosine - low * sine)
        turned.append(joint[HD:])
        result = jnp.concatenate([part.astype(LOW) for part in turned], 0)
        out_ref[:, columns] = result
        split_ref[line] = result


def merge(scalars, kept, came, cosine, sine, lines):
    tokens = kept.shape[1]
    whole = lambda value: pl.BlockSpec(value.shape, lambda i, s: (0,) * len(value.shape))
    outs = [
        jax.ShapeDtypeStruct((4 * HD, tokens), LOW),
        jax.ShapeDtypeStruct((lines, 4 * HD, tokens // lines), LOW),
    ]
    return pl.pallas_call(
        merge_kernel,
        grid_spec=pltpu.PrefetchScalarGridSpec(
            num_scalar_prefetch=1,
            grid=(1,),
            in_specs=[whole(value) for value in (kept, came, cosine, sine)],
            out_specs=[whole(value) for value in outs],
        ),
        out_shape=outs,
        compiler_params=pltpu.CompilerParams(vmem_limit_bytes=24 * 2**20),
        cost_estimate=pl.CostEstimate(
            flops=tokens * HD * 24, bytes_accessed=tokens * HD * 30, transcendentals=0
        ),
        name="merge",
    )(scalars, kept, came, cosine, sine)


def pack_kernel(scalars, gain_ref, query_ref, key_ref, value_ref, *outs):
    core = scalars[3]
    gain = gain_ref[...]
    wide = query_ref.shape[1] // KVH
    span = wide + 2 * HD
    for which in range(2):

        @pl.when(core == which)
        def _():
            for line in range(KVH // 2):
                head = 2 * line + which
                value = jnp.concatenate(
                    [
                        query_ref[:, head * wide : (head + 1) * wide].astype(F32),
                        key_ref[:, head * HD : (head + 1) * HD].astype(F32),
                        value_ref[:, head * HD : (head + 1) * HD].astype(F32),
                    ],
                    1,
                )
                place = (line % 2) * span
                outs[line // 2][:, place : place + span] = (value * gain).astype(LOW)


def pack(scalars, gain, query_weight, key_weight, value_weight):
    rows, width = query_weight.shape
    whole = lambda value: pl.BlockSpec(value.shape, lambda i, s: (0, 0))
    weights = (gain, query_weight, key_weight, value_weight)
    outs = [jax.ShapeDtypeStruct((rows, width // 2), LOW)] * 2
    return pl.pallas_call(
        pack_kernel,
        grid_spec=pltpu.PrefetchScalarGridSpec(
            num_scalar_prefetch=1,
            grid=(1,),
            in_specs=[whole(value) for value in weights],
            out_specs=[whole(value) for value in outs],
        ),
        out_shape=outs,
        compiler_params=pltpu.CompilerParams(vmem_limit_bytes=24 * 2**20),
        cost_estimate=pl.CostEstimate(
            flops=rows * width, bytes_accessed=rows * width * 6, transcendentals=0
        ),
        name="pack",
    )(scalars, *weights)


def spread_kernel(scalars, lin_ref, cosine_ref, sine_ref, own_ref, leaving_ref):
    cosine, sine = cosine_ref[...], sine_ref[...]

    def turn(start, factor):
        low = lin_ref[start : start + HD // 2, :]
        high = lin_ref[start + HD // 2 : start + HD, :]
        turned = ((low * cosine - high * sine) * factor, (high * cosine + low * sine) * factor)
        return jnp.concatenate([part.astype(LOW) for part in turned], 0)

    lead = scalars[0] == 0
    first, second = turn(0, HD**-0.5 / LN2), turn(HD, HD**-0.5 / LN2)

    @pl.when(lead)
    def _():
        own_ref[0:HD] = first
        leaving_ref[0:HD] = second

    @pl.when(jnp.logical_not(lead))
    def _():
        own_ref[0:HD] = second
        leaving_ref[0:HD] = first

    key = turn(2 * HD, 1.0)
    value = lin_ref[3 * HD : 4 * HD].astype(LOW)
    for ref in (own_ref, leaving_ref):
        ref[HD : 2 * HD] = key
        ref[2 * HD : 3 * HD] = value


def spread(scalars, lin, cosine, sine):
    tokens = lin.shape[1]
    step = 512
    column = lambda rows: pl.BlockSpec((rows, step), lambda i, s: (0, i))
    return pl.pallas_call(
        spread_kernel,
        grid_spec=pltpu.PrefetchScalarGridSpec(
            num_scalar_prefetch=1,
            grid=(tokens // step,),
            in_specs=[column(4 * HD), column(HD // 2), column(HD // 2)],
            out_specs=[column(3 * HD)] * 2,
        ),
        out_shape=[jax.ShapeDtypeStruct((3 * HD, tokens), LOW)] * 2,
        compiler_params=pltpu.CompilerParams(vmem_limit_bytes=24 * 2**20),
        cost_estimate=pl.CostEstimate(
            flops=tokens * HD * 24, bytes_accessed=tokens * HD * 36, transcendentals=0
        ),
        name="spread",
    )(scalars, lin, cosine, sine)


def swap(value, axis):
    return lax.ppermute(value, axis, [(0, 1), (1, 0)])


def swap_near(value):
    return lax.ppermute(value, "z", [(0, 1), (1, 0), (2, 3), (3, 2)])


def swap_far(value):
    return lax.ppermute(value, "z", [(0, 2), (2, 0), (1, 3), (3, 1)])


def tie(*values):
    return lax.optimization_barrier(values)


def in_order(place, own, other):
    return (jnp.where(place == 0, own, other), jnp.where(place == 0, other, own))


def both(place, own, other):
    return jnp.concatenate(in_order(place, own, other), 0)


def spread_out(value, first, second):
    other = swap(value, first)
    pair = jnp.stack(in_order(lax.axis_index(first), value, other))
    return pair, swap(pair, second)


def placed(pair, other, second):
    pairs = in_order(lax.axis_index(second), pair, other)
    grid = jnp.stack(pairs, 0 if second == "y" else 1)
    return grid.reshape(-1, *grid.shape[3:])


def pick(array, axis, at):
    return lax.dynamic_index_in_dim(array, at, axis, keepdims=False)


def halve(value, axis, along=0):
    at = lax.axis_index(axis)
    return pick(value, along, at), swap(pick(value, along, 1 - at), axis)


def halve_x(value):
    return halve(value.reshape(2, 2, -1, value.shape[-1]), "x", 1)


def halve_y(value):
    return halve(value.reshape(2, 2, -1, value.shape[-1]), "y", 0)


def fast_body(
    tokens,
    positions,
    first_gain,
    query_weight,
    key_weight,
    value_weight,
    output_weight,
    second_gain,
    gate_weight,
    up_weight,
    down_weight,
    cotangent,
):
    seq = ("z", "c")
    fsdp = ("y", "x")
    z, core, half = lax.axis_index("z"), lax.axis_index("c"), lax.axis_index("x")
    near = z % 2
    lines = lax.axis_size("z")
    seq_count = 2 * lines
    shards = lax.axis_size("y") * 2
    spot = z * 2 + core
    quarter = near * 2 + core
    rows = tokens[0]
    count, width = rows.shape
    chip_count = 2 * count
    half_len = count * seq_count
    seq_len = 2 * half_len

    begins = jnp.where(
        (spot == 0) & (half == 0),
        count - 1 - positions[0, count - 1],
        half * half_len + spot * count - positions[0, 0],
    )
    ends = begins + (seq_len - count)
    scalars = jnp.stack([half, begins, ends, core]).astype(jnp.int32)

    gain_one = first_gain.astype(F32)[:, None]
    gain_two = second_gain.astype(F32)[:, None]

    def row_scale(value):
        return lax.rsqrt(jnp.mean(value * value, -1, keepdims=True) + EPS)

    take = functools.partial(lax.dynamic_slice_in_dim, axis=1)
    take_rows = functools.partial(lax.dynamic_slice_in_dim, axis=0)
    gather = lambda value, axes: lax.all_gather(value, axes, axis=0, tiled=True)
    own_rows = rows.astype(F32)
    own_unit_scale = row_scale(own_rows)
    own_unit = own_rows * own_unit_scale
    units = gather(own_unit.astype(LOW), seq)
    wide = QH // KVH * HD
    qkv_shard = (
        jnp.concatenate(
            [
                take(query_weight, spot * wide, wide),
                take(key_weight, spot * HD, HD),
                take(value_weight, spot * HD, HD),
            ],
            1,
        ).astype(F32)
        * gain_one
    ).astype(LOW)
    out_rows = output_weight.shape[0] // 2
    out_shard = take_rows(output_weight, core * out_rows, out_rows)
    piece = down_weight.shape[0] // 4
    down_shard = take_rows(down_weight, quarter * piece, piece)
    gate_shard, up_shard = (
        (
            jnp.concatenate(
                [
                    take(weight, shard * 4 * piece + quarter * piece, piece)
                    for shard in range(shards)
                ],
                1,
            ).astype(F32)
            * gain_two
        ).astype(LOW)
        for weight in (gate_weight, up_weight)
    )
    side = lax.axis_index("y")
    qkv_pair = jnp.stack(in_order(half, qkv_shard, swap(qkv_shard, "x")))
    gate_pair = jnp.stack(in_order(half, gate_shard, swap(gate_shard, "x")))
    up_pair = jnp.stack(in_order(side, up_shard, swap(up_shard, "y")))
    qkv_pair, gate_pair, up_pair = tie(qkv_pair, gate_pair, up_pair)
    qkv_w = placed(qkv_pair, swap(qkv_pair, "y"), "y")
    gate_pair, up_pair = (gate_pair, swap(gate_pair, "y")), (up_pair, swap(up_pair, "x"))

    place = half * half_len + jnp.arange(half_len, dtype=jnp.int32)
    start = jnp.where(place >= ends, ends, jnp.where(place >= begins, begins, 0))
    freq = THETA ** (-(jnp.arange(HD // 2, dtype=F32) * 2.0 / HD))
    angle = freq[:, None] * (place - start).astype(F32)[None, :]
    cosine, sine = jnp.cos(angle), jnp.sin(angle)
    chip_rows = both(core, rows, swap(rows, "c"))
    units, own_cot, chip_rows = tie(units, cotangent[0], chip_rows)
    own, leaving = spread(scalars, contract(qkv_w, units, 0, 1), cosine, sine)
    leaving, down_shard, gate_pair, up_pair = tie(leaving, down_shard, gate_pair, up_pair)

    near_cot = swap_near(own_cot)
    down_pair = jnp.stack(in_order(side, down_shard, swap(down_shard, "y")))
    other, out_shard, down_pair, near_cot, chip_cot, gate_pair, up_pair = tie(
        swap(leaving, "x"),
        out_shard,
        down_pair,
        near_cot,
        both(core, own_cot, swap(own_cot, "c")),
        gate_pair,
        up_pair,
    )
    out_w = gather(out_shard, fsdp)
    down_other = swap(down_pair, "x")
    near_other = swap(near_cot, "c")
    head_low, head_full, log_total = attend_forward(scalars, own, other, chip_count)
    exchange = lambda value: lax.all_to_all(
        value, ("z", "x"), split_axis=0, concat_axis=0, tiled=True
    )
    head_low, down_other, near_other = tie(head_low, down_other, near_other)
    lead_shard, tail_shard = pack(scalars, gain_one, query_weight, key_weight, value_weight)
    lead_w, tail_w = gather(lead_shard, fsdp), gather(tail_shard, fsdp)
    heads, gate_w, up_w, near_cot, lead_shard = tie(
        exchange(head_low),
        placed(*gate_pair, "y"),
        placed(*up_pair, "x"),
        jnp.concatenate([near_cot, near_other], 0),
        lead_shard,
    )
    heads = heads.reshape(QH // 2 * HD, chip_count)

    mine_of = lambda value: take_rows(value, core * count, count)
    theirs_of = lambda value: take_rows(value, (1 - core) * count, count)
    branch = contract(heads, out_w, 0, 0).astype(LOW)
    middle = chip_rows.astype(F32) + (branch.astype(F32) + swap(branch, "c").astype(F32))
    middle_scale = row_scale(middle)
    chip_unit = middle * middle_scale
    own_middle, own_scale, own_middle_unit = (
        mine_of(middle),
        mine_of(middle_scale),
        mine_of(chip_unit),
    )
    chip_unit, down_pair, down_other = tie(chip_unit.astype(LOW), down_pair, down_other)
    down_w = placed(down_pair, down_other, "x")
    near_unit = swap_near(mine_of(chip_unit))
    near_unit = jnp.concatenate([near_unit, swap(near_unit, "c")], 0)

    def feed(unit):
        gate, upper = contract(unit, gate_w, 1, 0), contract(unit, up_w, 1, 0)
        sigma = jax.nn.sigmoid(gate)
        silu = gate * sigma
        return (silu * upper).astype(LOW), (gate, upper, sigma, silu)

    def feed_back(cot, kept):
        gate, upper, sigma, silu = kept
        grad_hidden = contract(cot, down_w, 1, 1)
        gate_low = (grad_hidden * upper * sigma * (1.0 + gate * (1.0 - sigma))).astype(LOW)
        upper_low = (grad_hidden * silu).astype(LOW)
        part = contract(gate_low, gate_w, 1, 1) + contract(upper_low, up_w, 1, 1)
        return gate_low, upper_low, part

    def chip_sum(chip_part, near_part):
        near_sum = near_part[:count].astype(F32) + swap(near_part[count:].astype(LOW), "c")
        own_sum = mine_of(chip_part).astype(F32) + swap(theirs_of(chip_part).astype(LOW), "c")
        return own_sum, near_sum.astype(LOW)

    stack = lambda first, second: jnp.concatenate([first, second], 0)
    scatter = lambda value: lax.psum_scatter(value, fsdp, scatter_dimension=0, tiled=True)
    chip_hidden, chip_kept = feed(chip_unit)
    near_hidden, near_kept = feed(near_unit)
    down_part = contract(
        stack(chip_hidden, near_hidden), stack(chip_cot, near_cot), 0, 0
    ).astype(LOW)
    near_cot, down_part = tie(near_cot, down_part)
    feed_own, feed_near = chip_sum(
        contract(chip_hidden, down_w, 1, 0), contract(near_hidden, down_w, 1, 0)
    )
    feed_near = swap_near(feed_near)
    near_gate, near_upper, near_part = feed_back(near_cot, near_kept)
    chip_gate, chip_upper, chip_part = feed_back(chip_cot, chip_kept)
    grad_two, near_sum = chip_sum(chip_part, near_part)

    def halves_first(value):
        cut = value.shape[-1] // 2
        return halve_x(value[:, :cut]), halve_y(value[:, cut:])

    def halves_second(firsts):
        return halve(sum(firsts[0]), "y"), halve(sum(firsts[1]), "x")

    def halves_end(seconds):
        return jnp.concatenate([sum(seconds[0]), sum(seconds[1])], 1)

    down_first = halves_first(down_part)
    near_sum, near_gate, near_upper = tie(near_sum, near_gate, near_upper)
    grad_two = grad_two + swap_near(near_sum).astype(F32)
    all_units = stack(chip_unit, near_unit)
    gate_part = contract(all_units, stack(chip_gate, near_gate), 0, 0).astype(LOW)
    gate_first = halves_first(gate_part)
    up_part = contract(all_units, stack(chip_upper, near_upper), 0, 0).astype(LOW)
    up_grad = scatter(up_part)
    grad_two, up_part, down_first = tie(grad_two, up_part, down_first)
    down_second = halves_second(down_first)
    grad_middle = own_cot.astype(F32) + own_scale * (
        grad_two - own_middle_unit * jnp.mean(grad_two * own_middle_unit, -1, keepdims=True)
    )
    own_branch = grad_middle.astype(LOW)
    grad_branch = both(core, own_branch, swap(own_branch, "c"))
    grad_heads = contract(out_w, grad_branch, 1, 1).astype(LOW)
    grad_heads, grad_branch, gate_first, down_second, lead_w, tail_w = tie(
        grad_heads, grad_branch, gate_first, down_second, lead_w, tail_w
    )

    down_grad = halves_end(down_second)
    down_far = swap_far(down_grad)
    gate_second = halves_second(gate_first)
    output_part = contract(heads, grad_branch, 1, 0).astype(LOW)
    output_grad = scatter(output_part)
    grad_head, output_part, gate_second, down_far, feed_near, up_grad = tie(
        exchange(grad_heads.reshape(2 * lines, HD, chip_count)),
        output_part,
        gate_second,
        down_far,
        feed_near,
        up_grad,
    )

    gate_grad = halves_end(gate_second)
    gate_far = swap_far(gate_grad)
    down_sum = down_grad + down_far
    down_near = swap_near(down_sum)
    kept, leaving = attend_backward(scalars, own, other, grad_head, head_full, log_total)
    kept, leaving, gate_far, down_near, up_grad, output_grad = tie(
        kept, leaving, gate_far, down_near, up_grad, output_grad
    )

    up_far = swap_far(up_grad)
    gate_sum = gate_grad + gate_far
    gate_near = swap_near(gate_sum)
    block_output = (own_middle + feed_own + feed_near.astype(F32)).astype(LOW)[None]
    came, up_far, gate_near, block_output = tie(
        swap(leaving, "x"), up_far, gate_near, block_output
    )

    place = lax.axis_index("z")
    inner = (place == 1) | (place == 2)
    qkv_low, by_line = merge(scalars, kept, came, cosine, sine, lines)
    token_grads = lax.all_to_all(by_line, "z", split_axis=0, concat_axis=0, tiled=True)
    qkv_part = contract(units, qkv_low, 0, 1).astype(LOW).reshape(shards, 2, -1, 4 * HD)
    qkv_first = halve_x(qkv_part[:, 0]), halve_y(qkv_part[:, 1])
    qkv_second = halves_second(qkv_first)
    output_came = lax.ppermute(output_grad, "z", [(0, 1), (3, 2)])
    up_sum = up_grad + up_far
    up_near = swap_near(up_sum)
    token_grads, output_came, up_near = tie(token_grads, output_came, up_near)

    output_sum = output_grad + output_came
    output_sum = output_sum + lax.ppermute(output_sum, "z", [(1, 2), (2, 1)])
    qkv_grad = jnp.concatenate([sum(qkv_second[0]), sum(qkv_second[1])], 0)
    token_grads = token_grads.reshape(-1, chip_count)
    split = lead_w.shape[1]
    grad_one = contract(token_grads[:split], lead_w, 0, 1) + contract(
        token_grads[split:], tail_w, 0, 1
    )
    all_qkv = gather(qkv_grad, seq)
    grad_one, all_qkv = tie(grad_one, all_qkv)
    grad_one = mine_of(grad_one) + swap(theirs_of(grad_one).astype(LOW), "c").astype(F32)
    grad_rows = own_unit_scale * (
        grad_one - own_unit * jnp.mean(grad_one * own_unit, -1, keepdims=True)
    )
    input_grad = (grad_middle + grad_rows).astype(LOW)[None]
    output_far = lax.ppermute(output_sum, "z", [(1, 0), (2, 3)])
    output_own = jnp.where(inner, output_sum, output_far)

    def four(value, near_value):
        return value, swap(value, "c"), near_value, swap(near_value, "c")

    order = jnp.stack([quarter, quarter ^ 1, quarter ^ 2, quarter ^ 3]).astype(jnp.int32)
    core_order = jnp.stack([core, 1 - core]).astype(jnp.int32)
    down_total = place_rows(order, four(down_sum, down_near))
    output_total = place_rows(core_order, (output_own, swap(output_own, "c")))
    gate_total, up_total, second_gain_grad = place_columns(
        order, gain_two, gate_weight, up_weight, four(gate_sum, gate_near), four(up_sum, up_near), shards
    )
    query_grad, key_grad, value_grad, first_gain_grad = place_heads(
        gain_one, query_weight, key_weight, value_weight, all_qkv
    )
    return (
        block_output,
        input_grad,
        first_gain_grad[:, 0],
        query_grad,
        key_grad,
        value_grad,
        output_total,
        second_gain_grad[:, 0],
        gate_total,
        up_total,
        down_total,
    )


def fast_solution(mesh):
    seq_count, shard_count = mesh.devices.shape
    fine = Mesh(
        mesh.devices.reshape(seq_count // 2, 2, shard_count // 2, 2), ("z", "c", "y", "x")
    )
    seq, fsdp = ("z", "c"), ("y", "x")
    matrix = P(fsdp, None)
    return jax.shard_map(
        fast_body,
        mesh=fine,
        in_specs=(
            P(fsdp, seq, None),
            P(fsdp, seq),
            P(fsdp),
            matrix,
            matrix,
            matrix,
            matrix,
            P(fsdp),
            matrix,
            matrix,
            matrix,
            P(fsdp, seq, None),
        ),
        out_specs=(
            P(fsdp, seq, None),
            P(fsdp, seq, None),
            P(fsdp),
            matrix,
            matrix,
            matrix,
            matrix,
            P(fsdp),
            matrix,
            matrix,
            matrix,
        ),
        check_vma=False,
    )


def solution(mesh):
    shape = dict(mesh.shape)
    if shape["seq"] == KVH and shape["fsdp"] == 4:
        return fast_solution(mesh)
    return plain_solution(mesh)


def shifted(value, axis, steps):
    count = lax.axis_size(axis)
    first, last = (max(0, -steps), min(count, count - steps))
    return lax.ppermute(value, axis, [(source, source + steps) for source in range(first, last)])


def rope_tables(position_rows):
    freq = THETA ** (-(jnp.arange(HD // 2, dtype=jnp.float32) * 2.0 / HD))
    angle = position_rows.astype(jnp.float32)[:, None] * freq[None, :]
    cosine = jnp.cos(angle)
    sine = jnp.sin(angle)
    return (jnp.concatenate([cosine, cosine], -1), jnp.concatenate([sine, sine], -1))


def rotate(values, cosine, sine):
    half = HD // 2
    turned = jnp.concatenate([-values[..., half:], values[..., :half]], -1)
    return values * cosine[:, None, :] + turned * sine[:, None, :]


def rotate_back(grads, cosine, sine):
    half = HD // 2
    scaled = grads * sine[:, None, :]
    turned = jnp.concatenate([scaled[..., half:], -scaled[..., :half]], -1)
    return grads * cosine[:, None, :] + turned


def norm_forward(rows, gain):
    scale = lax.rsqrt(jnp.mean(rows * rows, -1, keepdims=True) + EPS)
    unit = rows * scale
    return (unit * gain, unit, scale)


def norm_backward(grad_out, unit, scale, gain):
    grad_unit = grad_out * gain
    gain_grad = jnp.sum(grad_out * unit, 0)
    grad_rows = scale * (grad_unit - unit * jnp.mean(grad_unit * unit, -1, keepdims=True))
    return (grad_rows, gain_grad)


def plain_body(
    tokens,
    positions,
    first_gain,
    query_weight,
    key_weight,
    value_weight,
    output_weight,
    second_gain,
    gate_weight,
    up_weight,
    down_weight,
    cotangent,
):
    seq_count = lax.axis_size("seq")
    local_rows = tokens[0]
    token_count = local_rows.shape[0]
    half_len = token_count * seq_count
    rows_float = local_rows.astype(jnp.float32)
    gain_one, wq_full, wk_full, wv_full, wo_full = (
        lax.all_gather(first_gain, "fsdp", axis=0, tiled=True),
        lax.all_gather(query_weight, "fsdp", axis=0, tiled=True),
        lax.all_gather(key_weight, "fsdp", axis=0, tiled=True),
        lax.all_gather(value_weight, "fsdp", axis=0, tiled=True),
        lax.all_gather(output_weight, "fsdp", axis=0, tiled=True),
    )
    gain_one = gain_one.astype(jnp.float32)
    normed_one, unit_one, scale_one = norm_forward(rows_float, gain_one)
    normed_low = normed_one.astype(jnp.bfloat16)
    cosine, sine = rope_tables(positions[0])
    query_lin = jnp.dot(normed_low, wq_full, preferred_element_type=jnp.float32).reshape(
        token_count, QH, HD
    )
    key_lin = jnp.dot(normed_low, wk_full, preferred_element_type=jnp.float32).reshape(
        token_count, KVH, HD
    )
    value_lin = jnp.dot(normed_low, wv_full, preferred_element_type=jnp.float32).reshape(
        token_count, KVH, HD
    )
    query_rows = rotate(query_lin, cosine, sine).astype(jnp.bfloat16)
    key_rows = rotate(key_lin, cosine, sine).astype(jnp.bfloat16)
    value_rows = value_lin.astype(jnp.bfloat16)
    repeat = max(1, seq_count // KVH)
    if repeat > 1:
        key_rows = jnp.repeat(key_rows, repeat, axis=1)
        value_rows = jnp.repeat(value_rows, repeat, axis=1)
    query_heads, key_heads, value_heads = (
        lax.all_to_all(query_rows, "seq", split_axis=1, concat_axis=0, tiled=True),
        lax.all_to_all(key_rows, "seq", split_axis=1, concat_axis=0, tiled=True),
        lax.all_to_all(value_rows, "seq", split_axis=1, concat_axis=0, tiled=True),
    )
    head_count = query_heads.shape[1]
    pair_count = key_heads.shape[1]
    group = head_count // pair_count
    half_positions = lax.all_gather(positions[0], "seq", axis=0, tiled=True)
    key_prior, value_prior = shifted((key_heads, value_heads), "fsdp", 1)
    key_all = jnp.concatenate([key_prior, key_heads], 0)
    value_all = jnp.concatenate([value_prior, value_heads], 0)
    half_index = lax.axis_index("fsdp") % 2
    key_index = (half_index - 1) * half_len + jnp.arange(2 * half_len, dtype=jnp.int32)
    row_index = half_index * half_len + jnp.arange(half_len, dtype=jnp.int32)
    row_start = row_index - half_positions
    block = min(512, half_len)
    count = half_len // block
    factor = HD ** (-0.5)
    query_blocks = query_heads.reshape(count, block, pair_count, group, HD)
    index_blocks = row_index.reshape(count, block)
    start_blocks = row_start.reshape(count, block)

    def block_scores(query_block, index_block, start_block):
        scores = (
            jnp.einsum("bkgd,tkd->kgbt", query_block, key_all, preferred_element_type=jnp.float32)
            * factor
        )
        visible = (key_index[None, :] >= start_block[:, None]) & (
            key_index[None, :] <= index_block[:, None]
        )
        return jnp.where(visible, scores, -1e30)

    def forward_block(items):
        query_block, index_block, start_block = items
        scores = block_scores(query_block, index_block, start_block)
        top = jnp.max(scores, -1, keepdims=True)
        expo = jnp.exp(scores - top)
        total = jnp.sum(expo, -1, keepdims=True)
        probs_low = (expo / total).astype(jnp.bfloat16)
        mixed = jnp.einsum(
            "kgbt,tkd->bkgd", probs_low, value_all, preferred_element_type=jnp.float32
        )
        return (mixed.reshape(block, head_count, HD).astype(jnp.bfloat16), top + jnp.log(total))

    head_blocks, log_totals = lax.map(forward_block, (query_blocks, index_blocks, start_blocks))
    head_out = head_blocks.reshape(half_len, head_count, HD)
    token_heads = lax.all_to_all(head_out, "seq", split_axis=0, concat_axis=1, tiled=True)
    heads_flat = token_heads.reshape(token_count, QH * HD)
    middle = rows_float + jnp.dot(heads_flat, wo_full, preferred_element_type=jnp.float32)
    gain_two, wg_full, wu_full, wd_full = (
        lax.all_gather(second_gain, "fsdp", axis=0, tiled=True),
        lax.all_gather(gate_weight, "fsdp", axis=0, tiled=True),
        lax.all_gather(up_weight, "fsdp", axis=0, tiled=True),
        lax.all_gather(down_weight, "fsdp", axis=0, tiled=True),
    )
    gain_two = gain_two.astype(jnp.float32)
    normed_two, unit_two, scale_two = norm_forward(middle, gain_two)
    normed_two_low = normed_two.astype(jnp.bfloat16)
    gate = jnp.dot(normed_two_low, wg_full, preferred_element_type=jnp.float32)
    upper = jnp.dot(normed_two_low, wu_full, preferred_element_type=jnp.float32)
    hidden = (jax.nn.silu(gate) * upper).astype(jnp.bfloat16)
    result = middle + jnp.dot(hidden, wd_full, preferred_element_type=jnp.float32)
    block_output = result.astype(jnp.bfloat16)[None]
    grad_low = cotangent[0]
    grad_rows = grad_low.astype(jnp.float32)
    down_grad = jnp.einsum("tf,td->fd", hidden, grad_low, preferred_element_type=jnp.float32)
    grad_hidden = jnp.einsum("td,fd->tf", grad_low, wd_full, preferred_element_type=jnp.float32)
    sigma = jax.nn.sigmoid(gate)
    gate_low = (grad_hidden * upper * sigma * (1.0 + gate * (1.0 - sigma))).astype(jnp.bfloat16)
    upper_low = (grad_hidden * gate * sigma).astype(jnp.bfloat16)
    gate_grad = jnp.einsum(
        "td,tf->df", normed_two_low, gate_low, preferred_element_type=jnp.float32
    )
    up_grad = jnp.einsum("td,tf->df", normed_two_low, upper_low, preferred_element_type=jnp.float32)
    grad_normed_two = jnp.einsum(
        "tf,df->td", gate_low, wg_full, preferred_element_type=jnp.float32
    ) + jnp.einsum("tf,df->td", upper_low, wu_full, preferred_element_type=jnp.float32)
    grad_middle_norm, second_gain_grad = norm_backward(
        grad_normed_two, unit_two, scale_two, gain_two
    )
    grad_middle = grad_rows + grad_middle_norm
    grad_branch = grad_middle.astype(jnp.bfloat16)
    output_grad = jnp.einsum(
        "tc,td->cd", heads_flat, grad_branch, preferred_element_type=jnp.float32
    )
    grad_heads = (
        jnp.einsum("td,cd->tc", grad_branch, wo_full, preferred_element_type=jnp.float32)
        .astype(jnp.bfloat16)
        .reshape(token_count, QH, HD)
    )
    grad_head_rows = lax.all_to_all(grad_heads, "seq", split_axis=1, concat_axis=0, tiled=True)
    grad_blocks = grad_head_rows.reshape(count, block, pair_count, group, HD)

    def backward_block(carry, items):
        key_acc, value_acc = carry
        query_block, index_block, start_block, grad_block, log_block = items
        scores = block_scores(query_block, index_block, start_block)
        probs = jnp.exp(scores - log_block)
        probs_low = probs.astype(jnp.bfloat16)
        grad_probs = jnp.einsum(
            "bkgd,tkd->kgbt", grad_block, value_all, preferred_element_type=jnp.float32
        )
        grad_scores = (
            probs * (grad_probs - jnp.sum(probs * grad_probs, -1, keepdims=True))
        ).astype(jnp.bfloat16)
        query_grad_block = (
            jnp.einsum("kgbt,tkd->bkgd", grad_scores, key_all, preferred_element_type=jnp.float32)
            * factor
        )
        key_acc = (
            key_acc
            + jnp.einsum(
                "kgbt,bkgd->tkd", grad_scores, query_block, preferred_element_type=jnp.float32
            )
            * factor
        )
        value_acc = value_acc + jnp.einsum(
            "kgbt,bkgd->tkd", probs_low, grad_block, preferred_element_type=jnp.float32
        )
        return ((key_acc, value_acc), query_grad_block.reshape(block, head_count, HD))

    empty = jnp.zeros((2 * half_len, pair_count, HD), jnp.float32)
    (key_acc, value_acc), query_grad_blocks = lax.scan(
        backward_block,
        (empty, empty),
        (query_blocks, index_blocks, start_blocks, grad_blocks, log_totals),
    )
    key_back, value_back = (
        shifted(key_acc[:half_len].astype(jnp.bfloat16), "fsdp", -1).astype(jnp.float32),
        shifted(value_acc[:half_len].astype(jnp.bfloat16), "fsdp", -1).astype(jnp.float32),
    )
    key_local = key_acc[half_len:] + key_back
    value_local = value_acc[half_len:] + value_back
    query_grad_heads = query_grad_blocks.reshape(half_len, head_count, HD)
    grad_query_tok, grad_key_tok, grad_value_tok = (
        lax.all_to_all(
            query_grad_heads.astype(jnp.bfloat16), "seq", split_axis=0, concat_axis=1, tiled=True
        ).astype(query_grad_heads.dtype),
        lax.all_to_all(
            key_local.astype(jnp.bfloat16), "seq", split_axis=0, concat_axis=1, tiled=True
        ).astype(key_local.dtype),
        lax.all_to_all(
            value_local.astype(jnp.bfloat16), "seq", split_axis=0, concat_axis=1, tiled=True
        ).astype(value_local.dtype),
    )
    if repeat > 1:
        grad_key_tok = grad_key_tok.reshape(token_count, KVH, repeat, HD).sum(2)
        grad_value_tok = grad_value_tok.reshape(token_count, KVH, repeat, HD).sum(2)
    query_lin_grad = (
        rotate_back(grad_query_tok, cosine, sine).astype(jnp.bfloat16).reshape(token_count, QH * HD)
    )
    key_lin_grad = (
        rotate_back(grad_key_tok, cosine, sine).astype(jnp.bfloat16).reshape(token_count, KVH * HD)
    )
    value_lin_grad = grad_value_tok.astype(jnp.bfloat16).reshape(token_count, KVH * HD)
    query_grad = jnp.einsum(
        "td,tc->dc", normed_low, query_lin_grad, preferred_element_type=jnp.float32
    )
    key_grad = jnp.einsum("td,tc->dc", normed_low, key_lin_grad, preferred_element_type=jnp.float32)
    value_grad = jnp.einsum(
        "td,tc->dc", normed_low, value_lin_grad, preferred_element_type=jnp.float32
    )
    grad_normed_one = jnp.einsum(
        "tc,dc->td", query_lin_grad, wq_full, preferred_element_type=jnp.float32
    )
    grad_normed_one = grad_normed_one + jnp.einsum(
        "tc,dc->td", key_lin_grad, wk_full, preferred_element_type=jnp.float32
    )
    grad_normed_one = grad_normed_one + jnp.einsum(
        "tc,dc->td", value_lin_grad, wv_full, preferred_element_type=jnp.float32
    )
    grad_rows_one, first_gain_grad = norm_backward(grad_normed_one, unit_one, scale_one, gain_one)
    input_grad = (grad_middle + grad_rows_one).astype(jnp.bfloat16)[None]
    pieces = (
        lax.psum_scatter(
            first_gain_grad.astype(jnp.bfloat16), "fsdp", scatter_dimension=0, tiled=True
        ).astype(jnp.float32),
        lax.psum_scatter(
            query_grad.astype(jnp.bfloat16), "fsdp", scatter_dimension=0, tiled=True
        ).astype(jnp.float32),
        lax.psum_scatter(
            key_grad.astype(jnp.bfloat16), "fsdp", scatter_dimension=0, tiled=True
        ).astype(jnp.float32),
        lax.psum_scatter(
            value_grad.astype(jnp.bfloat16), "fsdp", scatter_dimension=0, tiled=True
        ).astype(jnp.float32),
        lax.psum_scatter(
            output_grad.astype(jnp.bfloat16), "fsdp", scatter_dimension=0, tiled=True
        ).astype(jnp.float32),
        lax.psum_scatter(
            second_gain_grad.astype(jnp.bfloat16), "fsdp", scatter_dimension=0, tiled=True
        ).astype(jnp.float32),
        lax.psum_scatter(
            gate_grad.astype(jnp.bfloat16), "fsdp", scatter_dimension=0, tiled=True
        ).astype(jnp.float32),
        lax.psum_scatter(
            up_grad.astype(jnp.bfloat16), "fsdp", scatter_dimension=0, tiled=True
        ).astype(jnp.float32),
        lax.psum_scatter(
            down_grad.astype(jnp.bfloat16), "fsdp", scatter_dimension=0, tiled=True
        ).astype(jnp.float32),
    )
    shares = (
        lax.psum(pieces[0].astype(jnp.bfloat16), "seq").astype(jnp.float32),
        lax.psum(pieces[1].astype(jnp.bfloat16), "seq").astype(jnp.float32),
        lax.psum(pieces[2].astype(jnp.bfloat16), "seq").astype(jnp.float32),
        lax.psum(pieces[3].astype(jnp.bfloat16), "seq").astype(jnp.float32),
        lax.psum(pieces[4].astype(jnp.bfloat16), "seq").astype(jnp.float32),
        lax.psum(pieces[5].astype(jnp.bfloat16), "seq").astype(jnp.float32),
        lax.psum(pieces[6].astype(jnp.bfloat16), "seq").astype(jnp.float32),
        lax.psum(pieces[7].astype(jnp.bfloat16), "seq").astype(jnp.float32),
        lax.psum(pieces[8].astype(jnp.bfloat16), "seq").astype(jnp.float32),
    )
    return (
        block_output,
        input_grad,
        shares[0],
        shares[1],
        shares[2],
        shares[3],
        shares[4],
        shares[5],
        shares[6],
        shares[7],
        shares[8],
    )


def plain_solution(mesh):
    placed = (
        P("fsdp", "seq", None),
        P("fsdp", "seq"),
        P("fsdp"),
        P("fsdp", None),
        P("fsdp", None),
        P("fsdp", None),
        P("fsdp", None),
        P("fsdp"),
        P("fsdp", None),
        P("fsdp", None),
        P("fsdp", None),
        P("fsdp", "seq", None),
    )
    return jax.shard_map(
        plain_body,
        mesh=mesh,
        in_specs=placed,
        out_specs=(
            P("fsdp", "seq", None),
            P("fsdp", "seq", None),
            P("fsdp"),
            P("fsdp", None),
            P("fsdp", None),
            P("fsdp", None),
            P("fsdp", None),
            P("fsdp"),
            P("fsdp", None),
            P("fsdp", None),
            P("fsdp", None),
        ),
        check_vma=False,
    )
```

```python
import functools
import math

import jax
import jax.numpy as jnp
from jax import lax
from jax.experimental import pallas as pl
from jax.experimental.pallas import tpu as pltpu
from jax.sharding import Mesh
from jax.sharding import PartitionSpec as P

QH = 16
KVH = 8
HD = 96


THETA = 100000.0
EPS = 1e-05
LOW = jnp.bfloat16
F32 = jnp.float32
NEG = -1e30
LN2 = math.log(2.0)


def contract(left, right, left_axis, right_axis):
    return lax.dot_general(
        left, right, (((left_axis,), (right_axis,)), ((), ())), preferred_element_type=F32
    )


def visible(first, second, query_block, key_block, size):
    key = key_block * size + lax.broadcasted_iota(jnp.int32, (size, size), 0)
    query = query_block * size + lax.broadcasted_iota(jnp.int32, (1, size), 1)
    start = jnp.where(query >= second, second, jnp.where(query >= first, first, 0))
    return (key >= start) & (key <= query)


def slot_of(block, count):
    return (block % (count // 2)) * 2 + block // (count // 2)


def forward_kernel(
    scalars,
    own_ref,
    other_ref,
    low_ref,
    full_ref,
    log_ref,
    query_s,
    key_s,
    value_s,
    top_s,
    total_s,
    mixed_s,
    *,
    size,
    count,
):
    half = scalars[0]
    first = scalars[1]
    second = scalars[2]
    here = pl.program_id(0)
    per_half = count // 2

    @pl.when(here == 0)
    def _():
        for ref, side in ((own_ref, half), (other_ref, 1 - half)):
            for step in range(per_half):
                block = side * per_half + step
                columns = slice(step * size, (step + 1) * size)
                query_s[block] = ref[0:HD, columns]
                key_s[block] = ref[HD : 2 * HD, columns].T
                value_s[block] = ref[2 * HD : 3 * HD, columns]

    query = query_s[here]
    top_s[...] = jnp.full_like(top_s, NEG)
    total_s[...] = jnp.zeros_like(total_s)
    mixed_s[...] = jnp.zeros_like(mixed_s)

    def add_block(block, masked):
        scores = contract(key_s[block], query, 1, 0)
        if masked:
            scores = jnp.where(visible(first, second, here, block, size), scores, NEG)
        old_top = top_s[...]
        top = jnp.maximum(old_top, jnp.max(scores, 0, keepdims=True))
        expo = jnp.exp2(scores - top)
        scale = jnp.exp2(old_top - top)
        top_s[...] = top
        total_s[...] = total_s[...] * scale + jnp.sum(expo, 0, keepdims=True)
        mixed_s[...] = mixed_s[...] * scale + contract(value_s[block], expo.astype(LOW), 1, 0)

    last = count - 1

    @pl.loop(1, jnp.where(here == last, 1, here))
    def _(block):
        add_block(block, False)

    @pl.loop(0, jnp.where(here == last, count, jnp.minimum(here + 1, 2)))
    def _(step):
        add_block(jnp.where(here == last, step, step * here), True)

    total = total_s[...]
    result = mixed_s[...] / total
    full_ref[0] = result
    low_ref[0] = result.astype(LOW)
    log_ref[0] = top_s[...] + jnp.log2(total)


def backward_kernel(
    scalars,
    own_ref,
    other_ref,
    grad_ref,
    full_ref,
    log_ref,
    kept_ref,
    leaving_ref,
    query_s,
    key_s,
    value_s,
    delta_s,
    query_grad_s,
    key_grad_s,
    value_grad_s,
    *,
    size,
    count,
):
    half = scalars[0]
    first = scalars[1]
    second = scalars[2]
    here = pl.program_id(0)
    per_half = count // 2

    @pl.when(here == 0)
    def _():
        for ref, side in ((own_ref, half), (other_ref, 1 - half)):
            for step in range(per_half):
                block = side * per_half + step
                columns = slice(step * size, (step + 1) * size)
                query_s[block] = ref[0:HD, columns]
                key_s[block] = ref[HD : 2 * HD, columns]
                value_s[block] = ref[2 * HD : 3 * HD, columns].T
        for block in range(count):
            delta_s[block] = jnp.sum(
                grad_ref[slot_of(block, count)].astype(F32) * full_ref[block], 0, keepdims=True
            )
        query_grad_s[...] = jnp.zeros_like(query_grad_s)

    key_grad_s[...] = jnp.zeros_like(key_grad_s)
    value_grad_s[...] = jnp.zeros_like(value_grad_s)
    key = key_s[here]
    key_rows = key.T
    value_rows = value_s[here]

    def add_block(block, masked):
        query = query_s[block]
        grad = grad_ref[slot_of(block, count)]
        scores = contract(key_rows, query, 1, 0)
        if masked:
            scores = jnp.where(visible(first, second, block, here, size), scores, NEG)
        probs = jnp.exp2(scores - log_ref[block])
        grad_probs = contract(value_rows, grad, 1, 0)
        grad_scores = (probs * (grad_probs - delta_s[block])).astype(LOW)
        value_grad_s[...] += contract(grad, probs.astype(LOW), 1, 1)
        key_grad_s[...] += contract(query, grad_scores, 1, 1)
        query_grad_s[block] += contract(key, grad_scores, 1, 0)

    last = count - 1

    @pl.loop(here + 1, jnp.where(here == 0, 1, last))
    def _(block):
        add_block(block, False)

    @pl.loop(0, jnp.where(here == 0, count, jnp.where(here == last, 1, 2)))
    def _(step):
        add_block(jnp.where(here == 0, step, jnp.where(step == 0, here, last)), True)

    side = here // per_half
    columns = pl.ds(pl.multiple_of((here % per_half) * size, size), size)

    def write(out_ref):
        out_ref[0:HD, columns] = (query_grad_s[here] * HD**-0.5).astype(LOW)
        out_ref[HD : 2 * HD, columns] = (key_grad_s[...] * LN2).astype(LOW)
        out_ref[2 * HD : 3 * HD, columns] = value_grad_s[...].astype(LOW)

    @pl.when(side == half)
    def _():
        write(kept_ref)

    @pl.when(side != half)
    def _():
        write(leaving_ref)


def attend_forward(scalars, own, other, size):
    count = 2 * own.shape[1] // size
    whole = lambda shape: pl.BlockSpec(shape, lambda i, s: (0,) * len(shape))
    pairs = count * (count + 1) // 2
    return pl.pallas_call(
        functools.partial(forward_kernel, size=size, count=count),
        grid_spec=pltpu.PrefetchScalarGridSpec(
            num_scalar_prefetch=1,
            grid=(count,),
            in_specs=[whole(own.shape), whole(other.shape)],
            out_specs=[
                pl.BlockSpec(
                    (1, HD, size), lambda i, s: (slot_of(i, count), 0, 0)
                ),
                pl.BlockSpec((1, HD, size), lambda i, s: (i, 0, 0)),
                pl.BlockSpec((1, 1, size), lambda i, s: (i, 0, 0)),
            ],
            scratch_shapes=[
                pltpu.VMEM((count, HD, size), LOW),
                pltpu.VMEM((count, size, HD), LOW),
                pltpu.VMEM((count, HD, size), LOW),
                pltpu.VMEM((1, size), F32),
                pltpu.VMEM((1, size), F32),
                pltpu.VMEM((HD, size), F32),
            ],
        ),
        out_shape=[
            jax.ShapeDtypeStruct((count, HD, size), LOW),
            jax.ShapeDtypeStruct((count, HD, size), F32),
            jax.ShapeDtypeStruct((count, 1, size), F32),
        ],
        compiler_params=pltpu.CompilerParams(
            dimension_semantics=("arbitrary",), vmem_limit_bytes=32 * 2**20
        ),
        cost_estimate=pl.CostEstimate(
            flops=pairs * size * size * HD * 32,
            bytes_accessed=10 * 2**20,
            transcendentals=pairs * size * size,
        ),
        name="attend_forward",
    )(scalars, own, other)


def attend_backward(scalars, own, other, grad, full, log_total):
    count, _, size = grad.shape
    whole = lambda shape: pl.BlockSpec(shape, lambda i, s: (0,) * len(shape))
    pairs = count * (count + 1) // 2
    out_shape = own.shape
    return pl.pallas_call(
        functools.partial(backward_kernel, size=size, count=count),
        grid_spec=pltpu.PrefetchScalarGridSpec(
            num_scalar_prefetch=1,
            grid=(count,),
            in_specs=[
                whole(own.shape),
                whole(other.shape),
                whole(grad.shape),
                whole(full.shape),
                whole(log_total.shape),
            ],
            out_specs=[whole(out_shape)] * 2,
            scratch_shapes=[
                pltpu.VMEM((count, HD, size), LOW),
                pltpu.VMEM((count, HD, size), LOW),
                pltpu.VMEM((count, size, HD), LOW),
                pltpu.VMEM((count, 1, size), F32),
                pltpu.VMEM((count, HD, size), F32),
                pltpu.VMEM((HD, size), F32),
                pltpu.VMEM((HD, size), F32),
            ],
        ),
        out_shape=[jax.ShapeDtypeStruct(out_shape, LOW)] * 2,
        compiler_params=pltpu.CompilerParams(
            dimension_semantics=("arbitrary",), vmem_limit_bytes=32 * 2**20
        ),
        cost_estimate=pl.CostEstimate(
            flops=pairs * size * size * HD * 42,
            bytes_accessed=16 * 2**20,
            transcendentals=pairs * size * size,
        ),
        name="attend_backward",
    )(scalars, own, other, grad, full, log_total)


def place_rows_kernel(order, *refs):
    pieces, out_ref = refs[:-1], refs[-1]
    size = pieces[0].shape[0]
    for index, piece in enumerate(pieces):
        start = pl.multiple_of(order[index] * size, size)
        out_ref[pl.ds(start, size), :] = piece[...].astype(F32)


def place_rows(order, pieces):
    size, width = pieces[0].shape
    total = size * len(pieces)
    step = 512
    return pl.pallas_call(
        place_rows_kernel,
        grid_spec=pltpu.PrefetchScalarGridSpec(
            num_scalar_prefetch=1,
            grid=(width // step,),
            in_specs=[pl.BlockSpec((size, step), lambda i, s: (0, i)) for _ in pieces],
            out_specs=pl.BlockSpec((total, step), lambda i, s: (0, i)),
        ),
        out_shape=jax.ShapeDtypeStruct((total, width), F32),
        compiler_params=pltpu.CompilerParams(vmem_limit_bytes=24 * 2**20),
        cost_estimate=pl.CostEstimate(
            flops=0, bytes_accessed=total * width * 6, transcendentals=0
        ),
        name="place_rows",
    )(order, *pieces)


def place_columns_kernel(order, gain_ref, gate_w_ref, up_w_ref, *refs):
    count = (len(refs) - 3) // 2
    gates, ups = refs[:count], refs[count : 2 * count]
    gate_ref, up_ref, sum_ref = refs[2 * count :]
    size = gates[0].shape[1]
    gain = gain_ref[...]
    total = jnp.zeros((gate_ref.shape[0], size), F32)
    for index in range(count):
        columns = pl.ds(pl.multiple_of(order[index] * size, size), size)
        gate, up = gates[index][...].astype(F32), ups[index][...].astype(F32)
        total += gate * gate_w_ref[:, columns].astype(F32)
        total += up * up_w_ref[:, columns].astype(F32)
        gate_ref[:, columns] = gate * gain
        up_ref[:, columns] = up * gain

    @pl.when(pl.program_id(0) == 0)
    def _():
        sum_ref[...] = jnp.zeros_like(sum_ref)

    sum_ref[...] += jnp.sum(total, 1, keepdims=True)


def place_columns(order, gain, gate_weight, up_weight, gates, ups, shards):
    rows, width = gate_weight.shape
    span = width // shards
    size = span // len(gates)
    wide = pl.BlockSpec((rows, span), lambda i, s: (0, i))
    thin = pl.BlockSpec((rows, 1), lambda i, s: (0, 0))
    pieces = [pl.BlockSpec((rows, size), lambda i, s: (0, i)) for _ in (*gates, *ups)]
    return pl.pallas_call(
        place_columns_kernel,
        grid_spec=pltpu.PrefetchScalarGridSpec(
            num_scalar_prefetch=1,
            grid=(shards,),
            in_specs=[thin, wide, wide, *pieces],
            out_specs=[wide, wide, thin],
        ),
        out_shape=[
            jax.ShapeDtypeStruct((rows, width), F32),
            jax.ShapeDtypeStruct((rows, width), F32),
            jax.ShapeDtypeStruct((rows, 1), F32),
        ],
        compiler_params=pltpu.CompilerParams(
            dimension_semantics=("arbitrary",), vmem_limit_bytes=24 * 2**20
        ),
        cost_estimate=pl.CostEstimate(
            flops=rows * width * 6, bytes_accessed=rows * width * 16, transcendentals=0
        ),
        name="place_columns",
    )(order, gain, gate_weight, up_weight, *gates, *ups)


def place_heads_kernel(gain_ref, query_w, key_w, value_w, all_ref, query_ref, key_ref, value_ref, sum_ref):
    rows = gain_ref.shape[0]
    wide = query_ref.shape[1] // KVH
    gain = gain_ref[...]
    total = jnp.zeros((rows, 4 * HD), F32)
    pieces = [all_ref[i * rows : (i + 1) * rows, :].astype(F32) for i in range(KVH)]
    for start in range(0, KVH, 2):
        value = jnp.concatenate([piece[:, :wide] for piece in pieces[start : start + 2]], 1)
        columns = slice(start * wide, (start + 2) * wide)
        total += value * query_w[:, columns].astype(F32)
        query_ref[:, columns] = value * gain
    for first, weight, out_ref in ((wide, key_w, key_ref), (wide + HD, value_w, value_ref)):
        for start in range(0, KVH, 4):
            value = jnp.concatenate(
                [piece[:, first : first + HD] for piece in pieces[start : start + 4]], 1
            )
            columns = slice(start * HD, (start + 4) * HD)
            total += value * weight[:, columns].astype(F32)
            out_ref[:, columns] = value * gain
    sum_ref[...] = jnp.sum(total, 1, keepdims=True)


def place_heads(gain, query_weight, key_weight, value_weight, pieces):
    weights = (query_weight, key_weight, value_weight)
    rows = gain.shape[0]
    return pl.pallas_call(
        place_heads_kernel,
        out_shape=[jax.ShapeDtypeStruct(weight.shape, F32) for weight in weights]
        + [jax.ShapeDtypeStruct((rows, 1), F32)],
        compiler_params=pltpu.CompilerParams(vmem_limit_bytes=32 * 2**20),
        cost_estimate=pl.CostEstimate(
            flops=rows * 3072 * 4, bytes_accessed=rows * 3072 * 8, transcendentals=0
        ),
        name="place_heads",
    )(gain, *weights, pieces)


def merge_kernel(scalars, kept_ref, came_ref, cosine_ref, sine_ref, out_ref, split_ref):
    lead = scalars[0] == 0
    lines, _, size = split_ref.shape
    for line in range(lines):
        columns = slice(line * size, (line + 1) * size)
        kept = kept_ref[:, columns].astype(F32)
        came = came_ref[:, columns].astype(F32)
        cosine, sine = cosine_ref[:, columns], sine_ref[:, columns]
        joint = kept[HD:] + came[HD:]
        first = jnp.where(lead, kept[:HD], came[:HD])
        second = jnp.where(lead, came[:HD], kept[:HD])
        turned = []
        for value in (first, second, joint[:HD]):
            low, high = value[: HD // 2], value[HD // 2 :]
            turned.append(low * cosine + high * sine)
            turned.append(high * cosine - low * sine)
        turned.append(joint[HD:])
        result = jnp.concatenate([part.astype(LOW) for part in turned], 0)
        out_ref[:, columns] = result
        split_ref[line] = result


def merge(scalars, kept, came, cosine, sine, lines):
    tokens = kept.shape[1]
    whole = lambda value: pl.BlockSpec(value.shape, lambda i, s: (0,) * len(value.shape))
    outs = [
        jax.ShapeDtypeStruct((4 * HD, tokens), LOW),
        jax.ShapeDtypeStruct((lines, 4 * HD, tokens // lines), LOW),
    ]
    return pl.pallas_call(
        merge_kernel,
        grid_spec=pltpu.PrefetchScalarGridSpec(
            num_scalar_prefetch=1,
            grid=(1,),
            in_specs=[whole(value) for value in (kept, came, cosine, sine)],
            out_specs=[whole(value) for value in outs],
        ),
        out_shape=outs,
        compiler_params=pltpu.CompilerParams(vmem_limit_bytes=24 * 2**20),
        cost_estimate=pl.CostEstimate(
            flops=tokens * HD * 24, bytes_accessed=tokens * HD * 30, transcendentals=0
        ),
        name="merge",
    )(scalars, kept, came, cosine, sine)


def pack_kernel(scalars, gain_ref, query_ref, key_ref, value_ref, *outs):
    core = scalars[3]
    gain = gain_ref[...]
    wide = query_ref.shape[1] // KVH
    span = wide + 2 * HD
    for which in range(2):

        @pl.when(core == which)
        def _():
            for line in range(KVH // 2):
                head = 2 * line + which
                value = jnp.concatenate(
                    [
                        query_ref[:, head * wide : (head + 1) * wide].astype(F32),
                        key_ref[:, head * HD : (head + 1) * HD].astype(F32),
                        value_ref[:, head * HD : (head + 1) * HD].astype(F32),
                    ],
                    1,
                )
                place = (line % 2) * span
                outs[line // 2][:, place : place + span] = (value * gain).astype(LOW)


def pack(scalars, gain, query_weight, key_weight, value_weight):
    rows, width = query_weight.shape
    whole = lambda value: pl.BlockSpec(value.shape, lambda i, s: (0, 0))
    weights = (gain, query_weight, key_weight, value_weight)
    outs = [jax.ShapeDtypeStruct((rows, width // 2), LOW)] * 2
    return pl.pallas_call(
        pack_kernel,
        grid_spec=pltpu.PrefetchScalarGridSpec(
            num_scalar_prefetch=1,
            grid=(1,),
            in_specs=[whole(value) for value in weights],
            out_specs=[whole(value) for value in outs],
        ),
        out_shape=outs,
        compiler_params=pltpu.CompilerParams(vmem_limit_bytes=24 * 2**20),
        cost_estimate=pl.CostEstimate(
            flops=rows * width, bytes_accessed=rows * width * 6, transcendentals=0
        ),
        name="pack",
    )(scalars, *weights)


def spread_kernel(scalars, lin_ref, cosine_ref, sine_ref, own_ref, leaving_ref):
    cosine, sine = cosine_ref[...], sine_ref[...]

    def turn(start, factor):
        low = lin_ref[start : start + HD // 2, :]
        high = lin_ref[start + HD // 2 : start + HD, :]
        turned = ((low * cosine - high * sine) * factor, (high * cosine + low * sine) * factor)
        return jnp.concatenate([part.astype(LOW) for part in turned], 0)

    lead = scalars[0] == 0
    first, second = turn(0, HD**-0.5 / LN2), turn(HD, HD**-0.5 / LN2)

    @pl.when(lead)
    def _():
        own_ref[0:HD] = first
        leaving_ref[0:HD] = second

    @pl.when(jnp.logical_not(lead))
    def _():
        own_ref[0:HD] = second
        leaving_ref[0:HD] = first

    key = turn(2 * HD, 1.0)
    value = lin_ref[3 * HD : 4 * HD].astype(LOW)
    for ref in (own_ref, leaving_ref):
        ref[HD : 2 * HD] = key
        ref[2 * HD : 3 * HD] = value


def spread(scalars, lin, cosine, sine):
    tokens = lin.shape[1]
    step = 512
    column = lambda rows: pl.BlockSpec((rows, step), lambda i, s: (0, i))
    return pl.pallas_call(
        spread_kernel,
        grid_spec=pltpu.PrefetchScalarGridSpec(
            num_scalar_prefetch=1,
            grid=(tokens // step,),
            in_specs=[column(4 * HD), column(HD // 2), column(HD // 2)],
            out_specs=[column(3 * HD)] * 2,
        ),
        out_shape=[jax.ShapeDtypeStruct((3 * HD, tokens), LOW)] * 2,
        compiler_params=pltpu.CompilerParams(vmem_limit_bytes=24 * 2**20),
        cost_estimate=pl.CostEstimate(
            flops=tokens * HD * 24, bytes_accessed=tokens * HD * 36, transcendentals=0
        ),
        name="spread",
    )(scalars, lin, cosine, sine)


def swap(value, axis):
    return lax.ppermute(value, axis, [(0, 1), (1, 0)])


def swap_near(value):
    return lax.ppermute(value, "z", [(0, 1), (1, 0), (2, 3), (3, 2)])


def swap_far(value):
    return lax.ppermute(value, "z", [(0, 2), (2, 0), (1, 3), (3, 1)])


def tie(*values):
    return lax.optimization_barrier(values)


def in_order(place, own, other):
    return (jnp.where(place == 0, own, other), jnp.where(place == 0, other, own))


def both(place, own, other):
    return jnp.concatenate(in_order(place, own, other), 0)


def spread_out(value, first, second):
    other = swap(value, first)
    pair = jnp.stack(in_order(lax.axis_index(first), value, other))
    return pair, swap(pair, second)


def placed(pair, other, second):
    pairs = in_order(lax.axis_index(second), pair, other)
    grid = jnp.stack(pairs, 0 if second == "y" else 1)
    return grid.reshape(-1, *grid.shape[3:])


def pick(array, axis, at):
    return lax.dynamic_index_in_dim(array, at, axis, keepdims=False)


def halve(value, axis, along=0):
    at = lax.axis_index(axis)
    return pick(value, along, at), swap(pick(value, along, 1 - at), axis)


def halve_x(value):
    return halve(value.reshape(2, 2, -1, value.shape[-1]), "x", 1)


def halve_y(value):
    return halve(value.reshape(2, 2, -1, value.shape[-1]), "y", 0)


def fast_body(
    tokens,
    positions,
    first_gain,
    query_weight,
    key_weight,
    value_weight,
    output_weight,
    second_gain,
    gate_weight,
    up_weight,
    down_weight,
    cotangent,
):
    seq = ("z", "c")
    fsdp = ("y", "x")
    z, core, half = lax.axis_index("z"), lax.axis_index("c"), lax.axis_index("x")
    near = z % 2
    lines = lax.axis_size("z")
    seq_count = 2 * lines
    shards = lax.axis_size("y") * 2
    spot = z * 2 + core
    quarter = near * 2 + core
    rows = tokens[0]
    count, width = rows.shape
    chip_count = 2 * count
    half_len = count * seq_count
    seq_len = 2 * half_len

    begins = jnp.where(
        (spot == 0) & (half == 0),
        count - 1 - positions[0, count - 1],
        half * half_len + spot * count - positions[0, 0],
    )
    ends = begins + (seq_len - count)
    scalars = jnp.stack([half, begins, ends, core]).astype(jnp.int32)

    gain_one = first_gain.astype(F32)[:, None]
    gain_two = second_gain.astype(F32)[:, None]

    def row_scale(value):
        return lax.rsqrt(jnp.mean(value * value, -1, keepdims=True) + EPS)

    take = functools.partial(lax.dynamic_slice_in_dim, axis=1)
    take_rows = functools.partial(lax.dynamic_slice_in_dim, axis=0)
    gather = lambda value, axes: lax.all_gather(value, axes, axis=0, tiled=True)
    own_rows = rows.astype(F32)
    own_unit_scale = row_scale(own_rows)
    own_unit = own_rows * own_unit_scale
    units = gather(own_unit.astype(LOW), seq)
    wide = QH // KVH * HD
    qkv_shard = (
        jnp.concatenate(
            [
                take(query_weight, spot * wide, wide),
                take(key_weight, spot * HD, HD),
                take(value_weight, spot * HD, HD),
            ],
            1,
        ).astype(F32)
        * gain_one
    ).astype(LOW)
    out_rows = output_weight.shape[0] // 2
    out_shard = take_rows(output_weight, core * out_rows, out_rows)
    piece = down_weight.shape[0] // 4
    down_shard = take_rows(down_weight, quarter * piece, piece)
    gate_shard, up_shard = (
        (
            jnp.concatenate(
                [
                    take(weight, shard * 4 * piece + quarter * piece, piece)
                    for shard in range(shards)
                ],
                1,
            ).astype(F32)
            * gain_two
        ).astype(LOW)
        for weight in (gate_weight, up_weight)
    )
    side = lax.axis_index("y")
    qkv_pair = jnp.stack(in_order(half, qkv_shard, swap(qkv_shard, "x")))
    gate_pair = jnp.stack(in_order(half, gate_shard, swap(gate_shard, "x")))
    up_pair = jnp.stack(in_order(side, up_shard, swap(up_shard, "y")))
    qkv_pair, gate_pair, up_pair = tie(qkv_pair, gate_pair, up_pair)
    qkv_w = placed(qkv_pair, swap(qkv_pair, "y"), "y")
    gate_pair, up_pair = (gate_pair, swap(gate_pair, "y")), (up_pair, swap(up_pair, "x"))

    place = half * half_len + jnp.arange(half_len, dtype=jnp.int32)
    start = jnp.where(place >= ends, ends, jnp.where(place >= begins, begins, 0))
    freq = THETA ** (-(jnp.arange(HD // 2, dtype=F32) * 2.0 / HD))
    angle = freq[:, None] * (place - start).astype(F32)[None, :]
    cosine, sine = jnp.cos(angle), jnp.sin(angle)
    chip_rows = both(core, rows, swap(rows, "c"))
    units, own_cot, chip_rows = tie(units, cotangent[0], chip_rows)
    own, leaving = spread(scalars, contract(qkv_w, units, 0, 1), cosine, sine)

    near_cot = swap_near(own_cot)
    other, out_shard, down_shard, near_cot, chip_cot, gate_pair, up_pair = tie(
        swap(leaving, "x"),
        out_shard,
        down_shard,
        near_cot,
        both(core, own_cot, swap(own_cot, "c")),
        gate_pair,
        up_pair,
    )
    out_w = gather(out_shard, fsdp)
    down_w = gather(down_shard, fsdp)
    near_other = swap(near_cot, "c")
    head_low, head_full, log_total = attend_forward(scalars, own, other, chip_count)
    exchange = lambda value: lax.all_to_all(
        value, ("z", "x"), split_axis=0, concat_axis=0, tiled=True
    )
    head_low, near_other = tie(head_low, near_other)
    lead_shard, tail_shard = pack(scalars, gain_one, query_weight, key_weight, value_weight)
    heads, gate_w, up_w, near_cot, lead_shard = tie(
        exchange(head_low),
        placed(*gate_pair, "y"),
        placed(*up_pair, "x"),
        jnp.concatenate([near_cot, near_other], 0),
        lead_shard,
    )
    lead_w = gather(lead_shard, fsdp)
    heads = heads.reshape(QH // 2 * HD, chip_count)

    mine_of = lambda value: take_rows(value, core * count, count)
    theirs_of = lambda value: take_rows(value, (1 - core) * count, count)
    branch = contract(heads, out_w, 0, 0).astype(LOW)
    middle = chip_rows.astype(F32) + (branch.astype(F32) + swap(branch, "c").astype(F32))
    middle_scale = row_scale(middle)
    chip_unit = middle * middle_scale
    own_middle, own_scale, own_middle_unit = (
        mine_of(middle),
        mine_of(middle_scale),
        mine_of(chip_unit),
    )
    chip_unit = chip_unit.astype(LOW)
    near_unit = swap_near(mine_of(chip_unit))
    near_unit = jnp.concatenate([near_unit, swap(near_unit, "c")], 0)

    def feed(unit):
        gate, upper = contract(unit, gate_w, 1, 0), contract(unit, up_w, 1, 0)
        sigma = jax.nn.sigmoid(gate)
        silu = gate * sigma
        return (silu * upper).astype(LOW), (gate, upper, sigma, silu)

    def feed_back(cot, kept):
        gate, upper, sigma, silu = kept
        grad_hidden = contract(cot, down_w, 1, 1)
        gate_low = (grad_hidden * upper * sigma * (1.0 + gate * (1.0 - sigma))).astype(LOW)
        upper_low = (grad_hidden * silu).astype(LOW)
        part = contract(gate_low, gate_w, 1, 1) + contract(upper_low, up_w, 1, 1)
        return gate_low, upper_low, part

    def chip_sum(chip_part, near_part):
        near_sum = near_part[:count].astype(F32) + swap(near_part[count:].astype(LOW), "c")
        own_sum = mine_of(chip_part).astype(F32) + swap(theirs_of(chip_part).astype(LOW), "c")
        return own_sum, near_sum.astype(LOW)

    stack = lambda first, second: jnp.concatenate([first, second], 0)
    scatter = lambda value: lax.psum_scatter(value, fsdp, scatter_dimension=0, tiled=True)
    chip_hidden, chip_kept = feed(chip_unit)
    near_hidden, near_kept = feed(near_unit)
    down_part = contract(
        stack(chip_hidden, near_hidden), stack(chip_cot, near_cot), 0, 0
    ).astype(LOW)
    feed_own, feed_near = chip_sum(
        contract(chip_hidden, down_w, 1, 0), contract(near_hidden, down_w, 1, 0)
    )
    near_cot, down_part, feed_near = tie(near_cot, down_part, feed_near)
    feed_near = swap_near(feed_near)
    down_grad = scatter(down_part)
    near_gate, near_upper, near_part = feed_back(near_cot, near_kept)
    chip_gate, chip_upper, chip_part = feed_back(chip_cot, chip_kept)
    grad_two, near_sum = chip_sum(chip_part, near_part)

    def halves_first(value):
        cut = value.shape[-1] // 2
        return halve_x(value[:, :cut]), halve_y(value[:, cut:])

    def halves_second(firsts):
        return halve(sum(firsts[0]), "y"), halve(sum(firsts[1]), "x")

    def halves_end(seconds):
        return jnp.concatenate([sum(seconds[0]), sum(seconds[1])], 1)

    near_sum, near_gate, near_upper = tie(near_sum, near_gate, near_upper)
    grad_two = grad_two + swap_near(near_sum).astype(F32)
    all_units = stack(chip_unit, near_unit)
    gate_part = contract(all_units, stack(chip_gate, near_gate), 0, 0).astype(LOW)
    gate_part, feed_near = tie(gate_part, feed_near)
    gate_half = halve_x(gate_part)
    up_part = contract(all_units, stack(chip_upper, near_upper), 0, 0).astype(LOW)
    up_half = halve_y(up_part)
    grad_two, up_part, lead_w, tail_shard = tie(grad_two, up_part, lead_w, tail_shard)
    tail_w = gather(tail_shard, fsdp)
    grad_middle = own_cot.astype(F32) + own_scale * (
        grad_two - own_middle_unit * jnp.mean(grad_two * own_middle_unit, -1, keepdims=True)
    )
    own_branch = grad_middle.astype(LOW)
    grad_branch = both(core, own_branch, swap(own_branch, "c"))
    grad_heads = contract(out_w, grad_branch, 1, 1).astype(LOW)
    grad_heads, grad_branch, gate_half, up_half, down_grad = tie(
        grad_heads, grad_branch, gate_half, up_half, down_grad
    )
    down_far = swap_far(down_grad)

    gate_half, up_half = halve(sum(gate_half), "y"), halve(sum(up_half), "x")
    output_part = contract(heads, grad_branch, 1, 0).astype(LOW)
    output_grad = scatter(output_part)
    grad_head, output_part, gate_half, up_half, down_far = tie(
        exchange(grad_heads.reshape(2 * lines, HD, chip_count)),
        output_part,
        gate_half,
        up_half,
        down_far,
    )

    gate_grad, up_grad = sum(gate_half), sum(up_half)
    gate_far = swap_far(gate_grad)
    down_sum = down_grad + down_far
    down_near = swap_near(down_sum)
    kept, leaving = attend_backward(scalars, own, other, grad_head, head_full, log_total)
    kept, leaving, gate_far, down_near, up_grad, tail_w, output_grad = tie(
        kept, leaving, gate_far, down_near, up_grad, tail_w, output_grad
    )

    up_far = swap_far(up_grad)
    gate_sum = gate_grad + gate_far
    gate_near = swap_near(gate_sum)
    block_output = (own_middle + feed_own + feed_near.astype(F32)).astype(LOW)[None]
    output_came = lax.ppermute(output_grad, "z", [(0, 1), (3, 2)])
    came, up_far, gate_near, output_came, block_output = tie(
        swap(leaving, "x"), up_far, gate_near, output_came, block_output
    )

    place = lax.axis_index("z")
    inner = (place == 1) | (place == 2)
    qkv_low, by_line = merge(scalars, kept, came, cosine, sine, lines)
    token_grads = lax.all_to_all(by_line, "z", split_axis=0, concat_axis=0, tiled=True)
    qkv_part = contract(units, qkv_low, 0, 1).astype(LOW).reshape(shards, 2, -1, 4 * HD)
    qkv_first = halve_x(qkv_part[:, 0]), halve_y(qkv_part[:, 1])
    qkv_second = halves_second(qkv_first)
    qkv_grad = jnp.concatenate([sum(qkv_second[0]), sum(qkv_second[1])], 0)
    output_sum = output_grad + output_came
    output_came = lax.ppermute(output_sum, "z", [(1, 2), (2, 1)])
    up_sum = up_grad + up_far
    up_near = swap_near(up_sum)
    token_grads, qkv_grad, output_came, up_near = tie(
        token_grads, qkv_grad, output_came, up_near
    )
    all_qkv = gather(qkv_grad, seq)
    output_sum = output_sum + output_came
    output_far = lax.ppermute(output_sum, "z", [(1, 0), (2, 3)])

    token_grads = token_grads.reshape(-1, chip_count)
    split = lead_w.shape[1]
    grad_one = contract(token_grads[:split], lead_w, 0, 1) + contract(
        token_grads[split:], tail_w, 0, 1
    )
    grad_one = mine_of(grad_one) + swap(theirs_of(grad_one).astype(LOW), "c").astype(F32)
    grad_rows = own_unit_scale * (
        grad_one - own_unit * jnp.mean(grad_one * own_unit, -1, keepdims=True)
    )
    input_grad = (grad_middle + grad_rows).astype(LOW)[None]
    output_own = jnp.where(inner, output_sum, output_far)

    def four(value, near_value):
        return value, swap(value, "c"), near_value, swap(near_value, "c")

    order = jnp.stack([quarter, quarter ^ 1, quarter ^ 2, quarter ^ 3]).astype(jnp.int32)
    core_order = jnp.stack([core, 1 - core]).astype(jnp.int32)
    down_total = place_rows(order, four(down_sum, down_near))
    output_total = place_rows(core_order, (output_own, swap(output_own, "c")))
    gate_total, up_total, second_gain_grad = place_columns(
        order, gain_two, gate_weight, up_weight, four(gate_sum, gate_near), four(up_sum, up_near), shards
    )
    query_grad, key_grad, value_grad, first_gain_grad = place_heads(
        gain_one, query_weight, key_weight, value_weight, all_qkv
    )
    return (
        block_output,
        input_grad,
        first_gain_grad[:, 0],
        query_grad,
        key_grad,
        value_grad,
        output_total,
        second_gain_grad[:, 0],
        gate_total,
        up_total,
        down_total,
    )


def fast_solution(mesh):
    seq_count, shard_count = mesh.devices.shape
    fine = Mesh(
        mesh.devices.reshape(seq_count // 2, 2, shard_count // 2, 2), ("z", "c", "y", "x")
    )
    seq, fsdp = ("z", "c"), ("y", "x")
    matrix = P(fsdp, None)
    return jax.shard_map(
        fast_body,
        mesh=fine,
        in_specs=(
            P(fsdp, seq, None),
            P(fsdp, seq),
            P(fsdp),
            matrix,
            matrix,
            matrix,
            matrix,
            P(fsdp),
            matrix,
            matrix,
            matrix,
            P(fsdp, seq, None),
        ),
        out_specs=(
            P(fsdp, seq, None),
            P(fsdp, seq, None),
            P(fsdp),
            matrix,
            matrix,
            matrix,
            matrix,
            P(fsdp),
            matrix,
            matrix,
            matrix,
        ),
        check_vma=False,
    )


def solution(mesh):
    shape = dict(mesh.shape)
    if shape["seq"] == KVH and shape["fsdp"] == 4:
        return fast_solution(mesh)
    return plain_solution(mesh)


def shifted(value, axis, steps):
    count = lax.axis_size(axis)
    first, last = (max(0, -steps), min(count, count - steps))
    return lax.ppermute(value, axis, [(source, source + steps) for source in range(first, last)])


def rope_tables(position_rows):
    freq = THETA ** (-(jnp.arange(HD // 2, dtype=jnp.float32) * 2.0 / HD))
    angle = position_rows.astype(jnp.float32)[:, None] * freq[None, :]
    cosine = jnp.cos(angle)
    sine = jnp.sin(angle)
    return (jnp.concatenate([cosine, cosine], -1), jnp.concatenate([sine, sine], -1))


def rotate(values, cosine, sine):
    half = HD // 2
    turned = jnp.concatenate([-values[..., half:], values[..., :half]], -1)
    return values * cosine[:, None, :] + turned * sine[:, None, :]


def rotate_back(grads, cosine, sine):
    half = HD // 2
    scaled = grads * sine[:, None, :]
    turned = jnp.concatenate([scaled[..., half:], -scaled[..., :half]], -1)
    return grads * cosine[:, None, :] + turned


def norm_forward(rows, gain):
    scale = lax.rsqrt(jnp.mean(rows * rows, -1, keepdims=True) + EPS)
    unit = rows * scale
    return (unit * gain, unit, scale)


def norm_backward(grad_out, unit, scale, gain):
    grad_unit = grad_out * gain
    gain_grad = jnp.sum(grad_out * unit, 0)
    grad_rows = scale * (grad_unit - unit * jnp.mean(grad_unit * unit, -1, keepdims=True))
    return (grad_rows, gain_grad)


def plain_body(
    tokens,
    positions,
    first_gain,
    query_weight,
    key_weight,
    value_weight,
    output_weight,
    second_gain,
    gate_weight,
    up_weight,
    down_weight,
    cotangent,
):
    seq_count = lax.axis_size("seq")
    local_rows = tokens[0]
    token_count = local_rows.shape[0]
    half_len = token_count * seq_count
    rows_float = local_rows.astype(jnp.float32)
    gain_one, wq_full, wk_full, wv_full, wo_full = (
        lax.all_gather(first_gain, "fsdp", axis=0, tiled=True),
        lax.all_gather(query_weight, "fsdp", axis=0, tiled=True),
        lax.all_gather(key_weight, "fsdp", axis=0, tiled=True),
        lax.all_gather(value_weight, "fsdp", axis=0, tiled=True),
        lax.all_gather(output_weight, "fsdp", axis=0, tiled=True),
    )
    gain_one = gain_one.astype(jnp.float32)
    normed_one, unit_one, scale_one = norm_forward(rows_float, gain_one)
    normed_low = normed_one.astype(jnp.bfloat16)
    cosine, sine = rope_tables(positions[0])
    query_lin = jnp.dot(normed_low, wq_full, preferred_element_type=jnp.float32).reshape(
        token_count, QH, HD
    )
    key_lin = jnp.dot(normed_low, wk_full, preferred_element_type=jnp.float32).reshape(
        token_count, KVH, HD
    )
    value_lin = jnp.dot(normed_low, wv_full, preferred_element_type=jnp.float32).reshape(
        token_count, KVH, HD
    )
    query_rows = rotate(query_lin, cosine, sine).astype(jnp.bfloat16)
    key_rows = rotate(key_lin, cosine, sine).astype(jnp.bfloat16)
    value_rows = value_lin.astype(jnp.bfloat16)
    repeat = max(1, seq_count // KVH)
    if repeat > 1:
        key_rows = jnp.repeat(key_rows, repeat, axis=1)
        value_rows = jnp.repeat(value_rows, repeat, axis=1)
    query_heads, key_heads, value_heads = (
        lax.all_to_all(query_rows, "seq", split_axis=1, concat_axis=0, tiled=True),
        lax.all_to_all(key_rows, "seq", split_axis=1, concat_axis=0, tiled=True),
        lax.all_to_all(value_rows, "seq", split_axis=1, concat_axis=0, tiled=True),
    )
    head_count = query_heads.shape[1]
    pair_count = key_heads.shape[1]
    group = head_count // pair_count
    half_positions = lax.all_gather(positions[0], "seq", axis=0, tiled=True)
    key_prior, value_prior = shifted((key_heads, value_heads), "fsdp", 1)
    key_all = jnp.concatenate([key_prior, key_heads], 0)
    value_all = jnp.concatenate([value_prior, value_heads], 0)
    half_index = lax.axis_index("fsdp") % 2
    key_index = (half_index - 1) * half_len + jnp.arange(2 * half_len, dtype=jnp.int32)
    row_index = half_index * half_len + jnp.arange(half_len, dtype=jnp.int32)
    row_start = row_index - half_positions
    block = min(512, half_len)
    count = half_len // block
    factor = HD ** (-0.5)
    query_blocks = query_heads.reshape(count, block, pair_count, group, HD)
    index_blocks = row_index.reshape(count, block)
    start_blocks = row_start.reshape(count, block)

    def block_scores(query_block, index_block, start_block):
        scores = (
            jnp.einsum("bkgd,tkd->kgbt", query_block, key_all, preferred_element_type=jnp.float32)
            * factor
        )
        visible = (key_index[None, :] >= start_block[:, None]) & (
            key_index[None, :] <= index_block[:, None]
        )
        return jnp.where(visible, scores, -1e30)

    def forward_block(items):
        query_block, index_block, start_block = items
        scores = block_scores(query_block, index_block, start_block)
        top = jnp.max(scores, -1, keepdims=True)
        expo = jnp.exp(scores - top)
        total = jnp.sum(expo, -1, keepdims=True)
        probs_low = (expo / total).astype(jnp.bfloat16)
        mixed = jnp.einsum(
            "kgbt,tkd->bkgd", probs_low, value_all, preferred_element_type=jnp.float32
        )
        return (mixed.reshape(block, head_count, HD).astype(jnp.bfloat16), top + jnp.log(total))

    head_blocks, log_totals = lax.map(forward_block, (query_blocks, index_blocks, start_blocks))
    head_out = head_blocks.reshape(half_len, head_count, HD)
    token_heads = lax.all_to_all(head_out, "seq", split_axis=0, concat_axis=1, tiled=True)
    heads_flat = token_heads.reshape(token_count, QH * HD)
    middle = rows_float + jnp.dot(heads_flat, wo_full, preferred_element_type=jnp.float32)
    gain_two, wg_full, wu_full, wd_full = (
        lax.all_gather(second_gain, "fsdp", axis=0, tiled=True),
        lax.all_gather(gate_weight, "fsdp", axis=0, tiled=True),
        lax.all_gather(up_weight, "fsdp", axis=0, tiled=True),
        lax.all_gather(down_weight, "fsdp", axis=0, tiled=True),
    )
    gain_two = gain_two.astype(jnp.float32)
    normed_two, unit_two, scale_two = norm_forward(middle, gain_two)
    normed_two_low = normed_two.astype(jnp.bfloat16)
    gate = jnp.dot(normed_two_low, wg_full, preferred_element_type=jnp.float32)
    upper = jnp.dot(normed_two_low, wu_full, preferred_element_type=jnp.float32)
    hidden = (jax.nn.silu(gate) * upper).astype(jnp.bfloat16)
    result = middle + jnp.dot(hidden, wd_full, preferred_element_type=jnp.float32)
    block_output = result.astype(jnp.bfloat16)[None]
    grad_low = cotangent[0]
    grad_rows = grad_low.astype(jnp.float32)
    down_grad = jnp.einsum("tf,td->fd", hidden, grad_low, preferred_element_type=jnp.float32)
    grad_hidden = jnp.einsum("td,fd->tf", grad_low, wd_full, preferred_element_type=jnp.float32)
    sigma = jax.nn.sigmoid(gate)
    gate_low = (grad_hidden * upper * sigma * (1.0 + gate * (1.0 - sigma))).astype(jnp.bfloat16)
    upper_low = (grad_hidden * gate * sigma).astype(jnp.bfloat16)
    gate_grad = jnp.einsum(
        "td,tf->df", normed_two_low, gate_low, preferred_element_type=jnp.float32
    )
    up_grad = jnp.einsum("td,tf->df", normed_two_low, upper_low, preferred_element_type=jnp.float32)
    grad_normed_two = jnp.einsum(
        "tf,df->td", gate_low, wg_full, preferred_element_type=jnp.float32
    ) + jnp.einsum("tf,df->td", upper_low, wu_full, preferred_element_type=jnp.float32)
    grad_middle_norm, second_gain_grad = norm_backward(
        grad_normed_two, unit_two, scale_two, gain_two
    )
    grad_middle = grad_rows + grad_middle_norm
    grad_branch = grad_middle.astype(jnp.bfloat16)
    output_grad = jnp.einsum(
        "tc,td->cd", heads_flat, grad_branch, preferred_element_type=jnp.float32
    )
    grad_heads = (
        jnp.einsum("td,cd->tc", grad_branch, wo_full, preferred_element_type=jnp.float32)
        .astype(jnp.bfloat16)
        .reshape(token_count, QH, HD)
    )
    grad_head_rows = lax.all_to_all(grad_heads, "seq", split_axis=1, concat_axis=0, tiled=True)
    grad_blocks = grad_head_rows.reshape(count, block, pair_count, group, HD)

    def backward_block(carry, items):
        key_acc, value_acc = carry
        query_block, index_block, start_block, grad_block, log_block = items
        scores = block_scores(query_block, index_block, start_block)
        probs = jnp.exp(scores - log_block)
        probs_low = probs.astype(jnp.bfloat16)
        grad_probs = jnp.einsum(
            "bkgd,tkd->kgbt", grad_block, value_all, preferred_element_type=jnp.float32
        )
        grad_scores = (
            probs * (grad_probs - jnp.sum(probs * grad_probs, -1, keepdims=True))
        ).astype(jnp.bfloat16)
        query_grad_block = (
            jnp.einsum("kgbt,tkd->bkgd", grad_scores, key_all, preferred_element_type=jnp.float32)
            * factor
        )
        key_acc = (
            key_acc
            + jnp.einsum(
                "kgbt,bkgd->tkd", grad_scores, query_block, preferred_element_type=jnp.float32
            )
            * factor
        )
        value_acc = value_acc + jnp.einsum(
            "kgbt,bkgd->tkd", probs_low, grad_block, preferred_element_type=jnp.float32
        )
        return ((key_acc, value_acc), query_grad_block.reshape(block, head_count, HD))

    empty = jnp.zeros((2 * half_len, pair_count, HD), jnp.float32)
    (key_acc, value_acc), query_grad_blocks = lax.scan(
        backward_block,
        (empty, empty),
        (query_blocks, index_blocks, start_blocks, grad_blocks, log_totals),
    )
    key_back, value_back = (
        shifted(key_acc[:half_len].astype(jnp.bfloat16), "fsdp", -1).astype(jnp.float32),
        shifted(value_acc[:half_len].astype(jnp.bfloat16), "fsdp", -1).astype(jnp.float32),
    )
    key_local = key_acc[half_len:] + key_back
    value_local = value_acc[half_len:] + value_back
    query_grad_heads = query_grad_blocks.reshape(half_len, head_count, HD)
    grad_query_tok, grad_key_tok, grad_value_tok = (
        lax.all_to_all(
            query_grad_heads.astype(jnp.bfloat16), "seq", split_axis=0, concat_axis=1, tiled=True
        ).astype(query_grad_heads.dtype),
        lax.all_to_all(
            key_local.astype(jnp.bfloat16), "seq", split_axis=0, concat_axis=1, tiled=True
        ).astype(key_local.dtype),
        lax.all_to_all(
            value_local.astype(jnp.bfloat16), "seq", split_axis=0, concat_axis=1, tiled=True
        ).astype(value_local.dtype),
    )
    if repeat > 1:
        grad_key_tok = grad_key_tok.reshape(token_count, KVH, repeat, HD).sum(2)
        grad_value_tok = grad_value_tok.reshape(token_count, KVH, repeat, HD).sum(2)
    query_lin_grad = (
        rotate_back(grad_query_tok, cosine, sine).astype(jnp.bfloat16).reshape(token_count, QH * HD)
    )
    key_lin_grad = (
        rotate_back(grad_key_tok, cosine, sine).astype(jnp.bfloat16).reshape(token_count, KVH * HD)
    )
    value_lin_grad = grad_value_tok.astype(jnp.bfloat16).reshape(token_count, KVH * HD)
    query_grad = jnp.einsum(
        "td,tc->dc", normed_low, query_lin_grad, preferred_element_type=jnp.float32
    )
    key_grad = jnp.einsum("td,tc->dc", normed_low, key_lin_grad, preferred_element_type=jnp.float32)
    value_grad = jnp.einsum(
        "td,tc->dc", normed_low, value_lin_grad, preferred_element_type=jnp.float32
    )
    grad_normed_one = jnp.einsum(
        "tc,dc->td", query_lin_grad, wq_full, preferred_element_type=jnp.float32
    )
    grad_normed_one = grad_normed_one + jnp.einsum(
        "tc,dc->td", key_lin_grad, wk_full, preferred_element_type=jnp.float32
    )
    grad_normed_one = grad_normed_one + jnp.einsum(
        "tc,dc->td", value_lin_grad, wv_full, preferred_element_type=jnp.float32
    )
    grad_rows_one, first_gain_grad = norm_backward(grad_normed_one, unit_one, scale_one, gain_one)
    input_grad = (grad_middle + grad_rows_one).astype(jnp.bfloat16)[None]
    pieces = (
        lax.psum_scatter(
            first_gain_grad.astype(jnp.bfloat16), "fsdp", scatter_dimension=0, tiled=True
        ).astype(jnp.float32),
        lax.psum_scatter(
            query_grad.astype(jnp.bfloat16), "fsdp", scatter_dimension=0, tiled=True
        ).astype(jnp.float32),
        lax.psum_scatter(
            key_grad.astype(jnp.bfloat16), "fsdp", scatter_dimension=0, tiled=True
        ).astype(jnp.float32),
        lax.psum_scatter(
            value_grad.astype(jnp.bfloat16), "fsdp", scatter_dimension=0, tiled=True
        ).astype(jnp.float32),
        lax.psum_scatter(
            output_grad.astype(jnp.bfloat16), "fsdp", scatter_dimension=0, tiled=True
        ).astype(jnp.float32),
        lax.psum_scatter(
            second_gain_grad.astype(jnp.bfloat16), "fsdp", scatter_dimension=0, tiled=True
        ).astype(jnp.float32),
        lax.psum_scatter(
            gate_grad.astype(jnp.bfloat16), "fsdp", scatter_dimension=0, tiled=True
        ).astype(jnp.float32),
        lax.psum_scatter(
            up_grad.astype(jnp.bfloat16), "fsdp", scatter_dimension=0, tiled=True
        ).astype(jnp.float32),
        lax.psum_scatter(
            down_grad.astype(jnp.bfloat16), "fsdp", scatter_dimension=0, tiled=True
        ).astype(jnp.float32),
    )
    shares = (
        lax.psum(pieces[0].astype(jnp.bfloat16), "seq").astype(jnp.float32),
        lax.psum(pieces[1].astype(jnp.bfloat16), "seq").astype(jnp.float32),
        lax.psum(pieces[2].astype(jnp.bfloat16), "seq").astype(jnp.float32),
        lax.psum(pieces[3].astype(jnp.bfloat16), "seq").astype(jnp.float32),
        lax.psum(pieces[4].astype(jnp.bfloat16), "seq").astype(jnp.float32),
        lax.psum(pieces[5].astype(jnp.bfloat16), "seq").astype(jnp.float32),
        lax.psum(pieces[6].astype(jnp.bfloat16), "seq").astype(jnp.float32),
        lax.psum(pieces[7].astype(jnp.bfloat16), "seq").astype(jnp.float32),
        lax.psum(pieces[8].astype(jnp.bfloat16), "seq").astype(jnp.float32),
    )
    return (
        block_output,
        input_grad,
        shares[0],
        shares[1],
        shares[2],
        shares[3],
        shares[4],
        shares[5],
        shares[6],
        shares[7],
        shares[8],
    )


def plain_solution(mesh):
    placed = (
        P("fsdp", "seq", None),
        P("fsdp", "seq"),
        P("fsdp"),
        P("fsdp", None),
        P("fsdp", None),
        P("fsdp", None),
        P("fsdp", None),
        P("fsdp"),
        P("fsdp", None),
        P("fsdp", None),
        P("fsdp", None),
        P("fsdp", "seq", None),
    )
    return jax.shard_map(
        plain_body,
        mesh=mesh,
        in_specs=placed,
        out_specs=(
            P("fsdp", "seq", None),
            P("fsdp", "seq", None),
            P("fsdp"),
            P("fsdp", None),
            P("fsdp", None),
            P("fsdp", None),
            P("fsdp", None),
            P("fsdp"),
            P("fsdp", None),
            P("fsdp", None),
            P("fsdp", None),
        ),
        check_vma=False,
    )
```

```python
import functools
import math

import jax
import jax.numpy as jnp
from jax import lax
from jax.experimental import pallas as pl
from jax.experimental.pallas import tpu as pltpu
from jax.sharding import Mesh
from jax.sharding import PartitionSpec as P

QH = 16
KVH = 8
HD = 96


THETA = 100000.0
EPS = 1e-05
LOW = jnp.bfloat16
F32 = jnp.float32
NEG = -1e30
LN2 = math.log(2.0)


def contract(left, right, left_axis, right_axis):
    return lax.dot_general(
        left, right, (((left_axis,), (right_axis,)), ((), ())), preferred_element_type=F32
    )


def visible(first, second, query_block, key_block, size):
    key = key_block * size + lax.broadcasted_iota(jnp.int32, (size, size), 0)
    query = query_block * size + lax.broadcasted_iota(jnp.int32, (1, size), 1)
    start = jnp.where(query >= second, second, jnp.where(query >= first, first, 0))
    return (key >= start) & (key <= query)


def slot_of(block, count):
    return (block % (count // 2)) * 2 + block // (count // 2)


def forward_kernel(
    scalars,
    own_ref,
    other_ref,
    low_ref,
    full_ref,
    log_ref,
    query_s,
    key_s,
    value_s,
    top_s,
    total_s,
    mixed_s,
    *,
    size,
    count,
):
    half = scalars[0]
    first = scalars[1]
    second = scalars[2]
    here = pl.program_id(0)
    per_half = count // 2

    @pl.when(here == 0)
    def _():
        for ref, side in ((own_ref, half), (other_ref, 1 - half)):
            for step in range(per_half):
                block = side * per_half + step
                columns = slice(step * size, (step + 1) * size)
                query_s[block] = ref[0:HD, columns]
                key_s[block] = ref[HD : 2 * HD, columns].T
                value_s[block] = ref[2 * HD : 3 * HD, columns]

    query = query_s[here]
    top_s[...] = jnp.full_like(top_s, NEG)
    total_s[...] = jnp.zeros_like(total_s)
    mixed_s[...] = jnp.zeros_like(mixed_s)

    def add_block(block, masked):
        scores = contract(key_s[block], query, 1, 0)
        if masked:
            scores = jnp.where(visible(first, second, here, block, size), scores, NEG)
        old_top = top_s[...]
        top = jnp.maximum(old_top, jnp.max(scores, 0, keepdims=True))
        expo = jnp.exp2(scores - top)
        scale = jnp.exp2(old_top - top)
        top_s[...] = top
        total_s[...] = total_s[...] * scale + jnp.sum(expo, 0, keepdims=True)
        mixed_s[...] = mixed_s[...] * scale + contract(value_s[block], expo.astype(LOW), 1, 0)

    last = count - 1

    @pl.loop(1, jnp.where(here == last, 1, here))
    def _(block):
        add_block(block, False)

    @pl.loop(0, jnp.where(here == last, count, jnp.minimum(here + 1, 2)))
    def _(step):
        add_block(jnp.where(here == last, step, step * here), True)

    total = total_s[...]
    result = mixed_s[...] / total
    full_ref[0] = result
    low_ref[0] = result.astype(LOW)
    log_ref[0] = top_s[...] + jnp.log2(total)


def backward_kernel(
    scalars,
    own_ref,
    other_ref,
    grad_ref,
    full_ref,
    log_ref,
    kept_ref,
    leaving_ref,
    query_s,
    key_s,
    value_s,
    delta_s,
    query_grad_s,
    key_grad_s,
    value_grad_s,
    *,
    size,
    count,
):
    half = scalars[0]
    first = scalars[1]
    second = scalars[2]
    here = pl.program_id(0)
    per_half = count // 2

    @pl.when(here == 0)
    def _():
        for ref, side in ((own_ref, half), (other_ref, 1 - half)):
            for step in range(per_half):
                block = side * per_half + step
                columns = slice(step * size, (step + 1) * size)
                query_s[block] = ref[0:HD, columns]
                key_s[block] = ref[HD : 2 * HD, columns]
                value_s[block] = ref[2 * HD : 3 * HD, columns].T
        for block in range(count):
            delta_s[block] = jnp.sum(
                grad_ref[slot_of(block, count)].astype(F32) * full_ref[block], 0, keepdims=True
            )
        query_grad_s[...] = jnp.zeros_like(query_grad_s)

    key_grad_s[...] = jnp.zeros_like(key_grad_s)
    value_grad_s[...] = jnp.zeros_like(value_grad_s)
    key = key_s[here]
    key_rows = key.T
    value_rows = value_s[here]

    def add_block(block, masked):
        query = query_s[block]
        grad = grad_ref[slot_of(block, count)]
        scores = contract(key_rows, query, 1, 0)
        if masked:
            scores = jnp.where(visible(first, second, block, here, size), scores, NEG)
        probs = jnp.exp2(scores - log_ref[block])
        grad_probs = contract(value_rows, grad, 1, 0)
        grad_scores = (probs * (grad_probs - delta_s[block])).astype(LOW)
        value_grad_s[...] += contract(grad, probs.astype(LOW), 1, 1)
        key_grad_s[...] += contract(query, grad_scores, 1, 1)
        query_grad_s[block] += contract(key, grad_scores, 1, 0)

    last = count - 1

    @pl.loop(here + 1, jnp.where(here == 0, 1, last))
    def _(block):
        add_block(block, False)

    @pl.loop(0, jnp.where(here == 0, count, jnp.where(here == last, 1, 2)))
    def _(step):
        add_block(jnp.where(here == 0, step, jnp.where(step == 0, here, last)), True)

    side = here // per_half
    columns = pl.ds(pl.multiple_of((here % per_half) * size, size), size)

    def write(out_ref):
        out_ref[0:HD, columns] = (query_grad_s[here] * HD**-0.5).astype(LOW)
        out_ref[HD : 2 * HD, columns] = (key_grad_s[...] * LN2).astype(LOW)
        out_ref[2 * HD : 3 * HD, columns] = value_grad_s[...].astype(LOW)

    @pl.when(side == half)
    def _():
        write(kept_ref)

    @pl.when(side != half)
    def _():
        write(leaving_ref)


def attend_forward(scalars, own, other, size):
    count = 2 * own.shape[1] // size
    whole = lambda shape: pl.BlockSpec(shape, lambda i, s: (0,) * len(shape))
    pairs = count * (count + 1) // 2
    return pl.pallas_call(
        functools.partial(forward_kernel, size=size, count=count),
        grid_spec=pltpu.PrefetchScalarGridSpec(
            num_scalar_prefetch=1,
            grid=(count,),
            in_specs=[whole(own.shape), whole(other.shape)],
            out_specs=[
                pl.BlockSpec(
                    (1, HD, size), lambda i, s: (slot_of(i, count), 0, 0)
                ),
                pl.BlockSpec((1, HD, size), lambda i, s: (i, 0, 0)),
                pl.BlockSpec((1, 1, size), lambda i, s: (i, 0, 0)),
            ],
            scratch_shapes=[
                pltpu.VMEM((count, HD, size), LOW),
                pltpu.VMEM((count, size, HD), LOW),
                pltpu.VMEM((count, HD, size), LOW),
                pltpu.VMEM((1, size), F32),
                pltpu.VMEM((1, size), F32),
                pltpu.VMEM((HD, size), F32),
            ],
        ),
        out_shape=[
            jax.ShapeDtypeStruct((count, HD, size), LOW),
            jax.ShapeDtypeStruct((count, HD, size), F32),
            jax.ShapeDtypeStruct((count, 1, size), F32),
        ],
        compiler_params=pltpu.CompilerParams(
            dimension_semantics=("arbitrary",), vmem_limit_bytes=32 * 2**20
        ),
        cost_estimate=pl.CostEstimate(
            flops=pairs * size * size * HD * 32,
            bytes_accessed=10 * 2**20,
            transcendentals=pairs * size * size,
        ),
        name="attend_forward",
    )(scalars, own, other)


def attend_backward(scalars, own, other, grad, full, log_total):
    count, _, size = grad.shape
    whole = lambda shape: pl.BlockSpec(shape, lambda i, s: (0,) * len(shape))
    pairs = count * (count + 1) // 2
    out_shape = own.shape
    return pl.pallas_call(
        functools.partial(backward_kernel, size=size, count=count),
        grid_spec=pltpu.PrefetchScalarGridSpec(
            num_scalar_prefetch=1,
            grid=(count,),
            in_specs=[
                whole(own.shape),
                whole(other.shape),
                whole(grad.shape),
                whole(full.shape),
                whole(log_total.shape),
            ],
            out_specs=[whole(out_shape)] * 2,
            scratch_shapes=[
                pltpu.VMEM((count, HD, size), LOW),
                pltpu.VMEM((count, HD, size), LOW),
                pltpu.VMEM((count, size, HD), LOW),
                pltpu.VMEM((count, 1, size), F32),
                pltpu.VMEM((count, HD, size), F32),
                pltpu.VMEM((HD, size), F32),
                pltpu.VMEM((HD, size), F32),
            ],
        ),
        out_shape=[jax.ShapeDtypeStruct(out_shape, LOW)] * 2,
        compiler_params=pltpu.CompilerParams(
            dimension_semantics=("arbitrary",), vmem_limit_bytes=32 * 2**20
        ),
        cost_estimate=pl.CostEstimate(
            flops=pairs * size * size * HD * 42,
            bytes_accessed=16 * 2**20,
            transcendentals=pairs * size * size,
        ),
        name="attend_backward",
    )(scalars, own, other, grad, full, log_total)


def place_rows_kernel(order, *refs):
    pieces, out_ref = refs[:-1], refs[-1]
    size = pieces[0].shape[0]
    for index, piece in enumerate(pieces):
        start = pl.multiple_of(order[index] * size, size)
        out_ref[pl.ds(start, size), :] = piece[...].astype(F32)


def place_rows(order, pieces):
    size, width = pieces[0].shape
    total = size * len(pieces)
    step = 512
    return pl.pallas_call(
        place_rows_kernel,
        grid_spec=pltpu.PrefetchScalarGridSpec(
            num_scalar_prefetch=1,
            grid=(width // step,),
            in_specs=[pl.BlockSpec((size, step), lambda i, s: (0, i)) for _ in pieces],
            out_specs=pl.BlockSpec((total, step), lambda i, s: (0, i)),
        ),
        out_shape=jax.ShapeDtypeStruct((total, width), F32),
        compiler_params=pltpu.CompilerParams(vmem_limit_bytes=24 * 2**20),
        cost_estimate=pl.CostEstimate(
            flops=0, bytes_accessed=total * width * 6, transcendentals=0
        ),
        name="place_rows",
    )(order, *pieces)


def place_columns_kernel(order, gain_ref, gate_w_ref, up_w_ref, *refs):
    count = (len(refs) - 3) // 2
    gates, ups = refs[:count], refs[count : 2 * count]
    gate_ref, up_ref, sum_ref = refs[2 * count :]
    size = gates[0].shape[1]
    gain = gain_ref[...]
    total = jnp.zeros((gate_ref.shape[0], size), F32)
    for index in range(count):
        columns = pl.ds(pl.multiple_of(order[index] * size, size), size)
        gate, up = gates[index][...].astype(F32), ups[index][...].astype(F32)
        total += gate * gate_w_ref[:, columns].astype(F32)
        total += up * up_w_ref[:, columns].astype(F32)
        gate_ref[:, columns] = gate * gain
        up_ref[:, columns] = up * gain

    @pl.when(pl.program_id(0) == 0)
    def _():
        sum_ref[...] = jnp.zeros_like(sum_ref)

    sum_ref[...] += jnp.sum(total, 1, keepdims=True)


def place_columns(order, gain, gate_weight, up_weight, gates, ups, shards):
    rows, width = gate_weight.shape
    span = width // shards
    size = span // len(gates)
    wide = pl.BlockSpec((rows, span), lambda i, s: (0, i))
    thin = pl.BlockSpec((rows, 1), lambda i, s: (0, 0))
    pieces = [pl.BlockSpec((rows, size), lambda i, s: (0, i)) for _ in (*gates, *ups)]
    return pl.pallas_call(
        place_columns_kernel,
        grid_spec=pltpu.PrefetchScalarGridSpec(
            num_scalar_prefetch=1,
            grid=(shards,),
            in_specs=[thin, wide, wide, *pieces],
            out_specs=[wide, wide, thin],
        ),
        out_shape=[
            jax.ShapeDtypeStruct((rows, width), F32),
            jax.ShapeDtypeStruct((rows, width), F32),
            jax.ShapeDtypeStruct((rows, 1), F32),
        ],
        compiler_params=pltpu.CompilerParams(
            dimension_semantics=("arbitrary",), vmem_limit_bytes=24 * 2**20
        ),
        cost_estimate=pl.CostEstimate(
            flops=rows * width * 6, bytes_accessed=rows * width * 16, transcendentals=0
        ),
        name="place_columns",
    )(order, gain, gate_weight, up_weight, *gates, *ups)


def place_heads_kernel(gain_ref, query_w, key_w, value_w, all_ref, query_ref, key_ref, value_ref, sum_ref):
    rows = gain_ref.shape[0]
    wide = query_ref.shape[1] // KVH
    gain = gain_ref[...]
    total = jnp.zeros((rows, 4 * HD), F32)
    pieces = [all_ref[i * rows : (i + 1) * rows, :].astype(F32) for i in range(KVH)]
    for start in range(0, KVH, 2):
        value = jnp.concatenate([piece[:, :wide] for piece in pieces[start : start + 2]], 1)
        columns = slice(start * wide, (start + 2) * wide)
        total += value * query_w[:, columns].astype(F32)
        query_ref[:, columns] = value * gain
    for first, weight, out_ref in ((wide, key_w, key_ref), (wide + HD, value_w, value_ref)):
        for start in range(0, KVH, 4):
            value = jnp.concatenate(
                [piece[:, first : first + HD] for piece in pieces[start : start + 4]], 1
            )
            columns = slice(start * HD, (start + 4) * HD)
            total += value * weight[:, columns].astype(F32)
            out_ref[:, columns] = value * gain
    sum_ref[...] = jnp.sum(total, 1, keepdims=True)


def place_heads(gain, query_weight, key_weight, value_weight, pieces):
    weights = (query_weight, key_weight, value_weight)
    rows = gain.shape[0]
    return pl.pallas_call(
        place_heads_kernel,
        out_shape=[jax.ShapeDtypeStruct(weight.shape, F32) for weight in weights]
        + [jax.ShapeDtypeStruct((rows, 1), F32)],
        compiler_params=pltpu.CompilerParams(vmem_limit_bytes=32 * 2**20),
        cost_estimate=pl.CostEstimate(
            flops=rows * 3072 * 4, bytes_accessed=rows * 3072 * 8, transcendentals=0
        ),
        name="place_heads",
    )(gain, *weights, pieces)


def merge_kernel(scalars, kept_ref, came_ref, cosine_ref, sine_ref, out_ref, split_ref):
    lead = scalars[0] == 0
    lines, _, size = split_ref.shape
    for line in range(lines):
        columns = slice(line * size, (line + 1) * size)
        kept = kept_ref[:, columns].astype(F32)
        came = came_ref[:, columns].astype(F32)
        cosine, sine = cosine_ref[:, columns], sine_ref[:, columns]
        joint = kept[HD:] + came[HD:]
        first = jnp.where(lead, kept[:HD], came[:HD])
        second = jnp.where(lead, came[:HD], kept[:HD])
        turned = []
        for value in (first, second, joint[:HD]):
            low, high = value[: HD // 2], value[HD // 2 :]
            turned.append(low * cosine + high * sine)
            turned.append(high * cosine - low * sine)
        turned.append(joint[HD:])
        result = jnp.concatenate([part.astype(LOW) for part in turned], 0)
        out_ref[:, columns] = result
        split_ref[line] = result


def merge(scalars, kept, came, cosine, sine, lines):
    tokens = kept.shape[1]
    whole = lambda value: pl.BlockSpec(value.shape, lambda i, s: (0,) * len(value.shape))
    outs = [
        jax.ShapeDtypeStruct((4 * HD, tokens), LOW),
        jax.ShapeDtypeStruct((lines, 4 * HD, tokens // lines), LOW),
    ]
    return pl.pallas_call(
        merge_kernel,
        grid_spec=pltpu.PrefetchScalarGridSpec(
            num_scalar_prefetch=1,
            grid=(1,),
            in_specs=[whole(value) for value in (kept, came, cosine, sine)],
            out_specs=[whole(value) for value in outs],
        ),
        out_shape=outs,
        compiler_params=pltpu.CompilerParams(vmem_limit_bytes=24 * 2**20),
        cost_estimate=pl.CostEstimate(
            flops=tokens * HD * 24, bytes_accessed=tokens * HD * 30, transcendentals=0
        ),
        name="merge",
    )(scalars, kept, came, cosine, sine)


def pack_kernel(scalars, gain_ref, query_ref, key_ref, value_ref, *outs):
    core = scalars[3]
    gain = gain_ref[...]
    wide = query_ref.shape[1] // KVH
    span = wide + 2 * HD
    for which in range(2):

        @pl.when(core == which)
        def _():
            for line in range(KVH // 2):
                head = 2 * line + which
                value = jnp.concatenate(
                    [
                        query_ref[:, head * wide : (head + 1) * wide].astype(F32),
                        key_ref[:, head * HD : (head + 1) * HD].astype(F32),
                        value_ref[:, head * HD : (head + 1) * HD].astype(F32),
                    ],
                    1,
                )
                place = (line % 2) * span
                outs[line // 2][:, place : place + span] = (value * gain).astype(LOW)


def pack(scalars, gain, query_weight, key_weight, value_weight):
    rows, width = query_weight.shape
    whole = lambda value: pl.BlockSpec(value.shape, lambda i, s: (0, 0))
    weights = (gain, query_weight, key_weight, value_weight)
    outs = [jax.ShapeDtypeStruct((rows, width // 2), LOW)] * 2
    return pl.pallas_call(
        pack_kernel,
        grid_spec=pltpu.PrefetchScalarGridSpec(
            num_scalar_prefetch=1,
            grid=(1,),
            in_specs=[whole(value) for value in weights],
            out_specs=[whole(value) for value in outs],
        ),
        out_shape=outs,
        compiler_params=pltpu.CompilerParams(vmem_limit_bytes=24 * 2**20),
        cost_estimate=pl.CostEstimate(
            flops=rows * width, bytes_accessed=rows * width * 6, transcendentals=0
        ),
        name="pack",
    )(scalars, *weights)


def spread_kernel(scalars, lin_ref, cosine_ref, sine_ref, own_ref, leaving_ref):
    cosine, sine = cosine_ref[...], sine_ref[...]

    def turn(start, factor):
        low = lin_ref[start : start + HD // 2, :]
        high = lin_ref[start + HD // 2 : start + HD, :]
        turned = ((low * cosine - high * sine) * factor, (high * cosine + low * sine) * factor)
        return jnp.concatenate([part.astype(LOW) for part in turned], 0)

    lead = scalars[0] == 0
    first, second = turn(0, HD**-0.5 / LN2), turn(HD, HD**-0.5 / LN2)

    @pl.when(lead)
    def _():
        own_ref[0:HD] = first
        leaving_ref[0:HD] = second

    @pl.when(jnp.logical_not(lead))
    def _():
        own_ref[0:HD] = second
        leaving_ref[0:HD] = first

    key = turn(2 * HD, 1.0)
    value = lin_ref[3 * HD : 4 * HD].astype(LOW)
    for ref in (own_ref, leaving_ref):
        ref[HD : 2 * HD] = key
        ref[2 * HD : 3 * HD] = value


def spread(scalars, lin, cosine, sine):
    tokens = lin.shape[1]
    step = 512
    column = lambda rows: pl.BlockSpec((rows, step), lambda i, s: (0, i))
    return pl.pallas_call(
        spread_kernel,
        grid_spec=pltpu.PrefetchScalarGridSpec(
            num_scalar_prefetch=1,
            grid=(tokens // step,),
            in_specs=[column(4 * HD), column(HD // 2), column(HD // 2)],
            out_specs=[column(3 * HD)] * 2,
        ),
        out_shape=[jax.ShapeDtypeStruct((3 * HD, tokens), LOW)] * 2,
        compiler_params=pltpu.CompilerParams(vmem_limit_bytes=24 * 2**20),
        cost_estimate=pl.CostEstimate(
            flops=tokens * HD * 24, bytes_accessed=tokens * HD * 36, transcendentals=0
        ),
        name="spread",
    )(scalars, lin, cosine, sine)


def swap(value, axis):
    return lax.ppermute(value, axis, [(0, 1), (1, 0)])


def swap_near(value):
    return lax.ppermute(value, "z", [(0, 1), (1, 0), (2, 3), (3, 2)])


def swap_far(value):
    return lax.ppermute(value, "z", [(0, 2), (2, 0), (1, 3), (3, 1)])


def tie(*values):
    return lax.optimization_barrier(values)


def in_order(place, own, other):
    return (jnp.where(place == 0, own, other), jnp.where(place == 0, other, own))


def both(place, own, other):
    return jnp.concatenate(in_order(place, own, other), 0)


def spread_out(value, first, second):
    other = swap(value, first)
    pair = jnp.stack(in_order(lax.axis_index(first), value, other))
    return pair, swap(pair, second)


def placed(pair, other, second):
    pairs = in_order(lax.axis_index(second), pair, other)
    grid = jnp.stack(pairs, 0 if second == "y" else 1)
    return grid.reshape(-1, *grid.shape[3:])


def pick(array, axis, at):
    return lax.dynamic_index_in_dim(array, at, axis, keepdims=False)


def halve(value, axis, along=0):
    at = lax.axis_index(axis)
    return pick(value, along, at), swap(pick(value, along, 1 - at), axis)


def halve_x(value):
    return halve(value.reshape(2, 2, -1, value.shape[-1]), "x", 1)


def halve_y(value):
    return halve(value.reshape(2, 2, -1, value.shape[-1]), "y", 0)


def fast_body(
    tokens,
    positions,
    first_gain,
    query_weight,
    key_weight,
    value_weight,
    output_weight,
    second_gain,
    gate_weight,
    up_weight,
    down_weight,
    cotangent,
):
    seq = ("z", "c")
    fsdp = ("y", "x")
    z, core, half = lax.axis_index("z"), lax.axis_index("c"), lax.axis_index("x")
    near = z % 2
    lines = lax.axis_size("z")
    seq_count = 2 * lines
    shards = lax.axis_size("y") * 2
    spot = z * 2 + core
    quarter = near * 2 + core
    rows = tokens[0]
    count, width = rows.shape
    chip_count = 2 * count
    half_len = count * seq_count
    seq_len = 2 * half_len

    begins = jnp.where(
        (spot == 0) & (half == 0),
        count - 1 - positions[0, count - 1],
        half * half_len + spot * count - positions[0, 0],
    )
    ends = begins + (seq_len - count)
    scalars = jnp.stack([half, begins, ends, core]).astype(jnp.int32)

    gain_one = first_gain.astype(F32)[:, None]
    gain_two = second_gain.astype(F32)[:, None]

    def row_scale(value):
        return lax.rsqrt(jnp.mean(value * value, -1, keepdims=True) + EPS)

    take = functools.partial(lax.dynamic_slice_in_dim, axis=1)
    take_rows = functools.partial(lax.dynamic_slice_in_dim, axis=0)
    gather = lambda value, axes: lax.all_gather(value, axes, axis=0, tiled=True)
    own_rows = rows.astype(F32)
    own_unit_scale = row_scale(own_rows)
    own_unit = own_rows * own_unit_scale
    units = gather(own_unit.astype(LOW), seq)
    wide = QH // KVH * HD
    qkv_shard = (
        jnp.concatenate(
            [
                take(query_weight, spot * wide, wide),
                take(key_weight, spot * HD, HD),
                take(value_weight, spot * HD, HD),
            ],
            1,
        ).astype(F32)
        * gain_one
    ).astype(LOW)
    out_rows = output_weight.shape[0] // 2
    out_shard = take_rows(output_weight, core * out_rows, out_rows)
    piece = down_weight.shape[0] // 4
    down_shard = take_rows(down_weight, quarter * piece, piece)
    gate_shard, up_shard = (
        (
            jnp.concatenate(
                [
                    take(weight, shard * 4 * piece + quarter * piece, piece)
                    for shard in range(shards)
                ],
                1,
            ).astype(F32)
            * gain_two
        ).astype(LOW)
        for weight in (gate_weight, up_weight)
    )
    side = lax.axis_index("y")
    qkv_pair = jnp.stack(in_order(half, qkv_shard, swap(qkv_shard, "x")))
    gate_pair = jnp.stack(in_order(half, gate_shard, swap(gate_shard, "x")))
    up_pair = jnp.stack(in_order(side, up_shard, swap(up_shard, "y")))
    qkv_pair, gate_pair, up_pair = tie(qkv_pair, gate_pair, up_pair)
    qkv_w = placed(qkv_pair, swap(qkv_pair, "y"), "y")
    gate_pair, up_pair = (gate_pair, swap(gate_pair, "y")), (up_pair, swap(up_pair, "x"))

    place = half * half_len + jnp.arange(half_len, dtype=jnp.int32)
    start = jnp.where(place >= ends, ends, jnp.where(place >= begins, begins, 0))
    freq = THETA ** (-(jnp.arange(HD // 2, dtype=F32) * 2.0 / HD))
    angle = freq[:, None] * (place - start).astype(F32)[None, :]
    cosine, sine = jnp.cos(angle), jnp.sin(angle)
    chip_rows = both(core, rows, swap(rows, "c"))
    units, own_cot, chip_rows = tie(units, cotangent[0], chip_rows)
    own, leaving = spread(scalars, contract(qkv_w, units, 0, 1), cosine, sine)

    near_cot = swap_near(own_cot)
    other, out_shard, down_shard, near_cot, chip_cot, gate_pair, up_pair = tie(
        swap(leaving, "x"),
        out_shard,
        down_shard,
        near_cot,
        both(core, own_cot, swap(own_cot, "c")),
        gate_pair,
        up_pair,
    )
    out_w = gather(out_shard, fsdp)
    down_w = gather(down_shard, fsdp)
    near_other = swap(near_cot, "c")
    head_low, head_full, log_total = attend_forward(scalars, own, other, chip_count)
    exchange = lambda value: lax.all_to_all(
        value, ("z", "x"), split_axis=0, concat_axis=0, tiled=True
    )
    head_low, near_other = tie(head_low, near_other)
    lead_shard, tail_shard = pack(scalars, gain_one, query_weight, key_weight, value_weight)
    heads, gate_w, up_w, near_cot, lead_shard = tie(
        exchange(head_low),
        placed(*gate_pair, "y"),
        placed(*up_pair, "x"),
        jnp.concatenate([near_cot, near_other], 0),
        lead_shard,
    )
    lead_w = gather(lead_shard, fsdp)
    heads = heads.reshape(QH // 2 * HD, chip_count)

    mine_of = lambda value: take_rows(value, core * count, count)
    theirs_of = lambda value: take_rows(value, (1 - core) * count, count)
    branch = contract(heads, out_w, 0, 0).astype(LOW)
    middle = chip_rows.astype(F32) + (branch.astype(F32) + swap(branch, "c").astype(F32))
    middle_scale = row_scale(middle)
    chip_unit = middle * middle_scale
    own_middle, own_scale, own_middle_unit = (
        mine_of(middle),
        mine_of(middle_scale),
        mine_of(chip_unit),
    )
    chip_unit = chip_unit.astype(LOW)
    near_unit = swap_near(mine_of(chip_unit))

    def feed(unit):
        gate, upper = contract(unit, gate_w, 1, 0), contract(unit, up_w, 1, 0)
        sigma = jax.nn.sigmoid(gate)
        silu = gate * sigma
        return (silu * upper).astype(LOW), (gate, upper, sigma, silu)

    def feed_back(cot, kept):
        gate, upper, sigma, silu = kept
        grad_hidden = contract(cot, down_w, 1, 1)
        gate_low = (grad_hidden * upper * sigma * (1.0 + gate * (1.0 - sigma))).astype(LOW)
        upper_low = (grad_hidden * silu).astype(LOW)
        part = contract(gate_low, gate_w, 1, 1) + contract(upper_low, up_w, 1, 1)
        return gate_low, upper_low, part

    def chip_sum(chip_part, near_part):
        near_sum = near_part[:count].astype(F32) + swap(near_part[count:].astype(LOW), "c")
        own_sum = mine_of(chip_part).astype(F32) + swap(theirs_of(chip_part).astype(LOW), "c")
        return own_sum, near_sum.astype(LOW)

    stack = lambda first, second: jnp.concatenate([first, second], 0)
    scatter = lambda value: lax.psum_scatter(value, fsdp, scatter_dimension=0, tiled=True)
    chip_hidden, chip_kept = feed(chip_unit)
    near_unit, chip_hidden = tie(near_unit, chip_hidden)
    near_unit = jnp.concatenate([near_unit, swap(near_unit, "c")], 0)
    near_hidden, near_kept = feed(near_unit)
    down_part = contract(
        stack(chip_hidden, near_hidden), stack(chip_cot, near_cot), 0, 0
    ).astype(LOW)
    feed_own, feed_near = chip_sum(
        contract(chip_hidden, down_w, 1, 0), contract(near_hidden, down_w, 1, 0)
    )
    near_cot, down_part, feed_near = tie(near_cot, down_part, feed_near)
    feed_near = swap_near(feed_near)
    down_grad = scatter(down_part)
    near_gate, near_upper, near_part = feed_back(near_cot, near_kept)
    chip_gate, chip_upper, chip_part = feed_back(chip_cot, chip_kept)
    grad_two, near_sum = chip_sum(chip_part, near_part)

    def halves_first(value):
        cut = value.shape[-1] // 2
        return halve_x(value[:, :cut]), halve_y(value[:, cut:])

    def halves_second(firsts):
        return halve(sum(firsts[0]), "y"), halve(sum(firsts[1]), "x")

    def halves_end(seconds):
        return jnp.concatenate([sum(seconds[0]), sum(seconds[1])], 1)

    near_sum, near_gate, near_upper = tie(near_sum, near_gate, near_upper)
    grad_two = grad_two + swap_near(near_sum).astype(F32)
    all_units = stack(chip_unit, near_unit)
    gate_part = contract(all_units, stack(chip_gate, near_gate), 0, 0).astype(LOW)
    gate_part, feed_near = tie(gate_part, feed_near)
    gate_grad = scatter(gate_part)
    up_part = contract(all_units, stack(chip_upper, near_upper), 0, 0).astype(LOW)
    up_grad = scatter(up_part)
    grad_two, up_part, lead_w = tie(grad_two, up_part, lead_w)
    grad_middle = own_cot.astype(F32) + own_scale * (
        grad_two - own_middle_unit * jnp.mean(grad_two * own_middle_unit, -1, keepdims=True)
    )
    own_branch = grad_middle.astype(LOW)
    grad_branch = both(core, own_branch, swap(own_branch, "c"))
    grad_heads = contract(out_w, grad_branch, 1, 1).astype(LOW)
    grad_heads, grad_branch, down_grad = tie(grad_heads, grad_branch, down_grad)
    down_far = swap_far(down_grad)

    output_part = contract(heads, grad_branch, 1, 0).astype(LOW)
    output_grad = scatter(output_part)
    grad_head, output_part, gate_grad, down_far = tie(
        exchange(grad_heads.reshape(2 * lines, HD, chip_count)),
        output_part,
        gate_grad,
        down_far,
    )

    gate_far = swap_far(gate_grad)
    down_sum = down_grad + down_far
    down_near = swap_near(down_sum)
    kept, leaving = attend_backward(scalars, own, other, grad_head, head_full, log_total)
    kept, leaving, gate_far, down_near, up_grad, tail_shard = tie(
        kept, leaving, gate_far, down_near, up_grad, tail_shard
    )
    tail_w = gather(tail_shard, fsdp)

    up_far = swap_far(up_grad)
    gate_sum = gate_grad + gate_far
    gate_near = swap_near(gate_sum)
    block_output = (own_middle + feed_own + feed_near.astype(F32)).astype(LOW)[None]
    came, up_far, gate_near, output_grad, block_output = tie(
        swap(leaving, "x"), up_far, gate_near, output_grad, block_output
    )

    qkv_low, by_line = merge(scalars, kept, came, cosine, sine, lines)
    token_grads = lax.all_to_all(by_line, "z", split_axis=0, concat_axis=0, tiled=True)
    qkv_part = contract(units, qkv_low, 0, 1).astype(LOW).reshape(shards, 2, -1, 4 * HD)
    qkv_first = halve_x(qkv_part[:, 0]), halve_y(qkv_part[:, 1])
    qkv_second = halves_second(qkv_first)
    qkv_grad = jnp.concatenate([sum(qkv_second[0]), sum(qkv_second[1])], 0)
    output_came = swap_near(output_grad)
    token_grads, qkv_grad, output_came = tie(token_grads, qkv_grad, output_came)
    all_qkv = gather(qkv_grad, seq)
    output_sum = output_grad + output_came
    output_far = swap_far(output_sum)
    up_sum = up_grad + up_far
    up_near = swap_near(up_sum)

    token_grads = token_grads.reshape(-1, chip_count)
    split = lead_w.shape[1]
    grad_one = contract(token_grads[:split], lead_w, 0, 1) + contract(
        token_grads[split:], tail_w, 0, 1
    )
    grad_one = mine_of(grad_one) + swap(theirs_of(grad_one).astype(LOW), "c").astype(F32)
    grad_rows = own_unit_scale * (
        grad_one - own_unit * jnp.mean(grad_one * own_unit, -1, keepdims=True)
    )
    input_grad = (grad_middle + grad_rows).astype(LOW)[None]

    def four(value, near_value):
        return value, swap(value, "c"), near_value, swap(near_value, "c")

    order = jnp.stack([quarter, quarter ^ 1, quarter ^ 2, quarter ^ 3]).astype(jnp.int32)
    core_order = jnp.stack([core, 1 - core]).astype(jnp.int32)
    down_total = place_rows(order, four(down_sum, down_near))
    gate_total, up_total, second_gain_grad = place_columns(
        order, gain_two, gate_weight, up_weight, four(gate_sum, gate_near), four(up_sum, up_near), shards
    )
    output_far, second_gain_grad = tie(output_far, second_gain_grad)
    output_own = output_sum + output_far
    output_total = place_rows(core_order, (output_own, swap(output_own, "c")))
    query_grad, key_grad, value_grad, first_gain_grad = place_heads(
        gain_one, query_weight, key_weight, value_weight, all_qkv
    )
    return (
        block_output,
        input_grad,
        first_gain_grad[:, 0],
        query_grad,
        key_grad,
        value_grad,
        output_total,
        second_gain_grad[:, 0],
        gate_total,
        up_total,
        down_total,
    )


def fast_solution(mesh):
    seq_count, shard_count = mesh.devices.shape
    fine = Mesh(
        mesh.devices.reshape(seq_count // 2, 2, shard_count // 2, 2), ("z", "c", "y", "x")
    )
    seq, fsdp = ("z", "c"), ("y", "x")
    matrix = P(fsdp, None)
    return jax.shard_map(
        fast_body,
        mesh=fine,
        in_specs=(
            P(fsdp, seq, None),
            P(fsdp, seq),
            P(fsdp),
            matrix,
            matrix,
            matrix,
            matrix,
            P(fsdp),
            matrix,
            matrix,
            matrix,
            P(fsdp, seq, None),
        ),
        out_specs=(
            P(fsdp, seq, None),
            P(fsdp, seq, None),
            P(fsdp),
            matrix,
            matrix,
            matrix,
            matrix,
            P(fsdp),
            matrix,
            matrix,
            matrix,
        ),
        check_vma=False,
    )


def solution(mesh):
    shape = dict(mesh.shape)
    if shape["seq"] == KVH and shape["fsdp"] == 4:
        return fast_solution(mesh)
    return plain_solution(mesh)


def shifted(value, axis, steps):
    count = lax.axis_size(axis)
    first, last = (max(0, -steps), min(count, count - steps))
    return lax.ppermute(value, axis, [(source, source + steps) for source in range(first, last)])


def rope_tables(position_rows):
    freq = THETA ** (-(jnp.arange(HD // 2, dtype=jnp.float32) * 2.0 / HD))
    angle = position_rows.astype(jnp.float32)[:, None] * freq[None, :]
    cosine = jnp.cos(angle)
    sine = jnp.sin(angle)
    return (jnp.concatenate([cosine, cosine], -1), jnp.concatenate([sine, sine], -1))


def rotate(values, cosine, sine):
    half = HD // 2
    turned = jnp.concatenate([-values[..., half:], values[..., :half]], -1)
    return values * cosine[:, None, :] + turned * sine[:, None, :]


def rotate_back(grads, cosine, sine):
    half = HD // 2
    scaled = grads * sine[:, None, :]
    turned = jnp.concatenate([scaled[..., half:], -scaled[..., :half]], -1)
    return grads * cosine[:, None, :] + turned


def norm_forward(rows, gain):
    scale = lax.rsqrt(jnp.mean(rows * rows, -1, keepdims=True) + EPS)
    unit = rows * scale
    return (unit * gain, unit, scale)


def norm_backward(grad_out, unit, scale, gain):
    grad_unit = grad_out * gain
    gain_grad = jnp.sum(grad_out * unit, 0)
    grad_rows = scale * (grad_unit - unit * jnp.mean(grad_unit * unit, -1, keepdims=True))
    return (grad_rows, gain_grad)


def plain_body(
    tokens,
    positions,
    first_gain,
    query_weight,
    key_weight,
    value_weight,
    output_weight,
    second_gain,
    gate_weight,
    up_weight,
    down_weight,
    cotangent,
):
    seq_count = lax.axis_size("seq")
    local_rows = tokens[0]
    token_count = local_rows.shape[0]
    half_len = token_count * seq_count
    rows_float = local_rows.astype(jnp.float32)
    gain_one, wq_full, wk_full, wv_full, wo_full = (
        lax.all_gather(first_gain, "fsdp", axis=0, tiled=True),
        lax.all_gather(query_weight, "fsdp", axis=0, tiled=True),
        lax.all_gather(key_weight, "fsdp", axis=0, tiled=True),
        lax.all_gather(value_weight, "fsdp", axis=0, tiled=True),
        lax.all_gather(output_weight, "fsdp", axis=0, tiled=True),
    )
    gain_one = gain_one.astype(jnp.float32)
    normed_one, unit_one, scale_one = norm_forward(rows_float, gain_one)
    normed_low = normed_one.astype(jnp.bfloat16)
    cosine, sine = rope_tables(positions[0])
    query_lin = jnp.dot(normed_low, wq_full, preferred_element_type=jnp.float32).reshape(
        token_count, QH, HD
    )
    key_lin = jnp.dot(normed_low, wk_full, preferred_element_type=jnp.float32).reshape(
        token_count, KVH, HD
    )
    value_lin = jnp.dot(normed_low, wv_full, preferred_element_type=jnp.float32).reshape(
        token_count, KVH, HD
    )
    query_rows = rotate(query_lin, cosine, sine).astype(jnp.bfloat16)
    key_rows = rotate(key_lin, cosine, sine).astype(jnp.bfloat16)
    value_rows = value_lin.astype(jnp.bfloat16)
    repeat = max(1, seq_count // KVH)
    if repeat > 1:
        key_rows = jnp.repeat(key_rows, repeat, axis=1)
        value_rows = jnp.repeat(value_rows, repeat, axis=1)
    query_heads, key_heads, value_heads = (
        lax.all_to_all(query_rows, "seq", split_axis=1, concat_axis=0, tiled=True),
        lax.all_to_all(key_rows, "seq", split_axis=1, concat_axis=0, tiled=True),
        lax.all_to_all(value_rows, "seq", split_axis=1, concat_axis=0, tiled=True),
    )
    head_count = query_heads.shape[1]
    pair_count = key_heads.shape[1]
    group = head_count // pair_count
    half_positions = lax.all_gather(positions[0], "seq", axis=0, tiled=True)
    key_prior, value_prior = shifted((key_heads, value_heads), "fsdp", 1)
    key_all = jnp.concatenate([key_prior, key_heads], 0)
    value_all = jnp.concatenate([value_prior, value_heads], 0)
    half_index = lax.axis_index("fsdp") % 2
    key_index = (half_index - 1) * half_len + jnp.arange(2 * half_len, dtype=jnp.int32)
    row_index = half_index * half_len + jnp.arange(half_len, dtype=jnp.int32)
    row_start = row_index - half_positions
    block = min(512, half_len)
    count = half_len // block
    factor = HD ** (-0.5)
    query_blocks = query_heads.reshape(count, block, pair_count, group, HD)
    index_blocks = row_index.reshape(count, block)
    start_blocks = row_start.reshape(count, block)

    def block_scores(query_block, index_block, start_block):
        scores = (
            jnp.einsum("bkgd,tkd->kgbt", query_block, key_all, preferred_element_type=jnp.float32)
            * factor
        )
        visible = (key_index[None, :] >= start_block[:, None]) & (
            key_index[None, :] <= index_block[:, None]
        )
        return jnp.where(visible, scores, -1e30)

    def forward_block(items):
        query_block, index_block, start_block = items
        scores = block_scores(query_block, index_block, start_block)
        top = jnp.max(scores, -1, keepdims=True)
        expo = jnp.exp(scores - top)
        total = jnp.sum(expo, -1, keepdims=True)
        probs_low = (expo / total).astype(jnp.bfloat16)
        mixed = jnp.einsum(
            "kgbt,tkd->bkgd", probs_low, value_all, preferred_element_type=jnp.float32
        )
        return (mixed.reshape(block, head_count, HD).astype(jnp.bfloat16), top + jnp.log(total))

    head_blocks, log_totals = lax.map(forward_block, (query_blocks, index_blocks, start_blocks))
    head_out = head_blocks.reshape(half_len, head_count, HD)
    token_heads = lax.all_to_all(head_out, "seq", split_axis=0, concat_axis=1, tiled=True)
    heads_flat = token_heads.reshape(token_count, QH * HD)
    middle = rows_float + jnp.dot(heads_flat, wo_full, preferred_element_type=jnp.float32)
    gain_two, wg_full, wu_full, wd_full = (
        lax.all_gather(second_gain, "fsdp", axis=0, tiled=True),
        lax.all_gather(gate_weight, "fsdp", axis=0, tiled=True),
        lax.all_gather(up_weight, "fsdp", axis=0, tiled=True),
        lax.all_gather(down_weight, "fsdp", axis=0, tiled=True),
    )
    gain_two = gain_two.astype(jnp.float32)
    normed_two, unit_two, scale_two = norm_forward(middle, gain_two)
    normed_two_low = normed_two.astype(jnp.bfloat16)
    gate = jnp.dot(normed_two_low, wg_full, preferred_element_type=jnp.float32)
    upper = jnp.dot(normed_two_low, wu_full, preferred_element_type=jnp.float32)
    hidden = (jax.nn.silu(gate) * upper).astype(jnp.bfloat16)
    result = middle + jnp.dot(hidden, wd_full, preferred_element_type=jnp.float32)
    block_output = result.astype(jnp.bfloat16)[None]
    grad_low = cotangent[0]
    grad_rows = grad_low.astype(jnp.float32)
    down_grad = jnp.einsum("tf,td->fd", hidden, grad_low, preferred_element_type=jnp.float32)
    grad_hidden = jnp.einsum("td,fd->tf", grad_low, wd_full, preferred_element_type=jnp.float32)
    sigma = jax.nn.sigmoid(gate)
    gate_low = (grad_hidden * upper * sigma * (1.0 + gate * (1.0 - sigma))).astype(jnp.bfloat16)
    upper_low = (grad_hidden * gate * sigma).astype(jnp.bfloat16)
    gate_grad = jnp.einsum(
        "td,tf->df", normed_two_low, gate_low, preferred_element_type=jnp.float32
    )
    up_grad = jnp.einsum("td,tf->df", normed_two_low, upper_low, preferred_element_type=jnp.float32)
    grad_normed_two = jnp.einsum(
        "tf,df->td", gate_low, wg_full, preferred_element_type=jnp.float32
    ) + jnp.einsum("tf,df->td", upper_low, wu_full, preferred_element_type=jnp.float32)
    grad_middle_norm, second_gain_grad = norm_backward(
        grad_normed_two, unit_two, scale_two, gain_two
    )
    grad_middle = grad_rows + grad_middle_norm
    grad_branch = grad_middle.astype(jnp.bfloat16)
    output_grad = jnp.einsum(
        "tc,td->cd", heads_flat, grad_branch, preferred_element_type=jnp.float32
    )
    grad_heads = (
        jnp.einsum("td,cd->tc", grad_branch, wo_full, preferred_element_type=jnp.float32)
        .astype(jnp.bfloat16)
        .reshape(token_count, QH, HD)
    )
    grad_head_rows = lax.all_to_all(grad_heads, "seq", split_axis=1, concat_axis=0, tiled=True)
    grad_blocks = grad_head_rows.reshape(count, block, pair_count, group, HD)

    def backward_block(carry, items):
        key_acc, value_acc = carry
        query_block, index_block, start_block, grad_block, log_block = items
        scores = block_scores(query_block, index_block, start_block)
        probs = jnp.exp(scores - log_block)
        probs_low = probs.astype(jnp.bfloat16)
        grad_probs = jnp.einsum(
            "bkgd,tkd->kgbt", grad_block, value_all, preferred_element_type=jnp.float32
        )
        grad_scores = (
            probs * (grad_probs - jnp.sum(probs * grad_probs, -1, keepdims=True))
        ).astype(jnp.bfloat16)
        query_grad_block = (
            jnp.einsum("kgbt,tkd->bkgd", grad_scores, key_all, preferred_element_type=jnp.float32)
            * factor
        )
        key_acc = (
            key_acc
            + jnp.einsum(
                "kgbt,bkgd->tkd", grad_scores, query_block, preferred_element_type=jnp.float32
            )
            * factor
        )
        value_acc = value_acc + jnp.einsum(
            "kgbt,bkgd->tkd", probs_low, grad_block, preferred_element_type=jnp.float32
        )
        return ((key_acc, value_acc), query_grad_block.reshape(block, head_count, HD))

    empty = jnp.zeros((2 * half_len, pair_count, HD), jnp.float32)
    (key_acc, value_acc), query_grad_blocks = lax.scan(
        backward_block,
        (empty, empty),
        (query_blocks, index_blocks, start_blocks, grad_blocks, log_totals),
    )
    key_back, value_back = (
        shifted(key_acc[:half_len].astype(jnp.bfloat16), "fsdp", -1).astype(jnp.float32),
        shifted(value_acc[:half_len].astype(jnp.bfloat16), "fsdp", -1).astype(jnp.float32),
    )
    key_local = key_acc[half_len:] + key_back
    value_local = value_acc[half_len:] + value_back
    query_grad_heads = query_grad_blocks.reshape(half_len, head_count, HD)
    grad_query_tok, grad_key_tok, grad_value_tok = (
        lax.all_to_all(
            query_grad_heads.astype(jnp.bfloat16), "seq", split_axis=0, concat_axis=1, tiled=True
        ).astype(query_grad_heads.dtype),
        lax.all_to_all(
            key_local.astype(jnp.bfloat16), "seq", split_axis=0, concat_axis=1, tiled=True
        ).astype(key_local.dtype),
        lax.all_to_all(
            value_local.astype(jnp.bfloat16), "seq", split_axis=0, concat_axis=1, tiled=True
        ).astype(value_local.dtype),
    )
    if repeat > 1:
        grad_key_tok = grad_key_tok.reshape(token_count, KVH, repeat, HD).sum(2)
        grad_value_tok = grad_value_tok.reshape(token_count, KVH, repeat, HD).sum(2)
    query_lin_grad = (
        rotate_back(grad_query_tok, cosine, sine).astype(jnp.bfloat16).reshape(token_count, QH * HD)
    )
    key_lin_grad = (
        rotate_back(grad_key_tok, cosine, sine).astype(jnp.bfloat16).reshape(token_count, KVH * HD)
    )
    value_lin_grad = grad_value_tok.astype(jnp.bfloat16).reshape(token_count, KVH * HD)
    query_grad = jnp.einsum(
        "td,tc->dc", normed_low, query_lin_grad, preferred_element_type=jnp.float32
    )
    key_grad = jnp.einsum("td,tc->dc", normed_low, key_lin_grad, preferred_element_type=jnp.float32)
    value_grad = jnp.einsum(
        "td,tc->dc", normed_low, value_lin_grad, preferred_element_type=jnp.float32
    )
    grad_normed_one = jnp.einsum(
        "tc,dc->td", query_lin_grad, wq_full, preferred_element_type=jnp.float32
    )
    grad_normed_one = grad_normed_one + jnp.einsum(
        "tc,dc->td", key_lin_grad, wk_full, preferred_element_type=jnp.float32
    )
    grad_normed_one = grad_normed_one + jnp.einsum(
        "tc,dc->td", value_lin_grad, wv_full, preferred_element_type=jnp.float32
    )
    grad_rows_one, first_gain_grad = norm_backward(grad_normed_one, unit_one, scale_one, gain_one)
    input_grad = (grad_middle + grad_rows_one).astype(jnp.bfloat16)[None]
    pieces = (
        lax.psum_scatter(
            first_gain_grad.astype(jnp.bfloat16), "fsdp", scatter_dimension=0, tiled=True
        ).astype(jnp.float32),
        lax.psum_scatter(
            query_grad.astype(jnp.bfloat16), "fsdp", scatter_dimension=0, tiled=True
        ).astype(jnp.float32),
        lax.psum_scatter(
            key_grad.astype(jnp.bfloat16), "fsdp", scatter_dimension=0, tiled=True
        ).astype(jnp.float32),
        lax.psum_scatter(
            value_grad.astype(jnp.bfloat16), "fsdp", scatter_dimension=0, tiled=True
        ).astype(jnp.float32),
        lax.psum_scatter(
            output_grad.astype(jnp.bfloat16), "fsdp", scatter_dimension=0, tiled=True
        ).astype(jnp.float32),
        lax.psum_scatter(
            second_gain_grad.astype(jnp.bfloat16), "fsdp", scatter_dimension=0, tiled=True
        ).astype(jnp.float32),
        lax.psum_scatter(
            gate_grad.astype(jnp.bfloat16), "fsdp", scatter_dimension=0, tiled=True
        ).astype(jnp.float32),
        lax.psum_scatter(
            up_grad.astype(jnp.bfloat16), "fsdp", scatter_dimension=0, tiled=True
        ).astype(jnp.float32),
        lax.psum_scatter(
            down_grad.astype(jnp.bfloat16), "fsdp", scatter_dimension=0, tiled=True
        ).astype(jnp.float32),
    )
    shares = (
        lax.psum(pieces[0].astype(jnp.bfloat16), "seq").astype(jnp.float32),
        lax.psum(pieces[1].astype(jnp.bfloat16), "seq").astype(jnp.float32),
        lax.psum(pieces[2].astype(jnp.bfloat16), "seq").astype(jnp.float32),
        lax.psum(pieces[3].astype(jnp.bfloat16), "seq").astype(jnp.float32),
        lax.psum(pieces[4].astype(jnp.bfloat16), "seq").astype(jnp.float32),
        lax.psum(pieces[5].astype(jnp.bfloat16), "seq").astype(jnp.float32),
        lax.psum(pieces[6].astype(jnp.bfloat16), "seq").astype(jnp.float32),
        lax.psum(pieces[7].astype(jnp.bfloat16), "seq").astype(jnp.float32),
        lax.psum(pieces[8].astype(jnp.bfloat16), "seq").astype(jnp.float32),
    )
    return (
        block_output,
        input_grad,
        shares[0],
        shares[1],
        shares[2],
        shares[3],
        shares[4],
        shares[5],
        shares[6],
        shares[7],
        shares[8],
    )


def plain_solution(mesh):
    placed = (
        P("fsdp", "seq", None),
        P("fsdp", "seq"),
        P("fsdp"),
        P("fsdp", None),
        P("fsdp", None),
        P("fsdp", None),
        P("fsdp", None),
        P("fsdp"),
        P("fsdp", None),
        P("fsdp", None),
        P("fsdp", None),
        P("fsdp", "seq", None),
    )
    return jax.shard_map(
        plain_body,
        mesh=mesh,
        in_specs=placed,
        out_specs=(
            P("fsdp", "seq", None),
            P("fsdp", "seq", None),
            P("fsdp"),
            P("fsdp", None),
            P("fsdp", None),
            P("fsdp", None),
            P("fsdp", None),
            P("fsdp"),
            P("fsdp", None),
            P("fsdp", None),
            P("fsdp", None),
        ),
        check_vma=False,
    )
```

```python
import functools
import math

import jax
import jax.numpy as jnp
from jax import lax
from jax.experimental import pallas as pl
from jax.experimental.pallas import tpu as pltpu
from jax.sharding import Mesh
from jax.sharding import PartitionSpec as P

QH = 16
KVH = 8
HD = 96


THETA = 100000.0
EPS = 1e-05
LOW = jnp.bfloat16
F32 = jnp.float32
NEG = -1e30
LN2 = math.log(2.0)


def contract(left, right, left_axis, right_axis):
    return lax.dot_general(
        left, right, (((left_axis,), (right_axis,)), ((), ())), preferred_element_type=F32
    )


def visible(first, second, query_block, key_block, size):
    key = key_block * size + lax.broadcasted_iota(jnp.int32, (size, size), 0)
    query = query_block * size + lax.broadcasted_iota(jnp.int32, (1, size), 1)
    start = jnp.where(query >= second, second, jnp.where(query >= first, first, 0))
    return (key >= start) & (key <= query)


def slot_of(block, count):
    return (block % (count // 2)) * 2 + block // (count // 2)


def forward_kernel(
    scalars,
    own_ref,
    other_ref,
    low_ref,
    full_ref,
    log_ref,
    query_s,
    key_s,
    value_s,
    top_s,
    total_s,
    mixed_s,
    *,
    size,
    count,
):
    half = scalars[0]
    first = scalars[1]
    second = scalars[2]
    here = pl.program_id(0)
    per_half = count // 2

    @pl.when(here == 0)
    def _():
        for ref, side in ((own_ref, half), (other_ref, 1 - half)):
            for step in range(per_half):
                block = side * per_half + step
                columns = slice(step * size, (step + 1) * size)
                query_s[block] = ref[0:HD, columns]
                key_s[block] = ref[HD : 2 * HD, columns].T
                value_s[block] = ref[2 * HD : 3 * HD, columns]

    query = query_s[here]
    top_s[...] = jnp.full_like(top_s, NEG)
    total_s[...] = jnp.zeros_like(total_s)
    mixed_s[...] = jnp.zeros_like(mixed_s)

    def add_block(block, masked):
        scores = contract(key_s[block], query, 1, 0)
        if masked:
            scores = jnp.where(visible(first, second, here, block, size), scores, NEG)
        old_top = top_s[...]
        top = jnp.maximum(old_top, jnp.max(scores, 0, keepdims=True))
        expo = jnp.exp2(scores - top)
        scale = jnp.exp2(old_top - top)
        top_s[...] = top
        total_s[...] = total_s[...] * scale + jnp.sum(expo, 0, keepdims=True)
        mixed_s[...] = mixed_s[...] * scale + contract(value_s[block], expo.astype(LOW), 1, 0)

    last = count - 1

    @pl.loop(1, jnp.where(here == last, 1, here))
    def _(block):
        add_block(block, False)

    @pl.loop(0, jnp.where(here == last, count, jnp.minimum(here + 1, 2)))
    def _(step):
        add_block(jnp.where(here == last, step, step * here), True)

    total = total_s[...]
    result = mixed_s[...] / total
    full_ref[0] = result
    low_ref[0] = result.astype(LOW)
    log_ref[0] = top_s[...] + jnp.log2(total)


def backward_kernel(
    scalars,
    own_ref,
    other_ref,
    grad_ref,
    full_ref,
    log_ref,
    kept_ref,
    leaving_ref,
    query_s,
    key_s,
    value_s,
    delta_s,
    query_grad_s,
    key_grad_s,
    value_grad_s,
    *,
    size,
    count,
):
    half = scalars[0]
    first = scalars[1]
    second = scalars[2]
    here = pl.program_id(0)
    per_half = count // 2

    @pl.when(here == 0)
    def _():
        for ref, side in ((own_ref, half), (other_ref, 1 - half)):
            for step in range(per_half):
                block = side * per_half + step
                columns = slice(step * size, (step + 1) * size)
                query_s[block] = ref[0:HD, columns]
                key_s[block] = ref[HD : 2 * HD, columns]
                value_s[block] = ref[2 * HD : 3 * HD, columns].T
        for block in range(count):
            delta_s[block] = jnp.sum(
                grad_ref[slot_of(block, count)].astype(F32) * full_ref[block], 0, keepdims=True
            )
        query_grad_s[...] = jnp.zeros_like(query_grad_s)

    key_grad_s[...] = jnp.zeros_like(key_grad_s)
    value_grad_s[...] = jnp.zeros_like(value_grad_s)
    key = key_s[here]
    key_rows = key.T
    value_rows = value_s[here]

    def add_block(block, masked):
        query = query_s[block]
        grad = grad_ref[slot_of(block, count)]
        scores = contract(key_rows, query, 1, 0)
        if masked:
            scores = jnp.where(visible(first, second, block, here, size), scores, NEG)
        probs = jnp.exp2(scores - log_ref[block])
        grad_probs = contract(value_rows, grad, 1, 0)
        grad_scores = (probs * (grad_probs - delta_s[block])).astype(LOW)
        value_grad_s[...] += contract(grad, probs.astype(LOW), 1, 1)
        key_grad_s[...] += contract(query, grad_scores, 1, 1)
        query_grad_s[block] += contract(key, grad_scores, 1, 0)

    last = count - 1

    @pl.loop(here + 1, jnp.where(here == 0, 1, last))
    def _(block):
        add_block(block, False)

    @pl.loop(0, jnp.where(here == 0, count, jnp.where(here == last, 1, 2)))
    def _(step):
        add_block(jnp.where(here == 0, step, jnp.where(step == 0, here, last)), True)

    side = here // per_half
    columns = pl.ds(pl.multiple_of((here % per_half) * size, size), size)

    def write(out_ref):
        out_ref[0:HD, columns] = (query_grad_s[here] * HD**-0.5).astype(LOW)
        out_ref[HD : 2 * HD, columns] = (key_grad_s[...] * LN2).astype(LOW)
        out_ref[2 * HD : 3 * HD, columns] = value_grad_s[...].astype(LOW)

    @pl.when(side == half)
    def _():
        write(kept_ref)

    @pl.when(side != half)
    def _():
        write(leaving_ref)


def attend_forward(scalars, own, other, size):
    count = 2 * own.shape[1] // size
    whole = lambda shape: pl.BlockSpec(shape, lambda i, s: (0,) * len(shape))
    pairs = count * (count + 1) // 2
    return pl.pallas_call(
        functools.partial(forward_kernel, size=size, count=count),
        grid_spec=pltpu.PrefetchScalarGridSpec(
            num_scalar_prefetch=1,
            grid=(count,),
            in_specs=[whole(own.shape), whole(other.shape)],
            out_specs=[
                pl.BlockSpec(
                    (1, HD, size), lambda i, s: (slot_of(i, count), 0, 0)
                ),
                pl.BlockSpec((1, HD, size), lambda i, s: (i, 0, 0)),
                pl.BlockSpec((1, 1, size), lambda i, s: (i, 0, 0)),
            ],
            scratch_shapes=[
                pltpu.VMEM((count, HD, size), LOW),
                pltpu.VMEM((count, size, HD), LOW),
                pltpu.VMEM((count, HD, size), LOW),
                pltpu.VMEM((1, size), F32),
                pltpu.VMEM((1, size), F32),
                pltpu.VMEM((HD, size), F32),
            ],
        ),
        out_shape=[
            jax.ShapeDtypeStruct((count, HD, size), LOW),
            jax.ShapeDtypeStruct((count, HD, size), F32),
            jax.ShapeDtypeStruct((count, 1, size), F32),
        ],
        compiler_params=pltpu.CompilerParams(
            dimension_semantics=("arbitrary",), vmem_limit_bytes=32 * 2**20
        ),
        cost_estimate=pl.CostEstimate(
            flops=pairs * size * size * HD * 32,
            bytes_accessed=10 * 2**20,
            transcendentals=pairs * size * size,
        ),
        name="attend_forward",
    )(scalars, own, other)


def attend_backward(scalars, own, other, grad, full, log_total):
    count, _, size = grad.shape
    whole = lambda shape: pl.BlockSpec(shape, lambda i, s: (0,) * len(shape))
    pairs = count * (count + 1) // 2
    out_shape = own.shape
    return pl.pallas_call(
        functools.partial(backward_kernel, size=size, count=count),
        grid_spec=pltpu.PrefetchScalarGridSpec(
            num_scalar_prefetch=1,
            grid=(count,),
            in_specs=[
                whole(own.shape),
                whole(other.shape),
                whole(grad.shape),
                whole(full.shape),
                whole(log_total.shape),
            ],
            out_specs=[whole(out_shape)] * 2,
            scratch_shapes=[
                pltpu.VMEM((count, HD, size), LOW),
                pltpu.VMEM((count, HD, size), LOW),
                pltpu.VMEM((count, size, HD), LOW),
                pltpu.VMEM((count, 1, size), F32),
                pltpu.VMEM((count, HD, size), F32),
                pltpu.VMEM((HD, size), F32),
                pltpu.VMEM((HD, size), F32),
            ],
        ),
        out_shape=[jax.ShapeDtypeStruct(out_shape, LOW)] * 2,
        compiler_params=pltpu.CompilerParams(
            dimension_semantics=("arbitrary",), vmem_limit_bytes=32 * 2**20
        ),
        cost_estimate=pl.CostEstimate(
            flops=pairs * size * size * HD * 42,
            bytes_accessed=16 * 2**20,
            transcendentals=pairs * size * size,
        ),
        name="attend_backward",
    )(scalars, own, other, grad, full, log_total)


def place_rows_kernel(order, *refs):
    pieces, out_ref = refs[:-1], refs[-1]
    size = pieces[0].shape[0]
    for index, piece in enumerate(pieces):
        start = pl.multiple_of(order[index] * size, size)
        out_ref[pl.ds(start, size), :] = piece[...].astype(F32)


def place_rows(order, pieces):
    size, width = pieces[0].shape
    total = size * len(pieces)
    step = 512
    return pl.pallas_call(
        place_rows_kernel,
        grid_spec=pltpu.PrefetchScalarGridSpec(
            num_scalar_prefetch=1,
            grid=(width // step,),
            in_specs=[pl.BlockSpec((size, step), lambda i, s: (0, i)) for _ in pieces],
            out_specs=pl.BlockSpec((total, step), lambda i, s: (0, i)),
        ),
        out_shape=jax.ShapeDtypeStruct((total, width), F32),
        compiler_params=pltpu.CompilerParams(vmem_limit_bytes=24 * 2**20),
        cost_estimate=pl.CostEstimate(
            flops=0, bytes_accessed=total * width * 6, transcendentals=0
        ),
        name="place_rows",
    )(order, *pieces)


def place_columns_kernel(order, gain_ref, gate_w_ref, up_w_ref, *refs):
    count = (len(refs) - 3) // 2
    gates, ups = refs[:count], refs[count : 2 * count]
    gate_ref, up_ref, sum_ref = refs[2 * count :]
    size = gates[0].shape[1]
    gain = gain_ref[...]
    total = jnp.zeros((gate_ref.shape[0], size), F32)
    for index in range(count):
        columns = pl.ds(pl.multiple_of(order[index] * size, size), size)
        gate, up = gates[index][...].astype(F32), ups[index][...].astype(F32)
        total += gate * gate_w_ref[:, columns].astype(F32)
        total += up * up_w_ref[:, columns].astype(F32)
        gate_ref[:, columns] = gate * gain
        up_ref[:, columns] = up * gain

    @pl.when(pl.program_id(0) == 0)
    def _():
        sum_ref[...] = jnp.zeros_like(sum_ref)

    sum_ref[...] += jnp.sum(total, 1, keepdims=True)


def place_columns(order, gain, gate_weight, up_weight, gates, ups, shards):
    rows, width = gate_weight.shape
    span = width // shards
    size = span // len(gates)
    wide = pl.BlockSpec((rows, span), lambda i, s: (0, i))
    thin = pl.BlockSpec((rows, 1), lambda i, s: (0, 0))
    pieces = [pl.BlockSpec((rows, size), lambda i, s: (0, i)) for _ in (*gates, *ups)]
    return pl.pallas_call(
        place_columns_kernel,
        grid_spec=pltpu.PrefetchScalarGridSpec(
            num_scalar_prefetch=1,
            grid=(shards,),
            in_specs=[thin, wide, wide, *pieces],
            out_specs=[wide, wide, thin],
        ),
        out_shape=[
            jax.ShapeDtypeStruct((rows, width), F32),
            jax.ShapeDtypeStruct((rows, width), F32),
            jax.ShapeDtypeStruct((rows, 1), F32),
        ],
        compiler_params=pltpu.CompilerParams(
            dimension_semantics=("arbitrary",), vmem_limit_bytes=24 * 2**20
        ),
        cost_estimate=pl.CostEstimate(
            flops=rows * width * 6, bytes_accessed=rows * width * 16, transcendentals=0
        ),
        name="place_columns",
    )(order, gain, gate_weight, up_weight, *gates, *ups)


def place_heads_kernel(gain_ref, query_w, key_w, value_w, all_ref, query_ref, key_ref, value_ref, sum_ref):
    rows = gain_ref.shape[0]
    wide = query_ref.shape[1] // KVH
    gain = gain_ref[...]
    total = jnp.zeros((rows, 4 * HD), F32)
    pieces = [all_ref[i * rows : (i + 1) * rows, :].astype(F32) for i in range(KVH)]
    for start in range(0, KVH, 2):
        value = jnp.concatenate([piece[:, :wide] for piece in pieces[start : start + 2]], 1)
        columns = slice(start * wide, (start + 2) * wide)
        total += value * query_w[:, columns].astype(F32)
        query_ref[:, columns] = value * gain
    for first, weight, out_ref in ((wide, key_w, key_ref), (wide + HD, value_w, value_ref)):
        for start in range(0, KVH, 4):
            value = jnp.concatenate(
                [piece[:, first : first + HD] for piece in pieces[start : start + 4]], 1
            )
            columns = slice(start * HD, (start + 4) * HD)
            total += value * weight[:, columns].astype(F32)
            out_ref[:, columns] = value * gain
    sum_ref[...] = jnp.sum(total, 1, keepdims=True)


def place_heads(gain, query_weight, key_weight, value_weight, pieces):
    weights = (query_weight, key_weight, value_weight)
    rows = gain.shape[0]
    return pl.pallas_call(
        place_heads_kernel,
        out_shape=[jax.ShapeDtypeStruct(weight.shape, F32) for weight in weights]
        + [jax.ShapeDtypeStruct((rows, 1), F32)],
        compiler_params=pltpu.CompilerParams(vmem_limit_bytes=32 * 2**20),
        cost_estimate=pl.CostEstimate(
            flops=rows * 3072 * 4, bytes_accessed=rows * 3072 * 8, transcendentals=0
        ),
        name="place_heads",
    )(gain, *weights, pieces)


def merge_kernel(scalars, kept_ref, came_ref, cosine_ref, sine_ref, out_ref, split_ref):
    lead = scalars[0] == 0
    lines, _, size = split_ref.shape
    for line in range(lines):
        columns = slice(line * size, (line + 1) * size)
        kept = kept_ref[:, columns].astype(F32)
        came = came_ref[:, columns].astype(F32)
        cosine, sine = cosine_ref[:, columns], sine_ref[:, columns]
        joint = kept[HD:] + came[HD:]
        first = jnp.where(lead, kept[:HD], came[:HD])
        second = jnp.where(lead, came[:HD], kept[:HD])
        turned = []
        for value in (first, second, joint[:HD]):
            low, high = value[: HD // 2], value[HD // 2 :]
            turned.append(low * cosine + high * sine)
            turned.append(high * cosine - low * sine)
        turned.append(joint[HD:])
        result = jnp.concatenate([part.astype(LOW) for part in turned], 0)
        out_ref[:, columns] = result
        split_ref[line] = result


def merge(scalars, kept, came, cosine, sine, lines):
    tokens = kept.shape[1]
    whole = lambda value: pl.BlockSpec(value.shape, lambda i, s: (0,) * len(value.shape))
    outs = [
        jax.ShapeDtypeStruct((4 * HD, tokens), LOW),
        jax.ShapeDtypeStruct((lines, 4 * HD, tokens // lines), LOW),
    ]
    return pl.pallas_call(
        merge_kernel,
        grid_spec=pltpu.PrefetchScalarGridSpec(
            num_scalar_prefetch=1,
            grid=(1,),
            in_specs=[whole(value) for value in (kept, came, cosine, sine)],
            out_specs=[whole(value) for value in outs],
        ),
        out_shape=outs,
        compiler_params=pltpu.CompilerParams(vmem_limit_bytes=24 * 2**20),
        cost_estimate=pl.CostEstimate(
            flops=tokens * HD * 24, bytes_accessed=tokens * HD * 30, transcendentals=0
        ),
        name="merge",
    )(scalars, kept, came, cosine, sine)


def pack_kernel(scalars, gain_ref, query_ref, key_ref, value_ref, *outs):
    core = scalars[3]
    gain = gain_ref[...]
    wide = query_ref.shape[1] // KVH
    span = wide + 2 * HD
    for which in range(2):

        @pl.when(core == which)
        def _():
            for line in range(KVH // 2):
                head = 2 * line + which
                value = jnp.concatenate(
                    [
                        query_ref[:, head * wide : (head + 1) * wide].astype(F32),
                        key_ref[:, head * HD : (head + 1) * HD].astype(F32),
                        value_ref[:, head * HD : (head + 1) * HD].astype(F32),
                    ],
                    1,
                )
                place = (line % 2) * span
                outs[line // 2][:, place : place + span] = (value * gain).astype(LOW)


def pack(scalars, gain, query_weight, key_weight, value_weight):
    rows, width = query_weight.shape
    whole = lambda value: pl.BlockSpec(value.shape, lambda i, s: (0, 0))
    weights = (gain, query_weight, key_weight, value_weight)
    outs = [jax.ShapeDtypeStruct((rows, width // 2), LOW)] * 2
    return pl.pallas_call(
        pack_kernel,
        grid_spec=pltpu.PrefetchScalarGridSpec(
            num_scalar_prefetch=1,
            grid=(1,),
            in_specs=[whole(value) for value in weights],
            out_specs=[whole(value) for value in outs],
        ),
        out_shape=outs,
        compiler_params=pltpu.CompilerParams(vmem_limit_bytes=24 * 2**20),
        cost_estimate=pl.CostEstimate(
            flops=rows * width, bytes_accessed=rows * width * 6, transcendentals=0
        ),
        name="pack",
    )(scalars, *weights)


def spread_kernel(scalars, lin_ref, cosine_ref, sine_ref, own_ref, leaving_ref):
    cosine, sine = cosine_ref[...], sine_ref[...]

    def turn(start, factor):
        low = lin_ref[start : start + HD // 2, :]
        high = lin_ref[start + HD // 2 : start + HD, :]
        turned = ((low * cosine - high * sine) * factor, (high * cosine + low * sine) * factor)
        return jnp.concatenate([part.astype(LOW) for part in turned], 0)

    lead = scalars[0] == 0
    first, second = turn(0, HD**-0.5 / LN2), turn(HD, HD**-0.5 / LN2)

    @pl.when(lead)
    def _():
        own_ref[0:HD] = first
        leaving_ref[0:HD] = second

    @pl.when(jnp.logical_not(lead))
    def _():
        own_ref[0:HD] = second
        leaving_ref[0:HD] = first

    key = turn(2 * HD, 1.0)
    value = lin_ref[3 * HD : 4 * HD].astype(LOW)
    for ref in (own_ref, leaving_ref):
        ref[HD : 2 * HD] = key
        ref[2 * HD : 3 * HD] = value


def spread(scalars, lin, cosine, sine):
    tokens = lin.shape[1]
    step = 512
    column = lambda rows: pl.BlockSpec((rows, step), lambda i, s: (0, i))
    return pl.pallas_call(
        spread_kernel,
        grid_spec=pltpu.PrefetchScalarGridSpec(
            num_scalar_prefetch=1,
            grid=(tokens // step,),
            in_specs=[column(4 * HD), column(HD // 2), column(HD // 2)],
            out_specs=[column(3 * HD)] * 2,
        ),
        out_shape=[jax.ShapeDtypeStruct((3 * HD, tokens), LOW)] * 2,
        compiler_params=pltpu.CompilerParams(vmem_limit_bytes=24 * 2**20),
        cost_estimate=pl.CostEstimate(
            flops=tokens * HD * 24, bytes_accessed=tokens * HD * 36, transcendentals=0
        ),
        name="spread",
    )(scalars, lin, cosine, sine)


def swap(value, axis):
    return lax.ppermute(value, axis, [(0, 1), (1, 0)])


def swap_near(value):
    return lax.ppermute(value, "z", [(0, 1), (1, 0), (2, 3), (3, 2)])


def swap_far(value):
    return lax.ppermute(value, "z", [(0, 2), (2, 0), (1, 3), (3, 1)])


def tie(*values):
    return lax.optimization_barrier(values)


def in_order(place, own, other):
    return (jnp.where(place == 0, own, other), jnp.where(place == 0, other, own))


def both(place, own, other):
    return jnp.concatenate(in_order(place, own, other), 0)


def spread_out(value, first, second):
    other = swap(value, first)
    pair = jnp.stack(in_order(lax.axis_index(first), value, other))
    return pair, swap(pair, second)


def placed(pair, other, second):
    pairs = in_order(lax.axis_index(second), pair, other)
    grid = jnp.stack(pairs, 0 if second == "y" else 1)
    return grid.reshape(-1, *grid.shape[3:])


def pick(array, axis, at):
    return lax.dynamic_index_in_dim(array, at, axis, keepdims=False)


def halve(value, axis, along=0):
    at = lax.axis_index(axis)
    return pick(value, along, at), swap(pick(value, along, 1 - at), axis)


def halve_x(value):
    return halve(value.reshape(2, 2, -1, value.shape[-1]), "x", 1)


def halve_y(value):
    return halve(value.reshape(2, 2, -1, value.shape[-1]), "y", 0)


def fast_body(
    tokens,
    positions,
    first_gain,
    query_weight,
    key_weight,
    value_weight,
    output_weight,
    second_gain,
    gate_weight,
    up_weight,
    down_weight,
    cotangent,
):
    seq = ("z", "c")
    fsdp = ("y", "x")
    z, core, half = lax.axis_index("z"), lax.axis_index("c"), lax.axis_index("x")
    near = z % 2
    lines = lax.axis_size("z")
    seq_count = 2 * lines
    shards = lax.axis_size("y") * 2
    spot = z * 2 + core
    quarter = near * 2 + core
    rows = tokens[0]
    count, width = rows.shape
    chip_count = 2 * count
    half_len = count * seq_count
    seq_len = 2 * half_len

    begins = jnp.where(
        (spot == 0) & (half == 0),
        count - 1 - positions[0, count - 1],
        half * half_len + spot * count - positions[0, 0],
    )
    ends = begins + (seq_len - count)
    scalars = jnp.stack([half, begins, ends, core]).astype(jnp.int32)

    gain_one = first_gain.astype(F32)[:, None]
    gain_two = second_gain.astype(F32)[:, None]

    def row_scale(value):
        return lax.rsqrt(jnp.mean(value * value, -1, keepdims=True) + EPS)

    take = functools.partial(lax.dynamic_slice_in_dim, axis=1)
    take_rows = functools.partial(lax.dynamic_slice_in_dim, axis=0)
    gather = lambda value, axes: lax.all_gather(value, axes, axis=0, tiled=True)
    own_rows = rows.astype(F32)
    own_unit_scale = row_scale(own_rows)
    own_unit = own_rows * own_unit_scale
    units = gather(own_unit.astype(LOW), seq)
    wide = QH // KVH * HD
    qkv_shard = (
        jnp.concatenate(
            [
                take(query_weight, spot * wide, wide),
                take(key_weight, spot * HD, HD),
                take(value_weight, spot * HD, HD),
            ],
            1,
        ).astype(F32)
        * gain_one
    ).astype(LOW)
    out_rows = output_weight.shape[0] // 2
    out_shard = take_rows(output_weight, core * out_rows, out_rows)
    piece = down_weight.shape[0] // 4
    down_shard = take_rows(down_weight, quarter * piece, piece)
    gate_shard, up_shard = (
        (
            jnp.concatenate(
                [
                    take(weight, shard * 4 * piece + quarter * piece, piece)
                    for shard in range(shards)
                ],
                1,
            ).astype(F32)
            * gain_two
        ).astype(LOW)
        for weight in (gate_weight, up_weight)
    )
    side = lax.axis_index("y")
    qkv_pair = jnp.stack(in_order(half, qkv_shard, swap(qkv_shard, "x")))
    gate_pair = jnp.stack(in_order(half, gate_shard, swap(gate_shard, "x")))
    up_pair = jnp.stack(in_order(side, up_shard, swap(up_shard, "y")))
    qkv_pair, gate_pair, up_pair = tie(qkv_pair, gate_pair, up_pair)
    qkv_w = placed(qkv_pair, swap(qkv_pair, "y"), "y")
    gate_pair, up_pair = (gate_pair, swap(gate_pair, "y")), (up_pair, swap(up_pair, "x"))

    place = half * half_len + jnp.arange(half_len, dtype=jnp.int32)
    start = jnp.where(place >= ends, ends, jnp.where(place >= begins, begins, 0))
    freq = THETA ** (-(jnp.arange(HD // 2, dtype=F32) * 2.0 / HD))
    angle = freq[:, None] * (place - start).astype(F32)[None, :]
    cosine, sine = jnp.cos(angle), jnp.sin(angle)
    chip_rows = both(core, rows, swap(rows, "c"))
    units, own_cot, chip_rows = tie(units, cotangent[0], chip_rows)
    own, leaving = spread(scalars, contract(qkv_w, units, 0, 1), cosine, sine)

    near_cot = swap_near(own_cot)
    other, out_shard, down_shard, near_cot, chip_cot, gate_pair, up_pair = tie(
        swap(leaving, "x"),
        out_shard,
        down_shard,
        near_cot,
        both(core, own_cot, swap(own_cot, "c")),
        gate_pair,
        up_pair,
    )
    out_w = gather(out_shard, fsdp)
    down_w = gather(down_shard, fsdp)
    near_other = swap(near_cot, "c")
    head_low, head_full, log_total = attend_forward(scalars, own, other, chip_count)
    exchange = lambda value: lax.all_to_all(
        value, ("z", "x"), split_axis=0, concat_axis=0, tiled=True
    )
    head_low, near_other = tie(head_low, near_other)
    lead_shard, tail_shard = pack(scalars, gain_one, query_weight, key_weight, value_weight)
    heads, gate_w, up_w, near_cot, lead_shard = tie(
        exchange(head_low),
        placed(*gate_pair, "y"),
        placed(*up_pair, "x"),
        jnp.concatenate([near_cot, near_other], 0),
        lead_shard,
    )
    lead_w = gather(lead_shard, fsdp)
    heads = heads.reshape(QH // 2 * HD, chip_count)

    mine_of = lambda value: take_rows(value, core * count, count)
    theirs_of = lambda value: take_rows(value, (1 - core) * count, count)
    branch = contract(heads, out_w, 0, 0).astype(LOW)
    middle = chip_rows.astype(F32) + (branch.astype(F32) + swap(branch, "c").astype(F32))
    middle_scale = row_scale(middle)
    chip_unit = middle * middle_scale
    own_middle, own_scale, own_middle_unit = (
        mine_of(middle),
        mine_of(middle_scale),
        mine_of(chip_unit),
    )
    chip_unit = chip_unit.astype(LOW)
    near_unit = swap_near(mine_of(chip_unit))

    def feed(unit):
        gate, upper = contract(unit, gate_w, 1, 0), contract(unit, up_w, 1, 0)
        sigma = jax.nn.sigmoid(gate)
        silu = gate * sigma
        return (silu * upper).astype(LOW), (gate, upper, sigma, silu)

    def feed_back(cot, kept):
        gate, upper, sigma, silu = kept
        grad_hidden = contract(cot, down_w, 1, 1)
        gate_low = (grad_hidden * upper * sigma * (1.0 + gate * (1.0 - sigma))).astype(LOW)
        upper_low = (grad_hidden * silu).astype(LOW)
        part = contract(gate_low, gate_w, 1, 1) + contract(upper_low, up_w, 1, 1)
        return gate_low, upper_low, part

    def chip_sum(chip_part, near_part):
        near_sum = near_part[:count].astype(F32) + swap(near_part[count:].astype(LOW), "c")
        own_sum = mine_of(chip_part).astype(F32) + swap(theirs_of(chip_part).astype(LOW), "c")
        return own_sum, near_sum.astype(LOW)

    stack = lambda first, second: jnp.concatenate([first, second], 0)
    scatter = lambda value: lax.psum_scatter(value, fsdp, scatter_dimension=0, tiled=True)
    chip_hidden, chip_kept = feed(chip_unit)
    near_unit, chip_hidden = tie(near_unit, chip_hidden)
    near_unit = jnp.concatenate([near_unit, swap(near_unit, "c")], 0)
    near_hidden, near_kept = feed(near_unit)
    down_part = contract(
        stack(chip_hidden, near_hidden), stack(chip_cot, near_cot), 0, 0
    ).astype(LOW)
    near_cot, down_part = tie(near_cot, down_part)
    near_gate, near_upper, near_part = feed_back(near_cot, near_kept)
    chip_gate, chip_upper, chip_part = feed_back(chip_cot, chip_kept)
    grad_two, near_sum = chip_sum(chip_part, near_part)

    def halves_first(value):
        cut = value.shape[-1] // 2
        return halve_x(value[:, :cut]), halve_y(value[:, cut:])

    def halves_second(firsts):
        return halve(sum(firsts[0]), "y"), halve(sum(firsts[1]), "x")

    def halves_end(seconds):
        return jnp.concatenate([sum(seconds[0]), sum(seconds[1])], 1)

    down_first = halves_first(down_part)
    near_sum, near_gate, near_upper, chip_part = tie(
        near_sum, near_gate, near_upper, chip_part
    )
    grad_came = swap_near(near_sum)
    all_units = stack(chip_unit, near_unit)
    gate_part = contract(all_units, stack(chip_gate, near_gate), 0, 0).astype(LOW)
    up_part = contract(all_units, stack(chip_upper, near_upper), 0, 0).astype(LOW)
    gate_part, up_part, down_first, grad_came = tie(gate_part, up_part, down_first, grad_came)
    down_second = halves_second(down_first)
    gate_grad, up_grad = scatter(gate_part), scatter(up_part)
    grad_two = grad_two + grad_came.astype(F32)
    grad_middle = own_cot.astype(F32) + own_scale * (
        grad_two - own_middle_unit * jnp.mean(grad_two * own_middle_unit, -1, keepdims=True)
    )
    own_branch, lead_w, down_second = tie(grad_middle.astype(LOW), lead_w, down_second)
    down_grad = halves_end(down_second)
    down_far = swap_far(down_grad)
    grad_branch = both(core, own_branch, swap(own_branch, "c"))
    grad_heads = contract(out_w, grad_branch, 1, 1).astype(LOW)
    grad_heads, grad_branch, chip_hidden, near_hidden = tie(
        grad_heads, grad_branch, chip_hidden, near_hidden
    )
    feed_own, feed_near = chip_sum(
        contract(chip_hidden, down_w, 1, 0), contract(near_hidden, down_w, 1, 0)
    )
    feed_near = swap_near(feed_near)
    output_part = contract(heads, grad_branch, 1, 0).astype(LOW)
    output_grad = scatter(output_part)
    grad_head, output_part, gate_grad, down_far = tie(
        exchange(grad_heads.reshape(2 * lines, HD, chip_count)),
        output_part,
        gate_grad,
        down_far,
    )

    gate_far = swap_far(gate_grad)
    down_sum = down_grad + down_far
    down_near = swap_near(down_sum)
    kept, leaving = attend_backward(scalars, own, other, grad_head, head_full, log_total)
    kept, leaving, gate_far, down_near, up_grad, tail_shard, feed_near = tie(
        kept, leaving, gate_far, down_near, up_grad, tail_shard, feed_near
    )
    tail_w = gather(tail_shard, fsdp)

    up_far = swap_far(up_grad)
    gate_sum = gate_grad + gate_far
    gate_near = swap_near(gate_sum)
    block_output = (own_middle + feed_own + feed_near.astype(F32)).astype(LOW)[None]
    came, up_far, gate_near, output_grad, block_output = tie(
        swap(leaving, "x"), up_far, gate_near, output_grad, block_output
    )

    qkv_low, by_line = merge(scalars, kept, came, cosine, sine, lines)
    token_grads = lax.all_to_all(by_line, "z", split_axis=0, concat_axis=0, tiled=True)
    qkv_part = contract(units, qkv_low, 0, 1).astype(LOW).reshape(shards, 2, -1, 4 * HD)
    qkv_first = halve_x(qkv_part[:, 0]), halve_y(qkv_part[:, 1])
    qkv_second = halves_second(qkv_first)
    qkv_grad = jnp.concatenate([sum(qkv_second[0]), sum(qkv_second[1])], 0)
    output_came = swap_near(output_grad)
    token_grads, qkv_grad, output_came = tie(token_grads, qkv_grad, output_came)
    all_qkv = gather(qkv_grad, seq)
    output_sum = output_grad + output_came
    output_far = swap_far(output_sum)
    up_sum = up_grad + up_far
    up_near = swap_near(up_sum)

    token_grads = token_grads.reshape(-1, chip_count)
    split = lead_w.shape[1]
    grad_one = contract(token_grads[:split], lead_w, 0, 1) + contract(
        token_grads[split:], tail_w, 0, 1
    )
    grad_came, output_far = tie(swap(theirs_of(grad_one).astype(LOW), "c"), output_far)
    grad_one = mine_of(grad_one) + grad_came.astype(F32)
    grad_rows = own_unit_scale * (
        grad_one - own_unit * jnp.mean(grad_one * own_unit, -1, keepdims=True)
    )
    input_grad = (grad_middle + grad_rows).astype(LOW)[None]

    def four(value, near_value):
        return value, swap(value, "c"), near_value, swap(near_value, "c")

    order = jnp.stack([quarter, quarter ^ 1, quarter ^ 2, quarter ^ 3]).astype(jnp.int32)
    core_order = jnp.stack([core, 1 - core]).astype(jnp.int32)
    down_total = place_rows(order, four(down_sum, down_near))
    gate_total, up_total, second_gain_grad = place_columns(
        order, gain_two, gate_weight, up_weight, four(gate_sum, gate_near), four(up_sum, up_near), shards
    )
    output_far, second_gain_grad = tie(output_far, second_gain_grad)
    output_own = output_sum + output_far
    output_total = place_rows(core_order, (output_own, swap(output_own, "c")))
    query_grad, key_grad, value_grad, first_gain_grad = place_heads(
        gain_one, query_weight, key_weight, value_weight, all_qkv
    )
    return (
        block_output,
        input_grad,
        first_gain_grad[:, 0],
        query_grad,
        key_grad,
        value_grad,
        output_total,
        second_gain_grad[:, 0],
        gate_total,
        up_total,
        down_total,
    )


def fast_solution(mesh):
    seq_count, shard_count = mesh.devices.shape
    fine = Mesh(
        mesh.devices.reshape(seq_count // 2, 2, shard_count // 2, 2), ("z", "c", "y", "x")
    )
    seq, fsdp = ("z", "c"), ("y", "x")
    matrix = P(fsdp, None)
    return jax.shard_map(
        fast_body,
        mesh=fine,
        in_specs=(
            P(fsdp, seq, None),
            P(fsdp, seq),
            P(fsdp),
            matrix,
            matrix,
            matrix,
            matrix,
            P(fsdp),
            matrix,
            matrix,
            matrix,
            P(fsdp, seq, None),
        ),
        out_specs=(
            P(fsdp, seq, None),
            P(fsdp, seq, None),
            P(fsdp),
            matrix,
            matrix,
            matrix,
            matrix,
            P(fsdp),
            matrix,
            matrix,
            matrix,
        ),
        check_vma=False,
    )


def solution(mesh):
    shape = dict(mesh.shape)
    if shape["seq"] == KVH and shape["fsdp"] == 4:
        return fast_solution(mesh)
    return plain_solution(mesh)


def shifted(value, axis, steps):
    count = lax.axis_size(axis)
    first, last = (max(0, -steps), min(count, count - steps))
    return lax.ppermute(value, axis, [(source, source + steps) for source in range(first, last)])


def rope_tables(position_rows):
    freq = THETA ** (-(jnp.arange(HD // 2, dtype=jnp.float32) * 2.0 / HD))
    angle = position_rows.astype(jnp.float32)[:, None] * freq[None, :]
    cosine = jnp.cos(angle)
    sine = jnp.sin(angle)
    return (jnp.concatenate([cosine, cosine], -1), jnp.concatenate([sine, sine], -1))


def rotate(values, cosine, sine):
    half = HD // 2
    turned = jnp.concatenate([-values[..., half:], values[..., :half]], -1)
    return values * cosine[:, None, :] + turned * sine[:, None, :]


def rotate_back(grads, cosine, sine):
    half = HD // 2
    scaled = grads * sine[:, None, :]
    turned = jnp.concatenate([scaled[..., half:], -scaled[..., :half]], -1)
    return grads * cosine[:, None, :] + turned


def norm_forward(rows, gain):
    scale = lax.rsqrt(jnp.mean(rows * rows, -1, keepdims=True) + EPS)
    unit = rows * scale
    return (unit * gain, unit, scale)


def norm_backward(grad_out, unit, scale, gain):
    grad_unit = grad_out * gain
    gain_grad = jnp.sum(grad_out * unit, 0)
    grad_rows = scale * (grad_unit - unit * jnp.mean(grad_unit * unit, -1, keepdims=True))
    return (grad_rows, gain_grad)


def plain_body(
    tokens,
    positions,
    first_gain,
    query_weight,
    key_weight,
    value_weight,
    output_weight,
    second_gain,
    gate_weight,
    up_weight,
    down_weight,
    cotangent,
):
    seq_count = lax.axis_size("seq")
    local_rows = tokens[0]
    token_count = local_rows.shape[0]
    half_len = token_count * seq_count
    rows_float = local_rows.astype(jnp.float32)
    gain_one, wq_full, wk_full, wv_full, wo_full = (
        lax.all_gather(first_gain, "fsdp", axis=0, tiled=True),
        lax.all_gather(query_weight, "fsdp", axis=0, tiled=True),
        lax.all_gather(key_weight, "fsdp", axis=0, tiled=True),
        lax.all_gather(value_weight, "fsdp", axis=0, tiled=True),
        lax.all_gather(output_weight, "fsdp", axis=0, tiled=True),
    )
    gain_one = gain_one.astype(jnp.float32)
    normed_one, unit_one, scale_one = norm_forward(rows_float, gain_one)
    normed_low = normed_one.astype(jnp.bfloat16)
    cosine, sine = rope_tables(positions[0])
    query_lin = jnp.dot(normed_low, wq_full, preferred_element_type=jnp.float32).reshape(
        token_count, QH, HD
    )
    key_lin = jnp.dot(normed_low, wk_full, preferred_element_type=jnp.float32).reshape(
        token_count, KVH, HD
    )
    value_lin = jnp.dot(normed_low, wv_full, preferred_element_type=jnp.float32).reshape(
        token_count, KVH, HD
    )
    query_rows = rotate(query_lin, cosine, sine).astype(jnp.bfloat16)
    key_rows = rotate(key_lin, cosine, sine).astype(jnp.bfloat16)
    value_rows = value_lin.astype(jnp.bfloat16)
    repeat = max(1, seq_count // KVH)
    if repeat > 1:
        key_rows = jnp.repeat(key_rows, repeat, axis=1)
        value_rows = jnp.repeat(value_rows, repeat, axis=1)
    query_heads, key_heads, value_heads = (
        lax.all_to_all(query_rows, "seq", split_axis=1, concat_axis=0, tiled=True),
        lax.all_to_all(key_rows, "seq", split_axis=1, concat_axis=0, tiled=True),
        lax.all_to_all(value_rows, "seq", split_axis=1, concat_axis=0, tiled=True),
    )
    head_count = query_heads.shape[1]
    pair_count = key_heads.shape[1]
    group = head_count // pair_count
    half_positions = lax.all_gather(positions[0], "seq", axis=0, tiled=True)
    key_prior, value_prior = shifted((key_heads, value_heads), "fsdp", 1)
    key_all = jnp.concatenate([key_prior, key_heads], 0)
    value_all = jnp.concatenate([value_prior, value_heads], 0)
    half_index = lax.axis_index("fsdp") % 2
    key_index = (half_index - 1) * half_len + jnp.arange(2 * half_len, dtype=jnp.int32)
    row_index = half_index * half_len + jnp.arange(half_len, dtype=jnp.int32)
    row_start = row_index - half_positions
    block = min(512, half_len)
    count = half_len // block
    factor = HD ** (-0.5)
    query_blocks = query_heads.reshape(count, block, pair_count, group, HD)
    index_blocks = row_index.reshape(count, block)
    start_blocks = row_start.reshape(count, block)

    def block_scores(query_block, index_block, start_block):
        scores = (
            jnp.einsum("bkgd,tkd->kgbt", query_block, key_all, preferred_element_type=jnp.float32)
            * factor
        )
        visible = (key_index[None, :] >= start_block[:, None]) & (
            key_index[None, :] <= index_block[:, None]
        )
        return jnp.where(visible, scores, -1e30)

    def forward_block(items):
        query_block, index_block, start_block = items
        scores = block_scores(query_block, index_block, start_block)
        top = jnp.max(scores, -1, keepdims=True)
        expo = jnp.exp(scores - top)
        total = jnp.sum(expo, -1, keepdims=True)
        probs_low = (expo / total).astype(jnp.bfloat16)
        mixed = jnp.einsum(
            "kgbt,tkd->bkgd", probs_low, value_all, preferred_element_type=jnp.float32
        )
        return (mixed.reshape(block, head_count, HD).astype(jnp.bfloat16), top + jnp.log(total))

    head_blocks, log_totals = lax.map(forward_block, (query_blocks, index_blocks, start_blocks))
    head_out = head_blocks.reshape(half_len, head_count, HD)
    token_heads = lax.all_to_all(head_out, "seq", split_axis=0, concat_axis=1, tiled=True)
    heads_flat = token_heads.reshape(token_count, QH * HD)
    middle = rows_float + jnp.dot(heads_flat, wo_full, preferred_element_type=jnp.float32)
    gain_two, wg_full, wu_full, wd_full = (
        lax.all_gather(second_gain, "fsdp", axis=0, tiled=True),
        lax.all_gather(gate_weight, "fsdp", axis=0, tiled=True),
        lax.all_gather(up_weight, "fsdp", axis=0, tiled=True),
        lax.all_gather(down_weight, "fsdp", axis=0, tiled=True),
    )
    gain_two = gain_two.astype(jnp.float32)
    normed_two, unit_two, scale_two = norm_forward(middle, gain_two)
    normed_two_low = normed_two.astype(jnp.bfloat16)
    gate = jnp.dot(normed_two_low, wg_full, preferred_element_type=jnp.float32)
    upper = jnp.dot(normed_two_low, wu_full, preferred_element_type=jnp.float32)
    hidden = (jax.nn.silu(gate) * upper).astype(jnp.bfloat16)
    result = middle + jnp.dot(hidden, wd_full, preferred_element_type=jnp.float32)
    block_output = result.astype(jnp.bfloat16)[None]
    grad_low = cotangent[0]
    grad_rows = grad_low.astype(jnp.float32)
    down_grad = jnp.einsum("tf,td->fd", hidden, grad_low, preferred_element_type=jnp.float32)
    grad_hidden = jnp.einsum("td,fd->tf", grad_low, wd_full, preferred_element_type=jnp.float32)
    sigma = jax.nn.sigmoid(gate)
    gate_low = (grad_hidden * upper * sigma * (1.0 + gate * (1.0 - sigma))).astype(jnp.bfloat16)
    upper_low = (grad_hidden * gate * sigma).astype(jnp.bfloat16)
    gate_grad = jnp.einsum(
        "td,tf->df", normed_two_low, gate_low, preferred_element_type=jnp.float32
    )
    up_grad = jnp.einsum("td,tf->df", normed_two_low, upper_low, preferred_element_type=jnp.float32)
    grad_normed_two = jnp.einsum(
        "tf,df->td", gate_low, wg_full, preferred_element_type=jnp.float32
    ) + jnp.einsum("tf,df->td", upper_low, wu_full, preferred_element_type=jnp.float32)
    grad_middle_norm, second_gain_grad = norm_backward(
        grad_normed_two, unit_two, scale_two, gain_two
    )
    grad_middle = grad_rows + grad_middle_norm
    grad_branch = grad_middle.astype(jnp.bfloat16)
    output_grad = jnp.einsum(
        "tc,td->cd", heads_flat, grad_branch, preferred_element_type=jnp.float32
    )
    grad_heads = (
        jnp.einsum("td,cd->tc", grad_branch, wo_full, preferred_element_type=jnp.float32)
        .astype(jnp.bfloat16)
        .reshape(token_count, QH, HD)
    )
    grad_head_rows = lax.all_to_all(grad_heads, "seq", split_axis=1, concat_axis=0, tiled=True)
    grad_blocks = grad_head_rows.reshape(count, block, pair_count, group, HD)

    def backward_block(carry, items):
        key_acc, value_acc = carry
        query_block, index_block, start_block, grad_block, log_block = items
        scores = block_scores(query_block, index_block, start_block)
        probs = jnp.exp(scores - log_block)
        probs_low = probs.astype(jnp.bfloat16)
        grad_probs = jnp.einsum(
            "bkgd,tkd->kgbt", grad_block, value_all, preferred_element_type=jnp.float32
        )
        grad_scores = (
            probs * (grad_probs - jnp.sum(probs * grad_probs, -1, keepdims=True))
        ).astype(jnp.bfloat16)
        query_grad_block = (
            jnp.einsum("kgbt,tkd->bkgd", grad_scores, key_all, preferred_element_type=jnp.float32)
            * factor
        )
        key_acc = (
            key_acc
            + jnp.einsum(
                "kgbt,bkgd->tkd", grad_scores, query_block, preferred_element_type=jnp.float32
            )
            * factor
        )
        value_acc = value_acc + jnp.einsum(
            "kgbt,bkgd->tkd", probs_low, grad_block, preferred_element_type=jnp.float32
        )
        return ((key_acc, value_acc), query_grad_block.reshape(block, head_count, HD))

    empty = jnp.zeros((2 * half_len, pair_count, HD), jnp.float32)
    (key_acc, value_acc), query_grad_blocks = lax.scan(
        backward_block,
        (empty, empty),
        (query_blocks, index_blocks, start_blocks, grad_blocks, log_totals),
    )
    key_back, value_back = (
        shifted(key_acc[:half_len].astype(jnp.bfloat16), "fsdp", -1).astype(jnp.float32),
        shifted(value_acc[:half_len].astype(jnp.bfloat16), "fsdp", -1).astype(jnp.float32),
    )
    key_local = key_acc[half_len:] + key_back
    value_local = value_acc[half_len:] + value_back
    query_grad_heads = query_grad_blocks.reshape(half_len, head_count, HD)
    grad_query_tok, grad_key_tok, grad_value_tok = (
        lax.all_to_all(
            query_grad_heads.astype(jnp.bfloat16), "seq", split_axis=0, concat_axis=1, tiled=True
        ).astype(query_grad_heads.dtype),
        lax.all_to_all(
            key_local.astype(jnp.bfloat16), "seq", split_axis=0, concat_axis=1, tiled=True
        ).astype(key_local.dtype),
        lax.all_to_all(
            value_local.astype(jnp.bfloat16), "seq", split_axis=0, concat_axis=1, tiled=True
        ).astype(value_local.dtype),
    )
    if repeat > 1:
        grad_key_tok = grad_key_tok.reshape(token_count, KVH, repeat, HD).sum(2)
        grad_value_tok = grad_value_tok.reshape(token_count, KVH, repeat, HD).sum(2)
    query_lin_grad = (
        rotate_back(grad_query_tok, cosine, sine).astype(jnp.bfloat16).reshape(token_count, QH * HD)
    )
    key_lin_grad = (
        rotate_back(grad_key_tok, cosine, sine).astype(jnp.bfloat16).reshape(token_count, KVH * HD)
    )
    value_lin_grad = grad_value_tok.astype(jnp.bfloat16).reshape(token_count, KVH * HD)
    query_grad = jnp.einsum(
        "td,tc->dc", normed_low, query_lin_grad, preferred_element_type=jnp.float32
    )
    key_grad = jnp.einsum("td,tc->dc", normed_low, key_lin_grad, preferred_element_type=jnp.float32)
    value_grad = jnp.einsum(
        "td,tc->dc", normed_low, value_lin_grad, preferred_element_type=jnp.float32
    )
    grad_normed_one = jnp.einsum(
        "tc,dc->td", query_lin_grad, wq_full, preferred_element_type=jnp.float32
    )
    grad_normed_one = grad_normed_one + jnp.einsum(
        "tc,dc->td", key_lin_grad, wk_full, preferred_element_type=jnp.float32
    )
    grad_normed_one = grad_normed_one + jnp.einsum(
        "tc,dc->td", value_lin_grad, wv_full, preferred_element_type=jnp.float32
    )
    grad_rows_one, first_gain_grad = norm_backward(grad_normed_one, unit_one, scale_one, gain_one)
    input_grad = (grad_middle + grad_rows_one).astype(jnp.bfloat16)[None]
    pieces = (
        lax.psum_scatter(
            first_gain_grad.astype(jnp.bfloat16), "fsdp", scatter_dimension=0, tiled=True
        ).astype(jnp.float32),
        lax.psum_scatter(
            query_grad.astype(jnp.bfloat16), "fsdp", scatter_dimension=0, tiled=True
        ).astype(jnp.float32),
        lax.psum_scatter(
            key_grad.astype(jnp.bfloat16), "fsdp", scatter_dimension=0, tiled=True
        ).astype(jnp.float32),
        lax.psum_scatter(
            value_grad.astype(jnp.bfloat16), "fsdp", scatter_dimension=0, tiled=True
        ).astype(jnp.float32),
        lax.psum_scatter(
            output_grad.astype(jnp.bfloat16), "fsdp", scatter_dimension=0, tiled=True
        ).astype(jnp.float32),
        lax.psum_scatter(
            second_gain_grad.astype(jnp.bfloat16), "fsdp", scatter_dimension=0, tiled=True
        ).astype(jnp.float32),
        lax.psum_scatter(
            gate_grad.astype(jnp.bfloat16), "fsdp", scatter_dimension=0, tiled=True
        ).astype(jnp.float32),
        lax.psum_scatter(
            up_grad.astype(jnp.bfloat16), "fsdp", scatter_dimension=0, tiled=True
        ).astype(jnp.float32),
        lax.psum_scatter(
            down_grad.astype(jnp.bfloat16), "fsdp", scatter_dimension=0, tiled=True
        ).astype(jnp.float32),
    )
    shares = (
        lax.psum(pieces[0].astype(jnp.bfloat16), "seq").astype(jnp.float32),
        lax.psum(pieces[1].astype(jnp.bfloat16), "seq").astype(jnp.float32),
        lax.psum(pieces[2].astype(jnp.bfloat16), "seq").astype(jnp.float32),
        lax.psum(pieces[3].astype(jnp.bfloat16), "seq").astype(jnp.float32),
        lax.psum(pieces[4].astype(jnp.bfloat16), "seq").astype(jnp.float32),
        lax.psum(pieces[5].astype(jnp.bfloat16), "seq").astype(jnp.float32),
        lax.psum(pieces[6].astype(jnp.bfloat16), "seq").astype(jnp.float32),
        lax.psum(pieces[7].astype(jnp.bfloat16), "seq").astype(jnp.float32),
        lax.psum(pieces[8].astype(jnp.bfloat16), "seq").astype(jnp.float32),
    )
    return (
        block_output,
        input_grad,
        shares[0],
        shares[1],
        shares[2],
        shares[3],
        shares[4],
        shares[5],
        shares[6],
        shares[7],
        shares[8],
    )


def plain_solution(mesh):
    placed = (
        P("fsdp", "seq", None),
        P("fsdp", "seq"),
        P("fsdp"),
        P("fsdp", None),
        P("fsdp", None),
        P("fsdp", None),
        P("fsdp", None),
        P("fsdp"),
        P("fsdp", None),
        P("fsdp", None),
        P("fsdp", None),
        P("fsdp", "seq", None),
    )
    return jax.shard_map(
        plain_body,
        mesh=mesh,
        in_specs=placed,
        out_specs=(
            P("fsdp", "seq", None),
            P("fsdp", "seq", None),
            P("fsdp"),
            P("fsdp", None),
            P("fsdp", None),
            P("fsdp", None),
            P("fsdp", None),
            P("fsdp"),
            P("fsdp", None),
            P("fsdp", None),
            P("fsdp", None),
        ),
        check_vma=False,
    )
```

```python
import functools
import math

import jax
import jax.numpy as jnp
from jax import lax
from jax.experimental import pallas as pl
from jax.experimental.pallas import tpu as pltpu
from jax.sharding import Mesh
from jax.sharding import PartitionSpec as P

QH = 16
KVH = 8
HD = 96


THETA = 100000.0
EPS = 1e-05
LOW = jnp.bfloat16
F32 = jnp.float32
NEG = -1e30
LN2 = math.log(2.0)


def contract(left, right, left_axis, right_axis):
    return lax.dot_general(
        left, right, (((left_axis,), (right_axis,)), ((), ())), preferred_element_type=F32
    )


def visible(first, second, query_block, key_block, size):
    key = key_block * size + lax.broadcasted_iota(jnp.int32, (size, size), 0)
    query = query_block * size + lax.broadcasted_iota(jnp.int32, (1, size), 1)
    start = jnp.where(query >= second, second, jnp.where(query >= first, first, 0))
    return (key >= start) & (key <= query)


def slot_of(block, count):
    return (block % (count // 2)) * 2 + block // (count // 2)


def forward_kernel(
    scalars,
    own_ref,
    other_ref,
    low_ref,
    full_ref,
    log_ref,
    query_s,
    key_s,
    value_s,
    top_s,
    total_s,
    mixed_s,
    *,
    size,
    count,
):
    half = scalars[0]
    first = scalars[1]
    second = scalars[2]
    here = pl.program_id(0)
    per_half = count // 2

    @pl.when(here == 0)
    def _():
        for ref, side in ((own_ref, half), (other_ref, 1 - half)):
            for step in range(per_half):
                block = side * per_half + step
                columns = slice(step * size, (step + 1) * size)
                query_s[block] = ref[0:HD, columns]
                key_s[block] = ref[HD : 2 * HD, columns].T
                value_s[block] = ref[2 * HD : 3 * HD, columns]

    query = query_s[here]
    top_s[...] = jnp.full_like(top_s, NEG)
    total_s[...] = jnp.zeros_like(total_s)
    mixed_s[...] = jnp.zeros_like(mixed_s)

    def add_block(block, masked):
        scores = contract(key_s[block], query, 1, 0)
        if masked:
            scores = jnp.where(visible(first, second, here, block, size), scores, NEG)
        old_top = top_s[...]
        top = jnp.maximum(old_top, jnp.max(scores, 0, keepdims=True))
        expo = jnp.exp2(scores - top)
        scale = jnp.exp2(old_top - top)
        top_s[...] = top
        total_s[...] = total_s[...] * scale + jnp.sum(expo, 0, keepdims=True)
        mixed_s[...] = mixed_s[...] * scale + contract(value_s[block], expo.astype(LOW), 1, 0)

    last = count - 1

    @pl.loop(1, jnp.where(here == last, 1, here))
    def _(block):
        add_block(block, False)

    @pl.loop(0, jnp.where(here == last, count, jnp.minimum(here + 1, 2)))
    def _(step):
        add_block(jnp.where(here == last, step, step * here), True)

    total = total_s[...]
    result = mixed_s[...] / total
    full_ref[0] = result
    low_ref[0] = result.astype(LOW)
    log_ref[0] = top_s[...] + jnp.log2(total)


def backward_kernel(
    scalars,
    own_ref,
    other_ref,
    grad_ref,
    full_ref,
    log_ref,
    kept_ref,
    leaving_ref,
    query_s,
    key_s,
    value_s,
    delta_s,
    query_grad_s,
    key_grad_s,
    value_grad_s,
    *,
    size,
    count,
):
    half = scalars[0]
    first = scalars[1]
    second = scalars[2]
    here = pl.program_id(0)
    per_half = count // 2

    @pl.when(here == 0)
    def _():
        for ref, side in ((own_ref, half), (other_ref, 1 - half)):
            for step in range(per_half):
                block = side * per_half + step
                columns = slice(step * size, (step + 1) * size)
                query_s[block] = ref[0:HD, columns]
                key_s[block] = ref[HD : 2 * HD, columns]
                value_s[block] = ref[2 * HD : 3 * HD, columns].T
        for block in range(count):
            delta_s[block] = jnp.sum(
                grad_ref[slot_of(block, count)].astype(F32) * full_ref[block], 0, keepdims=True
            )
        query_grad_s[...] = jnp.zeros_like(query_grad_s)

    key_grad_s[...] = jnp.zeros_like(key_grad_s)
    value_grad_s[...] = jnp.zeros_like(value_grad_s)
    key = key_s[here]
    key_rows = key.T
    value_rows = value_s[here]

    def add_block(block, masked):
        query = query_s[block]
        grad = grad_ref[slot_of(block, count)]
        scores = contract(key_rows, query, 1, 0)
        if masked:
            scores = jnp.where(visible(first, second, block, here, size), scores, NEG)
        probs = jnp.exp2(scores - log_ref[block])
        grad_probs = contract(value_rows, grad, 1, 0)
        grad_scores = (probs * (grad_probs - delta_s[block])).astype(LOW)
        value_grad_s[...] += contract(grad, probs.astype(LOW), 1, 1)
        key_grad_s[...] += contract(query, grad_scores, 1, 1)
        query_grad_s[block] += contract(key, grad_scores, 1, 0)

    last = count - 1

    @pl.loop(here + 1, jnp.where(here == 0, 1, last))
    def _(block):
        add_block(block, False)

    @pl.loop(0, jnp.where(here == 0, count, jnp.where(here == last, 1, 2)))
    def _(step):
        add_block(jnp.where(here == 0, step, jnp.where(step == 0, here, last)), True)

    side = here // per_half
    columns = pl.ds(pl.multiple_of((here % per_half) * size, size), size)

    def write(out_ref):
        out_ref[0:HD, columns] = (query_grad_s[here] * HD**-0.5).astype(LOW)
        out_ref[HD : 2 * HD, columns] = (key_grad_s[...] * LN2).astype(LOW)
        out_ref[2 * HD : 3 * HD, columns] = value_grad_s[...].astype(LOW)

    @pl.when(side == half)
    def _():
        write(kept_ref)

    @pl.when(side != half)
    def _():
        write(leaving_ref)


def attend_forward(scalars, own, other, size):
    count = 2 * own.shape[1] // size
    whole = lambda shape: pl.BlockSpec(shape, lambda i, s: (0,) * len(shape))
    pairs = count * (count + 1) // 2
    return pl.pallas_call(
        functools.partial(forward_kernel, size=size, count=count),
        grid_spec=pltpu.PrefetchScalarGridSpec(
            num_scalar_prefetch=1,
            grid=(count,),
            in_specs=[whole(own.shape), whole(other.shape)],
            out_specs=[
                pl.BlockSpec(
                    (1, HD, size), lambda i, s: (slot_of(i, count), 0, 0)
                ),
                pl.BlockSpec((1, HD, size), lambda i, s: (i, 0, 0)),
                pl.BlockSpec((1, 1, size), lambda i, s: (i, 0, 0)),
            ],
            scratch_shapes=[
                pltpu.VMEM((count, HD, size), LOW),
                pltpu.VMEM((count, size, HD), LOW),
                pltpu.VMEM((count, HD, size), LOW),
                pltpu.VMEM((1, size), F32),
                pltpu.VMEM((1, size), F32),
                pltpu.VMEM((HD, size), F32),
            ],
        ),
        out_shape=[
            jax.ShapeDtypeStruct((count, HD, size), LOW),
            jax.ShapeDtypeStruct((count, HD, size), F32),
            jax.ShapeDtypeStruct((count, 1, size), F32),
        ],
        compiler_params=pltpu.CompilerParams(
            dimension_semantics=("arbitrary",), vmem_limit_bytes=32 * 2**20
        ),
        cost_estimate=pl.CostEstimate(
            flops=pairs * size * size * HD * 32,
            bytes_accessed=10 * 2**20,
            transcendentals=pairs * size * size,
        ),
        name="attend_forward",
    )(scalars, own, other)


def attend_backward(scalars, own, other, grad, full, log_total):
    count, _, size = grad.shape
    whole = lambda shape: pl.BlockSpec(shape, lambda i, s: (0,) * len(shape))
    pairs = count * (count + 1) // 2
    out_shape = own.shape
    return pl.pallas_call(
        functools.partial(backward_kernel, size=size, count=count),
        grid_spec=pltpu.PrefetchScalarGridSpec(
            num_scalar_prefetch=1,
            grid=(count,),
            in_specs=[
                whole(own.shape),
                whole(other.shape),
                whole(grad.shape),
                whole(full.shape),
                whole(log_total.shape),
            ],
            out_specs=[whole(out_shape)] * 2,
            scratch_shapes=[
                pltpu.VMEM((count, HD, size), LOW),
                pltpu.VMEM((count, HD, size), LOW),
                pltpu.VMEM((count, size, HD), LOW),
                pltpu.VMEM((count, 1, size), F32),
                pltpu.VMEM((count, HD, size), F32),
                pltpu.VMEM((HD, size), F32),
                pltpu.VMEM((HD, size), F32),
            ],
        ),
        out_shape=[jax.ShapeDtypeStruct(out_shape, LOW)] * 2,
        compiler_params=pltpu.CompilerParams(
            dimension_semantics=("arbitrary",), vmem_limit_bytes=32 * 2**20
        ),
        cost_estimate=pl.CostEstimate(
            flops=pairs * size * size * HD * 42,
            bytes_accessed=16 * 2**20,
            transcendentals=pairs * size * size,
        ),
        name="attend_backward",
    )(scalars, own, other, grad, full, log_total)


def place_rows_kernel(order, *refs):
    pieces, out_ref = refs[:-1], refs[-1]
    size = pieces[0].shape[0]
    for index, piece in enumerate(pieces):
        start = pl.multiple_of(order[index] * size, size)
        out_ref[pl.ds(start, size), :] = piece[...].astype(F32)


def place_rows(order, pieces):
    size, width = pieces[0].shape
    total = size * len(pieces)
    step = 512
    return pl.pallas_call(
        place_rows_kernel,
        grid_spec=pltpu.PrefetchScalarGridSpec(
            num_scalar_prefetch=1,
            grid=(width // step,),
            in_specs=[pl.BlockSpec((size, step), lambda i, s: (0, i)) for _ in pieces],
            out_specs=pl.BlockSpec((total, step), lambda i, s: (0, i)),
        ),
        out_shape=jax.ShapeDtypeStruct((total, width), F32),
        compiler_params=pltpu.CompilerParams(vmem_limit_bytes=24 * 2**20),
        cost_estimate=pl.CostEstimate(
            flops=0, bytes_accessed=total * width * 6, transcendentals=0
        ),
        name="place_rows",
    )(order, *pieces)


def place_columns_kernel(order, gain_ref, gate_w_ref, up_w_ref, *refs):
    count = (len(refs) - 3) // 2
    gates, ups = refs[:count], refs[count : 2 * count]
    gate_ref, up_ref, sum_ref = refs[2 * count :]
    size = gates[0].shape[1]
    gain = gain_ref[...]
    total = jnp.zeros((gate_ref.shape[0], size), F32)
    for index in range(count):
        columns = pl.ds(pl.multiple_of(order[index] * size, size), size)
        gate, up = gates[index][...].astype(F32), ups[index][...].astype(F32)
        total += gate * gate_w_ref[:, columns].astype(F32)
        total += up * up_w_ref[:, columns].astype(F32)
        gate_ref[:, columns] = gate * gain
        up_ref[:, columns] = up * gain

    @pl.when(pl.program_id(0) == 0)
    def _():
        sum_ref[...] = jnp.zeros_like(sum_ref)

    sum_ref[...] += jnp.sum(total, 1, keepdims=True)


def place_columns(order, gain, gate_weight, up_weight, gates, ups, shards):
    rows, width = gate_weight.shape
    span = width // shards
    size = span // len(gates)
    wide = pl.BlockSpec((rows, span), lambda i, s: (0, i))
    thin = pl.BlockSpec((rows, 1), lambda i, s: (0, 0))
    pieces = [pl.BlockSpec((rows, size), lambda i, s: (0, i)) for _ in (*gates, *ups)]
    return pl.pallas_call(
        place_columns_kernel,
        grid_spec=pltpu.PrefetchScalarGridSpec(
            num_scalar_prefetch=1,
            grid=(shards,),
            in_specs=[thin, wide, wide, *pieces],
            out_specs=[wide, wide, thin],
        ),
        out_shape=[
            jax.ShapeDtypeStruct((rows, width), F32),
            jax.ShapeDtypeStruct((rows, width), F32),
            jax.ShapeDtypeStruct((rows, 1), F32),
        ],
        compiler_params=pltpu.CompilerParams(
            dimension_semantics=("arbitrary",), vmem_limit_bytes=24 * 2**20
        ),
        cost_estimate=pl.CostEstimate(
            flops=rows * width * 6, bytes_accessed=rows * width * 16, transcendentals=0
        ),
        name="place_columns",
    )(order, gain, gate_weight, up_weight, *gates, *ups)


def place_heads_kernel(gain_ref, query_w, key_w, value_w, all_ref, query_ref, key_ref, value_ref, sum_ref):
    rows = gain_ref.shape[0]
    wide = query_ref.shape[1] // KVH
    gain = gain_ref[...]
    total = jnp.zeros((rows, 4 * HD), F32)
    pieces = [all_ref[i * rows : (i + 1) * rows, :].astype(F32) for i in range(KVH)]
    for start in range(0, KVH, 2):
        value = jnp.concatenate([piece[:, :wide] for piece in pieces[start : start + 2]], 1)
        columns = slice(start * wide, (start + 2) * wide)
        total += value * query_w[:, columns].astype(F32)
        query_ref[:, columns] = value * gain
    for first, weight, out_ref in ((wide, key_w, key_ref), (wide + HD, value_w, value_ref)):
        for start in range(0, KVH, 4):
            value = jnp.concatenate(
                [piece[:, first : first + HD] for piece in pieces[start : start + 4]], 1
            )
            columns = slice(start * HD, (start + 4) * HD)
            total += value * weight[:, columns].astype(F32)
            out_ref[:, columns] = value * gain
    sum_ref[...] = jnp.sum(total, 1, keepdims=True)


def place_heads(gain, query_weight, key_weight, value_weight, pieces):
    weights = (query_weight, key_weight, value_weight)
    rows = gain.shape[0]
    return pl.pallas_call(
        place_heads_kernel,
        out_shape=[jax.ShapeDtypeStruct(weight.shape, F32) for weight in weights]
        + [jax.ShapeDtypeStruct((rows, 1), F32)],
        compiler_params=pltpu.CompilerParams(vmem_limit_bytes=32 * 2**20),
        cost_estimate=pl.CostEstimate(
            flops=rows * 3072 * 4, bytes_accessed=rows * 3072 * 8, transcendentals=0
        ),
        name="place_heads",
    )(gain, *weights, pieces)


def merge_kernel(scalars, kept_ref, came_ref, cosine_ref, sine_ref, out_ref, split_ref):
    lead = scalars[0] == 0
    lines, _, size = split_ref.shape
    for line in range(lines):
        columns = slice(line * size, (line + 1) * size)
        kept = kept_ref[:, columns].astype(F32)
        came = came_ref[:, columns].astype(F32)
        cosine, sine = cosine_ref[:, columns], sine_ref[:, columns]
        joint = kept[HD:] + came[HD:]
        first = jnp.where(lead, kept[:HD], came[:HD])
        second = jnp.where(lead, came[:HD], kept[:HD])
        turned = []
        for value in (first, second, joint[:HD]):
            low, high = value[: HD // 2], value[HD // 2 :]
            turned.append(low * cosine + high * sine)
            turned.append(high * cosine - low * sine)
        turned.append(joint[HD:])
        result = jnp.concatenate([part.astype(LOW) for part in turned], 0)
        out_ref[:, columns] = result
        split_ref[line] = result


def merge(scalars, kept, came, cosine, sine, lines):
    tokens = kept.shape[1]
    whole = lambda value: pl.BlockSpec(value.shape, lambda i, s: (0,) * len(value.shape))
    outs = [
        jax.ShapeDtypeStruct((4 * HD, tokens), LOW),
        jax.ShapeDtypeStruct((lines, 4 * HD, tokens // lines), LOW),
    ]
    return pl.pallas_call(
        merge_kernel,
        grid_spec=pltpu.PrefetchScalarGridSpec(
            num_scalar_prefetch=1,
            grid=(1,),
            in_specs=[whole(value) for value in (kept, came, cosine, sine)],
            out_specs=[whole(value) for value in outs],
        ),
        out_shape=outs,
        compiler_params=pltpu.CompilerParams(vmem_limit_bytes=24 * 2**20),
        cost_estimate=pl.CostEstimate(
            flops=tokens * HD * 24, bytes_accessed=tokens * HD * 30, transcendentals=0
        ),
        name="merge",
    )(scalars, kept, came, cosine, sine)


def pack_kernel(scalars, gain_ref, query_ref, key_ref, value_ref, *outs):
    core = scalars[3]
    gain = gain_ref[...]
    wide = query_ref.shape[1] // KVH
    span = wide + 2 * HD
    for which in range(2):

        @pl.when(core == which)
        def _():
            for line in range(KVH // 2):
                head = 2 * line + which
                value = jnp.concatenate(
                    [
                        query_ref[:, head * wide : (head + 1) * wide].astype(F32),
                        key_ref[:, head * HD : (head + 1) * HD].astype(F32),
                        value_ref[:, head * HD : (head + 1) * HD].astype(F32),
                    ],
                    1,
                )
                place = (line % 2) * span
                outs[line // 2][:, place : place + span] = (value * gain).astype(LOW)


def pack(scalars, gain, query_weight, key_weight, value_weight):
    rows, width = query_weight.shape
    whole = lambda value: pl.BlockSpec(value.shape, lambda i, s: (0, 0))
    weights = (gain, query_weight, key_weight, value_weight)
    outs = [jax.ShapeDtypeStruct((rows, width // 2), LOW)] * 2
    return pl.pallas_call(
        pack_kernel,
        grid_spec=pltpu.PrefetchScalarGridSpec(
            num_scalar_prefetch=1,
            grid=(1,),
            in_specs=[whole(value) for value in weights],
            out_specs=[whole(value) for value in outs],
        ),
        out_shape=outs,
        compiler_params=pltpu.CompilerParams(vmem_limit_bytes=24 * 2**20),
        cost_estimate=pl.CostEstimate(
            flops=rows * width, bytes_accessed=rows * width * 6, transcendentals=0
        ),
        name="pack",
    )(scalars, *weights)


def spread_kernel(scalars, lin_ref, cosine_ref, sine_ref, own_ref, leaving_ref):
    cosine, sine = cosine_ref[...], sine_ref[...]

    def turn(start, factor):
        low = lin_ref[start : start + HD // 2, :]
        high = lin_ref[start + HD // 2 : start + HD, :]
        turned = ((low * cosine - high * sine) * factor, (high * cosine + low * sine) * factor)
        return jnp.concatenate([part.astype(LOW) for part in turned], 0)

    lead = scalars[0] == 0
    first, second = turn(0, HD**-0.5 / LN2), turn(HD, HD**-0.5 / LN2)

    @pl.when(lead)
    def _():
        own_ref[0:HD] = first
        leaving_ref[0:HD] = second

    @pl.when(jnp.logical_not(lead))
    def _():
        own_ref[0:HD] = second
        leaving_ref[0:HD] = first

    key = turn(2 * HD, 1.0)
    value = lin_ref[3 * HD : 4 * HD].astype(LOW)
    for ref in (own_ref, leaving_ref):
        ref[HD : 2 * HD] = key
        ref[2 * HD : 3 * HD] = value


def spread(scalars, lin, cosine, sine):
    tokens = lin.shape[1]
    step = 512
    column = lambda rows: pl.BlockSpec((rows, step), lambda i, s: (0, i))
    return pl.pallas_call(
        spread_kernel,
        grid_spec=pltpu.PrefetchScalarGridSpec(
            num_scalar_prefetch=1,
            grid=(tokens // step,),
            in_specs=[column(4 * HD), column(HD // 2), column(HD // 2)],
            out_specs=[column(3 * HD)] * 2,
        ),
        out_shape=[jax.ShapeDtypeStruct((3 * HD, tokens), LOW)] * 2,
        compiler_params=pltpu.CompilerParams(vmem_limit_bytes=24 * 2**20),
        cost_estimate=pl.CostEstimate(
            flops=tokens * HD * 24, bytes_accessed=tokens * HD * 36, transcendentals=0
        ),
        name="spread",
    )(scalars, lin, cosine, sine)


def swap(value, axis):
    return lax.ppermute(value, axis, [(0, 1), (1, 0)])


def swap_near(value):
    return lax.ppermute(value, "z", [(0, 1), (1, 0), (2, 3), (3, 2)])


def swap_far(value):
    return lax.ppermute(value, "z", [(0, 2), (2, 0), (1, 3), (3, 1)])


def tie(*values):
    return lax.optimization_barrier(values)


def in_order(place, own, other):
    return (jnp.where(place == 0, own, other), jnp.where(place == 0, other, own))


def both(place, own, other):
    return jnp.concatenate(in_order(place, own, other), 0)


def spread_out(value, first, second):
    other = swap(value, first)
    pair = jnp.stack(in_order(lax.axis_index(first), value, other))
    return pair, swap(pair, second)


def placed(pair, other, second):
    pairs = in_order(lax.axis_index(second), pair, other)
    grid = jnp.stack(pairs, 0 if second == "y" else 1)
    return grid.reshape(-1, *grid.shape[3:])


def pick(array, axis, at):
    return lax.dynamic_index_in_dim(array, at, axis, keepdims=False)


def halve(value, axis, along=0):
    at = lax.axis_index(axis)
    return pick(value, along, at), swap(pick(value, along, 1 - at), axis)


def halve_x(value):
    return halve(value.reshape(2, 2, -1, value.shape[-1]), "x", 1)


def halve_y(value):
    return halve(value.reshape(2, 2, -1, value.shape[-1]), "y", 0)


def fast_body(
    tokens,
    positions,
    first_gain,
    query_weight,
    key_weight,
    value_weight,
    output_weight,
    second_gain,
    gate_weight,
    up_weight,
    down_weight,
    cotangent,
):
    seq = ("z", "c")
    fsdp = ("y", "x")
    z, core, half = lax.axis_index("z"), lax.axis_index("c"), lax.axis_index("x")
    near = z % 2
    lines = lax.axis_size("z")
    seq_count = 2 * lines
    shards = lax.axis_size("y") * 2
    spot = z * 2 + core
    quarter = near * 2 + core
    rows = tokens[0]
    count, width = rows.shape
    chip_count = 2 * count
    half_len = count * seq_count
    seq_len = 2 * half_len

    begins = jnp.where(
        (spot == 0) & (half == 0),
        count - 1 - positions[0, count - 1],
        half * half_len + spot * count - positions[0, 0],
    )
    ends = begins + (seq_len - count)
    scalars = jnp.stack([half, begins, ends, core]).astype(jnp.int32)

    gain_one = first_gain.astype(F32)[:, None]
    gain_two = second_gain.astype(F32)[:, None]

    def row_scale(value):
        return lax.rsqrt(jnp.mean(value * value, -1, keepdims=True) + EPS)

    take = functools.partial(lax.dynamic_slice_in_dim, axis=1)
    take_rows = functools.partial(lax.dynamic_slice_in_dim, axis=0)
    gather = lambda value, axes: lax.all_gather(value, axes, axis=0, tiled=True)
    own_rows = rows.astype(F32)
    own_unit_scale = row_scale(own_rows)
    own_unit = own_rows * own_unit_scale
    units = gather(own_unit.astype(LOW), seq)
    wide = QH // KVH * HD
    qkv_shard = (
        jnp.concatenate(
            [
                take(query_weight, spot * wide, wide),
                take(key_weight, spot * HD, HD),
                take(value_weight, spot * HD, HD),
            ],
            1,
        ).astype(F32)
        * gain_one
    ).astype(LOW)
    out_rows = output_weight.shape[0] // 2
    out_shard = take_rows(output_weight, core * out_rows, out_rows)
    piece = down_weight.shape[0] // 4
    down_shard = take_rows(down_weight, quarter * piece, piece)
    gate_shard, up_shard = (
        (
            jnp.concatenate(
                [
                    take(weight, shard * 4 * piece + quarter * piece, piece)
                    for shard in range(shards)
                ],
                1,
            ).astype(F32)
            * gain_two
        ).astype(LOW)
        for weight in (gate_weight, up_weight)
    )
    side = lax.axis_index("y")
    qkv_pair = jnp.stack(in_order(half, qkv_shard, swap(qkv_shard, "x")))
    gate_pair = jnp.stack(in_order(half, gate_shard, swap(gate_shard, "x")))
    up_pair = jnp.stack(in_order(side, up_shard, swap(up_shard, "y")))
    qkv_pair, gate_pair, up_pair = tie(qkv_pair, gate_pair, up_pair)
    qkv_w = placed(qkv_pair, swap(qkv_pair, "y"), "y")
    gate_pair, up_pair = (gate_pair, swap(gate_pair, "y")), (up_pair, swap(up_pair, "x"))

    place = half * half_len + jnp.arange(half_len, dtype=jnp.int32)
    start = jnp.where(place >= ends, ends, jnp.where(place >= begins, begins, 0))
    freq = THETA ** (-(jnp.arange(HD // 2, dtype=F32) * 2.0 / HD))
    angle = freq[:, None] * (place - start).astype(F32)[None, :]
    cosine, sine = jnp.cos(angle), jnp.sin(angle)
    chip_rows = both(core, rows, swap(rows, "c"))
    units, own_cot, chip_rows = tie(units, cotangent[0], chip_rows)
    own, leaving = spread(scalars, contract(qkv_w, units, 0, 1), cosine, sine)

    near_cot = swap_near(own_cot)
    other, out_shard, down_shard, near_cot, chip_cot, gate_pair, up_pair = tie(
        swap(leaving, "x"),
        out_shard,
        down_shard,
        near_cot,
        both(core, own_cot, swap(own_cot, "c")),
        gate_pair,
        up_pair,
    )
    out_w = gather(out_shard, fsdp)
    down_w = gather(down_shard, fsdp)
    near_other = swap(near_cot, "c")
    head_low, head_full, log_total = attend_forward(scalars, own, other, chip_count)
    exchange = lambda value: lax.all_to_all(
        value, ("z", "x"), split_axis=0, concat_axis=0, tiled=True
    )
    head_low, near_other = tie(head_low, near_other)
    lead_shard, tail_shard = pack(scalars, gain_one, query_weight, key_weight, value_weight)
    heads, gate_w, up_w, near_cot, lead_shard = tie(
        exchange(head_low),
        placed(*gate_pair, "y"),
        placed(*up_pair, "x"),
        jnp.concatenate([near_cot, near_other], 0),
        lead_shard,
    )
    lead_w = gather(lead_shard, fsdp)
    heads = heads.reshape(QH // 2 * HD, chip_count)

    mine_of = lambda value: take_rows(value, core * count, count)
    theirs_of = lambda value: take_rows(value, (1 - core) * count, count)
    branch = contract(heads, out_w, 0, 0).astype(LOW)
    middle = chip_rows.astype(F32) + (branch.astype(F32) + swap(branch, "c").astype(F32))
    middle_scale = row_scale(middle)
    chip_unit = middle * middle_scale
    own_middle, own_scale, own_middle_unit = (
        mine_of(middle),
        mine_of(middle_scale),
        mine_of(chip_unit),
    )
    chip_unit = chip_unit.astype(LOW)
    near_unit = swap_near(mine_of(chip_unit))

    def feed(unit):
        gate, upper = contract(unit, gate_w, 1, 0), contract(unit, up_w, 1, 0)
        sigma = jax.nn.sigmoid(gate)
        silu = gate * sigma
        return (silu * upper).astype(LOW), (gate, upper, sigma, silu)

    def feed_back(cot, kept):
        gate, upper, sigma, silu = kept
        grad_hidden = contract(cot, down_w, 1, 1)
        gate_low = (grad_hidden * upper * sigma * (1.0 + gate * (1.0 - sigma))).astype(LOW)
        upper_low = (grad_hidden * silu).astype(LOW)
        part = contract(gate_low, gate_w, 1, 1) + contract(upper_low, up_w, 1, 1)
        return gate_low, upper_low, part

    def chip_sum(chip_part, near_part):
        near_sum = near_part[:count].astype(F32) + swap(near_part[count:].astype(LOW), "c")
        own_sum = mine_of(chip_part).astype(F32) + swap(theirs_of(chip_part).astype(LOW), "c")
        return own_sum, near_sum.astype(LOW)

    stack = lambda first, second: jnp.concatenate([first, second], 0)
    scatter = lambda value: lax.psum_scatter(value, fsdp, scatter_dimension=0, tiled=True)
    chip_hidden, chip_kept = feed(chip_unit)
    near_unit, chip_hidden = tie(near_unit, chip_hidden)
    near_unit = jnp.concatenate([near_unit, swap(near_unit, "c")], 0)
    near_hidden, near_kept = feed(near_unit)
    down_part = contract(
        stack(chip_hidden, near_hidden), stack(chip_cot, near_cot), 0, 0
    ).astype(LOW)
    near_cot, down_part = tie(near_cot, down_part)
    near_gate, near_upper, near_part = feed_back(near_cot, near_kept)
    chip_gate, chip_upper, chip_part = feed_back(chip_cot, chip_kept)
    grad_two, near_sum = chip_sum(chip_part, near_part)

    def halves_first(value):
        cut = value.shape[-1] // 2
        return halve_x(value[:, :cut]), halve_y(value[:, cut:])

    def halves_second(firsts):
        return halve(sum(firsts[0]), "y"), halve(sum(firsts[1]), "x")

    def halves_end(seconds):
        return jnp.concatenate([sum(seconds[0]), sum(seconds[1])], 1)

    down_first = halves_first(down_part)
    near_sum, near_gate, near_upper, chip_part = tie(
        near_sum, near_gate, near_upper, chip_part
    )
    grad_came = swap_near(near_sum)
    all_units = stack(chip_unit, near_unit)
    gate_part = contract(all_units, stack(chip_gate, near_gate), 0, 0).astype(LOW)
    up_part = contract(all_units, stack(chip_upper, near_upper), 0, 0).astype(LOW)
    feed_own, feed_near = chip_sum(
        contract(chip_hidden, down_w, 1, 0), contract(near_hidden, down_w, 1, 0)
    )
    gate_part, up_part, down_first, grad_came, feed_near = tie(
        gate_part, up_part, down_first, grad_came, feed_near
    )
    feed_near = swap_near(feed_near)
    down_second = halves_second(down_first)
    gate_grad, up_grad = scatter(gate_part), scatter(up_part)
    grad_two = grad_two + grad_came.astype(F32)
    grad_middle = own_cot.astype(F32) + own_scale * (
        grad_two - own_middle_unit * jnp.mean(grad_two * own_middle_unit, -1, keepdims=True)
    )
    own_branch, lead_w = tie(grad_middle.astype(LOW), lead_w)
    grad_branch = both(core, own_branch, swap(own_branch, "c"))
    grad_heads = contract(out_w, grad_branch, 1, 1).astype(LOW)
    grad_heads, grad_branch, down_second, feed_near = tie(
        grad_heads, grad_branch, down_second, feed_near
    )
    down_grad = halves_end(down_second)
    down_far = swap_far(down_grad)
    output_part = contract(heads, grad_branch, 1, 0).astype(LOW)
    output_grad = scatter(output_part)
    grad_head, output_part, gate_grad = tie(
        exchange(grad_heads.reshape(2 * lines, HD, chip_count)), output_part, gate_grad
    )

    gate_far = swap_far(gate_grad)
    kept, leaving = attend_backward(scalars, own, other, grad_head, head_full, log_total)
    kept, leaving, gate_far, down_far, up_grad, tail_shard = tie(
        kept, leaving, gate_far, down_far, up_grad, tail_shard
    )
    down_sum = down_grad + down_far
    down_near = swap_near(down_sum)
    tail_w = gather(tail_shard, fsdp)

    up_far = swap_far(up_grad)
    gate_sum = gate_grad + gate_far
    gate_near = swap_near(gate_sum)
    block_output = (own_middle + feed_own + feed_near.astype(F32)).astype(LOW)[None]
    came, up_far, gate_near, down_near, block_output, output_grad = tie(
        swap(leaving, "x"), up_far, gate_near, down_near, block_output, output_grad
    )

    qkv_low, by_line = merge(scalars, kept, came, cosine, sine, lines)
    token_grads = lax.all_to_all(by_line, "z", split_axis=0, concat_axis=0, tiled=True)
    qkv_part = contract(units, qkv_low, 0, 1).astype(LOW).reshape(shards, 2, -1, 4 * HD)
    qkv_first = halve_x(qkv_part[:, 0]), halve_y(qkv_part[:, 1])
    qkv_second = halves_second(qkv_first)
    qkv_grad = jnp.concatenate([sum(qkv_second[0]), sum(qkv_second[1])], 0)
    output_came = swap_near(output_grad)
    up_sum = up_grad + up_far
    up_near = swap_near(up_sum)
    token_grads, qkv_grad, output_came, up_near = tie(
        token_grads, qkv_grad, output_came, up_near
    )
    all_qkv = gather(qkv_grad, seq)
    output_sum = output_grad + output_came
    output_far = swap_far(output_sum)

    token_grads = token_grads.reshape(-1, chip_count)
    split = lead_w.shape[1]
    grad_one = contract(token_grads[:split], lead_w, 0, 1) + contract(
        token_grads[split:], tail_w, 0, 1
    )
    grad_one = mine_of(grad_one) + swap(theirs_of(grad_one).astype(LOW), "c").astype(F32)
    grad_rows = own_unit_scale * (
        grad_one - own_unit * jnp.mean(grad_one * own_unit, -1, keepdims=True)
    )
    input_grad = (grad_middle + grad_rows).astype(LOW)[None]

    def four(value, near_value):
        return value, swap(value, "c"), near_value, swap(near_value, "c")

    order = jnp.stack([quarter, quarter ^ 1, quarter ^ 2, quarter ^ 3]).astype(jnp.int32)
    core_order = jnp.stack([core, 1 - core]).astype(jnp.int32)
    down_total = place_rows(order, four(down_sum, down_near))
    gate_total, up_total, second_gain_grad = place_columns(
        order, gain_two, gate_weight, up_weight, four(gate_sum, gate_near), four(up_sum, up_near), shards
    )
    output_far, second_gain_grad = tie(output_far, second_gain_grad)
    output_own = output_sum + output_far
    output_total = place_rows(core_order, (output_own, swap(output_own, "c")))
    query_grad, key_grad, value_grad, first_gain_grad = place_heads(
        gain_one, query_weight, key_weight, value_weight, all_qkv
    )
    return (
        block_output,
        input_grad,
        first_gain_grad[:, 0],
        query_grad,
        key_grad,
        value_grad,
        output_total,
        second_gain_grad[:, 0],
        gate_total,
        up_total,
        down_total,
    )


def fast_solution(mesh):
    seq_count, shard_count = mesh.devices.shape
    fine = Mesh(
        mesh.devices.reshape(seq_count // 2, 2, shard_count // 2, 2), ("z", "c", "y", "x")
    )
    seq, fsdp = ("z", "c"), ("y", "x")
    matrix = P(fsdp, None)
    return jax.shard_map(
        fast_body,
        mesh=fine,
        in_specs=(
            P(fsdp, seq, None),
            P(fsdp, seq),
            P(fsdp),
            matrix,
            matrix,
            matrix,
            matrix,
            P(fsdp),
            matrix,
            matrix,
            matrix,
            P(fsdp, seq, None),
        ),
        out_specs=(
            P(fsdp, seq, None),
            P(fsdp, seq, None),
            P(fsdp),
            matrix,
            matrix,
            matrix,
            matrix,
            P(fsdp),
            matrix,
            matrix,
            matrix,
        ),
        check_vma=False,
    )


def solution(mesh):
    shape = dict(mesh.shape)
    if shape["seq"] == KVH and shape["fsdp"] == 4:
        return fast_solution(mesh)
    return plain_solution(mesh)


def shifted(value, axis, steps):
    count = lax.axis_size(axis)
    first, last = (max(0, -steps), min(count, count - steps))
    return lax.ppermute(value, axis, [(source, source + steps) for source in range(first, last)])


def rope_tables(position_rows):
    freq = THETA ** (-(jnp.arange(HD // 2, dtype=jnp.float32) * 2.0 / HD))
    angle = position_rows.astype(jnp.float32)[:, None] * freq[None, :]
    cosine = jnp.cos(angle)
    sine = jnp.sin(angle)
    return (jnp.concatenate([cosine, cosine], -1), jnp.concatenate([sine, sine], -1))


def rotate(values, cosine, sine):
    half = HD // 2
    turned = jnp.concatenate([-values[..., half:], values[..., :half]], -1)
    return values * cosine[:, None, :] + turned * sine[:, None, :]


def rotate_back(grads, cosine, sine):
    half = HD // 2
    scaled = grads * sine[:, None, :]
    turned = jnp.concatenate([scaled[..., half:], -scaled[..., :half]], -1)
    return grads * cosine[:, None, :] + turned


def norm_forward(rows, gain):
    scale = lax.rsqrt(jnp.mean(rows * rows, -1, keepdims=True) + EPS)
    unit = rows * scale
    return (unit * gain, unit, scale)


def norm_backward(grad_out, unit, scale, gain):
    grad_unit = grad_out * gain
    gain_grad = jnp.sum(grad_out * unit, 0)
    grad_rows = scale * (grad_unit - unit * jnp.mean(grad_unit * unit, -1, keepdims=True))
    return (grad_rows, gain_grad)


def plain_body(
    tokens,
    positions,
    first_gain,
    query_weight,
    key_weight,
    value_weight,
    output_weight,
    second_gain,
    gate_weight,
    up_weight,
    down_weight,
    cotangent,
):
    seq_count = lax.axis_size("seq")
    local_rows = tokens[0]
    token_count = local_rows.shape[0]
    half_len = token_count * seq_count
    rows_float = local_rows.astype(jnp.float32)
    gain_one, wq_full, wk_full, wv_full, wo_full = (
        lax.all_gather(first_gain, "fsdp", axis=0, tiled=True),
        lax.all_gather(query_weight, "fsdp", axis=0, tiled=True),
        lax.all_gather(key_weight, "fsdp", axis=0, tiled=True),
        lax.all_gather(value_weight, "fsdp", axis=0, tiled=True),
        lax.all_gather(output_weight, "fsdp", axis=0, tiled=True),
    )
    gain_one = gain_one.astype(jnp.float32)
    normed_one, unit_one, scale_one = norm_forward(rows_float, gain_one)
    normed_low = normed_one.astype(jnp.bfloat16)
    cosine, sine = rope_tables(positions[0])
    query_lin = jnp.dot(normed_low, wq_full, preferred_element_type=jnp.float32).reshape(
        token_count, QH, HD
    )
    key_lin = jnp.dot(normed_low, wk_full, preferred_element_type=jnp.float32).reshape(
        token_count, KVH, HD
    )
    value_lin = jnp.dot(normed_low, wv_full, preferred_element_type=jnp.float32).reshape(
        token_count, KVH, HD
    )
    query_rows = rotate(query_lin, cosine, sine).astype(jnp.bfloat16)
    key_rows = rotate(key_lin, cosine, sine).astype(jnp.bfloat16)
    value_rows = value_lin.astype(jnp.bfloat16)
    repeat = max(1, seq_count // KVH)
    if repeat > 1:
        key_rows = jnp.repeat(key_rows, repeat, axis=1)
        value_rows = jnp.repeat(value_rows, repeat, axis=1)
    query_heads, key_heads, value_heads = (
        lax.all_to_all(query_rows, "seq", split_axis=1, concat_axis=0, tiled=True),
        lax.all_to_all(key_rows, "seq", split_axis=1, concat_axis=0, tiled=True),
        lax.all_to_all(value_rows, "seq", split_axis=1, concat_axis=0, tiled=True),
    )
    head_count = query_heads.shape[1]
    pair_count = key_heads.shape[1]
    group = head_count // pair_count
    half_positions = lax.all_gather(positions[0], "seq", axis=0, tiled=True)
    key_prior, value_prior = shifted((key_heads, value_heads), "fsdp", 1)
    key_all = jnp.concatenate([key_prior, key_heads], 0)
    value_all = jnp.concatenate([value_prior, value_heads], 0)
    half_index = lax.axis_index("fsdp") % 2
    key_index = (half_index - 1) * half_len + jnp.arange(2 * half_len, dtype=jnp.int32)
    row_index = half_index * half_len + jnp.arange(half_len, dtype=jnp.int32)
    row_start = row_index - half_positions
    block = min(512, half_len)
    count = half_len // block
    factor = HD ** (-0.5)
    query_blocks = query_heads.reshape(count, block, pair_count, group, HD)
    index_blocks = row_index.reshape(count, block)
    start_blocks = row_start.reshape(count, block)

    def block_scores(query_block, index_block, start_block):
        scores = (
            jnp.einsum("bkgd,tkd->kgbt", query_block, key_all, preferred_element_type=jnp.float32)
            * factor
        )
        visible = (key_index[None, :] >= start_block[:, None]) & (
            key_index[None, :] <= index_block[:, None]
        )
        return jnp.where(visible, scores, -1e30)

    def forward_block(items):
        query_block, index_block, start_block = items
        scores = block_scores(query_block, index_block, start_block)
        top = jnp.max(scores, -1, keepdims=True)
        expo = jnp.exp(scores - top)
        total = jnp.sum(expo, -1, keepdims=True)
        probs_low = (expo / total).astype(jnp.bfloat16)
        mixed = jnp.einsum(
            "kgbt,tkd->bkgd", probs_low, value_all, preferred_element_type=jnp.float32
        )
        return (mixed.reshape(block, head_count, HD).astype(jnp.bfloat16), top + jnp.log(total))

    head_blocks, log_totals = lax.map(forward_block, (query_blocks, index_blocks, start_blocks))
    head_out = head_blocks.reshape(half_len, head_count, HD)
    token_heads = lax.all_to_all(head_out, "seq", split_axis=0, concat_axis=1, tiled=True)
    heads_flat = token_heads.reshape(token_count, QH * HD)
    middle = rows_float + jnp.dot(heads_flat, wo_full, preferred_element_type=jnp.float32)
    gain_two, wg_full, wu_full, wd_full = (
        lax.all_gather(second_gain, "fsdp", axis=0, tiled=True),
        lax.all_gather(gate_weight, "fsdp", axis=0, tiled=True),
        lax.all_gather(up_weight, "fsdp", axis=0, tiled=True),
        lax.all_gather(down_weight, "fsdp", axis=0, tiled=True),
    )
    gain_two = gain_two.astype(jnp.float32)
    normed_two, unit_two, scale_two = norm_forward(middle, gain_two)
    normed_two_low = normed_two.astype(jnp.bfloat16)
    gate = jnp.dot(normed_two_low, wg_full, preferred_element_type=jnp.float32)
    upper = jnp.dot(normed_two_low, wu_full, preferred_element_type=jnp.float32)
    hidden = (jax.nn.silu(gate) * upper).astype(jnp.bfloat16)
    result = middle + jnp.dot(hidden, wd_full, preferred_element_type=jnp.float32)
    block_output = result.astype(jnp.bfloat16)[None]
    grad_low = cotangent[0]
    grad_rows = grad_low.astype(jnp.float32)
    down_grad = jnp.einsum("tf,td->fd", hidden, grad_low, preferred_element_type=jnp.float32)
    grad_hidden = jnp.einsum("td,fd->tf", grad_low, wd_full, preferred_element_type=jnp.float32)
    sigma = jax.nn.sigmoid(gate)
    gate_low = (grad_hidden * upper * sigma * (1.0 + gate * (1.0 - sigma))).astype(jnp.bfloat16)
    upper_low = (grad_hidden * gate * sigma).astype(jnp.bfloat16)
    gate_grad = jnp.einsum(
        "td,tf->df", normed_two_low, gate_low, preferred_element_type=jnp.float32
    )
    up_grad = jnp.einsum("td,tf->df", normed_two_low, upper_low, preferred_element_type=jnp.float32)
    grad_normed_two = jnp.einsum(
        "tf,df->td", gate_low, wg_full, preferred_element_type=jnp.float32
    ) + jnp.einsum("tf,df->td", upper_low, wu_full, preferred_element_type=jnp.float32)
    grad_middle_norm, second_gain_grad = norm_backward(
        grad_normed_two, unit_two, scale_two, gain_two
    )
    grad_middle = grad_rows + grad_middle_norm
    grad_branch = grad_middle.astype(jnp.bfloat16)
    output_grad = jnp.einsum(
        "tc,td->cd", heads_flat, grad_branch, preferred_element_type=jnp.float32
    )
    grad_heads = (
        jnp.einsum("td,cd->tc", grad_branch, wo_full, preferred_element_type=jnp.float32)
        .astype(jnp.bfloat16)
        .reshape(token_count, QH, HD)
    )
    grad_head_rows = lax.all_to_all(grad_heads, "seq", split_axis=1, concat_axis=0, tiled=True)
    grad_blocks = grad_head_rows.reshape(count, block, pair_count, group, HD)

    def backward_block(carry, items):
        key_acc, value_acc = carry
        query_block, index_block, start_block, grad_block, log_block = items
        scores = block_scores(query_block, index_block, start_block)
        probs = jnp.exp(scores - log_block)
        probs_low = probs.astype(jnp.bfloat16)
        grad_probs = jnp.einsum(
            "bkgd,tkd->kgbt", grad_block, value_all, preferred_element_type=jnp.float32
        )
        grad_scores = (
            probs * (grad_probs - jnp.sum(probs * grad_probs, -1, keepdims=True))
        ).astype(jnp.bfloat16)
        query_grad_block = (
            jnp.einsum("kgbt,tkd->bkgd", grad_scores, key_all, preferred_element_type=jnp.float32)
            * factor
        )
        key_acc = (
            key_acc
            + jnp.einsum(
                "kgbt,bkgd->tkd", grad_scores, query_block, preferred_element_type=jnp.float32
            )
            * factor
        )
        value_acc = value_acc + jnp.einsum(
            "kgbt,bkgd->tkd", probs_low, grad_block, preferred_element_type=jnp.float32
        )
        return ((key_acc, value_acc), query_grad_block.reshape(block, head_count, HD))

    empty = jnp.zeros((2 * half_len, pair_count, HD), jnp.float32)
    (key_acc, value_acc), query_grad_blocks = lax.scan(
        backward_block,
        (empty, empty),
        (query_blocks, index_blocks, start_blocks, grad_blocks, log_totals),
    )
    key_back, value_back = (
        shifted(key_acc[:half_len].astype(jnp.bfloat16), "fsdp", -1).astype(jnp.float32),
        shifted(value_acc[:half_len].astype(jnp.bfloat16), "fsdp", -1).astype(jnp.float32),
    )
    key_local = key_acc[half_len:] + key_back
    value_local = value_acc[half_len:] + value_back
    query_grad_heads = query_grad_blocks.reshape(half_len, head_count, HD)
    grad_query_tok, grad_key_tok, grad_value_tok = (
        lax.all_to_all(
            query_grad_heads.astype(jnp.bfloat16), "seq", split_axis=0, concat_axis=1, tiled=True
        ).astype(query_grad_heads.dtype),
        lax.all_to_all(
            key_local.astype(jnp.bfloat16), "seq", split_axis=0, concat_axis=1, tiled=True
        ).astype(key_local.dtype),
        lax.all_to_all(
            value_local.astype(jnp.bfloat16), "seq", split_axis=0, concat_axis=1, tiled=True
        ).astype(value_local.dtype),
    )
    if repeat > 1:
        grad_key_tok = grad_key_tok.reshape(token_count, KVH, repeat, HD).sum(2)
        grad_value_tok = grad_value_tok.reshape(token_count, KVH, repeat, HD).sum(2)
    query_lin_grad = (
        rotate_back(grad_query_tok, cosine, sine).astype(jnp.bfloat16).reshape(token_count, QH * HD)
    )
    key_lin_grad = (
        rotate_back(grad_key_tok, cosine, sine).astype(jnp.bfloat16).reshape(token_count, KVH * HD)
    )
    value_lin_grad = grad_value_tok.astype(jnp.bfloat16).reshape(token_count, KVH * HD)
    query_grad = jnp.einsum(
        "td,tc->dc", normed_low, query_lin_grad, preferred_element_type=jnp.float32
    )
    key_grad = jnp.einsum("td,tc->dc", normed_low, key_lin_grad, preferred_element_type=jnp.float32)
    value_grad = jnp.einsum(
        "td,tc->dc", normed_low, value_lin_grad, preferred_element_type=jnp.float32
    )
    grad_normed_one = jnp.einsum(
        "tc,dc->td", query_lin_grad, wq_full, preferred_element_type=jnp.float32
    )
    grad_normed_one = grad_normed_one + jnp.einsum(
        "tc,dc->td", key_lin_grad, wk_full, preferred_element_type=jnp.float32
    )
    grad_normed_one = grad_normed_one + jnp.einsum(
        "tc,dc->td", value_lin_grad, wv_full, preferred_element_type=jnp.float32
    )
    grad_rows_one, first_gain_grad = norm_backward(grad_normed_one, unit_one, scale_one, gain_one)
    input_grad = (grad_middle + grad_rows_one).astype(jnp.bfloat16)[None]
    pieces = (
        lax.psum_scatter(
            first_gain_grad.astype(jnp.bfloat16), "fsdp", scatter_dimension=0, tiled=True
        ).astype(jnp.float32),
        lax.psum_scatter(
            query_grad.astype(jnp.bfloat16), "fsdp", scatter_dimension=0, tiled=True
        ).astype(jnp.float32),
        lax.psum_scatter(
            key_grad.astype(jnp.bfloat16), "fsdp", scatter_dimension=0, tiled=True
        ).astype(jnp.float32),
        lax.psum_scatter(
            value_grad.astype(jnp.bfloat16), "fsdp", scatter_dimension=0, tiled=True
        ).astype(jnp.float32),
        lax.psum_scatter(
            output_grad.astype(jnp.bfloat16), "fsdp", scatter_dimension=0, tiled=True
        ).astype(jnp.float32),
        lax.psum_scatter(
            second_gain_grad.astype(jnp.bfloat16), "fsdp", scatter_dimension=0, tiled=True
        ).astype(jnp.float32),
        lax.psum_scatter(
            gate_grad.astype(jnp.bfloat16), "fsdp", scatter_dimension=0, tiled=True
        ).astype(jnp.float32),
        lax.psum_scatter(
            up_grad.astype(jnp.bfloat16), "fsdp", scatter_dimension=0, tiled=True
        ).astype(jnp.float32),
        lax.psum_scatter(
            down_grad.astype(jnp.bfloat16), "fsdp", scatter_dimension=0, tiled=True
        ).astype(jnp.float32),
    )
    shares = (
        lax.psum(pieces[0].astype(jnp.bfloat16), "seq").astype(jnp.float32),
        lax.psum(pieces[1].astype(jnp.bfloat16), "seq").astype(jnp.float32),
        lax.psum(pieces[2].astype(jnp.bfloat16), "seq").astype(jnp.float32),
        lax.psum(pieces[3].astype(jnp.bfloat16), "seq").astype(jnp.float32),
        lax.psum(pieces[4].astype(jnp.bfloat16), "seq").astype(jnp.float32),
        lax.psum(pieces[5].astype(jnp.bfloat16), "seq").astype(jnp.float32),
        lax.psum(pieces[6].astype(jnp.bfloat16), "seq").astype(jnp.float32),
        lax.psum(pieces[7].astype(jnp.bfloat16), "seq").astype(jnp.float32),
        lax.psum(pieces[8].astype(jnp.bfloat16), "seq").astype(jnp.float32),
    )
    return (
        block_output,
        input_grad,
        shares[0],
        shares[1],
        shares[2],
        shares[3],
        shares[4],
        shares[5],
        shares[6],
        shares[7],
        shares[8],
    )


def plain_solution(mesh):
    placed = (
        P("fsdp", "seq", None),
        P("fsdp", "seq"),
        P("fsdp"),
        P("fsdp", None),
        P("fsdp", None),
        P("fsdp", None),
        P("fsdp", None),
        P("fsdp"),
        P("fsdp", None),
        P("fsdp", None),
        P("fsdp", None),
        P("fsdp", "seq", None),
    )
    return jax.shard_map(
        plain_body,
        mesh=mesh,
        in_specs=placed,
        out_specs=(
            P("fsdp", "seq", None),
            P("fsdp", "seq", None),
            P("fsdp"),
            P("fsdp", None),
            P("fsdp", None),
            P("fsdp", None),
            P("fsdp", None),
            P("fsdp"),
            P("fsdp", None),
            P("fsdp", None),
            P("fsdp", None),
        ),
        check_vma=False,
    )
```

```python
import functools
import math

import jax
import jax.numpy as jnp
from jax import lax
from jax.experimental import pallas as pl
from jax.experimental.pallas import tpu as pltpu
from jax.sharding import Mesh
from jax.sharding import PartitionSpec as P

QH = 16
KVH = 8
HD = 96


THETA = 100000.0
EPS = 1e-05
LOW = jnp.bfloat16
F32 = jnp.float32
NEG = -1e30
LN2 = math.log(2.0)


def contract(left, right, left_axis, right_axis):
    return lax.dot_general(
        left, right, (((left_axis,), (right_axis,)), ((), ())), preferred_element_type=F32
    )


def visible(first, second, query_block, key_block, size):
    key = key_block * size + lax.broadcasted_iota(jnp.int32, (size, size), 0)
    query = query_block * size + lax.broadcasted_iota(jnp.int32, (1, size), 1)
    start = jnp.where(query >= second, second, jnp.where(query >= first, first, 0))
    return (key >= start) & (key <= query)


def slot_of(block, count):
    return (block % (count // 2)) * 2 + block // (count // 2)


def forward_kernel(
    scalars,
    own_ref,
    other_ref,
    low_ref,
    full_ref,
    log_ref,
    query_s,
    key_s,
    value_s,
    top_s,
    total_s,
    mixed_s,
    *,
    size,
    count,
):
    half = scalars[0]
    first = scalars[1]
    second = scalars[2]
    here = pl.program_id(0)
    per_half = count // 2

    @pl.when(here == 0)
    def _():
        for ref, side in ((own_ref, half), (other_ref, 1 - half)):
            for step in range(per_half):
                block = side * per_half + step
                columns = slice(step * size, (step + 1) * size)
                query_s[block] = ref[0:HD, columns]
                key_s[block] = ref[HD : 2 * HD, columns].T
                value_s[block] = ref[2 * HD : 3 * HD, columns]

    query = query_s[here]
    top_s[...] = jnp.full_like(top_s, NEG)
    total_s[...] = jnp.zeros_like(total_s)
    mixed_s[...] = jnp.zeros_like(mixed_s)

    def add_block(block, masked):
        scores = contract(key_s[block], query, 1, 0)
        if masked:
            scores = jnp.where(visible(first, second, here, block, size), scores, NEG)
        old_top = top_s[...]
        top = jnp.maximum(old_top, jnp.max(scores, 0, keepdims=True))
        expo = jnp.exp2(scores - top)
        scale = jnp.exp2(old_top - top)
        top_s[...] = top
        total_s[...] = total_s[...] * scale + jnp.sum(expo, 0, keepdims=True)
        mixed_s[...] = mixed_s[...] * scale + contract(value_s[block], expo.astype(LOW), 1, 0)

    last = count - 1

    @pl.loop(1, jnp.where(here == last, 1, here))
    def _(block):
        add_block(block, False)

    @pl.loop(0, jnp.where(here == last, count, jnp.minimum(here + 1, 2)))
    def _(step):
        add_block(jnp.where(here == last, step, step * here), True)

    total = total_s[...]
    result = mixed_s[...] / total
    full_ref[0] = result
    low_ref[0] = result.astype(LOW)
    log_ref[0] = top_s[...] + jnp.log2(total)


def backward_kernel(
    scalars,
    own_ref,
    other_ref,
    grad_ref,
    full_ref,
    log_ref,
    kept_ref,
    leaving_ref,
    query_s,
    key_s,
    value_s,
    delta_s,
    query_grad_s,
    key_grad_s,
    value_grad_s,
    *,
    size,
    count,
):
    half = scalars[0]
    first = scalars[1]
    second = scalars[2]
    here = pl.program_id(0)
    per_half = count // 2

    @pl.when(here == 0)
    def _():
        for ref, side in ((own_ref, half), (other_ref, 1 - half)):
            for step in range(per_half):
                block = side * per_half + step
                columns = slice(step * size, (step + 1) * size)
                query_s[block] = ref[0:HD, columns]
                key_s[block] = ref[HD : 2 * HD, columns]
                value_s[block] = ref[2 * HD : 3 * HD, columns].T
        for block in range(count):
            delta_s[block] = jnp.sum(
                grad_ref[slot_of(block, count)].astype(F32) * full_ref[block], 0, keepdims=True
            )
        query_grad_s[...] = jnp.zeros_like(query_grad_s)

    key_grad_s[...] = jnp.zeros_like(key_grad_s)
    value_grad_s[...] = jnp.zeros_like(value_grad_s)
    key = key_s[here]
    key_rows = key.T
    value_rows = value_s[here]

    def add_block(block, masked):
        query = query_s[block]
        grad = grad_ref[slot_of(block, count)]
        scores = contract(key_rows, query, 1, 0)
        if masked:
            scores = jnp.where(visible(first, second, block, here, size), scores, NEG)
        probs = jnp.exp2(scores - log_ref[block])
        grad_probs = contract(value_rows, grad, 1, 0)
        grad_scores = (probs * (grad_probs - delta_s[block])).astype(LOW)
        value_grad_s[...] += contract(grad, probs.astype(LOW), 1, 1)
        key_grad_s[...] += contract(query, grad_scores, 1, 1)
        query_grad_s[block] += contract(key, grad_scores, 1, 0)

    last = count - 1

    @pl.loop(here + 1, jnp.where(here == 0, 1, last))
    def _(block):
        add_block(block, False)

    @pl.loop(0, jnp.where(here == 0, count, jnp.where(here == last, 1, 2)))
    def _(step):
        add_block(jnp.where(here == 0, step, jnp.where(step == 0, here, last)), True)

    side = here // per_half
    columns = pl.ds(pl.multiple_of((here % per_half) * size, size), size)

    def write(out_ref):
        out_ref[0:HD, columns] = (query_grad_s[here] * HD**-0.5).astype(LOW)
        out_ref[HD : 2 * HD, columns] = (key_grad_s[...] * LN2).astype(LOW)
        out_ref[2 * HD : 3 * HD, columns] = value_grad_s[...].astype(LOW)

    @pl.when(side == half)
    def _():
        write(kept_ref)

    @pl.when(side != half)
    def _():
        write(leaving_ref)


def attend_forward(scalars, own, other, size):
    count = 2 * own.shape[1] // size
    whole = lambda shape: pl.BlockSpec(shape, lambda i, s: (0,) * len(shape))
    pairs = count * (count + 1) // 2
    return pl.pallas_call(
        functools.partial(forward_kernel, size=size, count=count),
        grid_spec=pltpu.PrefetchScalarGridSpec(
            num_scalar_prefetch=1,
            grid=(count,),
            in_specs=[whole(own.shape), whole(other.shape)],
            out_specs=[
                pl.BlockSpec(
                    (1, HD, size), lambda i, s: (slot_of(i, count), 0, 0)
                ),
                pl.BlockSpec((1, HD, size), lambda i, s: (i, 0, 0)),
                pl.BlockSpec((1, 1, size), lambda i, s: (i, 0, 0)),
            ],
            scratch_shapes=[
                pltpu.VMEM((count, HD, size), LOW),
                pltpu.VMEM((count, size, HD), LOW),
                pltpu.VMEM((count, HD, size), LOW),
                pltpu.VMEM((1, size), F32),
                pltpu.VMEM((1, size), F32),
                pltpu.VMEM((HD, size), F32),
            ],
        ),
        out_shape=[
            jax.ShapeDtypeStruct((count, HD, size), LOW),
            jax.ShapeDtypeStruct((count, HD, size), F32),
            jax.ShapeDtypeStruct((count, 1, size), F32),
        ],
        compiler_params=pltpu.CompilerParams(
            dimension_semantics=("arbitrary",), vmem_limit_bytes=32 * 2**20
        ),
        cost_estimate=pl.CostEstimate(
            flops=pairs * size * size * HD * 32,
            bytes_accessed=10 * 2**20,
            transcendentals=pairs * size * size,
        ),
        name="attend_forward",
    )(scalars, own, other)


def attend_backward(scalars, own, other, grad, full, log_total):
    count, _, size = grad.shape
    whole = lambda shape: pl.BlockSpec(shape, lambda i, s: (0,) * len(shape))
    pairs = count * (count + 1) // 2
    out_shape = own.shape
    return pl.pallas_call(
        functools.partial(backward_kernel, size=size, count=count),
        grid_spec=pltpu.PrefetchScalarGridSpec(
            num_scalar_prefetch=1,
            grid=(count,),
            in_specs=[
                whole(own.shape),
                whole(other.shape),
                whole(grad.shape),
                whole(full.shape),
                whole(log_total.shape),
            ],
            out_specs=[whole(out_shape)] * 2,
            scratch_shapes=[
                pltpu.VMEM((count, HD, size), LOW),
                pltpu.VMEM((count, HD, size), LOW),
                pltpu.VMEM((count, size, HD), LOW),
                pltpu.VMEM((count, 1, size), F32),
                pltpu.VMEM((count, HD, size), F32),
                pltpu.VMEM((HD, size), F32),
                pltpu.VMEM((HD, size), F32),
            ],
        ),
        out_shape=[jax.ShapeDtypeStruct(out_shape, LOW)] * 2,
        compiler_params=pltpu.CompilerParams(
            dimension_semantics=("arbitrary",), vmem_limit_bytes=32 * 2**20
        ),
        cost_estimate=pl.CostEstimate(
            flops=pairs * size * size * HD * 42,
            bytes_accessed=16 * 2**20,
            transcendentals=pairs * size * size,
        ),
        name="attend_backward",
    )(scalars, own, other, grad, full, log_total)


def place_rows_kernel(order, *refs):
    pieces, out_ref = refs[:-1], refs[-1]
    size = pieces[0].shape[0]
    for index, piece in enumerate(pieces):
        start = pl.multiple_of(order[index] * size, size)
        out_ref[pl.ds(start, size), :] = piece[...].astype(F32)


def place_rows(order, pieces):
    size, width = pieces[0].shape
    total = size * len(pieces)
    step = 512
    return pl.pallas_call(
        place_rows_kernel,
        grid_spec=pltpu.PrefetchScalarGridSpec(
            num_scalar_prefetch=1,
            grid=(width // step,),
            in_specs=[pl.BlockSpec((size, step), lambda i, s: (0, i)) for _ in pieces],
            out_specs=pl.BlockSpec((total, step), lambda i, s: (0, i)),
        ),
        out_shape=jax.ShapeDtypeStruct((total, width), F32),
        compiler_params=pltpu.CompilerParams(vmem_limit_bytes=24 * 2**20),
        cost_estimate=pl.CostEstimate(
            flops=0, bytes_accessed=total * width * 6, transcendentals=0
        ),
        name="place_rows",
    )(order, *pieces)


def place_columns_kernel(order, gain_ref, gate_w_ref, up_w_ref, *refs):
    count = (len(refs) - 3) // 2
    gates, ups = refs[:count], refs[count : 2 * count]
    gate_ref, up_ref, sum_ref = refs[2 * count :]
    size = gates[0].shape[1]
    gain = gain_ref[...]
    total = jnp.zeros((gate_ref.shape[0], size), F32)
    for index in range(count):
        columns = pl.ds(pl.multiple_of(order[index] * size, size), size)
        gate, up = gates[index][...].astype(F32), ups[index][...].astype(F32)
        total += gate * gate_w_ref[:, columns].astype(F32)
        total += up * up_w_ref[:, columns].astype(F32)
        gate_ref[:, columns] = gate * gain
        up_ref[:, columns] = up * gain

    @pl.when(pl.program_id(0) == 0)
    def _():
        sum_ref[...] = jnp.zeros_like(sum_ref)

    sum_ref[...] += jnp.sum(total, 1, keepdims=True)


def place_columns(order, gain, gate_weight, up_weight, gates, ups, shards):
    rows, width = gate_weight.shape
    span = width // shards
    size = span // len(gates)
    wide = pl.BlockSpec((rows, span), lambda i, s: (0, i))
    thin = pl.BlockSpec((rows, 1), lambda i, s: (0, 0))
    pieces = [pl.BlockSpec((rows, size), lambda i, s: (0, i)) for _ in (*gates, *ups)]
    return pl.pallas_call(
        place_columns_kernel,
        grid_spec=pltpu.PrefetchScalarGridSpec(
            num_scalar_prefetch=1,
            grid=(shards,),
            in_specs=[thin, wide, wide, *pieces],
            out_specs=[wide, wide, thin],
        ),
        out_shape=[
            jax.ShapeDtypeStruct((rows, width), F32),
            jax.ShapeDtypeStruct((rows, width), F32),
            jax.ShapeDtypeStruct((rows, 1), F32),
        ],
        compiler_params=pltpu.CompilerParams(
            dimension_semantics=("arbitrary",), vmem_limit_bytes=24 * 2**20
        ),
        cost_estimate=pl.CostEstimate(
            flops=rows * width * 6, bytes_accessed=rows * width * 16, transcendentals=0
        ),
        name="place_columns",
    )(order, gain, gate_weight, up_weight, *gates, *ups)


def place_heads_kernel(gain_ref, query_w, key_w, value_w, all_ref, query_ref, key_ref, value_ref, sum_ref):
    rows = gain_ref.shape[0]
    wide = query_ref.shape[1] // KVH
    gain = gain_ref[...]
    total = jnp.zeros((rows, 4 * HD), F32)
    pieces = [all_ref[i * rows : (i + 1) * rows, :].astype(F32) for i in range(KVH)]
    for start in range(0, KVH, 2):
        value = jnp.concatenate([piece[:, :wide] for piece in pieces[start : start + 2]], 1)
        columns = slice(start * wide, (start + 2) * wide)
        total += value * query_w[:, columns].astype(F32)
        query_ref[:, columns] = value * gain
    for first, weight, out_ref in ((wide, key_w, key_ref), (wide + HD, value_w, value_ref)):
        for start in range(0, KVH, 4):
            value = jnp.concatenate(
                [piece[:, first : first + HD] for piece in pieces[start : start + 4]], 1
            )
            columns = slice(start * HD, (start + 4) * HD)
            total += value * weight[:, columns].astype(F32)
            out_ref[:, columns] = value * gain
    sum_ref[...] = jnp.sum(total, 1, keepdims=True)


def place_heads(gain, query_weight, key_weight, value_weight, pieces):
    weights = (query_weight, key_weight, value_weight)
    rows = gain.shape[0]
    return pl.pallas_call(
        place_heads_kernel,
        out_shape=[jax.ShapeDtypeStruct(weight.shape, F32) for weight in weights]
        + [jax.ShapeDtypeStruct((rows, 1), F32)],
        compiler_params=pltpu.CompilerParams(vmem_limit_bytes=32 * 2**20),
        cost_estimate=pl.CostEstimate(
            flops=rows * 3072 * 4, bytes_accessed=rows * 3072 * 8, transcendentals=0
        ),
        name="place_heads",
    )(gain, *weights, pieces)


def merge_kernel(scalars, kept_ref, came_ref, cosine_ref, sine_ref, out_ref, split_ref):
    lead = scalars[0] == 0
    lines, _, size = split_ref.shape
    for line in range(lines):
        columns = slice(line * size, (line + 1) * size)
        kept = kept_ref[:, columns].astype(F32)
        came = came_ref[:, columns].astype(F32)
        cosine, sine = cosine_ref[:, columns], sine_ref[:, columns]
        joint = kept[HD:] + came[HD:]
        first = jnp.where(lead, kept[:HD], came[:HD])
        second = jnp.where(lead, came[:HD], kept[:HD])
        turned = []
        for value in (first, second, joint[:HD]):
            low, high = value[: HD // 2], value[HD // 2 :]
            turned.append(low * cosine + high * sine)
            turned.append(high * cosine - low * sine)
        turned.append(joint[HD:])
        result = jnp.concatenate([part.astype(LOW) for part in turned], 0)
        out_ref[:, columns] = result
        split_ref[line] = result


def merge(scalars, kept, came, cosine, sine, lines):
    tokens = kept.shape[1]
    whole = lambda value: pl.BlockSpec(value.shape, lambda i, s: (0,) * len(value.shape))
    outs = [
        jax.ShapeDtypeStruct((4 * HD, tokens), LOW),
        jax.ShapeDtypeStruct((lines, 4 * HD, tokens // lines), LOW),
    ]
    return pl.pallas_call(
        merge_kernel,
        grid_spec=pltpu.PrefetchScalarGridSpec(
            num_scalar_prefetch=1,
            grid=(1,),
            in_specs=[whole(value) for value in (kept, came, cosine, sine)],
            out_specs=[whole(value) for value in outs],
        ),
        out_shape=outs,
        compiler_params=pltpu.CompilerParams(vmem_limit_bytes=24 * 2**20),
        cost_estimate=pl.CostEstimate(
            flops=tokens * HD * 24, bytes_accessed=tokens * HD * 30, transcendentals=0
        ),
        name="merge",
    )(scalars, kept, came, cosine, sine)


def pack_kernel(scalars, gain_ref, query_ref, key_ref, value_ref, *outs):
    core = scalars[3]
    gain = gain_ref[...]
    wide = query_ref.shape[1] // KVH
    span = wide + 2 * HD
    for which in range(2):

        @pl.when(core == which)
        def _():
            for line in range(KVH // 2):
                head = 2 * line + which
                value = jnp.concatenate(
                    [
                        query_ref[:, head * wide : (head + 1) * wide].astype(F32),
                        key_ref[:, head * HD : (head + 1) * HD].astype(F32),
                        value_ref[:, head * HD : (head + 1) * HD].astype(F32),
                    ],
                    1,
                )
                place = (line % 2) * span
                outs[line // 2][:, place : place + span] = (value * gain).astype(LOW)


def pack(scalars, gain, query_weight, key_weight, value_weight):
    rows, width = query_weight.shape
    whole = lambda value: pl.BlockSpec(value.shape, lambda i, s: (0, 0))
    weights = (gain, query_weight, key_weight, value_weight)
    outs = [jax.ShapeDtypeStruct((rows, width // 2), LOW)] * 2
    return pl.pallas_call(
        pack_kernel,
        grid_spec=pltpu.PrefetchScalarGridSpec(
            num_scalar_prefetch=1,
            grid=(1,),
            in_specs=[whole(value) for value in weights],
            out_specs=[whole(value) for value in outs],
        ),
        out_shape=outs,
        compiler_params=pltpu.CompilerParams(vmem_limit_bytes=24 * 2**20),
        cost_estimate=pl.CostEstimate(
            flops=rows * width, bytes_accessed=rows * width * 6, transcendentals=0
        ),
        name="pack",
    )(scalars, *weights)


def spread_kernel(scalars, lin_ref, cosine_ref, sine_ref, own_ref, leaving_ref):
    cosine, sine = cosine_ref[...], sine_ref[...]

    def turn(start, factor):
        low = lin_ref[start : start + HD // 2, :]
        high = lin_ref[start + HD // 2 : start + HD, :]
        turned = ((low * cosine - high * sine) * factor, (high * cosine + low * sine) * factor)
        return jnp.concatenate([part.astype(LOW) for part in turned], 0)

    lead = scalars[0] == 0
    first, second = turn(0, HD**-0.5 / LN2), turn(HD, HD**-0.5 / LN2)

    @pl.when(lead)
    def _():
        own_ref[0:HD] = first
        leaving_ref[0:HD] = second

    @pl.when(jnp.logical_not(lead))
    def _():
        own_ref[0:HD] = second
        leaving_ref[0:HD] = first

    key = turn(2 * HD, 1.0)
    value = lin_ref[3 * HD : 4 * HD].astype(LOW)
    for ref in (own_ref, leaving_ref):
        ref[HD : 2 * HD] = key
        ref[2 * HD : 3 * HD] = value


def spread(scalars, lin, cosine, sine):
    tokens = lin.shape[1]
    step = 512
    column = lambda rows: pl.BlockSpec((rows, step), lambda i, s: (0, i))
    return pl.pallas_call(
        spread_kernel,
        grid_spec=pltpu.PrefetchScalarGridSpec(
            num_scalar_prefetch=1,
            grid=(tokens // step,),
            in_specs=[column(4 * HD), column(HD // 2), column(HD // 2)],
            out_specs=[column(3 * HD)] * 2,
        ),
        out_shape=[jax.ShapeDtypeStruct((3 * HD, tokens), LOW)] * 2,
        compiler_params=pltpu.CompilerParams(vmem_limit_bytes=24 * 2**20),
        cost_estimate=pl.CostEstimate(
            flops=tokens * HD * 24, bytes_accessed=tokens * HD * 36, transcendentals=0
        ),
        name="spread",
    )(scalars, lin, cosine, sine)


def swap(value, axis):
    return lax.ppermute(value, axis, [(0, 1), (1, 0)])


def swap_near(value):
    return lax.ppermute(value, "z", [(0, 1), (1, 0), (2, 3), (3, 2)])


def swap_far(value):
    return lax.ppermute(value, "z", [(0, 2), (2, 0), (1, 3), (3, 1)])


def tie(*values):
    return lax.optimization_barrier(values)


def in_order(place, own, other):
    return (jnp.where(place == 0, own, other), jnp.where(place == 0, other, own))


def both(place, own, other):
    return jnp.concatenate(in_order(place, own, other), 0)


def spread_out(value, first, second):
    other = swap(value, first)
    pair = jnp.stack(in_order(lax.axis_index(first), value, other))
    return pair, swap(pair, second)


def placed(pair, other, second):
    pairs = in_order(lax.axis_index(second), pair, other)
    grid = jnp.stack(pairs, 0 if second == "y" else 1)
    return grid.reshape(-1, *grid.shape[3:])


def pick(array, axis, at):
    return lax.dynamic_index_in_dim(array, at, axis, keepdims=False)


def halve(value, axis, along=0):
    at = lax.axis_index(axis)
    return pick(value, along, at), swap(pick(value, along, 1 - at), axis)


def halve_x(value):
    return halve(value.reshape(2, 2, -1, value.shape[-1]), "x", 1)


def halve_y(value):
    return halve(value.reshape(2, 2, -1, value.shape[-1]), "y", 0)


def fast_body(
    tokens,
    positions,
    first_gain,
    query_weight,
    key_weight,
    value_weight,
    output_weight,
    second_gain,
    gate_weight,
    up_weight,
    down_weight,
    cotangent,
):
    seq = ("z", "c")
    fsdp = ("y", "x")
    z, core, half = lax.axis_index("z"), lax.axis_index("c"), lax.axis_index("x")
    near = z % 2
    lines = lax.axis_size("z")
    seq_count = 2 * lines
    shards = lax.axis_size("y") * 2
    spot = z * 2 + core
    quarter = near * 2 + core
    rows = tokens[0]
    count, width = rows.shape
    chip_count = 2 * count
    half_len = count * seq_count
    seq_len = 2 * half_len

    begins = jnp.where(
        (spot == 0) & (half == 0),
        count - 1 - positions[0, count - 1],
        half * half_len + spot * count - positions[0, 0],
    )
    ends = begins + (seq_len - count)
    scalars = jnp.stack([half, begins, ends, core]).astype(jnp.int32)

    gain_one = first_gain.astype(F32)[:, None]
    gain_two = second_gain.astype(F32)[:, None]

    def row_scale(value):
        return lax.rsqrt(jnp.mean(value * value, -1, keepdims=True) + EPS)

    take = functools.partial(lax.dynamic_slice_in_dim, axis=1)
    take_rows = functools.partial(lax.dynamic_slice_in_dim, axis=0)
    gather = lambda value, axes: lax.all_gather(value, axes, axis=0, tiled=True)
    own_rows = rows.astype(F32)
    own_unit_scale = row_scale(own_rows)
    own_unit = own_rows * own_unit_scale
    units = gather(own_unit.astype(LOW), seq)
    wide = QH // KVH * HD
    qkv_shard = (
        jnp.concatenate(
            [
                take(query_weight, spot * wide, wide),
                take(key_weight, spot * HD, HD),
                take(value_weight, spot * HD, HD),
            ],
            1,
        ).astype(F32)
        * gain_one
    ).astype(LOW)
    out_rows = output_weight.shape[0] // 2
    out_shard = take_rows(output_weight, core * out_rows, out_rows)
    piece = down_weight.shape[0] // 4
    down_shard = take_rows(down_weight, quarter * piece, piece)
    gate_shard, up_shard = (
        (
            jnp.concatenate(
                [
                    take(weight, shard * 4 * piece + quarter * piece, piece)
                    for shard in range(shards)
                ],
                1,
            ).astype(F32)
            * gain_two
        ).astype(LOW)
        for weight in (gate_weight, up_weight)
    )
    side = lax.axis_index("y")
    qkv_pair = jnp.stack(in_order(half, qkv_shard, swap(qkv_shard, "x")))
    gate_pair = jnp.stack(in_order(half, gate_shard, swap(gate_shard, "x")))
    up_pair = jnp.stack(in_order(side, up_shard, swap(up_shard, "y")))
    qkv_pair, gate_pair, up_pair = tie(qkv_pair, gate_pair, up_pair)
    qkv_w = placed(qkv_pair, swap(qkv_pair, "y"), "y")
    gate_pair, up_pair = (gate_pair, swap(gate_pair, "y")), (up_pair, swap(up_pair, "x"))

    place = half * half_len + jnp.arange(half_len, dtype=jnp.int32)
    start = jnp.where(place >= ends, ends, jnp.where(place >= begins, begins, 0))
    freq = THETA ** (-(jnp.arange(HD // 2, dtype=F32) * 2.0 / HD))
    angle = freq[:, None] * (place - start).astype(F32)[None, :]
    cosine, sine = jnp.cos(angle), jnp.sin(angle)
    chip_rows = both(core, rows, swap(rows, "c"))
    units, own_cot, chip_rows = tie(units, cotangent[0], chip_rows)
    own, leaving = spread(scalars, contract(qkv_w, units, 0, 1), cosine, sine)

    near_cot = swap_near(own_cot)
    other, out_shard, down_shard, near_cot, chip_cot, gate_pair, up_pair = tie(
        swap(leaving, "x"),
        out_shard,
        down_shard,
        near_cot,
        both(core, own_cot, swap(own_cot, "c")),
        gate_pair,
        up_pair,
    )
    out_w = gather(out_shard, fsdp)
    down_w = gather(down_shard, fsdp)
    near_other = swap(near_cot, "c")
    head_low, head_full, log_total = attend_forward(scalars, own, other, chip_count)
    exchange = lambda value: lax.all_to_all(
        value, ("z", "x"), split_axis=0, concat_axis=0, tiled=True
    )
    head_low, near_other = tie(head_low, near_other)
    lead_shard, tail_shard = pack(scalars, gain_one, query_weight, key_weight, value_weight)
    heads, gate_w, up_w, near_cot, lead_shard = tie(
        exchange(head_low),
        placed(*gate_pair, "y"),
        placed(*up_pair, "x"),
        jnp.concatenate([near_cot, near_other], 0),
        lead_shard,
    )
    lead_w = gather(lead_shard, fsdp)
    heads = heads.reshape(QH // 2 * HD, chip_count)

    mine_of = lambda value: take_rows(value, core * count, count)
    theirs_of = lambda value: take_rows(value, (1 - core) * count, count)
    branch = contract(heads, out_w, 0, 0).astype(LOW)
    middle = chip_rows.astype(F32) + (branch.astype(F32) + swap(branch, "c").astype(F32))
    middle_scale = row_scale(middle)
    chip_unit = middle * middle_scale
    own_middle, own_scale, own_middle_unit = (
        mine_of(middle),
        mine_of(middle_scale),
        mine_of(chip_unit),
    )
    chip_unit = chip_unit.astype(LOW)
    near_unit = swap_near(mine_of(chip_unit))

    def feed(unit):
        gate, upper = contract(unit, gate_w, 1, 0), contract(unit, up_w, 1, 0)
        sigma = jax.nn.sigmoid(gate)
        silu = gate * sigma
        return (silu * upper).astype(LOW), (gate, upper, sigma, silu)

    def feed_back(cot, kept):
        gate, upper, sigma, silu = kept
        grad_hidden = contract(cot, down_w, 1, 1)
        gate_low = (grad_hidden * upper * sigma * (1.0 + gate * (1.0 - sigma))).astype(LOW)
        upper_low = (grad_hidden * silu).astype(LOW)
        part = contract(gate_low, gate_w, 1, 1) + contract(upper_low, up_w, 1, 1)
        return gate_low, upper_low, part

    def chip_sum(chip_part, near_part):
        near_sum = near_part[:count].astype(F32) + swap(near_part[count:].astype(LOW), "c")
        own_sum = mine_of(chip_part).astype(F32) + swap(theirs_of(chip_part).astype(LOW), "c")
        return own_sum, near_sum.astype(LOW)

    stack = lambda first, second: jnp.concatenate([first, second], 0)
    scatter = lambda value: lax.psum_scatter(value, fsdp, scatter_dimension=0, tiled=True)
    chip_hidden, chip_kept = feed(chip_unit)
    near_unit, chip_hidden = tie(near_unit, chip_hidden)
    near_unit = jnp.concatenate([near_unit, swap(near_unit, "c")], 0)
    near_hidden, near_kept = feed(near_unit)
    down_part = contract(
        stack(chip_hidden, near_hidden), stack(chip_cot, near_cot), 0, 0
    ).astype(LOW)
    near_cot, down_part = tie(near_cot, down_part)
    near_gate, near_upper, near_part = feed_back(near_cot, near_kept)
    chip_gate, chip_upper, chip_part = feed_back(chip_cot, chip_kept)
    grad_two, near_sum = chip_sum(chip_part, near_part)

    def halves_first(value):
        cut = value.shape[-1] // 2
        return halve_x(value[:, :cut]), halve_y(value[:, cut:])

    def halves_second(firsts):
        return halve(sum(firsts[0]), "y"), halve(sum(firsts[1]), "x")

    def halves_end(seconds):
        return jnp.concatenate([sum(seconds[0]), sum(seconds[1])], 1)

    down_first = halves_first(down_part)
    near_sum, near_gate, near_upper, chip_part = tie(
        near_sum, near_gate, near_upper, chip_part
    )
    grad_came = swap_near(near_sum)
    all_units = stack(chip_unit, near_unit)
    gate_part = contract(all_units, stack(chip_gate, near_gate), 0, 0).astype(LOW)
    up_part = contract(all_units, stack(chip_upper, near_upper), 0, 0).astype(LOW)
    feed_own, feed_near = chip_sum(
        contract(chip_hidden, down_w, 1, 0), contract(near_hidden, down_w, 1, 0)
    )
    gate_part, up_part, down_first, grad_came, feed_near = tie(
        gate_part, up_part, down_first, grad_came, feed_near
    )
    feed_near = swap_near(feed_near)
    down_second = halves_second(down_first)
    grad_two = grad_two + grad_came.astype(F32)
    grad_middle = own_cot.astype(F32) + own_scale * (
        grad_two - own_middle_unit * jnp.mean(grad_two * own_middle_unit, -1, keepdims=True)
    )
    own_branch, lead_w, down_second, gate_part, up_part = tie(
        grad_middle.astype(LOW), lead_w, down_second, gate_part, up_part
    )
    gate_grad, up_grad = scatter(gate_part), scatter(up_part)
    down_grad = halves_end(down_second)
    down_far = swap_far(down_grad)
    grad_branch = both(core, own_branch, swap(own_branch, "c"))
    grad_heads = contract(out_w, grad_branch, 1, 1).astype(LOW)
    grad_heads, grad_branch, feed_near = tie(grad_heads, grad_branch, feed_near)
    output_part = contract(heads, grad_branch, 1, 0).astype(LOW)
    output_grad = scatter(output_part)
    grad_head, output_part, gate_grad, down_far = tie(
        exchange(grad_heads.reshape(2 * lines, HD, chip_count)),
        output_part,
        gate_grad,
        down_far,
    )
    down_sum = down_grad + down_far
    down_near = swap_near(down_sum)

    gate_far = swap_far(gate_grad)
    kept, leaving = attend_backward(scalars, own, other, grad_head, head_full, log_total)
    kept, leaving, gate_far, down_near, tail_shard = tie(
        kept, leaving, gate_far, down_near, tail_shard
    )
    tail_w = gather(tail_shard, fsdp)

    up_far = swap_far(up_grad)
    gate_sum = gate_grad + gate_far
    gate_near = swap_near(gate_sum)
    block_output = (own_middle + feed_own + feed_near.astype(F32)).astype(LOW)[None]
    came, up_far, gate_near, block_output, output_grad = tie(
        swap(leaving, "x"), up_far, gate_near, block_output, output_grad
    )

    qkv_low, by_line = merge(scalars, kept, came, cosine, sine, lines)
    token_grads = lax.all_to_all(by_line, "z", split_axis=0, concat_axis=0, tiled=True)
    qkv_part = contract(units, qkv_low, 0, 1).astype(LOW).reshape(shards, 2, -1, 4 * HD)
    qkv_first = halve_x(qkv_part[:, 0]), halve_y(qkv_part[:, 1])
    output_came = swap_near(output_grad)
    qkv_first, output_came = tie(qkv_first, output_came)
    output_sum = output_grad + output_came
    output_far = swap_far(output_sum)
    qkv_second = halves_second(qkv_first)
    qkv_grad = jnp.concatenate([sum(qkv_second[0]), sum(qkv_second[1])], 0)
    all_qkv = gather(qkv_grad, seq)
    up_sum = up_grad + up_far
    up_near = swap_near(up_sum)
    token_grads, qkv_second, up_near = tie(token_grads, qkv_second, up_near)

    token_grads = token_grads.reshape(-1, chip_count)
    split = lead_w.shape[1]
    grad_one = contract(token_grads[:split], lead_w, 0, 1) + contract(
        token_grads[split:], tail_w, 0, 1
    )
    grad_one = mine_of(grad_one) + swap(theirs_of(grad_one).astype(LOW), "c").astype(F32)
    grad_rows = own_unit_scale * (
        grad_one - own_unit * jnp.mean(grad_one * own_unit, -1, keepdims=True)
    )
    input_grad = (grad_middle + grad_rows).astype(LOW)[None]

    def four(value, near_value):
        return value, swap(value, "c"), near_value, swap(near_value, "c")

    order = jnp.stack([quarter, quarter ^ 1, quarter ^ 2, quarter ^ 3]).astype(jnp.int32)
    core_order = jnp.stack([core, 1 - core]).astype(jnp.int32)
    down_total = place_rows(order, four(down_sum, down_near))
    gate_total, up_total, second_gain_grad = place_columns(
        order, gain_two, gate_weight, up_weight, four(gate_sum, gate_near), four(up_sum, up_near), shards
    )
    output_far, second_gain_grad, all_qkv = tie(output_far, second_gain_grad, all_qkv)
    output_own = output_sum + output_far
    output_total = place_rows(core_order, (output_own, swap(output_own, "c")))
    query_grad, key_grad, value_grad, first_gain_grad = place_heads(
        gain_one, query_weight, key_weight, value_weight, all_qkv
    )
    return (
        block_output,
        input_grad,
        first_gain_grad[:, 0],
        query_grad,
        key_grad,
        value_grad,
        output_total,
        second_gain_grad[:, 0],
        gate_total,
        up_total,
        down_total,
    )


def fast_solution(mesh):
    seq_count, shard_count = mesh.devices.shape
    fine = Mesh(
        mesh.devices.reshape(seq_count // 2, 2, shard_count // 2, 2), ("z", "c", "y", "x")
    )
    seq, fsdp = ("z", "c"), ("y", "x")
    matrix = P(fsdp, None)
    return jax.shard_map(
        fast_body,
        mesh=fine,
        in_specs=(
            P(fsdp, seq, None),
            P(fsdp, seq),
            P(fsdp),
            matrix,
            matrix,
            matrix,
            matrix,
            P(fsdp),
            matrix,
            matrix,
            matrix,
            P(fsdp, seq, None),
        ),
        out_specs=(
            P(fsdp, seq, None),
            P(fsdp, seq, None),
            P(fsdp),
            matrix,
            matrix,
            matrix,
            matrix,
            P(fsdp),
            matrix,
            matrix,
            matrix,
        ),
        check_vma=False,
    )


def solution(mesh):
    shape = dict(mesh.shape)
    if shape["seq"] == KVH and shape["fsdp"] == 4:
        return fast_solution(mesh)
    return plain_solution(mesh)


def shifted(value, axis, steps):
    count = lax.axis_size(axis)
    first, last = (max(0, -steps), min(count, count - steps))
    return lax.ppermute(value, axis, [(source, source + steps) for source in range(first, last)])


def rope_tables(position_rows):
    freq = THETA ** (-(jnp.arange(HD // 2, dtype=jnp.float32) * 2.0 / HD))
    angle = position_rows.astype(jnp.float32)[:, None] * freq[None, :]
    cosine = jnp.cos(angle)
    sine = jnp.sin(angle)
    return (jnp.concatenate([cosine, cosine], -1), jnp.concatenate([sine, sine], -1))


def rotate(values, cosine, sine):
    half = HD // 2
    turned = jnp.concatenate([-values[..., half:], values[..., :half]], -1)
    return values * cosine[:, None, :] + turned * sine[:, None, :]


def rotate_back(grads, cosine, sine):
    half = HD // 2
    scaled = grads * sine[:, None, :]
    turned = jnp.concatenate([scaled[..., half:], -scaled[..., :half]], -1)
    return grads * cosine[:, None, :] + turned


def norm_forward(rows, gain):
    scale = lax.rsqrt(jnp.mean(rows * rows, -1, keepdims=True) + EPS)
    unit = rows * scale
    return (unit * gain, unit, scale)


def norm_backward(grad_out, unit, scale, gain):
    grad_unit = grad_out * gain
    gain_grad = jnp.sum(grad_out * unit, 0)
    grad_rows = scale * (grad_unit - unit * jnp.mean(grad_unit * unit, -1, keepdims=True))
    return (grad_rows, gain_grad)


def plain_body(
    tokens,
    positions,
    first_gain,
    query_weight,
    key_weight,
    value_weight,
    output_weight,
    second_gain,
    gate_weight,
    up_weight,
    down_weight,
    cotangent,
):
    seq_count = lax.axis_size("seq")
    local_rows = tokens[0]
    token_count = local_rows.shape[0]
    half_len = token_count * seq_count
    rows_float = local_rows.astype(jnp.float32)
    gain_one, wq_full, wk_full, wv_full, wo_full = (
        lax.all_gather(first_gain, "fsdp", axis=0, tiled=True),
        lax.all_gather(query_weight, "fsdp", axis=0, tiled=True),
        lax.all_gather(key_weight, "fsdp", axis=0, tiled=True),
        lax.all_gather(value_weight, "fsdp", axis=0, tiled=True),
        lax.all_gather(output_weight, "fsdp", axis=0, tiled=True),
    )
    gain_one = gain_one.astype(jnp.float32)
    normed_one, unit_one, scale_one = norm_forward(rows_float, gain_one)
    normed_low = normed_one.astype(jnp.bfloat16)
    cosine, sine = rope_tables(positions[0])
    query_lin = jnp.dot(normed_low, wq_full, preferred_element_type=jnp.float32).reshape(
        token_count, QH, HD
    )
    key_lin = jnp.dot(normed_low, wk_full, preferred_element_type=jnp.float32).reshape(
        token_count, KVH, HD
    )
    value_lin = jnp.dot(normed_low, wv_full, preferred_element_type=jnp.float32).reshape(
        token_count, KVH, HD
    )
    query_rows = rotate(query_lin, cosine, sine).astype(jnp.bfloat16)
    key_rows = rotate(key_lin, cosine, sine).astype(jnp.bfloat16)
    value_rows = value_lin.astype(jnp.bfloat16)
    repeat = max(1, seq_count // KVH)
    if repeat > 1:
        key_rows = jnp.repeat(key_rows, repeat, axis=1)
        value_rows = jnp.repeat(value_rows, repeat, axis=1)
    query_heads, key_heads, value_heads = (
        lax.all_to_all(query_rows, "seq", split_axis=1, concat_axis=0, tiled=True),
        lax.all_to_all(key_rows, "seq", split_axis=1, concat_axis=0, tiled=True),
        lax.all_to_all(value_rows, "seq", split_axis=1, concat_axis=0, tiled=True),
    )
    head_count = query_heads.shape[1]
    pair_count = key_heads.shape[1]
    group = head_count // pair_count
    half_positions = lax.all_gather(positions[0], "seq", axis=0, tiled=True)
    key_prior, value_prior = shifted((key_heads, value_heads), "fsdp", 1)
    key_all = jnp.concatenate([key_prior, key_heads], 0)
    value_all = jnp.concatenate([value_prior, value_heads], 0)
    half_index = lax.axis_index("fsdp") % 2
    key_index = (half_index - 1) * half_len + jnp.arange(2 * half_len, dtype=jnp.int32)
    row_index = half_index * half_len + jnp.arange(half_len, dtype=jnp.int32)
    row_start = row_index - half_positions
    block = min(512, half_len)
    count = half_len // block
    factor = HD ** (-0.5)
    query_blocks = query_heads.reshape(count, block, pair_count, group, HD)
    index_blocks = row_index.reshape(count, block)
    start_blocks = row_start.reshape(count, block)

    def block_scores(query_block, index_block, start_block):
        scores = (
            jnp.einsum("bkgd,tkd->kgbt", query_block, key_all, preferred_element_type=jnp.float32)
            * factor
        )
        visible = (key_index[None, :] >= start_block[:, None]) & (
            key_index[None, :] <= index_block[:, None]
        )
        return jnp.where(visible, scores, -1e30)

    def forward_block(items):
        query_block, index_block, start_block = items
        scores = block_scores(query_block, index_block, start_block)
        top = jnp.max(scores, -1, keepdims=True)
        expo = jnp.exp(scores - top)
        total = jnp.sum(expo, -1, keepdims=True)
        probs_low = (expo / total).astype(jnp.bfloat16)
        mixed = jnp.einsum(
            "kgbt,tkd->bkgd", probs_low, value_all, preferred_element_type=jnp.float32
        )
        return (mixed.reshape(block, head_count, HD).astype(jnp.bfloat16), top + jnp.log(total))

    head_blocks, log_totals = lax.map(forward_block, (query_blocks, index_blocks, start_blocks))
    head_out = head_blocks.reshape(half_len, head_count, HD)
    token_heads = lax.all_to_all(head_out, "seq", split_axis=0, concat_axis=1, tiled=True)
    heads_flat = token_heads.reshape(token_count, QH * HD)
    middle = rows_float + jnp.dot(heads_flat, wo_full, preferred_element_type=jnp.float32)
    gain_two, wg_full, wu_full, wd_full = (
        lax.all_gather(second_gain, "fsdp", axis=0, tiled=True),
        lax.all_gather(gate_weight, "fsdp", axis=0, tiled=True),
        lax.all_gather(up_weight, "fsdp", axis=0, tiled=True),
        lax.all_gather(down_weight, "fsdp", axis=0, tiled=True),
    )
    gain_two = gain_two.astype(jnp.float32)
    normed_two, unit_two, scale_two = norm_forward(middle, gain_two)
    normed_two_low = normed_two.astype(jnp.bfloat16)
    gate = jnp.dot(normed_two_low, wg_full, preferred_element_type=jnp.float32)
    upper = jnp.dot(normed_two_low, wu_full, preferred_element_type=jnp.float32)
    hidden = (jax.nn.silu(gate) * upper).astype(jnp.bfloat16)
    result = middle + jnp.dot(hidden, wd_full, preferred_element_type=jnp.float32)
    block_output = result.astype(jnp.bfloat16)[None]
    grad_low = cotangent[0]
    grad_rows = grad_low.astype(jnp.float32)
    down_grad = jnp.einsum("tf,td->fd", hidden, grad_low, preferred_element_type=jnp.float32)
    grad_hidden = jnp.einsum("td,fd->tf", grad_low, wd_full, preferred_element_type=jnp.float32)
    sigma = jax.nn.sigmoid(gate)
    gate_low = (grad_hidden * upper * sigma * (1.0 + gate * (1.0 - sigma))).astype(jnp.bfloat16)
    upper_low = (grad_hidden * gate * sigma).astype(jnp.bfloat16)
    gate_grad = jnp.einsum(
        "td,tf->df", normed_two_low, gate_low, preferred_element_type=jnp.float32
    )
    up_grad = jnp.einsum("td,tf->df", normed_two_low, upper_low, preferred_element_type=jnp.float32)
    grad_normed_two = jnp.einsum(
        "tf,df->td", gate_low, wg_full, preferred_element_type=jnp.float32
    ) + jnp.einsum("tf,df->td", upper_low, wu_full, preferred_element_type=jnp.float32)
    grad_middle_norm, second_gain_grad = norm_backward(
        grad_normed_two, unit_two, scale_two, gain_two
    )
    grad_middle = grad_rows + grad_middle_norm
    grad_branch = grad_middle.astype(jnp.bfloat16)
    output_grad = jnp.einsum(
        "tc,td->cd", heads_flat, grad_branch, preferred_element_type=jnp.float32
    )
    grad_heads = (
        jnp.einsum("td,cd->tc", grad_branch, wo_full, preferred_element_type=jnp.float32)
        .astype(jnp.bfloat16)
        .reshape(token_count, QH, HD)
    )
    grad_head_rows = lax.all_to_all(grad_heads, "seq", split_axis=1, concat_axis=0, tiled=True)
    grad_blocks = grad_head_rows.reshape(count, block, pair_count, group, HD)

    def backward_block(carry, items):
        key_acc, value_acc = carry
        query_block, index_block, start_block, grad_block, log_block = items
        scores = block_scores(query_block, index_block, start_block)
        probs = jnp.exp(scores - log_block)
        probs_low = probs.astype(jnp.bfloat16)
        grad_probs = jnp.einsum(
            "bkgd,tkd->kgbt", grad_block, value_all, preferred_element_type=jnp.float32
        )
        grad_scores = (
            probs * (grad_probs - jnp.sum(probs * grad_probs, -1, keepdims=True))
        ).astype(jnp.bfloat16)
        query_grad_block = (
            jnp.einsum("kgbt,tkd->bkgd", grad_scores, key_all, preferred_element_type=jnp.float32)
            * factor
        )
        key_acc = (
            key_acc
            + jnp.einsum(
                "kgbt,bkgd->tkd", grad_scores, query_block, preferred_element_type=jnp.float32
            )
            * factor
        )
        value_acc = value_acc + jnp.einsum(
            "kgbt,bkgd->tkd", probs_low, grad_block, preferred_element_type=jnp.float32
        )
        return ((key_acc, value_acc), query_grad_block.reshape(block, head_count, HD))

    empty = jnp.zeros((2 * half_len, pair_count, HD), jnp.float32)
    (key_acc, value_acc), query_grad_blocks = lax.scan(
        backward_block,
        (empty, empty),
        (query_blocks, index_blocks, start_blocks, grad_blocks, log_totals),
    )
    key_back, value_back = (
        shifted(key_acc[:half_len].astype(jnp.bfloat16), "fsdp", -1).astype(jnp.float32),
        shifted(value_acc[:half_len].astype(jnp.bfloat16), "fsdp", -1).astype(jnp.float32),
    )
    key_local = key_acc[half_len:] + key_back
    value_local = value_acc[half_len:] + value_back
    query_grad_heads = query_grad_blocks.reshape(half_len, head_count, HD)
    grad_query_tok, grad_key_tok, grad_value_tok = (
        lax.all_to_all(
            query_grad_heads.astype(jnp.bfloat16), "seq", split_axis=0, concat_axis=1, tiled=True
        ).astype(query_grad_heads.dtype),
        lax.all_to_all(
            key_local.astype(jnp.bfloat16), "seq", split_axis=0, concat_axis=1, tiled=True
        ).astype(key_local.dtype),
        lax.all_to_all(
            value_local.astype(jnp.bfloat16), "seq", split_axis=0, concat_axis=1, tiled=True
        ).astype(value_local.dtype),
    )
    if repeat > 1:
        grad_key_tok = grad_key_tok.reshape(token_count, KVH, repeat, HD).sum(2)
        grad_value_tok = grad_value_tok.reshape(token_count, KVH, repeat, HD).sum(2)
    query_lin_grad = (
        rotate_back(grad_query_tok, cosine, sine).astype(jnp.bfloat16).reshape(token_count, QH * HD)
    )
    key_lin_grad = (
        rotate_back(grad_key_tok, cosine, sine).astype(jnp.bfloat16).reshape(token_count, KVH * HD)
    )
    value_lin_grad = grad_value_tok.astype(jnp.bfloat16).reshape(token_count, KVH * HD)
    query_grad = jnp.einsum(
        "td,tc->dc", normed_low, query_lin_grad, preferred_element_type=jnp.float32
    )
    key_grad = jnp.einsum("td,tc->dc", normed_low, key_lin_grad, preferred_element_type=jnp.float32)
    value_grad = jnp.einsum(
        "td,tc->dc", normed_low, value_lin_grad, preferred_element_type=jnp.float32
    )
    grad_normed_one = jnp.einsum(
        "tc,dc->td", query_lin_grad, wq_full, preferred_element_type=jnp.float32
    )
    grad_normed_one = grad_normed_one + jnp.einsum(
        "tc,dc->td", key_lin_grad, wk_full, preferred_element_type=jnp.float32
    )
    grad_normed_one = grad_normed_one + jnp.einsum(
        "tc,dc->td", value_lin_grad, wv_full, preferred_element_type=jnp.float32
    )
    grad_rows_one, first_gain_grad = norm_backward(grad_normed_one, unit_one, scale_one, gain_one)
    input_grad = (grad_middle + grad_rows_one).astype(jnp.bfloat16)[None]
    pieces = (
        lax.psum_scatter(
            first_gain_grad.astype(jnp.bfloat16), "fsdp", scatter_dimension=0, tiled=True
        ).astype(jnp.float32),
        lax.psum_scatter(
            query_grad.astype(jnp.bfloat16), "fsdp", scatter_dimension=0, tiled=True
        ).astype(jnp.float32),
        lax.psum_scatter(
            key_grad.astype(jnp.bfloat16), "fsdp", scatter_dimension=0, tiled=True
        ).astype(jnp.float32),
        lax.psum_scatter(
            value_grad.astype(jnp.bfloat16), "fsdp", scatter_dimension=0, tiled=True
        ).astype(jnp.float32),
        lax.psum_scatter(
            output_grad.astype(jnp.bfloat16), "fsdp", scatter_dimension=0, tiled=True
        ).astype(jnp.float32),
        lax.psum_scatter(
            second_gain_grad.astype(jnp.bfloat16), "fsdp", scatter_dimension=0, tiled=True
        ).astype(jnp.float32),
        lax.psum_scatter(
            gate_grad.astype(jnp.bfloat16), "fsdp", scatter_dimension=0, tiled=True
        ).astype(jnp.float32),
        lax.psum_scatter(
            up_grad.astype(jnp.bfloat16), "fsdp", scatter_dimension=0, tiled=True
        ).astype(jnp.float32),
        lax.psum_scatter(
            down_grad.astype(jnp.bfloat16), "fsdp", scatter_dimension=0, tiled=True
        ).astype(jnp.float32),
    )
    shares = (
        lax.psum(pieces[0].astype(jnp.bfloat16), "seq").astype(jnp.float32),
        lax.psum(pieces[1].astype(jnp.bfloat16), "seq").astype(jnp.float32),
        lax.psum(pieces[2].astype(jnp.bfloat16), "seq").astype(jnp.float32),
        lax.psum(pieces[3].astype(jnp.bfloat16), "seq").astype(jnp.float32),
        lax.psum(pieces[4].astype(jnp.bfloat16), "seq").astype(jnp.float32),
        lax.psum(pieces[5].astype(jnp.bfloat16), "seq").astype(jnp.float32),
        lax.psum(pieces[6].astype(jnp.bfloat16), "seq").astype(jnp.float32),
        lax.psum(pieces[7].astype(jnp.bfloat16), "seq").astype(jnp.float32),
        lax.psum(pieces[8].astype(jnp.bfloat16), "seq").astype(jnp.float32),
    )
    return (
        block_output,
        input_grad,
        shares[0],
        shares[1],
        shares[2],
        shares[3],
        shares[4],
        shares[5],
        shares[6],
        shares[7],
        shares[8],
    )


def plain_solution(mesh):
    placed = (
        P("fsdp", "seq", None),
        P("fsdp", "seq"),
        P("fsdp"),
        P("fsdp", None),
        P("fsdp", None),
        P("fsdp", None),
        P("fsdp", None),
        P("fsdp"),
        P("fsdp", None),
        P("fsdp", None),
        P("fsdp", None),
        P("fsdp", "seq", None),
    )
    return jax.shard_map(
        plain_body,
        mesh=mesh,
        in_specs=placed,
        out_specs=(
            P("fsdp", "seq", None),
            P("fsdp", "seq", None),
            P("fsdp"),
            P("fsdp", None),
            P("fsdp", None),
            P("fsdp", None),
            P("fsdp", None),
            P("fsdp"),
            P("fsdp", None),
            P("fsdp", None),
            P("fsdp", None),
        ),
        check_vma=False,
    )
```

```python
import functools
import math

import jax
import jax.numpy as jnp
from jax import lax
from jax.experimental import pallas as pl
from jax.experimental.pallas import tpu as pltpu
from jax.sharding import Mesh
from jax.sharding import PartitionSpec as P

QH = 16
KVH = 8
HD = 96


THETA = 100000.0
EPS = 1e-05
LOW = jnp.bfloat16
F32 = jnp.float32
NEG = -1e30
LN2 = math.log(2.0)


def contract(left, right, left_axis, right_axis):
    return lax.dot_general(
        left, right, (((left_axis,), (right_axis,)), ((), ())), preferred_element_type=F32
    )


def visible(first, second, query_block, key_block, size):
    key = key_block * size + lax.broadcasted_iota(jnp.int32, (size, size), 0)
    query = query_block * size + lax.broadcasted_iota(jnp.int32, (1, size), 1)
    start = jnp.where(query >= second, second, jnp.where(query >= first, first, 0))
    return (key >= start) & (key <= query)


def slot_of(block, count):
    return (block % (count // 2)) * 2 + block // (count // 2)


def forward_kernel(
    scalars,
    own_ref,
    other_ref,
    low_ref,
    full_ref,
    log_ref,
    query_s,
    key_s,
    value_s,
    top_s,
    total_s,
    mixed_s,
    *,
    size,
    count,
):
    half = scalars[0]
    first = scalars[1]
    second = scalars[2]
    here = pl.program_id(0)
    per_half = count // 2

    @pl.when(here == 0)
    def _():
        for ref, side in ((own_ref, half), (other_ref, 1 - half)):
            for step in range(per_half):
                block = side * per_half + step
                columns = slice(step * size, (step + 1) * size)
                query_s[block] = ref[0:HD, columns]
                key_s[block] = ref[HD : 2 * HD, columns].T
                value_s[block] = ref[2 * HD : 3 * HD, columns]

    query = query_s[here]
    top_s[...] = jnp.full_like(top_s, NEG)
    total_s[...] = jnp.zeros_like(total_s)
    mixed_s[...] = jnp.zeros_like(mixed_s)

    def add_block(block, masked):
        scores = contract(key_s[block], query, 1, 0)
        if masked:
            scores = jnp.where(visible(first, second, here, block, size), scores, NEG)
        old_top = top_s[...]
        top = jnp.maximum(old_top, jnp.max(scores, 0, keepdims=True))
        expo = jnp.exp2(scores - top)
        scale = jnp.exp2(old_top - top)
        top_s[...] = top
        total_s[...] = total_s[...] * scale + jnp.sum(expo, 0, keepdims=True)
        mixed_s[...] = mixed_s[...] * scale + contract(value_s[block], expo.astype(LOW), 1, 0)

    last = count - 1

    @pl.loop(1, jnp.where(here == last, 1, here))
    def _(block):
        add_block(block, False)

    @pl.loop(0, jnp.where(here == last, count, jnp.minimum(here + 1, 2)))
    def _(step):
        add_block(jnp.where(here == last, step, step * here), True)

    total = total_s[...]
    result = mixed_s[...] / total
    full_ref[0] = result
    low_ref[0] = result.astype(LOW)
    log_ref[0] = top_s[...] + jnp.log2(total)


def backward_kernel(
    scalars,
    own_ref,
    other_ref,
    grad_ref,
    full_ref,
    log_ref,
    kept_ref,
    leaving_ref,
    query_s,
    key_s,
    value_s,
    delta_s,
    query_grad_s,
    key_grad_s,
    value_grad_s,
    *,
    size,
    count,
):
    half = scalars[0]
    first = scalars[1]
    second = scalars[2]
    here = pl.program_id(0)
    per_half = count // 2

    @pl.when(here == 0)
    def _():
        for ref, side in ((own_ref, half), (other_ref, 1 - half)):
            for step in range(per_half):
                block = side * per_half + step
                columns = slice(step * size, (step + 1) * size)
                query_s[block] = ref[0:HD, columns]
                key_s[block] = ref[HD : 2 * HD, columns]
                value_s[block] = ref[2 * HD : 3 * HD, columns].T
        for block in range(count):
            delta_s[block] = jnp.sum(
                grad_ref[slot_of(block, count)].astype(F32) * full_ref[block], 0, keepdims=True
            )
        query_grad_s[...] = jnp.zeros_like(query_grad_s)

    key_grad_s[...] = jnp.zeros_like(key_grad_s)
    value_grad_s[...] = jnp.zeros_like(value_grad_s)
    key = key_s[here]
    key_rows = key.T
    value_rows = value_s[here]

    def add_block(block, masked):
        query = query_s[block]
        grad = grad_ref[slot_of(block, count)]
        scores = contract(key_rows, query, 1, 0)
        if masked:
            scores = jnp.where(visible(first, second, block, here, size), scores, NEG)
        probs = jnp.exp2(scores - log_ref[block])
        grad_probs = contract(value_rows, grad, 1, 0)
        grad_scores = (probs * (grad_probs - delta_s[block])).astype(LOW)
        value_grad_s[...] += contract(grad, probs.astype(LOW), 1, 1)
        key_grad_s[...] += contract(query, grad_scores, 1, 1)
        query_grad_s[block] += contract(key, grad_scores, 1, 0)

    last = count - 1

    @pl.loop(here + 1, jnp.where(here == 0, 1, last))
    def _(block):
        add_block(block, False)

    @pl.loop(0, jnp.where(here == 0, count, jnp.where(here == last, 1, 2)))
    def _(step):
        add_block(jnp.where(here == 0, step, jnp.where(step == 0, here, last)), True)

    side = here // per_half
    columns = pl.ds(pl.multiple_of((here % per_half) * size, size), size)

    def write(out_ref):
        out_ref[0:HD, columns] = (query_grad_s[here] * HD**-0.5).astype(LOW)
        out_ref[HD : 2 * HD, columns] = (key_grad_s[...] * LN2).astype(LOW)
        out_ref[2 * HD : 3 * HD, columns] = value_grad_s[...].astype(LOW)

    @pl.when(side == half)
    def _():
        write(kept_ref)

    @pl.when(side != half)
    def _():
        write(leaving_ref)


def attend_forward(scalars, own, other, size):
    count = 2 * own.shape[1] // size
    whole = lambda shape: pl.BlockSpec(shape, lambda i, s: (0,) * len(shape))
    pairs = count * (count + 1) // 2
    return pl.pallas_call(
        functools.partial(forward_kernel, size=size, count=count),
        grid_spec=pltpu.PrefetchScalarGridSpec(
            num_scalar_prefetch=1,
            grid=(count,),
            in_specs=[whole(own.shape), whole(other.shape)],
            out_specs=[
                pl.BlockSpec(
                    (1, HD, size), lambda i, s: (slot_of(i, count), 0, 0)
                ),
                pl.BlockSpec((1, HD, size), lambda i, s: (i, 0, 0)),
                pl.BlockSpec((1, 1, size), lambda i, s: (i, 0, 0)),
            ],
            scratch_shapes=[
                pltpu.VMEM((count, HD, size), LOW),
                pltpu.VMEM((count, size, HD), LOW),
                pltpu.VMEM((count, HD, size), LOW),
                pltpu.VMEM((1, size), F32),
                pltpu.VMEM((1, size), F32),
                pltpu.VMEM((HD, size), F32),
            ],
        ),
        out_shape=[
            jax.ShapeDtypeStruct((count, HD, size), LOW),
            jax.ShapeDtypeStruct((count, HD, size), F32),
            jax.ShapeDtypeStruct((count, 1, size), F32),
        ],
        compiler_params=pltpu.CompilerParams(
            dimension_semantics=("arbitrary",), vmem_limit_bytes=32 * 2**20
        ),
        cost_estimate=pl.CostEstimate(
            flops=pairs * size * size * HD * 32,
            bytes_accessed=10 * 2**20,
            transcendentals=pairs * size * size,
        ),
        name="attend_forward",
    )(scalars, own, other)


def attend_backward(scalars, own, other, grad, full, log_total):
    count, _, size = grad.shape
    whole = lambda shape: pl.BlockSpec(shape, lambda i, s: (0,) * len(shape))
    pairs = count * (count + 1) // 2
    out_shape = own.shape
    return pl.pallas_call(
        functools.partial(backward_kernel, size=size, count=count),
        grid_spec=pltpu.PrefetchScalarGridSpec(
            num_scalar_prefetch=1,
            grid=(count,),
            in_specs=[
                whole(own.shape),
                whole(other.shape),
                whole(grad.shape),
                whole(full.shape),
                whole(log_total.shape),
            ],
            out_specs=[whole(out_shape)] * 2,
            scratch_shapes=[
                pltpu.VMEM((count, HD, size), LOW),
                pltpu.VMEM((count, HD, size), LOW),
                pltpu.VMEM((count, size, HD), LOW),
                pltpu.VMEM((count, 1, size), F32),
                pltpu.VMEM((count, HD, size), F32),
                pltpu.VMEM((HD, size), F32),
                pltpu.VMEM((HD, size), F32),
            ],
        ),
        out_shape=[jax.ShapeDtypeStruct(out_shape, LOW)] * 2,
        compiler_params=pltpu.CompilerParams(
            dimension_semantics=("arbitrary",), vmem_limit_bytes=32 * 2**20
        ),
        cost_estimate=pl.CostEstimate(
            flops=pairs * size * size * HD * 42,
            bytes_accessed=16 * 2**20,
            transcendentals=pairs * size * size,
        ),
        name="attend_backward",
    )(scalars, own, other, grad, full, log_total)


def place_rows_kernel(order, *refs):
    pieces, out_ref = refs[:-1], refs[-1]
    size = pieces[0].shape[0]
    for index, piece in enumerate(pieces):
        start = pl.multiple_of(order[index] * size, size)
        out_ref[pl.ds(start, size), :] = piece[...].astype(F32)


def place_rows(order, pieces):
    size, width = pieces[0].shape
    total = size * len(pieces)
    step = 512
    return pl.pallas_call(
        place_rows_kernel,
        grid_spec=pltpu.PrefetchScalarGridSpec(
            num_scalar_prefetch=1,
            grid=(width // step,),
            in_specs=[pl.BlockSpec((size, step), lambda i, s: (0, i)) for _ in pieces],
            out_specs=pl.BlockSpec((total, step), lambda i, s: (0, i)),
        ),
        out_shape=jax.ShapeDtypeStruct((total, width), F32),
        compiler_params=pltpu.CompilerParams(vmem_limit_bytes=24 * 2**20),
        cost_estimate=pl.CostEstimate(
            flops=0, bytes_accessed=total * width * 6, transcendentals=0
        ),
        name="place_rows",
    )(order, *pieces)


def place_columns_kernel(order, gain_ref, gate_w_ref, up_w_ref, *refs):
    count = (len(refs) - 3) // 2
    gates, ups = refs[:count], refs[count : 2 * count]
    gate_ref, up_ref, sum_ref = refs[2 * count :]
    size = gates[0].shape[1]
    gain = gain_ref[...]
    total = jnp.zeros((gate_ref.shape[0], size), F32)
    for index in range(count):
        columns = pl.ds(pl.multiple_of(order[index] * size, size), size)
        gate, up = gates[index][...].astype(F32), ups[index][...].astype(F32)
        total += gate * gate_w_ref[:, columns].astype(F32)
        total += up * up_w_ref[:, columns].astype(F32)
        gate_ref[:, columns] = gate * gain
        up_ref[:, columns] = up * gain

    @pl.when(pl.program_id(0) == 0)
    def _():
        sum_ref[...] = jnp.zeros_like(sum_ref)

    sum_ref[...] += jnp.sum(total, 1, keepdims=True)


def place_columns(order, gain, gate_weight, up_weight, gates, ups, shards):
    rows, width = gate_weight.shape
    span = width // shards
    size = span // len(gates)
    wide = pl.BlockSpec((rows, span), lambda i, s: (0, i))
    thin = pl.BlockSpec((rows, 1), lambda i, s: (0, 0))
    pieces = [pl.BlockSpec((rows, size), lambda i, s: (0, i)) for _ in (*gates, *ups)]
    return pl.pallas_call(
        place_columns_kernel,
        grid_spec=pltpu.PrefetchScalarGridSpec(
            num_scalar_prefetch=1,
            grid=(shards,),
            in_specs=[thin, wide, wide, *pieces],
            out_specs=[wide, wide, thin],
        ),
        out_shape=[
            jax.ShapeDtypeStruct((rows, width), F32),
            jax.ShapeDtypeStruct((rows, width), F32),
            jax.ShapeDtypeStruct((rows, 1), F32),
        ],
        compiler_params=pltpu.CompilerParams(
            dimension_semantics=("arbitrary",), vmem_limit_bytes=24 * 2**20
        ),
        cost_estimate=pl.CostEstimate(
            flops=rows * width * 6, bytes_accessed=rows * width * 16, transcendentals=0
        ),
        name="place_columns",
    )(order, gain, gate_weight, up_weight, *gates, *ups)


def place_heads_kernel(gain_ref, query_w, key_w, value_w, all_ref, query_ref, key_ref, value_ref, sum_ref):
    rows = gain_ref.shape[0]
    wide = query_ref.shape[1] // KVH
    gain = gain_ref[...]
    total = jnp.zeros((rows, 4 * HD), F32)
    pieces = [all_ref[i * rows : (i + 1) * rows, :].astype(F32) for i in range(KVH)]
    for start in range(0, KVH, 2):
        value = jnp.concatenate([piece[:, :wide] for piece in pieces[start : start + 2]], 1)
        columns = slice(start * wide, (start + 2) * wide)
        total += value * query_w[:, columns].astype(F32)
        query_ref[:, columns] = value * gain
    for first, weight, out_ref in ((wide, key_w, key_ref), (wide + HD, value_w, value_ref)):
        for start in range(0, KVH, 4):
            value = jnp.concatenate(
                [piece[:, first : first + HD] for piece in pieces[start : start + 4]], 1
            )
            columns = slice(start * HD, (start + 4) * HD)
            total += value * weight[:, columns].astype(F32)
            out_ref[:, columns] = value * gain
    sum_ref[...] = jnp.sum(total, 1, keepdims=True)


def place_heads(gain, query_weight, key_weight, value_weight, pieces):
    weights = (query_weight, key_weight, value_weight)
    rows = gain.shape[0]
    return pl.pallas_call(
        place_heads_kernel,
        out_shape=[jax.ShapeDtypeStruct(weight.shape, F32) for weight in weights]
        + [jax.ShapeDtypeStruct((rows, 1), F32)],
        compiler_params=pltpu.CompilerParams(vmem_limit_bytes=32 * 2**20),
        cost_estimate=pl.CostEstimate(
            flops=rows * 3072 * 4, bytes_accessed=rows * 3072 * 8, transcendentals=0
        ),
        name="place_heads",
    )(gain, *weights, pieces)


def merge_kernel(scalars, kept_ref, came_ref, cosine_ref, sine_ref, out_ref, split_ref):
    lead = scalars[0] == 0
    lines, _, size = split_ref.shape
    for line in range(lines):
        columns = slice(line * size, (line + 1) * size)
        kept = kept_ref[:, columns].astype(F32)
        came = came_ref[:, columns].astype(F32)
        cosine, sine = cosine_ref[:, columns], sine_ref[:, columns]
        joint = kept[HD:] + came[HD:]
        first = jnp.where(lead, kept[:HD], came[:HD])
        second = jnp.where(lead, came[:HD], kept[:HD])
        turned = []
        for value in (first, second, joint[:HD]):
            low, high = value[: HD // 2], value[HD // 2 :]
            turned.append(low * cosine + high * sine)
            turned.append(high * cosine - low * sine)
        turned.append(joint[HD:])
        result = jnp.concatenate([part.astype(LOW) for part in turned], 0)
        out_ref[:, columns] = result
        split_ref[line] = result


def merge(scalars, kept, came, cosine, sine, lines):
    tokens = kept.shape[1]
    whole = lambda value: pl.BlockSpec(value.shape, lambda i, s: (0,) * len(value.shape))
    outs = [
        jax.ShapeDtypeStruct((4 * HD, tokens), LOW),
        jax.ShapeDtypeStruct((lines, 4 * HD, tokens // lines), LOW),
    ]
    return pl.pallas_call(
        merge_kernel,
        grid_spec=pltpu.PrefetchScalarGridSpec(
            num_scalar_prefetch=1,
            grid=(1,),
            in_specs=[whole(value) for value in (kept, came, cosine, sine)],
            out_specs=[whole(value) for value in outs],
        ),
        out_shape=outs,
        compiler_params=pltpu.CompilerParams(vmem_limit_bytes=24 * 2**20),
        cost_estimate=pl.CostEstimate(
            flops=tokens * HD * 24, bytes_accessed=tokens * HD * 30, transcendentals=0
        ),
        name="merge",
    )(scalars, kept, came, cosine, sine)


def pack_kernel(scalars, gain_ref, query_ref, key_ref, value_ref, *outs):
    core = scalars[3]
    gain = gain_ref[...]
    wide = query_ref.shape[1] // KVH
    span = wide + 2 * HD
    for which in range(2):

        @pl.when(core == which)
        def _():
            for line in range(KVH // 2):
                head = 2 * line + which
                value = jnp.concatenate(
                    [
                        query_ref[:, head * wide : (head + 1) * wide].astype(F32),
                        key_ref[:, head * HD : (head + 1) * HD].astype(F32),
                        value_ref[:, head * HD : (head + 1) * HD].astype(F32),
                    ],
                    1,
                )
                place = (line % 2) * span
                outs[line // 2][:, place : place + span] = (value * gain).astype(LOW)


def pack(scalars, gain, query_weight, key_weight, value_weight):
    rows, width = query_weight.shape
    whole = lambda value: pl.BlockSpec(value.shape, lambda i, s: (0, 0))
    weights = (gain, query_weight, key_weight, value_weight)
    outs = [jax.ShapeDtypeStruct((rows, width // 2), LOW)] * 2
    return pl.pallas_call(
        pack_kernel,
        grid_spec=pltpu.PrefetchScalarGridSpec(
            num_scalar_prefetch=1,
            grid=(1,),
            in_specs=[whole(value) for value in weights],
            out_specs=[whole(value) for value in outs],
        ),
        out_shape=outs,
        compiler_params=pltpu.CompilerParams(vmem_limit_bytes=24 * 2**20),
        cost_estimate=pl.CostEstimate(
            flops=rows * width, bytes_accessed=rows * width * 6, transcendentals=0
        ),
        name="pack",
    )(scalars, *weights)


def spread_kernel(scalars, lin_ref, cosine_ref, sine_ref, own_ref, leaving_ref):
    cosine, sine = cosine_ref[...], sine_ref[...]

    def turn(start, factor):
        low = lin_ref[start : start + HD // 2, :]
        high = lin_ref[start + HD // 2 : start + HD, :]
        turned = ((low * cosine - high * sine) * factor, (high * cosine + low * sine) * factor)
        return jnp.concatenate([part.astype(LOW) for part in turned], 0)

    lead = scalars[0] == 0
    first, second = turn(0, HD**-0.5 / LN2), turn(HD, HD**-0.5 / LN2)

    @pl.when(lead)
    def _():
        own_ref[0:HD] = first
        leaving_ref[0:HD] = second

    @pl.when(jnp.logical_not(lead))
    def _():
        own_ref[0:HD] = second
        leaving_ref[0:HD] = first

    key = turn(2 * HD, 1.0)
    value = lin_ref[3 * HD : 4 * HD].astype(LOW)
    for ref in (own_ref, leaving_ref):
        ref[HD : 2 * HD] = key
        ref[2 * HD : 3 * HD] = value


def spread(scalars, lin, cosine, sine):
    tokens = lin.shape[1]
    step = 512
    column = lambda rows: pl.BlockSpec((rows, step), lambda i, s: (0, i))
    return pl.pallas_call(
        spread_kernel,
        grid_spec=pltpu.PrefetchScalarGridSpec(
            num_scalar_prefetch=1,
            grid=(tokens // step,),
            in_specs=[column(4 * HD), column(HD // 2), column(HD // 2)],
            out_specs=[column(3 * HD)] * 2,
        ),
        out_shape=[jax.ShapeDtypeStruct((3 * HD, tokens), LOW)] * 2,
        compiler_params=pltpu.CompilerParams(vmem_limit_bytes=24 * 2**20),
        cost_estimate=pl.CostEstimate(
            flops=tokens * HD * 24, bytes_accessed=tokens * HD * 36, transcendentals=0
        ),
        name="spread",
    )(scalars, lin, cosine, sine)


def swap(value, axis):
    return lax.ppermute(value, axis, [(0, 1), (1, 0)])


def swap_near(value):
    return lax.ppermute(value, "z", [(0, 1), (1, 0), (2, 3), (3, 2)])


def swap_far(value):
    return lax.ppermute(value, "z", [(0, 2), (2, 0), (1, 3), (3, 1)])


def tie(*values):
    return lax.optimization_barrier(values)


def in_order(place, own, other):
    return (jnp.where(place == 0, own, other), jnp.where(place == 0, other, own))


def both(place, own, other):
    return jnp.concatenate(in_order(place, own, other), 0)


def spread_out(value, first, second):
    other = swap(value, first)
    pair = jnp.stack(in_order(lax.axis_index(first), value, other))
    return pair, swap(pair, second)


def placed(pair, other, second):
    pairs = in_order(lax.axis_index(second), pair, other)
    grid = jnp.stack(pairs, 0 if second == "y" else 1)
    return grid.reshape(-1, *grid.shape[3:])


def pick(array, axis, at):
    return lax.dynamic_index_in_dim(array, at, axis, keepdims=False)


def halve(value, axis, along=0):
    at = lax.axis_index(axis)
    return pick(value, along, at), swap(pick(value, along, 1 - at), axis)


def halve_x(value):
    return halve(value.reshape(2, 2, -1, value.shape[-1]), "x", 1)


def halve_y(value):
    return halve(value.reshape(2, 2, -1, value.shape[-1]), "y", 0)


def fast_body(
    tokens,
    positions,
    first_gain,
    query_weight,
    key_weight,
    value_weight,
    output_weight,
    second_gain,
    gate_weight,
    up_weight,
    down_weight,
    cotangent,
):
    seq = ("z", "c")
    fsdp = ("y", "x")
    z, core, half = lax.axis_index("z"), lax.axis_index("c"), lax.axis_index("x")
    near = z % 2
    lines = lax.axis_size("z")
    seq_count = 2 * lines
    shards = lax.axis_size("y") * 2
    spot = z * 2 + core
    quarter = near * 2 + core
    rows = tokens[0]
    count, width = rows.shape
    chip_count = 2 * count
    half_len = count * seq_count
    seq_len = 2 * half_len

    begins = jnp.where(
        (spot == 0) & (half == 0),
        count - 1 - positions[0, count - 1],
        half * half_len + spot * count - positions[0, 0],
    )
    ends = begins + (seq_len - count)
    scalars = jnp.stack([half, begins, ends, core]).astype(jnp.int32)

    gain_one = first_gain.astype(F32)[:, None]
    gain_two = second_gain.astype(F32)[:, None]

    def row_scale(value):
        return lax.rsqrt(jnp.mean(value * value, -1, keepdims=True) + EPS)

    take = functools.partial(lax.dynamic_slice_in_dim, axis=1)
    take_rows = functools.partial(lax.dynamic_slice_in_dim, axis=0)
    gather = lambda value, axes: lax.all_gather(value, axes, axis=0, tiled=True)
    own_rows = rows.astype(F32)
    own_unit_scale = row_scale(own_rows)
    own_unit = own_rows * own_unit_scale
    units = gather(own_unit.astype(LOW), seq)
    wide = QH // KVH * HD
    qkv_shard = (
        jnp.concatenate(
            [
                take(query_weight, spot * wide, wide),
                take(key_weight, spot * HD, HD),
                take(value_weight, spot * HD, HD),
            ],
            1,
        ).astype(F32)
        * gain_one
    ).astype(LOW)
    out_rows = output_weight.shape[0] // 2
    out_shard = take_rows(output_weight, core * out_rows, out_rows)
    piece = down_weight.shape[0] // 4
    down_shard = take_rows(down_weight, quarter * piece, piece)
    gate_shard, up_shard = (
        (
            jnp.concatenate(
                [
                    take(weight, shard * 4 * piece + quarter * piece, piece)
                    for shard in range(shards)
                ],
                1,
            ).astype(F32)
            * gain_two
        ).astype(LOW)
        for weight in (gate_weight, up_weight)
    )
    side = lax.axis_index("y")
    qkv_pair = jnp.stack(in_order(half, qkv_shard, swap(qkv_shard, "x")))
    gate_pair = jnp.stack(in_order(half, gate_shard, swap(gate_shard, "x")))
    up_pair = jnp.stack(in_order(side, up_shard, swap(up_shard, "y")))
    qkv_pair, gate_pair, up_pair = tie(qkv_pair, gate_pair, up_pair)
    qkv_w = placed(qkv_pair, swap(qkv_pair, "y"), "y")
    gate_pair, up_pair = (gate_pair, swap(gate_pair, "y")), (up_pair, swap(up_pair, "x"))

    place = half * half_len + jnp.arange(half_len, dtype=jnp.int32)
    start = jnp.where(place >= ends, ends, jnp.where(place >= begins, begins, 0))
    freq = THETA ** (-(jnp.arange(HD // 2, dtype=F32) * 2.0 / HD))
    angle = freq[:, None] * (place - start).astype(F32)[None, :]
    cosine, sine = jnp.cos(angle), jnp.sin(angle)
    chip_rows = both(core, rows, swap(rows, "c"))
    units, own_cot, chip_rows = tie(units, cotangent[0], chip_rows)
    own, leaving = spread(scalars, contract(qkv_w, units, 0, 1), cosine, sine)

    near_cot = swap_near(own_cot)
    other, out_shard, down_shard, near_cot, chip_cot, gate_pair, up_pair = tie(
        swap(leaving, "x"),
        out_shard,
        down_shard,
        near_cot,
        both(core, own_cot, swap(own_cot, "c")),
        gate_pair,
        up_pair,
    )
    out_w = gather(out_shard, fsdp)
    down_w = gather(down_shard, fsdp)
    near_other = swap(near_cot, "c")
    head_low, head_full, log_total = attend_forward(scalars, own, other, chip_count)
    exchange = lambda value: lax.all_to_all(
        value, ("z", "x"), split_axis=0, concat_axis=0, tiled=True
    )
    head_low, near_other = tie(head_low, near_other)
    lead_shard, tail_shard = pack(scalars, gain_one, query_weight, key_weight, value_weight)
    heads, gate_w, up_w, near_cot, lead_shard = tie(
        exchange(head_low),
        placed(*gate_pair, "y"),
        placed(*up_pair, "x"),
        jnp.concatenate([near_cot, near_other], 0),
        lead_shard,
    )
    lead_w = gather(lead_shard, fsdp)
    heads = heads.reshape(QH // 2 * HD, chip_count)

    mine_of = lambda value: take_rows(value, core * count, count)
    theirs_of = lambda value: take_rows(value, (1 - core) * count, count)
    branch = contract(heads, out_w, 0, 0).astype(LOW)
    middle = chip_rows.astype(F32) + (branch.astype(F32) + swap(branch, "c").astype(F32))
    middle_scale = row_scale(middle)
    chip_unit = middle * middle_scale
    own_middle, own_scale, own_middle_unit = (
        mine_of(middle),
        mine_of(middle_scale),
        mine_of(chip_unit),
    )
    chip_unit = chip_unit.astype(LOW)
    near_unit = swap_near(mine_of(chip_unit))

    def feed(unit):
        gate, upper = contract(unit, gate_w, 1, 0), contract(unit, up_w, 1, 0)
        sigma = jax.nn.sigmoid(gate)
        silu = gate * sigma
        return (silu * upper).astype(LOW), (gate, upper, sigma, silu)

    def feed_back(cot, kept):
        gate, upper, sigma, silu = kept
        grad_hidden = contract(cot, down_w, 1, 1)
        gate_low = (grad_hidden * upper * sigma * (1.0 + gate * (1.0 - sigma))).astype(LOW)
        upper_low = (grad_hidden * silu).astype(LOW)
        part = contract(gate_low, gate_w, 1, 1) + contract(upper_low, up_w, 1, 1)
        return gate_low, upper_low, part

    def chip_sum(chip_part, near_part):
        near_sum = near_part[:count].astype(F32) + swap(near_part[count:].astype(LOW), "c")
        own_sum = mine_of(chip_part).astype(F32) + swap(theirs_of(chip_part).astype(LOW), "c")
        return own_sum, near_sum.astype(LOW)

    stack = lambda first, second: jnp.concatenate([first, second], 0)
    scatter = lambda value: lax.psum_scatter(value, fsdp, scatter_dimension=0, tiled=True)
    chip_hidden, chip_kept = feed(chip_unit)
    near_unit, chip_hidden = tie(near_unit, chip_hidden)
    near_unit = jnp.concatenate([near_unit, swap(near_unit, "c")], 0)
    near_hidden, near_kept = feed(near_unit)
    down_part = contract(
        stack(chip_hidden, near_hidden), stack(chip_cot, near_cot), 0, 0
    ).astype(LOW)
    near_cot, down_part = tie(near_cot, down_part)
    near_gate, near_upper, near_part = feed_back(near_cot, near_kept)
    chip_gate, chip_upper, chip_part = feed_back(chip_cot, chip_kept)
    grad_two, near_sum = chip_sum(chip_part, near_part)

    def four(value, near_value):
        return value, swap(value, "c"), near_value, swap(near_value, "c")

    def halves_first(value):
        cut = value.shape[-1] // 2
        return halve_x(value[:, :cut]), halve_y(value[:, cut:])

    def halves_second(firsts):
        return halve(sum(firsts[0]), "y"), halve(sum(firsts[1]), "x")

    def halves_end(seconds):
        return jnp.concatenate([sum(seconds[0]), sum(seconds[1])], 1)

    down_first = halves_first(down_part)
    near_sum, near_gate, near_upper, chip_part = tie(
        near_sum, near_gate, near_upper, chip_part
    )
    grad_came = swap_near(near_sum)
    all_units = stack(chip_unit, near_unit)
    gate_part = contract(all_units, stack(chip_gate, near_gate), 0, 0).astype(LOW)
    up_part = contract(all_units, stack(chip_upper, near_upper), 0, 0).astype(LOW)
    feed_own, feed_near = chip_sum(
        contract(chip_hidden, down_w, 1, 0), contract(near_hidden, down_w, 1, 0)
    )
    gate_part, up_part, down_first, grad_came, feed_near = tie(
        gate_part, up_part, down_first, grad_came, feed_near
    )
    feed_near = swap_near(feed_near)
    down_second = halves_second(down_first)
    grad_two = grad_two + grad_came.astype(F32)
    grad_middle = own_cot.astype(F32) + own_scale * (
        grad_two - own_middle_unit * jnp.mean(grad_two * own_middle_unit, -1, keepdims=True)
    )
    own_branch, lead_w, down_second, gate_part, up_part = tie(
        grad_middle.astype(LOW), lead_w, down_second, gate_part, up_part
    )
    gate_grad, up_grad = scatter(gate_part), scatter(up_part)
    down_grad = halves_end(down_second)
    down_far = swap_far(down_grad)
    grad_branch = both(core, own_branch, swap(own_branch, "c"))
    grad_heads = contract(out_w, grad_branch, 1, 1).astype(LOW)
    grad_heads, grad_branch, down_far = tie(grad_heads, grad_branch, down_far)
    down_sum = down_grad + down_far
    output_part = contract(heads, grad_branch, 1, 0).astype(LOW)
    output_grad = scatter(output_part)
    grad_head, output_part, gate_grad, down_sum = tie(
        exchange(grad_heads.reshape(2 * lines, HD, chip_count)), output_part, gate_grad, down_sum
    )
    down_near = swap_near(down_sum)

    gate_far = swap_far(gate_grad)
    kept, leaving = attend_backward(scalars, own, other, grad_head, head_full, log_total)
    kept, leaving, gate_far, down_near, tail_shard, feed_near = tie(
        kept, leaving, gate_far, down_near, tail_shard, feed_near
    )
    tail_w = gather(tail_shard, fsdp)

    up_far = swap_far(up_grad)
    gate_sum = gate_grad + gate_far
    gate_near = swap_near(gate_sum)
    block_output = (own_middle + feed_own + feed_near.astype(F32)).astype(LOW)[None]
    came, up_far, gate_near, block_output, output_grad = tie(
        swap(leaving, "x"), up_far, gate_near, block_output, output_grad
    )

    qkv_low, by_line = merge(scalars, kept, came, cosine, sine, lines)
    token_grads = lax.all_to_all(by_line, "z", split_axis=0, concat_axis=0, tiled=True)
    qkv_part = contract(units, qkv_low, 0, 1).astype(LOW).reshape(shards, 2, -1, 4 * HD)
    qkv_first = halve_x(qkv_part[:, 0]), halve_y(qkv_part[:, 1])
    qkv_second = halves_second(qkv_first)
    qkv_grad = jnp.concatenate([sum(qkv_second[0]), sum(qkv_second[1])], 0)
    up_sum = up_grad + up_far
    up_near = swap_near(up_sum)
    down_pieces = four(down_sum, down_near)
    token_grads, qkv_grad, up_near, down_pieces = tie(
        token_grads, qkv_grad, up_near, down_pieces
    )
    all_qkv = gather(qkv_grad, seq)

    token_grads = token_grads.reshape(-1, chip_count)
    split = lead_w.shape[1]
    grad_one = contract(token_grads[:split], lead_w, 0, 1) + contract(
        token_grads[split:], tail_w, 0, 1
    )
    grad_one, output_came = tie(grad_one, swap_near(output_grad))
    output_sum = output_grad + output_came
    output_far = swap_far(output_sum)
    grad_one = mine_of(grad_one) + swap(theirs_of(grad_one).astype(LOW), "c").astype(F32)
    grad_rows = own_unit_scale * (
        grad_one - own_unit * jnp.mean(grad_one * own_unit, -1, keepdims=True)
    )
    input_grad = (grad_middle + grad_rows).astype(LOW)[None]

    order = jnp.stack([quarter, quarter ^ 1, quarter ^ 2, quarter ^ 3]).astype(jnp.int32)
    core_order = jnp.stack([core, 1 - core]).astype(jnp.int32)
    down_total = place_rows(order, down_pieces)
    gate_total, up_total, second_gain_grad = place_columns(
        order, gain_two, gate_weight, up_weight, four(gate_sum, gate_near), four(up_sum, up_near), shards
    )
    output_far, second_gain_grad, all_qkv = tie(output_far, second_gain_grad, all_qkv)
    output_own = output_sum + output_far
    output_total = place_rows(core_order, (output_own, swap(output_own, "c")))
    query_grad, key_grad, value_grad, first_gain_grad = place_heads(
        gain_one, query_weight, key_weight, value_weight, all_qkv
    )
    return (
        block_output,
        input_grad,
        first_gain_grad[:, 0],
        query_grad,
        key_grad,
        value_grad,
        output_total,
        second_gain_grad[:, 0],
        gate_total,
        up_total,
        down_total,
    )


def fast_solution(mesh):
    seq_count, shard_count = mesh.devices.shape
    fine = Mesh(
        mesh.devices.reshape(seq_count // 2, 2, shard_count // 2, 2), ("z", "c", "y", "x")
    )
    seq, fsdp = ("z", "c"), ("y", "x")
    matrix = P(fsdp, None)
    return jax.shard_map(
        fast_body,
        mesh=fine,
        in_specs=(
            P(fsdp, seq, None),
            P(fsdp, seq),
            P(fsdp),
            matrix,
            matrix,
            matrix,
            matrix,
            P(fsdp),
            matrix,
            matrix,
            matrix,
            P(fsdp, seq, None),
        ),
        out_specs=(
            P(fsdp, seq, None),
            P(fsdp, seq, None),
            P(fsdp),
            matrix,
            matrix,
            matrix,
            matrix,
            P(fsdp),
            matrix,
            matrix,
            matrix,
        ),
        check_vma=False,
    )


def solution(mesh):
    shape = dict(mesh.shape)
    if shape["seq"] == KVH and shape["fsdp"] == 4:
        return fast_solution(mesh)
    return plain_solution(mesh)


def shifted(value, axis, steps):
    count = lax.axis_size(axis)
    first, last = (max(0, -steps), min(count, count - steps))
    return lax.ppermute(value, axis, [(source, source + steps) for source in range(first, last)])


def rope_tables(position_rows):
    freq = THETA ** (-(jnp.arange(HD // 2, dtype=jnp.float32) * 2.0 / HD))
    angle = position_rows.astype(jnp.float32)[:, None] * freq[None, :]
    cosine = jnp.cos(angle)
    sine = jnp.sin(angle)
    return (jnp.concatenate([cosine, cosine], -1), jnp.concatenate([sine, sine], -1))


def rotate(values, cosine, sine):
    half = HD // 2
    turned = jnp.concatenate([-values[..., half:], values[..., :half]], -1)
    return values * cosine[:, None, :] + turned * sine[:, None, :]


def rotate_back(grads, cosine, sine):
    half = HD // 2
    scaled = grads * sine[:, None, :]
    turned = jnp.concatenate([scaled[..., half:], -scaled[..., :half]], -1)
    return grads * cosine[:, None, :] + turned


def norm_forward(rows, gain):
    scale = lax.rsqrt(jnp.mean(rows * rows, -1, keepdims=True) + EPS)
    unit = rows * scale
    return (unit * gain, unit, scale)


def norm_backward(grad_out, unit, scale, gain):
    grad_unit = grad_out * gain
    gain_grad = jnp.sum(grad_out * unit, 0)
    grad_rows = scale * (grad_unit - unit * jnp.mean(grad_unit * unit, -1, keepdims=True))
    return (grad_rows, gain_grad)


def plain_body(
    tokens,
    positions,
    first_gain,
    query_weight,
    key_weight,
    value_weight,
    output_weight,
    second_gain,
    gate_weight,
    up_weight,
    down_weight,
    cotangent,
):
    seq_count = lax.axis_size("seq")
    local_rows = tokens[0]
    token_count = local_rows.shape[0]
    half_len = token_count * seq_count
    rows_float = local_rows.astype(jnp.float32)
    gain_one, wq_full, wk_full, wv_full, wo_full = (
        lax.all_gather(first_gain, "fsdp", axis=0, tiled=True),
        lax.all_gather(query_weight, "fsdp", axis=0, tiled=True),
        lax.all_gather(key_weight, "fsdp", axis=0, tiled=True),
        lax.all_gather(value_weight, "fsdp", axis=0, tiled=True),
        lax.all_gather(output_weight, "fsdp", axis=0, tiled=True),
    )
    gain_one = gain_one.astype(jnp.float32)
    normed_one, unit_one, scale_one = norm_forward(rows_float, gain_one)
    normed_low = normed_one.astype(jnp.bfloat16)
    cosine, sine = rope_tables(positions[0])
    query_lin = jnp.dot(normed_low, wq_full, preferred_element_type=jnp.float32).reshape(
        token_count, QH, HD
    )
    key_lin = jnp.dot(normed_low, wk_full, preferred_element_type=jnp.float32).reshape(
        token_count, KVH, HD
    )
    value_lin = jnp.dot(normed_low, wv_full, preferred_element_type=jnp.float32).reshape(
        token_count, KVH, HD
    )
    query_rows = rotate(query_lin, cosine, sine).astype(jnp.bfloat16)
    key_rows = rotate(key_lin, cosine, sine).astype(jnp.bfloat16)
    value_rows = value_lin.astype(jnp.bfloat16)
    repeat = max(1, seq_count // KVH)
    if repeat > 1:
        key_rows = jnp.repeat(key_rows, repeat, axis=1)
        value_rows = jnp.repeat(value_rows, repeat, axis=1)
    query_heads, key_heads, value_heads = (
        lax.all_to_all(query_rows, "seq", split_axis=1, concat_axis=0, tiled=True),
        lax.all_to_all(key_rows, "seq", split_axis=1, concat_axis=0, tiled=True),
        lax.all_to_all(value_rows, "seq", split_axis=1, concat_axis=0, tiled=True),
    )
    head_count = query_heads.shape[1]
    pair_count = key_heads.shape[1]
    group = head_count // pair_count
    half_positions = lax.all_gather(positions[0], "seq", axis=0, tiled=True)
    key_prior, value_prior = shifted((key_heads, value_heads), "fsdp", 1)
    key_all = jnp.concatenate([key_prior, key_heads], 0)
    value_all = jnp.concatenate([value_prior, value_heads], 0)
    half_index = lax.axis_index("fsdp") % 2
    key_index = (half_index - 1) * half_len + jnp.arange(2 * half_len, dtype=jnp.int32)
    row_index = half_index * half_len + jnp.arange(half_len, dtype=jnp.int32)
    row_start = row_index - half_positions
    block = min(512, half_len)
    count = half_len // block
    factor = HD ** (-0.5)
    query_blocks = query_heads.reshape(count, block, pair_count, group, HD)
    index_blocks = row_index.reshape(count, block)
    start_blocks = row_start.reshape(count, block)

    def block_scores(query_block, index_block, start_block):
        scores = (
            jnp.einsum("bkgd,tkd->kgbt", query_block, key_all, preferred_element_type=jnp.float32)
            * factor
        )
        visible = (key_index[None, :] >= start_block[:, None]) & (
            key_index[None, :] <= index_block[:, None]
        )
        return jnp.where(visible, scores, -1e30)

    def forward_block(items):
        query_block, index_block, start_block = items
        scores = block_scores(query_block, index_block, start_block)
        top = jnp.max(scores, -1, keepdims=True)
        expo = jnp.exp(scores - top)
        total = jnp.sum(expo, -1, keepdims=True)
        probs_low = (expo / total).astype(jnp.bfloat16)
        mixed = jnp.einsum(
            "kgbt,tkd->bkgd", probs_low, value_all, preferred_element_type=jnp.float32
        )
        return (mixed.reshape(block, head_count, HD).astype(jnp.bfloat16), top + jnp.log(total))

    head_blocks, log_totals = lax.map(forward_block, (query_blocks, index_blocks, start_blocks))
    head_out = head_blocks.reshape(half_len, head_count, HD)
    token_heads = lax.all_to_all(head_out, "seq", split_axis=0, concat_axis=1, tiled=True)
    heads_flat = token_heads.reshape(token_count, QH * HD)
    middle = rows_float + jnp.dot(heads_flat, wo_full, preferred_element_type=jnp.float32)
    gain_two, wg_full, wu_full, wd_full = (
        lax.all_gather(second_gain, "fsdp", axis=0, tiled=True),
        lax.all_gather(gate_weight, "fsdp", axis=0, tiled=True),
        lax.all_gather(up_weight, "fsdp", axis=0, tiled=True),
        lax.all_gather(down_weight, "fsdp", axis=0, tiled=True),
    )
    gain_two = gain_two.astype(jnp.float32)
    normed_two, unit_two, scale_two = norm_forward(middle, gain_two)
    normed_two_low = normed_two.astype(jnp.bfloat16)
    gate = jnp.dot(normed_two_low, wg_full, preferred_element_type=jnp.float32)
    upper = jnp.dot(normed_two_low, wu_full, preferred_element_type=jnp.float32)
    hidden = (jax.nn.silu(gate) * upper).astype(jnp.bfloat16)
    result = middle + jnp.dot(hidden, wd_full, preferred_element_type=jnp.float32)
    block_output = result.astype(jnp.bfloat16)[None]
    grad_low = cotangent[0]
    grad_rows = grad_low.astype(jnp.float32)
    down_grad = jnp.einsum("tf,td->fd", hidden, grad_low, preferred_element_type=jnp.float32)
    grad_hidden = jnp.einsum("td,fd->tf", grad_low, wd_full, preferred_element_type=jnp.float32)
    sigma = jax.nn.sigmoid(gate)
    gate_low = (grad_hidden * upper * sigma * (1.0 + gate * (1.0 - sigma))).astype(jnp.bfloat16)
    upper_low = (grad_hidden * gate * sigma).astype(jnp.bfloat16)
    gate_grad = jnp.einsum(
        "td,tf->df", normed_two_low, gate_low, preferred_element_type=jnp.float32
    )
    up_grad = jnp.einsum("td,tf->df", normed_two_low, upper_low, preferred_element_type=jnp.float32)
    grad_normed_two = jnp.einsum(
        "tf,df->td", gate_low, wg_full, preferred_element_type=jnp.float32
    ) + jnp.einsum("tf,df->td", upper_low, wu_full, preferred_element_type=jnp.float32)
    grad_middle_norm, second_gain_grad = norm_backward(
        grad_normed_two, unit_two, scale_two, gain_two
    )
    grad_middle = grad_rows + grad_middle_norm
    grad_branch = grad_middle.astype(jnp.bfloat16)
    output_grad = jnp.einsum(
        "tc,td->cd", heads_flat, grad_branch, preferred_element_type=jnp.float32
    )
    grad_heads = (
        jnp.einsum("td,cd->tc", grad_branch, wo_full, preferred_element_type=jnp.float32)
        .astype(jnp.bfloat16)
        .reshape(token_count, QH, HD)
    )
    grad_head_rows = lax.all_to_all(grad_heads, "seq", split_axis=1, concat_axis=0, tiled=True)
    grad_blocks = grad_head_rows.reshape(count, block, pair_count, group, HD)

    def backward_block(carry, items):
        key_acc, value_acc = carry
        query_block, index_block, start_block, grad_block, log_block = items
        scores = block_scores(query_block, index_block, start_block)
        probs = jnp.exp(scores - log_block)
        probs_low = probs.astype(jnp.bfloat16)
        grad_probs = jnp.einsum(
            "bkgd,tkd->kgbt", grad_block, value_all, preferred_element_type=jnp.float32
        )
        grad_scores = (
            probs * (grad_probs - jnp.sum(probs * grad_probs, -1, keepdims=True))
        ).astype(jnp.bfloat16)
        query_grad_block = (
            jnp.einsum("kgbt,tkd->bkgd", grad_scores, key_all, preferred_element_type=jnp.float32)
            * factor
        )
        key_acc = (
            key_acc
            + jnp.einsum(
                "kgbt,bkgd->tkd", grad_scores, query_block, preferred_element_type=jnp.float32
            )
            * factor
        )
        value_acc = value_acc + jnp.einsum(
            "kgbt,bkgd->tkd", probs_low, grad_block, preferred_element_type=jnp.float32
        )
        return ((key_acc, value_acc), query_grad_block.reshape(block, head_count, HD))

    empty = jnp.zeros((2 * half_len, pair_count, HD), jnp.float32)
    (key_acc, value_acc), query_grad_blocks = lax.scan(
        backward_block,
        (empty, empty),
        (query_blocks, index_blocks, start_blocks, grad_blocks, log_totals),
    )
    key_back, value_back = (
        shifted(key_acc[:half_len].astype(jnp.bfloat16), "fsdp", -1).astype(jnp.float32),
        shifted(value_acc[:half_len].astype(jnp.bfloat16), "fsdp", -1).astype(jnp.float32),
    )
    key_local = key_acc[half_len:] + key_back
    value_local = value_acc[half_len:] + value_back
    query_grad_heads = query_grad_blocks.reshape(half_len, head_count, HD)
    grad_query_tok, grad_key_tok, grad_value_tok = (
        lax.all_to_all(
            query_grad_heads.astype(jnp.bfloat16), "seq", split_axis=0, concat_axis=1, tiled=True
        ).astype(query_grad_heads.dtype),
        lax.all_to_all(
            key_local.astype(jnp.bfloat16), "seq", split_axis=0, concat_axis=1, tiled=True
        ).astype(key_local.dtype),
        lax.all_to_all(
            value_local.astype(jnp.bfloat16), "seq", split_axis=0, concat_axis=1, tiled=True
        ).astype(value_local.dtype),
    )
    if repeat > 1:
        grad_key_tok = grad_key_tok.reshape(token_count, KVH, repeat, HD).sum(2)
        grad_value_tok = grad_value_tok.reshape(token_count, KVH, repeat, HD).sum(2)
    query_lin_grad = (
        rotate_back(grad_query_tok, cosine, sine).astype(jnp.bfloat16).reshape(token_count, QH * HD)
    )
    key_lin_grad = (
        rotate_back(grad_key_tok, cosine, sine).astype(jnp.bfloat16).reshape(token_count, KVH * HD)
    )
    value_lin_grad = grad_value_tok.astype(jnp.bfloat16).reshape(token_count, KVH * HD)
    query_grad = jnp.einsum(
        "td,tc->dc", normed_low, query_lin_grad, preferred_element_type=jnp.float32
    )
    key_grad = jnp.einsum("td,tc->dc", normed_low, key_lin_grad, preferred_element_type=jnp.float32)
    value_grad = jnp.einsum(
        "td,tc->dc", normed_low, value_lin_grad, preferred_element_type=jnp.float32
    )
    grad_normed_one = jnp.einsum(
        "tc,dc->td", query_lin_grad, wq_full, preferred_element_type=jnp.float32
    )
    grad_normed_one = grad_normed_one + jnp.einsum(
        "tc,dc->td", key_lin_grad, wk_full, preferred_element_type=jnp.float32
    )
    grad_normed_one = grad_normed_one + jnp.einsum(
        "tc,dc->td", value_lin_grad, wv_full, preferred_element_type=jnp.float32
    )
    grad_rows_one, first_gain_grad = norm_backward(grad_normed_one, unit_one, scale_one, gain_one)
    input_grad = (grad_middle + grad_rows_one).astype(jnp.bfloat16)[None]
    pieces = (
        lax.psum_scatter(
            first_gain_grad.astype(jnp.bfloat16), "fsdp", scatter_dimension=0, tiled=True
        ).astype(jnp.float32),
        lax.psum_scatter(
            query_grad.astype(jnp.bfloat16), "fsdp", scatter_dimension=0, tiled=True
        ).astype(jnp.float32),
        lax.psum_scatter(
            key_grad.astype(jnp.bfloat16), "fsdp", scatter_dimension=0, tiled=True
        ).astype(jnp.float32),
        lax.psum_scatter(
            value_grad.astype(jnp.bfloat16), "fsdp", scatter_dimension=0, tiled=True
        ).astype(jnp.float32),
        lax.psum_scatter(
            output_grad.astype(jnp.bfloat16), "fsdp", scatter_dimension=0, tiled=True
        ).astype(jnp.float32),
        lax.psum_scatter(
            second_gain_grad.astype(jnp.bfloat16), "fsdp", scatter_dimension=0, tiled=True
        ).astype(jnp.float32),
        lax.psum_scatter(
            gate_grad.astype(jnp.bfloat16), "fsdp", scatter_dimension=0, tiled=True
        ).astype(jnp.float32),
        lax.psum_scatter(
            up_grad.astype(jnp.bfloat16), "fsdp", scatter_dimension=0, tiled=True
        ).astype(jnp.float32),
        lax.psum_scatter(
            down_grad.astype(jnp.bfloat16), "fsdp", scatter_dimension=0, tiled=True
        ).astype(jnp.float32),
    )
    shares = (
        lax.psum(pieces[0].astype(jnp.bfloat16), "seq").astype(jnp.float32),
        lax.psum(pieces[1].astype(jnp.bfloat16), "seq").astype(jnp.float32),
        lax.psum(pieces[2].astype(jnp.bfloat16), "seq").astype(jnp.float32),
        lax.psum(pieces[3].astype(jnp.bfloat16), "seq").astype(jnp.float32),
        lax.psum(pieces[4].astype(jnp.bfloat16), "seq").astype(jnp.float32),
        lax.psum(pieces[5].astype(jnp.bfloat16), "seq").astype(jnp.float32),
        lax.psum(pieces[6].astype(jnp.bfloat16), "seq").astype(jnp.float32),
        lax.psum(pieces[7].astype(jnp.bfloat16), "seq").astype(jnp.float32),
        lax.psum(pieces[8].astype(jnp.bfloat16), "seq").astype(jnp.float32),
    )
    return (
        block_output,
        input_grad,
        shares[0],
        shares[1],
        shares[2],
        shares[3],
        shares[4],
        shares[5],
        shares[6],
        shares[7],
        shares[8],
    )


def plain_solution(mesh):
    placed = (
        P("fsdp", "seq", None),
        P("fsdp", "seq"),
        P("fsdp"),
        P("fsdp", None),
        P("fsdp", None),
        P("fsdp", None),
        P("fsdp", None),
        P("fsdp"),
        P("fsdp", None),
        P("fsdp", None),
        P("fsdp", None),
        P("fsdp", "seq", None),
    )
    return jax.shard_map(
        plain_body,
        mesh=mesh,
        in_specs=placed,
        out_specs=(
            P("fsdp", "seq", None),
            P("fsdp", "seq", None),
            P("fsdp"),
            P("fsdp", None),
            P("fsdp", None),
            P("fsdp", None),
            P("fsdp", None),
            P("fsdp"),
            P("fsdp", None),
            P("fsdp", None),
            P("fsdp", None),
        ),
        check_vma=False,
    )
```

```python
import functools
import math

import jax
import jax.numpy as jnp
from jax import lax
from jax.experimental import pallas as pl
from jax.experimental.pallas import tpu as pltpu
from jax.sharding import Mesh
from jax.sharding import PartitionSpec as P

QH = 16
KVH = 8
HD = 96


THETA = 100000.0
EPS = 1e-05
LOW = jnp.bfloat16
F32 = jnp.float32
NEG = -1e30
LN2 = math.log(2.0)


def contract(left, right, left_axis, right_axis):
    return lax.dot_general(
        left, right, (((left_axis,), (right_axis,)), ((), ())), preferred_element_type=F32
    )


def visible(first, second, query_start, key_start, queries, keys):
    key = key_start + lax.broadcasted_iota(jnp.int32, (keys, queries), 0)
    query = query_start + lax.broadcasted_iota(jnp.int32, (1, queries), 1)
    start = jnp.where(query >= second, second, jnp.where(query >= first, first, 0))
    return (key >= start) & (key <= query)


def halves_of(size):
    return slice(0, size // 2), slice(size // 2, size)


def slot_of(block, count):
    return (block % (count // 2)) * 2 + block // (count // 2)


def forward_kernel(
    scalars,
    own_ref,
    other_ref,
    low_ref,
    full_ref,
    log_ref,
    query_s,
    key_s,
    value_s,
    top_s,
    total_s,
    mixed_s,
    *,
    size,
    count,
):
    half = scalars[0]
    first = scalars[1]
    second = scalars[2]
    here = pl.program_id(0)
    per_half = count // 2

    @pl.when(here == 0)
    def _():
        for ref, side in ((own_ref, half), (other_ref, 1 - half)):
            for step in range(per_half):
                block = side * per_half + step
                columns = slice(step * size, (step + 1) * size)
                query_s[block] = ref[0:HD, columns]
                key_s[block] = ref[HD : 2 * HD, columns].T
                value_s[block] = ref[2 * HD : 3 * HD, columns]

    query = query_s[here]
    top_s[...] = jnp.full_like(top_s, NEG)
    total_s[...] = jnp.zeros_like(total_s)
    mixed_s[...] = jnp.zeros_like(mixed_s)

    def add_block(block, masked):
        keys, values = key_s[block], value_s[block]
        parts = halves_of(size)
        all_scores = [contract(keys, query[:, part], 1, 0) for part in parts]
        for part, scores in zip(parts, all_scores):
            if masked:
                seen = visible(
                    first, second, here * size + part.start, block * size, size // 2, size
                )
                scores = jnp.where(seen, scores, NEG)
            old_top = top_s[:, part]
            top = jnp.maximum(old_top, jnp.max(scores, 0, keepdims=True))
            expo = jnp.exp2(scores - top)
            scale = jnp.exp2(old_top - top)
            top_s[:, part] = top
            total_s[:, part] = total_s[:, part] * scale + jnp.sum(expo, 0, keepdims=True)
            mixed_s[:, part] = mixed_s[:, part] * scale + contract(
                values, expo.astype(LOW), 1, 0
            )

    last = count - 1

    @pl.loop(1, jnp.where(here == last, 1, here))
    def _(block):
        add_block(block, False)

    @pl.loop(0, jnp.where(here == last, count, jnp.minimum(here + 1, 2)))
    def _(step):
        add_block(jnp.where(here == last, step, step * here), True)

    total = total_s[...]
    result = mixed_s[...] / total
    full_ref[0] = result
    low_ref[0] = result.astype(LOW)
    log_ref[0] = top_s[...] + jnp.log2(total)


def backward_kernel(
    scalars,
    own_ref,
    other_ref,
    grad_ref,
    full_ref,
    log_ref,
    kept_ref,
    leaving_ref,
    query_s,
    key_s,
    value_s,
    delta_s,
    query_grad_s,
    key_grad_s,
    value_grad_s,
    *,
    size,
    count,
):
    half = scalars[0]
    first = scalars[1]
    second = scalars[2]
    here = pl.program_id(0)
    per_half = count // 2

    @pl.when(here == 0)
    def _():
        for ref, side in ((own_ref, half), (other_ref, 1 - half)):
            for step in range(per_half):
                block = side * per_half + step
                columns = slice(step * size, (step + 1) * size)
                query_s[block] = ref[0:HD, columns]
                key_s[block] = ref[HD : 2 * HD, columns]
                value_s[block] = ref[2 * HD : 3 * HD, columns].T
        for block in range(count):
            delta_s[block] = jnp.sum(
                grad_ref[slot_of(block, count)].astype(F32) * full_ref[block], 0, keepdims=True
            )
        query_grad_s[...] = jnp.zeros_like(query_grad_s)

    key_grad_s[...] = jnp.zeros_like(key_grad_s)
    value_grad_s[...] = jnp.zeros_like(value_grad_s)
    key = key_s[here]
    key_rows = key.T
    value_rows = value_s[here]

    def add_block(block, masked):
        query = query_s[block]
        grad = grad_ref[slot_of(block, count)]
        log_total, delta = log_ref[block], delta_s[block]
        parts = halves_of(size)
        products = [
            (contract(key_rows, query[:, part], 1, 0), contract(value_rows, grad[:, part], 1, 0))
            for part in parts
        ]
        for part, (scores, grad_probs) in zip(parts, products):
            if masked:
                seen = visible(
                    first, second, block * size + part.start, here * size, size // 2, size
                )
                scores = jnp.where(seen, scores, NEG)
            probs = jnp.exp2(scores - log_total[:, part])
            grad_scores = (probs * (grad_probs - delta[:, part])).astype(LOW)
            value_grad_s[...] += contract(grad[:, part], probs.astype(LOW), 1, 1)
            key_grad_s[...] += contract(query[:, part], grad_scores, 1, 1)
            query_grad_s[block, :, part] += contract(key, grad_scores, 1, 0)

    last = count - 1

    @pl.loop(here + 1, jnp.where(here == 0, 1, last))
    def _(block):
        add_block(block, False)

    @pl.loop(0, jnp.where(here == 0, count, jnp.where(here == last, 1, 2)))
    def _(step):
        add_block(jnp.where(here == 0, step, jnp.where(step == 0, here, last)), True)

    side = here // per_half
    columns = pl.ds(pl.multiple_of((here % per_half) * size, size), size)

    def write(out_ref):
        out_ref[0:HD, columns] = (query_grad_s[here] * HD**-0.5).astype(LOW)
        out_ref[HD : 2 * HD, columns] = (key_grad_s[...] * LN2).astype(LOW)
        out_ref[2 * HD : 3 * HD, columns] = value_grad_s[...].astype(LOW)

    @pl.when(side == half)
    def _():
        write(kept_ref)

    @pl.when(side != half)
    def _():
        write(leaving_ref)


def attend_forward(scalars, own, other, size):
    count = 2 * own.shape[1] // size
    whole = lambda shape: pl.BlockSpec(shape, lambda i, s: (0,) * len(shape))
    pairs = count * (count + 1) // 2
    return pl.pallas_call(
        functools.partial(forward_kernel, size=size, count=count),
        grid_spec=pltpu.PrefetchScalarGridSpec(
            num_scalar_prefetch=1,
            grid=(count,),
            in_specs=[whole(own.shape), whole(other.shape)],
            out_specs=[
                pl.BlockSpec(
                    (1, HD, size), lambda i, s: (slot_of(i, count), 0, 0)
                ),
                pl.BlockSpec((1, HD, size), lambda i, s: (i, 0, 0)),
                pl.BlockSpec((1, 1, size), lambda i, s: (i, 0, 0)),
            ],
            scratch_shapes=[
                pltpu.VMEM((count, HD, size), LOW),
                pltpu.VMEM((count, size, HD), LOW),
                pltpu.VMEM((count, HD, size), LOW),
                pltpu.VMEM((1, size), F32),
                pltpu.VMEM((1, size), F32),
                pltpu.VMEM((HD, size), F32),
            ],
        ),
        out_shape=[
            jax.ShapeDtypeStruct((count, HD, size), LOW),
            jax.ShapeDtypeStruct((count, HD, size), F32),
            jax.ShapeDtypeStruct((count, 1, size), F32),
        ],
        compiler_params=pltpu.CompilerParams(
            dimension_semantics=("arbitrary",), vmem_limit_bytes=32 * 2**20
        ),
        cost_estimate=pl.CostEstimate(
            flops=pairs * size * size * HD * 32,
            bytes_accessed=10 * 2**20,
            transcendentals=pairs * size * size,
        ),
        name="attend_forward",
    )(scalars, own, other)


def attend_backward(scalars, own, other, grad, full, log_total):
    count, _, size = grad.shape
    whole = lambda shape: pl.BlockSpec(shape, lambda i, s: (0,) * len(shape))
    pairs = count * (count + 1) // 2
    out_shape = own.shape
    return pl.pallas_call(
        functools.partial(backward_kernel, size=size, count=count),
        grid_spec=pltpu.PrefetchScalarGridSpec(
            num_scalar_prefetch=1,
            grid=(count,),
            in_specs=[
                whole(own.shape),
                whole(other.shape),
                whole(grad.shape),
                whole(full.shape),
                whole(log_total.shape),
            ],
            out_specs=[whole(out_shape)] * 2,
            scratch_shapes=[
                pltpu.VMEM((count, HD, size), LOW),
                pltpu.VMEM((count, HD, size), LOW),
                pltpu.VMEM((count, size, HD), LOW),
                pltpu.VMEM((count, 1, size), F32),
                pltpu.VMEM((count, HD, size), F32),
                pltpu.VMEM((HD, size), F32),
                pltpu.VMEM((HD, size), F32),
            ],
        ),
        out_shape=[jax.ShapeDtypeStruct(out_shape, LOW)] * 2,
        compiler_params=pltpu.CompilerParams(
            dimension_semantics=("arbitrary",), vmem_limit_bytes=32 * 2**20
        ),
        cost_estimate=pl.CostEstimate(
            flops=pairs * size * size * HD * 42,
            bytes_accessed=16 * 2**20,
            transcendentals=pairs * size * size,
        ),
        name="attend_backward",
    )(scalars, own, other, grad, full, log_total)


def place_rows_kernel(order, *refs):
    pieces, out_ref = refs[:-1], refs[-1]
    size = pieces[0].shape[0]
    for index, piece in enumerate(pieces):
        start = pl.multiple_of(order[index] * size, size)
        out_ref[pl.ds(start, size), :] = piece[...].astype(F32)


def place_rows(order, pieces):
    size, width = pieces[0].shape
    total = size * len(pieces)
    step = 512
    return pl.pallas_call(
        place_rows_kernel,
        grid_spec=pltpu.PrefetchScalarGridSpec(
            num_scalar_prefetch=1,
            grid=(width // step,),
            in_specs=[pl.BlockSpec((size, step), lambda i, s: (0, i)) for _ in pieces],
            out_specs=pl.BlockSpec((total, step), lambda i, s: (0, i)),
        ),
        out_shape=jax.ShapeDtypeStruct((total, width), F32),
        compiler_params=pltpu.CompilerParams(vmem_limit_bytes=24 * 2**20),
        cost_estimate=pl.CostEstimate(
            flops=0, bytes_accessed=total * width * 6, transcendentals=0
        ),
        name="place_rows",
    )(order, *pieces)


def place_columns_kernel(order, gain_ref, gate_w_ref, up_w_ref, *refs):
    count = (len(refs) - 3) // 2
    gates, ups = refs[:count], refs[count : 2 * count]
    gate_ref, up_ref, sum_ref = refs[2 * count :]
    size = gates[0].shape[1]
    gain = gain_ref[...]
    total = jnp.zeros((gate_ref.shape[0], size), F32)
    for index in range(count):
        columns = pl.ds(pl.multiple_of(order[index] * size, size), size)
        gate, up = gates[index][...].astype(F32), ups[index][...].astype(F32)
        total += gate * gate_w_ref[:, columns].astype(F32)
        total += up * up_w_ref[:, columns].astype(F32)
        gate_ref[:, columns] = gate * gain
        up_ref[:, columns] = up * gain

    @pl.when(pl.program_id(0) == 0)
    def _():
        sum_ref[...] = jnp.zeros_like(sum_ref)

    sum_ref[...] += jnp.sum(total, 1, keepdims=True)


def place_columns(order, gain, gate_weight, up_weight, gates, ups, shards):
    rows, width = gate_weight.shape
    span = width // shards
    size = span // len(gates)
    wide = pl.BlockSpec((rows, span), lambda i, s: (0, i))
    thin = pl.BlockSpec((rows, 1), lambda i, s: (0, 0))
    pieces = [pl.BlockSpec((rows, size), lambda i, s: (0, i)) for _ in (*gates, *ups)]
    return pl.pallas_call(
        place_columns_kernel,
        grid_spec=pltpu.PrefetchScalarGridSpec(
            num_scalar_prefetch=1,
            grid=(shards,),
            in_specs=[thin, wide, wide, *pieces],
            out_specs=[wide, wide, thin],
        ),
        out_shape=[
            jax.ShapeDtypeStruct((rows, width), F32),
            jax.ShapeDtypeStruct((rows, width), F32),
            jax.ShapeDtypeStruct((rows, 1), F32),
        ],
        compiler_params=pltpu.CompilerParams(
            dimension_semantics=("arbitrary",), vmem_limit_bytes=24 * 2**20
        ),
        cost_estimate=pl.CostEstimate(
            flops=rows * width * 6, bytes_accessed=rows * width * 16, transcendentals=0
        ),
        name="place_columns",
    )(order, gain, gate_weight, up_weight, *gates, *ups)


def place_heads_kernel(gain_ref, query_w, key_w, value_w, all_ref, query_ref, key_ref, value_ref, sum_ref):
    rows = gain_ref.shape[0]
    wide = query_ref.shape[1] // KVH
    gain = gain_ref[...]
    total = jnp.zeros((rows, 4 * HD), F32)
    pieces = [all_ref[i * rows : (i + 1) * rows, :].astype(F32) for i in range(KVH)]
    for start in range(0, KVH, 2):
        value = jnp.concatenate([piece[:, :wide] for piece in pieces[start : start + 2]], 1)
        columns = slice(start * wide, (start + 2) * wide)
        total += value * query_w[:, columns].astype(F32)
        query_ref[:, columns] = value * gain
    for first, weight, out_ref in ((wide, key_w, key_ref), (wide + HD, value_w, value_ref)):
        for start in range(0, KVH, 4):
            value = jnp.concatenate(
                [piece[:, first : first + HD] for piece in pieces[start : start + 4]], 1
            )
            columns = slice(start * HD, (start + 4) * HD)
            total += value * weight[:, columns].astype(F32)
            out_ref[:, columns] = value * gain
    sum_ref[...] = jnp.sum(total, 1, keepdims=True)


def place_heads(gain, query_weight, key_weight, value_weight, pieces):
    weights = (query_weight, key_weight, value_weight)
    rows = gain.shape[0]
    return pl.pallas_call(
        place_heads_kernel,
        out_shape=[jax.ShapeDtypeStruct(weight.shape, F32) for weight in weights]
        + [jax.ShapeDtypeStruct((rows, 1), F32)],
        compiler_params=pltpu.CompilerParams(vmem_limit_bytes=32 * 2**20),
        cost_estimate=pl.CostEstimate(
            flops=rows * 3072 * 4, bytes_accessed=rows * 3072 * 8, transcendentals=0
        ),
        name="place_heads",
    )(gain, *weights, pieces)


def merge_kernel(scalars, kept_ref, came_ref, cosine_ref, sine_ref, out_ref, split_ref):
    lead = scalars[0] == 0
    lines, _, size = split_ref.shape
    for line in range(lines):
        columns = slice(line * size, (line + 1) * size)
        kept = kept_ref[:, columns].astype(F32)
        came = came_ref[:, columns].astype(F32)
        cosine, sine = cosine_ref[:, columns], sine_ref[:, columns]
        joint = kept[HD:] + came[HD:]
        first = jnp.where(lead, kept[:HD], came[:HD])
        second = jnp.where(lead, came[:HD], kept[:HD])
        turned = []
        for value in (first, second, joint[:HD]):
            low, high = value[: HD // 2], value[HD // 2 :]
            turned.append(low * cosine + high * sine)
            turned.append(high * cosine - low * sine)
        turned.append(joint[HD:])
        result = jnp.concatenate([part.astype(LOW) for part in turned], 0)
        out_ref[:, columns] = result
        split_ref[line] = result


def merge(scalars, kept, came, cosine, sine, lines):
    tokens = kept.shape[1]
    whole = lambda value: pl.BlockSpec(value.shape, lambda i, s: (0,) * len(value.shape))
    outs = [
        jax.ShapeDtypeStruct((4 * HD, tokens), LOW),
        jax.ShapeDtypeStruct((lines, 4 * HD, tokens // lines), LOW),
    ]
    return pl.pallas_call(
        merge_kernel,
        grid_spec=pltpu.PrefetchScalarGridSpec(
            num_scalar_prefetch=1,
            grid=(1,),
            in_specs=[whole(value) for value in (kept, came, cosine, sine)],
            out_specs=[whole(value) for value in outs],
        ),
        out_shape=outs,
        compiler_params=pltpu.CompilerParams(vmem_limit_bytes=24 * 2**20),
        cost_estimate=pl.CostEstimate(
            flops=tokens * HD * 24, bytes_accessed=tokens * HD * 30, transcendentals=0
        ),
        name="merge",
    )(scalars, kept, came, cosine, sine)


def pack_kernel(scalars, gain_ref, query_ref, key_ref, value_ref, *outs):
    core = scalars[3]
    gain = gain_ref[...]
    wide = query_ref.shape[1] // KVH
    span = wide + 2 * HD
    for which in range(2):

        @pl.when(core == which)
        def _():
            for line in range(KVH // 2):
                head = 2 * line + which
                value = jnp.concatenate(
                    [
                        query_ref[:, head * wide : (head + 1) * wide].astype(F32),
                        key_ref[:, head * HD : (head + 1) * HD].astype(F32),
                        value_ref[:, head * HD : (head + 1) * HD].astype(F32),
                    ],
                    1,
                )
                place = (line % 2) * span
                outs[line // 2][:, place : place + span] = (value * gain).astype(LOW)


def pack(scalars, gain, query_weight, key_weight, value_weight):
    rows, width = query_weight.shape
    whole = lambda value: pl.BlockSpec(value.shape, lambda i, s: (0, 0))
    weights = (gain, query_weight, key_weight, value_weight)
    outs = [jax.ShapeDtypeStruct((rows, width // 2), LOW)] * 2
    return pl.pallas_call(
        pack_kernel,
        grid_spec=pltpu.PrefetchScalarGridSpec(
            num_scalar_prefetch=1,
            grid=(1,),
            in_specs=[whole(value) for value in weights],
            out_specs=[whole(value) for value in outs],
        ),
        out_shape=outs,
        compiler_params=pltpu.CompilerParams(vmem_limit_bytes=24 * 2**20),
        cost_estimate=pl.CostEstimate(
            flops=rows * width, bytes_accessed=rows * width * 6, transcendentals=0
        ),
        name="pack",
    )(scalars, *weights)


def spread_kernel(scalars, lin_ref, cosine_ref, sine_ref, own_ref, leaving_ref):
    cosine, sine = cosine_ref[...], sine_ref[...]

    def turn(start, factor):
        low = lin_ref[start : start + HD // 2, :]
        high = lin_ref[start + HD // 2 : start + HD, :]
        turned = ((low * cosine - high * sine) * factor, (high * cosine + low * sine) * factor)
        return jnp.concatenate([part.astype(LOW) for part in turned], 0)

    lead = scalars[0] == 0
    first, second = turn(0, HD**-0.5 / LN2), turn(HD, HD**-0.5 / LN2)

    @pl.when(lead)
    def _():
        own_ref[0:HD] = first
        leaving_ref[0:HD] = second

    @pl.when(jnp.logical_not(lead))
    def _():
        own_ref[0:HD] = second
        leaving_ref[0:HD] = first

    key = turn(2 * HD, 1.0)
    value = lin_ref[3 * HD : 4 * HD].astype(LOW)
    for ref in (own_ref, leaving_ref):
        ref[HD : 2 * HD] = key
        ref[2 * HD : 3 * HD] = value


def spread(scalars, lin, cosine, sine):
    tokens = lin.shape[1]
    step = 512
    column = lambda rows: pl.BlockSpec((rows, step), lambda i, s: (0, i))
    return pl.pallas_call(
        spread_kernel,
        grid_spec=pltpu.PrefetchScalarGridSpec(
            num_scalar_prefetch=1,
            grid=(tokens // step,),
            in_specs=[column(4 * HD), column(HD // 2), column(HD // 2)],
            out_specs=[column(3 * HD)] * 2,
        ),
        out_shape=[jax.ShapeDtypeStruct((3 * HD, tokens), LOW)] * 2,
        compiler_params=pltpu.CompilerParams(vmem_limit_bytes=24 * 2**20),
        cost_estimate=pl.CostEstimate(
            flops=tokens * HD * 24, bytes_accessed=tokens * HD * 36, transcendentals=0
        ),
        name="spread",
    )(scalars, lin, cosine, sine)


def swap(value, axis):
    return lax.ppermute(value, axis, [(0, 1), (1, 0)])


def swap_near(value):
    return lax.ppermute(value, "z", [(0, 1), (1, 0), (2, 3), (3, 2)])


def swap_far(value):
    return lax.ppermute(value, "z", [(0, 2), (2, 0), (1, 3), (3, 1)])


def tie(*values):
    return lax.optimization_barrier(values)


def in_order(place, own, other):
    return (jnp.where(place == 0, own, other), jnp.where(place == 0, other, own))


def both(place, own, other):
    return jnp.concatenate(in_order(place, own, other), 0)


def spread_out(value, first, second):
    other = swap(value, first)
    pair = jnp.stack(in_order(lax.axis_index(first), value, other))
    return pair, swap(pair, second)


def placed(pair, other, second):
    pairs = in_order(lax.axis_index(second), pair, other)
    grid = jnp.stack(pairs, 0 if second == "y" else 1)
    return grid.reshape(-1, *grid.shape[3:])


def pick(array, axis, at):
    return lax.dynamic_index_in_dim(array, at, axis, keepdims=False)


def halve(value, axis, along=0):
    at = lax.axis_index(axis)
    return pick(value, along, at), swap(pick(value, along, 1 - at), axis)


def halve_x(value):
    return halve(value.reshape(2, 2, -1, value.shape[-1]), "x", 1)


def halve_y(value):
    return halve(value.reshape(2, 2, -1, value.shape[-1]), "y", 0)


def fast_body(
    tokens,
    positions,
    first_gain,
    query_weight,
    key_weight,
    value_weight,
    output_weight,
    second_gain,
    gate_weight,
    up_weight,
    down_weight,
    cotangent,
):
    seq = ("z", "c")
    fsdp = ("y", "x")
    z, core, half = lax.axis_index("z"), lax.axis_index("c"), lax.axis_index("x")
    near = z % 2
    lines = lax.axis_size("z")
    seq_count = 2 * lines
    shards = lax.axis_size("y") * 2
    spot = z * 2 + core
    quarter = near * 2 + core
    rows = tokens[0]
    count, width = rows.shape
    chip_count = 2 * count
    half_len = count * seq_count
    seq_len = 2 * half_len

    begins = jnp.where(
        (spot == 0) & (half == 0),
        count - 1 - positions[0, count - 1],
        half * half_len + spot * count - positions[0, 0],
    )
    ends = begins + (seq_len - count)
    scalars = jnp.stack([half, begins, ends, core]).astype(jnp.int32)

    gain_one = first_gain.astype(F32)[:, None]
    gain_two = second_gain.astype(F32)[:, None]

    def row_scale(value):
        return lax.rsqrt(jnp.mean(value * value, -1, keepdims=True) + EPS)

    take = functools.partial(lax.dynamic_slice_in_dim, axis=1)
    take_rows = functools.partial(lax.dynamic_slice_in_dim, axis=0)
    gather = lambda value, axes: lax.all_gather(value, axes, axis=0, tiled=True)
    own_rows = rows.astype(F32)
    own_unit_scale = row_scale(own_rows)
    own_unit = own_rows * own_unit_scale
    units = gather(own_unit.astype(LOW), seq)
    wide = QH // KVH * HD
    qkv_shard = (
        jnp.concatenate(
            [
                take(query_weight, spot * wide, wide),
                take(key_weight, spot * HD, HD),
                take(value_weight, spot * HD, HD),
            ],
            1,
        ).astype(F32)
        * gain_one
    ).astype(LOW)
    out_rows = output_weight.shape[0] // 2
    out_shard = take_rows(output_weight, core * out_rows, out_rows)
    piece = down_weight.shape[0] // 4
    down_shard = take_rows(down_weight, quarter * piece, piece)
    gate_shard, up_shard = (
        (
            jnp.concatenate(
                [
                    take(weight, shard * 4 * piece + quarter * piece, piece)
                    for shard in range(shards)
                ],
                1,
            ).astype(F32)
            * gain_two
        ).astype(LOW)
        for weight in (gate_weight, up_weight)
    )
    side = lax.axis_index("y")
    qkv_pair = jnp.stack(in_order(half, qkv_shard, swap(qkv_shard, "x")))
    gate_pair = jnp.stack(in_order(half, gate_shard, swap(gate_shard, "x")))
    up_pair = jnp.stack(in_order(side, up_shard, swap(up_shard, "y")))
    qkv_pair, gate_pair, up_pair = tie(qkv_pair, gate_pair, up_pair)
    qkv_w = placed(qkv_pair, swap(qkv_pair, "y"), "y")
    gate_pair, up_pair = (gate_pair, swap(gate_pair, "y")), (up_pair, swap(up_pair, "x"))

    place = half * half_len + jnp.arange(half_len, dtype=jnp.int32)
    start = jnp.where(place >= ends, ends, jnp.where(place >= begins, begins, 0))
    freq = THETA ** (-(jnp.arange(HD // 2, dtype=F32) * 2.0 / HD))
    angle = freq[:, None] * (place - start).astype(F32)[None, :]
    cosine, sine = jnp.cos(angle), jnp.sin(angle)
    chip_rows = both(core, rows, swap(rows, "c"))
    units, own_cot, chip_rows = tie(units, cotangent[0], chip_rows)
    own, leaving = spread(scalars, contract(qkv_w, units, 0, 1), cosine, sine)

    near_cot = swap_near(own_cot)
    other, out_shard, down_shard, near_cot, chip_cot, gate_pair, up_pair = tie(
        swap(leaving, "x"),
        out_shard,
        down_shard,
        near_cot,
        both(core, own_cot, swap(own_cot, "c")),
        gate_pair,
        up_pair,
    )
    out_w = gather(out_shard, fsdp)
    down_w = gather(down_shard, fsdp)
    near_other = swap(near_cot, "c")
    head_low, head_full, log_total = attend_forward(scalars, own, other, chip_count)
    exchange = lambda value: lax.all_to_all(
        value, ("z", "x"), split_axis=0, concat_axis=0, tiled=True
    )
    head_low, near_other = tie(head_low, near_other)
    lead_shard, tail_shard = pack(scalars, gain_one, query_weight, key_weight, value_weight)
    heads, gate_w, up_w, near_cot, lead_shard = tie(
        exchange(head_low),
        placed(*gate_pair, "y"),
        placed(*up_pair, "x"),
        jnp.concatenate([near_cot, near_other], 0),
        lead_shard,
    )
    lead_w = gather(lead_shard, fsdp)
    heads = heads.reshape(QH // 2 * HD, chip_count)

    mine_of = lambda value: take_rows(value, core * count, count)
    theirs_of = lambda value: take_rows(value, (1 - core) * count, count)
    branch = contract(heads, out_w, 0, 0).astype(LOW)
    middle = chip_rows.astype(F32) + (branch.astype(F32) + swap(branch, "c").astype(F32))
    middle_scale = row_scale(middle)
    chip_unit = middle * middle_scale
    own_middle, own_scale, own_middle_unit = (
        mine_of(middle),
        mine_of(middle_scale),
        mine_of(chip_unit),
    )
    chip_unit = chip_unit.astype(LOW)
    near_unit = swap_near(mine_of(chip_unit))

    def feed(unit):
        gate, upper = contract(unit, gate_w, 1, 0), contract(unit, up_w, 1, 0)
        sigma = jax.nn.sigmoid(gate)
        silu = gate * sigma
        return (silu * upper).astype(LOW), (gate, upper, sigma, silu)

    def feed_back(cot, kept):
        gate, upper, sigma, silu = kept
        grad_hidden = contract(cot, down_w, 1, 1)
        gate_low = (grad_hidden * upper * sigma * (1.0 + gate * (1.0 - sigma))).astype(LOW)
        upper_low = (grad_hidden * silu).astype(LOW)
        part = contract(gate_low, gate_w, 1, 1) + contract(upper_low, up_w, 1, 1)
        return gate_low, upper_low, part

    def chip_sum(chip_part, near_part):
        near_sum = near_part[:count].astype(F32) + swap(near_part[count:].astype(LOW), "c")
        own_sum = mine_of(chip_part).astype(F32) + swap(theirs_of(chip_part).astype(LOW), "c")
        return own_sum, near_sum.astype(LOW)

    stack = lambda first, second: jnp.concatenate([first, second], 0)
    scatter = lambda value: lax.psum_scatter(value, fsdp, scatter_dimension=0, tiled=True)
    chip_hidden, chip_kept = feed(chip_unit)
    near_unit, chip_hidden = tie(near_unit, chip_hidden)
    near_unit = jnp.concatenate([near_unit, swap(near_unit, "c")], 0)
    near_hidden, near_kept = feed(near_unit)
    down_part = contract(
        stack(chip_hidden, near_hidden), stack(chip_cot, near_cot), 0, 0
    ).astype(LOW)
    near_cot, down_part = tie(near_cot, down_part)
    near_gate, near_upper, near_part = feed_back(near_cot, near_kept)
    chip_gate, chip_upper, chip_part = feed_back(chip_cot, chip_kept)
    grad_two, near_sum = chip_sum(chip_part, near_part)

    def four(value, near_value):
        return value, swap(value, "c"), near_value, swap(near_value, "c")

    def halves_first(value):
        cut = value.shape[-1] // 2
        return halve_x(value[:, :cut]), halve_y(value[:, cut:])

    def halves_second(firsts):
        return halve(sum(firsts[0]), "y"), halve(sum(firsts[1]), "x")

    def halves_end(seconds):
        return jnp.concatenate([sum(seconds[0]), sum(seconds[1])], 1)

    down_first = halves_first(down_part)
    near_sum, near_gate, near_upper, chip_part = tie(
        near_sum, near_gate, near_upper, chip_part
    )
    grad_came = swap_near(near_sum)
    all_units = stack(chip_unit, near_unit)
    gate_part = contract(all_units, stack(chip_gate, near_gate), 0, 0).astype(LOW)
    up_part = contract(all_units, stack(chip_upper, near_upper), 0, 0).astype(LOW)
    feed_own, feed_near = chip_sum(
        contract(chip_hidden, down_w, 1, 0), contract(near_hidden, down_w, 1, 0)
    )
    gate_part, up_part, down_first, grad_came, feed_near = tie(
        gate_part, up_part, down_first, grad_came, feed_near
    )
    feed_near = swap_near(feed_near)
    down_second = halves_second(down_first)
    grad_two = grad_two + grad_came.astype(F32)
    grad_middle = own_cot.astype(F32) + own_scale * (
        grad_two - own_middle_unit * jnp.mean(grad_two * own_middle_unit, -1, keepdims=True)
    )
    own_branch, lead_w, down_second, gate_part, up_part = tie(
        grad_middle.astype(LOW), lead_w, down_second, gate_part, up_part
    )
    gate_grad, up_grad = scatter(gate_part), scatter(up_part)
    down_grad = halves_end(down_second)
    down_far = swap_far(down_grad)
    grad_branch = both(core, own_branch, swap(own_branch, "c"))
    grad_heads = contract(out_w, grad_branch, 1, 1).astype(LOW)
    grad_heads, grad_branch, down_far = tie(grad_heads, grad_branch, down_far)
    down_sum = down_grad + down_far
    output_part = contract(heads, grad_branch, 1, 0).astype(LOW)
    output_grad = scatter(output_part)
    grad_head, output_part, gate_grad, down_sum = tie(
        exchange(grad_heads.reshape(2 * lines, HD, chip_count)), output_part, gate_grad, down_sum
    )
    down_near = swap_near(down_sum)

    gate_far = swap_far(gate_grad)
    kept, leaving = attend_backward(scalars, own, other, grad_head, head_full, log_total)
    kept, leaving, gate_far, down_near, tail_shard, feed_near = tie(
        kept, leaving, gate_far, down_near, tail_shard, feed_near
    )
    tail_w = gather(tail_shard, fsdp)

    up_far = swap_far(up_grad)
    gate_sum = gate_grad + gate_far
    gate_near = swap_near(gate_sum)
    block_output = (own_middle + feed_own + feed_near.astype(F32)).astype(LOW)[None]
    output_came = swap_near(output_grad)
    came, up_far, gate_near, block_output, output_grad, output_came = tie(
        swap(leaving, "x"), up_far, gate_near, block_output, output_grad, output_came
    )

    qkv_low, by_line = merge(scalars, kept, came, cosine, sine, lines)
    token_grads = lax.all_to_all(by_line, "z", split_axis=0, concat_axis=0, tiled=True)
    qkv_part = contract(units, qkv_low, 0, 1).astype(LOW).reshape(shards, 2, -1, 4 * HD)
    qkv_first = halve_x(qkv_part[:, 0]), halve_y(qkv_part[:, 1])
    qkv_second = halves_second(qkv_first)
    qkv_grad = jnp.concatenate([sum(qkv_second[0]), sum(qkv_second[1])], 0)
    up_sum = up_grad + up_far
    up_near = swap_near(up_sum)
    down_pieces = four(down_sum, down_near)
    token_grads, qkv_grad, up_near, down_pieces, output_came = tie(
        token_grads, qkv_grad, up_near, down_pieces, output_came
    )
    all_qkv = gather(qkv_grad, seq)
    output_sum = output_grad + output_came
    output_far = swap_far(output_sum)

    token_grads = token_grads.reshape(-1, chip_count)
    split = lead_w.shape[1]
    grad_one = contract(token_grads[:split], lead_w, 0, 1) + contract(
        token_grads[split:], tail_w, 0, 1
    )
    grad_one = mine_of(grad_one) + swap(theirs_of(grad_one).astype(LOW), "c").astype(F32)
    grad_rows = own_unit_scale * (
        grad_one - own_unit * jnp.mean(grad_one * own_unit, -1, keepdims=True)
    )
    input_grad = (grad_middle + grad_rows).astype(LOW)[None]

    order = jnp.stack([quarter, quarter ^ 1, quarter ^ 2, quarter ^ 3]).astype(jnp.int32)
    core_order = jnp.stack([core, 1 - core]).astype(jnp.int32)
    down_total = place_rows(order, down_pieces)
    gate_total, up_total, second_gain_grad = place_columns(
        order, gain_two, gate_weight, up_weight, four(gate_sum, gate_near), four(up_sum, up_near), shards
    )
    output_far, second_gain_grad, all_qkv = tie(output_far, second_gain_grad, all_qkv)
    output_own = output_sum + output_far
    output_total = place_rows(core_order, (output_own, swap(output_own, "c")))
    query_grad, key_grad, value_grad, first_gain_grad = place_heads(
        gain_one, query_weight, key_weight, value_weight, all_qkv
    )
    return (
        block_output,
        input_grad,
        first_gain_grad[:, 0],
        query_grad,
        key_grad,
        value_grad,
        output_total,
        second_gain_grad[:, 0],
        gate_total,
        up_total,
        down_total,
    )


def fast_solution(mesh):
    seq_count, shard_count = mesh.devices.shape
    fine = Mesh(
        mesh.devices.reshape(seq_count // 2, 2, shard_count // 2, 2), ("z", "c", "y", "x")
    )
    seq, fsdp = ("z", "c"), ("y", "x")
    matrix = P(fsdp, None)
    return jax.shard_map(
        fast_body,
        mesh=fine,
        in_specs=(
            P(fsdp, seq, None),
            P(fsdp, seq),
            P(fsdp),
            matrix,
            matrix,
            matrix,
            matrix,
            P(fsdp),
            matrix,
            matrix,
            matrix,
            P(fsdp, seq, None),
        ),
        out_specs=(
            P(fsdp, seq, None),
            P(fsdp, seq, None),
            P(fsdp),
            matrix,
            matrix,
            matrix,
            matrix,
            P(fsdp),
            matrix,
            matrix,
            matrix,
        ),
        check_vma=False,
    )


def solution(mesh):
    shape = dict(mesh.shape)
    if shape["seq"] == KVH and shape["fsdp"] == 4:
        return fast_solution(mesh)
    return plain_solution(mesh)


def shifted(value, axis, steps):
    count = lax.axis_size(axis)
    first, last = (max(0, -steps), min(count, count - steps))
    return lax.ppermute(value, axis, [(source, source + steps) for source in range(first, last)])


def rope_tables(position_rows):
    freq = THETA ** (-(jnp.arange(HD // 2, dtype=jnp.float32) * 2.0 / HD))
    angle = position_rows.astype(jnp.float32)[:, None] * freq[None, :]
    cosine = jnp.cos(angle)
    sine = jnp.sin(angle)
    return (jnp.concatenate([cosine, cosine], -1), jnp.concatenate([sine, sine], -1))


def rotate(values, cosine, sine):
    half = HD // 2
    turned = jnp.concatenate([-values[..., half:], values[..., :half]], -1)
    return values * cosine[:, None, :] + turned * sine[:, None, :]


def rotate_back(grads, cosine, sine):
    half = HD // 2
    scaled = grads * sine[:, None, :]
    turned = jnp.concatenate([scaled[..., half:], -scaled[..., :half]], -1)
    return grads * cosine[:, None, :] + turned


def norm_forward(rows, gain):
    scale = lax.rsqrt(jnp.mean(rows * rows, -1, keepdims=True) + EPS)
    unit = rows * scale
    return (unit * gain, unit, scale)


def norm_backward(grad_out, unit, scale, gain):
    grad_unit = grad_out * gain
    gain_grad = jnp.sum(grad_out * unit, 0)
    grad_rows = scale * (grad_unit - unit * jnp.mean(grad_unit * unit, -1, keepdims=True))
    return (grad_rows, gain_grad)


def plain_body(
    tokens,
    positions,
    first_gain,
    query_weight,
    key_weight,
    value_weight,
    output_weight,
    second_gain,
    gate_weight,
    up_weight,
    down_weight,
    cotangent,
):
    seq_count = lax.axis_size("seq")
    local_rows = tokens[0]
    token_count = local_rows.shape[0]
    half_len = token_count * seq_count
    rows_float = local_rows.astype(jnp.float32)
    gain_one, wq_full, wk_full, wv_full, wo_full = (
        lax.all_gather(first_gain, "fsdp", axis=0, tiled=True),
        lax.all_gather(query_weight, "fsdp", axis=0, tiled=True),
        lax.all_gather(key_weight, "fsdp", axis=0, tiled=True),
        lax.all_gather(value_weight, "fsdp", axis=0, tiled=True),
        lax.all_gather(output_weight, "fsdp", axis=0, tiled=True),
    )
    gain_one = gain_one.astype(jnp.float32)
    normed_one, unit_one, scale_one = norm_forward(rows_float, gain_one)
    normed_low = normed_one.astype(jnp.bfloat16)
    cosine, sine = rope_tables(positions[0])
    query_lin = jnp.dot(normed_low, wq_full, preferred_element_type=jnp.float32).reshape(
        token_count, QH, HD
    )
    key_lin = jnp.dot(normed_low, wk_full, preferred_element_type=jnp.float32).reshape(
        token_count, KVH, HD
    )
    value_lin = jnp.dot(normed_low, wv_full, preferred_element_type=jnp.float32).reshape(
        token_count, KVH, HD
    )
    query_rows = rotate(query_lin, cosine, sine).astype(jnp.bfloat16)
    key_rows = rotate(key_lin, cosine, sine).astype(jnp.bfloat16)
    value_rows = value_lin.astype(jnp.bfloat16)
    repeat = max(1, seq_count // KVH)
    if repeat > 1:
        key_rows = jnp.repeat(key_rows, repeat, axis=1)
        value_rows = jnp.repeat(value_rows, repeat, axis=1)
    query_heads, key_heads, value_heads = (
        lax.all_to_all(query_rows, "seq", split_axis=1, concat_axis=0, tiled=True),
        lax.all_to_all(key_rows, "seq", split_axis=1, concat_axis=0, tiled=True),
        lax.all_to_all(value_rows, "seq", split_axis=1, concat_axis=0, tiled=True),
    )
    head_count = query_heads.shape[1]
    pair_count = key_heads.shape[1]
    group = head_count // pair_count
    half_positions = lax.all_gather(positions[0], "seq", axis=0, tiled=True)
    key_prior, value_prior = shifted((key_heads, value_heads), "fsdp", 1)
    key_all = jnp.concatenate([key_prior, key_heads], 0)
    value_all = jnp.concatenate([value_prior, value_heads], 0)
    half_index = lax.axis_index("fsdp") % 2
    key_index = (half_index - 1) * half_len + jnp.arange(2 * half_len, dtype=jnp.int32)
    row_index = half_index * half_len + jnp.arange(half_len, dtype=jnp.int32)
    row_start = row_index - half_positions
    block = min(512, half_len)
    count = half_len // block
    factor = HD ** (-0.5)
    query_blocks = query_heads.reshape(count, block, pair_count, group, HD)
    index_blocks = row_index.reshape(count, block)
    start_blocks = row_start.reshape(count, block)

    def block_scores(query_block, index_block, start_block):
        scores = (
            jnp.einsum("bkgd,tkd->kgbt", query_block, key_all, preferred_element_type=jnp.float32)
            * factor
        )
        visible = (key_index[None, :] >= start_block[:, None]) & (
            key_index[None, :] <= index_block[:, None]
        )
        return jnp.where(visible, scores, -1e30)

    def forward_block(items):
        query_block, index_block, start_block = items
        scores = block_scores(query_block, index_block, start_block)
        top = jnp.max(scores, -1, keepdims=True)
        expo = jnp.exp(scores - top)
        total = jnp.sum(expo, -1, keepdims=True)
        probs_low = (expo / total).astype(jnp.bfloat16)
        mixed = jnp.einsum(
            "kgbt,tkd->bkgd", probs_low, value_all, preferred_element_type=jnp.float32
        )
        return (mixed.reshape(block, head_count, HD).astype(jnp.bfloat16), top + jnp.log(total))

    head_blocks, log_totals = lax.map(forward_block, (query_blocks, index_blocks, start_blocks))
    head_out = head_blocks.reshape(half_len, head_count, HD)
    token_heads = lax.all_to_all(head_out, "seq", split_axis=0, concat_axis=1, tiled=True)
    heads_flat = token_heads.reshape(token_count, QH * HD)
    middle = rows_float + jnp.dot(heads_flat, wo_full, preferred_element_type=jnp.float32)
    gain_two, wg_full, wu_full, wd_full = (
        lax.all_gather(second_gain, "fsdp", axis=0, tiled=True),
        lax.all_gather(gate_weight, "fsdp", axis=0, tiled=True),
        lax.all_gather(up_weight, "fsdp", axis=0, tiled=True),
        lax.all_gather(down_weight, "fsdp", axis=0, tiled=True),
    )
    gain_two = gain_two.astype(jnp.float32)
    normed_two, unit_two, scale_two = norm_forward(middle, gain_two)
    normed_two_low = normed_two.astype(jnp.bfloat16)
    gate = jnp.dot(normed_two_low, wg_full, preferred_element_type=jnp.float32)
    upper = jnp.dot(normed_two_low, wu_full, preferred_element_type=jnp.float32)
    hidden = (jax.nn.silu(gate) * upper).astype(jnp.bfloat16)
    result = middle + jnp.dot(hidden, wd_full, preferred_element_type=jnp.float32)
    block_output = result.astype(jnp.bfloat16)[None]
    grad_low = cotangent[0]
    grad_rows = grad_low.astype(jnp.float32)
    down_grad = jnp.einsum("tf,td->fd", hidden, grad_low, preferred_element_type=jnp.float32)
    grad_hidden = jnp.einsum("td,fd->tf", grad_low, wd_full, preferred_element_type=jnp.float32)
    sigma = jax.nn.sigmoid(gate)
    gate_low = (grad_hidden * upper * sigma * (1.0 + gate * (1.0 - sigma))).astype(jnp.bfloat16)
    upper_low = (grad_hidden * gate * sigma).astype(jnp.bfloat16)
    gate_grad = jnp.einsum(
        "td,tf->df", normed_two_low, gate_low, preferred_element_type=jnp.float32
    )
    up_grad = jnp.einsum("td,tf->df", normed_two_low, upper_low, preferred_element_type=jnp.float32)
    grad_normed_two = jnp.einsum(
        "tf,df->td", gate_low, wg_full, preferred_element_type=jnp.float32
    ) + jnp.einsum("tf,df->td", upper_low, wu_full, preferred_element_type=jnp.float32)
    grad_middle_norm, second_gain_grad = norm_backward(
        grad_normed_two, unit_two, scale_two, gain_two
    )
    grad_middle = grad_rows + grad_middle_norm
    grad_branch = grad_middle.astype(jnp.bfloat16)
    output_grad = jnp.einsum(
        "tc,td->cd", heads_flat, grad_branch, preferred_element_type=jnp.float32
    )
    grad_heads = (
        jnp.einsum("td,cd->tc", grad_branch, wo_full, preferred_element_type=jnp.float32)
        .astype(jnp.bfloat16)
        .reshape(token_count, QH, HD)
    )
    grad_head_rows = lax.all_to_all(grad_heads, "seq", split_axis=1, concat_axis=0, tiled=True)
    grad_blocks = grad_head_rows.reshape(count, block, pair_count, group, HD)

    def backward_block(carry, items):
        key_acc, value_acc = carry
        query_block, index_block, start_block, grad_block, log_block = items
        scores = block_scores(query_block, index_block, start_block)
        probs = jnp.exp(scores - log_block)
        probs_low = probs.astype(jnp.bfloat16)
        grad_probs = jnp.einsum(
            "bkgd,tkd->kgbt", grad_block, value_all, preferred_element_type=jnp.float32
        )
        grad_scores = (
            probs * (grad_probs - jnp.sum(probs * grad_probs, -1, keepdims=True))
        ).astype(jnp.bfloat16)
        query_grad_block = (
            jnp.einsum("kgbt,tkd->bkgd", grad_scores, key_all, preferred_element_type=jnp.float32)
            * factor
        )
        key_acc = (
            key_acc
            + jnp.einsum(
                "kgbt,bkgd->tkd", grad_scores, query_block, preferred_element_type=jnp.float32
            )
            * factor
        )
        value_acc = value_acc + jnp.einsum(
            "kgbt,bkgd->tkd", probs_low, grad_block, preferred_element_type=jnp.float32
        )
        return ((key_acc, value_acc), query_grad_block.reshape(block, head_count, HD))

    empty = jnp.zeros((2 * half_len, pair_count, HD), jnp.float32)
    (key_acc, value_acc), query_grad_blocks = lax.scan(
        backward_block,
        (empty, empty),
        (query_blocks, index_blocks, start_blocks, grad_blocks, log_totals),
    )
    key_back, value_back = (
        shifted(key_acc[:half_len].astype(jnp.bfloat16), "fsdp", -1).astype(jnp.float32),
        shifted(value_acc[:half_len].astype(jnp.bfloat16), "fsdp", -1).astype(jnp.float32),
    )
    key_local = key_acc[half_len:] + key_back
    value_local = value_acc[half_len:] + value_back
    query_grad_heads = query_grad_blocks.reshape(half_len, head_count, HD)
    grad_query_tok, grad_key_tok, grad_value_tok = (
        lax.all_to_all(
            query_grad_heads.astype(jnp.bfloat16), "seq", split_axis=0, concat_axis=1, tiled=True
        ).astype(query_grad_heads.dtype),
        lax.all_to_all(
            key_local.astype(jnp.bfloat16), "seq", split_axis=0, concat_axis=1, tiled=True
        ).astype(key_local.dtype),
        lax.all_to_all(
            value_local.astype(jnp.bfloat16), "seq", split_axis=0, concat_axis=1, tiled=True
        ).astype(value_local.dtype),
    )
    if repeat > 1:
        grad_key_tok = grad_key_tok.reshape(token_count, KVH, repeat, HD).sum(2)
        grad_value_tok = grad_value_tok.reshape(token_count, KVH, repeat, HD).sum(2)
    query_lin_grad = (
        rotate_back(grad_query_tok, cosine, sine).astype(jnp.bfloat16).reshape(token_count, QH * HD)
    )
    key_lin_grad = (
        rotate_back(grad_key_tok, cosine, sine).astype(jnp.bfloat16).reshape(token_count, KVH * HD)
    )
    value_lin_grad = grad_value_tok.astype(jnp.bfloat16).reshape(token_count, KVH * HD)
    query_grad = jnp.einsum(
        "td,tc->dc", normed_low, query_lin_grad, preferred_element_type=jnp.float32
    )
    key_grad = jnp.einsum("td,tc->dc", normed_low, key_lin_grad, preferred_element_type=jnp.float32)
    value_grad = jnp.einsum(
        "td,tc->dc", normed_low, value_lin_grad, preferred_element_type=jnp.float32
    )
    grad_normed_one = jnp.einsum(
        "tc,dc->td", query_lin_grad, wq_full, preferred_element_type=jnp.float32
    )
    grad_normed_one = grad_normed_one + jnp.einsum(
        "tc,dc->td", key_lin_grad, wk_full, preferred_element_type=jnp.float32
    )
    grad_normed_one = grad_normed_one + jnp.einsum(
        "tc,dc->td", value_lin_grad, wv_full, preferred_element_type=jnp.float32
    )
    grad_rows_one, first_gain_grad = norm_backward(grad_normed_one, unit_one, scale_one, gain_one)
    input_grad = (grad_middle + grad_rows_one).astype(jnp.bfloat16)[None]
    pieces = (
        lax.psum_scatter(
            first_gain_grad.astype(jnp.bfloat16), "fsdp", scatter_dimension=0, tiled=True
        ).astype(jnp.float32),
        lax.psum_scatter(
            query_grad.astype(jnp.bfloat16), "fsdp", scatter_dimension=0, tiled=True
        ).astype(jnp.float32),
        lax.psum_scatter(
            key_grad.astype(jnp.bfloat16), "fsdp", scatter_dimension=0, tiled=True
        ).astype(jnp.float32),
        lax.psum_scatter(
            value_grad.astype(jnp.bfloat16), "fsdp", scatter_dimension=0, tiled=True
        ).astype(jnp.float32),
        lax.psum_scatter(
            output_grad.astype(jnp.bfloat16), "fsdp", scatter_dimension=0, tiled=True
        ).astype(jnp.float32),
        lax.psum_scatter(
            second_gain_grad.astype(jnp.bfloat16), "fsdp", scatter_dimension=0, tiled=True
        ).astype(jnp.float32),
        lax.psum_scatter(
            gate_grad.astype(jnp.bfloat16), "fsdp", scatter_dimension=0, tiled=True
        ).astype(jnp.float32),
        lax.psum_scatter(
            up_grad.astype(jnp.bfloat16), "fsdp", scatter_dimension=0, tiled=True
        ).astype(jnp.float32),
        lax.psum_scatter(
            down_grad.astype(jnp.bfloat16), "fsdp", scatter_dimension=0, tiled=True
        ).astype(jnp.float32),
    )
    shares = (
        lax.psum(pieces[0].astype(jnp.bfloat16), "seq").astype(jnp.float32),
        lax.psum(pieces[1].astype(jnp.bfloat16), "seq").astype(jnp.float32),
        lax.psum(pieces[2].astype(jnp.bfloat16), "seq").astype(jnp.float32),
        lax.psum(pieces[3].astype(jnp.bfloat16), "seq").astype(jnp.float32),
        lax.psum(pieces[4].astype(jnp.bfloat16), "seq").astype(jnp.float32),
        lax.psum(pieces[5].astype(jnp.bfloat16), "seq").astype(jnp.float32),
        lax.psum(pieces[6].astype(jnp.bfloat16), "seq").astype(jnp.float32),
        lax.psum(pieces[7].astype(jnp.bfloat16), "seq").astype(jnp.float32),
        lax.psum(pieces[8].astype(jnp.bfloat16), "seq").astype(jnp.float32),
    )
    return (
        block_output,
        input_grad,
        shares[0],
        shares[1],
        shares[2],
        shares[3],
        shares[4],
        shares[5],
        shares[6],
        shares[7],
        shares[8],
    )


def plain_solution(mesh):
    placed = (
        P("fsdp", "seq", None),
        P("fsdp", "seq"),
        P("fsdp"),
        P("fsdp", None),
        P("fsdp", None),
        P("fsdp", None),
        P("fsdp", None),
        P("fsdp"),
        P("fsdp", None),
        P("fsdp", None),
        P("fsdp", None),
        P("fsdp", "seq", None),
    )
    return jax.shard_map(
        plain_body,
        mesh=mesh,
        in_specs=placed,
        out_specs=(
            P("fsdp", "seq", None),
            P("fsdp", "seq", None),
            P("fsdp"),
            P("fsdp", None),
            P("fsdp", None),
            P("fsdp", None),
            P("fsdp", None),
            P("fsdp"),
            P("fsdp", None),
            P("fsdp", None),
            P("fsdp", None),
        ),
        check_vma=False,
    )
```

```python
import functools
import math

import jax
import jax.numpy as jnp
from jax import lax
from jax.experimental import pallas as pl
from jax.experimental.pallas import tpu as pltpu
from jax.sharding import Mesh
from jax.sharding import PartitionSpec as P

QH = 16
KVH = 8
HD = 96


THETA = 100000.0
EPS = 1e-05
LOW = jnp.bfloat16
F32 = jnp.float32
NEG = -1e30
LN2 = math.log(2.0)


def contract(left, right, left_axis, right_axis):
    return lax.dot_general(
        left, right, (((left_axis,), (right_axis,)), ((), ())), preferred_element_type=F32
    )


def visible(first, second, query_start, key_start, queries, keys):
    key = key_start + lax.broadcasted_iota(jnp.int32, (keys, queries), 0)
    query = query_start + lax.broadcasted_iota(jnp.int32, (1, queries), 1)
    start = jnp.where(query >= second, second, jnp.where(query >= first, first, 0))
    return (key >= start) & (key <= query)


def halves_of(size):
    return slice(0, size // 2), slice(size // 2, size)


def slot_of(block, count):
    return (block % (count // 2)) * 2 + block // (count // 2)


def forward_kernel(
    scalars,
    own_ref,
    other_ref,
    low_ref,
    full_ref,
    log_ref,
    query_s,
    key_s,
    value_s,
    top_s,
    total_s,
    mixed_s,
    *,
    size,
    count,
):
    half = scalars[0]
    first = scalars[1]
    second = scalars[2]
    here = pl.program_id(0)
    per_half = count // 2

    @pl.when(here == 0)
    def _():
        for ref, side in ((own_ref, half), (other_ref, 1 - half)):
            for step in range(per_half):
                block = side * per_half + step
                columns = slice(step * size, (step + 1) * size)
                query_s[block] = ref[0:HD, columns]
                key_s[block] = ref[HD : 2 * HD, columns].T
                value_s[block] = ref[2 * HD : 3 * HD, columns]

    query = query_s[here]
    top_s[...] = jnp.full_like(top_s, NEG)
    total_s[...] = jnp.zeros_like(total_s)
    mixed_s[...] = jnp.zeros_like(mixed_s)

    def add_block(block, masked):
        keys, values = key_s[block], value_s[block]
        parts = halves_of(size)
        all_scores = [contract(keys, query[:, part], 1, 0) for part in parts]
        for part, scores in zip(parts, all_scores):
            if masked:
                seen = visible(
                    first, second, here * size + part.start, block * size, size // 2, size
                )
                scores = jnp.where(seen, scores, NEG)
            old_top = top_s[:, part]
            top = jnp.maximum(old_top, jnp.max(scores, 0, keepdims=True))
            expo = jnp.exp2(scores - top)
            scale = jnp.exp2(old_top - top)
            top_s[:, part] = top
            total_s[:, part] = total_s[:, part] * scale + jnp.sum(expo, 0, keepdims=True)
            mixed_s[:, part] = mixed_s[:, part] * scale + contract(
                values, expo.astype(LOW), 1, 0
            )

    last = count - 1

    @pl.loop(1, jnp.where(here == last, 1, here))
    def _(block):
        add_block(block, False)

    @pl.loop(0, jnp.where(here == last, count, jnp.minimum(here + 1, 2)))
    def _(step):
        add_block(jnp.where(here == last, step, step * here), True)

    total = total_s[...]
    result = mixed_s[...] / total
    full_ref[0] = result
    low_ref[0] = result.astype(LOW)
    log_ref[0] = top_s[...] + jnp.log2(total)


def backward_kernel(
    scalars,
    own_ref,
    other_ref,
    grad_ref,
    full_ref,
    log_ref,
    kept_ref,
    leaving_ref,
    query_s,
    key_s,
    value_s,
    delta_s,
    query_grad_s,
    key_grad_s,
    value_grad_s,
    *,
    size,
    count,
):
    half = scalars[0]
    first = scalars[1]
    second = scalars[2]
    here = pl.program_id(0)
    per_half = count // 2

    @pl.when(here == 0)
    def _():
        for ref, side in ((own_ref, half), (other_ref, 1 - half)):
            for step in range(per_half):
                block = side * per_half + step
                columns = slice(step * size, (step + 1) * size)
                query_s[block] = ref[0:HD, columns]
                key_s[block] = ref[HD : 2 * HD, columns]
                value_s[block] = ref[2 * HD : 3 * HD, columns].T
        for block in range(count):
            delta_s[block] = jnp.sum(
                grad_ref[slot_of(block, count)].astype(F32) * full_ref[block], 0, keepdims=True
            )
        query_grad_s[...] = jnp.zeros_like(query_grad_s)

    key_grad_s[...] = jnp.zeros_like(key_grad_s)
    value_grad_s[...] = jnp.zeros_like(value_grad_s)
    key = key_s[here]
    key_rows = key.T
    value_rows = value_s[here]

    def add_block(block, masked):
        query = query_s[block]
        grad = grad_ref[slot_of(block, count)]
        log_total, delta = log_ref[block], delta_s[block]
        parts = halves_of(size)
        products = [
            (contract(key_rows, query[:, part], 1, 0), contract(value_rows, grad[:, part], 1, 0))
            for part in parts
        ]
        for part, (scores, grad_probs) in zip(parts, products):
            if masked:
                seen = visible(
                    first, second, block * size + part.start, here * size, size // 2, size
                )
                scores = jnp.where(seen, scores, NEG)
            probs = jnp.exp2(scores - log_total[:, part])
            grad_scores = (probs * (grad_probs - delta[:, part])).astype(LOW)
            value_grad_s[...] += contract(grad[:, part], probs.astype(LOW), 1, 1)
            key_grad_s[...] += contract(query[:, part], grad_scores, 1, 1)
            query_grad_s[block, :, part] += contract(key, grad_scores, 1, 0)

    last = count - 1

    @pl.loop(here + 1, jnp.where(here == 0, 1, last))
    def _(block):
        add_block(block, False)

    @pl.loop(0, jnp.where(here == 0, count, jnp.where(here == last, 1, 2)))
    def _(step):
        add_block(jnp.where(here == 0, step, jnp.where(step == 0, here, last)), True)

    side = here // per_half
    columns = pl.ds(pl.multiple_of((here % per_half) * size, size), size)

    def write(out_ref):
        out_ref[0:HD, columns] = (query_grad_s[here] * HD**-0.5).astype(LOW)
        out_ref[HD : 2 * HD, columns] = (key_grad_s[...] * LN2).astype(LOW)
        out_ref[2 * HD : 3 * HD, columns] = value_grad_s[...].astype(LOW)

    @pl.when(side == half)
    def _():
        write(kept_ref)

    @pl.when(side != half)
    def _():
        write(leaving_ref)


def attend_forward(scalars, own, other, size):
    count = 2 * own.shape[1] // size
    whole = lambda shape: pl.BlockSpec(shape, lambda i, s: (0,) * len(shape))
    pairs = count * (count + 1) // 2
    return pl.pallas_call(
        functools.partial(forward_kernel, size=size, count=count),
        grid_spec=pltpu.PrefetchScalarGridSpec(
            num_scalar_prefetch=1,
            grid=(count,),
            in_specs=[whole(own.shape), whole(other.shape)],
            out_specs=[
                pl.BlockSpec(
                    (1, HD, size), lambda i, s: (slot_of(i, count), 0, 0)
                ),
                pl.BlockSpec((1, HD, size), lambda i, s: (i, 0, 0)),
                pl.BlockSpec((1, 1, size), lambda i, s: (i, 0, 0)),
            ],
            scratch_shapes=[
                pltpu.VMEM((count, HD, size), LOW),
                pltpu.VMEM((count, size, HD), LOW),
                pltpu.VMEM((count, HD, size), LOW),
                pltpu.VMEM((1, size), F32),
                pltpu.VMEM((1, size), F32),
                pltpu.VMEM((HD, size), F32),
            ],
        ),
        out_shape=[
            jax.ShapeDtypeStruct((count, HD, size), LOW),
            jax.ShapeDtypeStruct((count, HD, size), F32),
            jax.ShapeDtypeStruct((count, 1, size), F32),
        ],
        compiler_params=pltpu.CompilerParams(
            dimension_semantics=("arbitrary",), vmem_limit_bytes=32 * 2**20
        ),
        cost_estimate=pl.CostEstimate(
            flops=pairs * size * size * HD * 32,
            bytes_accessed=10 * 2**20,
            transcendentals=pairs * size * size,
        ),
        name="attend_forward",
    )(scalars, own, other)


def attend_backward(scalars, own, other, grad, full, log_total):
    count, _, size = grad.shape
    whole = lambda shape: pl.BlockSpec(shape, lambda i, s: (0,) * len(shape))
    pairs = count * (count + 1) // 2
    out_shape = own.shape
    return pl.pallas_call(
        functools.partial(backward_kernel, size=size, count=count),
        grid_spec=pltpu.PrefetchScalarGridSpec(
            num_scalar_prefetch=1,
            grid=(count,),
            in_specs=[
                whole(own.shape),
                whole(other.shape),
                whole(grad.shape),
                whole(full.shape),
                whole(log_total.shape),
            ],
            out_specs=[whole(out_shape)] * 2,
            scratch_shapes=[
                pltpu.VMEM((count, HD, size), LOW),
                pltpu.VMEM((count, HD, size), LOW),
                pltpu.VMEM((count, size, HD), LOW),
                pltpu.VMEM((count, 1, size), F32),
                pltpu.VMEM((count, HD, size), F32),
                pltpu.VMEM((HD, size), F32),
                pltpu.VMEM((HD, size), F32),
            ],
        ),
        out_shape=[jax.ShapeDtypeStruct(out_shape, LOW)] * 2,
        compiler_params=pltpu.CompilerParams(
            dimension_semantics=("arbitrary",), vmem_limit_bytes=32 * 2**20
        ),
        cost_estimate=pl.CostEstimate(
            flops=pairs * size * size * HD * 42,
            bytes_accessed=16 * 2**20,
            transcendentals=pairs * size * size,
        ),
        name="attend_backward",
    )(scalars, own, other, grad, full, log_total)


def place_rows_kernel(order, *refs):
    pieces, out_ref = refs[:-1], refs[-1]
    size = pieces[0].shape[0]
    for index, piece in enumerate(pieces):
        start = pl.multiple_of(order[index] * size, size)
        out_ref[pl.ds(start, size), :] = piece[...].astype(F32)


def place_rows(order, pieces):
    size, width = pieces[0].shape
    total = size * len(pieces)
    step = 512
    return pl.pallas_call(
        place_rows_kernel,
        grid_spec=pltpu.PrefetchScalarGridSpec(
            num_scalar_prefetch=1,
            grid=(width // step,),
            in_specs=[pl.BlockSpec((size, step), lambda i, s: (0, i)) for _ in pieces],
            out_specs=pl.BlockSpec((total, step), lambda i, s: (0, i)),
        ),
        out_shape=jax.ShapeDtypeStruct((total, width), F32),
        compiler_params=pltpu.CompilerParams(vmem_limit_bytes=24 * 2**20),
        cost_estimate=pl.CostEstimate(
            flops=0, bytes_accessed=total * width * 6, transcendentals=0
        ),
        name="place_rows",
    )(order, *pieces)


def place_columns_kernel(order, gain_ref, gate_w_ref, up_w_ref, *refs):
    count = (len(refs) - 3) // 2
    gates, ups = refs[:count], refs[count : 2 * count]
    gate_ref, up_ref, sum_ref = refs[2 * count :]
    size = gates[0].shape[1]
    gain = gain_ref[...]
    total = jnp.zeros((gate_ref.shape[0], size), F32)
    for index in range(count):
        columns = pl.ds(pl.multiple_of(order[index] * size, size), size)
        gate, up = gates[index][...].astype(F32), ups[index][...].astype(F32)
        total += gate * gate_w_ref[:, columns].astype(F32)
        total += up * up_w_ref[:, columns].astype(F32)
        gate_ref[:, columns] = gate * gain
        up_ref[:, columns] = up * gain

    @pl.when(pl.program_id(0) == 0)
    def _():
        sum_ref[...] = jnp.zeros_like(sum_ref)

    sum_ref[...] += jnp.sum(total, 1, keepdims=True)


def place_columns(order, gain, gate_weight, up_weight, gates, ups, shards):
    rows, width = gate_weight.shape
    span = width // shards
    size = span // len(gates)
    wide = pl.BlockSpec((rows, span), lambda i, s: (0, i))
    thin = pl.BlockSpec((rows, 1), lambda i, s: (0, 0))
    pieces = [pl.BlockSpec((rows, size), lambda i, s: (0, i)) for _ in (*gates, *ups)]
    return pl.pallas_call(
        place_columns_kernel,
        grid_spec=pltpu.PrefetchScalarGridSpec(
            num_scalar_prefetch=1,
            grid=(shards,),
            in_specs=[thin, wide, wide, *pieces],
            out_specs=[wide, wide, thin],
        ),
        out_shape=[
            jax.ShapeDtypeStruct((rows, width), F32),
            jax.ShapeDtypeStruct((rows, width), F32),
            jax.ShapeDtypeStruct((rows, 1), F32),
        ],
        compiler_params=pltpu.CompilerParams(
            dimension_semantics=("arbitrary",), vmem_limit_bytes=24 * 2**20
        ),
        cost_estimate=pl.CostEstimate(
            flops=rows * width * 6, bytes_accessed=rows * width * 16, transcendentals=0
        ),
        name="place_columns",
    )(order, gain, gate_weight, up_weight, *gates, *ups)


def place_heads_kernel(gain_ref, query_w, key_w, value_w, all_ref, query_ref, key_ref, value_ref, sum_ref):
    rows = gain_ref.shape[0]
    wide = query_ref.shape[1] // KVH
    gain = gain_ref[...]
    total = jnp.zeros((rows, 4 * HD), F32)
    pieces = [all_ref[i * rows : (i + 1) * rows, :].astype(F32) for i in range(KVH)]
    for start in range(0, KVH, 2):
        value = jnp.concatenate([piece[:, :wide] for piece in pieces[start : start + 2]], 1)
        columns = slice(start * wide, (start + 2) * wide)
        total += value * query_w[:, columns].astype(F32)
        query_ref[:, columns] = value * gain
    for first, weight, out_ref in ((wide, key_w, key_ref), (wide + HD, value_w, value_ref)):
        for start in range(0, KVH, 4):
            value = jnp.concatenate(
                [piece[:, first : first + HD] for piece in pieces[start : start + 4]], 1
            )
            columns = slice(start * HD, (start + 4) * HD)
            total += value * weight[:, columns].astype(F32)
            out_ref[:, columns] = value * gain
    sum_ref[...] = jnp.sum(total, 1, keepdims=True)


def place_heads(gain, query_weight, key_weight, value_weight, pieces):
    weights = (query_weight, key_weight, value_weight)
    rows = gain.shape[0]
    return pl.pallas_call(
        place_heads_kernel,
        out_shape=[jax.ShapeDtypeStruct(weight.shape, F32) for weight in weights]
        + [jax.ShapeDtypeStruct((rows, 1), F32)],
        compiler_params=pltpu.CompilerParams(vmem_limit_bytes=32 * 2**20),
        cost_estimate=pl.CostEstimate(
            flops=rows * 3072 * 4, bytes_accessed=rows * 3072 * 8, transcendentals=0
        ),
        name="place_heads",
    )(gain, *weights, pieces)


def merge_kernel(scalars, kept_ref, came_ref, cosine_ref, sine_ref, out_ref, split_ref):
    lead = scalars[0] == 0
    lines, _, size = split_ref.shape
    for line in range(lines):
        columns = slice(line * size, (line + 1) * size)
        kept = kept_ref[:, columns].astype(F32)
        came = came_ref[:, columns].astype(F32)
        cosine, sine = cosine_ref[:, columns], sine_ref[:, columns]
        joint = kept[HD:] + came[HD:]
        first = jnp.where(lead, kept[:HD], came[:HD])
        second = jnp.where(lead, came[:HD], kept[:HD])
        turned = []
        for value in (first, second, joint[:HD]):
            low, high = value[: HD // 2], value[HD // 2 :]
            turned.append(low * cosine + high * sine)
            turned.append(high * cosine - low * sine)
        turned.append(joint[HD:])
        result = jnp.concatenate([part.astype(LOW) for part in turned], 0)
        out_ref[:, columns] = result
        split_ref[line] = result


def merge(scalars, kept, came, cosine, sine, lines):
    tokens = kept.shape[1]
    whole = lambda value: pl.BlockSpec(value.shape, lambda i, s: (0,) * len(value.shape))
    outs = [
        jax.ShapeDtypeStruct((4 * HD, tokens), LOW),
        jax.ShapeDtypeStruct((lines, 4 * HD, tokens // lines), LOW),
    ]
    return pl.pallas_call(
        merge_kernel,
        grid_spec=pltpu.PrefetchScalarGridSpec(
            num_scalar_prefetch=1,
            grid=(1,),
            in_specs=[whole(value) for value in (kept, came, cosine, sine)],
            out_specs=[whole(value) for value in outs],
        ),
        out_shape=outs,
        compiler_params=pltpu.CompilerParams(vmem_limit_bytes=24 * 2**20),
        cost_estimate=pl.CostEstimate(
            flops=tokens * HD * 24, bytes_accessed=tokens * HD * 30, transcendentals=0
        ),
        name="merge",
    )(scalars, kept, came, cosine, sine)


def pack_kernel(scalars, gain_ref, query_ref, key_ref, value_ref, *outs):
    core = scalars[3]
    gain = gain_ref[...]
    wide = query_ref.shape[1] // KVH
    span = wide + 2 * HD
    for which in range(2):

        @pl.when(core == which)
        def _():
            for line in range(KVH // 2):
                head = 2 * line + which
                value = jnp.concatenate(
                    [
                        query_ref[:, head * wide : (head + 1) * wide].astype(F32),
                        key_ref[:, head * HD : (head + 1) * HD].astype(F32),
                        value_ref[:, head * HD : (head + 1) * HD].astype(F32),
                    ],
                    1,
                )
                place = (line % 2) * span
                outs[line // 2][:, place : place + span] = (value * gain).astype(LOW)


def pack(scalars, gain, query_weight, key_weight, value_weight):
    rows, width = query_weight.shape
    whole = lambda value: pl.BlockSpec(value.shape, lambda i, s: (0, 0))
    weights = (gain, query_weight, key_weight, value_weight)
    outs = [jax.ShapeDtypeStruct((rows, width // 2), LOW)] * 2
    return pl.pallas_call(
        pack_kernel,
        grid_spec=pltpu.PrefetchScalarGridSpec(
            num_scalar_prefetch=1,
            grid=(1,),
            in_specs=[whole(value) for value in weights],
            out_specs=[whole(value) for value in outs],
        ),
        out_shape=outs,
        compiler_params=pltpu.CompilerParams(vmem_limit_bytes=24 * 2**20),
        cost_estimate=pl.CostEstimate(
            flops=rows * width, bytes_accessed=rows * width * 6, transcendentals=0
        ),
        name="pack",
    )(scalars, *weights)


def spread_kernel(scalars, lin_ref, cosine_ref, sine_ref, own_ref, leaving_ref):
    cosine, sine = cosine_ref[...], sine_ref[...]

    def turn(start, factor):
        low = lin_ref[start : start + HD // 2, :]
        high = lin_ref[start + HD // 2 : start + HD, :]
        turned = ((low * cosine - high * sine) * factor, (high * cosine + low * sine) * factor)
        return jnp.concatenate([part.astype(LOW) for part in turned], 0)

    lead = scalars[0] == 0
    first, second = turn(0, HD**-0.5 / LN2), turn(HD, HD**-0.5 / LN2)

    @pl.when(lead)
    def _():
        own_ref[0:HD] = first
        leaving_ref[0:HD] = second

    @pl.when(jnp.logical_not(lead))
    def _():
        own_ref[0:HD] = second
        leaving_ref[0:HD] = first

    key = turn(2 * HD, 1.0)
    value = lin_ref[3 * HD : 4 * HD].astype(LOW)
    for ref in (own_ref, leaving_ref):
        ref[HD : 2 * HD] = key
        ref[2 * HD : 3 * HD] = value


def spread(scalars, lin, cosine, sine):
    tokens = lin.shape[1]
    step = 512
    column = lambda rows: pl.BlockSpec((rows, step), lambda i, s: (0, i))
    return pl.pallas_call(
        spread_kernel,
        grid_spec=pltpu.PrefetchScalarGridSpec(
            num_scalar_prefetch=1,
            grid=(tokens // step,),
            in_specs=[column(4 * HD), column(HD // 2), column(HD // 2)],
            out_specs=[column(3 * HD)] * 2,
        ),
        out_shape=[jax.ShapeDtypeStruct((3 * HD, tokens), LOW)] * 2,
        compiler_params=pltpu.CompilerParams(vmem_limit_bytes=24 * 2**20),
        cost_estimate=pl.CostEstimate(
            flops=tokens * HD * 24, bytes_accessed=tokens * HD * 36, transcendentals=0
        ),
        name="spread",
    )(scalars, lin, cosine, sine)


def swap(value, axis):
    return lax.ppermute(value, axis, [(0, 1), (1, 0)])


def swap_near(value):
    return lax.ppermute(value, "z", [(0, 1), (1, 0), (2, 3), (3, 2)])


def swap_far(value):
    return lax.ppermute(value, "z", [(0, 2), (2, 0), (1, 3), (3, 1)])


def tie(*values):
    return lax.optimization_barrier(values)


def in_order(place, own, other):
    return (jnp.where(place == 0, own, other), jnp.where(place == 0, other, own))


def both(place, own, other):
    return jnp.concatenate(in_order(place, own, other), 0)


def spread_out(value, first, second):
    other = swap(value, first)
    pair = jnp.stack(in_order(lax.axis_index(first), value, other))
    return pair, swap(pair, second)


def placed(pair, other, second):
    pairs = in_order(lax.axis_index(second), pair, other)
    grid = jnp.stack(pairs, 0 if second == "y" else 1)
    return grid.reshape(-1, *grid.shape[3:])


def pick(array, axis, at):
    return lax.dynamic_index_in_dim(array, at, axis, keepdims=False)


def halve(value, axis, along=0):
    at = lax.axis_index(axis)
    return pick(value, along, at), swap(pick(value, along, 1 - at), axis)


def halve_x(value):
    return halve(value.reshape(2, 2, -1, value.shape[-1]), "x", 1)


def halve_y(value):
    return halve(value.reshape(2, 2, -1, value.shape[-1]), "y", 0)


def fast_body(
    tokens,
    positions,
    first_gain,
    query_weight,
    key_weight,
    value_weight,
    output_weight,
    second_gain,
    gate_weight,
    up_weight,
    down_weight,
    cotangent,
):
    seq = ("z", "c")
    fsdp = ("y", "x")
    z, core, half = lax.axis_index("z"), lax.axis_index("c"), lax.axis_index("x")
    near = z % 2
    lines = lax.axis_size("z")
    seq_count = 2 * lines
    shards = lax.axis_size("y") * 2
    spot = z * 2 + core
    quarter = near * 2 + core
    rows = tokens[0]
    count, width = rows.shape
    chip_count = 2 * count
    half_len = count * seq_count
    seq_len = 2 * half_len

    begins = jnp.where(
        (spot == 0) & (half == 0),
        count - 1 - positions[0, count - 1],
        half * half_len + spot * count - positions[0, 0],
    )
    ends = begins + (seq_len - count)
    scalars = jnp.stack([half, begins, ends, core]).astype(jnp.int32)

    gain_one = first_gain.astype(F32)[:, None]
    gain_two = second_gain.astype(F32)[:, None]

    def row_scale(value):
        return lax.rsqrt(jnp.mean(value * value, -1, keepdims=True) + EPS)

    take = functools.partial(lax.dynamic_slice_in_dim, axis=1)
    take_rows = functools.partial(lax.dynamic_slice_in_dim, axis=0)
    gather = lambda value, axes: lax.all_gather(value, axes, axis=0, tiled=True)
    own_rows = rows.astype(F32)
    own_unit_scale = row_scale(own_rows)
    own_unit = own_rows * own_unit_scale
    units = gather(own_unit.astype(LOW), seq)
    wide = QH // KVH * HD
    qkv_shard = (
        jnp.concatenate(
            [
                take(query_weight, spot * wide, wide),
                take(key_weight, spot * HD, HD),
                take(value_weight, spot * HD, HD),
            ],
            1,
        ).astype(F32)
        * gain_one
    ).astype(LOW)
    out_rows = output_weight.shape[0] // 2
    out_shard = take_rows(output_weight, core * out_rows, out_rows)
    piece = down_weight.shape[0] // 4
    down_shard = take_rows(down_weight, quarter * piece, piece)
    gate_shard, up_shard = (
        (
            jnp.concatenate(
                [
                    take(weight, shard * 4 * piece + quarter * piece, piece)
                    for shard in range(shards)
                ],
                1,
            ).astype(F32)
            * gain_two
        ).astype(LOW)
        for weight in (gate_weight, up_weight)
    )
    side = lax.axis_index("y")
    qkv_pair = jnp.stack(in_order(half, qkv_shard, swap(qkv_shard, "x")))
    gate_pair = jnp.stack(in_order(half, gate_shard, swap(gate_shard, "x")))
    up_pair = jnp.stack(in_order(side, up_shard, swap(up_shard, "y")))
    qkv_pair, gate_pair, up_pair = tie(qkv_pair, gate_pair, up_pair)
    qkv_w = placed(qkv_pair, swap(qkv_pair, "y"), "y")
    gate_pair, up_pair = (gate_pair, swap(gate_pair, "y")), (up_pair, swap(up_pair, "x"))

    place = half * half_len + jnp.arange(half_len, dtype=jnp.int32)
    start = jnp.where(place >= ends, ends, jnp.where(place >= begins, begins, 0))
    freq = THETA ** (-(jnp.arange(HD // 2, dtype=F32) * 2.0 / HD))
    angle = freq[:, None] * (place - start).astype(F32)[None, :]
    cosine, sine = jnp.cos(angle), jnp.sin(angle)
    chip_rows = both(core, rows, swap(rows, "c"))
    units, own_cot, chip_rows = tie(units, cotangent[0], chip_rows)
    own, leaving = spread(scalars, contract(qkv_w, units, 0, 1), cosine, sine)

    near_cot = swap_near(own_cot)
    other, out_shard, down_shard, near_cot, chip_cot, gate_pair, up_pair = tie(
        swap(leaving, "x"),
        out_shard,
        down_shard,
        near_cot,
        both(core, own_cot, swap(own_cot, "c")),
        gate_pair,
        up_pair,
    )
    out_w = gather(out_shard, fsdp)
    down_w = gather(down_shard, fsdp)
    near_other = swap(near_cot, "c")
    head_low, head_full, log_total = attend_forward(scalars, own, other, chip_count)
    exchange = lambda value: lax.all_to_all(
        value, ("z", "x"), split_axis=0, concat_axis=0, tiled=True
    )
    head_low, near_other = tie(head_low, near_other)
    lead_shard, tail_shard = pack(scalars, gain_one, query_weight, key_weight, value_weight)
    heads, gate_w, up_w, near_cot, lead_shard = tie(
        exchange(head_low),
        placed(*gate_pair, "y"),
        placed(*up_pair, "x"),
        jnp.concatenate([near_cot, near_other], 0),
        lead_shard,
    )
    lead_w = gather(lead_shard, fsdp)
    heads = heads.reshape(QH // 2 * HD, chip_count)

    mine_of = lambda value: take_rows(value, core * count, count)
    theirs_of = lambda value: take_rows(value, (1 - core) * count, count)
    branch = contract(heads, out_w, 0, 0).astype(LOW)
    middle = chip_rows.astype(F32) + (branch.astype(F32) + swap(branch, "c").astype(F32))
    middle_scale = row_scale(middle)
    chip_unit = middle * middle_scale
    own_middle, own_scale, own_middle_unit = (
        mine_of(middle),
        mine_of(middle_scale),
        mine_of(chip_unit),
    )
    chip_unit = chip_unit.astype(LOW)
    near_unit = swap_near(mine_of(chip_unit))

    def feed(unit):
        gate, upper = contract(unit, gate_w, 1, 0), contract(unit, up_w, 1, 0)
        sigma = jax.nn.sigmoid(gate)
        silu = gate * sigma
        return (silu * upper).astype(LOW), (gate, upper, sigma, silu)

    def feed_back(cot, kept):
        gate, upper, sigma, silu = kept
        grad_hidden = contract(cot, down_w, 1, 1)
        gate_low = (grad_hidden * upper * sigma * (1.0 + gate * (1.0 - sigma))).astype(LOW)
        upper_low = (grad_hidden * silu).astype(LOW)
        part = contract(gate_low, gate_w, 1, 1) + contract(upper_low, up_w, 1, 1)
        return gate_low, upper_low, part

    def chip_sum(chip_part, near_part):
        near_sum = near_part[:count].astype(F32) + swap(near_part[count:].astype(LOW), "c")
        own_sum = mine_of(chip_part).astype(F32) + swap(theirs_of(chip_part).astype(LOW), "c")
        return own_sum, near_sum.astype(LOW)

    stack = lambda first, second: jnp.concatenate([first, second], 0)
    scatter = lambda value: lax.psum_scatter(value, fsdp, scatter_dimension=0, tiled=True)
    chip_hidden, chip_kept = feed(chip_unit)
    near_unit, chip_hidden = tie(near_unit, chip_hidden)
    near_unit = jnp.concatenate([near_unit, swap(near_unit, "c")], 0)
    near_hidden, near_kept = feed(near_unit)
    down_part = contract(
        stack(chip_hidden, near_hidden), stack(chip_cot, near_cot), 0, 0
    ).astype(LOW)
    near_cot, down_part = tie(near_cot, down_part)
    near_gate, near_upper, near_part = feed_back(near_cot, near_kept)
    chip_gate, chip_upper, chip_part = feed_back(chip_cot, chip_kept)
    grad_two, near_sum = chip_sum(chip_part, near_part)

    def four(value, near_value):
        return value, swap(value, "c"), near_value, swap(near_value, "c")

    def halves_first(value):
        cut = value.shape[-1] // 2
        return halve_x(value[:, :cut]), halve_y(value[:, cut:])

    def halves_second(firsts):
        return halve(sum(firsts[0]), "y"), halve(sum(firsts[1]), "x")

    def halves_end(seconds):
        return jnp.concatenate([sum(seconds[0]), sum(seconds[1])], 1)

    down_first = halves_first(down_part)
    near_sum, near_gate, near_upper, chip_part = tie(
        near_sum, near_gate, near_upper, chip_part
    )
    grad_came = swap_near(near_sum)
    all_units = stack(chip_unit, near_unit)
    gate_part = contract(all_units, stack(chip_gate, near_gate), 0, 0).astype(LOW)
    up_part = contract(all_units, stack(chip_upper, near_upper), 0, 0).astype(LOW)
    feed_own, feed_near = chip_sum(
        contract(chip_hidden, down_w, 1, 0), contract(near_hidden, down_w, 1, 0)
    )
    gate_part, up_part, down_first, grad_came, feed_near = tie(
        gate_part, up_part, down_first, grad_came, feed_near
    )
    feed_near = swap_near(feed_near)
    down_second = halves_second(down_first)
    grad_two = grad_two + grad_came.astype(F32)
    grad_middle = own_cot.astype(F32) + own_scale * (
        grad_two - own_middle_unit * jnp.mean(grad_two * own_middle_unit, -1, keepdims=True)
    )
    own_branch, lead_w, down_second, gate_part, up_part = tie(
        grad_middle.astype(LOW), lead_w, down_second, gate_part, up_part
    )
    gate_grad, up_grad = scatter(gate_part), scatter(up_part)
    down_grad = halves_end(down_second)
    down_far = swap_far(down_grad)
    grad_branch = both(core, own_branch, swap(own_branch, "c"))
    grad_heads = contract(out_w, grad_branch, 1, 1).astype(LOW)
    grad_heads, grad_branch, down_far = tie(grad_heads, grad_branch, down_far)
    down_sum = down_grad + down_far
    output_part = contract(heads, grad_branch, 1, 0).astype(LOW)
    output_first = halves_first(output_part)
    grad_head, output_first, gate_grad, down_sum = tie(
        exchange(grad_heads.reshape(2 * lines, HD, chip_count)), output_first, gate_grad, down_sum
    )
    output_second = halves_second(output_first)
    down_near = swap_near(down_sum)

    gate_far = swap_far(gate_grad)
    kept, leaving = attend_backward(scalars, own, other, grad_head, head_full, log_total)
    kept, leaving, gate_far, down_near, tail_shard, feed_near, output_second = tie(
        kept, leaving, gate_far, down_near, tail_shard, feed_near, output_second
    )
    output_grad = halves_end(output_second)
    tail_w = gather(tail_shard, fsdp)

    up_far = swap_far(up_grad)
    gate_sum = gate_grad + gate_far
    gate_near = swap_near(gate_sum)
    block_output = (own_middle + feed_own + feed_near.astype(F32)).astype(LOW)[None]
    output_came = swap_near(output_grad)
    came, up_far, gate_near, block_output, output_grad, output_came, tail_w = tie(
        swap(leaving, "x"), up_far, gate_near, block_output, output_grad, output_came, tail_w
    )

    qkv_low, by_line = merge(scalars, kept, came, cosine, sine, lines)
    token_grads = lax.all_to_all(by_line, "z", split_axis=0, concat_axis=0, tiled=True)
    qkv_part = contract(units, qkv_low, 0, 1).astype(LOW).reshape(shards, 2, -1, 4 * HD)
    qkv_first = halve_x(qkv_part[:, 0]), halve_y(qkv_part[:, 1])
    qkv_second = halves_second(qkv_first)
    qkv_grad = jnp.concatenate([sum(qkv_second[0]), sum(qkv_second[1])], 0)
    up_sum = up_grad + up_far
    up_near = swap_near(up_sum)
    down_pieces = four(down_sum, down_near)
    output_sum = output_grad + output_came
    output_far = swap_far(output_sum)
    token_grads, qkv_grad, up_near, down_pieces, output_far = tie(
        token_grads, qkv_grad, up_near, down_pieces, output_far
    )
    all_qkv = gather(qkv_grad, seq)

    token_grads = token_grads.reshape(-1, chip_count)
    split = lead_w.shape[1]
    grad_one = contract(token_grads[:split], lead_w, 0, 1) + contract(
        token_grads[split:], tail_w, 0, 1
    )
    grad_one = mine_of(grad_one) + swap(theirs_of(grad_one).astype(LOW), "c").astype(F32)
    grad_rows = own_unit_scale * (
        grad_one - own_unit * jnp.mean(grad_one * own_unit, -1, keepdims=True)
    )
    input_grad = (grad_middle + grad_rows).astype(LOW)[None]

    order = jnp.stack([quarter, quarter ^ 1, quarter ^ 2, quarter ^ 3]).astype(jnp.int32)
    core_order = jnp.stack([core, 1 - core]).astype(jnp.int32)
    down_total = place_rows(order, down_pieces)
    gate_total, up_total, second_gain_grad = place_columns(
        order, gain_two, gate_weight, up_weight, four(gate_sum, gate_near), four(up_sum, up_near), shards
    )
    output_own = output_sum + output_far
    output_total = place_rows(core_order, (output_own, swap(output_own, "c")))
    query_grad, key_grad, value_grad, first_gain_grad = place_heads(
        gain_one, query_weight, key_weight, value_weight, all_qkv
    )
    return (
        block_output,
        input_grad,
        first_gain_grad[:, 0],
        query_grad,
        key_grad,
        value_grad,
        output_total,
        second_gain_grad[:, 0],
        gate_total,
        up_total,
        down_total,
    )


def fast_solution(mesh):
    seq_count, shard_count = mesh.devices.shape
    fine = Mesh(
        mesh.devices.reshape(seq_count // 2, 2, shard_count // 2, 2), ("z", "c", "y", "x")
    )
    seq, fsdp = ("z", "c"), ("y", "x")
    matrix = P(fsdp, None)
    return jax.shard_map(
        fast_body,
        mesh=fine,
        in_specs=(
            P(fsdp, seq, None),
            P(fsdp, seq),
            P(fsdp),
            matrix,
            matrix,
            matrix,
            matrix,
            P(fsdp),
            matrix,
            matrix,
            matrix,
            P(fsdp, seq, None),
        ),
        out_specs=(
            P(fsdp, seq, None),
            P(fsdp, seq, None),
            P(fsdp),
            matrix,
            matrix,
            matrix,
            matrix,
            P(fsdp),
            matrix,
            matrix,
            matrix,
        ),
        check_vma=False,
    )


def solution(mesh):
    shape = dict(mesh.shape)
    if shape["seq"] == KVH and shape["fsdp"] == 4:
        return fast_solution(mesh)
    return plain_solution(mesh)


def shifted(value, axis, steps):
    count = lax.axis_size(axis)
    first, last = (max(0, -steps), min(count, count - steps))
    return lax.ppermute(value, axis, [(source, source + steps) for source in range(first, last)])


def rope_tables(position_rows):
    freq = THETA ** (-(jnp.arange(HD // 2, dtype=jnp.float32) * 2.0 / HD))
    angle = position_rows.astype(jnp.float32)[:, None] * freq[None, :]
    cosine = jnp.cos(angle)
    sine = jnp.sin(angle)
    return (jnp.concatenate([cosine, cosine], -1), jnp.concatenate([sine, sine], -1))


def rotate(values, cosine, sine):
    half = HD // 2
    turned = jnp.concatenate([-values[..., half:], values[..., :half]], -1)
    return values * cosine[:, None, :] + turned * sine[:, None, :]


def rotate_back(grads, cosine, sine):
    half = HD // 2
    scaled = grads * sine[:, None, :]
    turned = jnp.concatenate([scaled[..., half:], -scaled[..., :half]], -1)
    return grads * cosine[:, None, :] + turned


def norm_forward(rows, gain):
    scale = lax.rsqrt(jnp.mean(rows * rows, -1, keepdims=True) + EPS)
    unit = rows * scale
    return (unit * gain, unit, scale)


def norm_backward(grad_out, unit, scale, gain):
    grad_unit = grad_out * gain
    gain_grad = jnp.sum(grad_out * unit, 0)
    grad_rows = scale * (grad_unit - unit * jnp.mean(grad_unit * unit, -1, keepdims=True))
    return (grad_rows, gain_grad)


def plain_body(
    tokens,
    positions,
    first_gain,
    query_weight,
    key_weight,
    value_weight,
    output_weight,
    second_gain,
    gate_weight,
    up_weight,
    down_weight,
    cotangent,
):
    seq_count = lax.axis_size("seq")
    local_rows = tokens[0]
    token_count = local_rows.shape[0]
    half_len = token_count * seq_count
    rows_float = local_rows.astype(jnp.float32)
    gain_one, wq_full, wk_full, wv_full, wo_full = (
        lax.all_gather(first_gain, "fsdp", axis=0, tiled=True),
        lax.all_gather(query_weight, "fsdp", axis=0, tiled=True),
        lax.all_gather(key_weight, "fsdp", axis=0, tiled=True),
        lax.all_gather(value_weight, "fsdp", axis=0, tiled=True),
        lax.all_gather(output_weight, "fsdp", axis=0, tiled=True),
    )
    gain_one = gain_one.astype(jnp.float32)
    normed_one, unit_one, scale_one = norm_forward(rows_float, gain_one)
    normed_low = normed_one.astype(jnp.bfloat16)
    cosine, sine = rope_tables(positions[0])
    query_lin = jnp.dot(normed_low, wq_full, preferred_element_type=jnp.float32).reshape(
        token_count, QH, HD
    )
    key_lin = jnp.dot(normed_low, wk_full, preferred_element_type=jnp.float32).reshape(
        token_count, KVH, HD
    )
    value_lin = jnp.dot(normed_low, wv_full, preferred_element_type=jnp.float32).reshape(
        token_count, KVH, HD
    )
    query_rows = rotate(query_lin, cosine, sine).astype(jnp.bfloat16)
    key_rows = rotate(key_lin, cosine, sine).astype(jnp.bfloat16)
    value_rows = value_lin.astype(jnp.bfloat16)
    repeat = max(1, seq_count // KVH)
    if repeat > 1:
        key_rows = jnp.repeat(key_rows, repeat, axis=1)
        value_rows = jnp.repeat(value_rows, repeat, axis=1)
    query_heads, key_heads, value_heads = (
        lax.all_to_all(query_rows, "seq", split_axis=1, concat_axis=0, tiled=True),
        lax.all_to_all(key_rows, "seq", split_axis=1, concat_axis=0, tiled=True),
        lax.all_to_all(value_rows, "seq", split_axis=1, concat_axis=0, tiled=True),
    )
    head_count = query_heads.shape[1]
    pair_count = key_heads.shape[1]
    group = head_count // pair_count
    half_positions = lax.all_gather(positions[0], "seq", axis=0, tiled=True)
    key_prior, value_prior = shifted((key_heads, value_heads), "fsdp", 1)
    key_all = jnp.concatenate([key_prior, key_heads], 0)
    value_all = jnp.concatenate([value_prior, value_heads], 0)
    half_index = lax.axis_index("fsdp") % 2
    key_index = (half_index - 1) * half_len + jnp.arange(2 * half_len, dtype=jnp.int32)
    row_index = half_index * half_len + jnp.arange(half_len, dtype=jnp.int32)
    row_start = row_index - half_positions
    block = min(512, half_len)
    count = half_len // block
    factor = HD ** (-0.5)
    query_blocks = query_heads.reshape(count, block, pair_count, group, HD)
    index_blocks = row_index.reshape(count, block)
    start_blocks = row_start.reshape(count, block)

    def block_scores(query_block, index_block, start_block):
        scores = (
            jnp.einsum("bkgd,tkd->kgbt", query_block, key_all, preferred_element_type=jnp.float32)
            * factor
        )
        visible = (key_index[None, :] >= start_block[:, None]) & (
            key_index[None, :] <= index_block[:, None]
        )
        return jnp.where(visible, scores, -1e30)

    def forward_block(items):
        query_block, index_block, start_block = items
        scores = block_scores(query_block, index_block, start_block)
        top = jnp.max(scores, -1, keepdims=True)
        expo = jnp.exp(scores - top)
        total = jnp.sum(expo, -1, keepdims=True)
        probs_low = (expo / total).astype(jnp.bfloat16)
        mixed = jnp.einsum(
            "kgbt,tkd->bkgd", probs_low, value_all, preferred_element_type=jnp.float32
        )
        return (mixed.reshape(block, head_count, HD).astype(jnp.bfloat16), top + jnp.log(total))

    head_blocks, log_totals = lax.map(forward_block, (query_blocks, index_blocks, start_blocks))
    head_out = head_blocks.reshape(half_len, head_count, HD)
    token_heads = lax.all_to_all(head_out, "seq", split_axis=0, concat_axis=1, tiled=True)
    heads_flat = token_heads.reshape(token_count, QH * HD)
    middle = rows_float + jnp.dot(heads_flat, wo_full, preferred_element_type=jnp.float32)
    gain_two, wg_full, wu_full, wd_full = (
        lax.all_gather(second_gain, "fsdp", axis=0, tiled=True),
        lax.all_gather(gate_weight, "fsdp", axis=0, tiled=True),
        lax.all_gather(up_weight, "fsdp", axis=0, tiled=True),
        lax.all_gather(down_weight, "fsdp", axis=0, tiled=True),
    )
    gain_two = gain_two.astype(jnp.float32)
    normed_two, unit_two, scale_two = norm_forward(middle, gain_two)
    normed_two_low = normed_two.astype(jnp.bfloat16)
    gate = jnp.dot(normed_two_low, wg_full, preferred_element_type=jnp.float32)
    upper = jnp.dot(normed_two_low, wu_full, preferred_element_type=jnp.float32)
    hidden = (jax.nn.silu(gate) * upper).astype(jnp.bfloat16)
    result = middle + jnp.dot(hidden, wd_full, preferred_element_type=jnp.float32)
    block_output = result.astype(jnp.bfloat16)[None]
    grad_low = cotangent[0]
    grad_rows = grad_low.astype(jnp.float32)
    down_grad = jnp.einsum("tf,td->fd", hidden, grad_low, preferred_element_type=jnp.float32)
    grad_hidden = jnp.einsum("td,fd->tf", grad_low, wd_full, preferred_element_type=jnp.float32)
    sigma = jax.nn.sigmoid(gate)
    gate_low = (grad_hidden * upper * sigma * (1.0 + gate * (1.0 - sigma))).astype(jnp.bfloat16)
    upper_low = (grad_hidden * gate * sigma).astype(jnp.bfloat16)
    gate_grad = jnp.einsum(
        "td,tf->df", normed_two_low, gate_low, preferred_element_type=jnp.float32
    )
    up_grad = jnp.einsum("td,tf->df", normed_two_low, upper_low, preferred_element_type=jnp.float32)
    grad_normed_two = jnp.einsum(
        "tf,df->td", gate_low, wg_full, preferred_element_type=jnp.float32
    ) + jnp.einsum("tf,df->td", upper_low, wu_full, preferred_element_type=jnp.float32)
    grad_middle_norm, second_gain_grad = norm_backward(
        grad_normed_two, unit_two, scale_two, gain_two
    )
    grad_middle = grad_rows + grad_middle_norm
    grad_branch = grad_middle.astype(jnp.bfloat16)
    output_grad = jnp.einsum(
        "tc,td->cd", heads_flat, grad_branch, preferred_element_type=jnp.float32
    )
    grad_heads = (
        jnp.einsum("td,cd->tc", grad_branch, wo_full, preferred_element_type=jnp.float32)
        .astype(jnp.bfloat16)
        .reshape(token_count, QH, HD)
    )
    grad_head_rows = lax.all_to_all(grad_heads, "seq", split_axis=1, concat_axis=0, tiled=True)
    grad_blocks = grad_head_rows.reshape(count, block, pair_count, group, HD)

    def backward_block(carry, items):
        key_acc, value_acc = carry
        query_block, index_block, start_block, grad_block, log_block = items
        scores = block_scores(query_block, index_block, start_block)
        probs = jnp.exp(scores - log_block)
        probs_low = probs.astype(jnp.bfloat16)
        grad_probs = jnp.einsum(
            "bkgd,tkd->kgbt", grad_block, value_all, preferred_element_type=jnp.float32
        )
        grad_scores = (
            probs * (grad_probs - jnp.sum(probs * grad_probs, -1, keepdims=True))
        ).astype(jnp.bfloat16)
        query_grad_block = (
            jnp.einsum("kgbt,tkd->bkgd", grad_scores, key_all, preferred_element_type=jnp.float32)
            * factor
        )
        key_acc = (
            key_acc
            + jnp.einsum(
                "kgbt,bkgd->tkd", grad_scores, query_block, preferred_element_type=jnp.float32
            )
            * factor
        )
        value_acc = value_acc + jnp.einsum(
            "kgbt,bkgd->tkd", probs_low, grad_block, preferred_element_type=jnp.float32
        )
        return ((key_acc, value_acc), query_grad_block.reshape(block, head_count, HD))

    empty = jnp.zeros((2 * half_len, pair_count, HD), jnp.float32)
    (key_acc, value_acc), query_grad_blocks = lax.scan(
        backward_block,
        (empty, empty),
        (query_blocks, index_blocks, start_blocks, grad_blocks, log_totals),
    )
    key_back, value_back = (
        shifted(key_acc[:half_len].astype(jnp.bfloat16), "fsdp", -1).astype(jnp.float32),
        shifted(value_acc[:half_len].astype(jnp.bfloat16), "fsdp", -1).astype(jnp.float32),
    )
    key_local = key_acc[half_len:] + key_back
    value_local = value_acc[half_len:] + value_back
    query_grad_heads = query_grad_blocks.reshape(half_len, head_count, HD)
    grad_query_tok, grad_key_tok, grad_value_tok = (
        lax.all_to_all(
            query_grad_heads.astype(jnp.bfloat16), "seq", split_axis=0, concat_axis=1, tiled=True
        ).astype(query_grad_heads.dtype),
        lax.all_to_all(
            key_local.astype(jnp.bfloat16), "seq", split_axis=0, concat_axis=1, tiled=True
        ).astype(key_local.dtype),
        lax.all_to_all(
            value_local.astype(jnp.bfloat16), "seq", split_axis=0, concat_axis=1, tiled=True
        ).astype(value_local.dtype),
    )
    if repeat > 1:
        grad_key_tok = grad_key_tok.reshape(token_count, KVH, repeat, HD).sum(2)
        grad_value_tok = grad_value_tok.reshape(token_count, KVH, repeat, HD).sum(2)
    query_lin_grad = (
        rotate_back(grad_query_tok, cosine, sine).astype(jnp.bfloat16).reshape(token_count, QH * HD)
    )
    key_lin_grad = (
        rotate_back(grad_key_tok, cosine, sine).astype(jnp.bfloat16).reshape(token_count, KVH * HD)
    )
    value_lin_grad = grad_value_tok.astype(jnp.bfloat16).reshape(token_count, KVH * HD)
    query_grad = jnp.einsum(
        "td,tc->dc", normed_low, query_lin_grad, preferred_element_type=jnp.float32
    )
    key_grad = jnp.einsum("td,tc->dc", normed_low, key_lin_grad, preferred_element_type=jnp.float32)
    value_grad = jnp.einsum(
        "td,tc->dc", normed_low, value_lin_grad, preferred_element_type=jnp.float32
    )
    grad_normed_one = jnp.einsum(
        "tc,dc->td", query_lin_grad, wq_full, preferred_element_type=jnp.float32
    )
    grad_normed_one = grad_normed_one + jnp.einsum(
        "tc,dc->td", key_lin_grad, wk_full, preferred_element_type=jnp.float32
    )
    grad_normed_one = grad_normed_one + jnp.einsum(
        "tc,dc->td", value_lin_grad, wv_full, preferred_element_type=jnp.float32
    )
    grad_rows_one, first_gain_grad = norm_backward(grad_normed_one, unit_one, scale_one, gain_one)
    input_grad = (grad_middle + grad_rows_one).astype(jnp.bfloat16)[None]
    pieces = (
        lax.psum_scatter(
            first_gain_grad.astype(jnp.bfloat16), "fsdp", scatter_dimension=0, tiled=True
        ).astype(jnp.float32),
        lax.psum_scatter(
            query_grad.astype(jnp.bfloat16), "fsdp", scatter_dimension=0, tiled=True
        ).astype(jnp.float32),
        lax.psum_scatter(
            key_grad.astype(jnp.bfloat16), "fsdp", scatter_dimension=0, tiled=True
        ).astype(jnp.float32),
        lax.psum_scatter(
            value_grad.astype(jnp.bfloat16), "fsdp", scatter_dimension=0, tiled=True
        ).astype(jnp.float32),
        lax.psum_scatter(
            output_grad.astype(jnp.bfloat16), "fsdp", scatter_dimension=0, tiled=True
        ).astype(jnp.float32),
        lax.psum_scatter(
            second_gain_grad.astype(jnp.bfloat16), "fsdp", scatter_dimension=0, tiled=True
        ).astype(jnp.float32),
        lax.psum_scatter(
            gate_grad.astype(jnp.bfloat16), "fsdp", scatter_dimension=0, tiled=True
        ).astype(jnp.float32),
        lax.psum_scatter(
            up_grad.astype(jnp.bfloat16), "fsdp", scatter_dimension=0, tiled=True
        ).astype(jnp.float32),
        lax.psum_scatter(
            down_grad.astype(jnp.bfloat16), "fsdp", scatter_dimension=0, tiled=True
        ).astype(jnp.float32),
    )
    shares = (
        lax.psum(pieces[0].astype(jnp.bfloat16), "seq").astype(jnp.float32),
        lax.psum(pieces[1].astype(jnp.bfloat16), "seq").astype(jnp.float32),
        lax.psum(pieces[2].astype(jnp.bfloat16), "seq").astype(jnp.float32),
        lax.psum(pieces[3].astype(jnp.bfloat16), "seq").astype(jnp.float32),
        lax.psum(pieces[4].astype(jnp.bfloat16), "seq").astype(jnp.float32),
        lax.psum(pieces[5].astype(jnp.bfloat16), "seq").astype(jnp.float32),
        lax.psum(pieces[6].astype(jnp.bfloat16), "seq").astype(jnp.float32),
        lax.psum(pieces[7].astype(jnp.bfloat16), "seq").astype(jnp.float32),
        lax.psum(pieces[8].astype(jnp.bfloat16), "seq").astype(jnp.float32),
    )
    return (
        block_output,
        input_grad,
        shares[0],
        shares[1],
        shares[2],
        shares[3],
        shares[4],
        shares[5],
        shares[6],
        shares[7],
        shares[8],
    )


def plain_solution(mesh):
    placed = (
        P("fsdp", "seq", None),
        P("fsdp", "seq"),
        P("fsdp"),
        P("fsdp", None),
        P("fsdp", None),
        P("fsdp", None),
        P("fsdp", None),
        P("fsdp"),
        P("fsdp", None),
        P("fsdp", None),
        P("fsdp", None),
        P("fsdp", "seq", None),
    )
    return jax.shard_map(
        plain_body,
        mesh=mesh,
        in_specs=placed,
        out_specs=(
            P("fsdp", "seq", None),
            P("fsdp", "seq", None),
            P("fsdp"),
            P("fsdp", None),
            P("fsdp", None),
            P("fsdp", None),
            P("fsdp", None),
            P("fsdp"),
            P("fsdp", None),
            P("fsdp", None),
            P("fsdp", None),
        ),
        check_vma=False,
    )
```

```python
import functools
import math

import jax
import jax.numpy as jnp
from jax import lax
from jax.experimental import pallas as pl
from jax.experimental.pallas import tpu as pltpu
from jax.sharding import Mesh
from jax.sharding import PartitionSpec as P

QH = 16
KVH = 8
HD = 96


THETA = 100000.0
EPS = 1e-05
LOW = jnp.bfloat16
F32 = jnp.float32
NEG = -1e30
LN2 = math.log(2.0)


def contract(left, right, left_axis, right_axis):
    return lax.dot_general(
        left, right, (((left_axis,), (right_axis,)), ((), ())), preferred_element_type=F32
    )


def hide(scores, kind, first, second, query_start, key_start):
    if kind == "plain":
        return scores
    keys, queries = scores.shape
    key = key_start + lax.broadcasted_iota(jnp.int32, (keys, queries), 0)
    if kind == "keys":
        return jnp.where(key >= first, scores, NEG)
    query = query_start + lax.broadcasted_iota(jnp.int32, (1, queries), 1)
    if kind == "causal":
        return jnp.where(key <= query, scores, NEG)
    if kind == "queries":
        return scores + jnp.where(query >= second, NEG, 0.0)
    start = jnp.where(query >= second, second, jnp.where(query >= first, first, 0))
    return jnp.where((key >= start) & (key <= query), scores, NEG)


def halves_of(size):
    return slice(0, size // 2), slice(size // 2, size)


def slot_of(block, count):
    return (block % (count // 2)) * 2 + block // (count // 2)


def forward_kernel(
    scalars,
    own_ref,
    other_ref,
    low_ref,
    full_ref,
    log_ref,
    query_s,
    key_s,
    value_s,
    top_s,
    total_s,
    mixed_s,
    *,
    size,
    count,
):
    half = scalars[0]
    first = scalars[1]
    second = scalars[2]
    here = pl.program_id(0)
    per_half = count // 2

    @pl.when(here == 0)
    def _():
        for ref, side in ((own_ref, half), (other_ref, 1 - half)):
            for step in range(per_half):
                block = side * per_half + step
                columns = slice(step * size, (step + 1) * size)
                query_s[block] = ref[0:HD, columns]
                key_s[block] = ref[HD : 2 * HD, columns].T
                value_s[block] = ref[2 * HD : 3 * HD, columns]

    query = query_s[here]
    top_s[...] = jnp.full_like(top_s, NEG)
    total_s[...] = jnp.zeros_like(total_s)
    mixed_s[...] = jnp.zeros_like(mixed_s)

    def add_block(block, kind):
        keys, values = key_s[block], value_s[block]
        parts = halves_of(size)
        all_scores = [contract(keys, query[:, part], 1, 0) for part in parts]
        for part, scores in zip(parts, all_scores):
            scores = hide(
                scores, kind, first, second, here * size + part.start, block * size
            )
            old_top = top_s[:, part]
            top = jnp.maximum(old_top, jnp.max(scores, 0, keepdims=True))
            expo = jnp.exp2(scores - top)
            scale = jnp.exp2(old_top - top)
            top_s[:, part] = top
            total_s[:, part] = total_s[:, part] * scale + jnp.sum(expo, 0, keepdims=True)
            mixed_s[:, part] = mixed_s[:, part] * scale + contract(
                values, expo.astype(LOW), 1, 0
            )

    last = count - 1

    @pl.when(here == 0)
    def _():
        add_block(here, "full")

    @pl.when((here > 0) & (here < last))
    def _():
        add_block(0, "keys")

        @pl.loop(1, here)
        def _(block):
            add_block(block, "plain")

        add_block(here, "causal")

    @pl.when(here == last)
    def _():
        add_block(0, "full")

        @pl.loop(1, last)
        def _(block):
            add_block(block, "queries")

        add_block(last, "full")

    total = total_s[...]
    result = mixed_s[...] / total
    full_ref[0] = result
    low_ref[0] = result.astype(LOW)
    log_ref[0] = top_s[...] + jnp.log2(total)


def backward_kernel(
    scalars,
    own_ref,
    other_ref,
    grad_ref,
    full_ref,
    log_ref,
    kept_ref,
    leaving_ref,
    query_s,
    key_s,
    value_s,
    delta_s,
    query_grad_s,
    key_grad_s,
    value_grad_s,
    *,
    size,
    count,
):
    half = scalars[0]
    first = scalars[1]
    second = scalars[2]
    here = pl.program_id(0)
    per_half = count // 2

    @pl.when(here == 0)
    def _():
        for ref, side in ((own_ref, half), (other_ref, 1 - half)):
            for step in range(per_half):
                block = side * per_half + step
                columns = slice(step * size, (step + 1) * size)
                query_s[block] = ref[0:HD, columns]
                key_s[block] = ref[HD : 2 * HD, columns]
                value_s[block] = ref[2 * HD : 3 * HD, columns].T
        for block in range(count):
            delta_s[block] = jnp.sum(
                grad_ref[slot_of(block, count)].astype(F32) * full_ref[block], 0, keepdims=True
            )
        query_grad_s[...] = jnp.zeros_like(query_grad_s)

    key_grad_s[...] = jnp.zeros_like(key_grad_s)
    value_grad_s[...] = jnp.zeros_like(value_grad_s)
    key = key_s[here]
    key_rows = key.T
    value_rows = value_s[here]

    def add_block(block, kind):
        query = query_s[block]
        grad = grad_ref[slot_of(block, count)]
        log_total, delta = log_ref[block], delta_s[block]
        parts = halves_of(size)
        products = [
            (contract(key_rows, query[:, part], 1, 0), contract(value_rows, grad[:, part], 1, 0))
            for part in parts
        ]
        for part, (scores, grad_probs) in zip(parts, products):
            scores = hide(
                scores, kind, first, second, block * size + part.start, here * size
            )
            probs = jnp.exp2(scores - log_total[:, part])
            grad_scores = (probs * (grad_probs - delta[:, part])).astype(LOW)
            value_grad_s[...] += contract(grad[:, part], probs.astype(LOW), 1, 1)
            key_grad_s[...] += contract(query[:, part], grad_scores, 1, 1)
            query_grad_s[block, :, part] += contract(key, grad_scores, 1, 0)

    last = count - 1

    @pl.when(here == 0)
    def _():
        add_block(0, "full")

        @pl.loop(1, last)
        def _(block):
            add_block(block, "keys")

        add_block(last, "full")

    @pl.when((here > 0) & (here < last))
    def _():
        add_block(here, "causal")

        @pl.loop(here + 1, last)
        def _(block):
            add_block(block, "plain")

        add_block(last, "queries")

    @pl.when(here == last)
    def _():
        add_block(last, "full")

    side = here // per_half
    columns = pl.ds(pl.multiple_of((here % per_half) * size, size), size)

    def write(out_ref):
        out_ref[0:HD, columns] = (query_grad_s[here] * HD**-0.5).astype(LOW)
        out_ref[HD : 2 * HD, columns] = (key_grad_s[...] * LN2).astype(LOW)
        out_ref[2 * HD : 3 * HD, columns] = value_grad_s[...].astype(LOW)

    @pl.when(side == half)
    def _():
        write(kept_ref)

    @pl.when(side != half)
    def _():
        write(leaving_ref)


def attend_forward(scalars, own, other, size):
    count = 2 * own.shape[1] // size
    whole = lambda shape: pl.BlockSpec(shape, lambda i, s: (0,) * len(shape))
    pairs = count * (count + 1) // 2
    return pl.pallas_call(
        functools.partial(forward_kernel, size=size, count=count),
        grid_spec=pltpu.PrefetchScalarGridSpec(
            num_scalar_prefetch=1,
            grid=(count,),
            in_specs=[whole(own.shape), whole(other.shape)],
            out_specs=[
                pl.BlockSpec(
                    (1, HD, size), lambda i, s: (slot_of(i, count), 0, 0)
                ),
                pl.BlockSpec((1, HD, size), lambda i, s: (i, 0, 0)),
                pl.BlockSpec((1, 1, size), lambda i, s: (i, 0, 0)),
            ],
            scratch_shapes=[
                pltpu.VMEM((count, HD, size), LOW),
                pltpu.VMEM((count, size, HD), LOW),
                pltpu.VMEM((count, HD, size), LOW),
                pltpu.VMEM((1, size), F32),
                pltpu.VMEM((1, size), F32),
                pltpu.VMEM((HD, size), F32),
            ],
        ),
        out_shape=[
            jax.ShapeDtypeStruct((count, HD, size), LOW),
            jax.ShapeDtypeStruct((count, HD, size), F32),
            jax.ShapeDtypeStruct((count, 1, size), F32),
        ],
        compiler_params=pltpu.CompilerParams(
            dimension_semantics=("arbitrary",), vmem_limit_bytes=32 * 2**20
        ),
        cost_estimate=pl.CostEstimate(
            flops=pairs * size * size * HD * 32,
            bytes_accessed=10 * 2**20,
            transcendentals=pairs * size * size,
        ),
        name="attend_forward",
    )(scalars, own, other)


def attend_backward(scalars, own, other, grad, full, log_total):
    count, _, size = grad.shape
    whole = lambda shape: pl.BlockSpec(shape, lambda i, s: (0,) * len(shape))
    pairs = count * (count + 1) // 2
    out_shape = own.shape
    return pl.pallas_call(
        functools.partial(backward_kernel, size=size, count=count),
        grid_spec=pltpu.PrefetchScalarGridSpec(
            num_scalar_prefetch=1,
            grid=(count,),
            in_specs=[
                whole(own.shape),
                whole(other.shape),
                whole(grad.shape),
                whole(full.shape),
                whole(log_total.shape),
            ],
            out_specs=[whole(out_shape)] * 2,
            scratch_shapes=[
                pltpu.VMEM((count, HD, size), LOW),
                pltpu.VMEM((count, HD, size), LOW),
                pltpu.VMEM((count, size, HD), LOW),
                pltpu.VMEM((count, 1, size), F32),
                pltpu.VMEM((count, HD, size), F32),
                pltpu.VMEM((HD, size), F32),
                pltpu.VMEM((HD, size), F32),
            ],
        ),
        out_shape=[jax.ShapeDtypeStruct(out_shape, LOW)] * 2,
        compiler_params=pltpu.CompilerParams(
            dimension_semantics=("arbitrary",), vmem_limit_bytes=32 * 2**20
        ),
        cost_estimate=pl.CostEstimate(
            flops=pairs * size * size * HD * 42,
            bytes_accessed=16 * 2**20,
            transcendentals=pairs * size * size,
        ),
        name="attend_backward",
    )(scalars, own, other, grad, full, log_total)


def place_rows_kernel(order, *refs):
    pieces, out_ref = refs[:-1], refs[-1]
    size = pieces[0].shape[0]
    for index, piece in enumerate(pieces):
        start = pl.multiple_of(order[index] * size, size)
        out_ref[pl.ds(start, size), :] = piece[...].astype(F32)


def place_rows(order, pieces):
    size, width = pieces[0].shape
    total = size * len(pieces)
    step = 512
    return pl.pallas_call(
        place_rows_kernel,
        grid_spec=pltpu.PrefetchScalarGridSpec(
            num_scalar_prefetch=1,
            grid=(width // step,),
            in_specs=[pl.BlockSpec((size, step), lambda i, s: (0, i)) for _ in pieces],
            out_specs=pl.BlockSpec((total, step), lambda i, s: (0, i)),
        ),
        out_shape=jax.ShapeDtypeStruct((total, width), F32),
        compiler_params=pltpu.CompilerParams(vmem_limit_bytes=24 * 2**20),
        cost_estimate=pl.CostEstimate(
            flops=0, bytes_accessed=total * width * 6, transcendentals=0
        ),
        name="place_rows",
    )(order, *pieces)


def place_columns_kernel(order, gain_ref, gate_w_ref, up_w_ref, *refs):
    count = (len(refs) - 3) // 2
    gates, ups = refs[:count], refs[count : 2 * count]
    gate_ref, up_ref, sum_ref = refs[2 * count :]
    size = gates[0].shape[1]
    gain = gain_ref[...]
    total = jnp.zeros((gate_ref.shape[0], size), F32)
    for index in range(count):
        columns = pl.ds(pl.multiple_of(order[index] * size, size), size)
        gate, up = gates[index][...].astype(F32), ups[index][...].astype(F32)
        total += gate * gate_w_ref[:, columns].astype(F32)
        total += up * up_w_ref[:, columns].astype(F32)
        gate_ref[:, columns] = gate * gain
        up_ref[:, columns] = up * gain

    @pl.when(pl.program_id(0) == 0)
    def _():
        sum_ref[...] = jnp.zeros_like(sum_ref)

    sum_ref[...] += jnp.sum(total, 1, keepdims=True)


def place_columns(order, gain, gate_weight, up_weight, gates, ups, shards):
    rows, width = gate_weight.shape
    span = width // shards
    size = span // len(gates)
    wide = pl.BlockSpec((rows, span), lambda i, s: (0, i))
    thin = pl.BlockSpec((rows, 1), lambda i, s: (0, 0))
    pieces = [pl.BlockSpec((rows, size), lambda i, s: (0, i)) for _ in (*gates, *ups)]
    return pl.pallas_call(
        place_columns_kernel,
        grid_spec=pltpu.PrefetchScalarGridSpec(
            num_scalar_prefetch=1,
            grid=(shards,),
            in_specs=[thin, wide, wide, *pieces],
            out_specs=[wide, wide, thin],
        ),
        out_shape=[
            jax.ShapeDtypeStruct((rows, width), F32),
            jax.ShapeDtypeStruct((rows, width), F32),
            jax.ShapeDtypeStruct((rows, 1), F32),
        ],
        compiler_params=pltpu.CompilerParams(
            dimension_semantics=("arbitrary",), vmem_limit_bytes=24 * 2**20
        ),
        cost_estimate=pl.CostEstimate(
            flops=rows * width * 6, bytes_accessed=rows * width * 16, transcendentals=0
        ),
        name="place_columns",
    )(order, gain, gate_weight, up_weight, *gates, *ups)


def place_heads_kernel(gain_ref, query_w, key_w, value_w, all_ref, query_ref, key_ref, value_ref, sum_ref):
    rows = gain_ref.shape[0]
    wide = query_ref.shape[1] // KVH
    gain = gain_ref[...]
    total = jnp.zeros((rows, 4 * HD), F32)
    pieces = [all_ref[i * rows : (i + 1) * rows, :].astype(F32) for i in range(KVH)]
    for start in range(0, KVH, 2):
        value = jnp.concatenate([piece[:, :wide] for piece in pieces[start : start + 2]], 1)
        columns = slice(start * wide, (start + 2) * wide)
        total += value * query_w[:, columns].astype(F32)
        query_ref[:, columns] = value * gain
    for first, weight, out_ref in ((wide, key_w, key_ref), (wide + HD, value_w, value_ref)):
        for start in range(0, KVH, 4):
            value = jnp.concatenate(
                [piece[:, first : first + HD] for piece in pieces[start : start + 4]], 1
            )
            columns = slice(start * HD, (start + 4) * HD)
            total += value * weight[:, columns].astype(F32)
            out_ref[:, columns] = value * gain
    sum_ref[...] = jnp.sum(total, 1, keepdims=True)


def place_heads(gain, query_weight, key_weight, value_weight, pieces):
    weights = (query_weight, key_weight, value_weight)
    rows = gain.shape[0]
    return pl.pallas_call(
        place_heads_kernel,
        out_shape=[jax.ShapeDtypeStruct(weight.shape, F32) for weight in weights]
        + [jax.ShapeDtypeStruct((rows, 1), F32)],
        compiler_params=pltpu.CompilerParams(vmem_limit_bytes=32 * 2**20),
        cost_estimate=pl.CostEstimate(
            flops=rows * 3072 * 4, bytes_accessed=rows * 3072 * 8, transcendentals=0
        ),
        name="place_heads",
    )(gain, *weights, pieces)


def merge_kernel(scalars, kept_ref, came_ref, cosine_ref, sine_ref, out_ref, split_ref):
    lead = scalars[0] == 0
    lines, _, size = split_ref.shape
    for line in range(lines):
        columns = slice(line * size, (line + 1) * size)
        kept = kept_ref[:, columns].astype(F32)
        came = came_ref[:, columns].astype(F32)
        cosine, sine = cosine_ref[:, columns], sine_ref[:, columns]
        joint = kept[HD:] + came[HD:]
        first = jnp.where(lead, kept[:HD], came[:HD])
        second = jnp.where(lead, came[:HD], kept[:HD])
        turned = []
        for value in (first, second, joint[:HD]):
            low, high = value[: HD // 2], value[HD // 2 :]
            turned.append(low * cosine + high * sine)
            turned.append(high * cosine - low * sine)
        turned.append(joint[HD:])
        result = jnp.concatenate([part.astype(LOW) for part in turned], 0)
        out_ref[:, columns] = result
        split_ref[line] = result


def merge(scalars, kept, came, cosine, sine, lines):
    tokens = kept.shape[1]
    whole = lambda value: pl.BlockSpec(value.shape, lambda i, s: (0,) * len(value.shape))
    outs = [
        jax.ShapeDtypeStruct((4 * HD, tokens), LOW),
        jax.ShapeDtypeStruct((lines, 4 * HD, tokens // lines), LOW),
    ]
    return pl.pallas_call(
        merge_kernel,
        grid_spec=pltpu.PrefetchScalarGridSpec(
            num_scalar_prefetch=1,
            grid=(1,),
            in_specs=[whole(value) for value in (kept, came, cosine, sine)],
            out_specs=[whole(value) for value in outs],
        ),
        out_shape=outs,
        compiler_params=pltpu.CompilerParams(vmem_limit_bytes=24 * 2**20),
        cost_estimate=pl.CostEstimate(
            flops=tokens * HD * 24, bytes_accessed=tokens * HD * 30, transcendentals=0
        ),
        name="merge",
    )(scalars, kept, came, cosine, sine)


def pack_kernel(scalars, gain_ref, query_ref, key_ref, value_ref, *outs):
    core = scalars[3]
    gain = gain_ref[...]
    wide = query_ref.shape[1] // KVH
    span = wide + 2 * HD
    for which in range(2):

        @pl.when(core == which)
        def _():
            for line in range(KVH // 2):
                head = 2 * line + which
                value = jnp.concatenate(
                    [
                        query_ref[:, head * wide : (head + 1) * wide].astype(F32),
                        key_ref[:, head * HD : (head + 1) * HD].astype(F32),
                        value_ref[:, head * HD : (head + 1) * HD].astype(F32),
                    ],
                    1,
                )
                place = (line % 2) * span
                outs[line // 2][:, place : place + span] = (value * gain).astype(LOW)


def pack(scalars, gain, query_weight, key_weight, value_weight):
    rows, width = query_weight.shape
    whole = lambda value: pl.BlockSpec(value.shape, lambda i, s: (0, 0))
    weights = (gain, query_weight, key_weight, value_weight)
    outs = [jax.ShapeDtypeStruct((rows, width // 2), LOW)] * 2
    return pl.pallas_call(
        pack_kernel,
        grid_spec=pltpu.PrefetchScalarGridSpec(
            num_scalar_prefetch=1,
            grid=(1,),
            in_specs=[whole(value) for value in weights],
            out_specs=[whole(value) for value in outs],
        ),
        out_shape=outs,
        compiler_params=pltpu.CompilerParams(vmem_limit_bytes=24 * 2**20),
        cost_estimate=pl.CostEstimate(
            flops=rows * width, bytes_accessed=rows * width * 6, transcendentals=0
        ),
        name="pack",
    )(scalars, *weights)


def spread_kernel(scalars, lin_ref, cosine_ref, sine_ref, own_ref, leaving_ref):
    cosine, sine = cosine_ref[...], sine_ref[...]

    def turn(start, factor):
        low = lin_ref[start : start + HD // 2, :]
        high = lin_ref[start + HD // 2 : start + HD, :]
        turned = ((low * cosine - high * sine) * factor, (high * cosine + low * sine) * factor)
        return jnp.concatenate([part.astype(LOW) for part in turned], 0)

    lead = scalars[0] == 0
    first, second = turn(0, HD**-0.5 / LN2), turn(HD, HD**-0.5 / LN2)

    @pl.when(lead)
    def _():
        own_ref[0:HD] = first
        leaving_ref[0:HD] = second

    @pl.when(jnp.logical_not(lead))
    def _():
        own_ref[0:HD] = second
        leaving_ref[0:HD] = first

    key = turn(2 * HD, 1.0)
    value = lin_ref[3 * HD : 4 * HD].astype(LOW)
    for ref in (own_ref, leaving_ref):
        ref[HD : 2 * HD] = key
        ref[2 * HD : 3 * HD] = value


def spread(scalars, lin, cosine, sine):
    tokens = lin.shape[1]
    step = 512
    column = lambda rows: pl.BlockSpec((rows, step), lambda i, s: (0, i))
    return pl.pallas_call(
        spread_kernel,
        grid_spec=pltpu.PrefetchScalarGridSpec(
            num_scalar_prefetch=1,
            grid=(tokens // step,),
            in_specs=[column(4 * HD), column(HD // 2), column(HD // 2)],
            out_specs=[column(3 * HD)] * 2,
        ),
        out_shape=[jax.ShapeDtypeStruct((3 * HD, tokens), LOW)] * 2,
        compiler_params=pltpu.CompilerParams(vmem_limit_bytes=24 * 2**20),
        cost_estimate=pl.CostEstimate(
            flops=tokens * HD * 24, bytes_accessed=tokens * HD * 36, transcendentals=0
        ),
        name="spread",
    )(scalars, lin, cosine, sine)


def swap(value, axis):
    return lax.ppermute(value, axis, [(0, 1), (1, 0)])


def swap_near(value):
    return lax.ppermute(value, "z", [(0, 1), (1, 0), (2, 3), (3, 2)])


def swap_far(value):
    return lax.ppermute(value, "z", [(0, 2), (2, 0), (1, 3), (3, 1)])


def tie(*values):
    return lax.optimization_barrier(values)


def in_order(place, own, other):
    return (jnp.where(place == 0, own, other), jnp.where(place == 0, other, own))


def both(place, own, other):
    return jnp.concatenate(in_order(place, own, other), 0)


def spread_out(value, first, second):
    other = swap(value, first)
    pair = jnp.stack(in_order(lax.axis_index(first), value, other))
    return pair, swap(pair, second)


def placed(pair, other, second):
    pairs = in_order(lax.axis_index(second), pair, other)
    grid = jnp.stack(pairs, 0 if second == "y" else 1)
    return grid.reshape(-1, *grid.shape[3:])


def pick(array, axis, at):
    return lax.dynamic_index_in_dim(array, at, axis, keepdims=False)


def halve(value, axis, along=0):
    at = lax.axis_index(axis)
    return pick(value, along, at), swap(pick(value, along, 1 - at), axis)


def halve_x(value):
    return halve(value.reshape(2, 2, -1, value.shape[-1]), "x", 1)


def halve_y(value):
    return halve(value.reshape(2, 2, -1, value.shape[-1]), "y", 0)


def fast_body(
    tokens,
    positions,
    first_gain,
    query_weight,
    key_weight,
    value_weight,
    output_weight,
    second_gain,
    gate_weight,
    up_weight,
    down_weight,
    cotangent,
):
    seq = ("z", "c")
    fsdp = ("y", "x")
    z, core, half = lax.axis_index("z"), lax.axis_index("c"), lax.axis_index("x")
    near = z % 2
    lines = lax.axis_size("z")
    seq_count = 2 * lines
    shards = lax.axis_size("y") * 2
    spot = z * 2 + core
    quarter = near * 2 + core
    rows = tokens[0]
    count, width = rows.shape
    chip_count = 2 * count
    half_len = count * seq_count
    seq_len = 2 * half_len

    begins = jnp.where(
        (spot == 0) & (half == 0),
        count - 1 - positions[0, count - 1],
        half * half_len + spot * count - positions[0, 0],
    )
    ends = begins + (seq_len - count)
    scalars = jnp.stack([half, begins, ends, core]).astype(jnp.int32)

    gain_one = first_gain.astype(F32)[:, None]
    gain_two = second_gain.astype(F32)[:, None]

    def row_scale(value):
        return lax.rsqrt(jnp.mean(value * value, -1, keepdims=True) + EPS)

    take = functools.partial(lax.dynamic_slice_in_dim, axis=1)
    take_rows = functools.partial(lax.dynamic_slice_in_dim, axis=0)
    gather = lambda value, axes: lax.all_gather(value, axes, axis=0, tiled=True)
    own_rows = rows.astype(F32)
    own_unit_scale = row_scale(own_rows)
    own_unit = own_rows * own_unit_scale
    units = gather(own_unit.astype(LOW), seq)
    wide = QH // KVH * HD
    qkv_shard = (
        jnp.concatenate(
            [
                take(query_weight, spot * wide, wide),
                take(key_weight, spot * HD, HD),
                take(value_weight, spot * HD, HD),
            ],
            1,
        ).astype(F32)
        * gain_one
    ).astype(LOW)
    out_rows = output_weight.shape[0] // 2
    out_shard = take_rows(output_weight, core * out_rows, out_rows)
    piece = down_weight.shape[0] // 4
    down_shard = take_rows(down_weight, quarter * piece, piece)
    gate_shard, up_shard = (
        (
            jnp.concatenate(
                [
                    take(weight, shard * 4 * piece + quarter * piece, piece)
                    for shard in range(shards)
                ],
                1,
            ).astype(F32)
            * gain_two
        ).astype(LOW)
        for weight in (gate_weight, up_weight)
    )
    side = lax.axis_index("y")
    qkv_pair = jnp.stack(in_order(half, qkv_shard, swap(qkv_shard, "x")))
    gate_pair = jnp.stack(in_order(half, gate_shard, swap(gate_shard, "x")))
    up_pair = jnp.stack(in_order(side, up_shard, swap(up_shard, "y")))
    qkv_pair, gate_pair, up_pair = tie(qkv_pair, gate_pair, up_pair)
    qkv_w = placed(qkv_pair, swap(qkv_pair, "y"), "y")
    gate_pair, up_pair = (gate_pair, swap(gate_pair, "y")), (up_pair, swap(up_pair, "x"))

    place = half * half_len + jnp.arange(half_len, dtype=jnp.int32)
    start = jnp.where(place >= ends, ends, jnp.where(place >= begins, begins, 0))
    freq = THETA ** (-(jnp.arange(HD // 2, dtype=F32) * 2.0 / HD))
    angle = freq[:, None] * (place - start).astype(F32)[None, :]
    cosine, sine = jnp.cos(angle), jnp.sin(angle)
    chip_rows = both(core, rows, swap(rows, "c"))
    units, own_cot, chip_rows = tie(units, cotangent[0], chip_rows)
    own, leaving = spread(scalars, contract(qkv_w, units, 0, 1), cosine, sine)

    near_cot = swap_near(own_cot)
    other, out_shard, down_shard, near_cot, chip_cot, gate_pair, up_pair = tie(
        swap(leaving, "x"),
        out_shard,
        down_shard,
        near_cot,
        both(core, own_cot, swap(own_cot, "c")),
        gate_pair,
        up_pair,
    )
    out_w = gather(out_shard, fsdp)
    down_w = gather(down_shard, fsdp)
    near_other = swap(near_cot, "c")
    head_low, head_full, log_total = attend_forward(scalars, own, other, chip_count)
    exchange = lambda value: lax.all_to_all(
        value, ("z", "x"), split_axis=0, concat_axis=0, tiled=True
    )
    head_low, near_other = tie(head_low, near_other)
    lead_shard, tail_shard = pack(scalars, gain_one, query_weight, key_weight, value_weight)
    heads, gate_w, up_w, near_cot, lead_shard = tie(
        exchange(head_low),
        placed(*gate_pair, "y"),
        placed(*up_pair, "x"),
        jnp.concatenate([near_cot, near_other], 0),
        lead_shard,
    )
    lead_w = gather(lead_shard, fsdp)
    heads = heads.reshape(QH // 2 * HD, chip_count)

    mine_of = lambda value: take_rows(value, core * count, count)
    theirs_of = lambda value: take_rows(value, (1 - core) * count, count)
    branch = contract(heads, out_w, 0, 0).astype(LOW)
    middle = chip_rows.astype(F32) + (branch.astype(F32) + swap(branch, "c").astype(F32))
    middle_scale = row_scale(middle)
    chip_unit = middle * middle_scale
    own_middle, own_scale, own_middle_unit = (
        mine_of(middle),
        mine_of(middle_scale),
        mine_of(chip_unit),
    )
    chip_unit = chip_unit.astype(LOW)
    near_unit = swap_near(mine_of(chip_unit))

    def feed(unit):
        gate, upper = contract(unit, gate_w, 1, 0), contract(unit, up_w, 1, 0)
        sigma = jax.nn.sigmoid(gate)
        silu = gate * sigma
        return (silu * upper).astype(LOW), (gate, upper, sigma, silu)

    def feed_back(cot, kept):
        gate, upper, sigma, silu = kept
        grad_hidden = contract(cot, down_w, 1, 1)
        gate_low = (grad_hidden * upper * sigma * (1.0 + gate * (1.0 - sigma))).astype(LOW)
        upper_low = (grad_hidden * silu).astype(LOW)
        part = contract(gate_low, gate_w, 1, 1) + contract(upper_low, up_w, 1, 1)
        return gate_low, upper_low, part

    def chip_sum(chip_part, near_part):
        near_sum = near_part[:count].astype(F32) + swap(near_part[count:].astype(LOW), "c")
        own_sum = mine_of(chip_part).astype(F32) + swap(theirs_of(chip_part).astype(LOW), "c")
        return own_sum, near_sum.astype(LOW)

    stack = lambda first, second: jnp.concatenate([first, second], 0)
    scatter = lambda value: lax.psum_scatter(value, fsdp, scatter_dimension=0, tiled=True)
    chip_hidden, chip_kept = feed(chip_unit)
    near_unit, chip_hidden = tie(near_unit, chip_hidden)
    near_unit = jnp.concatenate([near_unit, swap(near_unit, "c")], 0)
    near_hidden, near_kept = feed(near_unit)
    down_part = contract(
        stack(chip_hidden, near_hidden), stack(chip_cot, near_cot), 0, 0
    ).astype(LOW)
    near_cot, down_part = tie(near_cot, down_part)
    near_gate, near_upper, near_part = feed_back(near_cot, near_kept)
    chip_gate, chip_upper, chip_part = feed_back(chip_cot, chip_kept)
    grad_two, near_sum = chip_sum(chip_part, near_part)

    def four(value, near_value):
        return value, swap(value, "c"), near_value, swap(near_value, "c")

    def halves_first(value):
        cut = value.shape[-1] // 2
        return halve_x(value[:, :cut]), halve_y(value[:, cut:])

    def halves_second(firsts):
        return halve(sum(firsts[0]), "y"), halve(sum(firsts[1]), "x")

    def halves_end(seconds):
        return jnp.concatenate([sum(seconds[0]), sum(seconds[1])], 1)

    down_first = halves_first(down_part)
    near_sum, near_gate, near_upper, chip_part = tie(
        near_sum, near_gate, near_upper, chip_part
    )
    grad_came = swap_near(near_sum)
    all_units = stack(chip_unit, near_unit)
    gate_part = contract(all_units, stack(chip_gate, near_gate), 0, 0).astype(LOW)
    up_part = contract(all_units, stack(chip_upper, near_upper), 0, 0).astype(LOW)
    feed_own, feed_near = chip_sum(
        contract(chip_hidden, down_w, 1, 0), contract(near_hidden, down_w, 1, 0)
    )
    gate_part, up_part, down_first, grad_came, feed_near = tie(
        gate_part, up_part, down_first, grad_came, feed_near
    )
    feed_near = swap_near(feed_near)
    down_second = halves_second(down_first)
    grad_two = grad_two + grad_came.astype(F32)
    grad_middle = own_cot.astype(F32) + own_scale * (
        grad_two - own_middle_unit * jnp.mean(grad_two * own_middle_unit, -1, keepdims=True)
    )
    own_branch, lead_w, down_second, gate_part, up_part = tie(
        grad_middle.astype(LOW), lead_w, down_second, gate_part, up_part
    )
    gate_grad, up_grad = scatter(gate_part), scatter(up_part)
    down_grad = halves_end(down_second)
    down_far = swap_far(down_grad)
    grad_branch = both(core, own_branch, swap(own_branch, "c"))
    grad_heads = contract(out_w, grad_branch, 1, 1).astype(LOW)
    grad_heads, grad_branch, down_far = tie(grad_heads, grad_branch, down_far)
    down_sum = down_grad + down_far
    output_part = contract(heads, grad_branch, 1, 0).astype(LOW)
    output_grad = scatter(output_part)
    grad_head, output_part, gate_grad, down_sum = tie(
        exchange(grad_heads.reshape(2 * lines, HD, chip_count)), output_part, gate_grad, down_sum
    )
    down_near = swap_near(down_sum)

    gate_far = swap_far(gate_grad)
    kept, leaving = attend_backward(scalars, own, other, grad_head, head_full, log_total)
    kept, leaving, gate_far, down_near, tail_shard, feed_near = tie(
        kept, leaving, gate_far, down_near, tail_shard, feed_near
    )
    tail_w = gather(tail_shard, fsdp)

    up_far = swap_far(up_grad)
    gate_sum = gate_grad + gate_far
    gate_near = swap_near(gate_sum)
    block_output = (own_middle + feed_own + feed_near.astype(F32)).astype(LOW)[None]
    came, up_far, gate_near, block_output, output_grad = tie(
        swap(leaving, "x"), up_far, gate_near, block_output, output_grad
    )
    output_came = swap_near(output_grad)

    qkv_low, by_line = merge(scalars, kept, came, cosine, sine, lines)
    token_grads = lax.all_to_all(by_line, "z", split_axis=0, concat_axis=0, tiled=True)
    qkv_part = contract(units, qkv_low, 0, 1).astype(LOW).reshape(shards, 2, -1, 4 * HD)
    qkv_first = halve_x(qkv_part[:, 0]), halve_y(qkv_part[:, 1])
    qkv_second = halves_second(qkv_first)
    qkv_grad = jnp.concatenate([sum(qkv_second[0]), sum(qkv_second[1])], 0)
    up_sum = up_grad + up_far
    up_near = swap_near(up_sum)
    down_pieces = four(down_sum, down_near)
    token_grads, qkv_grad, up_near, down_pieces, output_came = tie(
        token_grads, qkv_grad, up_near, down_pieces, output_came
    )
    all_qkv = gather(qkv_grad, seq)
    output_sum = output_grad + output_came
    output_far = swap_far(output_sum)

    token_grads = token_grads.reshape(-1, chip_count)
    split = lead_w.shape[1]
    grad_one = contract(token_grads[:split], lead_w, 0, 1) + contract(
        token_grads[split:], tail_w, 0, 1
    )
    grad_one = mine_of(grad_one) + swap(theirs_of(grad_one).astype(LOW), "c").astype(F32)
    grad_rows = own_unit_scale * (
        grad_one - own_unit * jnp.mean(grad_one * own_unit, -1, keepdims=True)
    )
    input_grad = (grad_middle + grad_rows).astype(LOW)[None]

    order = jnp.stack([quarter, quarter ^ 1, quarter ^ 2, quarter ^ 3]).astype(jnp.int32)
    core_order = jnp.stack([core, 1 - core]).astype(jnp.int32)
    down_total = place_rows(order, down_pieces)
    gate_total, up_total, second_gain_grad = place_columns(
        order, gain_two, gate_weight, up_weight, four(gate_sum, gate_near), four(up_sum, up_near), shards
    )
    output_far, second_gain_grad, all_qkv = tie(output_far, second_gain_grad, all_qkv)
    output_own = output_sum + output_far
    output_total = place_rows(core_order, (output_own, swap(output_own, "c")))
    query_grad, key_grad, value_grad, first_gain_grad = place_heads(
        gain_one, query_weight, key_weight, value_weight, all_qkv
    )
    return (
        block_output,
        input_grad,
        first_gain_grad[:, 0],
        query_grad,
        key_grad,
        value_grad,
        output_total,
        second_gain_grad[:, 0],
        gate_total,
        up_total,
        down_total,
    )


def fast_solution(mesh):
    seq_count, shard_count = mesh.devices.shape
    fine = Mesh(
        mesh.devices.reshape(seq_count // 2, 2, shard_count // 2, 2), ("z", "c", "y", "x")
    )
    seq, fsdp = ("z", "c"), ("y", "x")
    matrix = P(fsdp, None)
    return jax.shard_map(
        fast_body,
        mesh=fine,
        in_specs=(
            P(fsdp, seq, None),
            P(fsdp, seq),
            P(fsdp),
            matrix,
            matrix,
            matrix,
            matrix,
            P(fsdp),
            matrix,
            matrix,
            matrix,
            P(fsdp, seq, None),
        ),
        out_specs=(
            P(fsdp, seq, None),
            P(fsdp, seq, None),
            P(fsdp),
            matrix,
            matrix,
            matrix,
            matrix,
            P(fsdp),
            matrix,
            matrix,
            matrix,
        ),
        check_vma=False,
    )


def solution(mesh):
    shape = dict(mesh.shape)
    if shape["seq"] == KVH and shape["fsdp"] == 4:
        return fast_solution(mesh)
    return plain_solution(mesh)


def shifted(value, axis, steps):
    count = lax.axis_size(axis)
    first, last = (max(0, -steps), min(count, count - steps))
    return lax.ppermute(value, axis, [(source, source + steps) for source in range(first, last)])


def rope_tables(position_rows):
    freq = THETA ** (-(jnp.arange(HD // 2, dtype=jnp.float32) * 2.0 / HD))
    angle = position_rows.astype(jnp.float32)[:, None] * freq[None, :]
    cosine = jnp.cos(angle)
    sine = jnp.sin(angle)
    return (jnp.concatenate([cosine, cosine], -1), jnp.concatenate([sine, sine], -1))


def rotate(values, cosine, sine):
    half = HD // 2
    turned = jnp.concatenate([-values[..., half:], values[..., :half]], -1)
    return values * cosine[:, None, :] + turned * sine[:, None, :]


def rotate_back(grads, cosine, sine):
    half = HD // 2
    scaled = grads * sine[:, None, :]
    turned = jnp.concatenate([scaled[..., half:], -scaled[..., :half]], -1)
    return grads * cosine[:, None, :] + turned


def norm_forward(rows, gain):
    scale = lax.rsqrt(jnp.mean(rows * rows, -1, keepdims=True) + EPS)
    unit = rows * scale
    return (unit * gain, unit, scale)


def norm_backward(grad_out, unit, scale, gain):
    grad_unit = grad_out * gain
    gain_grad = jnp.sum(grad_out * unit, 0)
    grad_rows = scale * (grad_unit - unit * jnp.mean(grad_unit * unit, -1, keepdims=True))
    return (grad_rows, gain_grad)


def plain_body(
    tokens,
    positions,
    first_gain,
    query_weight,
    key_weight,
    value_weight,
    output_weight,
    second_gain,
    gate_weight,
    up_weight,
    down_weight,
    cotangent,
):
    seq_count = lax.axis_size("seq")
    local_rows = tokens[0]
    token_count = local_rows.shape[0]
    half_len = token_count * seq_count
    rows_float = local_rows.astype(jnp.float32)
    gain_one, wq_full, wk_full, wv_full, wo_full = (
        lax.all_gather(first_gain, "fsdp", axis=0, tiled=True),
        lax.all_gather(query_weight, "fsdp", axis=0, tiled=True),
        lax.all_gather(key_weight, "fsdp", axis=0, tiled=True),
        lax.all_gather(value_weight, "fsdp", axis=0, tiled=True),
        lax.all_gather(output_weight, "fsdp", axis=0, tiled=True),
    )
    gain_one = gain_one.astype(jnp.float32)
    normed_one, unit_one, scale_one = norm_forward(rows_float, gain_one)
    normed_low = normed_one.astype(jnp.bfloat16)
    cosine, sine = rope_tables(positions[0])
    query_lin = jnp.dot(normed_low, wq_full, preferred_element_type=jnp.float32).reshape(
        token_count, QH, HD
    )
    key_lin = jnp.dot(normed_low, wk_full, preferred_element_type=jnp.float32).reshape(
        token_count, KVH, HD
    )
    value_lin = jnp.dot(normed_low, wv_full, preferred_element_type=jnp.float32).reshape(
        token_count, KVH, HD
    )
    query_rows = rotate(query_lin, cosine, sine).astype(jnp.bfloat16)
    key_rows = rotate(key_lin, cosine, sine).astype(jnp.bfloat16)
    value_rows = value_lin.astype(jnp.bfloat16)
    repeat = max(1, seq_count // KVH)
    if repeat > 1:
        key_rows = jnp.repeat(key_rows, repeat, axis=1)
        value_rows = jnp.repeat(value_rows, repeat, axis=1)
    query_heads, key_heads, value_heads = (
        lax.all_to_all(query_rows, "seq", split_axis=1, concat_axis=0, tiled=True),
        lax.all_to_all(key_rows, "seq", split_axis=1, concat_axis=0, tiled=True),
        lax.all_to_all(value_rows, "seq", split_axis=1, concat_axis=0, tiled=True),
    )
    head_count = query_heads.shape[1]
    pair_count = key_heads.shape[1]
    group = head_count // pair_count
    half_positions = lax.all_gather(positions[0], "seq", axis=0, tiled=True)
    key_prior, value_prior = shifted((key_heads, value_heads), "fsdp", 1)
    key_all = jnp.concatenate([key_prior, key_heads], 0)
    value_all = jnp.concatenate([value_prior, value_heads], 0)
    half_index = lax.axis_index("fsdp") % 2
    key_index = (half_index - 1) * half_len + jnp.arange(2 * half_len, dtype=jnp.int32)
    row_index = half_index * half_len + jnp.arange(half_len, dtype=jnp.int32)
    row_start = row_index - half_positions
    block = min(512, half_len)
    count = half_len // block
    factor = HD ** (-0.5)
    query_blocks = query_heads.reshape(count, block, pair_count, group, HD)
    index_blocks = row_index.reshape(count, block)
    start_blocks = row_start.reshape(count, block)

    def block_scores(query_block, index_block, start_block):
        scores = (
            jnp.einsum("bkgd,tkd->kgbt", query_block, key_all, preferred_element_type=jnp.float32)
            * factor
        )
        visible = (key_index[None, :] >= start_block[:, None]) & (
            key_index[None, :] <= index_block[:, None]
        )
        return jnp.where(visible, scores, -1e30)

    def forward_block(items):
        query_block, index_block, start_block = items
        scores = block_scores(query_block, index_block, start_block)
        top = jnp.max(scores, -1, keepdims=True)
        expo = jnp.exp(scores - top)
        total = jnp.sum(expo, -1, keepdims=True)
        probs_low = (expo / total).astype(jnp.bfloat16)
        mixed = jnp.einsum(
            "kgbt,tkd->bkgd", probs_low, value_all, preferred_element_type=jnp.float32
        )
        return (mixed.reshape(block, head_count, HD).astype(jnp.bfloat16), top + jnp.log(total))

    head_blocks, log_totals = lax.map(forward_block, (query_blocks, index_blocks, start_blocks))
    head_out = head_blocks.reshape(half_len, head_count, HD)
    token_heads = lax.all_to_all(head_out, "seq", split_axis=0, concat_axis=1, tiled=True)
    heads_flat = token_heads.reshape(token_count, QH * HD)
    middle = rows_float + jnp.dot(heads_flat, wo_full, preferred_element_type=jnp.float32)
    gain_two, wg_full, wu_full, wd_full = (
        lax.all_gather(second_gain, "fsdp", axis=0, tiled=True),
        lax.all_gather(gate_weight, "fsdp", axis=0, tiled=True),
        lax.all_gather(up_weight, "fsdp", axis=0, tiled=True),
        lax.all_gather(down_weight, "fsdp", axis=0, tiled=True),
    )
    gain_two = gain_two.astype(jnp.float32)
    normed_two, unit_two, scale_two = norm_forward(middle, gain_two)
    normed_two_low = normed_two.astype(jnp.bfloat16)
    gate = jnp.dot(normed_two_low, wg_full, preferred_element_type=jnp.float32)
    upper = jnp.dot(normed_two_low, wu_full, preferred_element_type=jnp.float32)
    hidden = (jax.nn.silu(gate) * upper).astype(jnp.bfloat16)
    result = middle + jnp.dot(hidden, wd_full, preferred_element_type=jnp.float32)
    block_output = result.astype(jnp.bfloat16)[None]
    grad_low = cotangent[0]
    grad_rows = grad_low.astype(jnp.float32)
    down_grad = jnp.einsum("tf,td->fd", hidden, grad_low, preferred_element_type=jnp.float32)
    grad_hidden = jnp.einsum("td,fd->tf", grad_low, wd_full, preferred_element_type=jnp.float32)
    sigma = jax.nn.sigmoid(gate)
    gate_low = (grad_hidden * upper * sigma * (1.0 + gate * (1.0 - sigma))).astype(jnp.bfloat16)
    upper_low = (grad_hidden * gate * sigma).astype(jnp.bfloat16)
    gate_grad = jnp.einsum(
        "td,tf->df", normed_two_low, gate_low, preferred_element_type=jnp.float32
    )
    up_grad = jnp.einsum("td,tf->df", normed_two_low, upper_low, preferred_element_type=jnp.float32)
    grad_normed_two = jnp.einsum(
        "tf,df->td", gate_low, wg_full, preferred_element_type=jnp.float32
    ) + jnp.einsum("tf,df->td", upper_low, wu_full, preferred_element_type=jnp.float32)
    grad_middle_norm, second_gain_grad = norm_backward(
        grad_normed_two, unit_two, scale_two, gain_two
    )
    grad_middle = grad_rows + grad_middle_norm
    grad_branch = grad_middle.astype(jnp.bfloat16)
    output_grad = jnp.einsum(
        "tc,td->cd", heads_flat, grad_branch, preferred_element_type=jnp.float32
    )
    grad_heads = (
        jnp.einsum("td,cd->tc", grad_branch, wo_full, preferred_element_type=jnp.float32)
        .astype(jnp.bfloat16)
        .reshape(token_count, QH, HD)
    )
    grad_head_rows = lax.all_to_all(grad_heads, "seq", split_axis=1, concat_axis=0, tiled=True)
    grad_blocks = grad_head_rows.reshape(count, block, pair_count, group, HD)

    def backward_block(carry, items):
        key_acc, value_acc = carry
        query_block, index_block, start_block, grad_block, log_block = items
        scores = block_scores(query_block, index_block, start_block)
        probs = jnp.exp(scores - log_block)
        probs_low = probs.astype(jnp.bfloat16)
        grad_probs = jnp.einsum(
            "bkgd,tkd->kgbt", grad_block, value_all, preferred_element_type=jnp.float32
        )
        grad_scores = (
            probs * (grad_probs - jnp.sum(probs * grad_probs, -1, keepdims=True))
        ).astype(jnp.bfloat16)
        query_grad_block = (
            jnp.einsum("kgbt,tkd->bkgd", grad_scores, key_all, preferred_element_type=jnp.float32)
            * factor
        )
        key_acc = (
            key_acc
            + jnp.einsum(
                "kgbt,bkgd->tkd", grad_scores, query_block, preferred_element_type=jnp.float32
            )
            * factor
        )
        value_acc = value_acc + jnp.einsum(
            "kgbt,bkgd->tkd", probs_low, grad_block, preferred_element_type=jnp.float32
        )
        return ((key_acc, value_acc), query_grad_block.reshape(block, head_count, HD))

    empty = jnp.zeros((2 * half_len, pair_count, HD), jnp.float32)
    (key_acc, value_acc), query_grad_blocks = lax.scan(
        backward_block,
        (empty, empty),
        (query_blocks, index_blocks, start_blocks, grad_blocks, log_totals),
    )
    key_back, value_back = (
        shifted(key_acc[:half_len].astype(jnp.bfloat16), "fsdp", -1).astype(jnp.float32),
        shifted(value_acc[:half_len].astype(jnp.bfloat16), "fsdp", -1).astype(jnp.float32),
    )
    key_local = key_acc[half_len:] + key_back
    value_local = value_acc[half_len:] + value_back
    query_grad_heads = query_grad_blocks.reshape(half_len, head_count, HD)
    grad_query_tok, grad_key_tok, grad_value_tok = (
        lax.all_to_all(
            query_grad_heads.astype(jnp.bfloat16), "seq", split_axis=0, concat_axis=1, tiled=True
        ).astype(query_grad_heads.dtype),
        lax.all_to_all(
            key_local.astype(jnp.bfloat16), "seq", split_axis=0, concat_axis=1, tiled=True
        ).astype(key_local.dtype),
        lax.all_to_all(
            value_local.astype(jnp.bfloat16), "seq", split_axis=0, concat_axis=1, tiled=True
        ).astype(value_local.dtype),
    )
    if repeat > 1:
        grad_key_tok = grad_key_tok.reshape(token_count, KVH, repeat, HD).sum(2)
        grad_value_tok = grad_value_tok.reshape(token_count, KVH, repeat, HD).sum(2)
    query_lin_grad = (
        rotate_back(grad_query_tok, cosine, sine).astype(jnp.bfloat16).reshape(token_count, QH * HD)
    )
    key_lin_grad = (
        rotate_back(grad_key_tok, cosine, sine).astype(jnp.bfloat16).reshape(token_count, KVH * HD)
    )
    value_lin_grad = grad_value_tok.astype(jnp.bfloat16).reshape(token_count, KVH * HD)
    query_grad = jnp.einsum(
        "td,tc->dc", normed_low, query_lin_grad, preferred_element_type=jnp.float32
    )
    key_grad = jnp.einsum("td,tc->dc", normed_low, key_lin_grad, preferred_element_type=jnp.float32)
    value_grad = jnp.einsum(
        "td,tc->dc", normed_low, value_lin_grad, preferred_element_type=jnp.float32
    )
    grad_normed_one = jnp.einsum(
        "tc,dc->td", query_lin_grad, wq_full, preferred_element_type=jnp.float32
    )
    grad_normed_one = grad_normed_one + jnp.einsum(
        "tc,dc->td", key_lin_grad, wk_full, preferred_element_type=jnp.float32
    )
    grad_normed_one = grad_normed_one + jnp.einsum(
        "tc,dc->td", value_lin_grad, wv_full, preferred_element_type=jnp.float32
    )
    grad_rows_one, first_gain_grad = norm_backward(grad_normed_one, unit_one, scale_one, gain_one)
    input_grad = (grad_middle + grad_rows_one).astype(jnp.bfloat16)[None]
    pieces = (
        lax.psum_scatter(
            first_gain_grad.astype(jnp.bfloat16), "fsdp", scatter_dimension=0, tiled=True
        ).astype(jnp.float32),
        lax.psum_scatter(
            query_grad.astype(jnp.bfloat16), "fsdp", scatter_dimension=0, tiled=True
        ).astype(jnp.float32),
        lax.psum_scatter(
            key_grad.astype(jnp.bfloat16), "fsdp", scatter_dimension=0, tiled=True
        ).astype(jnp.float32),
        lax.psum_scatter(
            value_grad.astype(jnp.bfloat16), "fsdp", scatter_dimension=0, tiled=True
        ).astype(jnp.float32),
        lax.psum_scatter(
            output_grad.astype(jnp.bfloat16), "fsdp", scatter_dimension=0, tiled=True
        ).astype(jnp.float32),
        lax.psum_scatter(
            second_gain_grad.astype(jnp.bfloat16), "fsdp", scatter_dimension=0, tiled=True
        ).astype(jnp.float32),
        lax.psum_scatter(
            gate_grad.astype(jnp.bfloat16), "fsdp", scatter_dimension=0, tiled=True
        ).astype(jnp.float32),
        lax.psum_scatter(
            up_grad.astype(jnp.bfloat16), "fsdp", scatter_dimension=0, tiled=True
        ).astype(jnp.float32),
        lax.psum_scatter(
            down_grad.astype(jnp.bfloat16), "fsdp", scatter_dimension=0, tiled=True
        ).astype(jnp.float32),
    )
    shares = (
        lax.psum(pieces[0].astype(jnp.bfloat16), "seq").astype(jnp.float32),
        lax.psum(pieces[1].astype(jnp.bfloat16), "seq").astype(jnp.float32),
        lax.psum(pieces[2].astype(jnp.bfloat16), "seq").astype(jnp.float32),
        lax.psum(pieces[3].astype(jnp.bfloat16), "seq").astype(jnp.float32),
        lax.psum(pieces[4].astype(jnp.bfloat16), "seq").astype(jnp.float32),
        lax.psum(pieces[5].astype(jnp.bfloat16), "seq").astype(jnp.float32),
        lax.psum(pieces[6].astype(jnp.bfloat16), "seq").astype(jnp.float32),
        lax.psum(pieces[7].astype(jnp.bfloat16), "seq").astype(jnp.float32),
        lax.psum(pieces[8].astype(jnp.bfloat16), "seq").astype(jnp.float32),
    )
    return (
        block_output,
        input_grad,
        shares[0],
        shares[1],
        shares[2],
        shares[3],
        shares[4],
        shares[5],
        shares[6],
        shares[7],
        shares[8],
    )


def plain_solution(mesh):
    placed = (
        P("fsdp", "seq", None),
        P("fsdp", "seq"),
        P("fsdp"),
        P("fsdp", None),
        P("fsdp", None),
        P("fsdp", None),
        P("fsdp", None),
        P("fsdp"),
        P("fsdp", None),
        P("fsdp", None),
        P("fsdp", None),
        P("fsdp", "seq", None),
    )
    return jax.shard_map(
        plain_body,
        mesh=mesh,
        in_specs=placed,
        out_specs=(
            P("fsdp", "seq", None),
            P("fsdp", "seq", None),
            P("fsdp"),
            P("fsdp", None),
            P("fsdp", None),
            P("fsdp", None),
            P("fsdp", None),
            P("fsdp"),
            P("fsdp", None),
            P("fsdp", None),
            P("fsdp", None),
        ),
        check_vma=False,
    )
```

```python
import functools
import math

import jax
import jax.numpy as jnp
from jax import lax
from jax.experimental import pallas as pl
from jax.experimental.pallas import tpu as pltpu
from jax.sharding import Mesh
from jax.sharding import PartitionSpec as P

QH = 16
KVH = 8
HD = 96


THETA = 100000.0
EPS = 1e-05
LOW = jnp.bfloat16
F32 = jnp.float32
NEG = -1e30
LN2 = math.log(2.0)


def contract(left, right, left_axis, right_axis):
    return lax.dot_general(
        left, right, (((left_axis,), (right_axis,)), ((), ())), preferred_element_type=F32
    )


def hide(scores, kind, first, second, query_start, key_start):
    if kind == "plain":
        return scores
    keys, queries = scores.shape
    key = key_start + lax.broadcasted_iota(jnp.int32, (keys, queries), 0)
    if kind == "keys":
        return jnp.where(key >= first, scores, NEG)
    query = query_start + lax.broadcasted_iota(jnp.int32, (1, queries), 1)
    if kind == "causal":
        return jnp.where(key <= query, scores, NEG)
    if kind == "queries":
        return scores + jnp.where(query >= second, NEG, 0.0)
    start = jnp.where(query >= second, second, jnp.where(query >= first, first, 0))
    return jnp.where((key >= start) & (key <= query), scores, NEG)


def halves_of(size):
    return slice(0, size // 2), slice(size // 2, size)


def slot_of(block, count):
    return (block % (count // 2)) * 2 + block // (count // 2)


def forward_kernel(
    scalars,
    own_ref,
    other_ref,
    low_ref,
    full_ref,
    log_ref,
    query_s,
    key_s,
    value_s,
    top_s,
    total_s,
    mixed_s,
    *,
    size,
    count,
):
    half = scalars[0]
    first = scalars[1]
    second = scalars[2]
    here = pl.program_id(0)
    per_half = count // 2

    @pl.when(here == 0)
    def _():
        for ref, side in ((own_ref, half), (other_ref, 1 - half)):
            for step in range(per_half):
                block = side * per_half + step
                columns = slice(step * size, (step + 1) * size)
                query_s[block] = ref[0:HD, columns]
                key_s[block] = ref[HD : 2 * HD, columns].T
                value_s[block] = ref[2 * HD : 3 * HD, columns]

    query = query_s[here]
    top_s[...] = jnp.full_like(top_s, NEG)
    total_s[...] = jnp.zeros_like(total_s)
    mixed_s[...] = jnp.zeros_like(mixed_s)

    def add_block(block, kind):
        keys, values = key_s[block], value_s[block]
        parts = halves_of(size)
        all_scores = [contract(keys, query[:, part], 1, 0) for part in parts]
        for part, scores in zip(parts, all_scores):
            scores = hide(
                scores, kind, first, second, here * size + part.start, block * size
            )
            old_top = top_s[:, part]
            top = jnp.maximum(old_top, jnp.max(scores, 0, keepdims=True))
            expo = jnp.exp2(scores - top)
            scale = jnp.exp2(old_top - top)
            top_s[:, part] = top
            total_s[:, part] = total_s[:, part] * scale + jnp.sum(expo, 0, keepdims=True)
            mixed_s[:, part] = mixed_s[:, part] * scale + contract(
                values, expo.astype(LOW), 1, 0
            )

    last = count - 1

    @pl.when(here == 0)
    def _():
        add_block(here, "full")

    @pl.when((here > 0) & (here < last))
    def _():
        add_block(0, "keys")

        @pl.loop(1, here)
        def _(block):
            add_block(block, "plain")

        add_block(here, "causal")

    @pl.when(here == last)
    def _():
        add_block(0, "full")

        @pl.loop(1, last)
        def _(block):
            add_block(block, "queries")

        add_block(last, "full")

    total = total_s[...]
    result = mixed_s[...] / total
    full_ref[0] = result
    low_ref[0] = result.astype(LOW)
    log_ref[0] = top_s[...] + jnp.log2(total)


def backward_kernel(
    scalars,
    own_ref,
    other_ref,
    grad_ref,
    full_ref,
    log_ref,
    kept_ref,
    leaving_ref,
    query_s,
    key_s,
    value_s,
    delta_s,
    query_grad_s,
    key_grad_s,
    value_grad_s,
    *,
    size,
    count,
):
    half = scalars[0]
    first = scalars[1]
    second = scalars[2]
    here = pl.program_id(0)
    per_half = count // 2

    @pl.when(here == 0)
    def _():
        for ref, side in ((own_ref, half), (other_ref, 1 - half)):
            for step in range(per_half):
                block = side * per_half + step
                columns = slice(step * size, (step + 1) * size)
                query_s[block] = ref[0:HD, columns]
                key_s[block] = ref[HD : 2 * HD, columns]
                value_s[block] = ref[2 * HD : 3 * HD, columns].T
        for block in range(count):
            delta_s[block] = jnp.sum(
                grad_ref[slot_of(block, count)].astype(F32) * full_ref[block], 0, keepdims=True
            )
        query_grad_s[...] = jnp.zeros_like(query_grad_s)

    key_grad_s[...] = jnp.zeros_like(key_grad_s)
    value_grad_s[...] = jnp.zeros_like(value_grad_s)
    key = key_s[here]
    key_rows = key.T
    value_rows = value_s[here]

    def add_block(block, kind):
        query = query_s[block]
        grad = grad_ref[slot_of(block, count)]
        log_total, delta = log_ref[block], delta_s[block]
        parts = halves_of(size)
        products = [
            (contract(key_rows, query[:, part], 1, 0), contract(value_rows, grad[:, part], 1, 0))
            for part in parts
        ]
        for part, (scores, grad_probs) in zip(parts, products):
            scores = hide(
                scores, kind, first, second, block * size + part.start, here * size
            )
            probs = jnp.exp2(scores - log_total[:, part])
            grad_scores = (probs * (grad_probs - delta[:, part])).astype(LOW)
            value_grad_s[...] += contract(grad[:, part], probs.astype(LOW), 1, 1)
            key_grad_s[...] += contract(query[:, part], grad_scores, 1, 1)
            query_grad_s[block, :, part] += contract(key, grad_scores, 1, 0)

    last = count - 1

    @pl.when(here == 0)
    def _():
        add_block(0, "full")

        @pl.loop(1, last)
        def _(block):
            add_block(block, "keys")

        add_block(last, "full")

    @pl.when((here > 0) & (here < last))
    def _():
        add_block(here, "causal")

        @pl.loop(here + 1, last)
        def _(block):
            add_block(block, "plain")

        add_block(last, "queries")

    @pl.when(here == last)
    def _():
        add_block(last, "full")

    side = here // per_half
    columns = pl.ds(pl.multiple_of((here % per_half) * size, size), size)

    def write(out_ref):
        out_ref[0:HD, columns] = (query_grad_s[here] * HD**-0.5).astype(LOW)
        out_ref[HD : 2 * HD, columns] = (key_grad_s[...] * LN2).astype(LOW)
        out_ref[2 * HD : 3 * HD, columns] = value_grad_s[...].astype(LOW)

    @pl.when(side == half)
    def _():
        write(kept_ref)

    @pl.when(side != half)
    def _():
        write(leaving_ref)


def attend_forward(scalars, own, other, size):
    count = 2 * own.shape[1] // size
    whole = lambda shape: pl.BlockSpec(shape, lambda i, s: (0,) * len(shape))
    pairs = count * (count + 1) // 2
    return pl.pallas_call(
        functools.partial(forward_kernel, size=size, count=count),
        grid_spec=pltpu.PrefetchScalarGridSpec(
            num_scalar_prefetch=1,
            grid=(count,),
            in_specs=[whole(own.shape), whole(other.shape)],
            out_specs=[
                pl.BlockSpec(
                    (1, HD, size), lambda i, s: (slot_of(i, count), 0, 0)
                ),
                pl.BlockSpec((1, HD, size), lambda i, s: (i, 0, 0)),
                pl.BlockSpec((1, 1, size), lambda i, s: (i, 0, 0)),
            ],
            scratch_shapes=[
                pltpu.VMEM((count, HD, size), LOW),
                pltpu.VMEM((count, size, HD), LOW),
                pltpu.VMEM((count, HD, size), LOW),
                pltpu.VMEM((1, size), F32),
                pltpu.VMEM((1, size), F32),
                pltpu.VMEM((HD, size), F32),
            ],
        ),
        out_shape=[
            jax.ShapeDtypeStruct((count, HD, size), LOW),
            jax.ShapeDtypeStruct((count, HD, size), F32),
            jax.ShapeDtypeStruct((count, 1, size), F32),
        ],
        compiler_params=pltpu.CompilerParams(
            dimension_semantics=("arbitrary",), vmem_limit_bytes=32 * 2**20
        ),
        cost_estimate=pl.CostEstimate(
            flops=pairs * size * size * HD * 32,
            bytes_accessed=10 * 2**20,
            transcendentals=pairs * size * size,
        ),
        name="attend_forward",
    )(scalars, own, other)


def attend_backward(scalars, own, other, grad, full, log_total):
    count, _, size = grad.shape
    whole = lambda shape: pl.BlockSpec(shape, lambda i, s: (0,) * len(shape))
    pairs = count * (count + 1) // 2
    out_shape = own.shape
    return pl.pallas_call(
        functools.partial(backward_kernel, size=size, count=count),
        grid_spec=pltpu.PrefetchScalarGridSpec(
            num_scalar_prefetch=1,
            grid=(count,),
            in_specs=[
                whole(own.shape),
                whole(other.shape),
                whole(grad.shape),
                whole(full.shape),
                whole(log_total.shape),
            ],
            out_specs=[whole(out_shape)] * 2,
            scratch_shapes=[
                pltpu.VMEM((count, HD, size), LOW),
                pltpu.VMEM((count, HD, size), LOW),
                pltpu.VMEM((count, size, HD), LOW),
                pltpu.VMEM((count, 1, size), F32),
                pltpu.VMEM((count, HD, size), F32),
                pltpu.VMEM((HD, size), F32),
                pltpu.VMEM((HD, size), F32),
            ],
        ),
        out_shape=[jax.ShapeDtypeStruct(out_shape, LOW)] * 2,
        compiler_params=pltpu.CompilerParams(
            dimension_semantics=("arbitrary",), vmem_limit_bytes=32 * 2**20
        ),
        cost_estimate=pl.CostEstimate(
            flops=pairs * size * size * HD * 42,
            bytes_accessed=16 * 2**20,
            transcendentals=pairs * size * size,
        ),
        name="attend_backward",
    )(scalars, own, other, grad, full, log_total)


def place_rows_kernel(order, *refs):
    pieces, out_ref = refs[:-1], refs[-1]
    size = pieces[0].shape[0]
    for index, piece in enumerate(pieces):
        start = pl.multiple_of(order[index] * size, size)
        out_ref[pl.ds(start, size), :] = piece[...].astype(F32)


def place_rows(order, pieces):
    size, width = pieces[0].shape
    total = size * len(pieces)
    step = 512
    return pl.pallas_call(
        place_rows_kernel,
        grid_spec=pltpu.PrefetchScalarGridSpec(
            num_scalar_prefetch=1,
            grid=(width // step,),
            in_specs=[pl.BlockSpec((size, step), lambda i, s: (0, i)) for _ in pieces],
            out_specs=pl.BlockSpec((total, step), lambda i, s: (0, i)),
        ),
        out_shape=jax.ShapeDtypeStruct((total, width), F32),
        compiler_params=pltpu.CompilerParams(vmem_limit_bytes=24 * 2**20),
        cost_estimate=pl.CostEstimate(
            flops=0, bytes_accessed=total * width * 6, transcendentals=0
        ),
        name="place_rows",
    )(order, *pieces)


def place_columns_kernel(order, gain_ref, gate_w_ref, up_w_ref, *refs):
    count = (len(refs) - 3) // 2
    gates, ups = refs[:count], refs[count : 2 * count]
    gate_ref, up_ref, sum_ref = refs[2 * count :]
    size = gates[0].shape[1]
    gain = gain_ref[...]
    total = jnp.zeros((gate_ref.shape[0], size), F32)
    for index in range(count):
        columns = pl.ds(pl.multiple_of(order[index] * size, size), size)
        gate, up = gates[index][...].astype(F32), ups[index][...].astype(F32)
        total += gate * gate_w_ref[:, columns].astype(F32)
        total += up * up_w_ref[:, columns].astype(F32)
        gate_ref[:, columns] = gate * gain
        up_ref[:, columns] = up * gain

    @pl.when(pl.program_id(0) == 0)
    def _():
        sum_ref[...] = jnp.zeros_like(sum_ref)

    sum_ref[...] += jnp.sum(total, 1, keepdims=True)


def place_columns(order, gain, gate_weight, up_weight, gates, ups, shards):
    rows, width = gate_weight.shape
    span = width // shards
    size = span // len(gates)
    wide = pl.BlockSpec((rows, span), lambda i, s: (0, i))
    thin = pl.BlockSpec((rows, 1), lambda i, s: (0, 0))
    pieces = [pl.BlockSpec((rows, size), lambda i, s: (0, i)) for _ in (*gates, *ups)]
    return pl.pallas_call(
        place_columns_kernel,
        grid_spec=pltpu.PrefetchScalarGridSpec(
            num_scalar_prefetch=1,
            grid=(shards,),
            in_specs=[thin, wide, wide, *pieces],
            out_specs=[wide, wide, thin],
        ),
        out_shape=[
            jax.ShapeDtypeStruct((rows, width), F32),
            jax.ShapeDtypeStruct((rows, width), F32),
            jax.ShapeDtypeStruct((rows, 1), F32),
        ],
        compiler_params=pltpu.CompilerParams(
            dimension_semantics=("arbitrary",), vmem_limit_bytes=24 * 2**20
        ),
        cost_estimate=pl.CostEstimate(
            flops=rows * width * 6, bytes_accessed=rows * width * 16, transcendentals=0
        ),
        name="place_columns",
    )(order, gain, gate_weight, up_weight, *gates, *ups)


def place_heads_kernel(gain_ref, query_w, key_w, value_w, all_ref, query_ref, key_ref, value_ref, sum_ref):
    rows = gain_ref.shape[0]
    wide = query_ref.shape[1] // KVH
    gain = gain_ref[...]
    total = jnp.zeros((rows, 4 * HD), F32)
    pieces = [all_ref[i * rows : (i + 1) * rows, :].astype(F32) for i in range(KVH)]
    for start in range(0, KVH, 2):
        value = jnp.concatenate([piece[:, :wide] for piece in pieces[start : start + 2]], 1)
        columns = slice(start * wide, (start + 2) * wide)
        total += value * query_w[:, columns].astype(F32)
        query_ref[:, columns] = value * gain
    for first, weight, out_ref in ((wide, key_w, key_ref), (wide + HD, value_w, value_ref)):
        for start in range(0, KVH, 4):
            value = jnp.concatenate(
                [piece[:, first : first + HD] for piece in pieces[start : start + 4]], 1
            )
            columns = slice(start * HD, (start + 4) * HD)
            total += value * weight[:, columns].astype(F32)
            out_ref[:, columns] = value * gain
    sum_ref[...] = jnp.sum(total, 1, keepdims=True)


def place_heads(gain, query_weight, key_weight, value_weight, pieces):
    weights = (query_weight, key_weight, value_weight)
    rows = gain.shape[0]
    return pl.pallas_call(
        place_heads_kernel,
        out_shape=[jax.ShapeDtypeStruct(weight.shape, F32) for weight in weights]
        + [jax.ShapeDtypeStruct((rows, 1), F32)],
        compiler_params=pltpu.CompilerParams(vmem_limit_bytes=32 * 2**20),
        cost_estimate=pl.CostEstimate(
            flops=rows * 3072 * 4, bytes_accessed=rows * 3072 * 8, transcendentals=0
        ),
        name="place_heads",
    )(gain, *weights, pieces)


def merge_kernel(scalars, kept_ref, came_ref, cosine_ref, sine_ref, out_ref, split_ref):
    lead = scalars[0] == 0
    lines, _, size = split_ref.shape
    for line in range(lines):
        columns = slice(line * size, (line + 1) * size)
        kept = kept_ref[:, columns].astype(F32)
        came = came_ref[:, columns].astype(F32)
        cosine, sine = cosine_ref[:, columns], sine_ref[:, columns]
        joint = kept[HD:] + came[HD:]
        first = jnp.where(lead, kept[:HD], came[:HD])
        second = jnp.where(lead, came[:HD], kept[:HD])
        turned = []
        for value in (first, second, joint[:HD]):
            low, high = value[: HD // 2], value[HD // 2 :]
            turned.append(low * cosine + high * sine)
            turned.append(high * cosine - low * sine)
        turned.append(joint[HD:])
        result = jnp.concatenate([part.astype(LOW) for part in turned], 0)
        out_ref[:, columns] = result
        split_ref[line] = result


def merge(scalars, kept, came, cosine, sine, lines):
    tokens = kept.shape[1]
    whole = lambda value: pl.BlockSpec(value.shape, lambda i, s: (0,) * len(value.shape))
    outs = [
        jax.ShapeDtypeStruct((4 * HD, tokens), LOW),
        jax.ShapeDtypeStruct((lines, 4 * HD, tokens // lines), LOW),
    ]
    return pl.pallas_call(
        merge_kernel,
        grid_spec=pltpu.PrefetchScalarGridSpec(
            num_scalar_prefetch=1,
            grid=(1,),
            in_specs=[whole(value) for value in (kept, came, cosine, sine)],
            out_specs=[whole(value) for value in outs],
        ),
        out_shape=outs,
        compiler_params=pltpu.CompilerParams(vmem_limit_bytes=24 * 2**20),
        cost_estimate=pl.CostEstimate(
            flops=tokens * HD * 24, bytes_accessed=tokens * HD * 30, transcendentals=0
        ),
        name="merge",
    )(scalars, kept, came, cosine, sine)


def pack_kernel(scalars, gain_ref, query_ref, key_ref, value_ref, *outs):
    core = scalars[3]
    gain = gain_ref[...]
    wide = query_ref.shape[1] // KVH
    span = wide + 2 * HD
    for which in range(2):

        @pl.when(core == which)
        def _():
            for line in range(KVH // 2):
                head = 2 * line + which
                value = jnp.concatenate(
                    [
                        query_ref[:, head * wide : (head + 1) * wide].astype(F32),
                        key_ref[:, head * HD : (head + 1) * HD].astype(F32),
                        value_ref[:, head * HD : (head + 1) * HD].astype(F32),
                    ],
                    1,
                )
                place = (line % 2) * span
                outs[line // 2][:, place : place + span] = (value * gain).astype(LOW)


def pack(scalars, gain, query_weight, key_weight, value_weight):
    rows, width = query_weight.shape
    whole = lambda value: pl.BlockSpec(value.shape, lambda i, s: (0, 0))
    weights = (gain, query_weight, key_weight, value_weight)
    outs = [jax.ShapeDtypeStruct((rows, width // 2), LOW)] * 2
    return pl.pallas_call(
        pack_kernel,
        grid_spec=pltpu.PrefetchScalarGridSpec(
            num_scalar_prefetch=1,
            grid=(1,),
            in_specs=[whole(value) for value in weights],
            out_specs=[whole(value) for value in outs],
        ),
        out_shape=outs,
        compiler_params=pltpu.CompilerParams(vmem_limit_bytes=24 * 2**20),
        cost_estimate=pl.CostEstimate(
            flops=rows * width, bytes_accessed=rows * width * 6, transcendentals=0
        ),
        name="pack",
    )(scalars, *weights)


def spread_kernel(scalars, lin_ref, cosine_ref, sine_ref, own_ref, leaving_ref):
    cosine, sine = cosine_ref[...], sine_ref[...]

    def turn(start, factor):
        low = lin_ref[start : start + HD // 2, :]
        high = lin_ref[start + HD // 2 : start + HD, :]
        turned = ((low * cosine - high * sine) * factor, (high * cosine + low * sine) * factor)
        return jnp.concatenate([part.astype(LOW) for part in turned], 0)

    lead = scalars[0] == 0
    first, second = turn(0, HD**-0.5 / LN2), turn(HD, HD**-0.5 / LN2)

    @pl.when(lead)
    def _():
        own_ref[0:HD] = first
        leaving_ref[0:HD] = second

    @pl.when(jnp.logical_not(lead))
    def _():
        own_ref[0:HD] = second
        leaving_ref[0:HD] = first

    key = turn(2 * HD, 1.0)
    value = lin_ref[3 * HD : 4 * HD].astype(LOW)
    for ref in (own_ref, leaving_ref):
        ref[HD : 2 * HD] = key
        ref[2 * HD : 3 * HD] = value


def spread(scalars, lin, cosine, sine):
    tokens = lin.shape[1]
    step = 512
    column = lambda rows: pl.BlockSpec((rows, step), lambda i, s: (0, i))
    return pl.pallas_call(
        spread_kernel,
        grid_spec=pltpu.PrefetchScalarGridSpec(
            num_scalar_prefetch=1,
            grid=(tokens // step,),
            in_specs=[column(4 * HD), column(HD // 2), column(HD // 2)],
            out_specs=[column(3 * HD)] * 2,
        ),
        out_shape=[jax.ShapeDtypeStruct((3 * HD, tokens), LOW)] * 2,
        compiler_params=pltpu.CompilerParams(vmem_limit_bytes=24 * 2**20),
        cost_estimate=pl.CostEstimate(
            flops=tokens * HD * 24, bytes_accessed=tokens * HD * 36, transcendentals=0
        ),
        name="spread",
    )(scalars, lin, cosine, sine)


def swap(value, axis):
    return lax.ppermute(value, axis, [(0, 1), (1, 0)])


def swap_near(value):
    return lax.ppermute(value, "z", [(0, 1), (1, 0), (2, 3), (3, 2)])


def swap_far(value):
    return lax.ppermute(value, "z", [(0, 2), (2, 0), (1, 3), (3, 1)])


def tie(*values):
    return lax.optimization_barrier(values)


def in_order(place, own, other):
    return (jnp.where(place == 0, own, other), jnp.where(place == 0, other, own))


def both(place, own, other):
    return jnp.concatenate(in_order(place, own, other), 0)


def spread_out(value, first, second):
    other = swap(value, first)
    pair = jnp.stack(in_order(lax.axis_index(first), value, other))
    return pair, swap(pair, second)


def placed(pair, other, second):
    pairs = in_order(lax.axis_index(second), pair, other)
    grid = jnp.stack(pairs, 0 if second == "y" else 1)
    return grid.reshape(-1, *grid.shape[3:])


def pick(array, axis, at):
    return lax.dynamic_index_in_dim(array, at, axis, keepdims=False)


def halve(value, axis, along=0):
    at = lax.axis_index(axis)
    return pick(value, along, at), swap(pick(value, along, 1 - at), axis)


def halve_x(value):
    return halve(value.reshape(2, 2, -1, value.shape[-1]), "x", 1)


def halve_y(value):
    return halve(value.reshape(2, 2, -1, value.shape[-1]), "y", 0)


def fast_body(
    tokens,
    positions,
    first_gain,
    query_weight,
    key_weight,
    value_weight,
    output_weight,
    second_gain,
    gate_weight,
    up_weight,
    down_weight,
    cotangent,
):
    seq = ("z", "c")
    fsdp = ("y", "x")
    z, core, half = lax.axis_index("z"), lax.axis_index("c"), lax.axis_index("x")
    near = z % 2
    lines = lax.axis_size("z")
    seq_count = 2 * lines
    shards = lax.axis_size("y") * 2
    spot = z * 2 + core
    quarter = near * 2 + core
    rows = tokens[0]
    count, width = rows.shape
    chip_count = 2 * count
    half_len = count * seq_count
    seq_len = 2 * half_len

    begins = jnp.where(
        (spot == 0) & (half == 0),
        count - 1 - positions[0, count - 1],
        half * half_len + spot * count - positions[0, 0],
    )
    ends = begins + (seq_len - count)
    scalars = jnp.stack([half, begins, ends, core]).astype(jnp.int32)

    gain_one = first_gain.astype(F32)[:, None]
    gain_two = second_gain.astype(F32)[:, None]

    def row_scale(value):
        return lax.rsqrt(jnp.mean(value * value, -1, keepdims=True) + EPS)

    take = functools.partial(lax.dynamic_slice_in_dim, axis=1)
    take_rows = functools.partial(lax.dynamic_slice_in_dim, axis=0)
    gather = lambda value, axes: lax.all_gather(value, axes, axis=0, tiled=True)
    own_rows = rows.astype(F32)
    own_unit_scale = row_scale(own_rows)
    own_unit = own_rows * own_unit_scale
    units = gather(own_unit.astype(LOW), seq)
    wide = QH // KVH * HD
    qkv_shard = (
        jnp.concatenate(
            [
                take(query_weight, spot * wide, wide),
                take(key_weight, spot * HD, HD),
                take(value_weight, spot * HD, HD),
            ],
            1,
        ).astype(F32)
        * gain_one
    ).astype(LOW)
    out_rows = output_weight.shape[0] // 2
    out_shard = take_rows(output_weight, core * out_rows, out_rows)
    piece = down_weight.shape[0] // 4
    down_shard = take_rows(down_weight, quarter * piece, piece)
    gate_shard, up_shard = (
        (
            jnp.concatenate(
                [
                    take(weight, shard * 4 * piece + quarter * piece, piece)
                    for shard in range(shards)
                ],
                1,
            ).astype(F32)
            * gain_two
        ).astype(LOW)
        for weight in (gate_weight, up_weight)
    )
    side = lax.axis_index("y")
    qkv_pair = jnp.stack(in_order(half, qkv_shard, swap(qkv_shard, "x")))
    gate_pair = jnp.stack(in_order(half, gate_shard, swap(gate_shard, "x")))
    up_pair = jnp.stack(in_order(side, up_shard, swap(up_shard, "y")))
    qkv_pair, gate_pair, up_pair = tie(qkv_pair, gate_pair, up_pair)
    qkv_w = placed(qkv_pair, swap(qkv_pair, "y"), "y")
    gate_pair, up_pair = (gate_pair, swap(gate_pair, "y")), (up_pair, swap(up_pair, "x"))

    place = half * half_len + jnp.arange(half_len, dtype=jnp.int32)
    start = jnp.where(place >= ends, ends, jnp.where(place >= begins, begins, 0))
    freq = THETA ** (-(jnp.arange(HD // 2, dtype=F32) * 2.0 / HD))
    angle = freq[:, None] * (place - start).astype(F32)[None, :]
    cosine, sine = jnp.cos(angle), jnp.sin(angle)
    chip_rows = both(core, rows, swap(rows, "c"))
    units, own_cot, chip_rows = tie(units, cotangent[0], chip_rows)
    own, leaving = spread(scalars, contract(qkv_w, units, 0, 1), cosine, sine)

    near_cot = swap_near(own_cot)
    other, out_shard, down_shard, near_cot, chip_cot, gate_pair, up_pair = tie(
        swap(leaving, "x"),
        out_shard,
        down_shard,
        near_cot,
        both(core, own_cot, swap(own_cot, "c")),
        gate_pair,
        up_pair,
    )
    out_w = gather(out_shard, fsdp)
    down_w = gather(down_shard, fsdp)
    near_other = swap(near_cot, "c")
    head_low, head_full, log_total = attend_forward(scalars, own, other, chip_count)
    exchange = lambda value: lax.all_to_all(
        value, ("z", "x"), split_axis=0, concat_axis=0, tiled=True
    )
    head_low, near_other = tie(head_low, near_other)
    lead_shard, tail_shard = pack(scalars, gain_one, query_weight, key_weight, value_weight)
    heads, gate_w, up_w, near_cot, lead_shard = tie(
        exchange(head_low),
        placed(*gate_pair, "y"),
        placed(*up_pair, "x"),
        jnp.concatenate([near_cot, near_other], 0),
        lead_shard,
    )
    lead_w = gather(lead_shard, fsdp)
    heads = heads.reshape(QH // 2 * HD, chip_count)

    mine_of = lambda value: take_rows(value, core * count, count)
    theirs_of = lambda value: take_rows(value, (1 - core) * count, count)
    branch = contract(heads, out_w, 0, 0).astype(LOW)
    middle = chip_rows.astype(F32) + (branch.astype(F32) + swap(branch, "c").astype(F32))
    middle_scale = row_scale(middle)
    chip_unit = middle * middle_scale
    own_middle, own_scale, own_middle_unit = (
        mine_of(middle),
        mine_of(middle_scale),
        mine_of(chip_unit),
    )
    chip_unit = chip_unit.astype(LOW)
    near_unit = swap_near(mine_of(chip_unit))

    def feed(unit):
        gate, upper = contract(unit, gate_w, 1, 0), contract(unit, up_w, 1, 0)
        sigma = jax.nn.sigmoid(gate)
        silu = gate * sigma
        return (silu * upper).astype(LOW), (gate, upper, sigma, silu)

    def feed_back(cot, kept):
        gate, upper, sigma, silu = kept
        grad_hidden = contract(cot, down_w, 1, 1)
        gate_low = (grad_hidden * upper * sigma * (1.0 + gate * (1.0 - sigma))).astype(LOW)
        upper_low = (grad_hidden * silu).astype(LOW)
        part = contract(gate_low, gate_w, 1, 1) + contract(upper_low, up_w, 1, 1)
        return gate_low, upper_low, part

    def chip_sum(chip_part, near_part):
        near_sum = near_part[:count].astype(F32) + swap(near_part[count:].astype(LOW), "c")
        own_sum = mine_of(chip_part).astype(F32) + swap(theirs_of(chip_part).astype(LOW), "c")
        return own_sum, near_sum.astype(LOW)

    stack = lambda first, second: jnp.concatenate([first, second], 0)
    scatter = lambda value: lax.psum_scatter(value, fsdp, scatter_dimension=0, tiled=True)
    chip_hidden, chip_kept = feed(chip_unit)
    near_unit, chip_hidden = tie(near_unit, chip_hidden)
    near_unit = jnp.concatenate([near_unit, swap(near_unit, "c")], 0)
    near_hidden, near_kept = feed(near_unit)
    down_part = contract(
        stack(chip_hidden, near_hidden), stack(chip_cot, near_cot), 0, 0
    ).astype(LOW)
    near_cot, down_part = tie(near_cot, down_part)
    near_gate, near_upper, near_part = feed_back(near_cot, near_kept)
    chip_gate, chip_upper, chip_part = feed_back(chip_cot, chip_kept)
    grad_two, near_sum = chip_sum(chip_part, near_part)

    def four(value, near_value):
        return value, swap(value, "c"), near_value, swap(near_value, "c")

    def halves_first(value):
        cut = value.shape[-1] // 2
        return halve_x(value[:, :cut]), halve_y(value[:, cut:])

    def halves_second(firsts):
        return halve(sum(firsts[0]), "y"), halve(sum(firsts[1]), "x")

    def halves_end(seconds):
        return jnp.concatenate([sum(seconds[0]), sum(seconds[1])], 1)

    down_first = halves_first(down_part)
    near_sum, near_gate, near_upper, chip_part = tie(
        near_sum, near_gate, near_upper, chip_part
    )
    grad_came = swap_near(near_sum)
    all_units = stack(chip_unit, near_unit)
    gate_part = contract(all_units, stack(chip_gate, near_gate), 0, 0).astype(LOW)
    up_part = contract(all_units, stack(chip_upper, near_upper), 0, 0).astype(LOW)
    feed_own, feed_near = chip_sum(
        contract(chip_hidden, down_w, 1, 0), contract(near_hidden, down_w, 1, 0)
    )
    gate_part, up_part, down_first, grad_came, feed_near = tie(
        gate_part, up_part, down_first, grad_came, feed_near
    )
    feed_near = swap_near(feed_near)
    down_second = halves_second(down_first)
    grad_two = grad_two + grad_came.astype(F32)
    grad_middle = own_cot.astype(F32) + own_scale * (
        grad_two - own_middle_unit * jnp.mean(grad_two * own_middle_unit, -1, keepdims=True)
    )
    own_branch, lead_w, down_second, gate_part, up_part = tie(
        grad_middle.astype(LOW), lead_w, down_second, gate_part, up_part
    )
    gate_grad, up_grad = scatter(gate_part), scatter(up_part)
    down_grad = halves_end(down_second)
    down_far = swap_far(down_grad)
    grad_branch = both(core, own_branch, swap(own_branch, "c"))
    grad_heads = contract(out_w, grad_branch, 1, 1).astype(LOW)
    grad_heads, grad_branch, down_far, feed_near = tie(
        grad_heads, grad_branch, down_far, feed_near
    )
    down_sum = down_grad + down_far
    output_part = contract(heads, grad_branch, 1, 0).astype(LOW)
    output_grad = scatter(output_part)
    grad_head, output_part, gate_grad, down_sum = tie(
        exchange(grad_heads.reshape(2 * lines, HD, chip_count)), output_part, gate_grad, down_sum
    )
    down_near = swap_near(down_sum)

    gate_far = swap_far(gate_grad)
    kept, leaving = attend_backward(scalars, own, other, grad_head, head_full, log_total)
    kept, leaving, gate_far, down_near, tail_shard = tie(
        kept, leaving, gate_far, down_near, tail_shard
    )
    tail_w = gather(tail_shard, fsdp)

    up_far = swap_far(up_grad)
    gate_sum = gate_grad + gate_far
    gate_near = swap_near(gate_sum)
    block_output = (own_middle + feed_own + feed_near.astype(F32)).astype(LOW)[None]
    came, up_far, gate_near, block_output, output_grad = tie(
        swap(leaving, "x"), up_far, gate_near, block_output, output_grad
    )
    output_came = swap_near(output_grad)

    qkv_low, by_line = merge(scalars, kept, came, cosine, sine, lines)
    token_grads = lax.all_to_all(by_line, "z", split_axis=0, concat_axis=0, tiled=True)
    qkv_part = contract(units, qkv_low, 0, 1).astype(LOW).reshape(shards, 2, -1, 4 * HD)
    qkv_first = halve_x(qkv_part[:, 0]), halve_y(qkv_part[:, 1])
    qkv_second = halves_second(qkv_first)
    qkv_grad = jnp.concatenate([sum(qkv_second[0]), sum(qkv_second[1])], 0)
    up_sum = up_grad + up_far
    up_near = swap_near(up_sum)
    down_pieces = four(down_sum, down_near)
    token_grads, qkv_grad, up_near, down_pieces, output_came = tie(
        token_grads, qkv_grad, up_near, down_pieces, output_came
    )
    all_qkv = gather(qkv_grad, seq)
    output_sum = output_grad + output_came
    output_far = swap_far(output_sum)

    token_grads = token_grads.reshape(-1, chip_count)
    split = lead_w.shape[1]
    grad_one = contract(token_grads[:split], lead_w, 0, 1) + contract(
        token_grads[split:], tail_w, 0, 1
    )
    grad_one = mine_of(grad_one) + swap(theirs_of(grad_one).astype(LOW), "c").astype(F32)
    grad_rows = own_unit_scale * (
        grad_one - own_unit * jnp.mean(grad_one * own_unit, -1, keepdims=True)
    )
    input_grad = (grad_middle + grad_rows).astype(LOW)[None]

    order = jnp.stack([quarter, quarter ^ 1, quarter ^ 2, quarter ^ 3]).astype(jnp.int32)
    core_order = jnp.stack([core, 1 - core]).astype(jnp.int32)
    down_total = place_rows(order, down_pieces)
    gate_total, up_total, second_gain_grad = place_columns(
        order, gain_two, gate_weight, up_weight, four(gate_sum, gate_near), four(up_sum, up_near), shards
    )
    output_far, second_gain_grad, input_grad = tie(output_far, second_gain_grad, input_grad)
    output_own = output_sum + output_far
    output_total = place_rows(core_order, (output_own, swap(output_own, "c")))
    query_grad, key_grad, value_grad, first_gain_grad = place_heads(
        gain_one, query_weight, key_weight, value_weight, all_qkv
    )
    return (
        block_output,
        input_grad,
        first_gain_grad[:, 0],
        query_grad,
        key_grad,
        value_grad,
        output_total,
        second_gain_grad[:, 0],
        gate_total,
        up_total,
        down_total,
    )


def fast_solution(mesh):
    seq_count, shard_count = mesh.devices.shape
    fine = Mesh(
        mesh.devices.reshape(seq_count // 2, 2, shard_count // 2, 2), ("z", "c", "y", "x")
    )
    seq, fsdp = ("z", "c"), ("y", "x")
    matrix = P(fsdp, None)
    return jax.shard_map(
        fast_body,
        mesh=fine,
        in_specs=(
            P(fsdp, seq, None),
            P(fsdp, seq),
            P(fsdp),
            matrix,
            matrix,
            matrix,
            matrix,
            P(fsdp),
            matrix,
            matrix,
            matrix,
            P(fsdp, seq, None),
        ),
        out_specs=(
            P(fsdp, seq, None),
            P(fsdp, seq, None),
            P(fsdp),
            matrix,
            matrix,
            matrix,
            matrix,
            P(fsdp),
            matrix,
            matrix,
            matrix,
        ),
        check_vma=False,
    )


def solution(mesh):
    shape = dict(mesh.shape)
    if shape["seq"] == KVH and shape["fsdp"] == 4:
        return fast_solution(mesh)
    return plain_solution(mesh)


def shifted(value, axis, steps):
    count = lax.axis_size(axis)
    first, last = (max(0, -steps), min(count, count - steps))
    return lax.ppermute(value, axis, [(source, source + steps) for source in range(first, last)])


def rope_tables(position_rows):
    freq = THETA ** (-(jnp.arange(HD // 2, dtype=jnp.float32) * 2.0 / HD))
    angle = position_rows.astype(jnp.float32)[:, None] * freq[None, :]
    cosine = jnp.cos(angle)
    sine = jnp.sin(angle)
    return (jnp.concatenate([cosine, cosine], -1), jnp.concatenate([sine, sine], -1))


def rotate(values, cosine, sine):
    half = HD // 2
    turned = jnp.concatenate([-values[..., half:], values[..., :half]], -1)
    return values * cosine[:, None, :] + turned * sine[:, None, :]


def rotate_back(grads, cosine, sine):
    half = HD // 2
    scaled = grads * sine[:, None, :]
    turned = jnp.concatenate([scaled[..., half:], -scaled[..., :half]], -1)
    return grads * cosine[:, None, :] + turned


def norm_forward(rows, gain):
    scale = lax.rsqrt(jnp.mean(rows * rows, -1, keepdims=True) + EPS)
    unit = rows * scale
    return (unit * gain, unit, scale)


def norm_backward(grad_out, unit, scale, gain):
    grad_unit = grad_out * gain
    gain_grad = jnp.sum(grad_out * unit, 0)
    grad_rows = scale * (grad_unit - unit * jnp.mean(grad_unit * unit, -1, keepdims=True))
    return (grad_rows, gain_grad)


def plain_body(
    tokens,
    positions,
    first_gain,
    query_weight,
    key_weight,
    value_weight,
    output_weight,
    second_gain,
    gate_weight,
    up_weight,
    down_weight,
    cotangent,
):
    seq_count = lax.axis_size("seq")
    local_rows = tokens[0]
    token_count = local_rows.shape[0]
    half_len = token_count * seq_count
    rows_float = local_rows.astype(jnp.float32)
    gain_one, wq_full, wk_full, wv_full, wo_full = (
        lax.all_gather(first_gain, "fsdp", axis=0, tiled=True),
        lax.all_gather(query_weight, "fsdp", axis=0, tiled=True),
        lax.all_gather(key_weight, "fsdp", axis=0, tiled=True),
        lax.all_gather(value_weight, "fsdp", axis=0, tiled=True),
        lax.all_gather(output_weight, "fsdp", axis=0, tiled=True),
    )
    gain_one = gain_one.astype(jnp.float32)
    normed_one, unit_one, scale_one = norm_forward(rows_float, gain_one)
    normed_low = normed_one.astype(jnp.bfloat16)
    cosine, sine = rope_tables(positions[0])
    query_lin = jnp.dot(normed_low, wq_full, preferred_element_type=jnp.float32).reshape(
        token_count, QH, HD
    )
    key_lin = jnp.dot(normed_low, wk_full, preferred_element_type=jnp.float32).reshape(
        token_count, KVH, HD
    )
    value_lin = jnp.dot(normed_low, wv_full, preferred_element_type=jnp.float32).reshape(
        token_count, KVH, HD
    )
    query_rows = rotate(query_lin, cosine, sine).astype(jnp.bfloat16)
    key_rows = rotate(key_lin, cosine, sine).astype(jnp.bfloat16)
    value_rows = value_lin.astype(jnp.bfloat16)
    repeat = max(1, seq_count // KVH)
    if repeat > 1:
        key_rows = jnp.repeat(key_rows, repeat, axis=1)
        value_rows = jnp.repeat(value_rows, repeat, axis=1)
    query_heads, key_heads, value_heads = (
        lax.all_to_all(query_rows, "seq", split_axis=1, concat_axis=0, tiled=True),
        lax.all_to_all(key_rows, "seq", split_axis=1, concat_axis=0, tiled=True),
        lax.all_to_all(value_rows, "seq", split_axis=1, concat_axis=0, tiled=True),
    )
    head_count = query_heads.shape[1]
    pair_count = key_heads.shape[1]
    group = head_count // pair_count
    half_positions = lax.all_gather(positions[0], "seq", axis=0, tiled=True)
    key_prior, value_prior = shifted((key_heads, value_heads), "fsdp", 1)
    key_all = jnp.concatenate([key_prior, key_heads], 0)
    value_all = jnp.concatenate([value_prior, value_heads], 0)
    half_index = lax.axis_index("fsdp") % 2
    key_index = (half_index - 1) * half_len + jnp.arange(2 * half_len, dtype=jnp.int32)
    row_index = half_index * half_len + jnp.arange(half_len, dtype=jnp.int32)
    row_start = row_index - half_positions
    block = min(512, half_len)
    count = half_len // block
    factor = HD ** (-0.5)
    query_blocks = query_heads.reshape(count, block, pair_count, group, HD)
    index_blocks = row_index.reshape(count, block)
    start_blocks = row_start.reshape(count, block)

    def block_scores(query_block, index_block, start_block):
        scores = (
            jnp.einsum("bkgd,tkd->kgbt", query_block, key_all, preferred_element_type=jnp.float32)
            * factor
        )
        visible = (key_index[None, :] >= start_block[:, None]) & (
            key_index[None, :] <= index_block[:, None]
        )
        return jnp.where(visible, scores, -1e30)

    def forward_block(items):
        query_block, index_block, start_block = items
        scores = block_scores(query_block, index_block, start_block)
        top = jnp.max(scores, -1, keepdims=True)
        expo = jnp.exp(scores - top)
        total = jnp.sum(expo, -1, keepdims=True)
        probs_low = (expo / total).astype(jnp.bfloat16)
        mixed = jnp.einsum(
            "kgbt,tkd->bkgd", probs_low, value_all, preferred_element_type=jnp.float32
        )
        return (mixed.reshape(block, head_count, HD).astype(jnp.bfloat16), top + jnp.log(total))

    head_blocks, log_totals = lax.map(forward_block, (query_blocks, index_blocks, start_blocks))
    head_out = head_blocks.reshape(half_len, head_count, HD)
    token_heads = lax.all_to_all(head_out, "seq", split_axis=0, concat_axis=1, tiled=True)
    heads_flat = token_heads.reshape(token_count, QH * HD)
    middle = rows_float + jnp.dot(heads_flat, wo_full, preferred_element_type=jnp.float32)
    gain_two, wg_full, wu_full, wd_full = (
        lax.all_gather(second_gain, "fsdp", axis=0, tiled=True),
        lax.all_gather(gate_weight, "fsdp", axis=0, tiled=True),
        lax.all_gather(up_weight, "fsdp", axis=0, tiled=True),
        lax.all_gather(down_weight, "fsdp", axis=0, tiled=True),
    )
    gain_two = gain_two.astype(jnp.float32)
    normed_two, unit_two, scale_two = norm_forward(middle, gain_two)
    normed_two_low = normed_two.astype(jnp.bfloat16)
    gate = jnp.dot(normed_two_low, wg_full, preferred_element_type=jnp.float32)
    upper = jnp.dot(normed_two_low, wu_full, preferred_element_type=jnp.float32)
    hidden = (jax.nn.silu(gate) * upper).astype(jnp.bfloat16)
    result = middle + jnp.dot(hidden, wd_full, preferred_element_type=jnp.float32)
    block_output = result.astype(jnp.bfloat16)[None]
    grad_low = cotangent[0]
    grad_rows = grad_low.astype(jnp.float32)
    down_grad = jnp.einsum("tf,td->fd", hidden, grad_low, preferred_element_type=jnp.float32)
    grad_hidden = jnp.einsum("td,fd->tf", grad_low, wd_full, preferred_element_type=jnp.float32)
    sigma = jax.nn.sigmoid(gate)
    gate_low = (grad_hidden * upper * sigma * (1.0 + gate * (1.0 - sigma))).astype(jnp.bfloat16)
    upper_low = (grad_hidden * gate * sigma).astype(jnp.bfloat16)
    gate_grad = jnp.einsum(
        "td,tf->df", normed_two_low, gate_low, preferred_element_type=jnp.float32
    )
    up_grad = jnp.einsum("td,tf->df", normed_two_low, upper_low, preferred_element_type=jnp.float32)
    grad_normed_two = jnp.einsum(
        "tf,df->td", gate_low, wg_full, preferred_element_type=jnp.float32
    ) + jnp.einsum("tf,df->td", upper_low, wu_full, preferred_element_type=jnp.float32)
    grad_middle_norm, second_gain_grad = norm_backward(
        grad_normed_two, unit_two, scale_two, gain_two
    )
    grad_middle = grad_rows + grad_middle_norm
    grad_branch = grad_middle.astype(jnp.bfloat16)
    output_grad = jnp.einsum(
        "tc,td->cd", heads_flat, grad_branch, preferred_element_type=jnp.float32
    )
    grad_heads = (
        jnp.einsum("td,cd->tc", grad_branch, wo_full, preferred_element_type=jnp.float32)
        .astype(jnp.bfloat16)
        .reshape(token_count, QH, HD)
    )
    grad_head_rows = lax.all_to_all(grad_heads, "seq", split_axis=1, concat_axis=0, tiled=True)
    grad_blocks = grad_head_rows.reshape(count, block, pair_count, group, HD)

    def backward_block(carry, items):
        key_acc, value_acc = carry
        query_block, index_block, start_block, grad_block, log_block = items
        scores = block_scores(query_block, index_block, start_block)
        probs = jnp.exp(scores - log_block)
        probs_low = probs.astype(jnp.bfloat16)
        grad_probs = jnp.einsum(
            "bkgd,tkd->kgbt", grad_block, value_all, preferred_element_type=jnp.float32
        )
        grad_scores = (
            probs * (grad_probs - jnp.sum(probs * grad_probs, -1, keepdims=True))
        ).astype(jnp.bfloat16)
        query_grad_block = (
            jnp.einsum("kgbt,tkd->bkgd", grad_scores, key_all, preferred_element_type=jnp.float32)
            * factor
        )
        key_acc = (
            key_acc
            + jnp.einsum(
                "kgbt,bkgd->tkd", grad_scores, query_block, preferred_element_type=jnp.float32
            )
            * factor
        )
        value_acc = value_acc + jnp.einsum(
            "kgbt,bkgd->tkd", probs_low, grad_block, preferred_element_type=jnp.float32
        )
        return ((key_acc, value_acc), query_grad_block.reshape(block, head_count, HD))

    empty = jnp.zeros((2 * half_len, pair_count, HD), jnp.float32)
    (key_acc, value_acc), query_grad_blocks = lax.scan(
        backward_block,
        (empty, empty),
        (query_blocks, index_blocks, start_blocks, grad_blocks, log_totals),
    )
    key_back, value_back = (
        shifted(key_acc[:half_len].astype(jnp.bfloat16), "fsdp", -1).astype(jnp.float32),
        shifted(value_acc[:half_len].astype(jnp.bfloat16), "fsdp", -1).astype(jnp.float32),
    )
    key_local = key_acc[half_len:] + key_back
    value_local = value_acc[half_len:] + value_back
    query_grad_heads = query_grad_blocks.reshape(half_len, head_count, HD)
    grad_query_tok, grad_key_tok, grad_value_tok = (
        lax.all_to_all(
            query_grad_heads.astype(jnp.bfloat16), "seq", split_axis=0, concat_axis=1, tiled=True
        ).astype(query_grad_heads.dtype),
        lax.all_to_all(
            key_local.astype(jnp.bfloat16), "seq", split_axis=0, concat_axis=1, tiled=True
        ).astype(key_local.dtype),
        lax.all_to_all(
            value_local.astype(jnp.bfloat16), "seq", split_axis=0, concat_axis=1, tiled=True
        ).astype(value_local.dtype),
    )
    if repeat > 1:
        grad_key_tok = grad_key_tok.reshape(token_count, KVH, repeat, HD).sum(2)
        grad_value_tok = grad_value_tok.reshape(token_count, KVH, repeat, HD).sum(2)
    query_lin_grad = (
        rotate_back(grad_query_tok, cosine, sine).astype(jnp.bfloat16).reshape(token_count, QH * HD)
    )
    key_lin_grad = (
        rotate_back(grad_key_tok, cosine, sine).astype(jnp.bfloat16).reshape(token_count, KVH * HD)
    )
    value_lin_grad = grad_value_tok.astype(jnp.bfloat16).reshape(token_count, KVH * HD)
    query_grad = jnp.einsum(
        "td,tc->dc", normed_low, query_lin_grad, preferred_element_type=jnp.float32
    )
    key_grad = jnp.einsum("td,tc->dc", normed_low, key_lin_grad, preferred_element_type=jnp.float32)
    value_grad = jnp.einsum(
        "td,tc->dc", normed_low, value_lin_grad, preferred_element_type=jnp.float32
    )
    grad_normed_one = jnp.einsum(
        "tc,dc->td", query_lin_grad, wq_full, preferred_element_type=jnp.float32
    )
    grad_normed_one = grad_normed_one + jnp.einsum(
        "tc,dc->td", key_lin_grad, wk_full, preferred_element_type=jnp.float32
    )
    grad_normed_one = grad_normed_one + jnp.einsum(
        "tc,dc->td", value_lin_grad, wv_full, preferred_element_type=jnp.float32
    )
    grad_rows_one, first_gain_grad = norm_backward(grad_normed_one, unit_one, scale_one, gain_one)
    input_grad = (grad_middle + grad_rows_one).astype(jnp.bfloat16)[None]
    pieces = (
        lax.psum_scatter(
            first_gain_grad.astype(jnp.bfloat16), "fsdp", scatter_dimension=0, tiled=True
        ).astype(jnp.float32),
        lax.psum_scatter(
            query_grad.astype(jnp.bfloat16), "fsdp", scatter_dimension=0, tiled=True
        ).astype(jnp.float32),
        lax.psum_scatter(
            key_grad.astype(jnp.bfloat16), "fsdp", scatter_dimension=0, tiled=True
        ).astype(jnp.float32),
        lax.psum_scatter(
            value_grad.astype(jnp.bfloat16), "fsdp", scatter_dimension=0, tiled=True
        ).astype(jnp.float32),
        lax.psum_scatter(
            output_grad.astype(jnp.bfloat16), "fsdp", scatter_dimension=0, tiled=True
        ).astype(jnp.float32),
        lax.psum_scatter(
            second_gain_grad.astype(jnp.bfloat16), "fsdp", scatter_dimension=0, tiled=True
        ).astype(jnp.float32),
        lax.psum_scatter(
            gate_grad.astype(jnp.bfloat16), "fsdp", scatter_dimension=0, tiled=True
        ).astype(jnp.float32),
        lax.psum_scatter(
            up_grad.astype(jnp.bfloat16), "fsdp", scatter_dimension=0, tiled=True
        ).astype(jnp.float32),
        lax.psum_scatter(
            down_grad.astype(jnp.bfloat16), "fsdp", scatter_dimension=0, tiled=True
        ).astype(jnp.float32),
    )
    shares = (
        lax.psum(pieces[0].astype(jnp.bfloat16), "seq").astype(jnp.float32),
        lax.psum(pieces[1].astype(jnp.bfloat16), "seq").astype(jnp.float32),
        lax.psum(pieces[2].astype(jnp.bfloat16), "seq").astype(jnp.float32),
        lax.psum(pieces[3].astype(jnp.bfloat16), "seq").astype(jnp.float32),
        lax.psum(pieces[4].astype(jnp.bfloat16), "seq").astype(jnp.float32),
        lax.psum(pieces[5].astype(jnp.bfloat16), "seq").astype(jnp.float32),
        lax.psum(pieces[6].astype(jnp.bfloat16), "seq").astype(jnp.float32),
        lax.psum(pieces[7].astype(jnp.bfloat16), "seq").astype(jnp.float32),
        lax.psum(pieces[8].astype(jnp.bfloat16), "seq").astype(jnp.float32),
    )
    return (
        block_output,
        input_grad,
        shares[0],
        shares[1],
        shares[2],
        shares[3],
        shares[4],
        shares[5],
        shares[6],
        shares[7],
        shares[8],
    )


def plain_solution(mesh):
    placed = (
        P("fsdp", "seq", None),
        P("fsdp", "seq"),
        P("fsdp"),
        P("fsdp", None),
        P("fsdp", None),
        P("fsdp", None),
        P("fsdp", None),
        P("fsdp"),
        P("fsdp", None),
        P("fsdp", None),
        P("fsdp", None),
        P("fsdp", "seq", None),
    )
    return jax.shard_map(
        plain_body,
        mesh=mesh,
        in_specs=placed,
        out_specs=(
            P("fsdp", "seq", None),
            P("fsdp", "seq", None),
            P("fsdp"),
            P("fsdp", None),
            P("fsdp", None),
            P("fsdp", None),
            P("fsdp", None),
            P("fsdp"),
            P("fsdp", None),
            P("fsdp", None),
            P("fsdp", None),
        ),
        check_vma=False,
    )
```
